32 devices in a mesh: expert: 4 (over y, x), context: 4 (over z), dp: 2 (over core).
Axes of the slice: x: 2, y: 2, z: 4, core: 2. Of those that a mesh axis runs over, the one named last changes fastest.
Arguments:
- layer_input: bfloat16 [8, 1024, 1536], P(('expert', 'dp'), 'context'), may hold values from -6 to 6
- gain_attn: bfloat16 [1536], P(('expert', 'context', 'dp')), may hold values from 0.5 to 1.5
- query_key_value_weight: bfloat16 [1536, 2048], P(('expert', 'context', 'dp')), may hold values from -0.15625 to 0.15625
- w_out: bfloat16 [1536, 1536], P(None, ('expert', 'context', 'dp')), may hold values from -2 to 2
- w_router: bfloat16 [1536, 8], P(('expert', 'context', 'dp')), may hold values from -0.078125 to 0.078125
- gain_ffn: bfloat16 [1536], P(('expert', 'context', 'dp')), may hold values from 0.5 to 1.5
- w_gate_up: bfloat16 [8, 1536, 1536], P('expert'), may hold values from -0.15625 to 0.15625
- w_down: bfloat16 [8, 768, 1536], P('expert'), may hold values from -0.625 to 0.625
- routes: int32 [8, 1024, 4], P(('expert', 'dp'), 'context'), may hold values from 0 to 7, all different within a row; in each aligned block of 256 rows (0 to 255, 256 to 511, ..., all dimensions but the last counted through in order) at most 256 rows name the same one
- d_out: bfloat16 [8, 1024, 1536], P(('expert', 'dp'), 'context'), may hold values from -6 to 6
Outputs:
- layer_output: bfloat16 [8, 1024, 1536], P(('expert', 'dp'), 'context')
- d_x: bfloat16 [8, 1024, 1536], P(('expert', 'dp'), 'context')
- g_gain_attn: float32 [1536], P(('expert', 'context', 'dp'))
- g_w_qkv: float32 [1536, 2048], P(('expert', 'context', 'dp'))
- g_w_out: float32 [1536, 1536], P(None, ('expert', 'context', 'dp'))
- g_w_router: float32 [1536, 8], P(('expert', 'context', 'dp'))
- g_gain_ffn: float32 [1536], P(('expert', 'context', 'dp'))
- g_w_gate_up: float32 [8, 1536, 1536], P('expert', ('context', 'dp'))
- g_w_down: float32 [8, 768, 1536], P('expert', None, ('context', 'dp'))
The draws below stay inside these ranges and needn't reach their ends.
Inputs may be any that keep to these rules, and one draw needn't show every extreme that they name: `routes`: each token names 4 different experts. In each aligned block of 256 tokens (the tokens of one device) no expert is named by more than 256 tokens, a bound that some block reaches.
All inputs are finite; a program needn't handle non-finite values.
Results may differ from the reference program's by a relative error of at most 0.018.
Values may be sent and summed in bfloat16 or wider, within the bound.
A program may use at most 256 MiB of HBM per device.

```python
import math
import jax
import jax.numpy as jnp
import numpy as np
from jax import lax

MODEL_DIMENSION = 1536
QUERY_HEADS = 12
KEY_VALUE_HEADS = 2
HEAD_DIMENSION = 128
FF = 768
TOP = 4
TOK_DEV = 256
EXPERTS = 8
SEQUENCE_LENGTH = 1024
SEQS = 8
CAP = 256


def with_spikes(entries, key, source, target, parts, factor):
    owner, partner = [(jnp.arange(entries.shape[dim]) // (entries.shape[dim] // parts)).reshape([-1 if axis == dim else 1 for axis in range(entries.ndim)]) for dim in (source, target)]
    chosen = jax.random.permutation(key, parts)[partner]
    strong = (owner == chosen) | (owner == (partner + parts // 2) % parts)
    return jnp.where(strong, factor * entries, entries)


def levels(own_key, shape, shards, least, top_value):
    gain = 1.0
    for dim, shards_of in shards:
        heights = jax.random.uniform(jax.random.fold_in(jax.random.fold_in(own_key, 6), dim), (shards_of,), jnp.float32, least / len(shards), top_value / len(shards))
        gain = gain * jnp.repeat(jnp.exp(heights), shape[dim] // shards_of).reshape((-1,) + (1,) * (len(shape) - 1 - dim))
    return gain


def assign_block(rng, own, number, rows, amount, top, reach, slope):
    order = jax.random.permutation(rng, amount)
    heavy_load, ordinary = shares(amount, rows * top, reach, slope, True), shares(amount, rows * top, reach, slope, False)
    places = jnp.arange(amount)

    def named(tallies, offset_by):
        used = int((tallies > 0).sum())
        fixed = max(1, used // 4)
        moved = fixed + (places - fixed + offset_by * (used - fixed)) % max(1, amount - fixed)
        return jnp.zeros((amount,), jnp.int32).at[order[jnp.where(places < fixed, places, moved)]].set(jnp.asarray(tallies, jnp.int32))

    tallies = jnp.where(number % 4 == 0, named(heavy_load, number // 4), named(ordinary, number - number // 4 - 1))
    mixed = jax.random.permutation(jax.random.fold_in(own, 3), amount)
    donor, sink = mixed[0:amount // 2 * 2:2], mixed[1:amount // 2 * 2:2]
    margin = jnp.minimum(tallies[donor] - 1, reach - tallies[sink]) // 2
    margin = jnp.where((donor == order[0]) | (sink == order[0]) | (tallies[sink] == 0), 0, jnp.maximum(margin, 0))
    moved = jax.random.randint(jax.random.fold_in(own, 4), (amount // 2,), 0, 1 << 20) % (margin + 1)
    tallies = tallies.at[donor].add(-moved).at[sink].add(moved)
    labels = jnp.searchsorted(jnp.cumsum(tallies), jnp.arange(rows * top), side="right").astype(jnp.int32)
    grid = labels.reshape(top, rows).T
    grid = grid[jax.random.permutation(jax.random.fold_in(own, 1), rows)]
    offset_by = jax.random.randint(jax.random.fold_in(own, 2), (rows, 1), 0, top)
    return jnp.take_along_axis(grid, (jnp.arange(top)[None, :] + offset_by) % top, axis=1)


def shares(amount, total, reach, skew, full):
    loads = [(1 << 20) // math.isqrt(grade ** skew) + 1 for grade in range(1, amount + 1)]
    largest = reach if full else min(reach, max(-(-total // amount), total * loads[0] // sum(loads)))
    least = 1 if total - largest >= amount - 1 else 0
    counts, spare = [largest] + [least] * (amount - 1), total - largest - least * (amount - 1)
    while spare > 0:
        free = [i for i in range(1, amount) if counts[i] < largest] or [i for i in range(1, amount) if counts[i] < reach]
        mass, remaining = sum([loads[i] for i in free]), spare
        for i in free:
            addition = min(reach - counts[i], max(1, remaining * loads[i] // mass), spare)
            counts[i] = counts[i] + addition
            spare = spare - addition
    return np.array(counts)


def bell_draw(stream_key, extent, spread, limit, shards=(), kind=jnp.bfloat16):
    entries = jax.random.normal(stream_key, extent, jnp.float32) * spread
    if len(shards) > 0:
        entries = levels(stream_key, extent, shards, -0.22, 0.18) * entries
    return jnp.clip(entries, min=-limit, max=limit).astype(kind)


def bell_draw_with(own_key, dims, scale, limit, shards, heavy, kind=jnp.bfloat16):
    drawn = scale * jax.random.normal(own_key, dims, jnp.float32)
    if shards:
        drawn = drawn * levels(own_key, dims, shards, -0.22, 0.18)
    return jnp.clip(with_spikes(drawn, jax.random.fold_in(own_key, 3), *heavy), -limit, limit).astype(kind)


def setup_inputs(seed: int = 0) -> dict:
    splits = jax.random.split(jax.random.key(seed), 11)
    layer_input = bell_draw(splits[0], (SEQS, SEQUENCE_LENGTH, MODEL_DIMENSION), 1.0, 6.0, ((0, 8), (1, 4)))
    gain_attn = jnp.clip(1.0 + 0.1 * jax.random.normal(splits[1], (MODEL_DIMENSION,), jnp.float32), 0.5, 1.5).astype(jnp.bfloat16)
    query_key_value_weight = bell_draw(splits[2], (MODEL_DIMENSION, (QUERY_HEADS + 2 * KEY_VALUE_HEADS) * HEAD_DIMENSION), MODEL_DIMENSION ** -0.5, 0.15625, ((0, 32),))
    w_out = bell_draw(splits[3], (QUERY_HEADS * HEAD_DIMENSION, MODEL_DIMENSION), (max(1, QUERY_HEADS * HEAD_DIMENSION // 192)) ** -0.5, 2.0, ((1, 32),))
    w_router = bell_draw(splits[4], (MODEL_DIMENSION, EXPERTS), (4 * MODEL_DIMENSION) ** -0.5, 0.078125, ((0, 32),))
    gain_ffn = jnp.clip(1.0 + 0.1 * jax.random.normal(splits[5], (MODEL_DIMENSION,), jnp.float32), 0.5, 1.5).astype(jnp.bfloat16)
    w_gate_up = bell_draw(splits[6], (EXPERTS, MODEL_DIMENSION, 2 * FF), MODEL_DIMENSION ** -0.5, 0.15625, ((0, 4),))
    w_down = bell_draw(splits[7], (EXPERTS, FF, MODEL_DIMENSION), (FF // 8) ** -0.5, 0.625, ((0, 4),))
    routes_keys = jax.random.split(jax.random.fold_in(splits[8], 1), SEQS * SEQUENCE_LENGTH // TOK_DEV)
    routes_turns = jax.random.permutation(jax.random.fold_in(splits[8], 3), SEQS * SEQUENCE_LENGTH // TOK_DEV)
    routes = jax.vmap(lambda own, number: assign_block(jax.random.fold_in(splits[8], 2), own, number, TOK_DEV, EXPERTS, TOP, CAP, 2))(routes_keys, routes_turns).reshape((SEQS, SEQUENCE_LENGTH, TOP))
    d_out = bell_draw_with(splits[9], (SEQS, SEQUENCE_LENGTH, MODEL_DIMENSION), 1.0, 6.0, ((0, 8), (1, 4)), (0, 2, 8, 2.0))
    return dict(layer_input=layer_input, gain_attn=gain_attn, query_key_value_weight=query_key_value_weight, w_out=w_out, w_router=w_router, gain_ffn=gain_ffn, w_gate_up=w_gate_up, w_down=w_down, routes=routes, d_out=d_out)


EPSILON = 1e-06
ROPE_BASE = 10000.0
MASKED = -1e+30
HIGHEST = lax.Precision.HIGHEST

@jax.custom_vjp
def lower_precision(v):
    return lax.optimization_barrier(v.astype(jnp.bfloat16)).astype(jnp.float32)

@jax.custom_vjp
def low_back(v):
    return v

def low_keep(v):
    return (lower_precision(v), None)

def low_pass(kept, grad):
    return (grad,)

def back_keep(v):
    return (v, None)

def back_low(kept, grad):
    return (lower_precision(grad),)
lower_precision.defvjp(low_keep, low_pass)
low_back.defvjp(back_keep, back_low)

def rms_scale(values, weights):
    inverse = lax.rsqrt(lax.optimization_barrier(jnp.mean(values * values, axis=-1, keepdims=True)) + EPSILON)
    return values * inverse * weights

def rope_tables(positions, width):
    halfway = width // 2
    fraction = jnp.arange(halfway, dtype=jnp.float32) * (2.0 / width)
    frequency = jnp.exp(-math.log(ROPE_BASE) * fraction)
    angles = positions.astype(jnp.float32)[:, None] * frequency[None, :]
    cosine_values = jnp.cos(angles)
    sine_values = jnp.sin(angles)
    return (jnp.concatenate([cosine_values, cosine_values], -1), jnp.concatenate([sine_values, sine_values], -1))

def rotate_half(values, cosine_values, sine_values):
    halfway = values.shape[-1] // 2
    turned = jnp.concatenate([-values[..., halfway:], values[..., :halfway]], -1)
    return values * cosine_values[:, None, :] + turned * sine_values[:, None, :]

def attend_causal(triple):
    query_rows, keys_in, values_in = triple
    length_tokens = query_rows.shape[0]
    grouped_rows = query_rows.reshape(length_tokens, KEY_VALUE_HEADS, QUERY_HEADS // KEY_VALUE_HEADS, HEAD_DIMENSION)
    raw_scores = low_back(jnp.einsum('tkgd,skd->kgts', grouped_rows, keys_in, precision=HIGHEST))
    places = jnp.arange(length_tokens)
    scores = jnp.where(places[None, :] <= places[:, None], raw_scores * HEAD_DIMENSION ** (-0.5), MASKED)
    probs = jax.nn.softmax(scores, axis=-1)
    mixed_heads = jnp.einsum('kgts,skd->tkgd', lower_precision(probs), values_in, precision=HIGHEST)
    return mixed_heads.reshape(length_tokens, QUERY_HEADS * HEAD_DIMENSION)

def forward(token_rows, gain_attn, query_key_value_weight, w_out, w_router, gain_ffn, w_gate_up, w_down, routes):
    sequence_count = token_rows.shape[0]
    flat_rows = token_rows.reshape(-1, MODEL_DIMENSION)
    normed1 = rms_scale(flat_rows, gain_attn)
    inputs1 = lower_precision(normed1)
    query_key_value = low_back(jnp.dot(inputs1, query_key_value_weight, precision=HIGHEST))
    positions = jnp.tile(jnp.arange(SEQUENCE_LENGTH), sequence_count)
    cosine_values, sine_values = rope_tables(positions, HEAD_DIMENSION)
    query_width = QUERY_HEADS * HEAD_DIMENSION
    key_width = KEY_VALUE_HEADS * HEAD_DIMENSION
    query_heads = lower_precision(rotate_half(query_key_value[:, :query_width].reshape(-1, QUERY_HEADS, HEAD_DIMENSION), cosine_values, sine_values))
    key = lower_precision(rotate_half(query_key_value[:, query_width:query_width + key_width].reshape(-1, KEY_VALUE_HEADS, HEAD_DIMENSION), cosine_values, sine_values))
    value_heads = lower_precision(query_key_value[:, query_width + key_width:].reshape(-1, KEY_VALUE_HEADS, HEAD_DIMENSION))
    mixed_heads = lax.map(jax.checkpoint(attend_causal), (query_heads.reshape(sequence_count, SEQUENCE_LENGTH, QUERY_HEADS, HEAD_DIMENSION), key.reshape(sequence_count, SEQUENCE_LENGTH, KEY_VALUE_HEADS, HEAD_DIMENSION), value_heads.reshape(sequence_count, SEQUENCE_LENGTH, KEY_VALUE_HEADS, HEAD_DIMENSION)))
    heads = lower_precision(low_back(mixed_heads.reshape(-1, QUERY_HEADS * HEAD_DIMENSION)))
    attn = low_back(jnp.dot(heads, w_out, precision=HIGHEST))
    hidden = flat_rows + attn
    normed2 = rms_scale(hidden, gain_ffn)
    expert_in = lower_precision(normed2)
    logits = low_back(jnp.dot(inputs1, w_router, precision=HIGHEST))
    chosen_ids = routes.reshape(-1, TOP)
    chosen = jnp.take_along_axis(logits, chosen_ids, axis=1)
    gates = jax.nn.softmax(chosen, axis=-1)
    pair_ids = chosen_ids.reshape(-1)
    marks = (pair_ids[:, None] == jnp.arange(EXPERTS)[None, :]).astype(jnp.int32)
    position = lax.optimization_barrier(jnp.sum((jnp.cumsum(marks, 0) - 1) * marks, 1))
    room = flat_rows.shape[0] // TOK_DEV * CAP
    slot = (pair_ids * room + position).astype(jnp.int32)
    owner = (jnp.arange(pair_ids.shape[0]) // TOP).astype(jnp.int32)
    slot_owner = jnp.zeros((EXPERTS * room,), jnp.int32).at[slot].set(owner)
    filled = jnp.zeros((EXPERTS * room,), jnp.float32).at[slot].set(1.0)
    taken = low_back(expert_in[slot_owner]) * filled[:, None]
    stacked = taken.reshape(EXPERTS, room, MODEL_DIMENSION)
    gate_up = low_back(jnp.einsum('erd,edf->erf', stacked, w_gate_up, precision=HIGHEST))
    act = lower_precision(jax.nn.silu(gate_up[..., :FF]) * gate_up[..., FF:])
    outputs = lower_precision(low_back(jnp.einsum('erf,efd->erd', act, w_down, precision=HIGHEST)))
    pair_out = outputs.reshape(-1, MODEL_DIMENSION)[slot].reshape(-1, TOP, MODEL_DIMENSION)
    mixture = lax.optimization_barrier(jnp.sum(gates[:, :, None] * pair_out, 1))
    return (hidden + mixture).reshape(token_rows.shape)

def reference(layer_input, gain_attn, query_key_value_weight, w_out, w_router, gain_ffn, w_gate_up, w_down, routes, d_out):
    weights = tuple((w.astype(jnp.float32) for w in (gain_attn, query_key_value_weight, w_out, w_router, gain_ffn, w_gate_up, w_down)))
    group_size = math.gcd(SEQS, max(1, 4096 // SEQUENCE_LENGTH))
    group_count = SEQS // group_size
    rows_in = layer_input.reshape(group_count, group_size, SEQUENCE_LENGTH, MODEL_DIMENSION)
    ids_in = routes.reshape(group_count, group_size, SEQUENCE_LENGTH, TOP)
    cot_in = d_out.reshape(group_count, group_size, SEQUENCE_LENGTH, MODEL_DIMENSION)

    def one_group(totals, piece):
        rows_now, ids_now, cot_now = piece

        def local_forward(rows_arg, *weight_args):
            return forward(rows_arg, *weight_args, ids_now)
        result, pull = jax.vjp(local_forward, rows_now.astype(jnp.float32), *weights)
        grads = pull(cot_now.astype(jnp.float32))
        totals = tuple((a + b for a, b in zip(totals, grads[1:])))
        return (totals, (result.astype(jnp.bfloat16), grads[0].astype(jnp.bfloat16)))
    start = tuple((jnp.zeros_like(w) for w in weights))
    totals, (outputs, d_rows) = lax.scan(one_group, start, (rows_in, ids_in, cot_in))
    return (outputs.reshape(SEQS, SEQUENCE_LENGTH, MODEL_DIMENSION), d_rows.reshape(SEQS, SEQUENCE_LENGTH, MODEL_DIMENSION), totals[0], totals[1], totals[2], totals[3], totals[4], totals[5], totals[6])
```

```python
import functools
import math

import jax
import jax.numpy as jnp
from jax import lax
from jax.experimental import pallas as pl
from jax.experimental.pallas import tpu as pltpu
from jax.sharding import PartitionSpec as P

QUERY_HEADS = 12
KEY_VALUE_HEADS = 2
HEAD_DIMENSION = 128
TOP = 4
EXP_DEV = 2

EPSILON = 1e-06
ROPE_BASE = 10000.0
MASKED = -1e30

F32 = jnp.float32
BF16 = jnp.bfloat16


def rope_tables(positions, width):
    halfway = width // 2
    fraction = jnp.arange(halfway, dtype=jnp.float32) * (2.0 / width)
    frequency = jnp.exp(-math.log(ROPE_BASE) * fraction)
    angles = positions.astype(jnp.float32)[:, None] * frequency[None, :]
    cosine_values = jnp.cos(angles)
    sine_values = jnp.sin(angles)
    return (
        jnp.concatenate([cosine_values, cosine_values], -1),
        jnp.concatenate([sine_values, sine_values], -1),
    )


def rotate_half(values, cosine_values, sine_values):
    halfway = values.shape[-1] // 2
    turned = jnp.concatenate([-values[..., halfway:], values[..., :halfway]], -1)
    return values * cosine_values[:, None, :] + turned * sine_values[:, None, :]


def rotate_back(grads, cosine_values, sine_values):
    halfway = grads.shape[-1] // 2
    scaled = grads * sine_values[:, None, :]
    turned = jnp.concatenate([scaled[..., halfway:], -scaled[..., :halfway]], -1)
    return grads * cosine_values[:, None, :] + turned


def dot_nt(a, b):
    return lax.dot_general(a, b, (((1,), (1,)), ((), ())), preferred_element_type=F32)


def dot_tn(a, b):
    return lax.dot_general(a, b, (((0,), (0,)), ((), ())), preferred_element_type=F32)


def dot_nn(a, b):
    return jnp.dot(a, b, preferred_element_type=F32)


def masked_probs(first_row, query, key):
    scores = dot_nt(query, key) * (HEAD_DIMENSION**-0.5)
    rows = first_row + lax.broadcasted_iota(jnp.int32, scores.shape, 0)
    columns = lax.broadcasted_iota(jnp.int32, scores.shape, 1)
    scores = jnp.where(columns <= rows, scores, MASKED)
    expd = jnp.exp(scores - jnp.max(scores, axis=-1, keepdims=True))
    return expd / jnp.sum(expd, axis=-1, keepdims=True)


def attend_forward_kernel(first_ref, query_ref, key_ref, value_ref, heads_ref):
    probs = masked_probs(first_ref[0], query_ref[...], key_ref[...])
    heads_ref[...] = dot_nn(probs.astype(BF16), value_ref[...]).astype(BF16)


def attend_forward(first_row, query, key_value):
    tokens, width = query.shape
    length = key_value.shape[0]
    group = QUERY_HEADS // KEY_VALUE_HEADS
    size = HEAD_DIMENSION
    return pl.pallas_call(
        attend_forward_kernel,
        grid_spec=pltpu.PrefetchScalarGridSpec(
            num_scalar_prefetch=1,
            grid=(QUERY_HEADS,),
            in_specs=[
                pl.BlockSpec((tokens, size), lambda h, s: (0, h)),
                pl.BlockSpec((length, size), lambda h, s: (0, h // group)),
                pl.BlockSpec((length, size), lambda h, s: (0, KEY_VALUE_HEADS + h // group)),
            ],
            out_specs=pl.BlockSpec((tokens, size), lambda h, s: (0, h)),
        ),
        out_shape=jax.ShapeDtypeStruct((tokens, width), BF16),
        compiler_params=pltpu.CompilerParams(vmem_limit_bytes=32 * 1024 * 1024),
        cost_estimate=pl.CostEstimate(
            flops=4 * tokens * length * width, bytes_accessed=4 * tokens * width, transcendentals=0
        ),
    )(first_row, query, key_value, key_value)


def attend_backward_kernel(
    first_ref, query_ref, key_ref, value_ref, grad_ref, d_query_ref, d_key_ref, d_value_ref
):
    query, key, value, grad = query_ref[...], key_ref[...], value_ref[...], grad_ref[...]
    probs = masked_probs(first_ref[0], query, key)
    d_probs = dot_nt(grad, value)
    inner = jnp.sum(probs * d_probs, axis=-1, keepdims=True)
    d_raw = (probs * (d_probs - inner) * (HEAD_DIMENSION**-0.5)).astype(BF16)
    d_query_ref[...] = dot_nn(d_raw, key)
    d_key = dot_tn(d_raw, query)
    d_value = dot_tn(probs.astype(BF16), grad)

    @pl.when(pl.program_id(1) == 0)
    def _():
        d_key_ref[...] = d_key
        d_value_ref[...] = d_value

    @pl.when(pl.program_id(1) > 0)
    def _():
        d_key_ref[...] += d_key
        d_value_ref[...] += d_value


def attend_backward(first_row, query, key_value, grad):
    tokens, width = query.shape
    length = key_value.shape[0]
    group = QUERY_HEADS // KEY_VALUE_HEADS
    size = HEAD_DIMENSION
    row_spec = pl.BlockSpec((tokens, size), lambda j, g, s: (0, j * group + g))
    return pl.pallas_call(
        attend_backward_kernel,
        grid_spec=pltpu.PrefetchScalarGridSpec(
            num_scalar_prefetch=1,
            grid=(KEY_VALUE_HEADS, group),
            in_specs=[
                row_spec,
                pl.BlockSpec((length, size), lambda j, g, s: (0, j)),
                pl.BlockSpec((length, size), lambda j, g, s: (0, KEY_VALUE_HEADS + j)),
                row_spec,
            ],
            out_specs=[
                row_spec,
                pl.BlockSpec((length, size), lambda j, g, s: (0, j)),
                pl.BlockSpec((length, size), lambda j, g, s: (0, j)),
            ],
        ),
        out_shape=[
            jax.ShapeDtypeStruct((tokens, width), F32),
            jax.ShapeDtypeStruct((length, KEY_VALUE_HEADS * size), F32),
            jax.ShapeDtypeStruct((length, KEY_VALUE_HEADS * size), F32),
        ],
        compiler_params=pltpu.CompilerParams(vmem_limit_bytes=32 * 1024 * 1024),
        cost_estimate=pl.CostEstimate(
            flops=10 * tokens * length * width, bytes_accessed=8 * tokens * width, transcendentals=0
        ),
    )(first_row, query, key_value, key_value, grad)


def exchange(values, axis, mask):
    size = lax.axis_size(axis)
    return lax.ppermute(values, axis, [(i, i ^ mask) for i in range(size)])


def axis_masks(axis):
    size = lax.axis_size(axis)
    masks, bit = [], 1
    while bit < size:
        masks.append(bit)
        bit *= 2
    return masks


def cube_gather(values, axis, masks):
    held = {0: values}
    for mask in masks:
        for r, block in list(held.items()):
            held[r ^ mask] = exchange(block, axis, mask)
    return [held[r] for r in range(lax.axis_size(axis))]


def cube_scatter(blocks, axis, masks):
    held = dict(enumerate(blocks))
    for mask in masks:
        kept = {}
        for r in list(held):
            if not r & mask:
                arrived = exchange(held[r ^ mask].astype(BF16), axis, mask)
                kept[r] = held[r].astype(F32) + arrived.astype(F32)
        held = kept
    return held[0]


def line_steps(values, axis, up):
    size = lax.axis_size(axis)
    pairs = [(i, i + 1) if up else (i + 1, i) for i in range(size - 1)]
    return lax.ppermute(values, axis, pairs)


def line_gather(values, axis, both=True):
    size = lax.axis_size(axis)
    me = lax.axis_index(axis)
    result = jnp.zeros((size + 1,) + values.shape, values.dtype)
    result = lax.dynamic_update_index_in_dim(result, values, me, 0)
    up = down = values
    for step in range(1, size):
        up = line_steps(up, axis, True)
        result = lax.dynamic_update_index_in_dim(
            result, up, jnp.where(me - step >= 0, me - step, size), 0
        )
        if both:
            down = line_steps(down, axis, False)
            result = lax.dynamic_update_index_in_dim(result, down, jnp.minimum(me + step, size), 0)
    return result[:size]


def line_scatter(take, axis, up=True, down=True):
    size = lax.axis_size(axis)
    me = lax.axis_index(axis)
    total = take(me).astype(F32)
    for active, sign in ((up, 1), (down, -1)):
        if not active:
            continue
        arrived = None
        for step in range(1, size):
            block = take((me + sign * (size - step)) % size).astype(F32)
            if arrived is not None:
                block = block + arrived.astype(F32)
            arrived = line_steps(block.astype(BF16), axis, sign > 0)
        total = total + arrived.astype(F32)
    return total


def gather_rows(shard):
    ne, nc, nd = (lax.axis_size(a) for a in ("expert", "context", "dp"))
    rows, width = shard.shape
    lines = line_gather(shard, "context")
    masks = axis_masks("expert")
    half = width // 256 * 128
    parts = [lines[..., :half], lines[..., half:]]
    me = lax.axis_index("expert")
    result = jnp.zeros((ne, nc, rows, width), shard.dtype)
    for start, part, order in ((0, parts[0], masks), (half, parts[1], masks[::-1])):
        for r, block in enumerate(cube_gather(part, "expert", order)):
            result = lax.dynamic_update_slice(result, block[None], (me ^ r, 0, 0, start))
    core = lax.axis_index("dp")
    whole = jnp.zeros((ne, nc, nd, rows, width), shard.dtype)
    for r, block in enumerate(cube_gather(result, "dp", axis_masks("dp"))):
        whole = lax.dynamic_update_slice(whole, block[:, :, None], (0, 0, core ^ r, 0, 0))
    return whole.reshape(-1, width)


def scatter_rows(grad):
    ne, nc, nd = (lax.axis_size(a) for a in ("expert", "context", "dp"))
    width = grad.shape[-1]
    rows = grad.shape[0] // (ne * nc * nd)
    blocks = grad.reshape(ne, nc, nd, rows, width)
    core, me = lax.axis_index("dp"), lax.axis_index("expert")
    mine = cube_scatter(
        [
            lax.dynamic_index_in_dim(blocks, core ^ r, 2, keepdims=False)
            for r in range(nd)
        ],
        "dp",
        axis_masks("dp"),
    )
    masks = axis_masks("expert")
    half = width // 256 * 128
    sums = []
    for part, order in ((mine[..., :half], masks), (mine[..., half:], masks[::-1])):
        sums.append(
            cube_scatter(
                [lax.dynamic_index_in_dim(part, me ^ r, 0, keepdims=False) for r in range(ne)],
                "expert",
                order,
            )
        )
    lines = jnp.concatenate(sums, -1)
    return line_scatter(
        lambda j: lax.dynamic_index_in_dim(lines, j, 0, keepdims=False), "context"
    )


def plane_gather(rows):
    masks = axis_masks("expert")
    half = rows.shape[-1] // 2
    left = cube_gather(rows[:, :half], "expert", masks)
    right = cube_gather(rows[:, half:], "expert", masks[::-1])
    return jnp.concatenate([jnp.concatenate(p, -1) for p in zip(left, right)], 0)


def plane_scatter(partial, tokens):
    masks = axis_masks("expert")
    size = lax.axis_size("expert")
    half = partial.shape[-1] // 2
    blocks = partial.reshape(size, tokens, -1)
    left = cube_scatter([blocks[r, :, :half] for r in range(size)], "expert", masks)
    right = cube_scatter([blocks[r, :, half:] for r in range(size)], "expert", masks[::-1])
    return jnp.concatenate([left, right], -1)


def local(
    layer_input,
    gain_attn,
    query_key_value_weight,
    w_out,
    w_router,
    gain_ffn,
    w_gate_up,
    w_down,
    routes,
    d_out,
):
    tokens = layer_input.shape[1]
    model_width = layer_input.shape[2]
    ne, nc, nd = (lax.axis_size(a) for a in ("expert", "context", "dp"))
    expert_total = EXP_DEV * ne
    ff = w_down.shape[1]
    me = lax.axis_index("expert")
    first_row = lax.axis_index("context") * tokens
    query_width = QUERY_HEADS * HEAD_DIMENSION
    key_width = KEY_VALUE_HEADS * HEAD_DIMENSION
    qkv_width = query_width + 2 * key_width

    small = jnp.concatenate([w_router, gain_attn[:, None], gain_ffn[:, None]], -1)
    small = jnp.pad(small, ((0, 0), (0, 128 - small.shape[1])))
    gathered = gather_rows(jnp.concatenate([query_key_value_weight, small], -1))
    out_turned = gather_rows(w_out.T)
    qkv_weight = gathered[:, :qkv_width]
    router_weight = gathered[:, qkv_width : qkv_width + expert_total]
    gains = gathered[:, qkv_width + expert_total : qkv_width + expert_total + 2].T.astype(F32)
    gain_first, gain_second = gains[0], gains[1]
    cotangent_all = plane_gather(d_out[0])

    token_rows = layer_input[0].astype(F32)
    scale1 = lax.rsqrt(jnp.mean(token_rows * token_rows, -1, keepdims=True) + EPSILON)
    inputs1 = (token_rows * scale1 * gain_first).astype(BF16)
    query_key_value = dot_nn(inputs1, qkv_weight)
    cosine_values, sine_values = rope_tables(first_row + jnp.arange(tokens), HEAD_DIMENSION)
    rotated = rotate_half(
        query_key_value[:, : query_width + key_width].reshape(tokens, -1, HEAD_DIMENSION),
        cosine_values,
        sine_values,
    ).reshape(tokens, -1)
    query = rotated[:, :query_width].astype(BF16)
    key_value_local = jnp.concatenate(
        [rotated[:, query_width:], query_key_value[:, query_width + key_width :]], -1
    ).astype(BF16)
    key_value = line_gather(key_value_local, "context", both=False).reshape(nc * tokens, -1)
    first = first_row.astype(jnp.int32).reshape(1)
    heads = attend_forward(first, query, key_value)

    logits = dot_nn(inputs1, router_weight)
    chosen_ids = routes[0]
    picks = (chosen_ids[:, :, None] == jnp.arange(expert_total)[None, None, :]).astype(F32)
    chosen = jnp.sum(picks * logits[:, None, :], -1)
    gates = jax.nn.softmax(chosen, axis=-1)
    gate_dense = jnp.sum(picks * gates[:, :, None], 1).T
    gate_blocks = cube_gather(gate_dense, "expert", axis_masks("expert"))
    gate_local = jnp.concatenate(
        [lax.dynamic_slice_in_dim(b, me * EXP_DEV, EXP_DEV, 0) for b in gate_blocks], 1
    )

    attn = dot_nt(heads, out_turned)
    hidden = token_rows + attn
    scale2 = lax.rsqrt(jnp.mean(hidden * hidden, -1, keepdims=True) + EPSILON)
    expert_in = (hidden * scale2 * gain_second).astype(BF16)

    rows_all = plane_gather(expert_in)
    gate_up = jnp.einsum("td,edf->etf", rows_all, w_gate_up, preferred_element_type=F32)
    gate_part, up_part = gate_up[..., :ff], gate_up[..., ff:]
    sigma = jax.nn.sigmoid(gate_part)
    silu = gate_part * sigma
    act = silu * up_part
    gate_column = gate_local[:, :, None]
    act_gated = (act * gate_column).astype(BF16)
    partial_out = jnp.einsum("etf,efd->td", act_gated, w_down, preferred_element_type=F32)
    mixture = plane_scatter(partial_out.astype(BF16), tokens)
    layer_result = (hidden + mixture).astype(BF16)

    d_act_raw = jnp.einsum("td,efd->etf", cotangent_all, w_down, preferred_element_type=F32)
    d_gates_local = jnp.sum(d_act_raw * act, -1)
    d_act = d_act_raw * gate_column
    d_gate_part = d_act * up_part * sigma * (1.0 + gate_part * (1.0 - sigma))
    d_up_part = d_act * silu
    d_gate_up = jnp.concatenate([d_gate_part, d_up_part], -1).astype(BF16)
    d_rows = jnp.einsum("etf,edf->td", d_gate_up, w_gate_up, preferred_element_type=F32)
    grad_down = jnp.einsum("td,etf->edf", cotangent_all, act_gated, preferred_element_type=F32)
    grad_gate_up = jnp.einsum("td,etf->edf", rows_all, d_gate_up, preferred_element_type=F32)

    d_expert_in = plane_scatter(d_rows.astype(BF16), tokens)
    d_gate_blocks = d_gates_local.reshape(EXP_DEV, ne, tokens)
    d_gates_dense = jnp.zeros((expert_total, tokens), F32)
    for r in range(ne):
        arrived = d_gate_blocks[:, r]
        if r:
            arrived = exchange(arrived, "expert", r)
        d_gates_dense = lax.dynamic_update_slice(d_gates_dense, arrived, ((me ^ r) * EXP_DEV, 0))
    d_gates = jnp.sum(picks * d_gates_dense.T[:, None, :], -1)
    d_chosen = gates * (d_gates - jnp.sum(gates * d_gates, -1, keepdims=True))
    d_logits = jnp.sum(picks * d_chosen[:, :, None], 1).astype(BF16)
    grad_router = dot_tn(inputs1, d_logits)

    core = lax.axis_index("dp")
    part = model_width // (nc * nd)

    def scatter_experts(grad):
        blocks = grad.reshape(EXP_DEV, nc, nd, part, -1)
        mine = cube_scatter(
            [lax.dynamic_index_in_dim(blocks, core ^ r, 2, keepdims=False) for r in range(nd)],
            "dp",
            axis_masks("dp"),
        )
        return line_scatter(
            lambda j: lax.dynamic_index_in_dim(mine, j, 1, keepdims=False), "context"
        )

    sum_gate_up = scatter_experts(grad_gate_up)
    sum_down = jnp.swapaxes(scatter_experts(grad_down), 1, 2)

    cotangent = d_out[0].astype(F32)
    scaled2 = d_expert_in * gain_second
    d_hidden = (
        cotangent
        + scale2 * scaled2
        - hidden * (scale2 * scale2 * scale2) * jnp.mean(scaled2 * hidden, -1, keepdims=True)
    )
    grad_gain_second = jnp.sum(d_expert_in * hidden * scale2, 0)
    d_attn = d_hidden.astype(BF16)
    grad_out_turned = dot_tn(d_attn, heads)
    sum_out = scatter_rows(grad_out_turned).T
    d_heads = dot_nn(d_attn, out_turned).astype(BF16)
    d_query, d_key_all, d_value_all = attend_backward(first, query, key_value, d_heads)
    d_key_value_all = jnp.concatenate([d_key_all, d_value_all], -1).reshape(nc, tokens, -1)
    d_key_value = line_scatter(
        lambda j: lax.dynamic_index_in_dim(d_key_value_all, j, 0, keepdims=False),
        "context",
        up=False,
    )
    d_rotated = rotate_back(
        jnp.concatenate([d_query, d_key_value[:, :key_width]], -1).reshape(
            tokens, -1, HEAD_DIMENSION
        ),
        cosine_values,
        sine_values,
    ).reshape(tokens, -1)
    d_qkv = jnp.concatenate([d_rotated, d_key_value[:, key_width:]], -1).astype(BF16)
    d_inputs = dot_nt(d_qkv, qkv_weight) + dot_nt(d_logits, router_weight)
    grad_gain_first = jnp.sum(d_inputs * token_rows * scale1, 0)
    grad_qkv = dot_tn(inputs1, d_qkv)
    small_grads = jnp.concatenate(
        [grad_router, grad_gain_first[:, None], grad_gain_second[:, None]], -1
    )
    small_grads = jnp.pad(small_grads, ((0, 0), (0, 128 - small_grads.shape[1])))
    sum_rows = scatter_rows(jnp.concatenate([grad_qkv, small_grads], -1))
    sum_qkv = sum_rows[:, :qkv_width]
    sum_router = sum_rows[:, qkv_width : qkv_width + expert_total]
    sum_gain_first = sum_rows[:, qkv_width + expert_total]
    sum_gain_second = sum_rows[:, qkv_width + expert_total + 1]
    scaled1 = d_inputs * gain_first
    d_input_rows = (
        d_hidden
        + scale1 * scaled1
        - token_rows
        * (scale1 * scale1 * scale1)
        * jnp.mean(scaled1 * token_rows, -1, keepdims=True)
    ).astype(BF16)
    return (
        layer_result[None],
        d_input_rows[None],
        sum_gain_first,
        sum_qkv,
        sum_out,
        sum_router,
        sum_gain_second,
        sum_gate_up,
        sum_down,
    )


def solution(mesh):
    in_specs = (
        P(("expert", "dp"), "context", None),
        P(("expert", "context", "dp")),
        P(("expert", "context", "dp"), None),
        P(None, ("expert", "context", "dp")),
        P(("expert", "context", "dp"), None),
        P(("expert", "context", "dp")),
        P("expert", None, None),
        P("expert", None, None),
        P(("expert", "dp"), "context", None),
        P(("expert", "dp"), "context", None),
    )
    out_specs = (
        P(("expert", "dp"), "context", None),
        P(("expert", "dp"), "context", None),
        P(("expert", "context", "dp")),
        P(("expert", "context", "dp"), None),
        P(None, ("expert", "context", "dp")),
        P(("expert", "context", "dp"), None),
        P(("expert", "context", "dp")),
        P("expert", ("context", "dp"), None),
        P("expert", None, ("context", "dp")),
    )
    return jax.shard_map(local, mesh=mesh, in_specs=in_specs, out_specs=out_specs, check_vma=False)
```

```python
import functools
import math

import jax
import jax.numpy as jnp
from jax import lax
from jax.experimental import pallas as pl
from jax.experimental.pallas import tpu as pltpu
from jax.sharding import PartitionSpec as P

QUERY_HEADS = 12
KEY_VALUE_HEADS = 2
HEAD_DIMENSION = 128
TOP = 4
EXP_DEV = 2

EPSILON = 1e-06
ROPE_BASE = 10000.0
MASKED = -1e30

F32 = jnp.float32
BF16 = jnp.bfloat16


def rope_tables(positions, width):
    halfway = width // 2
    fraction = jnp.arange(halfway, dtype=jnp.float32) * (2.0 / width)
    frequency = jnp.exp(-math.log(ROPE_BASE) * fraction)
    angles = positions.astype(jnp.float32)[:, None] * frequency[None, :]
    cosine_values = jnp.cos(angles)
    sine_values = jnp.sin(angles)
    return (
        jnp.concatenate([cosine_values, cosine_values], -1),
        jnp.concatenate([sine_values, sine_values], -1),
    )


def rotate_half(values, cosine_values, sine_values):
    halfway = values.shape[-1] // 2
    turned = jnp.concatenate([-values[..., halfway:], values[..., :halfway]], -1)
    return values * cosine_values[:, None, :] + turned * sine_values[:, None, :]


def rotate_back(grads, cosine_values, sine_values):
    halfway = grads.shape[-1] // 2
    scaled = grads * sine_values[:, None, :]
    turned = jnp.concatenate([scaled[..., halfway:], -scaled[..., :halfway]], -1)
    return grads * cosine_values[:, None, :] + turned


def dot_nt(a, b):
    return lax.dot_general(a, b, (((1,), (1,)), ((), ())), preferred_element_type=F32)


def dot_tn(a, b):
    return lax.dot_general(a, b, (((0,), (0,)), ((), ())), preferred_element_type=F32)


def dot_nn(a, b):
    return jnp.dot(a, b, preferred_element_type=F32)


def masked_probs(first_row, query, key):
    scores = dot_nt(query, key) * (HEAD_DIMENSION**-0.5)
    rows = first_row + lax.broadcasted_iota(jnp.int32, scores.shape, 0)
    columns = lax.broadcasted_iota(jnp.int32, scores.shape, 1)
    scores = jnp.where(columns <= rows, scores, MASKED)
    expd = jnp.exp(scores - jnp.max(scores, axis=-1, keepdims=True))
    return expd / jnp.sum(expd, axis=-1, keepdims=True)


def attend_forward_kernel(first_ref, query_ref, key_ref, value_ref, heads_ref):
    probs = masked_probs(first_ref[0], query_ref[...], key_ref[...])
    heads_ref[...] = dot_nn(probs.astype(BF16), value_ref[...]).astype(BF16)


def attend_forward(first_row, query, key_value):
    tokens, width = query.shape
    length = key_value.shape[0]
    group = QUERY_HEADS // KEY_VALUE_HEADS
    size = HEAD_DIMENSION
    return pl.pallas_call(
        attend_forward_kernel,
        grid_spec=pltpu.PrefetchScalarGridSpec(
            num_scalar_prefetch=1,
            grid=(QUERY_HEADS,),
            in_specs=[
                pl.BlockSpec((tokens, size), lambda h, s: (0, h)),
                pl.BlockSpec((length, size), lambda h, s: (0, h // group)),
                pl.BlockSpec((length, size), lambda h, s: (0, KEY_VALUE_HEADS + h // group)),
            ],
            out_specs=pl.BlockSpec((tokens, size), lambda h, s: (0, h)),
        ),
        out_shape=jax.ShapeDtypeStruct((tokens, width), BF16),
        compiler_params=pltpu.CompilerParams(vmem_limit_bytes=32 * 1024 * 1024),
        cost_estimate=pl.CostEstimate(
            flops=4 * tokens * length * width, bytes_accessed=4 * tokens * width, transcendentals=0
        ),
    )(first_row, query, key_value, key_value)


def attend_backward_kernel(
    first_ref, query_ref, key_ref, value_ref, grad_ref, d_query_ref, d_key_ref, d_value_ref
):
    query, key, value, grad = query_ref[...], key_ref[...], value_ref[...], grad_ref[...]
    probs = masked_probs(first_ref[0], query, key)
    d_probs = dot_nt(grad, value)
    inner = jnp.sum(probs * d_probs, axis=-1, keepdims=True)
    d_raw = (probs * (d_probs - inner) * (HEAD_DIMENSION**-0.5)).astype(BF16)
    d_query_ref[...] = dot_nn(d_raw, key)
    d_key = dot_tn(d_raw, query)
    d_value = dot_tn(probs.astype(BF16), grad)

    @pl.when(pl.program_id(1) == 0)
    def _():
        d_key_ref[...] = d_key
        d_value_ref[...] = d_value

    @pl.when(pl.program_id(1) > 0)
    def _():
        d_key_ref[...] += d_key
        d_value_ref[...] += d_value


def attend_backward(first_row, query, key_value, grad):
    tokens, width = query.shape
    length = key_value.shape[0]
    group = QUERY_HEADS // KEY_VALUE_HEADS
    size = HEAD_DIMENSION
    row_spec = pl.BlockSpec((tokens, size), lambda j, g, s: (0, j * group + g))
    return pl.pallas_call(
        attend_backward_kernel,
        grid_spec=pltpu.PrefetchScalarGridSpec(
            num_scalar_prefetch=1,
            grid=(KEY_VALUE_HEADS, group),
            in_specs=[
                row_spec,
                pl.BlockSpec((length, size), lambda j, g, s: (0, j)),
                pl.BlockSpec((length, size), lambda j, g, s: (0, KEY_VALUE_HEADS + j)),
                row_spec,
            ],
            out_specs=[
                row_spec,
                pl.BlockSpec((length, size), lambda j, g, s: (0, j)),
                pl.BlockSpec((length, size), lambda j, g, s: (0, j)),
            ],
        ),
        out_shape=[
            jax.ShapeDtypeStruct((tokens, width), F32),
            jax.ShapeDtypeStruct((length, KEY_VALUE_HEADS * size), F32),
            jax.ShapeDtypeStruct((length, KEY_VALUE_HEADS * size), F32),
        ],
        compiler_params=pltpu.CompilerParams(vmem_limit_bytes=32 * 1024 * 1024),
        cost_estimate=pl.CostEstimate(
            flops=10 * tokens * length * width, bytes_accessed=8 * tokens * width, transcendentals=0
        ),
    )(first_row, query, key_value, key_value, grad)


def exchange(values, axis, mask):
    size = lax.axis_size(axis)
    return lax.ppermute(values, axis, [(i, i ^ mask) for i in range(size)])


def axis_masks(axis):
    size = lax.axis_size(axis)
    masks, bit = [], 1
    while bit < size:
        masks.append(bit)
        bit *= 2
    return masks


def cube_gather(values, axis, masks):
    held = {0: values}
    for mask in masks:
        for r, block in list(held.items()):
            held[r ^ mask] = exchange(block, axis, mask)
    return [held[r] for r in range(lax.axis_size(axis))]


def cube_scatter(blocks, axis, masks):
    held = dict(enumerate(blocks))
    for mask in masks:
        kept = {}
        for r in list(held):
            if not r & mask:
                arrived = exchange(held[r ^ mask].astype(BF16), axis, mask)
                kept[r] = held[r].astype(F32) + arrived.astype(F32)
        held = kept
    return held[0]


def line_steps(values, axis, up):
    size = lax.axis_size(axis)
    pairs = [(i, i + 1) if up else (i + 1, i) for i in range(size - 1)]
    return lax.ppermute(values, axis, pairs)


def line_gather(values, axis, both=True):
    size = lax.axis_size(axis)
    me = lax.axis_index(axis)
    result = jnp.zeros((size + 1,) + values.shape, values.dtype)
    result = lax.dynamic_update_index_in_dim(result, values, me, 0)
    up = down = values
    for step in range(1, size):
        up = line_steps(up, axis, True)
        result = lax.dynamic_update_index_in_dim(
            result, up, jnp.where(me - step >= 0, me - step, size), 0
        )
        if both:
            down = line_steps(down, axis, False)
            result = lax.dynamic_update_index_in_dim(result, down, jnp.minimum(me + step, size), 0)
    return result[:size]


def line_scatter(take, axis, up=True, down=True):
    size = lax.axis_size(axis)
    me = lax.axis_index(axis)
    total = take(me).astype(F32)
    for active, sign in ((up, 1), (down, -1)):
        if not active:
            continue
        arrived = None
        for step in range(1, size):
            block = take((me + sign * (size - step)) % size).astype(F32)
            if arrived is not None:
                block = block + arrived.astype(F32)
            arrived = line_steps(block.astype(BF16), axis, sign > 0)
        total = total + arrived.astype(F32)
    return total


def gather_rows(shard):
    ne, nc, nd = (lax.axis_size(a) for a in ("expert", "context", "dp"))
    rows, width = shard.shape
    lines = line_gather(shard, "context")
    masks = axis_masks("expert")
    half = width // 256 * 128
    parts = [lines[..., :half], lines[..., half:]]
    me = lax.axis_index("expert")
    result = jnp.zeros((ne, nc, rows, width), shard.dtype)
    for start, part, order in ((0, parts[0], masks), (half, parts[1], masks[::-1])):
        for r, block in enumerate(cube_gather(part, "expert", order)):
            result = lax.dynamic_update_slice(result, block[None], (me ^ r, 0, 0, start))
    core = lax.axis_index("dp")
    whole = jnp.zeros((ne, nc, nd, rows, width), shard.dtype)
    for r, block in enumerate(cube_gather(result, "dp", axis_masks("dp"))):
        whole = lax.dynamic_update_slice(whole, block[:, :, None], (0, 0, core ^ r, 0, 0))
    return whole.reshape(-1, width)


def scatter_rows(grad):
    ne, nc, nd = (lax.axis_size(a) for a in ("expert", "context", "dp"))
    width = grad.shape[-1]
    rows = grad.shape[0] // (ne * nc * nd)
    blocks = grad.reshape(ne, nc, nd, rows, width)
    core, me = lax.axis_index("dp"), lax.axis_index("expert")
    mine = cube_scatter(
        [
            lax.dynamic_index_in_dim(blocks, core ^ r, 2, keepdims=False)
            for r in range(nd)
        ],
        "dp",
        axis_masks("dp"),
    )
    masks = axis_masks("expert")
    half = width // 256 * 128
    sums = []
    for part, order in ((mine[..., :half], masks), (mine[..., half:], masks[::-1])):
        sums.append(
            cube_scatter(
                [lax.dynamic_index_in_dim(part, me ^ r, 0, keepdims=False) for r in range(ne)],
                "expert",
                order,
            )
        )
    lines = jnp.concatenate(sums, -1)
    return line_scatter(
        lambda j: lax.dynamic_index_in_dim(lines, j, 0, keepdims=False), "context"
    )


def plane_gather(rows):
    masks = axis_masks("expert")
    half = rows.shape[-1] // 2
    left = cube_gather(rows[:, :half], "expert", masks)
    right = cube_gather(rows[:, half:], "expert", masks[::-1])
    return jnp.concatenate([jnp.concatenate(p, -1) for p in zip(left, right)], 0)


def plane_scatter(partial, tokens):
    masks = axis_masks("expert")
    size = lax.axis_size("expert")
    half = partial.shape[-1] // 2
    blocks = partial.reshape(size, tokens, -1)
    left = cube_scatter([blocks[r, :, :half] for r in range(size)], "expert", masks)
    right = cube_scatter([blocks[r, :, half:] for r in range(size)], "expert", masks[::-1])
    return jnp.concatenate([left, right], -1)


MESH = pl.DeviceIdType.MESH
MIB = 1024 * 1024
SMALL = 128
GATE_ROWS = 16


def flip(index, mask):
    bit = 1
    while bit <= mask:
        if mask & bit:
            index = index + bit - 2 * bit * lax.rem(lax.div(index, bit), 2)
        bit *= 2
    return index


class Wire:
    def __init__(self, sends, recvs):
        self.sends, self.recvs = sends, recvs
        self.n_sends = self.n_recvs = 0
        self.open = []

    def slots(self, count):
        first = self.n_recvs
        self.n_recvs += count
        return first

    def start(self, src, dst, recv, device, when=None):
        copy = pltpu.make_async_remote_copy(
            src_ref=src,
            dst_ref=dst,
            send_sem=self.sends.at[self.n_sends],
            recv_sem=self.recvs.at[recv],
            device_id=device,
            device_id_type=MESH,
        )
        self.n_sends += 1
        guard(when, copy.start)
        self.open.append((when, copy))

    def arrived(self, dst, recv, device):
        pltpu.make_async_remote_copy(
            src_ref=dst,
            dst_ref=dst,
            send_sem=self.sends.at[0],
            recv_sem=self.recvs.at[recv],
            device_id=device,
            device_id_type=MESH,
        ).wait_recv()

    def finish(self):
        for when, copy in self.open:
            guard(when, copy.wait_send)
        self.open = []


def guard(when, action):
    if when is None:
        action()
    else:
        pl.when(when)(action)


def greet(targets):
    barrier = pltpu.get_barrier_semaphore()
    for device, when in targets:
        guard(
            when,
            lambda device=device: pl.semaphore_signal(
                barrier, inc=1, device_id=device, device_id_type=MESH
            ),
        )
    count = sum(1 if when is None else when.astype(jnp.int32) for _, when in targets)
    pl.semaphore_wait(barrier, count)


def plane_ids(e):
    return {m: {"expert": flip(e, m)} for m in (1, 2, 3)}


class RowsGather:
    def __init__(self, wire, ref, e, z, c, nc, half):
        self.wire, self.ref, self.e, self.z, self.c, self.nc = wire, ref, e, z, c, nc
        self.cols = (pl.ds(0, half), pl.ds(half, ref.shape[-1] - half))
        self.line = wire.slots(nc)
        self.plane = wire.slots(nc * 6)
        self.core = wire.slots(nc)
        self.ids = plane_ids(e)
        self.steps = []
        for k in range(nc):
            self.steps.append(functools.partial(self.spread, k))
            if k:
                self.steps.append(functools.partial(self.forward, k - 1))
            if k > 1:
                self.steps.append(functools.partial(self.share, k - 2))
        self.steps.append(functools.partial(self.forward, nc - 1))
        self.steps.append(functools.partial(self.share, nc - 2))
        self.steps.append(functools.partial(self.share, nc - 1))
        self.steps.append(self.complete)

    def at(self, r, zs, half):
        return self.ref.at[flip(self.e, r), zs, self.c, :, self.cols[half]]

    def slot(self, k, r, half):
        return self.plane + k * 6 + (r - 1) * 2 + half

    def spread(self, k):
        wire, z, nc = self.wire, self.z, self.nc
        zs = flip(z, k)
        whole = self.ref.at[self.e, zs, self.c]
        if k:
            wire.arrived(whole, self.line + zs, {"context": zs})
        wire.start(
            whole, whole, self.line + zs, {"context": z + 1}, when=(zs <= z) & (z < nc - 1)
        )
        wire.start(whole, whole, self.line + zs, {"context": z - 1}, when=(zs >= z) & (z > 0))
        for half, mask in ((0, 1), (1, 2), (1, 1), (0, 2)):
            part = self.at(0, zs, half)
            wire.start(part, part, self.slot(k, mask, half), self.ids[mask])

    def forward(self, k):
        zs = flip(self.z, k)
        for half, mask in ((0, 1), (1, 2)):
            part = self.at(mask, zs, half)
            self.wire.arrived(part, self.slot(k, mask, half), self.ids[mask])
            self.wire.start(part, part, self.slot(k, 3, half), self.ids[3 - mask])

    def share(self, k):
        zs = flip(self.z, k)
        for r, half in ((1, 1), (2, 0), (3, 0), (3, 1)):
            self.wire.arrived(self.at(r, zs, half), self.slot(k, r, half), self.ids[r])
        part = self.ref.at[:, zs, self.c]
        self.wire.start(part, part, self.core + k, {"dp": 1 - self.c})

    def complete(self):
        for k in range(self.nc):
            zs = flip(self.z, k)
            self.wire.arrived(self.ref.at[:, zs, 1 - self.c], self.core + k, {"dp": 1 - self.c})

    def step(self):
        if self.steps:
            self.steps.pop(0)()

    def run(self):
        while self.steps:
            self.step()


class PlaneGather:
    def __init__(self, wire, ref, e):
        self.wire, self.ref = wire, ref
        self.half = ref.shape[-1] // 2
        self.ids = plane_ids(e)
        self.first = wire.slots(6)
        self.steps = [self.spread, self.forward, self.complete]

    def at(self, r, half):
        return self.ref.at[r, :, pl.ds(half * self.half, self.half)]

    def slot(self, r, half):
        return self.first + (r - 1) * 2 + half

    def spread(self):
        for half, mask in ((0, 1), (1, 2), (1, 1), (0, 2)):
            self.wire.start(
                self.at(0, half), self.at(mask, half), self.slot(mask, half), self.ids[mask]
            )

    def forward(self):
        for half, mask in ((0, 1), (1, 2)):
            self.wire.arrived(self.at(mask, half), self.slot(mask, half), self.ids[mask])
            self.wire.start(
                self.at(mask, half), self.at(3, half), self.slot(3, half), self.ids[3 - mask]
            )

    def near(self, r):
        half = 1 if r == 1 else 0
        self.wire.arrived(self.at(r, half), self.slot(r, half), self.ids[r])

    def far(self):
        for half in (0, 1):
            self.wire.arrived(self.at(3, half), self.slot(3, half), self.ids[3])

    def complete(self):
        self.near(1)
        self.near(2)
        self.far()

    def step(self):
        if self.steps:
            self.steps.pop(0)()

    def run(self):
        while self.steps:
            self.step()


def swap_halves(values):
    return pltpu.roll(values, HEAD_DIMENSION // 2, 1)


def front_kernel(
    nc,
    experts,
    x_ref,
    q_shard,
    o_shard,
    cot_ref,
    cos_ref,
    sin_ref,
    routes_ref,
    q_all,
    o_all,
    cot_all,
    gate_all,
    inputs_ref,
    query_ref,
    kv_ref,
    heads_ref,
    hidden_ref,
    expert_in_ref,
    qkv_scr,
    sends,
    recvs,
):
    e, z, c = (lax.axis_index(a) for a in ("expert", "context", "dp"))
    size = HEAD_DIMENSION
    tokens, width = x_ref.shape
    query_width = QUERY_HEADS * size
    kv_width = 2 * KEY_VALUE_HEADS * size
    wire = Wire(sends, recvs)
    ids = plane_ids(e)
    greet(
        [(ids[m], None) for m in (1, 2, 3)]
        + [({"dp": 1 - c}, None), ({"context": z + 1}, z < nc - 1), ({"context": z - 1}, z > 0)]
    )
    q_all[e, z, c] = q_shard[...]
    o_all[e, z, c] = o_shard[...]
    cot_all[0] = cot_ref[...]

    gather_q = RowsGather(wire, q_all, e, z, c, nc, 1024)
    gather_o = RowsGather(wire, o_all, e, z, c, nc, 768)
    gather_cot = PlaneGather(wire, cot_all, e)
    gather_q.run()
    gather_o.step()

    small = q_all[:, :, :, :, pl.ds(query_width + kv_width, SMALL)].reshape(width, SMALL)
    small = jnp.transpose(small.astype(F32))
    gain_first, gain_second = small[experts : experts + 1], small[experts + 1 : experts + 2]
    rows = x_ref[...].astype(F32)
    scale1 = lax.rsqrt(jnp.mean(rows * rows, -1, keepdims=True) + EPSILON)
    inputs_ref[...] = (rows * scale1 * gain_first).astype(BF16)

    def project(first, count):
        weight = q_all[:, :, :, :, pl.ds(first, count)].reshape(width, count)
        qkv_scr[:, pl.ds(first, count)] = dot_nn(inputs_ref[...], weight)

    project(query_width, kv_width)

    def turned(column):
        head = qkv_scr[:, pl.ds(column, size)]
        return (head * cos_ref[...] + swap_halves(head) * sin_ref[...]).astype(BF16)

    for j in range(KEY_VALUE_HEADS):
        kv_ref[z, :, pl.ds(j * size, size)] = turned(query_width + j * size)
    values = pl.ds(kv_width // 2, kv_width // 2)
    kv_ref[z, :, values] = qkv_scr[:, pl.ds(query_width + kv_width // 2, kv_width // 2)].astype(
        BF16
    )
    line = wire.slots(nc)
    wire.start(kv_ref.at[z], kv_ref.at[z], line, {"context": z + 1}, when=z < nc - 1)
    for later in range(1, nc):

        def clear(later=later):
            kv_ref[z + later] = jnp.zeros(kv_ref.shape[1:], BF16)

        pl.when(z + later < nc)(clear)
    gather_o.step()

    @pl.loop(0, query_width // 256)
    def _(n):
        project(pl.multiple_of(n * 256, 256), 256)

    gather_o.step()
    project(query_width + kv_width, SMALL)
    gather_o.step()

    @pl.loop(0, QUERY_HEADS)
    def _(h):
        column = pl.multiple_of(h * size, size)
        query_ref[:, pl.ds(column, size)] = turned(column)

    gather_o.step()

    logits = qkv_scr[:, pl.ds(query_width + kv_width, SMALL)]
    lanes = lax.broadcasted_iota(jnp.int32, logits.shape, 1)
    named = lanes == routes_ref[:, 0:1]
    for k in range(1, TOP):
        named = named | (lanes == routes_ref[:, k : k + 1])
    logits = jnp.where(named, logits, MASKED)
    expd = jnp.exp(logits - jnp.max(logits, -1, keepdims=True))
    gates = expd / jnp.sum(expd, -1, keepdims=True)
    gate_all[0] = jnp.transpose(gates)[:GATE_ROWS]
    gate_slot = wire.slots(3)
    for r in (1, 2, 3):
        wire.start(gate_all.at[0], gate_all.at[r], gate_slot + r - 1, ids[r])

    gather_o.step()
    for step in range(1, nc):

        def pass_on(step=step):
            block = kv_ref.at[z - step]
            wire.arrived(block, line + step - 1, {"context": z - 1})

        pl.when(z >= step)(pass_on)
        wire.start(
            kv_ref.at[z - step],
            kv_ref.at[z - step],
            line + step,
            {"context": z + 1},
            when=(z >= step) & (z < nc - 1),
        )
        gather_o.step()
    gather_o.step()
    gather_o.step()

    length = nc * tokens
    group = QUERY_HEADS // KEY_VALUE_HEADS
    group_steps = 3
    for first in range(0, QUERY_HEADS, group_steps):
        j = first // group
        key = kv_ref[:, :, pl.ds(j * size, size)].reshape(length, size)
        value = kv_ref[:, :, pl.ds(kv_width // 2 + j * size, size)].reshape(length, size)

        @pl.loop(first, first + group_steps)
        def _(h):
            column = pl.multiple_of(h * size, size)
            scores = dot_nt(query_ref[:, pl.ds(column, size)], key) * (size**-0.5)
            row = z * tokens + lax.broadcasted_iota(jnp.int32, scores.shape, 0)
            place = lax.broadcasted_iota(jnp.int32, scores.shape, 1)
            scores = jnp.where(place <= row, scores, MASKED)
            expd = jnp.exp(scores - jnp.max(scores, -1, keepdims=True))
            total = jnp.sum(expd, -1, keepdims=True)
            mixed = dot_nn(expd.astype(BF16), value) / total
            heads_ref[:, pl.ds(column, size)] = mixed.astype(BF16)

        gather_o.step()
        gather_o.step()
        if first == 0:
            gather_o.run()
            gather_cot.step()
        else:
            gather_cot.step()

    gather_o.run()
    part = width // q_all.shape[0]
    for block in range(q_all.shape[0]):
        weight = o_all[block].reshape(part, width)
        columns = pl.ds(block * part, part)
        hidden_ref[:, columns] = x_ref[:, columns].astype(F32) + dot_nt(heads_ref[...], weight)
    hidden = hidden_ref[...]
    scale2 = lax.rsqrt(jnp.mean(hidden * hidden, -1, keepdims=True) + EPSILON)
    expert_in_ref[...] = (hidden * scale2 * gain_second).astype(BF16)
    gather_cot.run()
    for r in (1, 2, 3):
        wire.arrived(gate_all.at[r], gate_slot + r - 1, ids[r])
    wire.finish()


def front(x, q_shard, o_shard, cot, cosine, sine, routes, sizes):
    ne, nc, nd = sizes
    tokens, width = x.shape
    rows, q_width = q_shard.shape
    shapes = [
        ((ne, nc, nd, rows, q_width), BF16),
        ((ne, nc, nd, rows, width), BF16),
        ((ne, tokens, width), BF16),
        ((ne, GATE_ROWS, tokens), F32),
        ((tokens, width), BF16),
        ((tokens, QUERY_HEADS * HEAD_DIMENSION), BF16),
        ((nc, tokens, 2 * KEY_VALUE_HEADS * HEAD_DIMENSION), BF16),
        ((tokens, QUERY_HEADS * HEAD_DIMENSION), BF16),
        ((tokens, width), F32),
        ((tokens, width), BF16),
    ]
    copies = 128
    return pl.pallas_call(
        functools.partial(front_kernel, nc, EXP_DEV * ne),
        out_shape=[jax.ShapeDtypeStruct(*s) for s in shapes],
        in_specs=[pl.BlockSpec(memory_space=pltpu.VMEM)] * 7,
        out_specs=[pl.BlockSpec(memory_space=pltpu.VMEM)] * len(shapes),
        scratch_shapes=[
            pltpu.VMEM((tokens, q_width), F32),
            pltpu.SemaphoreType.DMA((copies,)),
            pltpu.SemaphoreType.DMA((copies,)),
        ],
        compiler_params=pltpu.CompilerParams(
            collective_id=0, has_side_effects=True, vmem_limit_bytes=56 * MIB
        ),
    )(x, q_shard, o_shard, cot, cosine, sine, routes)


def local_plain(
    layer_input,
    gain_attn,
    query_key_value_weight,
    w_out,
    w_router,
    gain_ffn,
    w_gate_up,
    w_down,
    routes,
    d_out,
):
    tokens = layer_input.shape[1]
    model_width = layer_input.shape[2]
    ne, nc, nd = (lax.axis_size(a) for a in ("expert", "context", "dp"))
    expert_total = EXP_DEV * ne
    ff = w_down.shape[1]
    me = lax.axis_index("expert")
    first_row = lax.axis_index("context") * tokens
    query_width = QUERY_HEADS * HEAD_DIMENSION
    key_width = KEY_VALUE_HEADS * HEAD_DIMENSION
    qkv_width = query_width + 2 * key_width

    small = jnp.concatenate([w_router, gain_attn[:, None], gain_ffn[:, None]], -1)
    small = jnp.pad(small, ((0, 0), (0, 128 - small.shape[1])))
    gathered = gather_rows(jnp.concatenate([query_key_value_weight, small], -1))
    out_turned = gather_rows(w_out.T)
    qkv_weight = gathered[:, :qkv_width]
    router_weight = gathered[:, qkv_width : qkv_width + expert_total]
    gains = gathered[:, qkv_width + expert_total : qkv_width + expert_total + 2].T.astype(F32)
    gain_first, gain_second = gains[0], gains[1]
    cotangent_all = plane_gather(d_out[0])

    token_rows = layer_input[0].astype(F32)
    scale1 = lax.rsqrt(jnp.mean(token_rows * token_rows, -1, keepdims=True) + EPSILON)
    inputs1 = (token_rows * scale1 * gain_first).astype(BF16)
    query_key_value = dot_nn(inputs1, qkv_weight)
    cosine_values, sine_values = rope_tables(first_row + jnp.arange(tokens), HEAD_DIMENSION)
    rotated = rotate_half(
        query_key_value[:, : query_width + key_width].reshape(tokens, -1, HEAD_DIMENSION),
        cosine_values,
        sine_values,
    ).reshape(tokens, -1)
    query = rotated[:, :query_width].astype(BF16)
    key_value_local = jnp.concatenate(
        [rotated[:, query_width:], query_key_value[:, query_width + key_width :]], -1
    ).astype(BF16)
    key_value = line_gather(key_value_local, "context", both=False).reshape(nc * tokens, -1)
    first = first_row.astype(jnp.int32).reshape(1)
    heads = attend_forward(first, query, key_value)

    logits = dot_nn(inputs1, router_weight)
    chosen_ids = routes[0]
    picks = (chosen_ids[:, :, None] == jnp.arange(expert_total)[None, None, :]).astype(F32)
    chosen = jnp.sum(picks * logits[:, None, :], -1)
    gates = jax.nn.softmax(chosen, axis=-1)
    gate_dense = jnp.sum(picks * gates[:, :, None], 1).T
    gate_blocks = cube_gather(gate_dense, "expert", axis_masks("expert"))
    gate_local = jnp.concatenate(
        [lax.dynamic_slice_in_dim(b, me * EXP_DEV, EXP_DEV, 0) for b in gate_blocks], 1
    )

    attn = dot_nt(heads, out_turned)
    hidden = token_rows + attn
    scale2 = lax.rsqrt(jnp.mean(hidden * hidden, -1, keepdims=True) + EPSILON)
    expert_in = (hidden * scale2 * gain_second).astype(BF16)

    rows_all = plane_gather(expert_in)
    gate_up = jnp.einsum("td,edf->etf", rows_all, w_gate_up, preferred_element_type=F32)
    gate_part, up_part = gate_up[..., :ff], gate_up[..., ff:]
    sigma = jax.nn.sigmoid(gate_part)
    silu = gate_part * sigma
    act = silu * up_part
    gate_column = gate_local[:, :, None]
    act_gated = (act * gate_column).astype(BF16)
    partial_out = jnp.einsum("etf,efd->td", act_gated, w_down, preferred_element_type=F32)
    mixture = plane_scatter(partial_out.astype(BF16), tokens)
    layer_result = (hidden + mixture).astype(BF16)

    d_act_raw = jnp.einsum("td,efd->etf", cotangent_all, w_down, preferred_element_type=F32)
    d_gates_local = jnp.sum(d_act_raw * act, -1)
    d_act = d_act_raw * gate_column
    d_gate_part = d_act * up_part * sigma * (1.0 + gate_part * (1.0 - sigma))
    d_up_part = d_act * silu
    d_gate_up = jnp.concatenate([d_gate_part, d_up_part], -1).astype(BF16)
    d_rows = jnp.einsum("etf,edf->td", d_gate_up, w_gate_up, preferred_element_type=F32)
    grad_down = jnp.einsum("td,etf->edf", cotangent_all, act_gated, preferred_element_type=F32)
    grad_gate_up = jnp.einsum("td,etf->edf", rows_all, d_gate_up, preferred_element_type=F32)

    d_expert_in = plane_scatter(d_rows.astype(BF16), tokens)
    d_gate_blocks = d_gates_local.reshape(EXP_DEV, ne, tokens)
    d_gates_dense = jnp.zeros((expert_total, tokens), F32)
    for r in range(ne):
        arrived = d_gate_blocks[:, r]
        if r:
            arrived = exchange(arrived, "expert", r)
        d_gates_dense = lax.dynamic_update_slice(d_gates_dense, arrived, ((me ^ r) * EXP_DEV, 0))
    d_gates = jnp.sum(picks * d_gates_dense.T[:, None, :], -1)
    d_chosen = gates * (d_gates - jnp.sum(gates * d_gates, -1, keepdims=True))
    d_logits = jnp.sum(picks * d_chosen[:, :, None], 1).astype(BF16)
    grad_router = dot_tn(inputs1, d_logits)

    core = lax.axis_index("dp")
    part = model_width // (nc * nd)

    def scatter_experts(grad):
        blocks = grad.reshape(EXP_DEV, nc, nd, part, -1)
        mine = cube_scatter(
            [lax.dynamic_index_in_dim(blocks, core ^ r, 2, keepdims=False) for r in range(nd)],
            "dp",
            axis_masks("dp"),
        )
        return line_scatter(
            lambda j: lax.dynamic_index_in_dim(mine, j, 1, keepdims=False), "context"
        )

    sum_gate_up = scatter_experts(grad_gate_up)
    sum_down = jnp.swapaxes(scatter_experts(grad_down), 1, 2)

    cotangent = d_out[0].astype(F32)
    scaled2 = d_expert_in * gain_second
    d_hidden = (
        cotangent
        + scale2 * scaled2
        - hidden * (scale2 * scale2 * scale2) * jnp.mean(scaled2 * hidden, -1, keepdims=True)
    )
    grad_gain_second = jnp.sum(d_expert_in * hidden * scale2, 0)
    d_attn = d_hidden.astype(BF16)
    grad_out_turned = dot_tn(d_attn, heads)
    sum_out = scatter_rows(grad_out_turned).T
    d_heads = dot_nn(d_attn, out_turned).astype(BF16)
    d_query, d_key_all, d_value_all = attend_backward(first, query, key_value, d_heads)
    d_key_value_all = jnp.concatenate([d_key_all, d_value_all], -1).reshape(nc, tokens, -1)
    d_key_value = line_scatter(
        lambda j: lax.dynamic_index_in_dim(d_key_value_all, j, 0, keepdims=False),
        "context",
        up=False,
    )
    d_rotated = rotate_back(
        jnp.concatenate([d_query, d_key_value[:, :key_width]], -1).reshape(
            tokens, -1, HEAD_DIMENSION
        ),
        cosine_values,
        sine_values,
    ).reshape(tokens, -1)
    d_qkv = jnp.concatenate([d_rotated, d_key_value[:, key_width:]], -1).astype(BF16)
    d_inputs = dot_nt(d_qkv, qkv_weight) + dot_nt(d_logits, router_weight)
    grad_gain_first = jnp.sum(d_inputs * token_rows * scale1, 0)
    grad_qkv = dot_tn(inputs1, d_qkv)
    small_grads = jnp.concatenate(
        [grad_router, grad_gain_first[:, None], grad_gain_second[:, None]], -1
    )
    small_grads = jnp.pad(small_grads, ((0, 0), (0, 128 - small_grads.shape[1])))
    sum_rows = scatter_rows(jnp.concatenate([grad_qkv, small_grads], -1))
    sum_qkv = sum_rows[:, :qkv_width]
    sum_router = sum_rows[:, qkv_width : qkv_width + expert_total]
    sum_gain_first = sum_rows[:, qkv_width + expert_total]
    sum_gain_second = sum_rows[:, qkv_width + expert_total + 1]
    scaled1 = d_inputs * gain_first
    d_input_rows = (
        d_hidden
        + scale1 * scaled1
        - token_rows
        * (scale1 * scale1 * scale1)
        * jnp.mean(scaled1 * token_rows, -1, keepdims=True)
    ).astype(BF16)
    return (
        layer_result[None],
        d_input_rows[None],
        sum_gain_first,
        sum_qkv,
        sum_out,
        sum_router,
        sum_gain_second,
        sum_gate_up,
        sum_down,
    )


def local_fused(
    layer_input,
    gain_attn,
    query_key_value_weight,
    w_out,
    w_router,
    gain_ffn,
    w_gate_up,
    w_down,
    routes,
    d_out,
):
    tokens = layer_input.shape[1]
    model_width = layer_input.shape[2]
    ne, nc, nd = sizes = tuple(lax.axis_size(a) for a in ("expert", "context", "dp"))
    expert_total = EXP_DEV * ne
    ff = w_down.shape[1]
    me = lax.axis_index("expert")
    first_row = lax.axis_index("context") * tokens
    query_width = QUERY_HEADS * HEAD_DIMENSION
    key_width = KEY_VALUE_HEADS * HEAD_DIMENSION
    qkv_width = query_width + 2 * key_width

    small = jnp.concatenate([w_router, gain_attn[:, None], gain_ffn[:, None]], -1)
    small = jnp.pad(small, ((0, 0), (0, SMALL - small.shape[1])))
    cosine_values, sine_values = rope_tables(first_row + jnp.arange(tokens), HEAD_DIMENSION)
    sign = jnp.where(jnp.arange(HEAD_DIMENSION) < HEAD_DIMENSION // 2, -1.0, 1.0)
    (
        q_all,
        o_all,
        cotangent_all,
        gate_all,
        inputs1,
        query,
        key_value,
        heads,
        hidden,
        expert_in,
    ) = front(
        layer_input[0],
        jnp.concatenate([query_key_value_weight, small], -1),
        w_out.T,
        d_out[0],
        cosine_values,
        sine_values * sign,
        routes[0],
        sizes,
    )
    q_all = q_all.reshape(model_width, -1)
    out_turned = o_all.reshape(model_width, -1)
    cotangent_all = cotangent_all.reshape(ne * tokens, -1)
    key_value = key_value.reshape(nc * tokens, -1)
    qkv_weight = q_all[:, :qkv_width]
    router_weight = q_all[:, qkv_width : qkv_width + expert_total]
    gains = q_all[:, qkv_width + expert_total : qkv_width + expert_total + 2].T.astype(F32)
    gain_first, gain_second = gains[0], gains[1]
    token_rows = layer_input[0].astype(F32)
    scale1 = lax.rsqrt(jnp.mean(token_rows * token_rows, -1, keepdims=True) + EPSILON)
    scale2 = lax.rsqrt(jnp.mean(hidden * hidden, -1, keepdims=True) + EPSILON)
    first = first_row.astype(jnp.int32).reshape(1)
    gate_local = lax.dynamic_slice_in_dim(gate_all, me * EXP_DEV, EXP_DEV, 1)
    gate_local = jnp.swapaxes(gate_local, 0, 1).reshape(EXP_DEV, ne * tokens)
    gates = gate_all[0, :expert_total].T

    rows_all = plane_gather(expert_in)
    gate_up = jnp.einsum("td,edf->etf", rows_all, w_gate_up, preferred_element_type=F32)
    gate_part, up_part = gate_up[..., :ff], gate_up[..., ff:]
    sigma = jax.nn.sigmoid(gate_part)
    silu = gate_part * sigma
    act = silu * up_part
    gate_column = gate_local[:, :, None]
    act_gated = (act * gate_column).astype(BF16)
    partial_out = jnp.einsum("etf,efd->td", act_gated, w_down, preferred_element_type=F32)
    mixture = plane_scatter(partial_out.astype(BF16), tokens)
    layer_result = (hidden + mixture).astype(BF16)

    d_act_raw = jnp.einsum("td,efd->etf", cotangent_all, w_down, preferred_element_type=F32)
    d_gates_local = jnp.sum(d_act_raw * act, -1)
    d_act = d_act_raw * gate_column
    d_gate_part = d_act * up_part * sigma * (1.0 + gate_part * (1.0 - sigma))
    d_up_part = d_act * silu
    d_gate_up = jnp.concatenate([d_gate_part, d_up_part], -1).astype(BF16)
    d_rows = jnp.einsum("etf,edf->td", d_gate_up, w_gate_up, preferred_element_type=F32)
    grad_down = jnp.einsum("td,etf->edf", cotangent_all, act_gated, preferred_element_type=F32)
    grad_gate_up = jnp.einsum("td,etf->edf", rows_all, d_gate_up, preferred_element_type=F32)

    d_expert_in = plane_scatter(d_rows.astype(BF16), tokens)
    d_gate_blocks = d_gates_local.reshape(EXP_DEV, ne, tokens)
    d_gates = jnp.zeros((expert_total, tokens), F32)
    for r in range(ne):
        arrived = d_gate_blocks[:, r]
        if r:
            arrived = exchange(arrived, "expert", r)
        d_gates = lax.dynamic_update_slice(d_gates, arrived, ((me ^ r) * EXP_DEV, 0))
    d_gates = d_gates.T
    d_logits = (gates * (d_gates - jnp.sum(gates * d_gates, -1, keepdims=True))).astype(BF16)
    grad_router = dot_tn(inputs1, d_logits)

    core = lax.axis_index("dp")
    part = model_width // (nc * nd)

    def scatter_experts(grad):
        blocks = grad.reshape(EXP_DEV, nc, nd, part, -1)
        mine = cube_scatter(
            [lax.dynamic_index_in_dim(blocks, core ^ r, 2, keepdims=False) for r in range(nd)],
            "dp",
            axis_masks("dp"),
        )
        return line_scatter(
            lambda j: lax.dynamic_index_in_dim(mine, j, 1, keepdims=False), "context"
        )

    sum_gate_up = scatter_experts(grad_gate_up)
    sum_down = jnp.swapaxes(scatter_experts(grad_down), 1, 2)

    cotangent = d_out[0].astype(F32)
    scaled2 = d_expert_in * gain_second
    d_hidden = (
        cotangent
        + scale2 * scaled2
        - hidden * (scale2 * scale2 * scale2) * jnp.mean(scaled2 * hidden, -1, keepdims=True)
    )
    grad_gain_second = jnp.sum(d_expert_in * hidden * scale2, 0)
    d_attn = d_hidden.astype(BF16)
    grad_out_turned = dot_tn(d_attn, heads)
    sum_out = scatter_rows(grad_out_turned).T
    d_heads = dot_nn(d_attn, out_turned).astype(BF16)
    d_query, d_key_all, d_value_all = attend_backward(first, query, key_value, d_heads)
    d_key_value_all = jnp.concatenate([d_key_all, d_value_all], -1).reshape(nc, tokens, -1)
    d_key_value = line_scatter(
        lambda j: lax.dynamic_index_in_dim(d_key_value_all, j, 0, keepdims=False),
        "context",
        up=False,
    )
    d_rotated = rotate_back(
        jnp.concatenate([d_query, d_key_value[:, :key_width]], -1).reshape(
            tokens, -1, HEAD_DIMENSION
        ),
        cosine_values,
        sine_values,
    ).reshape(tokens, -1)
    d_qkv = jnp.concatenate([d_rotated, d_key_value[:, key_width:]], -1).astype(BF16)
    d_inputs = dot_nt(d_qkv, qkv_weight) + dot_nt(d_logits, router_weight)
    grad_gain_first = jnp.sum(d_inputs * token_rows * scale1, 0)
    grad_qkv = dot_tn(inputs1, d_qkv)
    small_grads = jnp.concatenate(
        [grad_router, grad_gain_first[:, None], grad_gain_second[:, None]], -1
    )
    small_grads = jnp.pad(small_grads, ((0, 0), (0, SMALL - small_grads.shape[1])))
    sum_rows = scatter_rows(jnp.concatenate([grad_qkv, small_grads], -1))
    sum_qkv = sum_rows[:, :qkv_width]
    sum_router = sum_rows[:, qkv_width : qkv_width + expert_total]
    sum_gain_first = sum_rows[:, qkv_width + expert_total]
    sum_gain_second = sum_rows[:, qkv_width + expert_total + 1]
    scaled1 = d_inputs * gain_first
    d_input_rows = (
        d_hidden
        + scale1 * scaled1
        - token_rows
        * (scale1 * scale1 * scale1)
        * jnp.mean(scaled1 * token_rows, -1, keepdims=True)
    ).astype(BF16)
    return (
        layer_result[None],
        d_input_rows[None],
        sum_gain_first,
        sum_qkv,
        sum_out,
        sum_router,
        sum_gain_second,
        sum_gate_up,
        sum_down,
    )


def solution(mesh):
    in_specs = (
        P(("expert", "dp"), "context", None),
        P(("expert", "context", "dp")),
        P(("expert", "context", "dp"), None),
        P(None, ("expert", "context", "dp")),
        P(("expert", "context", "dp"), None),
        P(("expert", "context", "dp")),
        P("expert", None, None),
        P("expert", None, None),
        P(("expert", "dp"), "context", None),
        P(("expert", "dp"), "context", None),
    )
    out_specs = (
        P(("expert", "dp"), "context", None),
        P(("expert", "dp"), "context", None),
        P(("expert", "context", "dp")),
        P(("expert", "context", "dp"), None),
        P(None, ("expert", "context", "dp")),
        P(("expert", "context", "dp"), None),
        P(("expert", "context", "dp")),
        P("expert", ("context", "dp"), None),
        P("expert", None, ("context", "dp")),
    )
    sizes = tuple(mesh.shape[a] for a in ("expert", "context", "dp"))
    local = local_fused if sizes[0] == 4 and sizes[2] == 2 else local_plain
    return jax.shard_map(local, mesh=mesh, in_specs=in_specs, out_specs=out_specs, check_vma=False)
```

```python
import functools
import math

import jax
import jax.numpy as jnp
from jax import lax
from jax.experimental import pallas as pl
from jax.experimental.pallas import tpu as pltpu
from jax.sharding import PartitionSpec as P

QUERY_HEADS = 12
KEY_VALUE_HEADS = 2
HEAD_DIMENSION = 128
TOP = 4
EXP_DEV = 2

EPSILON = 1e-06
ROPE_BASE = 10000.0
MASKED = -1e30

F32 = jnp.float32
BF16 = jnp.bfloat16


def rope_tables(positions, width):
    halfway = width // 2
    fraction = jnp.arange(halfway, dtype=jnp.float32) * (2.0 / width)
    frequency = jnp.exp(-math.log(ROPE_BASE) * fraction)
    angles = positions.astype(jnp.float32)[:, None] * frequency[None, :]
    cosine_values = jnp.cos(angles)
    sine_values = jnp.sin(angles)
    return (
        jnp.concatenate([cosine_values, cosine_values], -1),
        jnp.concatenate([sine_values, sine_values], -1),
    )


def rotate_half(values, cosine_values, sine_values):
    halfway = values.shape[-1] // 2
    turned = jnp.concatenate([-values[..., halfway:], values[..., :halfway]], -1)
    return values * cosine_values[:, None, :] + turned * sine_values[:, None, :]


def rotate_back(grads, cosine_values, sine_values):
    halfway = grads.shape[-1] // 2
    scaled = grads * sine_values[:, None, :]
    turned = jnp.concatenate([scaled[..., halfway:], -scaled[..., :halfway]], -1)
    return grads * cosine_values[:, None, :] + turned


def dot_nt(a, b):
    return lax.dot_general(a, b, (((1,), (1,)), ((), ())), preferred_element_type=F32)


def dot_tn(a, b):
    return lax.dot_general(a, b, (((0,), (0,)), ((), ())), preferred_element_type=F32)


def dot_nn(a, b):
    return jnp.dot(a, b, preferred_element_type=F32)


def masked_probs(first_row, query, key):
    scores = dot_nt(query, key) * (HEAD_DIMENSION**-0.5)
    rows = first_row + lax.broadcasted_iota(jnp.int32, scores.shape, 0)
    columns = lax.broadcasted_iota(jnp.int32, scores.shape, 1)
    scores = jnp.where(columns <= rows, scores, MASKED)
    expd = jnp.exp(scores - jnp.max(scores, axis=-1, keepdims=True))
    return expd / jnp.sum(expd, axis=-1, keepdims=True)


def attend_forward_kernel(first_ref, query_ref, key_ref, value_ref, heads_ref):
    probs = masked_probs(first_ref[0], query_ref[...], key_ref[...])
    heads_ref[...] = dot_nn(probs.astype(BF16), value_ref[...]).astype(BF16)


def attend_forward(first_row, query, key_value):
    tokens, width = query.shape
    length = key_value.shape[0]
    group = QUERY_HEADS // KEY_VALUE_HEADS
    size = HEAD_DIMENSION
    return pl.pallas_call(
        attend_forward_kernel,
        grid_spec=pltpu.PrefetchScalarGridSpec(
            num_scalar_prefetch=1,
            grid=(QUERY_HEADS,),
            in_specs=[
                pl.BlockSpec((tokens, size), lambda h, s: (0, h)),
                pl.BlockSpec((length, size), lambda h, s: (0, h // group)),
                pl.BlockSpec((length, size), lambda h, s: (0, KEY_VALUE_HEADS + h // group)),
            ],
            out_specs=pl.BlockSpec((tokens, size), lambda h, s: (0, h)),
        ),
        out_shape=jax.ShapeDtypeStruct((tokens, width), BF16),
        compiler_params=pltpu.CompilerParams(vmem_limit_bytes=32 * 1024 * 1024),
        cost_estimate=pl.CostEstimate(
            flops=4 * tokens * length * width, bytes_accessed=4 * tokens * width, transcendentals=0
        ),
    )(first_row, query, key_value, key_value)


def attend_backward_kernel(
    first_ref, query_ref, key_ref, value_ref, grad_ref, d_query_ref, d_key_ref, d_value_ref
):
    query, key, value, grad = query_ref[...], key_ref[...], value_ref[...], grad_ref[...]
    probs = masked_probs(first_ref[0], query, key)
    d_probs = dot_nt(grad, value)
    inner = jnp.sum(probs * d_probs, axis=-1, keepdims=True)
    d_raw = (probs * (d_probs - inner) * (HEAD_DIMENSION**-0.5)).astype(BF16)
    d_query_ref[...] = dot_nn(d_raw, key)
    d_key = dot_tn(d_raw, query)
    d_value = dot_tn(probs.astype(BF16), grad)

    @pl.when(pl.program_id(1) == 0)
    def _():
        d_key_ref[...] = d_key
        d_value_ref[...] = d_value

    @pl.when(pl.program_id(1) > 0)
    def _():
        d_key_ref[...] += d_key
        d_value_ref[...] += d_value


def attend_backward(first_row, query, key_value, grad):
    tokens, width = query.shape
    length = key_value.shape[0]
    group = QUERY_HEADS // KEY_VALUE_HEADS
    size = HEAD_DIMENSION
    row_spec = pl.BlockSpec((tokens, size), lambda j, g, s: (0, j * group + g))
    return pl.pallas_call(
        attend_backward_kernel,
        grid_spec=pltpu.PrefetchScalarGridSpec(
            num_scalar_prefetch=1,
            grid=(KEY_VALUE_HEADS, group),
            in_specs=[
                row_spec,
                pl.BlockSpec((length, size), lambda j, g, s: (0, j)),
                pl.BlockSpec((length, size), lambda j, g, s: (0, KEY_VALUE_HEADS + j)),
                row_spec,
            ],
            out_specs=[
                row_spec,
                pl.BlockSpec((length, size), lambda j, g, s: (0, j)),
                pl.BlockSpec((length, size), lambda j, g, s: (0, j)),
            ],
        ),
        out_shape=[
            jax.ShapeDtypeStruct((tokens, width), F32),
            jax.ShapeDtypeStruct((length, KEY_VALUE_HEADS * size), F32),
            jax.ShapeDtypeStruct((length, KEY_VALUE_HEADS * size), F32),
        ],
        compiler_params=pltpu.CompilerParams(vmem_limit_bytes=32 * 1024 * 1024),
        cost_estimate=pl.CostEstimate(
            flops=10 * tokens * length * width, bytes_accessed=8 * tokens * width, transcendentals=0
        ),
    )(first_row, query, key_value, key_value, grad)


def exchange(values, axis, mask):
    size = lax.axis_size(axis)
    return lax.ppermute(values, axis, [(i, i ^ mask) for i in range(size)])


def axis_masks(axis):
    size = lax.axis_size(axis)
    masks, bit = [], 1
    while bit < size:
        masks.append(bit)
        bit *= 2
    return masks


def cube_gather(values, axis, masks):
    held = {0: values}
    for mask in masks:
        for r, block in list(held.items()):
            held[r ^ mask] = exchange(block, axis, mask)
    return [held[r] for r in range(lax.axis_size(axis))]


def cube_scatter(blocks, axis, masks):
    held = dict(enumerate(blocks))
    for mask in masks:
        kept = {}
        for r in list(held):
            if not r & mask:
                arrived = exchange(held[r ^ mask].astype(BF16), axis, mask)
                kept[r] = held[r].astype(F32) + arrived.astype(F32)
        held = kept
    return held[0]


def line_steps(values, axis, up):
    size = lax.axis_size(axis)
    pairs = [(i, i + 1) if up else (i + 1, i) for i in range(size - 1)]
    return lax.ppermute(values, axis, pairs)


def line_gather(values, axis, both=True):
    size = lax.axis_size(axis)
    me = lax.axis_index(axis)
    result = jnp.zeros((size + 1,) + values.shape, values.dtype)
    result = lax.dynamic_update_index_in_dim(result, values, me, 0)
    up = down = values
    for step in range(1, size):
        up = line_steps(up, axis, True)
        result = lax.dynamic_update_index_in_dim(
            result, up, jnp.where(me - step >= 0, me - step, size), 0
        )
        if both:
            down = line_steps(down, axis, False)
            result = lax.dynamic_update_index_in_dim(result, down, jnp.minimum(me + step, size), 0)
    return result[:size]


def line_scatter(take, axis, up=True, down=True):
    size = lax.axis_size(axis)
    me = lax.axis_index(axis)
    total = take(me).astype(F32)
    for active, sign in ((up, 1), (down, -1)):
        if not active:
            continue
        arrived = None
        for step in range(1, size):
            block = take((me + sign * (size - step)) % size).astype(F32)
            if arrived is not None:
                block = block + arrived.astype(F32)
            arrived = line_steps(block.astype(BF16), axis, sign > 0)
        total = total + arrived.astype(F32)
    return total


def gather_rows(shard):
    ne, nc, nd = (lax.axis_size(a) for a in ("expert", "context", "dp"))
    rows, width = shard.shape
    lines = line_gather(shard, "context")
    masks = axis_masks("expert")
    half = width // 256 * 128
    parts = [lines[..., :half], lines[..., half:]]
    me = lax.axis_index("expert")
    result = jnp.zeros((ne, nc, rows, width), shard.dtype)
    for start, part, order in ((0, parts[0], masks), (half, parts[1], masks[::-1])):
        for r, block in enumerate(cube_gather(part, "expert", order)):
            result = lax.dynamic_update_slice(result, block[None], (me ^ r, 0, 0, start))
    core = lax.axis_index("dp")
    whole = jnp.zeros((ne, nc, nd, rows, width), shard.dtype)
    for r, block in enumerate(cube_gather(result, "dp", axis_masks("dp"))):
        whole = lax.dynamic_update_slice(whole, block[:, :, None], (0, 0, core ^ r, 0, 0))
    return whole.reshape(-1, width)


def scatter_rows(grad):
    ne, nc, nd = (lax.axis_size(a) for a in ("expert", "context", "dp"))
    width = grad.shape[-1]
    rows = grad.shape[0] // (ne * nc * nd)
    blocks = grad.reshape(ne, nc, nd, rows, width)
    core, me = lax.axis_index("dp"), lax.axis_index("expert")
    mine = cube_scatter(
        [
            lax.dynamic_index_in_dim(blocks, core ^ r, 2, keepdims=False)
            for r in range(nd)
        ],
        "dp",
        axis_masks("dp"),
    )
    masks = axis_masks("expert")
    half = width // 256 * 128
    sums = []
    for part, order in ((mine[..., :half], masks), (mine[..., half:], masks[::-1])):
        sums.append(
            cube_scatter(
                [lax.dynamic_index_in_dim(part, me ^ r, 0, keepdims=False) for r in range(ne)],
                "expert",
                order,
            )
        )
    lines = jnp.concatenate(sums, -1)
    return line_scatter(
        lambda j: lax.dynamic_index_in_dim(lines, j, 0, keepdims=False), "context"
    )


def plane_gather(rows):
    masks = axis_masks("expert")
    half = rows.shape[-1] // 2
    left = cube_gather(rows[:, :half], "expert", masks)
    right = cube_gather(rows[:, half:], "expert", masks[::-1])
    return jnp.concatenate([jnp.concatenate(p, -1) for p in zip(left, right)], 0)


def plane_scatter(partial, tokens):
    masks = axis_masks("expert")
    size = lax.axis_size("expert")
    half = partial.shape[-1] // 2
    blocks = partial.reshape(size, tokens, -1)
    left = cube_scatter([blocks[r, :, :half] for r in range(size)], "expert", masks)
    right = cube_scatter([blocks[r, :, half:] for r in range(size)], "expert", masks[::-1])
    return jnp.concatenate([left, right], -1)


MESH = pl.DeviceIdType.MESH
MIB = 1024 * 1024
SMALL = 128
GATE_ROWS = 16


def flip(index, mask):
    bit = 1
    while bit <= mask:
        if mask & bit:
            index = index + bit - 2 * bit * lax.rem(lax.div(index, bit), 2)
        bit *= 2
    return index


class Wire:
    def __init__(self, sends, recvs):
        self.sends, self.recvs = sends, recvs
        self.n_sends = self.n_recvs = 0
        self.open = []

    def slots(self, count):
        first = self.n_recvs
        self.n_recvs += count
        return first

    def start(self, src, dst, recv, device, when=None):
        copy = pltpu.make_async_remote_copy(
            src_ref=src,
            dst_ref=dst,
            send_sem=self.sends.at[self.n_sends],
            recv_sem=self.recvs.at[recv],
            device_id=device,
            device_id_type=MESH,
        )
        self.n_sends += 1
        guard(when, copy.start)
        self.open.append((when, copy))

    def arrived(self, dst, recv, device):
        pltpu.make_async_remote_copy(
            src_ref=dst,
            dst_ref=dst,
            send_sem=self.sends.at[0],
            recv_sem=self.recvs.at[recv],
            device_id=device,
            device_id_type=MESH,
        ).wait_recv()

    def finish(self):
        for when, copy in self.open:
            guard(when, copy.wait_send)
        self.open = []


def guard(when, action):
    if when is None:
        action()
    else:
        pl.when(when)(action)


def greet(targets):
    barrier = pltpu.get_barrier_semaphore()
    for device, when in targets:
        guard(
            when,
            lambda device=device: pl.semaphore_signal(
                barrier, inc=1, device_id=device, device_id_type=MESH
            ),
        )
    count = sum(1 if when is None else when.astype(jnp.int32) for _, when in targets)
    pl.semaphore_wait(barrier, count)


def plane_ids(e):
    return {m: {"expert": flip(e, m)} for m in (1, 2, 3)}


class RowsGather:
    def __init__(self, wire, ref, e, z, c, nc, half):
        self.wire, self.ref, self.e, self.z, self.c, self.nc = wire, ref, e, z, c, nc
        self.cols = (pl.ds(0, half), pl.ds(half, ref.shape[-1] - half))
        self.line = wire.slots(nc)
        self.plane = wire.slots(nc * 6)
        self.core = wire.slots(nc)
        self.ids = plane_ids(e)
        self.steps = []
        for k in range(nc):
            self.steps.append(functools.partial(self.spread, k))
            if k:
                self.steps.append(functools.partial(self.forward, k - 1))
            if k > 1:
                self.steps.append(functools.partial(self.share, k - 2))
        self.steps.append(functools.partial(self.forward, nc - 1))
        self.steps.append(functools.partial(self.share, nc - 2))
        self.steps.append(functools.partial(self.share, nc - 1))
        self.steps.append(self.complete)

    def at(self, r, zs, half):
        return self.ref.at[flip(self.e, r), zs, self.c, :, self.cols[half]]

    def slot(self, k, r, half):
        return self.plane + k * 6 + (r - 1) * 2 + half

    def spread(self, k):
        wire, z, nc = self.wire, self.z, self.nc
        zs = flip(z, k)
        whole = self.ref.at[self.e, zs, self.c]
        if k:
            wire.arrived(whole, self.line + zs, {"context": zs})
        wire.start(
            whole, whole, self.line + zs, {"context": z + 1}, when=(zs <= z) & (z < nc - 1)
        )
        wire.start(whole, whole, self.line + zs, {"context": z - 1}, when=(zs >= z) & (z > 0))
        for half, mask in ((0, 1), (1, 2), (1, 1), (0, 2)):
            part = self.at(0, zs, half)
            wire.start(part, part, self.slot(k, mask, half), self.ids[mask])

    def forward(self, k):
        zs = flip(self.z, k)
        for half, mask in ((0, 1), (1, 2)):
            part = self.at(mask, zs, half)
            self.wire.arrived(part, self.slot(k, mask, half), self.ids[mask])
            self.wire.start(part, part, self.slot(k, 3, half), self.ids[3 - mask])

    def share(self, k):
        zs = flip(self.z, k)
        for r, half in ((1, 1), (2, 0), (3, 0), (3, 1)):
            self.wire.arrived(self.at(r, zs, half), self.slot(k, r, half), self.ids[r])
        part = self.ref.at[:, zs, self.c]
        self.wire.start(part, part, self.core + k, {"dp": 1 - self.c})

    def complete(self):
        for k in range(self.nc):
            zs = flip(self.z, k)
            self.wire.arrived(self.ref.at[:, zs, 1 - self.c], self.core + k, {"dp": 1 - self.c})

    def step(self):
        if self.steps:
            self.steps.pop(0)()

    def run(self):
        while self.steps:
            self.step()


class PlaneGather:
    def __init__(self, wire, ref, e):
        self.wire, self.ref = wire, ref
        self.half = ref.shape[-1] // 2
        self.ids = plane_ids(e)
        self.first = wire.slots(6)
        self.steps = [self.spread, self.forward, self.complete]

    def at(self, r, half):
        return self.ref.at[r, :, pl.ds(half * self.half, self.half)]

    def slot(self, r, half):
        return self.first + (r - 1) * 2 + half

    def spread(self):
        for half, mask in ((0, 1), (1, 2), (1, 1), (0, 2)):
            self.wire.start(
                self.at(0, half), self.at(mask, half), self.slot(mask, half), self.ids[mask]
            )

    def forward(self):
        for half, mask in ((0, 1), (1, 2)):
            self.wire.arrived(self.at(mask, half), self.slot(mask, half), self.ids[mask])
            self.wire.start(
                self.at(mask, half), self.at(3, half), self.slot(3, half), self.ids[3 - mask]
            )

    def near(self, r):
        half = 1 if r == 1 else 0
        self.wire.arrived(self.at(r, half), self.slot(r, half), self.ids[r])

    def far(self):
        for half in (0, 1):
            self.wire.arrived(self.at(3, half), self.slot(3, half), self.ids[3])

    def complete(self):
        self.near(1)
        self.near(2)
        self.far()

    def step(self):
        if self.steps:
            self.steps.pop(0)()

    def run(self):
        while self.steps:
            self.step()


def swap_halves(values):
    return pltpu.roll(values, HEAD_DIMENSION // 2, 1)


def front_kernel(
    nc,
    experts,
    x_ref,
    q_shard,
    o_shard,
    cot_ref,
    cos_ref,
    sin_ref,
    routes_ref,
    q_all,
    o_all,
    cot_all,
    gate_all,
    inputs_ref,
    query_ref,
    kv_ref,
    heads_ref,
    hidden_ref,
    expert_in_ref,
    qkv_scr,
    sends,
    recvs,
):
    e, z, c = (lax.axis_index(a) for a in ("expert", "context", "dp"))
    size = HEAD_DIMENSION
    tokens, width = x_ref.shape
    query_width = QUERY_HEADS * size
    kv_width = 2 * KEY_VALUE_HEADS * size
    wire = Wire(sends, recvs)
    ids = plane_ids(e)
    greet(
        [(ids[m], None) for m in (1, 2, 3)]
        + [({"dp": 1 - c}, None), ({"context": z + 1}, z < nc - 1), ({"context": z - 1}, z > 0)]
    )
    q_all[e, z, c] = q_shard[...]
    o_all[e, z, c] = o_shard[...]
    cot_all[0] = cot_ref[...]

    gather_q = RowsGather(wire, q_all, e, z, c, nc, 1024)
    gather_o = RowsGather(wire, o_all, e, z, c, nc, 768)
    gather_cot = PlaneGather(wire, cot_all, e)
    gather_q.run()
    gather_o.step()

    small = q_all[:, :, :, :, pl.ds(query_width + kv_width, SMALL)].reshape(width, SMALL)
    small = jnp.transpose(small.astype(F32))
    gain_first, gain_second = small[experts : experts + 1], small[experts + 1 : experts + 2]
    rows = x_ref[...].astype(F32)
    scale1 = lax.rsqrt(jnp.mean(rows * rows, -1, keepdims=True) + EPSILON)
    inputs_ref[...] = (rows * scale1 * gain_first).astype(BF16)

    def project(first, count):
        weight = q_all[:, :, :, :, pl.ds(first, count)].reshape(width, count)
        qkv_scr[:, pl.ds(first, count)] = dot_nn(inputs_ref[...], weight)

    project(query_width, kv_width)

    def turned(column):
        head = qkv_scr[:, pl.ds(column, size)]
        return (head * cos_ref[...] + swap_halves(head) * sin_ref[...]).astype(BF16)

    for j in range(KEY_VALUE_HEADS):
        kv_ref[z, :, pl.ds(j * size, size)] = turned(query_width + j * size)
    values = pl.ds(kv_width // 2, kv_width // 2)
    kv_ref[z, :, values] = qkv_scr[:, pl.ds(query_width + kv_width // 2, kv_width // 2)].astype(
        BF16
    )
    line = wire.slots(nc)
    wire.start(kv_ref.at[z], kv_ref.at[z], line, {"context": z + 1}, when=z < nc - 1)
    for later in range(1, nc):

        def clear(later=later):
            kv_ref[z + later] = jnp.zeros(kv_ref.shape[1:], BF16)

        pl.when(z + later < nc)(clear)
    gather_o.step()

    @pl.loop(0, query_width // 256)
    def _(n):
        project(pl.multiple_of(n * 256, 256), 256)

    gather_o.step()
    project(query_width + kv_width, SMALL)
    gather_o.step()

    @pl.loop(0, QUERY_HEADS)
    def _(h):
        column = pl.multiple_of(h * size, size)
        query_ref[:, pl.ds(column, size)] = turned(column)

    gather_o.step()

    logits = qkv_scr[:, pl.ds(query_width + kv_width, SMALL)]
    lanes = lax.broadcasted_iota(jnp.int32, logits.shape, 1)
    named = lanes == routes_ref[:, 0:1]
    for k in range(1, TOP):
        named = named | (lanes == routes_ref[:, k : k + 1])
    logits = jnp.where(named, logits, MASKED)
    expd = jnp.exp(logits - jnp.max(logits, -1, keepdims=True))
    gates = expd / jnp.sum(expd, -1, keepdims=True)
    gate_all[0] = jnp.transpose(gates)[:GATE_ROWS]
    gate_slot = wire.slots(3)
    for r in (1, 2, 3):
        wire.start(gate_all.at[0], gate_all.at[r], gate_slot + r - 1, ids[r])

    gather_o.step()
    for step in range(1, nc):

        def pass_on(step=step):
            block = kv_ref.at[z - step]
            wire.arrived(block, line + step - 1, {"context": z - 1})

        pl.when(z >= step)(pass_on)
        wire.start(
            kv_ref.at[z - step],
            kv_ref.at[z - step],
            line + step,
            {"context": z + 1},
            when=(z >= step) & (z < nc - 1),
        )
        gather_o.step()
    gather_o.step()
    gather_o.step()

    length = nc * tokens
    group = QUERY_HEADS // KEY_VALUE_HEADS
    group_steps = 3
    for first in range(0, QUERY_HEADS, group_steps):
        j = first // group
        key = kv_ref[:, :, pl.ds(j * size, size)].reshape(length, size)
        value = kv_ref[:, :, pl.ds(kv_width // 2 + j * size, size)].reshape(length, size)

        @pl.loop(first, first + group_steps)
        def _(h):
            column = pl.multiple_of(h * size, size)
            scores = dot_nt(query_ref[:, pl.ds(column, size)], key) * (size**-0.5)
            row = z * tokens + lax.broadcasted_iota(jnp.int32, scores.shape, 0)
            place = lax.broadcasted_iota(jnp.int32, scores.shape, 1)
            scores = jnp.where(place <= row, scores, MASKED)
            expd = jnp.exp(scores - jnp.max(scores, -1, keepdims=True))
            total = jnp.sum(expd, -1, keepdims=True)
            mixed = dot_nn(expd.astype(BF16), value) / total
            heads_ref[:, pl.ds(column, size)] = mixed.astype(BF16)

        gather_o.step()
        gather_o.step()
        if first == 0:
            gather_o.run()
            gather_cot.step()
        else:
            gather_cot.step()

    gather_o.run()
    part = width // q_all.shape[0]
    for block in range(q_all.shape[0]):
        weight = o_all[block].reshape(part, width)
        columns = pl.ds(block * part, part)
        hidden_ref[:, columns] = x_ref[:, columns].astype(F32) + dot_nt(heads_ref[...], weight)
    hidden = hidden_ref[...]
    scale2 = lax.rsqrt(jnp.mean(hidden * hidden, -1, keepdims=True) + EPSILON)
    expert_in_ref[...] = (hidden * scale2 * gain_second).astype(BF16)
    gather_cot.run()
    for r in (1, 2, 3):
        wire.arrived(gate_all.at[r], gate_slot + r - 1, ids[r])
    wire.finish()


def front(x, q_shard, o_shard, cot, cosine, sine, routes, sizes):
    ne, nc, nd = sizes
    tokens, width = x.shape
    rows, q_width = q_shard.shape
    shapes = [
        ((ne, nc, nd, rows, q_width), BF16),
        ((ne, nc, nd, rows, width), BF16),
        ((ne, tokens, width), BF16),
        ((ne, GATE_ROWS, tokens), F32),
        ((tokens, width), BF16),
        ((tokens, QUERY_HEADS * HEAD_DIMENSION), BF16),
        ((nc, tokens, 2 * KEY_VALUE_HEADS * HEAD_DIMENSION), BF16),
        ((tokens, QUERY_HEADS * HEAD_DIMENSION), BF16),
        ((tokens, width), F32),
        ((tokens, width), BF16),
    ]
    copies = 128
    return pl.pallas_call(
        functools.partial(front_kernel, nc, EXP_DEV * ne),
        out_shape=[jax.ShapeDtypeStruct(*s) for s in shapes],
        in_specs=[pl.BlockSpec(memory_space=pltpu.VMEM)] * 7,
        out_specs=[pl.BlockSpec(memory_space=pltpu.VMEM)] * len(shapes),
        scratch_shapes=[
            pltpu.VMEM((tokens, q_width), F32),
            pltpu.SemaphoreType.DMA((copies,)),
            pltpu.SemaphoreType.DMA((copies,)),
        ],
        compiler_params=pltpu.CompilerParams(
            collective_id=0, has_side_effects=True, vmem_limit_bytes=56 * MIB
        ),
    )(x, q_shard, o_shard, cot, cosine, sine, routes)


class PlaneScatter:
    def __init__(self, wire, part, land, e):
        self.wire, self.part, self.land = wire, part, land
        self.half = part.shape[-1] // 2
        self.ids = plane_ids(e)
        self.first = wire.slots(6)

    def at(self, r, half):
        return self.part.at[r - 1, :, pl.ds(half * self.half, self.half)]

    def send(self, r, half, mask, slot):
        self.wire.start(self.at(r, half), self.land.at[slot], self.first + slot, self.ids[mask])

    def near(self, r):
        self.send(r, r - 1, r, r - 1)

    def far(self):
        self.send(3, 0, 1, 2)
        self.send(3, 1, 2, 3)

    def relay(self):
        for half, r in ((0, 2), (1, 1)):
            slot = 2 + half
            self.wire.arrived(self.land.at[slot], self.first + slot, self.ids[3 - r])
            part = self.at(r, half)
            part[...] = (part[...].astype(F32) + self.land[slot].astype(F32)).astype(BF16)
            self.send(r, half, r, 4 + half)

    def total(self, own):
        for slot, half, mask in ((0, 0, 1), (1, 1, 2), (4, 0, 2), (5, 1, 1)):
            self.wire.arrived(self.land.at[slot], self.first + slot, self.ids[mask])
            columns = pl.ds(half * self.half, self.half)
            own[:, columns] += self.land[slot].astype(F32)


def experts_kernel(
    x_ref,
    cot_all,
    gates_ref,
    w_gu,
    w_dn,
    mixture_ref,
    d_in_ref,
    d_gate_ref,
    grad_gu,
    grad_dn,
    x_all,
    a_all,
    dgu_all,
    y_part,
    dx_part,
    y_land,
    dx_land,
    dg_lanes,
    dg_part,
    dg_land,
    stage_gu,
    stage_dn,
    sends,
    recvs,
    stage_sems,
):
    e = lax.axis_index("expert")
    tokens, width = x_ref.shape
    ff = w_dn.shape[1]
    blocks = x_all.shape[0]
    wire = Wire(sends, recvs)
    ids = plane_ids(e)
    greet([(ids[m], None) for m in (1, 2, 3)])
    x_all[0] = x_ref[...]
    gather = PlaneGather(wire, x_all, e)
    scatter_dx = PlaneScatter(wire, dx_part, dx_land, e)
    scatter_y = PlaneScatter(wire, y_part, y_land, e)
    dg_slot = wire.slots(3)
    gather.spread()
    step = 256
    wide = 512

    def block(r):
        dg_lanes[...] = jnp.zeros_like(dg_lanes)
        for i in range(EXP_DEV):

            @pl.loop(0, ff // step)
            def _(f):
                column = pl.multiple_of(f * step, step)
                rows, grads = x_all[r], cot_all[r]
                gate_part = dot_nn(rows, w_gu[i, :, pl.ds(column, step)])
                up_part = dot_nn(rows, w_gu[i, :, pl.ds(ff + column, step)])
                raw = dot_nt(grads, w_dn[i, pl.ds(column, step), :])
                gate = gates_ref[r][:, i : i + 1]
                sigma = jax.nn.sigmoid(gate_part)
                silu = gate_part * sigma
                act = silu * up_part
                lanes = lax.broadcasted_iota(jnp.int32, dg_lanes.shape, 1)
                dg_lanes[...] += jnp.where(
                    lanes == e * EXP_DEV + i, jnp.sum(act * raw, -1, keepdims=True), 0.0
                )
                a_all[r, :, pl.ds(i * ff + column, step)] = (act * gate).astype(BF16)
                d_act = raw * gate
                d_gate_part = d_act * up_part * sigma * (1.0 + gate_part * (1.0 - sigma))
                first = i * 2 * ff + column
                dgu_all[r, :, pl.ds(first, step)] = d_gate_part.astype(BF16)
                dgu_all[r, :, pl.ds(first + ff, step)] = (d_act * silu).astype(BF16)

        @pl.loop(0, width // wide)
        def _(n):
            columns = pl.ds(pl.multiple_of(n * wide, wide), wide)
            d_rows = dot_nt(dgu_all[r, :, pl.ds(0, 2 * ff)], w_gu[0, columns, :])
            d_rows += dot_nt(dgu_all[r, :, pl.ds(2 * ff, 2 * ff)], w_gu[1, columns, :])
            weight = w_dn[:, :, columns].reshape(EXP_DEV * ff, wide)
            out = dot_nn(a_all[r], weight)
            if r == 0:
                d_in_ref[:, columns] = d_rows
                mixture_ref[:, columns] = out
            else:
                dx_part[r - 1, :, columns] = d_rows.astype(BF16)
                y_part[r - 1, :, columns] = out.astype(BF16)

        dg_part[r] = jnp.transpose(dg_lanes[...])[:GATE_ROWS]
        if r:
            wire.start(dg_part.at[r], dg_land.at[r - 1], dg_slot + r - 1, ids[r])

    block(0)
    gather.forward()
    gather.near(1)
    block(1)
    scatter_dx.near(1)
    gather.near(2)
    block(2)
    scatter_dx.near(2)
    gather.far()
    block(3)
    scatter_dx.far()
    scatter_y.near(1)
    scatter_y.near(2)
    scatter_y.far()

    def stage(n, slot):
        rows = pl.ds(pl.multiple_of(n * step, step), step)
        return [
            pltpu.make_async_copy(stage_gu.at[slot], grad_gu.at[:, rows, :], stage_sems.at[0, slot]),
            pltpu.make_async_copy(stage_dn.at[slot], grad_dn.at[:, rows, :], stage_sems.at[1, slot]),
        ]

    def weight_grads(first, last):
        @pl.loop(first, last)
        def _(n):
            slot = lax.rem(n, 2)
            columns = pl.ds(pl.multiple_of(n * step, step), step)

            @pl.when(n >= 2)
            def _():
                for copy in stage(n - 2, slot):
                    copy.wait()

            rows = x_all[:, :, columns].reshape(blocks * tokens, step)
            grads = cot_all[:, :, columns].reshape(blocks * tokens, step)
            for i in range(EXP_DEV):
                d_gate_up = dgu_all[:, :, pl.ds(i * 2 * ff, 2 * ff)].reshape(blocks * tokens, 2 * ff)
                stage_gu[slot, i] = dot_tn(rows, d_gate_up).astype(BF16)
                act = a_all[:, :, pl.ds(i * ff, ff)].reshape(blocks * tokens, ff)
                stage_dn[slot, i] = dot_tn(grads, act).astype(BF16)
            for copy in stage(n, slot):
                copy.start()

    chunks = width // step
    weight_grads(0, chunks // 3)
    scatter_dx.relay()
    weight_grads(chunks // 3, 2 * chunks // 3)
    scatter_y.relay()
    weight_grads(2 * chunks // 3, chunks)
    scatter_dx.total(d_in_ref)
    scatter_y.total(mixture_ref)
    total = dg_part[0]
    for r in (1, 2, 3):
        wire.arrived(dg_land.at[r - 1], dg_slot + r - 1, ids[r])
        total = total + dg_land[r - 1]
    d_gate_ref[...] = total
    for n in (chunks - 2, chunks - 1):
        for copy in stage(n, n % 2):
            copy.wait()
    wire.finish()


def experts(expert_in, cot_all, gates, w_gate_up, w_down):
    blocks, tokens, width = cot_all.shape
    held, ff = w_down.shape[0], w_down.shape[1]
    shapes = [
        ((tokens, width), F32),
        ((tokens, width), F32),
        ((GATE_ROWS, tokens), F32),
        ((held, width, 2 * ff), BF16),
        ((held, width, ff), BF16),
    ]
    copies = 32
    vmem = pl.BlockSpec(memory_space=pltpu.VMEM)
    anywhere = pl.BlockSpec(memory_space=pl.ANY)
    return pl.pallas_call(
        experts_kernel,
        out_shape=[jax.ShapeDtypeStruct(*s) for s in shapes],
        in_specs=[vmem] * 5,
        out_specs=[vmem] * 3 + [anywhere] * 2,
        scratch_shapes=[
            pltpu.VMEM((blocks, tokens, width), BF16),
            pltpu.VMEM((blocks, tokens, held * ff), BF16),
            pltpu.VMEM((blocks, tokens, held * 2 * ff), BF16),
            pltpu.VMEM((blocks - 1, tokens, width), BF16),
            pltpu.VMEM((blocks - 1, tokens, width), BF16),
            pltpu.VMEM((6, tokens, width // 2), BF16),
            pltpu.VMEM((6, tokens, width // 2), BF16),
            pltpu.VMEM((tokens, SMALL), F32),
            pltpu.VMEM((blocks, GATE_ROWS, tokens), F32),
            pltpu.VMEM((blocks - 1, GATE_ROWS, tokens), F32),
            pltpu.VMEM((2, held, 256, 2 * ff), BF16),
            pltpu.VMEM((2, held, 256, ff), BF16),
            pltpu.SemaphoreType.DMA((copies,)),
            pltpu.SemaphoreType.DMA((copies,)),
            pltpu.SemaphoreType.DMA((2, 2)),
        ],
        compiler_params=pltpu.CompilerParams(
            collective_id=1, has_side_effects=True, vmem_limit_bytes=60 * MIB
        ),
    )(expert_in, cot_all, gates, w_gate_up, w_down)


def local_plain(
    layer_input,
    gain_attn,
    query_key_value_weight,
    w_out,
    w_router,
    gain_ffn,
    w_gate_up,
    w_down,
    routes,
    d_out,
):
    tokens = layer_input.shape[1]
    model_width = layer_input.shape[2]
    ne, nc, nd = (lax.axis_size(a) for a in ("expert", "context", "dp"))
    expert_total = EXP_DEV * ne
    ff = w_down.shape[1]
    me = lax.axis_index("expert")
    first_row = lax.axis_index("context") * tokens
    query_width = QUERY_HEADS * HEAD_DIMENSION
    key_width = KEY_VALUE_HEADS * HEAD_DIMENSION
    qkv_width = query_width + 2 * key_width

    small = jnp.concatenate([w_router, gain_attn[:, None], gain_ffn[:, None]], -1)
    small = jnp.pad(small, ((0, 0), (0, 128 - small.shape[1])))
    gathered = gather_rows(jnp.concatenate([query_key_value_weight, small], -1))
    out_turned = gather_rows(w_out.T)
    qkv_weight = gathered[:, :qkv_width]
    router_weight = gathered[:, qkv_width : qkv_width + expert_total]
    gains = gathered[:, qkv_width + expert_total : qkv_width + expert_total + 2].T.astype(F32)
    gain_first, gain_second = gains[0], gains[1]
    cotangent_all = plane_gather(d_out[0])

    token_rows = layer_input[0].astype(F32)
    scale1 = lax.rsqrt(jnp.mean(token_rows * token_rows, -1, keepdims=True) + EPSILON)
    inputs1 = (token_rows * scale1 * gain_first).astype(BF16)
    query_key_value = dot_nn(inputs1, qkv_weight)
    cosine_values, sine_values = rope_tables(first_row + jnp.arange(tokens), HEAD_DIMENSION)
    rotated = rotate_half(
        query_key_value[:, : query_width + key_width].reshape(tokens, -1, HEAD_DIMENSION),
        cosine_values,
        sine_values,
    ).reshape(tokens, -1)
    query = rotated[:, :query_width].astype(BF16)
    key_value_local = jnp.concatenate(
        [rotated[:, query_width:], query_key_value[:, query_width + key_width :]], -1
    ).astype(BF16)
    key_value = line_gather(key_value_local, "context", both=False).reshape(nc * tokens, -1)
    first = first_row.astype(jnp.int32).reshape(1)
    heads = attend_forward(first, query, key_value)

    logits = dot_nn(inputs1, router_weight)
    chosen_ids = routes[0]
    picks = (chosen_ids[:, :, None] == jnp.arange(expert_total)[None, None, :]).astype(F32)
    chosen = jnp.sum(picks * logits[:, None, :], -1)
    gates = jax.nn.softmax(chosen, axis=-1)
    gate_dense = jnp.sum(picks * gates[:, :, None], 1).T
    gate_blocks = cube_gather(gate_dense, "expert", axis_masks("expert"))
    gate_local = jnp.concatenate(
        [lax.dynamic_slice_in_dim(b, me * EXP_DEV, EXP_DEV, 0) for b in gate_blocks], 1
    )

    attn = dot_nt(heads, out_turned)
    hidden = token_rows + attn
    scale2 = lax.rsqrt(jnp.mean(hidden * hidden, -1, keepdims=True) + EPSILON)
    expert_in = (hidden * scale2 * gain_second).astype(BF16)

    rows_all = plane_gather(expert_in)
    gate_up = jnp.einsum("td,edf->etf", rows_all, w_gate_up, preferred_element_type=F32)
    gate_part, up_part = gate_up[..., :ff], gate_up[..., ff:]
    sigma = jax.nn.sigmoid(gate_part)
    silu = gate_part * sigma
    act = silu * up_part
    gate_column = gate_local[:, :, None]
    act_gated = (act * gate_column).astype(BF16)
    partial_out = jnp.einsum("etf,efd->td", act_gated, w_down, preferred_element_type=F32)
    mixture = plane_scatter(partial_out.astype(BF16), tokens)
    layer_result = (hidden + mixture).astype(BF16)

    d_act_raw = jnp.einsum("td,efd->etf", cotangent_all, w_down, preferred_element_type=F32)
    d_gates_local = jnp.sum(d_act_raw * act, -1)
    d_act = d_act_raw * gate_column
    d_gate_part = d_act * up_part * sigma * (1.0 + gate_part * (1.0 - sigma))
    d_up_part = d_act * silu
    d_gate_up = jnp.concatenate([d_gate_part, d_up_part], -1).astype(BF16)
    d_rows = jnp.einsum("etf,edf->td", d_gate_up, w_gate_up, preferred_element_type=F32)
    grad_down = jnp.einsum("td,etf->edf", cotangent_all, act_gated, preferred_element_type=F32)
    grad_gate_up = jnp.einsum("td,etf->edf", rows_all, d_gate_up, preferred_element_type=F32)

    d_expert_in = plane_scatter(d_rows.astype(BF16), tokens)
    d_gate_blocks = d_gates_local.reshape(EXP_DEV, ne, tokens)
    d_gates_dense = jnp.zeros((expert_total, tokens), F32)
    for r in range(ne):
        arrived = d_gate_blocks[:, r]
        if r:
            arrived = exchange(arrived, "expert", r)
        d_gates_dense = lax.dynamic_update_slice(d_gates_dense, arrived, ((me ^ r) * EXP_DEV, 0))
    d_gates = jnp.sum(picks * d_gates_dense.T[:, None, :], -1)
    d_chosen = gates * (d_gates - jnp.sum(gates * d_gates, -1, keepdims=True))
    d_logits = jnp.sum(picks * d_chosen[:, :, None], 1).astype(BF16)
    grad_router = dot_tn(inputs1, d_logits)

    core = lax.axis_index("dp")
    part = model_width // (nc * nd)

    def scatter_experts(grad):
        blocks = grad.reshape(EXP_DEV, nc, nd, part, -1)
        mine = cube_scatter(
            [lax.dynamic_index_in_dim(blocks, core ^ r, 2, keepdims=False) for r in range(nd)],
            "dp",
            axis_masks("dp"),
        )
        return line_scatter(
            lambda j: lax.dynamic_index_in_dim(mine, j, 1, keepdims=False), "context"
        )

    sum_gate_up = scatter_experts(grad_gate_up)
    sum_down = jnp.swapaxes(scatter_experts(grad_down), 1, 2)

    cotangent = d_out[0].astype(F32)
    scaled2 = d_expert_in * gain_second
    d_hidden = (
        cotangent
        + scale2 * scaled2
        - hidden * (scale2 * scale2 * scale2) * jnp.mean(scaled2 * hidden, -1, keepdims=True)
    )
    grad_gain_second = jnp.sum(d_expert_in * hidden * scale2, 0)
    d_attn = d_hidden.astype(BF16)
    grad_out_turned = dot_tn(d_attn, heads)
    sum_out = scatter_rows(grad_out_turned).T
    d_heads = dot_nn(d_attn, out_turned).astype(BF16)
    d_query, d_key_all, d_value_all = attend_backward(first, query, key_value, d_heads)
    d_key_value_all = jnp.concatenate([d_key_all, d_value_all], -1).reshape(nc, tokens, -1)
    d_key_value = line_scatter(
        lambda j: lax.dynamic_index_in_dim(d_key_value_all, j, 0, keepdims=False),
        "context",
        up=False,
    )
    d_rotated = rotate_back(
        jnp.concatenate([d_query, d_key_value[:, :key_width]], -1).reshape(
            tokens, -1, HEAD_DIMENSION
        ),
        cosine_values,
        sine_values,
    ).reshape(tokens, -1)
    d_qkv = jnp.concatenate([d_rotated, d_key_value[:, key_width:]], -1).astype(BF16)
    d_inputs = dot_nt(d_qkv, qkv_weight) + dot_nt(d_logits, router_weight)
    grad_gain_first = jnp.sum(d_inputs * token_rows * scale1, 0)
    grad_qkv = dot_tn(inputs1, d_qkv)
    small_grads = jnp.concatenate(
        [grad_router, grad_gain_first[:, None], grad_gain_second[:, None]], -1
    )
    small_grads = jnp.pad(small_grads, ((0, 0), (0, 128 - small_grads.shape[1])))
    sum_rows = scatter_rows(jnp.concatenate([grad_qkv, small_grads], -1))
    sum_qkv = sum_rows[:, :qkv_width]
    sum_router = sum_rows[:, qkv_width : qkv_width + expert_total]
    sum_gain_first = sum_rows[:, qkv_width + expert_total]
    sum_gain_second = sum_rows[:, qkv_width + expert_total + 1]
    scaled1 = d_inputs * gain_first
    d_input_rows = (
        d_hidden
        + scale1 * scaled1
        - token_rows
        * (scale1 * scale1 * scale1)
        * jnp.mean(scaled1 * token_rows, -1, keepdims=True)
    ).astype(BF16)
    return (
        layer_result[None],
        d_input_rows[None],
        sum_gain_first,
        sum_qkv,
        sum_out,
        sum_router,
        sum_gain_second,
        sum_gate_up,
        sum_down,
    )


def local_fused(
    layer_input,
    gain_attn,
    query_key_value_weight,
    w_out,
    w_router,
    gain_ffn,
    w_gate_up,
    w_down,
    routes,
    d_out,
):
    tokens = layer_input.shape[1]
    model_width = layer_input.shape[2]
    ne, nc, nd = sizes = tuple(lax.axis_size(a) for a in ("expert", "context", "dp"))
    expert_total = EXP_DEV * ne
    me = lax.axis_index("expert")
    first_row = lax.axis_index("context") * tokens
    query_width = QUERY_HEADS * HEAD_DIMENSION
    key_width = KEY_VALUE_HEADS * HEAD_DIMENSION
    qkv_width = query_width + 2 * key_width

    small = jnp.concatenate([w_router, gain_attn[:, None], gain_ffn[:, None]], -1)
    small = jnp.pad(small, ((0, 0), (0, SMALL - small.shape[1])))
    cosine_values, sine_values = rope_tables(first_row + jnp.arange(tokens), HEAD_DIMENSION)
    sign = jnp.where(jnp.arange(HEAD_DIMENSION) < HEAD_DIMENSION // 2, -1.0, 1.0)
    (
        q_all,
        o_all,
        cotangent_all,
        gate_all,
        inputs1,
        query,
        key_value,
        heads,
        hidden,
        expert_in,
    ) = front(
        layer_input[0],
        jnp.concatenate([query_key_value_weight, small], -1),
        w_out.T,
        d_out[0],
        cosine_values,
        sine_values * sign,
        routes[0],
        sizes,
    )
    q_all = q_all.reshape(model_width, -1)
    out_turned = o_all.reshape(model_width, -1)
    key_value = key_value.reshape(nc * tokens, -1)
    qkv_weight = q_all[:, :qkv_width]
    router_weight = q_all[:, qkv_width : qkv_width + expert_total]
    gains = q_all[:, qkv_width + expert_total : qkv_width + expert_total + 2].T.astype(F32)
    gain_first, gain_second = gains[0], gains[1]
    token_rows = layer_input[0].astype(F32)
    scale1 = lax.rsqrt(jnp.mean(token_rows * token_rows, -1, keepdims=True) + EPSILON)
    scale2 = lax.rsqrt(jnp.mean(hidden * hidden, -1, keepdims=True) + EPSILON)
    first = first_row.astype(jnp.int32).reshape(1)
    gate_local = jnp.swapaxes(
        lax.dynamic_slice_in_dim(gate_all, me * EXP_DEV, EXP_DEV, 1), 1, 2
    )
    gates = gate_all[0, :expert_total].T

    mixture, d_expert_in, d_gates, grad_gate_up, grad_down = experts(
        expert_in, cotangent_all, gate_local, w_gate_up, w_down
    )
    layer_result = (hidden + mixture).astype(BF16)
    d_gates = d_gates[:expert_total].T
    d_logits = (gates * (d_gates - jnp.sum(gates * d_gates, -1, keepdims=True))).astype(BF16)
    grad_router = dot_tn(inputs1, d_logits)

    shards = ("context", "dp")
    sum_gate_up = lax.psum_scatter(grad_gate_up, shards, scatter_dimension=1, tiled=True)
    sum_gate_up = sum_gate_up.astype(F32)
    sum_down = lax.psum_scatter(grad_down, shards, scatter_dimension=1, tiled=True)
    sum_down = jnp.swapaxes(sum_down, 1, 2).astype(F32)

    cotangent = d_out[0].astype(F32)
    scaled2 = d_expert_in * gain_second
    d_hidden = (
        cotangent
        + scale2 * scaled2
        - hidden * (scale2 * scale2 * scale2) * jnp.mean(scaled2 * hidden, -1, keepdims=True)
    )
    grad_gain_second = jnp.sum(d_expert_in * hidden * scale2, 0)
    d_attn = d_hidden.astype(BF16)
    grad_out_turned = dot_tn(d_attn, heads)
    sum_out = scatter_rows(grad_out_turned).T
    d_heads = dot_nn(d_attn, out_turned).astype(BF16)
    d_query, d_key_all, d_value_all = attend_backward(first, query, key_value, d_heads)
    d_key_value_all = jnp.concatenate([d_key_all, d_value_all], -1).reshape(nc, tokens, -1)
    d_key_value = line_scatter(
        lambda j: lax.dynamic_index_in_dim(d_key_value_all, j, 0, keepdims=False),
        "context",
        up=False,
    )
    d_rotated = rotate_back(
        jnp.concatenate([d_query, d_key_value[:, :key_width]], -1).reshape(
            tokens, -1, HEAD_DIMENSION
        ),
        cosine_values,
        sine_values,
    ).reshape(tokens, -1)
    d_qkv = jnp.concatenate([d_rotated, d_key_value[:, key_width:]], -1).astype(BF16)
    d_inputs = dot_nt(d_qkv, qkv_weight) + dot_nt(d_logits, router_weight)
    grad_gain_first = jnp.sum(d_inputs * token_rows * scale1, 0)
    grad_qkv = dot_tn(inputs1, d_qkv)
    small_grads = jnp.concatenate(
        [grad_router, grad_gain_first[:, None], grad_gain_second[:, None]], -1
    )
    small_grads = jnp.pad(small_grads, ((0, 0), (0, SMALL - small_grads.shape[1])))
    sum_rows = scatter_rows(jnp.concatenate([grad_qkv, small_grads], -1))
    sum_qkv = sum_rows[:, :qkv_width]
    sum_router = sum_rows[:, qkv_width : qkv_width + expert_total]
    sum_gain_first = sum_rows[:, qkv_width + expert_total]
    sum_gain_second = sum_rows[:, qkv_width + expert_total + 1]
    scaled1 = d_inputs * gain_first
    d_input_rows = (
        d_hidden
        + scale1 * scaled1
        - token_rows
        * (scale1 * scale1 * scale1)
        * jnp.mean(scaled1 * token_rows, -1, keepdims=True)
    ).astype(BF16)
    return (
        layer_result[None],
        d_input_rows[None],
        sum_gain_first,
        sum_qkv,
        sum_out,
        sum_router,
        sum_gain_second,
        sum_gate_up,
        sum_down,
    )


def solution(mesh):
    in_specs = (
        P(("expert", "dp"), "context", None),
        P(("expert", "context", "dp")),
        P(("expert", "context", "dp"), None),
        P(None, ("expert", "context", "dp")),
        P(("expert", "context", "dp"), None),
        P(("expert", "context", "dp")),
        P("expert", None, None),
        P("expert", None, None),
        P(("expert", "dp"), "context", None),
        P(("expert", "dp"), "context", None),
    )
    out_specs = (
        P(("expert", "dp"), "context", None),
        P(("expert", "dp"), "context", None),
        P(("expert", "context", "dp")),
        P(("expert", "context", "dp"), None),
        P(None, ("expert", "context", "dp")),
        P(("expert", "context", "dp"), None),
        P(("expert", "context", "dp")),
        P("expert", ("context", "dp"), None),
        P("expert", None, ("context", "dp")),
    )
    sizes = tuple(mesh.shape[a] for a in ("expert", "context", "dp"))
    local = local_fused if sizes[0] == 4 and sizes[2] == 2 else local_plain
    return jax.shard_map(local, mesh=mesh, in_specs=in_specs, out_specs=out_specs, check_vma=False)
```

```python
import functools
import math

import jax
import jax.numpy as jnp
from jax import lax
from jax.experimental import pallas as pl
from jax.experimental.pallas import tpu as pltpu
from jax.sharding import PartitionSpec as P

QUERY_HEADS = 12
KEY_VALUE_HEADS = 2
HEAD_DIMENSION = 128
TOP = 4
EXP_DEV = 2

EPSILON = 1e-06
ROPE_BASE = 10000.0
MASKED = -1e30

F32 = jnp.float32
BF16 = jnp.bfloat16


def rope_tables(positions, width):
    halfway = width // 2
    fraction = jnp.arange(halfway, dtype=jnp.float32) * (2.0 / width)
    frequency = jnp.exp(-math.log(ROPE_BASE) * fraction)
    angles = positions.astype(jnp.float32)[:, None] * frequency[None, :]
    cosine_values = jnp.cos(angles)
    sine_values = jnp.sin(angles)
    return (
        jnp.concatenate([cosine_values, cosine_values], -1),
        jnp.concatenate([sine_values, sine_values], -1),
    )


def rotate_half(values, cosine_values, sine_values):
    halfway = values.shape[-1] // 2
    turned = jnp.concatenate([-values[..., halfway:], values[..., :halfway]], -1)
    return values * cosine_values[:, None, :] + turned * sine_values[:, None, :]


def rotate_back(grads, cosine_values, sine_values):
    halfway = grads.shape[-1] // 2
    scaled = grads * sine_values[:, None, :]
    turned = jnp.concatenate([scaled[..., halfway:], -scaled[..., :halfway]], -1)
    return grads * cosine_values[:, None, :] + turned


def dot_nt(a, b):
    return lax.dot_general(a, b, (((1,), (1,)), ((), ())), preferred_element_type=F32)


def dot_tn(a, b):
    return lax.dot_general(a, b, (((0,), (0,)), ((), ())), preferred_element_type=F32)


def dot_nn(a, b):
    return jnp.dot(a, b, preferred_element_type=F32)


def masked_probs(first_row, query, key):
    scores = dot_nt(query, key) * (HEAD_DIMENSION**-0.5)
    rows = first_row + lax.broadcasted_iota(jnp.int32, scores.shape, 0)
    columns = lax.broadcasted_iota(jnp.int32, scores.shape, 1)
    scores = jnp.where(columns <= rows, scores, MASKED)
    expd = jnp.exp(scores - jnp.max(scores, axis=-1, keepdims=True))
    return expd / jnp.sum(expd, axis=-1, keepdims=True)


def attend_forward_kernel(first_ref, query_ref, key_ref, value_ref, heads_ref):
    probs = masked_probs(first_ref[0], query_ref[...], key_ref[...])
    heads_ref[...] = dot_nn(probs.astype(BF16), value_ref[...]).astype(BF16)


def attend_forward(first_row, query, key_value):
    tokens, width = query.shape
    length = key_value.shape[0]
    group = QUERY_HEADS // KEY_VALUE_HEADS
    size = HEAD_DIMENSION
    return pl.pallas_call(
        attend_forward_kernel,
        grid_spec=pltpu.PrefetchScalarGridSpec(
            num_scalar_prefetch=1,
            grid=(QUERY_HEADS,),
            in_specs=[
                pl.BlockSpec((tokens, size), lambda h, s: (0, h)),
                pl.BlockSpec((length, size), lambda h, s: (0, h // group)),
                pl.BlockSpec((length, size), lambda h, s: (0, KEY_VALUE_HEADS + h // group)),
            ],
            out_specs=pl.BlockSpec((tokens, size), lambda h, s: (0, h)),
        ),
        out_shape=jax.ShapeDtypeStruct((tokens, width), BF16),
        compiler_params=pltpu.CompilerParams(vmem_limit_bytes=32 * 1024 * 1024),
        cost_estimate=pl.CostEstimate(
            flops=4 * tokens * length * width, bytes_accessed=4 * tokens * width, transcendentals=0
        ),
    )(first_row, query, key_value, key_value)


def attend_backward_kernel(
    first_ref, query_ref, key_ref, value_ref, grad_ref, d_query_ref, d_key_ref, d_value_ref
):
    query, key, value, grad = query_ref[...], key_ref[...], value_ref[...], grad_ref[...]
    probs = masked_probs(first_ref[0], query, key)
    d_probs = dot_nt(grad, value)
    inner = jnp.sum(probs * d_probs, axis=-1, keepdims=True)
    d_raw = (probs * (d_probs - inner) * (HEAD_DIMENSION**-0.5)).astype(BF16)
    d_query_ref[...] = dot_nn(d_raw, key)
    d_key = dot_tn(d_raw, query)
    d_value = dot_tn(probs.astype(BF16), grad)

    @pl.when(pl.program_id(1) == 0)
    def _():
        d_key_ref[...] = d_key
        d_value_ref[...] = d_value

    @pl.when(pl.program_id(1) > 0)
    def _():
        d_key_ref[...] += d_key
        d_value_ref[...] += d_value


def attend_backward(first_row, query, key_value, grad):
    tokens, width = query.shape
    length = key_value.shape[0]
    group = QUERY_HEADS // KEY_VALUE_HEADS
    size = HEAD_DIMENSION
    row_spec = pl.BlockSpec((tokens, size), lambda j, g, s: (0, j * group + g))
    return pl.pallas_call(
        attend_backward_kernel,
        grid_spec=pltpu.PrefetchScalarGridSpec(
            num_scalar_prefetch=1,
            grid=(KEY_VALUE_HEADS, group),
            in_specs=[
                row_spec,
                pl.BlockSpec((length, size), lambda j, g, s: (0, j)),
                pl.BlockSpec((length, size), lambda j, g, s: (0, KEY_VALUE_HEADS + j)),
                row_spec,
            ],
            out_specs=[
                row_spec,
                pl.BlockSpec((length, size), lambda j, g, s: (0, j)),
                pl.BlockSpec((length, size), lambda j, g, s: (0, j)),
            ],
        ),
        out_shape=[
            jax.ShapeDtypeStruct((tokens, width), F32),
            jax.ShapeDtypeStruct((length, KEY_VALUE_HEADS * size), F32),
            jax.ShapeDtypeStruct((length, KEY_VALUE_HEADS * size), F32),
        ],
        compiler_params=pltpu.CompilerParams(vmem_limit_bytes=32 * 1024 * 1024),
        cost_estimate=pl.CostEstimate(
            flops=10 * tokens * length * width, bytes_accessed=8 * tokens * width, transcendentals=0
        ),
    )(first_row, query, key_value, key_value, grad)


def exchange(values, axis, mask):
    size = lax.axis_size(axis)
    return lax.ppermute(values, axis, [(i, i ^ mask) for i in range(size)])


def axis_masks(axis):
    size = lax.axis_size(axis)
    masks, bit = [], 1
    while bit < size:
        masks.append(bit)
        bit *= 2
    return masks


def cube_gather(values, axis, masks):
    held = {0: values}
    for mask in masks:
        for r, block in list(held.items()):
            held[r ^ mask] = exchange(block, axis, mask)
    return [held[r] for r in range(lax.axis_size(axis))]


def cube_scatter(blocks, axis, masks):
    held = dict(enumerate(blocks))
    for mask in masks:
        kept = {}
        for r in list(held):
            if not r & mask:
                arrived = exchange(held[r ^ mask].astype(BF16), axis, mask)
                kept[r] = held[r].astype(F32) + arrived.astype(F32)
        held = kept
    return held[0]


def line_steps(values, axis, up):
    size = lax.axis_size(axis)
    pairs = [(i, i + 1) if up else (i + 1, i) for i in range(size - 1)]
    return lax.ppermute(values, axis, pairs)


def line_gather(values, axis, both=True):
    size = lax.axis_size(axis)
    me = lax.axis_index(axis)
    result = jnp.zeros((size + 1,) + values.shape, values.dtype)
    result = lax.dynamic_update_index_in_dim(result, values, me, 0)
    up = down = values
    for step in range(1, size):
        up = line_steps(up, axis, True)
        result = lax.dynamic_update_index_in_dim(
            result, up, jnp.where(me - step >= 0, me - step, size), 0
        )
        if both:
            down = line_steps(down, axis, False)
            result = lax.dynamic_update_index_in_dim(result, down, jnp.minimum(me + step, size), 0)
    return result[:size]


def line_scatter(take, axis, up=True, down=True):
    size = lax.axis_size(axis)
    me = lax.axis_index(axis)
    total = take(me).astype(F32)
    for active, sign in ((up, 1), (down, -1)):
        if not active:
            continue
        arrived = None
        for step in range(1, size):
            block = take((me + sign * (size - step)) % size).astype(F32)
            if arrived is not None:
                block = block + arrived.astype(F32)
            arrived = line_steps(block.astype(BF16), axis, sign > 0)
        total = total + arrived.astype(F32)
    return total


def gather_rows(shard):
    ne, nc, nd = (lax.axis_size(a) for a in ("expert", "context", "dp"))
    rows, width = shard.shape
    lines = line_gather(shard, "context")
    masks = axis_masks("expert")
    half = width // 256 * 128
    parts = [lines[..., :half], lines[..., half:]]
    me = lax.axis_index("expert")
    result = jnp.zeros((ne, nc, rows, width), shard.dtype)
    for start, part, order in ((0, parts[0], masks), (half, parts[1], masks[::-1])):
        for r, block in enumerate(cube_gather(part, "expert", order)):
            result = lax.dynamic_update_slice(result, block[None], (me ^ r, 0, 0, start))
    core = lax.axis_index("dp")
    whole = jnp.zeros((ne, nc, nd, rows, width), shard.dtype)
    for r, block in enumerate(cube_gather(result, "dp", axis_masks("dp"))):
        whole = lax.dynamic_update_slice(whole, block[:, :, None], (0, 0, core ^ r, 0, 0))
    return whole.reshape(-1, width)


def scatter_rows(grad):
    ne, nc, nd = (lax.axis_size(a) for a in ("expert", "context", "dp"))
    width = grad.shape[-1]
    rows = grad.shape[0] // (ne * nc * nd)
    blocks = grad.reshape(ne, nc, nd, rows, width)
    core, me = lax.axis_index("dp"), lax.axis_index("expert")
    mine = cube_scatter(
        [
            lax.dynamic_index_in_dim(blocks, core ^ r, 2, keepdims=False)
            for r in range(nd)
        ],
        "dp",
        axis_masks("dp"),
    )
    masks = axis_masks("expert")
    half = width // 256 * 128
    sums = []
    for part, order in ((mine[..., :half], masks), (mine[..., half:], masks[::-1])):
        sums.append(
            cube_scatter(
                [lax.dynamic_index_in_dim(part, me ^ r, 0, keepdims=False) for r in range(ne)],
                "expert",
                order,
            )
        )
    lines = jnp.concatenate(sums, -1)
    return line_scatter(
        lambda j: lax.dynamic_index_in_dim(lines, j, 0, keepdims=False), "context"
    )


def plane_gather(rows):
    masks = axis_masks("expert")
    half = rows.shape[-1] // 2
    left = cube_gather(rows[:, :half], "expert", masks)
    right = cube_gather(rows[:, half:], "expert", masks[::-1])
    return jnp.concatenate([jnp.concatenate(p, -1) for p in zip(left, right)], 0)


def plane_scatter(partial, tokens):
    masks = axis_masks("expert")
    size = lax.axis_size("expert")
    half = partial.shape[-1] // 2
    blocks = partial.reshape(size, tokens, -1)
    left = cube_scatter([blocks[r, :, :half] for r in range(size)], "expert", masks)
    right = cube_scatter([blocks[r, :, half:] for r in range(size)], "expert", masks[::-1])
    return jnp.concatenate([left, right], -1)


MESH = pl.DeviceIdType.MESH
MIB = 1024 * 1024
SMALL = 128
GATE_ROWS = 16


def flip(index, mask):
    bit = 1
    while bit <= mask:
        if mask & bit:
            index = index + bit - 2 * bit * lax.rem(lax.div(index, bit), 2)
        bit *= 2
    return index


class Wire:
    def __init__(self, sends, recvs):
        self.sends, self.recvs = sends, recvs
        self.n_sends = self.n_recvs = 0
        self.open = []

    def slots(self, count):
        first = self.n_recvs
        self.n_recvs += count
        return first

    def start(self, src, dst, recv, device, when=None):
        copy = pltpu.make_async_remote_copy(
            src_ref=src,
            dst_ref=dst,
            send_sem=self.sends.at[self.n_sends],
            recv_sem=self.recvs.at[recv],
            device_id=device,
            device_id_type=MESH,
        )
        self.n_sends += 1
        guard(when, copy.start)
        self.open.append((when, copy))

    def arrived(self, dst, recv, device):
        pltpu.make_async_remote_copy(
            src_ref=dst,
            dst_ref=dst,
            send_sem=self.sends.at[0],
            recv_sem=self.recvs.at[recv],
            device_id=device,
            device_id_type=MESH,
        ).wait_recv()

    def finish(self):
        for when, copy in self.open:
            guard(when, copy.wait_send)
        self.open = []


def guard(when, action):
    if when is None:
        action()
    else:
        pl.when(when)(action)


def greet(targets):
    barrier = pltpu.get_barrier_semaphore()
    for device, when in targets:
        guard(
            when,
            lambda device=device: pl.semaphore_signal(
                barrier, inc=1, device_id=device, device_id_type=MESH
            ),
        )
    count = sum(1 if when is None else when.astype(jnp.int32) for _, when in targets)
    pl.semaphore_wait(barrier, count)


def plane_ids(e):
    return {m: {"expert": flip(e, m)} for m in (1, 2, 3)}


class RowsGather:
    def __init__(self, wire, ref, e, z, c, nc, half):
        self.wire, self.ref, self.e, self.z, self.c, self.nc = wire, ref, e, z, c, nc
        self.cols = (pl.ds(0, half), pl.ds(half, ref.shape[-1] - half))
        self.line = wire.slots(nc)
        self.plane = wire.slots(nc * 6)
        self.core = wire.slots(nc)
        self.ids = plane_ids(e)
        self.steps = []
        for k in range(nc):
            self.steps.append(functools.partial(self.spread, k))
            if k:
                self.steps.append(functools.partial(self.forward, k - 1))
            if k > 1:
                self.steps.append(functools.partial(self.share, k - 2))
        self.steps.append(functools.partial(self.forward, nc - 1))
        self.steps.append(functools.partial(self.share, nc - 2))
        self.steps.append(functools.partial(self.share, nc - 1))
        self.steps.append(self.complete)

    def at(self, r, zs, half):
        return self.ref.at[flip(self.e, r), zs, self.c, :, self.cols[half]]

    def slot(self, k, r, half):
        return self.plane + k * 6 + (r - 1) * 2 + half

    def spread(self, k):
        wire, z, nc = self.wire, self.z, self.nc
        zs = flip(z, k)
        whole = self.ref.at[self.e, zs, self.c]
        if k:
            wire.arrived(whole, self.line + zs, {"context": zs})
        wire.start(
            whole, whole, self.line + zs, {"context": z + 1}, when=(zs <= z) & (z < nc - 1)
        )
        wire.start(whole, whole, self.line + zs, {"context": z - 1}, when=(zs >= z) & (z > 0))
        for half, mask in ((0, 1), (1, 2), (1, 1), (0, 2)):
            part = self.at(0, zs, half)
            wire.start(part, part, self.slot(k, mask, half), self.ids[mask])

    def forward(self, k):
        zs = flip(self.z, k)
        for half, mask in ((0, 1), (1, 2)):
            part = self.at(mask, zs, half)
            self.wire.arrived(part, self.slot(k, mask, half), self.ids[mask])
            self.wire.start(part, part, self.slot(k, 3, half), self.ids[3 - mask])

    def share(self, k):
        zs = flip(self.z, k)
        for r, half in ((1, 1), (2, 0), (3, 0), (3, 1)):
            self.wire.arrived(self.at(r, zs, half), self.slot(k, r, half), self.ids[r])
        part = self.ref.at[:, zs, self.c]
        self.wire.start(part, part, self.core + k, {"dp": 1 - self.c})

    def complete(self):
        for k in range(self.nc):
            zs = flip(self.z, k)
            self.wire.arrived(self.ref.at[:, zs, 1 - self.c], self.core + k, {"dp": 1 - self.c})

    def step(self):
        if self.steps:
            self.steps.pop(0)()

    def run(self):
        while self.steps:
            self.step()


class PlaneGather:
    def __init__(self, wire, ref, e):
        self.wire, self.ref = wire, ref
        self.half = ref.shape[-1] // 2
        self.ids = plane_ids(e)
        self.first = wire.slots(6)
        self.steps = [self.spread, self.forward, self.complete]

    def at(self, r, half):
        return self.ref.at[r, :, pl.ds(half * self.half, self.half)]

    def slot(self, r, half):
        return self.first + (r - 1) * 2 + half

    def spread(self):
        for half, mask in ((0, 1), (1, 2), (1, 1), (0, 2)):
            self.wire.start(
                self.at(0, half), self.at(mask, half), self.slot(mask, half), self.ids[mask]
            )

    def forward(self):
        for half, mask in ((0, 1), (1, 2)):
            self.wire.arrived(self.at(mask, half), self.slot(mask, half), self.ids[mask])
            self.wire.start(
                self.at(mask, half), self.at(3, half), self.slot(3, half), self.ids[3 - mask]
            )

    def near(self, r):
        half = 1 if r == 1 else 0
        self.wire.arrived(self.at(r, half), self.slot(r, half), self.ids[r])

    def far(self):
        for half in (0, 1):
            self.wire.arrived(self.at(3, half), self.slot(3, half), self.ids[3])

    def complete(self):
        self.near(1)
        self.near(2)
        self.far()

    def step(self):
        if self.steps:
            self.steps.pop(0)()

    def run(self):
        while self.steps:
            self.step()


def swap_halves(values):
    return pltpu.roll(values, HEAD_DIMENSION // 2, 1)


def front_kernel(
    nc,
    experts,
    x_ref,
    q_shard,
    o_shard,
    cot_ref,
    cos_ref,
    sin_ref,
    routes_ref,
    q_all,
    o_all,
    cot_all,
    gate_all,
    inputs_ref,
    query_ref,
    kv_ref,
    heads_ref,
    hidden_ref,
    expert_in_ref,
    gains_ref,
    qkv_scr,
    sends,
    recvs,
):
    e, z, c = (lax.axis_index(a) for a in ("expert", "context", "dp"))
    size = HEAD_DIMENSION
    tokens, width = x_ref.shape
    query_width = QUERY_HEADS * size
    kv_width = 2 * KEY_VALUE_HEADS * size
    wire = Wire(sends, recvs)
    ids = plane_ids(e)
    greet(
        [(ids[m], None) for m in (1, 2, 3)]
        + [({"dp": 1 - c}, None), ({"context": z + 1}, z < nc - 1), ({"context": z - 1}, z > 0)]
    )
    q_all[e, z, c] = q_shard[...]
    o_all[e, z, c] = o_shard[...]
    cot_all[0] = cot_ref[...]

    gather_q = RowsGather(wire, q_all, e, z, c, nc, 1024)
    gather_o = RowsGather(wire, o_all, e, z, c, nc, 768)
    gather_cot = PlaneGather(wire, cot_all, e)
    gather_q.run()
    gather_o.step()

    small = q_all[:, :, :, :, pl.ds(query_width + kv_width, SMALL)].reshape(width, SMALL)
    small = jnp.transpose(small.astype(F32))
    gain_first, gain_second = small[experts : experts + 1], small[experts + 1 : experts + 2]
    gains_ref[0:1] = gain_first
    gains_ref[1:2] = gain_second
    rows = x_ref[...].astype(F32)
    scale1 = lax.rsqrt(jnp.mean(rows * rows, -1, keepdims=True) + EPSILON)
    inputs_ref[...] = (rows * scale1 * gain_first).astype(BF16)

    def project(first, count):
        weight = q_all[:, :, :, :, pl.ds(first, count)].reshape(width, count)
        qkv_scr[:, pl.ds(first, count)] = dot_nn(inputs_ref[...], weight)

    project(query_width, kv_width)

    def turned(column):
        head = qkv_scr[:, pl.ds(column, size)]
        return (head * cos_ref[...] + swap_halves(head) * sin_ref[...]).astype(BF16)

    for j in range(KEY_VALUE_HEADS):
        kv_ref[z, :, pl.ds(j * size, size)] = turned(query_width + j * size)
    values = pl.ds(kv_width // 2, kv_width // 2)
    kv_ref[z, :, values] = qkv_scr[:, pl.ds(query_width + kv_width // 2, kv_width // 2)].astype(
        BF16
    )
    line = wire.slots(nc)
    wire.start(kv_ref.at[z], kv_ref.at[z], line, {"context": z + 1}, when=z < nc - 1)
    for later in range(1, nc):

        def clear(later=later):
            kv_ref[z + later] = jnp.zeros(kv_ref.shape[1:], BF16)

        pl.when(z + later < nc)(clear)
    gather_o.step()

    @pl.loop(0, query_width // 256)
    def _(n):
        project(pl.multiple_of(n * 256, 256), 256)

    gather_o.step()
    project(query_width + kv_width, SMALL)
    gather_o.step()

    @pl.loop(0, QUERY_HEADS)
    def _(h):
        column = pl.multiple_of(h * size, size)
        query_ref[:, pl.ds(column, size)] = turned(column)

    gather_o.step()

    logits = qkv_scr[:, pl.ds(query_width + kv_width, SMALL)]
    lanes = lax.broadcasted_iota(jnp.int32, logits.shape, 1)
    named = lanes == routes_ref[:, 0:1]
    for k in range(1, TOP):
        named = named | (lanes == routes_ref[:, k : k + 1])
    logits = jnp.where(named, logits, MASKED)
    expd = jnp.exp(logits - jnp.max(logits, -1, keepdims=True))
    gates = expd / jnp.sum(expd, -1, keepdims=True)
    gate_all[0] = jnp.transpose(gates)[:GATE_ROWS]
    gate_slot = wire.slots(3)
    for r in (1, 2, 3):
        wire.start(gate_all.at[0], gate_all.at[r], gate_slot + r - 1, ids[r])

    gather_o.step()
    for step in range(1, nc):

        def pass_on(step=step):
            block = kv_ref.at[z - step]
            wire.arrived(block, line + step - 1, {"context": z - 1})

        pl.when(z >= step)(pass_on)
        wire.start(
            kv_ref.at[z - step],
            kv_ref.at[z - step],
            line + step,
            {"context": z + 1},
            when=(z >= step) & (z < nc - 1),
        )
        gather_o.step()
    gather_o.step()
    gather_o.step()

    length = nc * tokens
    group = QUERY_HEADS // KEY_VALUE_HEADS
    group_steps = 3
    for first in range(0, QUERY_HEADS, group_steps):
        j = first // group
        key = kv_ref[:, :, pl.ds(j * size, size)].reshape(length, size)
        value = kv_ref[:, :, pl.ds(kv_width // 2 + j * size, size)].reshape(length, size)

        @pl.loop(first, first + group_steps)
        def _(h):
            column = pl.multiple_of(h * size, size)
            scores = dot_nt(query_ref[:, pl.ds(column, size)], key) * (size**-0.5)
            row = z * tokens + lax.broadcasted_iota(jnp.int32, scores.shape, 0)
            place = lax.broadcasted_iota(jnp.int32, scores.shape, 1)
            scores = jnp.where(place <= row, scores, MASKED)
            expd = jnp.exp(scores - jnp.max(scores, -1, keepdims=True))
            total = jnp.sum(expd, -1, keepdims=True)
            mixed = dot_nn(expd.astype(BF16), value) / total
            heads_ref[:, pl.ds(column, size)] = mixed.astype(BF16)

        gather_o.step()
        gather_o.step()
        if first == 0:
            gather_o.run()
            gather_cot.step()
        else:
            gather_cot.step()

    gather_o.run()
    part = width // q_all.shape[0]
    for block in range(q_all.shape[0]):
        weight = o_all[block].reshape(part, width)
        columns = pl.ds(block * part, part)
        hidden_ref[:, columns] = x_ref[:, columns].astype(F32) + dot_nt(heads_ref[...], weight)
    hidden = hidden_ref[...]
    scale2 = lax.rsqrt(jnp.mean(hidden * hidden, -1, keepdims=True) + EPSILON)
    expert_in_ref[...] = (hidden * scale2 * gain_second).astype(BF16)
    gather_cot.run()
    for r in (1, 2, 3):
        wire.arrived(gate_all.at[r], gate_slot + r - 1, ids[r])
    wire.finish()


def front(x, q_shard, o_shard, cot, cosine, sine, routes, sizes):
    ne, nc, nd = sizes
    tokens, width = x.shape
    rows, q_width = q_shard.shape
    shapes = [
        ((ne, nc, nd, rows, q_width), BF16),
        ((ne, nc, nd, rows, width), BF16),
        ((ne, tokens, width), BF16),
        ((ne, GATE_ROWS, tokens), F32),
        ((tokens, width), BF16),
        ((tokens, QUERY_HEADS * HEAD_DIMENSION), BF16),
        ((nc, tokens, 2 * KEY_VALUE_HEADS * HEAD_DIMENSION), BF16),
        ((tokens, QUERY_HEADS * HEAD_DIMENSION), BF16),
        ((tokens, width), F32),
        ((tokens, width), BF16),
        ((8, width), F32),
    ]
    copies = 128
    return pl.pallas_call(
        functools.partial(front_kernel, nc, EXP_DEV * ne),
        out_shape=[jax.ShapeDtypeStruct(*s) for s in shapes],
        in_specs=[pl.BlockSpec(memory_space=pltpu.VMEM)] * 7,
        out_specs=[pl.BlockSpec(memory_space=pltpu.VMEM)] * len(shapes),
        scratch_shapes=[
            pltpu.VMEM((tokens, q_width), F32),
            pltpu.SemaphoreType.DMA((copies,)),
            pltpu.SemaphoreType.DMA((copies,)),
        ],
        compiler_params=pltpu.CompilerParams(
            collective_id=0, has_side_effects=True, vmem_limit_bytes=56 * MIB
        ),
    )(x, q_shard, o_shard, cot, cosine, sine, routes)


class PlaneScatter:
    def __init__(self, wire, part, land, e):
        self.wire, self.part, self.land = wire, part, land
        self.half = part.shape[-1] // 2
        self.ids = plane_ids(e)
        self.first = wire.slots(6)

    def at(self, r, half):
        return self.part.at[r - 1, :, pl.ds(half * self.half, self.half)]

    def send(self, r, half, mask, slot):
        self.wire.start(self.at(r, half), self.land.at[slot], self.first + slot, self.ids[mask])

    def near(self, r):
        self.send(r, r - 1, r, r - 1)

    def far(self):
        self.send(3, 0, 1, 2)
        self.send(3, 1, 2, 3)

    def relay(self):
        for half, r in ((0, 2), (1, 1)):
            slot = 2 + half
            self.wire.arrived(self.land.at[slot], self.first + slot, self.ids[3 - r])
            part = self.at(r, half)
            part[...] = (part[...].astype(F32) + self.land[slot].astype(F32)).astype(BF16)
            self.send(r, half, r, 4 + half)

    def total(self, own):
        for slot, half, mask in ((0, 0, 1), (1, 1, 2), (4, 0, 2), (5, 1, 1)):
            self.wire.arrived(self.land.at[slot], self.first + slot, self.ids[mask])
            columns = pl.ds(half * self.half, self.half)
            own[:, columns] += self.land[slot].astype(F32)


def experts_kernel(
    nc,
    x_ref,
    cot_all,
    gates_ref,
    w_gu,
    w_dn,
    mixture_ref,
    d_in_ref,
    d_gate_ref,
    grad_own,
    grad_core,
    x_all,
    a_all,
    dgu_all,
    y_part,
    dx_part,
    y_land,
    dx_land,
    dg_lanes,
    dg_part,
    dg_land,
    stage,
    sends,
    recvs,
    stage_sems,
    hand_sends,
):
    e, z, c = (lax.axis_index(a) for a in ("expert", "context", "dp"))
    tokens, width = x_ref.shape
    ff = w_dn.shape[1]
    blocks = x_all.shape[0]
    wire = Wire(sends, recvs)
    ids = plane_ids(e)
    greet([(ids[m], None) for m in (1, 2, 3)] + [({"dp": 1 - c}, None)])
    x_all[0] = x_ref[...]
    gather = PlaneGather(wire, x_all, e)
    scatter_dx = PlaneScatter(wire, dx_part, dx_land, e)
    scatter_y = PlaneScatter(wire, y_part, y_land, e)
    dg_slot = wire.slots(3)
    core_slot = wire.slots(nc)
    gather.spread()
    step = 256
    wide = 512

    def block(r):
        dg_lanes[...] = jnp.zeros_like(dg_lanes)
        for i in range(EXP_DEV):

            @pl.loop(0, ff // step)
            def _(f):
                column = pl.multiple_of(f * step, step)
                rows, grads = x_all[r], cot_all[r]
                gate_part = dot_nn(rows, w_gu[i, :, pl.ds(column, step)])
                up_part = dot_nn(rows, w_gu[i, :, pl.ds(ff + column, step)])
                raw = dot_nt(grads, w_dn[i, pl.ds(column, step), :])
                gate = gates_ref[r][:, i : i + 1]
                sigma = jax.nn.sigmoid(gate_part)
                silu = gate_part * sigma
                act = silu * up_part
                lanes = lax.broadcasted_iota(jnp.int32, dg_lanes.shape, 1)
                dg_lanes[...] += jnp.where(
                    lanes == e * EXP_DEV + i, jnp.sum(act * raw, -1, keepdims=True), 0.0
                )
                a_all[r, :, pl.ds(i * ff + column, step)] = (act * gate).astype(BF16)
                d_act = raw * gate
                d_gate_part = d_act * up_part * sigma * (1.0 + gate_part * (1.0 - sigma))
                first = i * 2 * ff + column
                dgu_all[r, :, pl.ds(first, step)] = d_gate_part.astype(BF16)
                dgu_all[r, :, pl.ds(first + ff, step)] = (d_act * silu).astype(BF16)

        @pl.loop(0, width // wide)
        def _(n):
            columns = pl.ds(pl.multiple_of(n * wide, wide), wide)
            d_rows = dot_nt(dgu_all[r, :, pl.ds(0, 2 * ff)], w_gu[0, columns, :])
            d_rows += dot_nt(dgu_all[r, :, pl.ds(2 * ff, 2 * ff)], w_gu[1, columns, :])
            weight = w_dn[:, :, columns].reshape(EXP_DEV * ff, wide)
            out = dot_nn(a_all[r], weight)
            if r == 0:
                d_in_ref[:, columns] = d_rows
                mixture_ref[:, columns] = out
            else:
                dx_part[r - 1, :, columns] = d_rows.astype(BF16)
                y_part[r - 1, :, columns] = out.astype(BF16)

        dg_part[r] = jnp.transpose(dg_lanes[...])[:GATE_ROWS]
        if r:
            wire.start(dg_part.at[r], dg_land.at[r - 1], dg_slot + r - 1, ids[r])

    block(0)
    gather.forward()
    gather.near(1)
    block(1)
    scatter_dx.near(1)
    scatter_y.near(1)
    gather.near(2)
    block(2)
    scatter_dx.near(2)
    scatter_y.near(2)
    gather.far()
    block(3)
    scatter_dx.far()
    scatter_y.far()

    def keep(j, slot):
        return pltpu.make_async_copy(stage.at[slot, c], grad_own.at[j], stage_sems.at[slot])

    def hand(n, j, slot):
        return pltpu.make_async_remote_copy(
            src_ref=stage.at[slot, 1 - c],
            dst_ref=grad_core.at[j],
            send_sem=hand_sends.at[n],
            recv_sem=recvs.at[core_slot + n],
            device_id={"dp": 1 - c},
            device_id_type=MESH,
        )

    def order(n):
        return flip(z, nc - 1 - n)

    def weight_grads(n):
        j, slot = order(n), n % 2
        if n >= 2:
            keep(order(n - 2), slot).wait()
            hand(n - 2, order(n - 2), slot).wait_send()
        rows_of = width // nc
        columns = pl.ds(pl.multiple_of(j * rows_of, rows_of), rows_of)
        for first, source, grad in (
            (0, x_all, dgu_all),
            (EXP_DEV * 2 * ff, cot_all, a_all),
        ):
            rows = source[:, :, columns].reshape(blocks * tokens, rows_of)

            @pl.loop(0, grad.shape[-1] // ff)
            def _(i):
                column = pl.multiple_of(i * ff, ff)
                part = grad[:, :, pl.ds(column, ff)].reshape(blocks * tokens, ff)
                result = dot_tn(rows, part).astype(BF16).reshape(2, rows_of // 2, ff)
                stage[slot, :, :, pl.ds(first + column, ff)] = result

        keep(j, slot).start()
        hand(n, j, slot).start()

    weight_grads(0)
    scatter_dx.relay()
    for n in range(1, nc - 1):
        weight_grads(n)
    scatter_y.relay()
    weight_grads(nc - 1)
    scatter_dx.total(d_in_ref)
    scatter_y.total(mixture_ref)
    total = dg_part[0]
    for r in (1, 2, 3):
        wire.arrived(dg_land.at[r - 1], dg_slot + r - 1, ids[r])
        total = total + dg_land[r - 1]
    d_gate_ref[...] = total
    for n in range(nc - 2, nc):
        keep(order(n), n % 2).wait()
        hand(n, order(n), n % 2).wait_send()
    for n in range(nc):
        hand(n, order(n), n % 2).wait_recv()
    wire.finish()


def experts(expert_in, cot_all, gates, w_gate_up, w_down, nc):
    blocks, tokens, width = cot_all.shape
    held, ff = w_down.shape[0], w_down.shape[1]
    grads = held * 3 * ff
    shapes = [
        ((tokens, width), F32),
        ((tokens, width), F32),
        ((GATE_ROWS, tokens), F32),
        ((nc, width // nc // 2, grads), BF16),
        ((nc, width // nc // 2, grads), BF16),
    ]
    copies = 32
    vmem = pl.BlockSpec(memory_space=pltpu.VMEM)
    anywhere = pl.BlockSpec(memory_space=pl.ANY)
    return pl.pallas_call(
        functools.partial(experts_kernel, nc),
        out_shape=[jax.ShapeDtypeStruct(*s) for s in shapes],
        in_specs=[vmem] * 5,
        out_specs=[vmem] * 3 + [anywhere] * 2,
        scratch_shapes=[
            pltpu.VMEM((blocks, tokens, width), BF16),
            pltpu.VMEM((blocks, tokens, held * ff), BF16),
            pltpu.VMEM((blocks, tokens, held * 2 * ff), BF16),
            pltpu.VMEM((blocks - 1, tokens, width), BF16),
            pltpu.VMEM((blocks - 1, tokens, width), BF16),
            pltpu.VMEM((6, tokens, width // 2), BF16),
            pltpu.VMEM((6, tokens, width // 2), BF16),
            pltpu.VMEM((tokens, SMALL), F32),
            pltpu.VMEM((blocks, GATE_ROWS, tokens), F32),
            pltpu.VMEM((blocks - 1, GATE_ROWS, tokens), F32),
            pltpu.VMEM((2, 2, width // nc // 2, grads), BF16),
            pltpu.SemaphoreType.DMA((copies,)),
            pltpu.SemaphoreType.DMA((copies,)),
            pltpu.SemaphoreType.DMA((2,)),
            pltpu.SemaphoreType.DMA((nc,)),
        ],
        compiler_params=pltpu.CompilerParams(
            collective_id=1, has_side_effects=True, vmem_limit_bytes=60 * MIB
        ),
    )(expert_in, cot_all, gates, w_gate_up, w_down)


class LineScatter:
    def __init__(self, wire, block, lands, z, nc, up=True):
        self.wire, self.block, self.lands, self.z, self.nc = wire, block, lands, z, nc
        self.up = up
        self.first = [wire.slots(nc - 1), wire.slots(nc - 1)]

    def arrive(self, way, index, j):
        land = self.lands[way].at[index]
        self.wire.arrived(land, self.first[way] + index, {"context": self.z})
        block = self.block(j)
        block[...] = (block[...].astype(F32) + self.lands[way][index].astype(F32)).astype(BF16)

    def move(self, way, j):
        z, nc = self.z, self.nc
        inner, index, near = ((z > 0), j - z, z + 1) if way == 0 else ((z < nc - 1), z - j, z - 1)
        wanted = (j > z) if way == 0 else (j < z)
        pl.when(wanted & inner)(lambda: self.arrive(way, index, j))
        self.wire.start(
            self.block(j),
            self.lands[way].at[index - 1],
            self.first[way] + index - 1,
            {"context": near},
            when=wanted,
        )

    def step(self, s):
        if self.up:
            self.move(0, self.nc - s)
        self.move(1, s - 1)

    def last(self):
        if self.up:
            pl.when(self.z > 0)(lambda: self.arrive(0, 0, self.z))
        pl.when(self.z < self.nc - 1)(lambda: self.arrive(1, 0, self.z))


class RowsScatter:
    def __init__(self, wire, buf, core, plane, lines, e, z, c, nc, width, half):
        self.wire, self.buf, self.core, self.plane = wire, buf, core, plane
        self.e, self.z, self.c, self.width = e, z, c, width
        self.cols = (pl.ds(0, half), pl.ds(half, width - half))
        self.sizes = (half, width - half)
        self.ids = plane_ids(e)
        self.core_slot = wire.slots(1)
        self.first = wire.slots(6)
        self.line = LineScatter(
            wire,
            lambda j: buf.at[c, e, j, :, pl.ds(0, width)],
            [lines.at[0], lines.at[1]],
            z,
            nc,
        )

    def share(self):
        self.wire.start(
            self.buf.at[1 - self.c, :, :, :, pl.ds(0, self.width)],
            self.core,
            self.core_slot,
            {"dp": 1 - self.c},
        )

    def land(self, slot, half):
        return self.plane.at[slot, :, :, pl.ds(0, self.sizes[half])]

    def at(self, r, half):
        return self.buf.at[self.c, flip(self.e, r), :, :, self.cols[half]]

    def send(self, r, half, mask, slot):
        self.wire.start(
            self.at(r, half), self.land(slot, half), self.first + slot, self.ids[mask]
        )

    def merge(self):
        self.wire.arrived(self.core, self.core_slot, {"dp": 1 - self.c})
        for r in (3, 1, 2, 0):
            block = flip(self.e, r)
            part = self.buf.at[self.c, block, :, :, pl.ds(0, self.width)]
            part[...] = (part[...].astype(F32) + self.core[block].astype(F32)).astype(BF16)
            if r == 3:
                self.send(3, 0, 1, 2)
                self.send(3, 1, 2, 3)
            elif r:
                self.send(r, r - 1, r, r - 1)

    def add(self, r, half, slot, mask):
        land = self.land(slot, half)
        self.wire.arrived(land, self.first + slot, self.ids[mask])
        part = self.at(r, half)
        part[...] = (part[...].astype(F32) + land[...].astype(F32)).astype(BF16)

    def relay(self):
        for half, r in ((0, 2), (1, 1)):
            self.add(r, half, 2 + half, 3 - r)
            self.send(r, half, r, 4 + half)

    def total(self):
        for slot, half, mask in ((0, 0, 1), (1, 1, 2), (4, 0, 2), (5, 1, 1)):
            self.add(0, half, slot, mask)


class ExpertLine:
    pieces = 2

    def __init__(self, wire, own, core, sums, lands, bufs, sems, z, nc):
        self.wire, self.own, self.core, self.sums, self.lands = wire, own, core, sums, lands
        self.bufs, self.sems, self.z, self.nc = bufs, sems, z, nc
        self.rows = own.shape[1] // self.pieces
        self.first = [wire.slots((nc - 1) * self.pieces) for _ in range(2)]

    def piece(self, ref, j, p):
        return ref.at[j, pl.ds(p * self.rows, self.rows), :]

    def load(self, source, number):
        return pltpu.make_async_copy(source, self.bufs.at[number], self.sems.at[number])

    def slot(self, way, index, p):
        return self.first[way] + index * self.pieces + p

    def add(self, way, index, p):
        land = self.piece(self.lands[way], index, p)
        self.wire.arrived(land, self.slot(way, index, p), {"context": self.z})
        copy = self.load(land, 2)
        copy.start()
        copy.wait()
        self.bufs[0] = (self.bufs[0].astype(F32) + self.bufs[2].astype(F32)).astype(BF16)

    def base(self, j, p):
        copies = [self.load(self.piece(s, j, p), n) for n, s in enumerate((self.own, self.core))]
        for copy in copies:
            copy.start()
        for copy in copies:
            copy.wait()
        self.bufs[0] = (self.bufs[0].astype(F32) + self.bufs[1].astype(F32)).astype(BF16)

    def move(self, way, j, inner_only):
        z, nc = self.z, self.nc
        inner, index, near = ((z > 0), j - z, z + 1) if way == 0 else ((z < nc - 1), z - j, z - 1)
        wanted = (j > z) if way == 0 else (j < z)
        wanted = wanted & (inner if inner_only else jnp.logical_not(inner))
        for p in range(self.pieces):

            def prepare(p=p):
                self.base(j, p)
                if inner_only:
                    self.add(way, index, p)
                copy = pltpu.make_async_copy(
                    self.bufs.at[0], self.piece(self.sums, j, p), self.sems.at[3]
                )
                copy.start()
                copy.wait()

            pl.when(wanted)(prepare)
            self.wire.start(
                self.piece(self.sums, j, p),
                self.piece(self.lands[way], index - 1, p),
                self.slot(way, index - 1, p),
                {"context": near},
                when=wanted,
            )

    def step(self, s, inner_only):
        self.move(0, self.nc - s, inner_only)
        self.move(1, s - 1, inner_only)

    def last(self, result):
        z = self.z
        for p in range(self.pieces):
            self.base(z, p)
            pl.when(z > 0)(lambda: self.add(0, 0, p))
            pl.when(z < self.nc - 1)(lambda: self.add(1, 0, p))
            result[pl.ds(p * self.rows, self.rows), :] = self.bufs[0].astype(F32)


def tail_kernel(
    nc,
    experts,
    x_ref,
    inputs_ref,
    query_ref,
    kv_ref,
    heads_ref,
    hidden_ref,
    cot_ref,
    d_in_ref,
    gate_ref,
    d_gate_ref,
    gains_ref,
    cos_ref,
    sin_ref,
    q_hbm,
    o_hbm,
    own_hbm,
    core_hbm,
    d_x_ref,
    sum_q_ref,
    sum_o_ref,
    sum_e_ref,
    sums_hbm,
    up_hbm,
    down_hbm,
    weight,
    grads,
    core_o,
    core_q,
    plane_o,
    plane_q,
    lines_o,
    lines_q,
    d_hidden_ref,
    d_attn_ref,
    d_heads_ref,
    d_all_ref,
    d_inputs_ref,
    rows_ref,
    dkv_acc,
    dkv_ref,
    dkv_land,
    bufs,
    sends,
    recvs,
    sends_o,
    recvs_o,
    local_sems,
):
    e, z, c = (lax.axis_index(a) for a in ("expert", "context", "dp"))
    size = HEAD_DIMENSION
    tokens, width = x_ref.shape
    query_width = QUERY_HEADS * size
    key_width = KEY_VALUE_HEADS * size
    qkv_width = query_width + 2 * key_width
    planes = weight.shape[0]
    part = width // planes
    wire, wire_o = Wire(sends, recvs), Wire(sends_o, recvs_o)
    ids = plane_ids(e)
    greet(
        [(ids[m], None) for m in (1, 2)]
        + [({"dp": 1 - c}, None), ({"context": z + 1}, z < nc - 1), ({"context": z - 1}, z > 0)]
    )
    load_o = pltpu.make_async_copy(
        o_hbm, weight.at[:, :, :, :, pl.ds(0, width)], local_sems.at[4]
    )
    load_o.start()
    expert = ExpertLine(
        wire, own_hbm, core_hbm, sums_hbm, (up_hbm, down_hbm), bufs, local_sems, z, nc
    )
    scatter_o = RowsScatter(wire_o, grads, core_o, plane_o, lines_o, e, z, c, nc, width, 768)
    scatter_q = RowsScatter(
        wire, grads, core_q, plane_q, lines_q, e, z, c, nc, qkv_width + SMALL, 1024
    )
    scatter_kv = LineScatter(
        wire, lambda j: dkv_ref.at[j], [dkv_land, dkv_land], z, nc, up=False
    )
    expert.step(1, False)

    hidden, d_in = hidden_ref[...], d_in_ref[...]
    scale2 = lax.rsqrt(jnp.mean(hidden * hidden, -1, keepdims=True) + EPSILON)
    scaled = d_in * gains_ref[1:2]
    mean = jnp.mean(scaled * hidden, -1, keepdims=True)
    d_hidden = cot_ref[...].astype(F32) + scale2 * scaled - hidden * (scale2 * scale2 * scale2 * mean)
    d_hidden_ref[...] = d_hidden
    d_attn_ref[...] = d_hidden.astype(BF16)
    rows_ref[...] = jnp.zeros_like(rows_ref)
    rows_ref[experts + 1 : experts + 2, :] = jnp.sum(d_in * hidden * scale2, 0, keepdims=True)

    @pl.loop(0, planes)
    def _(block):
        columns = pl.ds(pl.multiple_of(block * part, part), part)
        result = dot_tn(d_attn_ref[:, columns], heads_ref[...]).astype(BF16)
        result = result.reshape(nc, 2, part // nc // 2, width)
        for half in range(2):
            grads[half, block, :, :, pl.ds(0, width)] = result[:, half]

    scatter_o.share()
    load_o.wait()

    @pl.loop(0, query_width // 256)
    def _(n):
        columns = pl.ds(pl.multiple_of(n * 256, 256), 256)
        out = weight[:, :, :, :, columns].reshape(width, 256)
        d_heads_ref[:, columns] = dot_nn(d_attn_ref[...], out).astype(BF16)

    load_q = pltpu.make_async_copy(q_hbm, weight, local_sems.at[4])
    load_q.start()
    scatter_o.merge()

    length = nc * tokens
    group = QUERY_HEADS // KEY_VALUE_HEADS
    dkv_acc[...] = jnp.zeros_like(dkv_acc)
    for j in range(KEY_VALUE_HEADS):
        key_columns, value_columns = pl.ds(j * size, size), pl.ds(key_width + j * size, size)
        key = kv_ref[:, :, key_columns].reshape(length, size)
        value = kv_ref[:, :, value_columns].reshape(length, size)

        @pl.loop(j * group, (j + 1) * group)
        def _(h):
            columns = pl.ds(pl.multiple_of(h * size, size), size)
            query, grad = query_ref[:, columns], d_heads_ref[:, columns]
            probs = masked_probs(z * tokens, query, key)
            d_probs = dot_nt(grad, value)
            inner = jnp.sum(probs * d_probs, axis=-1, keepdims=True)
            d_raw = (probs * (d_probs - inner) * (size**-0.5)).astype(BF16)
            d_query = dot_nn(d_raw, key)
            d_query = d_query * cos_ref[...] - swap_halves(d_query) * sin_ref[...]
            d_all_ref[:, columns] = d_query.astype(BF16)
            dkv_acc[:, key_columns] += dot_tn(d_raw, query)
            dkv_acc[:, value_columns] += dot_tn(probs.astype(BF16), grad)

        if j == 0:
            scatter_o.relay()
    for j in range(nc):
        dkv_ref[j] = dkv_acc[pl.ds(j * tokens, tokens), :].astype(BF16)
    scatter_kv.step(1)
    scatter_o.total()
    scatter_o.line.step(1)
    scatter_kv.step(2)
    expert.step(1, True)
    scatter_o.line.step(2)
    for s in range(3, nc):
        scatter_kv.step(s)
        scatter_o.line.step(s)
    scatter_kv.last()
    expert.step(2, False)

    for h in range(KEY_VALUE_HEADS):
        grad = dkv_ref[z, :, pl.ds(h * size, size)].astype(F32)
        grad = grad * cos_ref[...] - swap_halves(grad) * sin_ref[...]
        d_all_ref[:, pl.ds(query_width + h * size, size)] = grad.astype(BF16)
    values = pl.ds(key_width, key_width)
    d_all_ref[:, pl.ds(query_width + key_width, key_width)] = dkv_ref[z, :, values]

    gates = gate_ref[...]
    d_gates = d_gate_ref[...]
    d_logits = gates * (d_gates - jnp.sum(gates * d_gates, 0, keepdims=True))
    d_logits = jnp.concatenate(
        [d_logits, jnp.zeros((SMALL - d_logits.shape[0], tokens), F32)], 0
    )
    d_all_ref[:, pl.ds(qkv_width, SMALL)] = jnp.transpose(d_logits).astype(BF16)

    load_q.wait()
    for block in range(planes):
        rows = weight[block].reshape(part, qkv_width + SMALL)
        d_inputs_ref[:, pl.ds(block * part, part)] = dot_nt(d_all_ref[...], rows)
    rows = x_ref[...].astype(F32)
    scale1 = lax.rsqrt(jnp.mean(rows * rows, -1, keepdims=True) + EPSILON)
    d_inputs = d_inputs_ref[...]
    rows_ref[experts : experts + 1, :] = jnp.sum(d_inputs * rows * scale1, 0, keepdims=True)
    scatter_o.line.last()
    sum_o_ref[...] = grads[c, e, z, :, pl.ds(0, width)].astype(F32)
    wire_o.finish()

    @pl.loop(0, planes)
    def _(block):
        columns = pl.ds(pl.multiple_of(block * part, part), part)
        left = inputs_ref[:, columns]
        extra = jnp.transpose(rows_ref[:, columns])
        for first, count in ((0, 1024), (1024, qkv_width - 1024), (qkv_width, SMALL)):
            result = dot_tn(left, d_all_ref[:, pl.ds(first, count)])
            if first == qkv_width:
                result = result + extra
            result = result.astype(BF16).reshape(nc, 2, part // nc // 2, count)
            for half in range(2):
                grads[half, block, :, :, pl.ds(first, count)] = result[:, half]

    scatter_q.share()
    scaled = d_inputs_ref[...] * gains_ref[0:1]
    rows = x_ref[...].astype(F32)
    scale1 = lax.rsqrt(jnp.mean(rows * rows, -1, keepdims=True) + EPSILON)
    mean = jnp.mean(scaled * rows, -1, keepdims=True)
    d_x = d_hidden_ref[...] + scale1 * scaled - rows * (scale1 * scale1 * scale1 * mean)
    d_x_ref[...] = d_x.astype(BF16)
    scatter_q.merge()
    expert.step(2, True)
    expert.step(3, False)
    scatter_q.relay()
    scatter_q.total()
    for s in range(1, nc):
        scatter_q.line.step(s)
        if s > 2:
            expert.step(s, True)
            if s < nc - 1:
                expert.step(s + 1, False)
    scatter_q.line.last()
    sum_q_ref[...] = grads[c, e, z].astype(F32)
    expert.last(sum_e_ref)
    wire.finish()


def tail(operands, sizes):
    ne, nc, nd = sizes
    x, inputs1, query, kv = operands[:4]
    q_all, o_all, own = operands[13], operands[14], operands[15]
    tokens, width = x.shape
    rows, q_width = q_all.shape[-2:]
    shard, e_width = own.shape[1:]
    kv_width = kv.shape[-1]
    line = (nc - 1, shard, e_width)
    shapes = [
        ((tokens, width), BF16),
        ((rows, q_width), F32),
        ((rows, width), F32),
        ((shard, e_width), F32),
        ((nc, shard, e_width), BF16),
        (line, BF16),
        (line, BF16),
    ]
    copies = 64
    vmem = pl.BlockSpec(memory_space=pltpu.VMEM)
    anywhere = pl.BlockSpec(memory_space=pl.ANY)
    return pl.pallas_call(
        functools.partial(tail_kernel, nc, EXP_DEV * ne),
        out_shape=[jax.ShapeDtypeStruct(*s) for s in shapes],
        in_specs=[vmem] * 13 + [anywhere] * 4,
        out_specs=[vmem] * 4 + [anywhere] * 3,
        scratch_shapes=[
            pltpu.VMEM((ne, nc, nd, rows, q_width), BF16),
            pltpu.VMEM((nd, ne, nc, rows, q_width), BF16),
            pltpu.VMEM((ne, nc, rows, width), BF16),
            pltpu.VMEM((ne, nc, rows, q_width), BF16),
            pltpu.VMEM((6, nc, rows, 768), BF16),
            pltpu.VMEM((6, nc, rows, q_width - 1024), BF16),
            pltpu.VMEM((2, nc - 1, rows, width), BF16),
            pltpu.VMEM((2, nc - 1, rows, q_width), BF16),
            pltpu.VMEM((tokens, width), F32),
            pltpu.VMEM((tokens, width), BF16),
            pltpu.VMEM((tokens, width), BF16),
            pltpu.VMEM((tokens, q_width), BF16),
            pltpu.VMEM((tokens, width), F32),
            pltpu.VMEM((SMALL, width), F32),
            pltpu.VMEM((nc * tokens, kv_width), F32),
            pltpu.VMEM((nc, tokens, kv_width), BF16),
            pltpu.VMEM((nc - 1, tokens, kv_width), BF16),
            pltpu.VMEM((3, shard // ExpertLine.pieces, e_width), BF16),
            pltpu.SemaphoreType.DMA((copies,)),
            pltpu.SemaphoreType.DMA((copies,)),
            pltpu.SemaphoreType.DMA((32,)),
            pltpu.SemaphoreType.DMA((32,)),
            pltpu.SemaphoreType.DMA((5,)),
        ],
        compiler_params=pltpu.CompilerParams(
            collective_id=2, has_side_effects=True, vmem_limit_bytes=62 * MIB
        ),
    )(*operands)


def local_plain(
    layer_input,
    gain_attn,
    query_key_value_weight,
    w_out,
    w_router,
    gain_ffn,
    w_gate_up,
    w_down,
    routes,
    d_out,
):
    tokens = layer_input.shape[1]
    model_width = layer_input.shape[2]
    ne, nc, nd = (lax.axis_size(a) for a in ("expert", "context", "dp"))
    expert_total = EXP_DEV * ne
    ff = w_down.shape[1]
    me = lax.axis_index("expert")
    first_row = lax.axis_index("context") * tokens
    query_width = QUERY_HEADS * HEAD_DIMENSION
    key_width = KEY_VALUE_HEADS * HEAD_DIMENSION
    qkv_width = query_width + 2 * key_width

    small = jnp.concatenate([w_router, gain_attn[:, None], gain_ffn[:, None]], -1)
    small = jnp.pad(small, ((0, 0), (0, 128 - small.shape[1])))
    gathered = gather_rows(jnp.concatenate([query_key_value_weight, small], -1))
    out_turned = gather_rows(w_out.T)
    qkv_weight = gathered[:, :qkv_width]
    router_weight = gathered[:, qkv_width : qkv_width + expert_total]
    gains = gathered[:, qkv_width + expert_total : qkv_width + expert_total + 2].T.astype(F32)
    gain_first, gain_second = gains[0], gains[1]
    cotangent_all = plane_gather(d_out[0])

    token_rows = layer_input[0].astype(F32)
    scale1 = lax.rsqrt(jnp.mean(token_rows * token_rows, -1, keepdims=True) + EPSILON)
    inputs1 = (token_rows * scale1 * gain_first).astype(BF16)
    query_key_value = dot_nn(inputs1, qkv_weight)
    cosine_values, sine_values = rope_tables(first_row + jnp.arange(tokens), HEAD_DIMENSION)
    rotated = rotate_half(
        query_key_value[:, : query_width + key_width].reshape(tokens, -1, HEAD_DIMENSION),
        cosine_values,
        sine_values,
    ).reshape(tokens, -1)
    query = rotated[:, :query_width].astype(BF16)
    key_value_local = jnp.concatenate(
        [rotated[:, query_width:], query_key_value[:, query_width + key_width :]], -1
    ).astype(BF16)
    key_value = line_gather(key_value_local, "context", both=False).reshape(nc * tokens, -1)
    first = first_row.astype(jnp.int32).reshape(1)
    heads = attend_forward(first, query, key_value)

    logits = dot_nn(inputs1, router_weight)
    chosen_ids = routes[0]
    picks = (chosen_ids[:, :, None] == jnp.arange(expert_total)[None, None, :]).astype(F32)
    chosen = jnp.sum(picks * logits[:, None, :], -1)
    gates = jax.nn.softmax(chosen, axis=-1)
    gate_dense = jnp.sum(picks * gates[:, :, None], 1).T
    gate_blocks = cube_gather(gate_dense, "expert", axis_masks("expert"))
    gate_local = jnp.concatenate(
        [lax.dynamic_slice_in_dim(b, me * EXP_DEV, EXP_DEV, 0) for b in gate_blocks], 1
    )

    attn = dot_nt(heads, out_turned)
    hidden = token_rows + attn
    scale2 = lax.rsqrt(jnp.mean(hidden * hidden, -1, keepdims=True) + EPSILON)
    expert_in = (hidden * scale2 * gain_second).astype(BF16)

    rows_all = plane_gather(expert_in)
    gate_up = jnp.einsum("td,edf->etf", rows_all, w_gate_up, preferred_element_type=F32)
    gate_part, up_part = gate_up[..., :ff], gate_up[..., ff:]
    sigma = jax.nn.sigmoid(gate_part)
    silu = gate_part * sigma
    act = silu * up_part
    gate_column = gate_local[:, :, None]
    act_gated = (act * gate_column).astype(BF16)
    partial_out = jnp.einsum("etf,efd->td", act_gated, w_down, preferred_element_type=F32)
    mixture = plane_scatter(partial_out.astype(BF16), tokens)
    layer_result = (hidden + mixture).astype(BF16)

    d_act_raw = jnp.einsum("td,efd->etf", cotangent_all, w_down, preferred_element_type=F32)
    d_gates_local = jnp.sum(d_act_raw * act, -1)
    d_act = d_act_raw * gate_column
    d_gate_part = d_act * up_part * sigma * (1.0 + gate_part * (1.0 - sigma))
    d_up_part = d_act * silu
    d_gate_up = jnp.concatenate([d_gate_part, d_up_part], -1).astype(BF16)
    d_rows = jnp.einsum("etf,edf->td", d_gate_up, w_gate_up, preferred_element_type=F32)
    grad_down = jnp.einsum("td,etf->edf", cotangent_all, act_gated, preferred_element_type=F32)
    grad_gate_up = jnp.einsum("td,etf->edf", rows_all, d_gate_up, preferred_element_type=F32)

    d_expert_in = plane_scatter(d_rows.astype(BF16), tokens)
    d_gate_blocks = d_gates_local.reshape(EXP_DEV, ne, tokens)
    d_gates_dense = jnp.zeros((expert_total, tokens), F32)
    for r in range(ne):
        arrived = d_gate_blocks[:, r]
        if r:
            arrived = exchange(arrived, "expert", r)
        d_gates_dense = lax.dynamic_update_slice(d_gates_dense, arrived, ((me ^ r) * EXP_DEV, 0))
    d_gates = jnp.sum(picks * d_gates_dense.T[:, None, :], -1)
    d_chosen = gates * (d_gates - jnp.sum(gates * d_gates, -1, keepdims=True))
    d_logits = jnp.sum(picks * d_chosen[:, :, None], 1).astype(BF16)
    grad_router = dot_tn(inputs1, d_logits)

    core = lax.axis_index("dp")
    part = model_width // (nc * nd)

    def scatter_experts(grad):
        blocks = grad.reshape(EXP_DEV, nc, nd, part, -1)
        mine = cube_scatter(
            [lax.dynamic_index_in_dim(blocks, core ^ r, 2, keepdims=False) for r in range(nd)],
            "dp",
            axis_masks("dp"),
        )
        return line_scatter(
            lambda j: lax.dynamic_index_in_dim(mine, j, 1, keepdims=False), "context"
        )

    sum_gate_up = scatter_experts(grad_gate_up)
    sum_down = jnp.swapaxes(scatter_experts(grad_down), 1, 2)

    cotangent = d_out[0].astype(F32)
    scaled2 = d_expert_in * gain_second
    d_hidden = (
        cotangent
        + scale2 * scaled2
        - hidden * (scale2 * scale2 * scale2) * jnp.mean(scaled2 * hidden, -1, keepdims=True)
    )
    grad_gain_second = jnp.sum(d_expert_in * hidden * scale2, 0)
    d_attn = d_hidden.astype(BF16)
    grad_out_turned = dot_tn(d_attn, heads)
    sum_out = scatter_rows(grad_out_turned).T
    d_heads = dot_nn(d_attn, out_turned).astype(BF16)
    d_query, d_key_all, d_value_all = attend_backward(first, query, key_value, d_heads)
    d_key_value_all = jnp.concatenate([d_key_all, d_value_all], -1).reshape(nc, tokens, -1)
    d_key_value = line_scatter(
        lambda j: lax.dynamic_index_in_dim(d_key_value_all, j, 0, keepdims=False),
        "context",
        up=False,
    )
    d_rotated = rotate_back(
        jnp.concatenate([d_query, d_key_value[:, :key_width]], -1).reshape(
            tokens, -1, HEAD_DIMENSION
        ),
        cosine_values,
        sine_values,
    ).reshape(tokens, -1)
    d_qkv = jnp.concatenate([d_rotated, d_key_value[:, key_width:]], -1).astype(BF16)
    d_inputs = dot_nt(d_qkv, qkv_weight) + dot_nt(d_logits, router_weight)
    grad_gain_first = jnp.sum(d_inputs * token_rows * scale1, 0)
    grad_qkv = dot_tn(inputs1, d_qkv)
    small_grads = jnp.concatenate(
        [grad_router, grad_gain_first[:, None], grad_gain_second[:, None]], -1
    )
    small_grads = jnp.pad(small_grads, ((0, 0), (0, 128 - small_grads.shape[1])))
    sum_rows = scatter_rows(jnp.concatenate([grad_qkv, small_grads], -1))
    sum_qkv = sum_rows[:, :qkv_width]
    sum_router = sum_rows[:, qkv_width : qkv_width + expert_total]
    sum_gain_first = sum_rows[:, qkv_width + expert_total]
    sum_gain_second = sum_rows[:, qkv_width + expert_total + 1]
    scaled1 = d_inputs * gain_first
    d_input_rows = (
        d_hidden
        + scale1 * scaled1
        - token_rows
        * (scale1 * scale1 * scale1)
        * jnp.mean(scaled1 * token_rows, -1, keepdims=True)
    ).astype(BF16)
    return (
        layer_result[None],
        d_input_rows[None],
        sum_gain_first,
        sum_qkv,
        sum_out,
        sum_router,
        sum_gain_second,
        sum_gate_up,
        sum_down,
    )


def local_fused(
    layer_input,
    gain_attn,
    query_key_value_weight,
    w_out,
    w_router,
    gain_ffn,
    w_gate_up,
    w_down,
    routes,
    d_out,
):
    tokens = layer_input.shape[1]
    ne, nc, nd = sizes = tuple(lax.axis_size(a) for a in ("expert", "context", "dp"))
    expert_total = EXP_DEV * ne
    ff = w_down.shape[1]
    me = lax.axis_index("expert")
    first_row = lax.axis_index("context") * tokens
    query_width = QUERY_HEADS * HEAD_DIMENSION
    key_width = KEY_VALUE_HEADS * HEAD_DIMENSION
    qkv_width = query_width + 2 * key_width

    small = jnp.concatenate([w_router, gain_attn[:, None], gain_ffn[:, None]], -1)
    small = jnp.pad(small, ((0, 0), (0, SMALL - small.shape[1])))
    cosine_values, sine_values = rope_tables(first_row + jnp.arange(tokens), HEAD_DIMENSION)
    sign = jnp.where(jnp.arange(HEAD_DIMENSION) < HEAD_DIMENSION // 2, -1.0, 1.0)
    (
        q_all,
        o_all,
        cotangent_all,
        gate_all,
        inputs1,
        query,
        key_value,
        heads,
        hidden,
        expert_in,
        gains,
    ) = front(
        layer_input[0],
        jnp.concatenate([query_key_value_weight, small], -1),
        w_out.T,
        d_out[0],
        cosine_values,
        sine_values * sign,
        routes[0],
        sizes,
    )
    gate_local = jnp.swapaxes(
        lax.dynamic_slice_in_dim(gate_all, me * EXP_DEV, EXP_DEV, 1), 1, 2
    )
    mixture, d_expert_in, d_gates, grad_own, grad_core = experts(
        expert_in, cotangent_all, gate_local, w_gate_up, w_down, nc
    )
    layer_result = (hidden + mixture).astype(BF16)
    d_x, sum_rows, sum_out, sum_experts = tail(
        (
            layer_input[0],
            inputs1,
            query,
            key_value,
            heads,
            hidden,
            d_out[0],
            d_expert_in,
            gate_all[0],
            d_gates,
            gains,
            cosine_values,
            sine_values * sign,
            q_all,
            o_all,
            grad_own,
            grad_core,
        ),
        sizes,
    )[:4]
    sum_gate_up = jnp.stack([sum_experts[:, i * 2 * ff : (i + 1) * 2 * ff] for i in range(EXP_DEV)])
    sum_down = sum_experts[:, EXP_DEV * 2 * ff :].reshape(-1, EXP_DEV, ff)
    return (
        layer_result[None],
        d_x[None],
        sum_rows[:, qkv_width + expert_total],
        sum_rows[:, :qkv_width],
        sum_out.T,
        sum_rows[:, qkv_width : qkv_width + expert_total],
        sum_rows[:, qkv_width + expert_total + 1],
        sum_gate_up,
        jnp.transpose(sum_down, (1, 2, 0)),
    )


def solution(mesh):
    in_specs = (
        P(("expert", "dp"), "context", None),
        P(("expert", "context", "dp")),
        P(("expert", "context", "dp"), None),
        P(None, ("expert", "context", "dp")),
        P(("expert", "context", "dp"), None),
        P(("expert", "context", "dp")),
        P("expert", None, None),
        P("expert", None, None),
        P(("expert", "dp"), "context", None),
        P(("expert", "dp"), "context", None),
    )
    out_specs = (
        P(("expert", "dp"), "context", None),
        P(("expert", "dp"), "context", None),
        P(("expert", "context", "dp")),
        P(("expert", "context", "dp"), None),
        P(None, ("expert", "context", "dp")),
        P(("expert", "context", "dp"), None),
        P(("expert", "context", "dp")),
        P("expert", ("context", "dp"), None),
        P("expert", None, ("context", "dp")),
    )
    sizes = tuple(mesh.shape[a] for a in ("expert", "context", "dp"))
    local = local_fused if sizes[0] == 4 and sizes[2] == 2 else local_plain
    return jax.shard_map(local, mesh=mesh, in_specs=in_specs, out_specs=out_specs, check_vma=False)
```

```python
import functools
import math

import jax
import jax.numpy as jnp
from jax import lax
from jax.experimental import pallas as pl
from jax.experimental.pallas import tpu as pltpu
from jax.sharding import PartitionSpec as P

QUERY_HEADS = 12
KEY_VALUE_HEADS = 2
HEAD_DIMENSION = 128
TOP = 4
EXP_DEV = 2

EPSILON = 1e-06
ROPE_BASE = 10000.0
MASKED = -1e30

F32 = jnp.float32
BF16 = jnp.bfloat16


def rope_tables(positions, width):
    halfway = width // 2
    fraction = jnp.arange(halfway, dtype=jnp.float32) * (2.0 / width)
    frequency = jnp.exp(-math.log(ROPE_BASE) * fraction)
    angles = positions.astype(jnp.float32)[:, None] * frequency[None, :]
    cosine_values = jnp.cos(angles)
    sine_values = jnp.sin(angles)
    return (
        jnp.concatenate([cosine_values, cosine_values], -1),
        jnp.concatenate([sine_values, sine_values], -1),
    )


def rotate_half(values, cosine_values, sine_values):
    halfway = values.shape[-1] // 2
    turned = jnp.concatenate([-values[..., halfway:], values[..., :halfway]], -1)
    return values * cosine_values[:, None, :] + turned * sine_values[:, None, :]


def rotate_back(grads, cosine_values, sine_values):
    halfway = grads.shape[-1] // 2
    scaled = grads * sine_values[:, None, :]
    turned = jnp.concatenate([scaled[..., halfway:], -scaled[..., :halfway]], -1)
    return grads * cosine_values[:, None, :] + turned


def dot_nt(a, b):
    return lax.dot_general(a, b, (((1,), (1,)), ((), ())), preferred_element_type=F32)


def dot_tn(a, b):
    return lax.dot_general(a, b, (((0,), (0,)), ((), ())), preferred_element_type=F32)


def dot_nn(a, b):
    return jnp.dot(a, b, preferred_element_type=F32)


def masked_probs(first_row, query, key):
    scores = dot_nt(query, key) * (HEAD_DIMENSION**-0.5)
    rows = first_row + lax.broadcasted_iota(jnp.int32, scores.shape, 0)
    columns = lax.broadcasted_iota(jnp.int32, scores.shape, 1)
    scores = jnp.where(columns <= rows, scores, MASKED)
    expd = jnp.exp(scores - jnp.max(scores, axis=-1, keepdims=True))
    return expd / jnp.sum(expd, axis=-1, keepdims=True)


def attend_forward_kernel(first_ref, query_ref, key_ref, value_ref, heads_ref):
    probs = masked_probs(first_ref[0], query_ref[...], key_ref[...])
    heads_ref[...] = dot_nn(probs.astype(BF16), value_ref[...]).astype(BF16)


def attend_forward(first_row, query, key_value):
    tokens, width = query.shape
    length = key_value.shape[0]
    group = QUERY_HEADS // KEY_VALUE_HEADS
    size = HEAD_DIMENSION
    return pl.pallas_call(
        attend_forward_kernel,
        grid_spec=pltpu.PrefetchScalarGridSpec(
            num_scalar_prefetch=1,
            grid=(QUERY_HEADS,),
            in_specs=[
                pl.BlockSpec((tokens, size), lambda h, s: (0, h)),
                pl.BlockSpec((length, size), lambda h, s: (0, h // group)),
                pl.BlockSpec((length, size), lambda h, s: (0, KEY_VALUE_HEADS + h // group)),
            ],
            out_specs=pl.BlockSpec((tokens, size), lambda h, s: (0, h)),
        ),
        out_shape=jax.ShapeDtypeStruct((tokens, width), BF16),
        compiler_params=pltpu.CompilerParams(vmem_limit_bytes=32 * 1024 * 1024),
        cost_estimate=pl.CostEstimate(
            flops=4 * tokens * length * width, bytes_accessed=4 * tokens * width, transcendentals=0
        ),
    )(first_row, query, key_value, key_value)


def attend_backward_kernel(
    first_ref, query_ref, key_ref, value_ref, grad_ref, d_query_ref, d_key_ref, d_value_ref
):
    query, key, value, grad = query_ref[...], key_ref[...], value_ref[...], grad_ref[...]
    probs = masked_probs(first_ref[0], query, key)
    d_probs = dot_nt(grad, value)
    inner = jnp.sum(probs * d_probs, axis=-1, keepdims=True)
    d_raw = (probs * (d_probs - inner) * (HEAD_DIMENSION**-0.5)).astype(BF16)
    d_query_ref[...] = dot_nn(d_raw, key)
    d_key = dot_tn(d_raw, query)
    d_value = dot_tn(probs.astype(BF16), grad)

    @pl.when(pl.program_id(1) == 0)
    def _():
        d_key_ref[...] = d_key
        d_value_ref[...] = d_value

    @pl.when(pl.program_id(1) > 0)
    def _():
        d_key_ref[...] += d_key
        d_value_ref[...] += d_value


def attend_backward(first_row, query, key_value, grad):
    tokens, width = query.shape
    length = key_value.shape[0]
    group = QUERY_HEADS // KEY_VALUE_HEADS
    size = HEAD_DIMENSION
    row_spec = pl.BlockSpec((tokens, size), lambda j, g, s: (0, j * group + g))
    return pl.pallas_call(
        attend_backward_kernel,
        grid_spec=pltpu.PrefetchScalarGridSpec(
            num_scalar_prefetch=1,
            grid=(KEY_VALUE_HEADS, group),
            in_specs=[
                row_spec,
                pl.BlockSpec((length, size), lambda j, g, s: (0, j)),
                pl.BlockSpec((length, size), lambda j, g, s: (0, KEY_VALUE_HEADS + j)),
                row_spec,
            ],
            out_specs=[
                row_spec,
                pl.BlockSpec((length, size), lambda j, g, s: (0, j)),
                pl.BlockSpec((length, size), lambda j, g, s: (0, j)),
            ],
        ),
        out_shape=[
            jax.ShapeDtypeStruct((tokens, width), F32),
            jax.ShapeDtypeStruct((length, KEY_VALUE_HEADS * size), F32),
            jax.ShapeDtypeStruct((length, KEY_VALUE_HEADS * size), F32),
        ],
        compiler_params=pltpu.CompilerParams(vmem_limit_bytes=32 * 1024 * 1024),
        cost_estimate=pl.CostEstimate(
            flops=10 * tokens * length * width, bytes_accessed=8 * tokens * width, transcendentals=0
        ),
    )(first_row, query, key_value, key_value, grad)


def exchange(values, axis, mask):
    size = lax.axis_size(axis)
    return lax.ppermute(values, axis, [(i, i ^ mask) for i in range(size)])


def axis_masks(axis):
    size = lax.axis_size(axis)
    masks, bit = [], 1
    while bit < size:
        masks.append(bit)
        bit *= 2
    return masks


def cube_gather(values, axis, masks):
    held = {0: values}
    for mask in masks:
        for r, block in list(held.items()):
            held[r ^ mask] = exchange(block, axis, mask)
    return [held[r] for r in range(lax.axis_size(axis))]


def cube_scatter(blocks, axis, masks):
    held = dict(enumerate(blocks))
    for mask in masks:
        kept = {}
        for r in list(held):
            if not r & mask:
                arrived = exchange(held[r ^ mask].astype(BF16), axis, mask)
                kept[r] = held[r].astype(F32) + arrived.astype(F32)
        held = kept
    return held[0]


def line_steps(values, axis, up):
    size = lax.axis_size(axis)
    pairs = [(i, i + 1) if up else (i + 1, i) for i in range(size - 1)]
    return lax.ppermute(values, axis, pairs)


def line_gather(values, axis, both=True):
    size = lax.axis_size(axis)
    me = lax.axis_index(axis)
    result = jnp.zeros((size + 1,) + values.shape, values.dtype)
    result = lax.dynamic_update_index_in_dim(result, values, me, 0)
    up = down = values
    for step in range(1, size):
        up = line_steps(up, axis, True)
        result = lax.dynamic_update_index_in_dim(
            result, up, jnp.where(me - step >= 0, me - step, size), 0
        )
        if both:
            down = line_steps(down, axis, False)
            result = lax.dynamic_update_index_in_dim(result, down, jnp.minimum(me + step, size), 0)
    return result[:size]


def line_scatter(take, axis, up=True, down=True):
    size = lax.axis_size(axis)
    me = lax.axis_index(axis)
    total = take(me).astype(F32)
    for active, sign in ((up, 1), (down, -1)):
        if not active:
            continue
        arrived = None
        for step in range(1, size):
            block = take((me + sign * (size - step)) % size).astype(F32)
            if arrived is not None:
                block = block + arrived.astype(F32)
            arrived = line_steps(block.astype(BF16), axis, sign > 0)
        total = total + arrived.astype(F32)
    return total


def gather_rows(shard):
    ne, nc, nd = (lax.axis_size(a) for a in ("expert", "context", "dp"))
    rows, width = shard.shape
    lines = line_gather(shard, "context")
    masks = axis_masks("expert")
    half = width // 256 * 128
    parts = [lines[..., :half], lines[..., half:]]
    me = lax.axis_index("expert")
    result = jnp.zeros((ne, nc, rows, width), shard.dtype)
    for start, part, order in ((0, parts[0], masks), (half, parts[1], masks[::-1])):
        for r, block in enumerate(cube_gather(part, "expert", order)):
            result = lax.dynamic_update_slice(result, block[None], (me ^ r, 0, 0, start))
    core = lax.axis_index("dp")
    whole = jnp.zeros((ne, nc, nd, rows, width), shard.dtype)
    for r, block in enumerate(cube_gather(result, "dp", axis_masks("dp"))):
        whole = lax.dynamic_update_slice(whole, block[:, :, None], (0, 0, core ^ r, 0, 0))
    return whole.reshape(-1, width)


def scatter_rows(grad):
    ne, nc, nd = (lax.axis_size(a) for a in ("expert", "context", "dp"))
    width = grad.shape[-1]
    rows = grad.shape[0] // (ne * nc * nd)
    blocks = grad.reshape(ne, nc, nd, rows, width)
    core, me = lax.axis_index("dp"), lax.axis_index("expert")
    mine = cube_scatter(
        [
            lax.dynamic_index_in_dim(blocks, core ^ r, 2, keepdims=False)
            for r in range(nd)
        ],
        "dp",
        axis_masks("dp"),
    )
    masks = axis_masks("expert")
    half = width // 256 * 128
    sums = []
    for part, order in ((mine[..., :half], masks), (mine[..., half:], masks[::-1])):
        sums.append(
            cube_scatter(
                [lax.dynamic_index_in_dim(part, me ^ r, 0, keepdims=False) for r in range(ne)],
                "expert",
                order,
            )
        )
    lines = jnp.concatenate(sums, -1)
    return line_scatter(
        lambda j: lax.dynamic_index_in_dim(lines, j, 0, keepdims=False), "context"
    )


def plane_gather(rows):
    masks = axis_masks("expert")
    half = rows.shape[-1] // 2
    left = cube_gather(rows[:, :half], "expert", masks)
    right = cube_gather(rows[:, half:], "expert", masks[::-1])
    return jnp.concatenate([jnp.concatenate(p, -1) for p in zip(left, right)], 0)


def plane_scatter(partial, tokens):
    masks = axis_masks("expert")
    size = lax.axis_size("expert")
    half = partial.shape[-1] // 2
    blocks = partial.reshape(size, tokens, -1)
    left = cube_scatter([blocks[r, :, :half] for r in range(size)], "expert", masks)
    right = cube_scatter([blocks[r, :, half:] for r in range(size)], "expert", masks[::-1])
    return jnp.concatenate([left, right], -1)


MESH = pl.DeviceIdType.MESH
MIB = 1024 * 1024
SMALL = 128
GATE_ROWS = 16


def flip(index, mask):
    bit = 1
    while bit <= mask:
        if mask & bit:
            index = index + bit - 2 * bit * lax.rem(lax.div(index, bit), 2)
        bit *= 2
    return index


class Wire:
    def __init__(self, sends, recvs):
        self.sends, self.recvs = sends, recvs
        self.n_sends = self.n_recvs = 0
        self.open = []

    def slots(self, count):
        first = self.n_recvs
        self.n_recvs += count
        return first

    def start(self, src, dst, recv, device, when=None):
        copy = pltpu.make_async_remote_copy(
            src_ref=src,
            dst_ref=dst,
            send_sem=self.sends.at[self.n_sends],
            recv_sem=self.recvs.at[recv],
            device_id=device,
            device_id_type=MESH,
        )
        self.n_sends += 1
        guard(when, copy.start)
        self.open.append((when, copy))

    def arrived(self, dst, recv, device):
        pltpu.make_async_remote_copy(
            src_ref=dst,
            dst_ref=dst,
            send_sem=self.sends.at[0],
            recv_sem=self.recvs.at[recv],
            device_id=device,
            device_id_type=MESH,
        ).wait_recv()

    def finish(self):
        for when, copy in self.open:
            guard(when, copy.wait_send)
        self.open = []


def guard(when, action):
    if when is None:
        action()
    else:
        pl.when(when)(action)


def greet(targets):
    barrier = pltpu.get_barrier_semaphore()
    for device, when in targets:
        guard(
            when,
            lambda device=device: pl.semaphore_signal(
                barrier, inc=1, device_id=device, device_id_type=MESH
            ),
        )
    count = sum(1 if when is None else when.astype(jnp.int32) for _, when in targets)
    pl.semaphore_wait(barrier, count)


def plane_ids(e):
    return {m: {"expert": flip(e, m)} for m in (1, 2, 3)}


class RowsGather:
    def __init__(self, wire, ref, e, z, c, nc, half):
        self.wire, self.ref, self.e, self.z, self.c, self.nc = wire, ref, e, z, c, nc
        self.cols = (pl.ds(0, half), pl.ds(half, ref.shape[-1] - half))
        self.line = wire.slots(nc)
        self.plane = wire.slots(nc * 6)
        self.core = wire.slots(nc)
        self.ids = plane_ids(e)
        self.steps = []
        for k in range(nc):
            self.steps.append(functools.partial(self.spread, k))
            if k:
                self.steps.append(functools.partial(self.forward, k - 1))
            if k > 1:
                self.steps.append(functools.partial(self.share, k - 2))
        self.steps.append(functools.partial(self.forward, nc - 1))
        self.steps.append(functools.partial(self.share, nc - 2))
        self.steps.append(functools.partial(self.share, nc - 1))
        self.steps.append(self.complete)

    def at(self, r, zs, half):
        return self.ref.at[flip(self.e, r), zs, self.c, :, self.cols[half]]

    def slot(self, k, r, half):
        return self.plane + k * 6 + (r - 1) * 2 + half

    def spread(self, k):
        wire, z, nc = self.wire, self.z, self.nc
        zs = flip(z, k)
        whole = self.ref.at[self.e, zs, self.c]
        if k:
            wire.arrived(whole, self.line + zs, {"context": zs})
        wire.start(
            whole, whole, self.line + zs, {"context": z + 1}, when=(zs <= z) & (z < nc - 1)
        )
        wire.start(whole, whole, self.line + zs, {"context": z - 1}, when=(zs >= z) & (z > 0))
        for half, mask in ((0, 1), (1, 2), (1, 1), (0, 2)):
            part = self.at(0, zs, half)
            wire.start(part, part, self.slot(k, mask, half), self.ids[mask])

    def forward(self, k):
        zs = flip(self.z, k)
        for half, mask in ((0, 1), (1, 2)):
            part = self.at(mask, zs, half)
            self.wire.arrived(part, self.slot(k, mask, half), self.ids[mask])
            self.wire.start(part, part, self.slot(k, 3, half), self.ids[3 - mask])

    def share(self, k):
        zs = flip(self.z, k)
        for r, half in ((1, 1), (2, 0), (3, 0), (3, 1)):
            self.wire.arrived(self.at(r, zs, half), self.slot(k, r, half), self.ids[r])
        part = self.ref.at[:, zs, self.c]
        self.wire.start(part, part, self.core + k, {"dp": 1 - self.c})

    def complete(self):
        for k in range(self.nc):
            zs = flip(self.z, k)
            self.wire.arrived(self.ref.at[:, zs, 1 - self.c], self.core + k, {"dp": 1 - self.c})

    def step(self):
        if self.steps:
            self.steps.pop(0)()

    def run(self):
        while self.steps:
            self.step()


class PlaneGather:
    def __init__(self, wire, ref, e):
        self.wire, self.ref = wire, ref
        self.half = ref.shape[-1] // 2
        self.ids = plane_ids(e)
        self.first = wire.slots(6)
        self.steps = [self.spread, self.forward, self.complete]

    def at(self, r, half):
        return self.ref.at[r, :, pl.ds(half * self.half, self.half)]

    def slot(self, r, half):
        return self.first + (r - 1) * 2 + half

    def spread(self):
        for half, mask in ((0, 1), (1, 2), (1, 1), (0, 2)):
            self.wire.start(
                self.at(0, half), self.at(mask, half), self.slot(mask, half), self.ids[mask]
            )

    def forward(self):
        for half, mask in ((0, 1), (1, 2)):
            self.wire.arrived(self.at(mask, half), self.slot(mask, half), self.ids[mask])
            self.wire.start(
                self.at(mask, half), self.at(3, half), self.slot(3, half), self.ids[3 - mask]
            )

    def near(self, r):
        half = 1 if r == 1 else 0
        self.wire.arrived(self.at(r, half), self.slot(r, half), self.ids[r])

    def far(self):
        for half in (0, 1):
            self.wire.arrived(self.at(3, half), self.slot(3, half), self.ids[3])

    def complete(self):
        self.near(1)
        self.near(2)
        self.far()

    def step(self):
        if self.steps:
            self.steps.pop(0)()

    def run(self):
        while self.steps:
            self.step()


def swap_halves(values):
    return pltpu.roll(values, HEAD_DIMENSION // 2, 1)


def front_kernel(
    nc,
    experts,
    x_ref,
    q_shard,
    o_shard,
    cot_ref,
    cos_ref,
    sin_ref,
    routes_ref,
    q_all,
    o_all,
    cot_all,
    gate_all,
    inputs_ref,
    query_ref,
    kv_ref,
    heads_ref,
    hidden_ref,
    expert_in_ref,
    gains_ref,
    qkv_scr,
    sends,
    recvs,
):
    e, z, c = (lax.axis_index(a) for a in ("expert", "context", "dp"))
    size = HEAD_DIMENSION
    tokens, width = x_ref.shape
    query_width = QUERY_HEADS * size
    kv_width = 2 * KEY_VALUE_HEADS * size
    wire = Wire(sends, recvs)
    ids = plane_ids(e)
    greet(
        [(ids[m], None) for m in (1, 2, 3)]
        + [({"dp": 1 - c}, None), ({"context": z + 1}, z < nc - 1), ({"context": z - 1}, z > 0)]
    )
    q_all[e, z, c] = q_shard[...]
    o_all[e, z, c] = o_shard[...]
    cot_all[0] = cot_ref[...]

    gather_q = RowsGather(wire, q_all, e, z, c, nc, 1024)
    gather_o = RowsGather(wire, o_all, e, z, c, nc, 768)
    gather_cot = PlaneGather(wire, cot_all, e)
    gather_q.run()
    gather_o.step()

    small = q_all[:, :, :, :, pl.ds(query_width + kv_width, SMALL)].reshape(width, SMALL)
    small = jnp.transpose(small.astype(F32))
    gain_first, gain_second = small[experts : experts + 1], small[experts + 1 : experts + 2]
    gains_ref[0:1] = gain_first
    gains_ref[1:2] = gain_second
    rows = x_ref[...].astype(F32)
    scale1 = lax.rsqrt(jnp.mean(rows * rows, -1, keepdims=True) + EPSILON)
    inputs_ref[...] = (rows * scale1 * gain_first).astype(BF16)

    def project(first, count):
        weight = q_all[:, :, :, :, pl.ds(first, count)].reshape(width, count)
        qkv_scr[:, pl.ds(first, count)] = dot_nn(inputs_ref[...], weight)

    project(query_width, kv_width)

    def turned(column):
        head = qkv_scr[:, pl.ds(column, size)]
        return (head * cos_ref[...] + swap_halves(head) * sin_ref[...]).astype(BF16)

    for j in range(KEY_VALUE_HEADS):
        kv_ref[z, :, pl.ds(j * size, size)] = turned(query_width + j * size)
    values = pl.ds(kv_width // 2, kv_width // 2)
    kv_ref[z, :, values] = qkv_scr[:, pl.ds(query_width + kv_width // 2, kv_width // 2)].astype(
        BF16
    )
    line = wire.slots(nc)
    wire.start(kv_ref.at[z], kv_ref.at[z], line, {"context": z + 1}, when=z < nc - 1)
    for later in range(1, nc):

        def clear(later=later):
            kv_ref[z + later] = jnp.zeros(kv_ref.shape[1:], BF16)

        pl.when(z + later < nc)(clear)
    gather_o.step()

    @pl.loop(0, query_width // 256)
    def _(n):
        project(pl.multiple_of(n * 256, 256), 256)

    gather_o.step()
    project(query_width + kv_width, SMALL)
    gather_o.step()

    @pl.loop(0, QUERY_HEADS)
    def _(h):
        column = pl.multiple_of(h * size, size)
        query_ref[:, pl.ds(column, size)] = turned(column)

    gather_o.step()

    logits = qkv_scr[:, pl.ds(query_width + kv_width, SMALL)]
    lanes = lax.broadcasted_iota(jnp.int32, logits.shape, 1)
    named = lanes == routes_ref[:, 0:1]
    for k in range(1, TOP):
        named = named | (lanes == routes_ref[:, k : k + 1])
    logits = jnp.where(named, logits, MASKED)
    expd = jnp.exp(logits - jnp.max(logits, -1, keepdims=True))
    gates = expd / jnp.sum(expd, -1, keepdims=True)
    gate_all[0] = jnp.transpose(gates)[:GATE_ROWS]
    gate_slot = wire.slots(3)
    for r in (1, 2, 3):
        wire.start(gate_all.at[0], gate_all.at[r], gate_slot + r - 1, ids[r])

    gather_o.step()
    for step in range(1, nc):

        def pass_on(step=step):
            block = kv_ref.at[z - step]
            wire.arrived(block, line + step - 1, {"context": z - 1})

        pl.when(z >= step)(pass_on)
        wire.start(
            kv_ref.at[z - step],
            kv_ref.at[z - step],
            line + step,
            {"context": z + 1},
            when=(z >= step) & (z < nc - 1),
        )
        gather_o.step()
    gather_o.step()
    gather_o.step()

    length = nc * tokens
    group = QUERY_HEADS // KEY_VALUE_HEADS
    group_steps = 3
    for first in range(0, QUERY_HEADS, group_steps):
        j = first // group
        key = kv_ref[:, :, pl.ds(j * size, size)].reshape(length, size)
        value = kv_ref[:, :, pl.ds(kv_width // 2 + j * size, size)].reshape(length, size)

        @pl.loop(first, first + group_steps)
        def _(h):
            column = pl.multiple_of(h * size, size)
            scores = dot_nt(query_ref[:, pl.ds(column, size)], key) * (size**-0.5)
            row = z * tokens + lax.broadcasted_iota(jnp.int32, scores.shape, 0)
            place = lax.broadcasted_iota(jnp.int32, scores.shape, 1)
            scores = jnp.where(place <= row, scores, MASKED)
            expd = jnp.exp(scores - jnp.max(scores, -1, keepdims=True))
            total = jnp.sum(expd, -1, keepdims=True)
            mixed = dot_nn(expd.astype(BF16), value) / total
            heads_ref[:, pl.ds(column, size)] = mixed.astype(BF16)

        gather_o.step()
        gather_o.step()
        if first == 0:
            gather_o.run()
            gather_cot.step()
        else:
            gather_cot.step()

    gather_o.run()
    part = width // q_all.shape[0]
    for block in range(q_all.shape[0]):
        weight = o_all[block].reshape(part, width)
        columns = pl.ds(block * part, part)
        hidden_ref[:, columns] = x_ref[:, columns].astype(F32) + dot_nt(heads_ref[...], weight)
    hidden = hidden_ref[...]
    scale2 = lax.rsqrt(jnp.mean(hidden * hidden, -1, keepdims=True) + EPSILON)
    expert_in_ref[...] = (hidden * scale2 * gain_second).astype(BF16)
    gather_cot.run()
    for r in (1, 2, 3):
        wire.arrived(gate_all.at[r], gate_slot + r - 1, ids[r])
    wire.finish()


def front(x, q_shard, o_shard, cot, cosine, sine, routes, sizes):
    ne, nc, nd = sizes
    tokens, width = x.shape
    rows, q_width = q_shard.shape
    shapes = [
        ((ne, nc, nd, rows, q_width), BF16),
        ((ne, nc, nd, rows, width), BF16),
        ((ne, tokens, width), BF16),
        ((ne, GATE_ROWS, tokens), F32),
        ((tokens, width), BF16),
        ((tokens, QUERY_HEADS * HEAD_DIMENSION), BF16),
        ((nc, tokens, 2 * KEY_VALUE_HEADS * HEAD_DIMENSION), BF16),
        ((tokens, QUERY_HEADS * HEAD_DIMENSION), BF16),
        ((tokens, width), F32),
        ((tokens, width), BF16),
        ((8, width), F32),
    ]
    copies = 128
    return pl.pallas_call(
        functools.partial(front_kernel, nc, EXP_DEV * ne),
        out_shape=[jax.ShapeDtypeStruct(*s) for s in shapes],
        in_specs=[pl.BlockSpec(memory_space=pltpu.VMEM)] * 7,
        out_specs=[pl.BlockSpec(memory_space=pltpu.VMEM)] * len(shapes),
        scratch_shapes=[
            pltpu.VMEM((tokens, q_width), F32),
            pltpu.SemaphoreType.DMA((copies,)),
            pltpu.SemaphoreType.DMA((copies,)),
        ],
        compiler_params=pltpu.CompilerParams(
            collective_id=0, has_side_effects=True, vmem_limit_bytes=56 * MIB
        ),
    )(x, q_shard, o_shard, cot, cosine, sine, routes)


class PlaneScatter:
    def __init__(self, wire, part, land, e):
        self.wire, self.part, self.land = wire, part, land
        self.half = part.shape[-1] // 2
        self.ids = plane_ids(e)
        self.first = wire.slots(6)

    def at(self, r, half):
        return self.part.at[r - 1, :, pl.ds(half * self.half, self.half)]

    def send(self, r, half, mask, slot):
        self.wire.start(self.at(r, half), self.land.at[slot], self.first + slot, self.ids[mask])

    def near(self, r):
        self.send(r, r - 1, r, r - 1)

    def far(self):
        self.send(3, 0, 1, 2)
        self.send(3, 1, 2, 3)

    def relay(self):
        for half, r in ((0, 2), (1, 1)):
            slot = 2 + half
            self.wire.arrived(self.land.at[slot], self.first + slot, self.ids[3 - r])
            part = self.at(r, half)
            part[...] = (part[...].astype(F32) + self.land[slot].astype(F32)).astype(BF16)
            self.send(r, half, r, 4 + half)

    def total(self, own):
        for slot, half, mask in ((0, 0, 1), (1, 1, 2), (4, 0, 2), (5, 1, 1)):
            self.wire.arrived(self.land.at[slot], self.first + slot, self.ids[mask])
            columns = pl.ds(half * self.half, self.half)
            own[:, columns] += self.land[slot].astype(F32)


def experts_kernel(
    nc,
    x_ref,
    cot_all,
    gates_ref,
    w_gu,
    w_dn,
    mixture_ref,
    d_in_ref,
    d_gate_ref,
    grad_ref,
    x_all,
    a_all,
    dgu_all,
    y_part,
    dx_part,
    y_land,
    dx_land,
    dg_lanes,
    dg_part,
    dg_land,
    stage,
    sends,
    recvs,
    stage_sems,
):
    e = lax.axis_index("expert")
    tokens, width = x_ref.shape
    ff = w_dn.shape[1]
    blocks = x_all.shape[0]
    wire = Wire(sends, recvs)
    ids = plane_ids(e)
    greet([(ids[m], None) for m in (1, 2, 3)])
    x_all[0] = x_ref[...]
    gather = PlaneGather(wire, x_all, e)
    scatter_dx = PlaneScatter(wire, dx_part, dx_land, e)
    scatter_y = PlaneScatter(wire, y_part, y_land, e)
    dg_slot = wire.slots(3)
    gather.spread()
    step = 256
    wide = 512

    def block(r):
        dg_lanes[...] = jnp.zeros_like(dg_lanes)
        for i in range(EXP_DEV):

            @pl.loop(0, ff // step)
            def _(f):
                column = pl.multiple_of(f * step, step)
                rows, grads = x_all[r], cot_all[r]
                gate_part = dot_nn(rows, w_gu[i, :, pl.ds(column, step)])
                up_part = dot_nn(rows, w_gu[i, :, pl.ds(ff + column, step)])
                raw = dot_nt(grads, w_dn[i, pl.ds(column, step), :])
                gate = gates_ref[r][:, i : i + 1]
                sigma = jax.nn.sigmoid(gate_part)
                silu = gate_part * sigma
                act = silu * up_part
                lanes = lax.broadcasted_iota(jnp.int32, dg_lanes.shape, 1)
                dg_lanes[...] += jnp.where(
                    lanes == e * EXP_DEV + i, jnp.sum(act * raw, -1, keepdims=True), 0.0
                )
                a_all[r, :, pl.ds(i * ff + column, step)] = (act * gate).astype(BF16)
                d_act = raw * gate
                d_gate_part = d_act * up_part * sigma * (1.0 + gate_part * (1.0 - sigma))
                first = i * 2 * ff + column
                dgu_all[r, :, pl.ds(first, step)] = d_gate_part.astype(BF16)
                dgu_all[r, :, pl.ds(first + ff, step)] = (d_act * silu).astype(BF16)

        @pl.loop(0, width // wide)
        def _(n):
            columns = pl.ds(pl.multiple_of(n * wide, wide), wide)
            d_rows = dot_nt(dgu_all[r, :, pl.ds(0, 2 * ff)], w_gu[0, columns, :])
            d_rows += dot_nt(dgu_all[r, :, pl.ds(2 * ff, 2 * ff)], w_gu[1, columns, :])
            weight = w_dn[:, :, columns].reshape(EXP_DEV * ff, wide)
            out = dot_nn(a_all[r], weight)
            if r == 0:
                d_in_ref[:, columns] = d_rows
                mixture_ref[:, columns] = out
            else:
                dx_part[r - 1, :, columns] = d_rows.astype(BF16)
                y_part[r - 1, :, columns] = out.astype(BF16)

        dg_part[r] = jnp.transpose(dg_lanes[...])[:GATE_ROWS]
        if r:
            wire.start(dg_part.at[r], dg_land.at[r - 1], dg_slot + r - 1, ids[r])

    block(0)
    gather.forward()
    gather.near(1)
    block(1)
    scatter_dx.near(1)
    scatter_y.near(1)
    gather.near(2)
    block(2)
    scatter_dx.near(2)
    scatter_y.near(2)
    gather.far()
    block(3)
    scatter_dx.far()
    scatter_y.far()

    def keep(j, slot):
        return pltpu.make_async_copy(stage.at[slot], grad_ref.at[j], stage_sems.at[slot])

    def weight_grads(n):
        slot = n % 2
        if n >= 2:
            keep(n - 2, slot).wait()
        rows_of = width // nc
        columns = pl.ds(n * rows_of, rows_of)
        for first, source, grad in (
            (0, x_all, dgu_all),
            (EXP_DEV * 2 * ff, cot_all, a_all),
        ):
            rows = source[:, :, columns].reshape(blocks * tokens, rows_of)

            @pl.loop(0, grad.shape[-1] // ff)
            def _(i):
                column = pl.multiple_of(i * ff, ff)
                part = grad[:, :, pl.ds(column, ff)].reshape(blocks * tokens, ff)
                stage[slot, :, pl.ds(first + column, ff)] = dot_tn(rows, part).astype(BF16)

        keep(n, slot).start()

    weight_grads(0)
    scatter_dx.relay()
    for n in range(1, nc - 1):
        weight_grads(n)
    scatter_y.relay()
    weight_grads(nc - 1)
    scatter_dx.total(d_in_ref)
    scatter_y.total(mixture_ref)
    total = dg_part[0]
    for r in (1, 2, 3):
        wire.arrived(dg_land.at[r - 1], dg_slot + r - 1, ids[r])
        total = total + dg_land[r - 1]
    d_gate_ref[...] = total
    for n in range(nc - 2, nc):
        keep(n, n % 2).wait()
    wire.finish()


def experts(expert_in, cot_all, gates, w_gate_up, w_down, nc):
    blocks, tokens, width = cot_all.shape
    held, ff = w_down.shape[0], w_down.shape[1]
    grads = held * 3 * ff
    shapes = [
        ((tokens, width), F32),
        ((tokens, width), F32),
        ((GATE_ROWS, tokens), F32),
        ((nc, width // nc, grads), BF16),
    ]
    copies = 32
    vmem = pl.BlockSpec(memory_space=pltpu.VMEM)
    anywhere = pl.BlockSpec(memory_space=pl.ANY)
    return pl.pallas_call(
        functools.partial(experts_kernel, nc),
        out_shape=[jax.ShapeDtypeStruct(*s) for s in shapes],
        in_specs=[vmem] * 5,
        out_specs=[vmem] * 3 + [anywhere],
        scratch_shapes=[
            pltpu.VMEM((blocks, tokens, width), BF16),
            pltpu.VMEM((blocks, tokens, held * ff), BF16),
            pltpu.VMEM((blocks, tokens, held * 2 * ff), BF16),
            pltpu.VMEM((blocks - 1, tokens, width), BF16),
            pltpu.VMEM((blocks - 1, tokens, width), BF16),
            pltpu.VMEM((6, tokens, width // 2), BF16),
            pltpu.VMEM((6, tokens, width // 2), BF16),
            pltpu.VMEM((tokens, SMALL), F32),
            pltpu.VMEM((blocks, GATE_ROWS, tokens), F32),
            pltpu.VMEM((blocks - 1, GATE_ROWS, tokens), F32),
            pltpu.VMEM((2, width // nc, grads), BF16),
            pltpu.SemaphoreType.DMA((copies,)),
            pltpu.SemaphoreType.DMA((copies,)),
            pltpu.SemaphoreType.DMA((2,)),
        ],
        compiler_params=pltpu.CompilerParams(
            collective_id=1, has_side_effects=True, vmem_limit_bytes=60 * MIB
        ),
    )(expert_in, cot_all, gates, w_gate_up, w_down)


class LineScatter:
    def __init__(self, wire, block, lands, z, nc, up=True):
        self.wire, self.block, self.lands, self.z, self.nc = wire, block, lands, z, nc
        self.up = up
        self.first = [wire.slots(nc - 1), wire.slots(nc - 1)]

    def arrive(self, way, index, j):
        land = self.lands[way].at[index]
        self.wire.arrived(land, self.first[way] + index, {"context": self.z})
        block = self.block(j)
        block[...] = (block[...].astype(F32) + self.lands[way][index].astype(F32)).astype(BF16)

    def move(self, way, j):
        z, nc = self.z, self.nc
        inner, index, near = ((z > 0), j - z, z + 1) if way == 0 else ((z < nc - 1), z - j, z - 1)
        wanted = (j > z) if way == 0 else (j < z)
        pl.when(wanted & inner)(lambda: self.arrive(way, index, j))
        self.wire.start(
            self.block(j),
            self.lands[way].at[index - 1],
            self.first[way] + index - 1,
            {"context": near},
            when=wanted,
        )

    def step(self, s):
        if self.up:
            self.move(0, self.nc - s)
        self.move(1, s - 1)

    def last(self):
        if self.up:
            pl.when(self.z > 0)(lambda: self.arrive(0, 0, self.z))
        pl.when(self.z < self.nc - 1)(lambda: self.arrive(1, 0, self.z))


class RowsScatter:
    def __init__(self, wire, buf, core, plane, lines, e, z, c, nc, width, half):
        self.wire, self.buf, self.core, self.plane = wire, buf, core, plane
        self.e, self.z, self.c, self.width = e, z, c, width
        self.cols = (pl.ds(0, half), pl.ds(half, width - half))
        self.sizes = (half, width - half)
        self.ids = plane_ids(e)
        self.core_slot = wire.slots(1)
        self.first = wire.slots(6)
        self.line = LineScatter(
            wire,
            lambda j: buf.at[c, e, j, :, pl.ds(0, width)],
            [lines.at[0], lines.at[1]],
            z,
            nc,
        )

    def share(self):
        self.wire.start(
            self.buf.at[1 - self.c, :, :, :, pl.ds(0, self.width)],
            self.core,
            self.core_slot,
            {"dp": 1 - self.c},
        )

    def land(self, slot, half):
        return self.plane.at[slot, :, :, pl.ds(0, self.sizes[half])]

    def at(self, r, half):
        return self.buf.at[self.c, flip(self.e, r), :, :, self.cols[half]]

    def send(self, r, half, mask, slot):
        self.wire.start(
            self.at(r, half), self.land(slot, half), self.first + slot, self.ids[mask]
        )

    def merge(self):
        self.wire.arrived(self.core, self.core_slot, {"dp": 1 - self.c})
        for r in (3, 1, 2, 0):
            block = flip(self.e, r)
            part = self.buf.at[self.c, block, :, :, pl.ds(0, self.width)]
            part[...] = (part[...].astype(F32) + self.core[block].astype(F32)).astype(BF16)
            if r == 3:
                self.send(3, 0, 1, 2)
                self.send(3, 1, 2, 3)
            elif r:
                self.send(r, r - 1, r, r - 1)

    def add(self, r, half, slot, mask):
        land = self.land(slot, half)
        self.wire.arrived(land, self.first + slot, self.ids[mask])
        part = self.at(r, half)
        part[...] = (part[...].astype(F32) + land[...].astype(F32)).astype(BF16)

    def relay(self):
        for half, r in ((0, 2), (1, 1)):
            self.add(r, half, 2 + half, 3 - r)
            self.send(r, half, r, 4 + half)

    def total(self):
        for slot, half, mask in ((0, 0, 1), (1, 1, 2), (4, 0, 2), (5, 1, 1)):
            self.add(0, half, slot, mask)


def tail_kernel(
    nc,
    experts,
    x_ref,
    inputs_ref,
    query_ref,
    kv_ref,
    heads_ref,
    hidden_ref,
    cot_ref,
    d_in_ref,
    gate_ref,
    d_gate_ref,
    gains_ref,
    cos_ref,
    sin_ref,
    q_hbm,
    o_hbm,
    d_x_ref,
    sum_q_ref,
    sum_o_ref,
    weight,
    grads,
    core_o,
    core_q,
    plane_o,
    plane_q,
    lines_o,
    lines_q,
    d_hidden_ref,
    d_attn_ref,
    d_heads_ref,
    d_all_ref,
    d_inputs_ref,
    rows_ref,
    dkv_acc,
    dkv_ref,
    dkv_land,
    sends,
    recvs,
    sends_o,
    recvs_o,
    local_sems,
):
    e, z, c = (lax.axis_index(a) for a in ("expert", "context", "dp"))
    size = HEAD_DIMENSION
    tokens, width = x_ref.shape
    query_width = QUERY_HEADS * size
    key_width = KEY_VALUE_HEADS * size
    qkv_width = query_width + 2 * key_width
    planes = weight.shape[0]
    part = width // planes
    wire, wire_o = Wire(sends, recvs), Wire(sends_o, recvs_o)
    ids = plane_ids(e)
    greet(
        [(ids[m], None) for m in (1, 2)]
        + [({"dp": 1 - c}, None), ({"context": z + 1}, z < nc - 1), ({"context": z - 1}, z > 0)]
    )
    load_o = pltpu.make_async_copy(
        o_hbm, weight.at[:, :, :, :, pl.ds(0, width)], local_sems.at[4]
    )
    load_o.start()
    scatter_o = RowsScatter(wire_o, grads, core_o, plane_o, lines_o, e, z, c, nc, width, 768)
    scatter_q = RowsScatter(
        wire, grads, core_q, plane_q, lines_q, e, z, c, nc, qkv_width + SMALL, 1024
    )
    scatter_kv = LineScatter(
        wire, lambda j: dkv_ref.at[j], [dkv_land, dkv_land], z, nc, up=False
    )

    hidden, d_in = hidden_ref[...], d_in_ref[...]
    scale2 = lax.rsqrt(jnp.mean(hidden * hidden, -1, keepdims=True) + EPSILON)
    scaled = d_in * gains_ref[1:2]
    mean = jnp.mean(scaled * hidden, -1, keepdims=True)
    d_hidden = cot_ref[...].astype(F32) + scale2 * scaled - hidden * (scale2 * scale2 * scale2 * mean)
    d_hidden_ref[...] = d_hidden
    d_attn_ref[...] = d_hidden.astype(BF16)
    rows_ref[...] = jnp.zeros_like(rows_ref)
    rows_ref[experts + 1 : experts + 2, :] = jnp.sum(d_in * hidden * scale2, 0, keepdims=True)

    @pl.loop(0, planes)
    def _(block):
        columns = pl.ds(pl.multiple_of(block * part, part), part)
        result = dot_tn(d_attn_ref[:, columns], heads_ref[...]).astype(BF16)
        result = result.reshape(nc, 2, part // nc // 2, width)
        for half in range(2):
            grads[half, block, :, :, pl.ds(0, width)] = result[:, half]

    scatter_o.share()
    load_o.wait()

    @pl.loop(0, query_width // 256)
    def _(n):
        columns = pl.ds(pl.multiple_of(n * 256, 256), 256)
        out = weight[:, :, :, :, columns].reshape(width, 256)
        d_heads_ref[:, columns] = dot_nn(d_attn_ref[...], out).astype(BF16)

    load_q = pltpu.make_async_copy(q_hbm, weight, local_sems.at[4])
    load_q.start()
    scatter_o.merge()

    length = nc * tokens
    group = QUERY_HEADS // KEY_VALUE_HEADS
    dkv_acc[...] = jnp.zeros_like(dkv_acc)
    for j in range(KEY_VALUE_HEADS):
        key_columns, value_columns = pl.ds(j * size, size), pl.ds(key_width + j * size, size)
        key = kv_ref[:, :, key_columns].reshape(length, size)
        value = kv_ref[:, :, value_columns].reshape(length, size)

        @pl.loop(j * group, (j + 1) * group)
        def _(h):
            columns = pl.ds(pl.multiple_of(h * size, size), size)
            query, grad = query_ref[:, columns], d_heads_ref[:, columns]
            probs = masked_probs(z * tokens, query, key)
            d_probs = dot_nt(grad, value)
            inner = jnp.sum(probs * d_probs, axis=-1, keepdims=True)
            d_raw = (probs * (d_probs - inner) * (size**-0.5)).astype(BF16)
            d_query = dot_nn(d_raw, key)
            d_query = d_query * cos_ref[...] - swap_halves(d_query) * sin_ref[...]
            d_all_ref[:, columns] = d_query.astype(BF16)
            dkv_acc[:, key_columns] += dot_tn(d_raw, query)
            dkv_acc[:, value_columns] += dot_tn(probs.astype(BF16), grad)

        if j == 0:
            scatter_o.relay()
    for j in range(nc):
        dkv_ref[j] = dkv_acc[pl.ds(j * tokens, tokens), :].astype(BF16)
    scatter_kv.step(1)
    scatter_o.total()
    scatter_o.line.step(1)
    scatter_kv.step(2)
    scatter_o.line.step(2)
    for s in range(3, nc):
        scatter_kv.step(s)
        scatter_o.line.step(s)
    scatter_kv.last()

    for h in range(KEY_VALUE_HEADS):
        grad = dkv_ref[z, :, pl.ds(h * size, size)].astype(F32)
        grad = grad * cos_ref[...] - swap_halves(grad) * sin_ref[...]
        d_all_ref[:, pl.ds(query_width + h * size, size)] = grad.astype(BF16)
    values = pl.ds(key_width, key_width)
    d_all_ref[:, pl.ds(query_width + key_width, key_width)] = dkv_ref[z, :, values]

    gates = gate_ref[...]
    d_gates = d_gate_ref[...]
    d_logits = gates * (d_gates - jnp.sum(gates * d_gates, 0, keepdims=True))
    d_logits = jnp.concatenate(
        [d_logits, jnp.zeros((SMALL - d_logits.shape[0], tokens), F32)], 0
    )
    d_all_ref[:, pl.ds(qkv_width, SMALL)] = jnp.transpose(d_logits).astype(BF16)

    load_q.wait()
    for block in range(planes):
        rows = weight[block].reshape(part, qkv_width + SMALL)
        d_inputs_ref[:, pl.ds(block * part, part)] = dot_nt(d_all_ref[...], rows)
    rows = x_ref[...].astype(F32)
    scale1 = lax.rsqrt(jnp.mean(rows * rows, -1, keepdims=True) + EPSILON)
    d_inputs = d_inputs_ref[...]
    rows_ref[experts : experts + 1, :] = jnp.sum(d_inputs * rows * scale1, 0, keepdims=True)
    scatter_o.line.last()
    sum_o_ref[...] = grads[c, e, z, :, pl.ds(0, width)].astype(F32)
    wire_o.finish()

    @pl.loop(0, planes)
    def _(block):
        columns = pl.ds(pl.multiple_of(block * part, part), part)
        left = inputs_ref[:, columns]
        extra = jnp.transpose(rows_ref[:, columns])
        for first, count in ((0, 1024), (1024, qkv_width - 1024), (qkv_width, SMALL)):
            result = dot_tn(left, d_all_ref[:, pl.ds(first, count)])
            if first == qkv_width:
                result = result + extra
            result = result.astype(BF16).reshape(nc, 2, part // nc // 2, count)
            for half in range(2):
                grads[half, block, :, :, pl.ds(first, count)] = result[:, half]

    scatter_q.share()
    scaled = d_inputs_ref[...] * gains_ref[0:1]
    rows = x_ref[...].astype(F32)
    scale1 = lax.rsqrt(jnp.mean(rows * rows, -1, keepdims=True) + EPSILON)
    mean = jnp.mean(scaled * rows, -1, keepdims=True)
    d_x = d_hidden_ref[...] + scale1 * scaled - rows * (scale1 * scale1 * scale1 * mean)
    d_x_ref[...] = d_x.astype(BF16)
    scatter_q.merge()
    scatter_q.relay()
    scatter_q.total()
    for s in range(1, nc):
        scatter_q.line.step(s)
    scatter_q.line.last()
    sum_q_ref[...] = grads[c, e, z].astype(F32)
    wire.finish()


def tail(operands, sizes):
    ne, nc, nd = sizes
    x, inputs1, query, kv = operands[:4]
    q_all = operands[13]
    tokens, width = x.shape
    rows, q_width = q_all.shape[-2:]
    kv_width = kv.shape[-1]
    shapes = [
        ((tokens, width), BF16),
        ((rows, q_width), F32),
        ((rows, width), F32),
    ]
    copies = 64
    vmem = pl.BlockSpec(memory_space=pltpu.VMEM)
    anywhere = pl.BlockSpec(memory_space=pl.ANY)
    return pl.pallas_call(
        functools.partial(tail_kernel, nc, EXP_DEV * ne),
        out_shape=[jax.ShapeDtypeStruct(*s) for s in shapes],
        in_specs=[vmem] * 13 + [anywhere] * 2,
        out_specs=[vmem] * 3,
        scratch_shapes=[
            pltpu.VMEM((ne, nc, nd, rows, q_width), BF16),
            pltpu.VMEM((nd, ne, nc, rows, q_width), BF16),
            pltpu.VMEM((ne, nc, rows, width), BF16),
            pltpu.VMEM((ne, nc, rows, q_width), BF16),
            pltpu.VMEM((6, nc, rows, 768), BF16),
            pltpu.VMEM((6, nc, rows, q_width - 1024), BF16),
            pltpu.VMEM((2, nc - 1, rows, width), BF16),
            pltpu.VMEM((2, nc - 1, rows, q_width), BF16),
            pltpu.VMEM((tokens, width), F32),
            pltpu.VMEM((tokens, width), BF16),
            pltpu.VMEM((tokens, width), BF16),
            pltpu.VMEM((tokens, q_width), BF16),
            pltpu.VMEM((tokens, width), F32),
            pltpu.VMEM((SMALL, width), F32),
            pltpu.VMEM((nc * tokens, kv_width), F32),
            pltpu.VMEM((nc, tokens, kv_width), BF16),
            pltpu.VMEM((nc - 1, tokens, kv_width), BF16),
            pltpu.SemaphoreType.DMA((copies,)),
            pltpu.SemaphoreType.DMA((copies,)),
            pltpu.SemaphoreType.DMA((32,)),
            pltpu.SemaphoreType.DMA((32,)),
            pltpu.SemaphoreType.DMA((5,)),
        ],
        compiler_params=pltpu.CompilerParams(
            collective_id=2, has_side_effects=True, vmem_limit_bytes=62 * MIB
        ),
    )(*operands)


def local_plain(
    layer_input,
    gain_attn,
    query_key_value_weight,
    w_out,
    w_router,
    gain_ffn,
    w_gate_up,
    w_down,
    routes,
    d_out,
):
    tokens = layer_input.shape[1]
    model_width = layer_input.shape[2]
    ne, nc, nd = (lax.axis_size(a) for a in ("expert", "context", "dp"))
    expert_total = EXP_DEV * ne
    ff = w_down.shape[1]
    me = lax.axis_index("expert")
    first_row = lax.axis_index("context") * tokens
    query_width = QUERY_HEADS * HEAD_DIMENSION
    key_width = KEY_VALUE_HEADS * HEAD_DIMENSION
    qkv_width = query_width + 2 * key_width

    small = jnp.concatenate([w_router, gain_attn[:, None], gain_ffn[:, None]], -1)
    small = jnp.pad(small, ((0, 0), (0, 128 - small.shape[1])))
    gathered = gather_rows(jnp.concatenate([query_key_value_weight, small], -1))
    out_turned = gather_rows(w_out.T)
    qkv_weight = gathered[:, :qkv_width]
    router_weight = gathered[:, qkv_width : qkv_width + expert_total]
    gains = gathered[:, qkv_width + expert_total : qkv_width + expert_total + 2].T.astype(F32)
    gain_first, gain_second = gains[0], gains[1]
    cotangent_all = plane_gather(d_out[0])

    token_rows = layer_input[0].astype(F32)
    scale1 = lax.rsqrt(jnp.mean(token_rows * token_rows, -1, keepdims=True) + EPSILON)
    inputs1 = (token_rows * scale1 * gain_first).astype(BF16)
    query_key_value = dot_nn(inputs1, qkv_weight)
    cosine_values, sine_values = rope_tables(first_row + jnp.arange(tokens), HEAD_DIMENSION)
    rotated = rotate_half(
        query_key_value[:, : query_width + key_width].reshape(tokens, -1, HEAD_DIMENSION),
        cosine_values,
        sine_values,
    ).reshape(tokens, -1)
    query = rotated[:, :query_width].astype(BF16)
    key_value_local = jnp.concatenate(
        [rotated[:, query_width:], query_key_value[:, query_width + key_width :]], -1
    ).astype(BF16)
    key_value = line_gather(key_value_local, "context", both=False).reshape(nc * tokens, -1)
    first = first_row.astype(jnp.int32).reshape(1)
    heads = attend_forward(first, query, key_value)

    logits = dot_nn(inputs1, router_weight)
    chosen_ids = routes[0]
    picks = (chosen_ids[:, :, None] == jnp.arange(expert_total)[None, None, :]).astype(F32)
    chosen = jnp.sum(picks * logits[:, None, :], -1)
    gates = jax.nn.softmax(chosen, axis=-1)
    gate_dense = jnp.sum(picks * gates[:, :, None], 1).T
    gate_blocks = cube_gather(gate_dense, "expert", axis_masks("expert"))
    gate_local = jnp.concatenate(
        [lax.dynamic_slice_in_dim(b, me * EXP_DEV, EXP_DEV, 0) for b in gate_blocks], 1
    )

    attn = dot_nt(heads, out_turned)
    hidden = token_rows + attn
    scale2 = lax.rsqrt(jnp.mean(hidden * hidden, -1, keepdims=True) + EPSILON)
    expert_in = (hidden * scale2 * gain_second).astype(BF16)

    rows_all = plane_gather(expert_in)
    gate_up = jnp.einsum("td,edf->etf", rows_all, w_gate_up, preferred_element_type=F32)
    gate_part, up_part = gate_up[..., :ff], gate_up[..., ff:]
    sigma = jax.nn.sigmoid(gate_part)
    silu = gate_part * sigma
    act = silu * up_part
    gate_column = gate_local[:, :, None]
    act_gated = (act * gate_column).astype(BF16)
    partial_out = jnp.einsum("etf,efd->td", act_gated, w_down, preferred_element_type=F32)
    mixture = plane_scatter(partial_out.astype(BF16), tokens)
    layer_result = (hidden + mixture).astype(BF16)

    d_act_raw = jnp.einsum("td,efd->etf", cotangent_all, w_down, preferred_element_type=F32)
    d_gates_local = jnp.sum(d_act_raw * act, -1)
    d_act = d_act_raw * gate_column
    d_gate_part = d_act * up_part * sigma * (1.0 + gate_part * (1.0 - sigma))
    d_up_part = d_act * silu
    d_gate_up = jnp.concatenate([d_gate_part, d_up_part], -1).astype(BF16)
    d_rows = jnp.einsum("etf,edf->td", d_gate_up, w_gate_up, preferred_element_type=F32)
    grad_down = jnp.einsum("td,etf->edf", cotangent_all, act_gated, preferred_element_type=F32)
    grad_gate_up = jnp.einsum("td,etf->edf", rows_all, d_gate_up, preferred_element_type=F32)

    d_expert_in = plane_scatter(d_rows.astype(BF16), tokens)
    d_gate_blocks = d_gates_local.reshape(EXP_DEV, ne, tokens)
    d_gates_dense = jnp.zeros((expert_total, tokens), F32)
    for r in range(ne):
        arrived = d_gate_blocks[:, r]
        if r:
            arrived = exchange(arrived, "expert", r)
        d_gates_dense = lax.dynamic_update_slice(d_gates_dense, arrived, ((me ^ r) * EXP_DEV, 0))
    d_gates = jnp.sum(picks * d_gates_dense.T[:, None, :], -1)
    d_chosen = gates * (d_gates - jnp.sum(gates * d_gates, -1, keepdims=True))
    d_logits = jnp.sum(picks * d_chosen[:, :, None], 1).astype(BF16)
    grad_router = dot_tn(inputs1, d_logits)

    core = lax.axis_index("dp")
    part = model_width // (nc * nd)

    def scatter_experts(grad):
        blocks = grad.reshape(EXP_DEV, nc, nd, part, -1)
        mine = cube_scatter(
            [lax.dynamic_index_in_dim(blocks, core ^ r, 2, keepdims=False) for r in range(nd)],
            "dp",
            axis_masks("dp"),
        )
        return line_scatter(
            lambda j: lax.dynamic_index_in_dim(mine, j, 1, keepdims=False), "context"
        )

    sum_gate_up = scatter_experts(grad_gate_up)
    sum_down = jnp.swapaxes(scatter_experts(grad_down), 1, 2)

    cotangent = d_out[0].astype(F32)
    scaled2 = d_expert_in * gain_second
    d_hidden = (
        cotangent
        + scale2 * scaled2
        - hidden * (scale2 * scale2 * scale2) * jnp.mean(scaled2 * hidden, -1, keepdims=True)
    )
    grad_gain_second = jnp.sum(d_expert_in * hidden * scale2, 0)
    d_attn = d_hidden.astype(BF16)
    grad_out_turned = dot_tn(d_attn, heads)
    sum_out = scatter_rows(grad_out_turned).T
    d_heads = dot_nn(d_attn, out_turned).astype(BF16)
    d_query, d_key_all, d_value_all = attend_backward(first, query, key_value, d_heads)
    d_key_value_all = jnp.concatenate([d_key_all, d_value_all], -1).reshape(nc, tokens, -1)
    d_key_value = line_scatter(
        lambda j: lax.dynamic_index_in_dim(d_key_value_all, j, 0, keepdims=False),
        "context",
        up=False,
    )
    d_rotated = rotate_back(
        jnp.concatenate([d_query, d_key_value[:, :key_width]], -1).reshape(
            tokens, -1, HEAD_DIMENSION
        ),
        cosine_values,
        sine_values,
    ).reshape(tokens, -1)
    d_qkv = jnp.concatenate([d_rotated, d_key_value[:, key_width:]], -1).astype(BF16)
    d_inputs = dot_nt(d_qkv, qkv_weight) + dot_nt(d_logits, router_weight)
    grad_gain_first = jnp.sum(d_inputs * token_rows * scale1, 0)
    grad_qkv = dot_tn(inputs1, d_qkv)
    small_grads = jnp.concatenate(
        [grad_router, grad_gain_first[:, None], grad_gain_second[:, None]], -1
    )
    small_grads = jnp.pad(small_grads, ((0, 0), (0, 128 - small_grads.shape[1])))
    sum_rows = scatter_rows(jnp.concatenate([grad_qkv, small_grads], -1))
    sum_qkv = sum_rows[:, :qkv_width]
    sum_router = sum_rows[:, qkv_width : qkv_width + expert_total]
    sum_gain_first = sum_rows[:, qkv_width + expert_total]
    sum_gain_second = sum_rows[:, qkv_width + expert_total + 1]
    scaled1 = d_inputs * gain_first
    d_input_rows = (
        d_hidden
        + scale1 * scaled1
        - token_rows
        * (scale1 * scale1 * scale1)
        * jnp.mean(scaled1 * token_rows, -1, keepdims=True)
    ).astype(BF16)
    return (
        layer_result[None],
        d_input_rows[None],
        sum_gain_first,
        sum_qkv,
        sum_out,
        sum_router,
        sum_gain_second,
        sum_gate_up,
        sum_down,
    )


def local_fused(
    layer_input,
    gain_attn,
    query_key_value_weight,
    w_out,
    w_router,
    gain_ffn,
    w_gate_up,
    w_down,
    routes,
    d_out,
):
    tokens = layer_input.shape[1]
    ne, nc, nd = sizes = tuple(lax.axis_size(a) for a in ("expert", "context", "dp"))
    expert_total = EXP_DEV * ne
    ff = w_down.shape[1]
    me = lax.axis_index("expert")
    first_row = lax.axis_index("context") * tokens
    query_width = QUERY_HEADS * HEAD_DIMENSION
    key_width = KEY_VALUE_HEADS * HEAD_DIMENSION
    qkv_width = query_width + 2 * key_width

    small = jnp.concatenate([w_router, gain_attn[:, None], gain_ffn[:, None]], -1)
    small = jnp.pad(small, ((0, 0), (0, SMALL - small.shape[1])))
    cosine_values, sine_values = rope_tables(first_row + jnp.arange(tokens), HEAD_DIMENSION)
    sign = jnp.where(jnp.arange(HEAD_DIMENSION) < HEAD_DIMENSION // 2, -1.0, 1.0)
    (
        q_all,
        o_all,
        cotangent_all,
        gate_all,
        inputs1,
        query,
        key_value,
        heads,
        hidden,
        expert_in,
        gains,
    ) = front(
        layer_input[0],
        jnp.concatenate([query_key_value_weight, small], -1),
        w_out.T,
        d_out[0],
        cosine_values,
        sine_values * sign,
        routes[0],
        sizes,
    )
    gate_local = jnp.swapaxes(
        lax.dynamic_slice_in_dim(gate_all, me * EXP_DEV, EXP_DEV, 1), 1, 2
    )
    mixture, d_expert_in, d_gates, grad_experts = experts(
        expert_in, cotangent_all, gate_local, w_gate_up, w_down, nc
    )
    layer_result = (hidden + mixture).astype(BF16)
    sum_experts = lax.psum_scatter(
        grad_experts.reshape(-1, grad_experts.shape[-1]),
        ("context", "dp"),
        scatter_dimension=0,
        tiled=True,
    ).astype(F32)
    d_x, sum_rows, sum_out = tail(
        (
            layer_input[0],
            inputs1,
            query,
            key_value,
            heads,
            hidden,
            d_out[0],
            d_expert_in,
            gate_all[0],
            d_gates,
            gains,
            cosine_values,
            sine_values * sign,
            q_all,
            o_all,
        ),
        sizes,
    )
    sum_gate_up = jnp.stack([sum_experts[:, i * 2 * ff : (i + 1) * 2 * ff] for i in range(EXP_DEV)])
    sum_down = sum_experts[:, EXP_DEV * 2 * ff :].reshape(-1, EXP_DEV, ff)
    return (
        layer_result[None],
        d_x[None],
        sum_rows[:, qkv_width + expert_total],
        sum_rows[:, :qkv_width],
        sum_out.T,
        sum_rows[:, qkv_width : qkv_width + expert_total],
        sum_rows[:, qkv_width + expert_total + 1],
        sum_gate_up,
        jnp.transpose(sum_down, (1, 2, 0)),
    )


def solution(mesh):
    in_specs = (
        P(("expert", "dp"), "context", None),
        P(("expert", "context", "dp")),
        P(("expert", "context", "dp"), None),
        P(None, ("expert", "context", "dp")),
        P(("expert", "context", "dp"), None),
        P(("expert", "context", "dp")),
        P("expert", None, None),
        P("expert", None, None),
        P(("expert", "dp"), "context", None),
        P(("expert", "dp"), "context", None),
    )
    out_specs = (
        P(("expert", "dp"), "context", None),
        P(("expert", "dp"), "context", None),
        P(("expert", "context", "dp")),
        P(("expert", "context", "dp"), None),
        P(None, ("expert", "context", "dp")),
        P(("expert", "context", "dp"), None),
        P(("expert", "context", "dp")),
        P("expert", ("context", "dp"), None),
        P("expert", None, ("context", "dp")),
    )
    sizes = tuple(mesh.shape[a] for a in ("expert", "context", "dp"))
    local = local_fused if sizes[0] == 4 and sizes[2] == 2 else local_plain
    return jax.shard_map(local, mesh=mesh, in_specs=in_specs, out_specs=out_specs, check_vma=False)
```

```python
import functools
import math

import jax
import jax.numpy as jnp
from jax import lax
from jax.experimental import pallas as pl
from jax.experimental.pallas import tpu as pltpu
from jax.sharding import PartitionSpec as P

QUERY_HEADS = 12
KEY_VALUE_HEADS = 2
HEAD_DIMENSION = 128
TOP = 4
EXP_DEV = 2

EPSILON = 1e-06
ROPE_BASE = 10000.0
MASKED = -1e30

F32 = jnp.float32
BF16 = jnp.bfloat16


def rope_tables(positions, width):
    halfway = width // 2
    fraction = jnp.arange(halfway, dtype=jnp.float32) * (2.0 / width)
    frequency = jnp.exp(-math.log(ROPE_BASE) * fraction)
    angles = positions.astype(jnp.float32)[:, None] * frequency[None, :]
    cosine_values = jnp.cos(angles)
    sine_values = jnp.sin(angles)
    return (
        jnp.concatenate([cosine_values, cosine_values], -1),
        jnp.concatenate([sine_values, sine_values], -1),
    )


def rotate_half(values, cosine_values, sine_values):
    halfway = values.shape[-1] // 2
    turned = jnp.concatenate([-values[..., halfway:], values[..., :halfway]], -1)
    return values * cosine_values[:, None, :] + turned * sine_values[:, None, :]


def rotate_back(grads, cosine_values, sine_values):
    halfway = grads.shape[-1] // 2
    scaled = grads * sine_values[:, None, :]
    turned = jnp.concatenate([scaled[..., halfway:], -scaled[..., :halfway]], -1)
    return grads * cosine_values[:, None, :] + turned


def dot_nt(a, b):
    return lax.dot_general(a, b, (((1,), (1,)), ((), ())), preferred_element_type=F32)


def dot_tn(a, b):
    return lax.dot_general(a, b, (((0,), (0,)), ((), ())), preferred_element_type=F32)


def dot_nn(a, b):
    return jnp.dot(a, b, preferred_element_type=F32)


def masked_probs(first_row, query, key):
    scores = dot_nt(query, key) * (HEAD_DIMENSION**-0.5)
    rows = first_row + lax.broadcasted_iota(jnp.int32, scores.shape, 0)
    columns = lax.broadcasted_iota(jnp.int32, scores.shape, 1)
    scores = jnp.where(columns <= rows, scores, MASKED)
    expd = jnp.exp(scores - jnp.max(scores, axis=-1, keepdims=True))
    return expd / jnp.sum(expd, axis=-1, keepdims=True)


def attend_forward_kernel(first_ref, query_ref, key_ref, value_ref, heads_ref):
    probs = masked_probs(first_ref[0], query_ref[...], key_ref[...])
    heads_ref[...] = dot_nn(probs.astype(BF16), value_ref[...]).astype(BF16)


def attend_forward(first_row, query, key_value):
    tokens, width = query.shape
    length = key_value.shape[0]
    group = QUERY_HEADS // KEY_VALUE_HEADS
    size = HEAD_DIMENSION
    return pl.pallas_call(
        attend_forward_kernel,
        grid_spec=pltpu.PrefetchScalarGridSpec(
            num_scalar_prefetch=1,
            grid=(QUERY_HEADS,),
            in_specs=[
                pl.BlockSpec((tokens, size), lambda h, s: (0, h)),
                pl.BlockSpec((length, size), lambda h, s: (0, h // group)),
                pl.BlockSpec((length, size), lambda h, s: (0, KEY_VALUE_HEADS + h // group)),
            ],
            out_specs=pl.BlockSpec((tokens, size), lambda h, s: (0, h)),
        ),
        out_shape=jax.ShapeDtypeStruct((tokens, width), BF16),
        compiler_params=pltpu.CompilerParams(vmem_limit_bytes=32 * 1024 * 1024),
        cost_estimate=pl.CostEstimate(
            flops=4 * tokens * length * width, bytes_accessed=4 * tokens * width, transcendentals=0
        ),
    )(first_row, query, key_value, key_value)


def attend_backward_kernel(
    first_ref, query_ref, key_ref, value_ref, grad_ref, d_query_ref, d_key_ref, d_value_ref
):
    query, key, value, grad = query_ref[...], key_ref[...], value_ref[...], grad_ref[...]
    probs = masked_probs(first_ref[0], query, key)
    d_probs = dot_nt(grad, value)
    inner = jnp.sum(probs * d_probs, axis=-1, keepdims=True)
    d_raw = (probs * (d_probs - inner) * (HEAD_DIMENSION**-0.5)).astype(BF16)
    d_query_ref[...] = dot_nn(d_raw, key)
    d_key = dot_tn(d_raw, query)
    d_value = dot_tn(probs.astype(BF16), grad)

    @pl.when(pl.program_id(1) == 0)
    def _():
        d_key_ref[...] = d_key
        d_value_ref[...] = d_value

    @pl.when(pl.program_id(1) > 0)
    def _():
        d_key_ref[...] += d_key
        d_value_ref[...] += d_value


def attend_backward(first_row, query, key_value, grad):
    tokens, width = query.shape
    length = key_value.shape[0]
    group = QUERY_HEADS // KEY_VALUE_HEADS
    size = HEAD_DIMENSION
    row_spec = pl.BlockSpec((tokens, size), lambda j, g, s: (0, j * group + g))
    return pl.pallas_call(
        attend_backward_kernel,
        grid_spec=pltpu.PrefetchScalarGridSpec(
            num_scalar_prefetch=1,
            grid=(KEY_VALUE_HEADS, group),
            in_specs=[
                row_spec,
                pl.BlockSpec((length, size), lambda j, g, s: (0, j)),
                pl.BlockSpec((length, size), lambda j, g, s: (0, KEY_VALUE_HEADS + j)),
                row_spec,
            ],
            out_specs=[
                row_spec,
                pl.BlockSpec((length, size), lambda j, g, s: (0, j)),
                pl.BlockSpec((length, size), lambda j, g, s: (0, j)),
            ],
        ),
        out_shape=[
            jax.ShapeDtypeStruct((tokens, width), F32),
            jax.ShapeDtypeStruct((length, KEY_VALUE_HEADS * size), F32),
            jax.ShapeDtypeStruct((length, KEY_VALUE_HEADS * size), F32),
        ],
        compiler_params=pltpu.CompilerParams(vmem_limit_bytes=32 * 1024 * 1024),
        cost_estimate=pl.CostEstimate(
            flops=10 * tokens * length * width, bytes_accessed=8 * tokens * width, transcendentals=0
        ),
    )(first_row, query, key_value, key_value, grad)


def exchange(values, axis, mask):
    size = lax.axis_size(axis)
    return lax.ppermute(values, axis, [(i, i ^ mask) for i in range(size)])


def axis_masks(axis):
    size = lax.axis_size(axis)
    masks, bit = [], 1
    while bit < size:
        masks.append(bit)
        bit *= 2
    return masks


def cube_gather(values, axis, masks):
    held = {0: values}
    for mask in masks:
        for r, block in list(held.items()):
            held[r ^ mask] = exchange(block, axis, mask)
    return [held[r] for r in range(lax.axis_size(axis))]


def cube_scatter(blocks, axis, masks):
    held = dict(enumerate(blocks))
    for mask in masks:
        kept = {}
        for r in list(held):
            if not r & mask:
                arrived = exchange(held[r ^ mask].astype(BF16), axis, mask)
                kept[r] = held[r].astype(F32) + arrived.astype(F32)
        held = kept
    return held[0]


def line_steps(values, axis, up):
    size = lax.axis_size(axis)
    pairs = [(i, i + 1) if up else (i + 1, i) for i in range(size - 1)]
    return lax.ppermute(values, axis, pairs)


def line_gather(values, axis, both=True):
    size = lax.axis_size(axis)
    me = lax.axis_index(axis)
    result = jnp.zeros((size + 1,) + values.shape, values.dtype)
    result = lax.dynamic_update_index_in_dim(result, values, me, 0)
    up = down = values
    for step in range(1, size):
        up = line_steps(up, axis, True)
        result = lax.dynamic_update_index_in_dim(
            result, up, jnp.where(me - step >= 0, me - step, size), 0
        )
        if both:
            down = line_steps(down, axis, False)
            result = lax.dynamic_update_index_in_dim(result, down, jnp.minimum(me + step, size), 0)
    return result[:size]


def line_scatter(take, axis, up=True, down=True):
    size = lax.axis_size(axis)
    me = lax.axis_index(axis)
    total = take(me).astype(F32)
    for active, sign in ((up, 1), (down, -1)):
        if not active:
            continue
        arrived = None
        for step in range(1, size):
            block = take((me + sign * (size - step)) % size).astype(F32)
            if arrived is not None:
                block = block + arrived.astype(F32)
            arrived = line_steps(block.astype(BF16), axis, sign > 0)
        total = total + arrived.astype(F32)
    return total


def gather_rows(shard):
    ne, nc, nd = (lax.axis_size(a) for a in ("expert", "context", "dp"))
    rows, width = shard.shape
    lines = line_gather(shard, "context")
    masks = axis_masks("expert")
    half = width // 256 * 128
    parts = [lines[..., :half], lines[..., half:]]
    me = lax.axis_index("expert")
    result = jnp.zeros((ne, nc, rows, width), shard.dtype)
    for start, part, order in ((0, parts[0], masks), (half, parts[1], masks[::-1])):
        for r, block in enumerate(cube_gather(part, "expert", order)):
            result = lax.dynamic_update_slice(result, block[None], (me ^ r, 0, 0, start))
    core = lax.axis_index("dp")
    whole = jnp.zeros((ne, nc, nd, rows, width), shard.dtype)
    for r, block in enumerate(cube_gather(result, "dp", axis_masks("dp"))):
        whole = lax.dynamic_update_slice(whole, block[:, :, None], (0, 0, core ^ r, 0, 0))
    return whole.reshape(-1, width)


def scatter_rows(grad):
    ne, nc, nd = (lax.axis_size(a) for a in ("expert", "context", "dp"))
    width = grad.shape[-1]
    rows = grad.shape[0] // (ne * nc * nd)
    blocks = grad.reshape(ne, nc, nd, rows, width)
    core, me = lax.axis_index("dp"), lax.axis_index("expert")
    mine = cube_scatter(
        [
            lax.dynamic_index_in_dim(blocks, core ^ r, 2, keepdims=False)
            for r in range(nd)
        ],
        "dp",
        axis_masks("dp"),
    )
    masks = axis_masks("expert")
    half = width // 256 * 128
    sums = []
    for part, order in ((mine[..., :half], masks), (mine[..., half:], masks[::-1])):
        sums.append(
            cube_scatter(
                [lax.dynamic_index_in_dim(part, me ^ r, 0, keepdims=False) for r in range(ne)],
                "expert",
                order,
            )
        )
    lines = jnp.concatenate(sums, -1)
    return line_scatter(
        lambda j: lax.dynamic_index_in_dim(lines, j, 0, keepdims=False), "context"
    )


def plane_gather(rows):
    masks = axis_masks("expert")
    half = rows.shape[-1] // 2
    left = cube_gather(rows[:, :half], "expert", masks)
    right = cube_gather(rows[:, half:], "expert", masks[::-1])
    return jnp.concatenate([jnp.concatenate(p, -1) for p in zip(left, right)], 0)


def plane_scatter(partial, tokens):
    masks = axis_masks("expert")
    size = lax.axis_size("expert")
    half = partial.shape[-1] // 2
    blocks = partial.reshape(size, tokens, -1)
    left = cube_scatter([blocks[r, :, :half] for r in range(size)], "expert", masks)
    right = cube_scatter([blocks[r, :, half:] for r in range(size)], "expert", masks[::-1])
    return jnp.concatenate([left, right], -1)


MESH = pl.DeviceIdType.MESH
MIB = 1024 * 1024
SMALL = 128
GATE_ROWS = 16


def flip(index, mask):
    bit = 1
    while bit <= mask:
        if mask & bit:
            index = index + bit - 2 * bit * lax.rem(lax.div(index, bit), 2)
        bit *= 2
    return index


class Wire:
    def __init__(self, sends, recvs):
        self.sends, self.recvs = sends, recvs
        self.n_sends = self.n_recvs = 0
        self.open = []

    def slots(self, count):
        first = self.n_recvs
        self.n_recvs += count
        return first

    def start(self, src, dst, recv, device, when=None):
        copy = pltpu.make_async_remote_copy(
            src_ref=src,
            dst_ref=dst,
            send_sem=self.sends.at[self.n_sends],
            recv_sem=self.recvs.at[recv],
            device_id=device,
            device_id_type=MESH,
        )
        self.n_sends += 1
        guard(when, copy.start)
        self.open.append((when, copy))

    def arrived(self, dst, recv, device):
        pltpu.make_async_remote_copy(
            src_ref=dst,
            dst_ref=dst,
            send_sem=self.sends.at[0],
            recv_sem=self.recvs.at[recv],
            device_id=device,
            device_id_type=MESH,
        ).wait_recv()

    def finish(self):
        for when, copy in self.open:
            guard(when, copy.wait_send)
        self.open = []


def guard(when, action):
    if when is None:
        action()
    else:
        pl.when(when)(action)


def greet(targets):
    barrier = pltpu.get_barrier_semaphore()
    for device, when in targets:
        guard(
            when,
            lambda device=device: pl.semaphore_signal(
                barrier, inc=1, device_id=device, device_id_type=MESH
            ),
        )
    count = sum(1 if when is None else when.astype(jnp.int32) for _, when in targets)
    pl.semaphore_wait(barrier, count)


def plane_ids(e):
    return {m: {"expert": flip(e, m)} for m in (1, 2, 3)}


class RowsGather:
    def __init__(self, wire, ref, e, z, c, nc, half):
        self.wire, self.ref, self.e, self.z, self.c, self.nc = wire, ref, e, z, c, nc
        self.cols = (pl.ds(0, half), pl.ds(half, ref.shape[-1] - half))
        self.line = wire.slots(nc)
        self.plane = wire.slots(nc * 6)
        self.core = wire.slots(nc)
        self.ids = plane_ids(e)
        self.steps = []
        for k in range(nc):
            self.steps.append(functools.partial(self.spread, k))
            if k:
                self.steps.append(functools.partial(self.forward, k - 1))
            if k > 1:
                self.steps.append(functools.partial(self.share, k - 2))
        self.steps.append(functools.partial(self.forward, nc - 1))
        self.steps.append(functools.partial(self.share, nc - 2))
        self.steps.append(functools.partial(self.share, nc - 1))
        self.steps.append(self.complete)

    def at(self, r, zs, half):
        return self.ref.at[flip(self.e, r), zs, self.c, :, self.cols[half]]

    def slot(self, k, r, half):
        return self.plane + k * 6 + (r - 1) * 2 + half

    def spread(self, k):
        wire, z, nc = self.wire, self.z, self.nc
        zs = flip(z, k)
        whole = self.ref.at[self.e, zs, self.c]
        if k:
            wire.arrived(whole, self.line + zs, {"context": zs})
        wire.start(
            whole, whole, self.line + zs, {"context": z + 1}, when=(zs <= z) & (z < nc - 1)
        )
        wire.start(whole, whole, self.line + zs, {"context": z - 1}, when=(zs >= z) & (z > 0))
        for half, mask in ((0, 1), (1, 2), (1, 1), (0, 2)):
            part = self.at(0, zs, half)
            wire.start(part, part, self.slot(k, mask, half), self.ids[mask])

    def forward(self, k):
        zs = flip(self.z, k)
        for half, mask in ((0, 1), (1, 2)):
            part = self.at(mask, zs, half)
            self.wire.arrived(part, self.slot(k, mask, half), self.ids[mask])
            self.wire.start(part, part, self.slot(k, 3, half), self.ids[3 - mask])

    def share(self, k):
        zs = flip(self.z, k)
        for r, half in ((1, 1), (2, 0), (3, 0), (3, 1)):
            self.wire.arrived(self.at(r, zs, half), self.slot(k, r, half), self.ids[r])
        part = self.ref.at[:, zs, self.c]
        self.wire.start(part, part, self.core + k, {"dp": 1 - self.c})

    def complete(self):
        for k in range(self.nc):
            zs = flip(self.z, k)
            self.wire.arrived(self.ref.at[:, zs, 1 - self.c], self.core + k, {"dp": 1 - self.c})

    def step(self):
        if self.steps:
            self.steps.pop(0)()

    def run(self):
        while self.steps:
            self.step()


class PlaneGather:
    def __init__(self, wire, ref, e):
        self.wire, self.ref = wire, ref
        self.half = ref.shape[-1] // 2
        self.ids = plane_ids(e)
        self.first = wire.slots(6)
        self.steps = [self.spread, self.forward, self.complete]

    def at(self, r, half):
        return self.ref.at[r, :, pl.ds(half * self.half, self.half)]

    def slot(self, r, half):
        return self.first + (r - 1) * 2 + half

    def spread(self):
        for half, mask in ((0, 1), (1, 2), (1, 1), (0, 2)):
            self.wire.start(
                self.at(0, half), self.at(mask, half), self.slot(mask, half), self.ids[mask]
            )

    def forward(self):
        for half, mask in ((0, 1), (1, 2)):
            self.wire.arrived(self.at(mask, half), self.slot(mask, half), self.ids[mask])
            self.wire.start(
                self.at(mask, half), self.at(3, half), self.slot(3, half), self.ids[3 - mask]
            )

    def near(self, r):
        half = 1 if r == 1 else 0
        self.wire.arrived(self.at(r, half), self.slot(r, half), self.ids[r])

    def far(self):
        for half in (0, 1):
            self.wire.arrived(self.at(3, half), self.slot(3, half), self.ids[3])

    def complete(self):
        self.near(1)
        self.near(2)
        self.far()

    def step(self):
        if self.steps:
            self.steps.pop(0)()

    def run(self):
        while self.steps:
            self.step()


def swap_halves(values):
    return pltpu.roll(values, HEAD_DIMENSION // 2, 1)


def front_kernel(
    nc,
    experts,
    x_ref,
    q_shard,
    o_shard,
    cot_ref,
    cos_ref,
    sin_ref,
    routes_ref,
    q_all,
    o_all,
    cot_all,
    gate_all,
    inputs_ref,
    query_ref,
    kv_ref,
    heads_ref,
    hidden_ref,
    expert_in_ref,
    gains_ref,
    qkv_scr,
    sends,
    recvs,
):
    e, z, c = (lax.axis_index(a) for a in ("expert", "context", "dp"))
    size = HEAD_DIMENSION
    tokens, width = x_ref.shape
    query_width = QUERY_HEADS * size
    kv_width = 2 * KEY_VALUE_HEADS * size
    wire = Wire(sends, recvs)
    ids = plane_ids(e)
    greet(
        [(ids[m], None) for m in (1, 2, 3)]
        + [({"dp": 1 - c}, None), ({"context": z + 1}, z < nc - 1), ({"context": z - 1}, z > 0)]
    )
    q_all[e, z, c] = q_shard[...]
    o_all[e, z, c] = o_shard[...]
    cot_all[0] = cot_ref[...]

    gather_q = RowsGather(wire, q_all, e, z, c, nc, 1024)
    gather_o = RowsGather(wire, o_all, e, z, c, nc, 768)
    gather_cot = PlaneGather(wire, cot_all, e)
    gather_q.run()
    gather_o.step()

    small = q_all[:, :, :, :, pl.ds(query_width + kv_width, SMALL)].reshape(width, SMALL)
    small = jnp.transpose(small.astype(F32))
    gain_first, gain_second = small[experts : experts + 1], small[experts + 1 : experts + 2]
    gains_ref[0:1] = gain_first
    gains_ref[1:2] = gain_second
    rows = x_ref[...].astype(F32)
    scale1 = lax.rsqrt(jnp.mean(rows * rows, -1, keepdims=True) + EPSILON)
    inputs_ref[...] = (rows * scale1 * gain_first).astype(BF16)

    def project(first, count):
        weight = q_all[:, :, :, :, pl.ds(first, count)].reshape(width, count)
        qkv_scr[:, pl.ds(first, count)] = dot_nn(inputs_ref[...], weight)

    project(query_width, kv_width)

    def turned(column):
        head = qkv_scr[:, pl.ds(column, size)]
        return (head * cos_ref[...] + swap_halves(head) * sin_ref[...]).astype(BF16)

    for j in range(KEY_VALUE_HEADS):
        kv_ref[z, :, pl.ds(j * size, size)] = turned(query_width + j * size)
    values = pl.ds(kv_width // 2, kv_width // 2)
    kv_ref[z, :, values] = qkv_scr[:, pl.ds(query_width + kv_width // 2, kv_width // 2)].astype(
        BF16
    )
    line = wire.slots(nc)
    wire.start(kv_ref.at[z], kv_ref.at[z], line, {"context": z + 1}, when=z < nc - 1)
    for later in range(1, nc):

        def clear(later=later):
            kv_ref[z + later] = jnp.zeros(kv_ref.shape[1:], BF16)

        pl.when(z + later < nc)(clear)
    gather_o.step()

    @pl.loop(0, query_width // 256)
    def _(n):
        project(pl.multiple_of(n * 256, 256), 256)

    gather_o.step()
    project(query_width + kv_width, SMALL)
    gather_o.step()

    @pl.loop(0, QUERY_HEADS)
    def _(h):
        column = pl.multiple_of(h * size, size)
        query_ref[:, pl.ds(column, size)] = turned(column)

    gather_o.step()

    logits = qkv_scr[:, pl.ds(query_width + kv_width, SMALL)]
    lanes = lax.broadcasted_iota(jnp.int32, logits.shape, 1)
    named = lanes == routes_ref[:, 0:1]
    for k in range(1, TOP):
        named = named | (lanes == routes_ref[:, k : k + 1])
    logits = jnp.where(named, logits, MASKED)
    expd = jnp.exp(logits - jnp.max(logits, -1, keepdims=True))
    gates = expd / jnp.sum(expd, -1, keepdims=True)
    gate_all[0] = jnp.transpose(gates)[:GATE_ROWS]
    gate_slot = wire.slots(3)
    for r in (1, 2, 3):
        wire.start(gate_all.at[0], gate_all.at[r], gate_slot + r - 1, ids[r])

    gather_o.step()
    for step in range(1, nc):

        def pass_on(step=step):
            block = kv_ref.at[z - step]
            wire.arrived(block, line + step - 1, {"context": z - 1})

        pl.when(z >= step)(pass_on)
        wire.start(
            kv_ref.at[z - step],
            kv_ref.at[z - step],
            line + step,
            {"context": z + 1},
            when=(z >= step) & (z < nc - 1),
        )
        gather_o.step()
    gather_o.step()
    gather_o.step()

    length = nc * tokens
    group = QUERY_HEADS // KEY_VALUE_HEADS
    group_steps = 3
    for first in range(0, QUERY_HEADS, group_steps):
        j = first // group
        key = kv_ref[:, :, pl.ds(j * size, size)].reshape(length, size)
        value = kv_ref[:, :, pl.ds(kv_width // 2 + j * size, size)].reshape(length, size)

        @pl.loop(first, first + group_steps)
        def _(h):
            column = pl.multiple_of(h * size, size)
            scores = dot_nt(query_ref[:, pl.ds(column, size)], key) * (size**-0.5)
            row = z * tokens + lax.broadcasted_iota(jnp.int32, scores.shape, 0)
            place = lax.broadcasted_iota(jnp.int32, scores.shape, 1)
            scores = jnp.where(place <= row, scores, MASKED)
            expd = jnp.exp(scores - jnp.max(scores, -1, keepdims=True))
            total = jnp.sum(expd, -1, keepdims=True)
            mixed = dot_nn(expd.astype(BF16), value) / total
            heads_ref[:, pl.ds(column, size)] = mixed.astype(BF16)

        gather_o.step()
        gather_o.step()
        if first == 0:
            gather_o.run()
            gather_cot.step()
        else:
            gather_cot.step()

    gather_o.run()
    part = width // q_all.shape[0]
    for block in range(q_all.shape[0]):
        weight = o_all[block].reshape(part, width)
        columns = pl.ds(block * part, part)
        hidden_ref[:, columns] = x_ref[:, columns].astype(F32) + dot_nt(heads_ref[...], weight)
    hidden = hidden_ref[...]
    scale2 = lax.rsqrt(jnp.mean(hidden * hidden, -1, keepdims=True) + EPSILON)
    expert_in_ref[...] = (hidden * scale2 * gain_second).astype(BF16)
    gather_cot.run()
    for r in (1, 2, 3):
        wire.arrived(gate_all.at[r], gate_slot + r - 1, ids[r])
    wire.finish()


def front(x, q_shard, o_shard, cot, cosine, sine, routes, sizes):
    ne, nc, nd = sizes
    tokens, width = x.shape
    rows, q_width = q_shard.shape
    shapes = [
        ((ne, nc, nd, rows, q_width), BF16),
        ((ne, nc, nd, rows, width), BF16),
        ((ne, tokens, width), BF16),
        ((ne, GATE_ROWS, tokens), F32),
        ((tokens, width), BF16),
        ((tokens, QUERY_HEADS * HEAD_DIMENSION), BF16),
        ((nc, tokens, 2 * KEY_VALUE_HEADS * HEAD_DIMENSION), BF16),
        ((tokens, QUERY_HEADS * HEAD_DIMENSION), BF16),
        ((tokens, width), F32),
        ((tokens, width), BF16),
        ((8, width), F32),
    ]
    copies = 128
    return pl.pallas_call(
        functools.partial(front_kernel, nc, EXP_DEV * ne),
        out_shape=[jax.ShapeDtypeStruct(*s) for s in shapes],
        in_specs=[pl.BlockSpec(memory_space=pltpu.VMEM)] * 7,
        out_specs=[pl.BlockSpec(memory_space=pltpu.VMEM)] * len(shapes),
        scratch_shapes=[
            pltpu.VMEM((tokens, q_width), F32),
            pltpu.SemaphoreType.DMA((copies,)),
            pltpu.SemaphoreType.DMA((copies,)),
        ],
        compiler_params=pltpu.CompilerParams(
            collective_id=0, has_side_effects=True, vmem_limit_bytes=56 * MIB
        ),
    )(x, q_shard, o_shard, cot, cosine, sine, routes)


class PlaneScatter:
    def __init__(self, wire, land, ids):
        self.wire, self.part, self.land, self.ids = wire, None, land, ids
        self.half = land.shape[-1]
        self.first = wire.slots(6)

    def at(self, r, half):
        return self.part.at[r - 1, :, pl.ds(half * self.half, self.half)]

    def send(self, r, half, mask, slot):
        self.wire.start(self.at(r, half), self.land.at[slot], self.first + slot, self.ids[mask])

    def near(self, r):
        self.send(r, r - 1, r, r - 1)

    def far(self):
        self.send(3, 0, 1, 2)
        self.send(3, 1, 2, 3)

    def relay(self):
        for half, r in ((0, 2), (1, 1)):
            slot = 2 + half
            self.wire.arrived(self.land.at[slot], self.first + slot, self.ids[3 - r])
            part = self.at(r, half)
            part[...] = (part[...].astype(F32) + self.land[slot].astype(F32)).astype(BF16)
            self.send(r, half, r, 4 + half)

    def total(self, own):
        for slot, half, mask in ((0, 0, 1), (1, 1, 2), (4, 0, 2), (5, 1, 1)):
            self.wire.arrived(self.land.at[slot], self.first + slot, self.ids[mask])
            columns = pl.ds(half * self.half, self.half)
            own[:, columns] += self.land[slot].astype(F32)


class LineScatter:
    def __init__(self, wire, block, lands, z, nc, up=True):
        self.wire, self.block, self.lands, self.z, self.nc = wire, block, lands, z, nc
        self.up = up
        self.first = [wire.slots(nc - 1), wire.slots(nc - 1)]

    def arrive(self, way, index, j):
        land = self.lands[way].at[index]
        self.wire.arrived(land, self.first[way] + index, {"context": self.z})
        block = self.block(j)
        block[...] = (block[...].astype(F32) + self.lands[way][index].astype(F32)).astype(BF16)

    def move(self, way, j):
        z, nc = self.z, self.nc
        inner, index, near = ((z > 0), j - z, z + 1) if way == 0 else ((z < nc - 1), z - j, z - 1)
        wanted = (j > z) if way == 0 else (j < z)
        pl.when(wanted & inner)(lambda: self.arrive(way, index, j))
        self.wire.start(
            self.block(j),
            self.lands[way].at[index - 1],
            self.first[way] + index - 1,
            {"context": near},
            when=wanted,
        )

    def step(self, s):
        if self.up:
            self.move(0, self.nc - s)
        self.move(1, s - 1)

    def last(self):
        if self.up:
            pl.when(self.z > 0)(lambda: self.arrive(0, 0, self.z))
        pl.when(self.z < self.nc - 1)(lambda: self.arrive(1, 0, self.z))


class RowsScatter:
    def __init__(self, wire, buf, core, plane, lines, e, z, c, nc, start, width, half):
        self.wire, self.buf, self.core, self.plane = wire, buf, core, plane
        self.e, self.c = e, c
        self.all = pl.ds(start, width)
        self.cols = (pl.ds(start, half), pl.ds(start + half, width - half))
        self.ids = plane_ids(e)
        self.core_slot = wire.slots(1)
        self.first = wire.slots(6)
        rows = buf.shape[2] // nc
        self.line = LineScatter(
            wire,
            lambda j: buf.at[c, e, pl.ds(pl.multiple_of(j * rows, rows), rows), self.all],
            lines,
            z,
            nc,
        )

    def share(self):
        self.wire.start(
            self.buf.at[1 - self.c, :, :, self.all], self.core, self.core_slot, {"dp": 1 - self.c}
        )

    def at(self, r, half):
        return self.buf.at[self.c, flip(self.e, r), :, self.cols[half]]

    def send(self, r, half, mask, slot):
        self.wire.start(
            self.at(r, half), self.plane(slot, half), self.first + slot, self.ids[mask]
        )

    def merge(self, before=None):
        self.wire.arrived(self.core, self.core_slot, {"dp": 1 - self.c})
        for r in (3, 1, 2, 0):
            block = flip(self.e, r)
            part = self.buf.at[self.c, block, :, self.all]
            part[...] = (part[...].astype(F32) + self.core[block].astype(F32)).astype(BF16)
            if r == 3:
                if before is not None:
                    before()
                self.send(3, 0, 1, 2)
                self.send(3, 1, 2, 3)
            elif r:
                self.send(r, r - 1, r, r - 1)

    def add(self, r, half, slot, mask):
        land = self.plane(slot, half)
        self.wire.arrived(land, self.first + slot, self.ids[mask])
        part = self.at(r, half)
        part[...] = (part[...].astype(F32) + land[...].astype(F32)).astype(BF16)

    def relay(self):
        for half, r in ((0, 2), (1, 1)):
            self.add(r, half, 2 + half, 3 - r)
            self.send(r, half, r, 4 + half)

    def total(self):
        for slot, half, mask in ((0, 0, 1), (1, 1, 2), (4, 0, 2), (5, 1, 1)):
            self.add(0, half, slot, mask)


class ExpertLine:
    pieces = 2

    def __init__(self, wire, base, core, land, ins, outs, sems, z, nc):
        self.wire, self.base, self.core, self.land = wire, base, core, land
        self.ins, self.outs, self.sems, self.z, self.nc = ins, outs, sems, z, nc
        self.end = (z == 0) | (z == nc - 1)
        self.inner = jnp.logical_not(self.end)
        self.first = wire.slots((nc + 1) * self.pieces)
        self.sent = []

    def combine(self, sources, dest, out):
        step = self.ins.shape[2]
        count = dest.shape[0] // step

        def loads(p):
            rows = pl.ds(p * step, step)
            return [
                pltpu.make_async_copy(
                    source.at[rows], self.ins.at[k, p % 2], self.sems.at[2 * k + p % 2]
                )
                for k, source in enumerate(sources)
            ]

        def store(p):
            return pltpu.make_async_copy(
                out.at[p % 2], dest.at[pl.ds(p * step, step)], self.sems.at[8 + p % 2]
            )

        for copy in loads(0):
            copy.start()
        for p in range(count):
            if p + 1 < count:
                for copy in loads(p + 1):
                    copy.start()
            for copy in loads(p):
                copy.wait()
            if p > 1:
                store(p - 2).wait()
            total = self.ins[0, p % 2].astype(F32)
            for k in range(1, len(sources)):
                total = total + self.ins[k, p % 2].astype(F32)
            out[p % 2] = total.astype(out.dtype)
            store(p).start()
        for p in range(max(0, count - 2), count):
            store(p).wait()

    def cores(self, r):
        j = flip(self.z, r)
        self.combine([self.base.at[j], self.core.at[j]], self.base.at[j], self.outs[0])

    def rows(self, p):
        rows = self.base.shape[1] // self.pieces
        return pl.ds(p * rows, rows)

    def copy(self, r, p, number):
        target, slot = flip(self.z, r), self.z
        if r == 3:
            target = jnp.where(self.end, flip(self.z, 1), target)
            slot = jnp.where(self.end, self.nc, slot)
        return pltpu.make_async_remote_copy(
            src_ref=self.base.at[flip(self.z, r), self.rows(p)],
            dst_ref=self.land.at[slot, self.rows(p)],
            send_sem=self.wire.sends.at[number],
            recv_sem=self.wire.recvs.at[self.first + slot * self.pieces + p],
            device_id={"context": target},
            device_id_type=MESH,
        )

    def send(self, r, p, when=None):
        number = len(self.sent)
        guard(when, self.copy(r, p, number).start)
        self.sent.append((when, r, p, number))

    def finish(self):
        for when, r, p, number in self.sent:
            guard(when, self.copy(r, p, number).wait_send)

    def arrived(self, slot):
        for p in range(self.pieces):
            self.wire.arrived(
                self.land.at[slot, self.rows(p)],
                self.first + slot * self.pieces + p,
                {"context": self.z},
            )

    def relay(self):
        def add():
            self.arrived(self.nc)
            j = flip(self.z, 2)
            self.combine([self.base.at[j], self.land.at[self.nc]], self.base.at[j], self.outs[0])

        pl.when(self.inner)(add)

    def last(self, result):
        z = self.z
        near = [self.base.at[z], self.land.at[flip(z, 1)], self.land.at[flip(z, 2)]]
        self.arrived(flip(z, 1))
        self.arrived(flip(z, 2))
        pl.when(self.end)(lambda: self.combine(near, result, self.outs[1]))

        def inner():
            self.arrived(flip(z, 3))
            self.combine(near + [self.land.at[flip(z, 3)]], result, self.outs[1])

        pl.when(self.inner)(inner)


def back_kernel(
    nc,
    experts,
    gates_ref,
    gate_ref,
    gains_ref,
    cos_ref,
    sin_ref,
    expert_in_hbm,
    cot_hbm,
    w_gu_hbm,
    w_dn_hbm,
    x_hbm,
    inputs_hbm,
    query_hbm,
    kv_hbm,
    heads_hbm,
    hidden_hbm,
    q_hbm,
    o_hbm,
    layer_ref,
    d_x_ref,
    sum_q_ref,
    sum_o_ref,
    sum_e_hbm,
    base_hbm,
    core_hbm,
    land_hbm,
    x_all,
    y_land,
    dx_land,
    core_q,
    plane_q,
    plane_k,
    lines_o,
    lines_q,
    lines_k,
    dkv_land,
    d_in_ref,
    mixture_ref,
    dg_lanes,
    dg_part,
    dg_land,
    ins,
    out_low,
    out_wide,
    sends_1,
    recvs_1,
    sends_2,
    recvs_2,
    sends_e,
    recvs_e,
    hand_sends,
    hand_recvs,
    stage_sems,
    load_sems,
    sum_sems,
    credits,
):
    e, z, c = (lax.axis_index(a) for a in ("expert", "context", "dp"))
    size = HEAD_DIMENSION
    blocks, tokens, width = cot_hbm.shape
    ff = w_dn_hbm.shape[1]
    query_width = QUERY_HEADS * size
    key_width = KEY_VALUE_HEADS * size
    qkv_width = query_width + 2 * key_width
    rest = q_hbm.shape[-1] - query_width
    grad_width = base_hbm.shape[-1]
    ids = plane_ids(e)
    sibling = {"dp": 1 - c}
    wire_1, wire_2, wire_e = Wire(sends_1, recvs_1), Wire(sends_2, recvs_2), Wire(sends_e, recvs_e)
    expert = ExpertLine(
        wire_e, base_hbm, core_hbm, land_hbm, ins, (out_low, out_wide), sum_sems, z, nc
    )
    gather = PlaneGather(wire_1, x_all, e)
    scatter_dx = PlaneScatter(wire_1, dx_land, ids)
    scatter_y = PlaneScatter(wire_1, y_land, ids)
    dg_slot = wire_1.slots(3)

    def token_phase(w_gu, w_dn, cot_all, a_all, dgu_all, y_part, dx_part, stage):
        scatter_dx.part, scatter_y.part = dx_part, y_part
        loads = [
            pltpu.make_async_copy(source, dest, load_sems.at[n])
            for n, (source, dest) in enumerate(
                ((expert_in_hbm, x_all.at[0]), (w_gu_hbm, w_gu), (w_dn_hbm, w_dn), (cot_hbm, cot_all))
            )
        ]
        for copy in loads:
            copy.start()
        greet(
            [(ids[m], None) for m in (1, 2, 3)]
            + [(sibling, None), ({"context": flip(z, 2)}, None)]
            + [({"context": z + 1}, z < nc - 1), ({"context": z - 1}, z > 0)]
        )
        loads[0].wait()
        gather.spread()
        for copy in loads[1:]:
            copy.wait()
        step = 256
        wide = 512

        def block(r):
            dg_lanes[...] = jnp.zeros_like(dg_lanes)
            for i in range(EXP_DEV):

                @pl.loop(0, ff // step)
                def _(f):
                    column = pl.multiple_of(f * step, step)
                    rows, grads = x_all[r], cot_all[r]
                    gate_part = dot_nn(rows, w_gu[i, :, pl.ds(column, step)])
                    up_part = dot_nn(rows, w_gu[i, :, pl.ds(ff + column, step)])
                    raw = dot_nt(grads, w_dn[i, pl.ds(column, step), :])
                    gate = gates_ref[r][:, i : i + 1]
                    sigma = jax.nn.sigmoid(gate_part)
                    silu = gate_part * sigma
                    act = silu * up_part
                    lanes = lax.broadcasted_iota(jnp.int32, dg_lanes.shape, 1)
                    dg_lanes[...] += jnp.where(
                        lanes == e * EXP_DEV + i, jnp.sum(act * raw, -1, keepdims=True), 0.0
                    )
                    a_all[r, :, pl.ds(i * ff + column, step)] = (act * gate).astype(BF16)
                    d_act = raw * gate
                    d_gate_part = d_act * up_part * sigma * (1.0 + gate_part * (1.0 - sigma))
                    first = i * 2 * ff + column
                    dgu_all[r, :, pl.ds(first, step)] = d_gate_part.astype(BF16)
                    dgu_all[r, :, pl.ds(first + ff, step)] = (d_act * silu).astype(BF16)

            @pl.loop(0, width // wide)
            def _(n):
                columns = pl.ds(pl.multiple_of(n * wide, wide), wide)
                d_rows = dot_nt(dgu_all[r, :, pl.ds(0, 2 * ff)], w_gu[0, columns, :])
                d_rows += dot_nt(dgu_all[r, :, pl.ds(2 * ff, 2 * ff)], w_gu[1, columns, :])
                weight = w_dn[:, :, columns].reshape(EXP_DEV * ff, wide)
                out = dot_nn(a_all[r], weight)
                if r == 0:
                    d_in_ref[:, columns] = d_rows
                    mixture_ref[:, columns] = out
                else:
                    dx_part[r - 1, :, columns] = d_rows.astype(BF16)
                    y_part[r - 1, :, columns] = out.astype(BF16)

            dg_part[r] = jnp.transpose(dg_lanes[...])[:GATE_ROWS]
            if r:
                wire_1.start(dg_part.at[r], dg_land.at[r - 1], dg_slot + r - 1, ids[r])

        block(0)
        gather.forward()
        gather.near(1)
        block(1)
        scatter_dx.near(1)
        scatter_y.near(1)
        gather.near(2)
        block(2)
        scatter_dx.near(2)
        scatter_y.near(2)
        gather.far()
        block(3)
        scatter_dx.far()
        scatter_y.far()

        half_rows = width // nc // 2

        def keep(r, slot):
            return pltpu.make_async_copy(
                stage.at[slot, c], base_hbm.at[flip(z, r)], stage_sems.at[slot]
            )

        def hand(r, slot):
            return pltpu.make_async_remote_copy(
                src_ref=stage.at[slot, 1 - c],
                dst_ref=core_hbm.at[flip(z, r)],
                send_sem=hand_sends.at[r],
                recv_sem=hand_recvs.at[r],
                device_id=sibling,
                device_id_type=MESH,
            )

        def weight_grads(r):
            slot = r % 2
            if r + 2 < nc:
                hand(r + 2, slot).wait_send()
            columns = pl.ds(pl.multiple_of(flip(z, r) * 2 * half_rows, 2 * half_rows), 2 * half_rows)
            for first, source, grad in ((0, x_all, dgu_all), (EXP_DEV * 2 * ff, cot_all, a_all)):
                rows = source[:, :, columns].reshape(blocks * tokens, 2 * half_rows)

                @pl.loop(0, grad.shape[-1] // ff)
                def _(i):
                    column = pl.multiple_of(i * ff, ff)
                    part = grad[:, :, pl.ds(column, ff)].reshape(blocks * tokens, ff)
                    result = dot_tn(rows, part).astype(BF16).reshape(2, half_rows, ff)
                    stage[slot, :, :, pl.ds(pl.multiple_of(first + column, ff), ff)] = result

            keep(r, slot).start()
            hand(r, slot).start()

        def settle(r):
            keep(r, r % 2).wait()
            hand(r, r % 2).wait_recv()
            expert.cores(r)

        weight_grads(3)
        scatter_dx.relay()
        weight_grads(2)
        settle(3)
        expert.send(3, 0)
        expert.send(3, 1)
        scatter_y.relay()
        weight_grads(1)
        settle(2)
        expert.send(2, 0, when=expert.end)
        weight_grads(0)
        settle(1)
        scatter_dx.total(d_in_ref)
        for r in (1, 2):
            pl.semaphore_signal(credits.at[r], inc=1, device_id=ids[r], device_id_type=MESH)
        keep(0, 0).wait()
        for r in (1, 0):
            hand(r, r % 2).wait_send()
        wire_1.finish()
        pl.semaphore_signal(credits.at[0], inc=1, device_id=sibling, device_id_type=MESH)

    def token_rows_phase(
        weight,
        grads_o,
        grads_q,
        x_ref,
        inputs_ref,
        query_ref,
        kv_ref,
        heads_ref,
        hidden_ref,
        cot_ref,
        d_hidden_ref,
        d_attn_ref,
        d_heads_ref,
        d_all_ref,
        d_inputs_ref,
        rows_ref,
        dkv_acc,
        dkv_ref,
    ):
        planes = grads_o.shape[1]
        part = width // planes
        sources = (
            (hidden_hbm, hidden_ref),
            (cot_hbm.at[0], cot_ref),
            (o_hbm, weight.at[:, pl.ds(0, width)]),
            (heads_hbm, heads_ref),
            (query_hbm, query_ref),
            (kv_hbm, kv_ref),
            (x_hbm, x_ref),
            (inputs_hbm, inputs_ref),
        )
        loads = [
            pltpu.make_async_copy(source, dest, load_sems.at[4 + n])
            for n, (source, dest) in enumerate(sources)
        ]
        for copy in loads:
            copy.start()

        def rows_scatter(buf, core, plane, lines, start, count, half):
            return RowsScatter(
                wire_2,
                buf,
                core,
                plane,
                [lines.at[0], lines.at[1]],
                e,
                z,
                c,
                nc,
                start,
                count,
                half,
            )

        rows_of = part // 2
        scatter_o = rows_scatter(
            grads_o,
            x_all.at[:, pl.ds(0, rows_of)],
            lambda slot, half: dx_land.at[slot, pl.ds(0, rows_of)],
            lines_o,
            0,
            width,
            width // 2,
        )
        scatter_q = rows_scatter(
            grads_q,
            core_q.at[:, :, pl.ds(0, query_width)],
            lambda slot, half: plane_q.at[slot],
            lines_q,
            0,
            query_width,
            query_width // 2,
        )
        rest_half = rest // 256 * 128
        scatter_k = rows_scatter(
            grads_q,
            core_q.at[:, :, pl.ds(query_width, rest)],
            lambda slot, half: plane_k.at[
                slot, :, pl.ds(0, rest - rest_half if half else rest_half)
            ],
            lines_k,
            query_width,
            rest,
            rest_half,
        )
        scatter_kv = [
            LineScatter(
                wire_2,
                lambda j, h=h: dkv_ref.at[h, j],
                [dkv_land.at[h], dkv_land.at[h]],
                z,
                nc,
                up=False,
            )
            for h in range(KEY_VALUE_HEADS)
        ]

        loads[0].wait()
        loads[1].wait()
        hidden, d_in = hidden_ref[...], d_in_ref[...]
        scale2 = lax.rsqrt(jnp.mean(hidden * hidden, -1, keepdims=True) + EPSILON)
        scaled = d_in * gains_ref[1:2]
        mean = jnp.mean(scaled * hidden, -1, keepdims=True)
        d_hidden = cot_ref[...].astype(F32) + scale2 * scaled
        d_hidden = d_hidden - hidden * (scale2 * scale2 * scale2 * mean)
        d_hidden_ref[...] = d_hidden
        d_attn_ref[...] = d_hidden.astype(BF16)
        rows_ref[...] = jnp.zeros_like(rows_ref)
        rows_ref[experts + 1 : experts + 2, :] = jnp.sum(d_in * hidden * scale2, 0, keepdims=True)

        loads[2].wait()

        @pl.loop(0, query_width // 256)
        def _(n):
            columns = pl.ds(pl.multiple_of(n * 256, 256), 256)
            d_heads_ref[:, columns] = dot_nn(d_attn_ref[...], weight[:, columns]).astype(BF16)

        load_q = pltpu.make_async_copy(q_hbm, weight, load_sems.at[0])
        load_q.start()
        loads[3].wait()

        def row_grads(buf, left, right, first, count, extra=None):
            @pl.loop(0, planes)
            def _(block):
                columns = pl.ds(pl.multiple_of(block * part, part), part)
                result = dot_tn(left[:, columns], right)
                if extra is not None:
                    result = result + extra(columns)
                result = result.astype(BF16).reshape(nc, 2, part // nc // 2, count)
                for half in range(2):
                    buf[half, block, :, pl.ds(first, count)] = result[:, half].reshape(
                        part // 2, count
                    )

        row_grads(grads_o, d_attn_ref, heads_ref[...], 0, width)
        pl.semaphore_wait(credits.at[0], 1)
        scatter_o.share()

        length = nc * tokens
        group = QUERY_HEADS // KEY_VALUE_HEADS
        for copy in loads[4:6]:
            copy.wait()
        dkv_acc[...] = jnp.zeros_like(dkv_acc)

        def attend(j, first, last):
            key = kv_ref[:, :, pl.ds(j * size, size)].reshape(length, size)
            value = kv_ref[:, :, pl.ds(key_width + j * size, size)].reshape(length, size)

            @pl.loop(j * group + first, j * group + last)
            def _(h):
                columns = pl.ds(pl.multiple_of(h * size, size), size)
                query, grad = query_ref[:, columns], d_heads_ref[:, columns]
                probs = masked_probs(z * tokens, query, key)
                d_probs = dot_nt(grad, value)
                inner = jnp.sum(probs * d_probs, axis=-1, keepdims=True)
                d_raw = (probs * (d_probs - inner) * (size**-0.5)).astype(BF16)
                d_query = dot_nn(d_raw, key)
                d_query = d_query * cos_ref[...] - swap_halves(d_query) * sin_ref[...]
                d_all_ref[:, columns] = d_query.astype(BF16)
                dkv_acc[j, :, pl.ds(0, size)] += dot_tn(d_raw, query)
                dkv_acc[j, :, pl.ds(size, size)] += dot_tn(probs.astype(BF16), grad)

        def round_kv(j):
            for block in range(nc):
                rows = dkv_acc[j, pl.ds(block * tokens, tokens), :]
                dkv_ref[j, block] = rows.astype(BF16)

        def enter():
            pl.semaphore_wait(credits.at[1], 1)
            pl.semaphore_wait(credits.at[2], 1)

        attend(0, 0, group)
        round_kv(0)
        scatter_kv[0].step(1)
        scatter_o.merge(enter)
        attend(1, 0, group // 2)
        scatter_kv[0].step(2)
        attend(1, group // 2, group)
        round_kv(1)
        scatter_kv[1].step(1)
        scatter_kv[0].step(3)
        scatter_o.relay()

        for copy in loads[6:]:
            copy.wait()
        row_grads(grads_q, inputs_ref, d_all_ref[:, pl.ds(0, query_width)], 0, query_width)
        scatter_q.share()
        scatter_kv[1].step(2)
        scatter_y.total(mixture_ref)
        layer_ref[...] = (hidden_ref[...] + mixture_ref[...]).astype(BF16)
        scatter_kv[1].step(3)
        for r in (1, 2):
            scatter_kv[r - 1].last()
        expert.send(2, 1, when=expert.end)
        expert.send(1, 0)
        scatter_o.total()
        scatter_q.merge()

        for h in range(KEY_VALUE_HEADS):
            grad = dkv_ref[h, z, :, pl.ds(0, size)].astype(F32)
            grad = grad * cos_ref[...] - swap_halves(grad) * sin_ref[...]
            d_all_ref[:, pl.ds(query_width + h * size, size)] = grad.astype(BF16)
            d_all_ref[:, pl.ds(query_width + key_width + h * size, size)] = dkv_ref[
                h, z, :, pl.ds(size, size)
            ]

        total = dg_part[0]
        for r in (1, 2, 3):
            wire_1.arrived(dg_land.at[r - 1], dg_slot + r - 1, ids[r])
            total = total + dg_land[r - 1]
        gates = gate_ref[...]
        d_logits = gates * (total - jnp.sum(gates * total, 0, keepdims=True))
        d_logits = jnp.concatenate(
            [d_logits, jnp.zeros((SMALL - d_logits.shape[0], tokens), F32)], 0
        )
        d_all_ref[:, pl.ds(qkv_width, SMALL)] = jnp.transpose(d_logits).astype(BF16)

        load_q.wait()

        @pl.loop(0, planes)
        def _(block):
            columns = pl.ds(pl.multiple_of(block * part, part), part)
            d_inputs_ref[:, columns] = dot_nt(d_all_ref[...], weight[columns, :])

        rows = x_ref[...].astype(F32)
        scale1 = lax.rsqrt(jnp.mean(rows * rows, -1, keepdims=True) + EPSILON)
        d_inputs = d_inputs_ref[...]
        rows_ref[experts : experts + 1, :] = jnp.sum(d_inputs * rows * scale1, 0, keepdims=True)

        def extra(columns):
            small = jnp.transpose(rows_ref[:, columns])
            return jnp.concatenate([jnp.zeros((part, rest - SMALL), F32), small], 1)

        row_grads(
            grads_q, inputs_ref, d_all_ref[:, pl.ds(query_width, rest)], query_width, rest, extra
        )
        scatter_k.share()
        pltpu.make_async_remote_copy(
            src_ref=core_hbm.at[z],
            dst_ref=core_hbm.at[z],
            send_sem=hand_sends.at[0],
            recv_sem=hand_recvs.at[0],
            device_id=sibling,
            device_id_type=MESH,
        ).wait_recv()
        expert.cores(0)
        expert.relay()
        expert.send(2, 0, when=expert.inner)
        expert.send(2, 1, when=expert.inner)
        expert.send(1, 1)
        scatter_q.relay()
        scatter_k.merge()
        scaled = d_inputs_ref[...] * gains_ref[0:1]
        rows = x_ref[...].astype(F32)
        scale1 = lax.rsqrt(jnp.mean(rows * rows, -1, keepdims=True) + EPSILON)
        mean = jnp.mean(scaled * rows, -1, keepdims=True)
        d_x = d_hidden_ref[...] + scale1 * scaled - rows * (scale1 * scale1 * scale1 * mean)
        d_x_ref[...] = d_x.astype(BF16)
        scatter_q.total()
        scatter_k.relay()
        scatter_o.line.step(1)
        scatter_q.line.step(1)
        scatter_k.total()
        scatter_k.line.step(1)
        for s in range(2, nc):
            for scatter in (scatter_o, scatter_q, scatter_k):
                scatter.line.step(s)
        for scatter in (scatter_o, scatter_q, scatter_k):
            scatter.line.last()
        sum_o_ref[...] = scatter_o.line.block(z)[...].astype(F32)
        sum_q_ref[...] = grads_q[c, e, pl.ds(pl.multiple_of(z * (rows_of // nc), rows_of // nc), rows_of // nc)].astype(F32)
        expert.last(sum_e_hbm)
        wire_2.finish()
        expert.finish()

    held = EXP_DEV
    pl.run_scoped(
        token_phase,
        pltpu.VMEM((held, width, 2 * ff), BF16),
        pltpu.VMEM((held, ff, width), BF16),
        pltpu.VMEM((blocks, tokens, width), BF16),
        pltpu.VMEM((blocks, tokens, held * ff), BF16),
        pltpu.VMEM((blocks, tokens, held * 2 * ff), BF16),
        pltpu.VMEM((blocks - 1, tokens, width), BF16),
        pltpu.VMEM((blocks - 1, tokens, width), BF16),
        pltpu.VMEM((2, 2, width // nc // 2, grad_width), BF16),
    )
    rows_half = width // blocks // 2
    pl.run_scoped(
        token_rows_phase,
        pltpu.VMEM((width, qkv_width + SMALL), BF16),
        pltpu.VMEM((2, blocks, rows_half, width), BF16),
        pltpu.VMEM((2, blocks, rows_half, qkv_width + SMALL), BF16),
        pltpu.VMEM((tokens, width), BF16),
        pltpu.VMEM((tokens, width), BF16),
        pltpu.VMEM((tokens, query_width), BF16),
        pltpu.VMEM((nc, tokens, 2 * key_width), BF16),
        pltpu.VMEM((tokens, query_width), BF16),
        pltpu.VMEM((tokens, width), F32),
        pltpu.VMEM((tokens, width), BF16),
        pltpu.VMEM((tokens, width), F32),
        pltpu.VMEM((tokens, width), BF16),
        pltpu.VMEM((tokens, query_width), BF16),
        pltpu.VMEM((tokens, qkv_width + SMALL), BF16),
        pltpu.VMEM((tokens, width), F32),
        pltpu.VMEM((SMALL, width), F32),
        pltpu.VMEM((KEY_VALUE_HEADS, nc * tokens, 2 * size), F32),
        pltpu.VMEM((KEY_VALUE_HEADS, nc, tokens, 2 * size), BF16),
    )


def back(operands, sizes):
    ne, nc, nd = sizes
    cot, w_gu, w_dn, x = operands[6], operands[7], operands[8], operands[9]
    q_all = operands[15]
    tokens, width = x.shape
    held, ff = w_dn.shape[0], w_dn.shape[1]
    q_width = q_all.shape[-1]
    rows = width // (ne * nc * nd)
    rest = q_width - QUERY_HEADS * HEAD_DIMENSION
    rest_half = rest // 256 * 128
    shard, grads = width // (nc * nd), held * 3 * ff
    kv_size = 2 * HEAD_DIMENSION
    shapes = [
        ((tokens, width), BF16),
        ((tokens, width), BF16),
        ((rows, q_width), F32),
        ((rows, width), F32),
        ((shard, grads), F32),
        ((nc, shard, grads), BF16),
        ((nc, shard, grads), BF16),
        ((nc + 1, shard, grads), BF16),
    ]
    vmem = pl.BlockSpec(memory_space=pltpu.VMEM)
    anywhere = pl.BlockSpec(memory_space=pl.ANY)
    step = 16
    return pl.pallas_call(
        functools.partial(back_kernel, nc, EXP_DEV * ne),
        out_shape=[jax.ShapeDtypeStruct(*s) for s in shapes],
        in_specs=[vmem] * 5 + [anywhere] * (len(operands) - 5),
        out_specs=[vmem] * 4 + [anywhere] * 4,
        scratch_shapes=[
            pltpu.VMEM((ne, tokens, width), BF16),
            pltpu.VMEM((6, tokens, width // 2), BF16),
            pltpu.VMEM((6, tokens, width // 2), BF16),
            pltpu.VMEM((ne, nc * rows, q_width), BF16),
            pltpu.VMEM((6, nc * rows, QUERY_HEADS * HEAD_DIMENSION // 2), BF16),
            pltpu.VMEM((6, nc * rows, rest - rest_half), BF16),
            pltpu.VMEM((2, nc - 1, rows, width), BF16),
            pltpu.VMEM((2, nc - 1, rows, QUERY_HEADS * HEAD_DIMENSION), BF16),
            pltpu.VMEM((2, nc - 1, rows, rest), BF16),
            pltpu.VMEM((KEY_VALUE_HEADS, nc - 1, tokens, kv_size), BF16),
            pltpu.VMEM((tokens, width), F32),
            pltpu.VMEM((tokens, width), F32),
            pltpu.VMEM((tokens, SMALL), F32),
            pltpu.VMEM((ne, GATE_ROWS, tokens), F32),
            pltpu.VMEM((ne - 1, GATE_ROWS, tokens), F32),
            pltpu.VMEM((4, 2, step, grads), BF16),
            pltpu.VMEM((2, step, grads), BF16),
            pltpu.VMEM((2, step, grads), F32),
            pltpu.SemaphoreType.DMA((32,)),
            pltpu.SemaphoreType.DMA((32,)),
            pltpu.SemaphoreType.DMA((64,)),
            pltpu.SemaphoreType.DMA((64,)),
            pltpu.SemaphoreType.DMA((8,)),
            pltpu.SemaphoreType.DMA((2 * nc + 2,)),
            pltpu.SemaphoreType.DMA((nc,)),
            pltpu.SemaphoreType.DMA((nc,)),
            pltpu.SemaphoreType.DMA((2,)),
            pltpu.SemaphoreType.DMA((12,)),
            pltpu.SemaphoreType.DMA((10,)),
            pltpu.SemaphoreType.REGULAR((3,)),
        ],
        compiler_params=pltpu.CompilerParams(
            collective_id=1, has_side_effects=True, vmem_limit_bytes=63 * MIB
        ),
    )(*operands)


def local_plain(
    layer_input,
    gain_attn,
    query_key_value_weight,
    w_out,
    w_router,
    gain_ffn,
    w_gate_up,
    w_down,
    routes,
    d_out,
):
    tokens = layer_input.shape[1]
    model_width = layer_input.shape[2]
    ne, nc, nd = (lax.axis_size(a) for a in ("expert", "context", "dp"))
    expert_total = EXP_DEV * ne
    ff = w_down.shape[1]
    me = lax.axis_index("expert")
    first_row = lax.axis_index("context") * tokens
    query_width = QUERY_HEADS * HEAD_DIMENSION
    key_width = KEY_VALUE_HEADS * HEAD_DIMENSION
    qkv_width = query_width + 2 * key_width

    small = jnp.concatenate([w_router, gain_attn[:, None], gain_ffn[:, None]], -1)
    small = jnp.pad(small, ((0, 0), (0, 128 - small.shape[1])))
    gathered = gather_rows(jnp.concatenate([query_key_value_weight, small], -1))
    out_turned = gather_rows(w_out.T)
    qkv_weight = gathered[:, :qkv_width]
    router_weight = gathered[:, qkv_width : qkv_width + expert_total]
    gains = gathered[:, qkv_width + expert_total : qkv_width + expert_total + 2].T.astype(F32)
    gain_first, gain_second = gains[0], gains[1]
    cotangent_all = plane_gather(d_out[0])

    token_rows = layer_input[0].astype(F32)
    scale1 = lax.rsqrt(jnp.mean(token_rows * token_rows, -1, keepdims=True) + EPSILON)
    inputs1 = (token_rows * scale1 * gain_first).astype(BF16)
    query_key_value = dot_nn(inputs1, qkv_weight)
    cosine_values, sine_values = rope_tables(first_row + jnp.arange(tokens), HEAD_DIMENSION)
    rotated = rotate_half(
        query_key_value[:, : query_width + key_width].reshape(tokens, -1, HEAD_DIMENSION),
        cosine_values,
        sine_values,
    ).reshape(tokens, -1)
    query = rotated[:, :query_width].astype(BF16)
    key_value_local = jnp.concatenate(
        [rotated[:, query_width:], query_key_value[:, query_width + key_width :]], -1
    ).astype(BF16)
    key_value = line_gather(key_value_local, "context", both=False).reshape(nc * tokens, -1)
    first = first_row.astype(jnp.int32).reshape(1)
    heads = attend_forward(first, query, key_value)

    logits = dot_nn(inputs1, router_weight)
    chosen_ids = routes[0]
    picks = (chosen_ids[:, :, None] == jnp.arange(expert_total)[None, None, :]).astype(F32)
    chosen = jnp.sum(picks * logits[:, None, :], -1)
    gates = jax.nn.softmax(chosen, axis=-1)
    gate_dense = jnp.sum(picks * gates[:, :, None], 1).T
    gate_blocks = cube_gather(gate_dense, "expert", axis_masks("expert"))
    gate_local = jnp.concatenate(
        [lax.dynamic_slice_in_dim(b, me * EXP_DEV, EXP_DEV, 0) for b in gate_blocks], 1
    )

    attn = dot_nt(heads, out_turned)
    hidden = token_rows + attn
    scale2 = lax.rsqrt(jnp.mean(hidden * hidden, -1, keepdims=True) + EPSILON)
    expert_in = (hidden * scale2 * gain_second).astype(BF16)

    rows_all = plane_gather(expert_in)
    gate_up = jnp.einsum("td,edf->etf", rows_all, w_gate_up, preferred_element_type=F32)
    gate_part, up_part = gate_up[..., :ff], gate_up[..., ff:]
    sigma = jax.nn.sigmoid(gate_part)
    silu = gate_part * sigma
    act = silu * up_part
    gate_column = gate_local[:, :, None]
    act_gated = (act * gate_column).astype(BF16)
    partial_out = jnp.einsum("etf,efd->td", act_gated, w_down, preferred_element_type=F32)
    mixture = plane_scatter(partial_out.astype(BF16), tokens)
    layer_result = (hidden + mixture).astype(BF16)

    d_act_raw = jnp.einsum("td,efd->etf", cotangent_all, w_down, preferred_element_type=F32)
    d_gates_local = jnp.sum(d_act_raw * act, -1)
    d_act = d_act_raw * gate_column
    d_gate_part = d_act * up_part * sigma * (1.0 + gate_part * (1.0 - sigma))
    d_up_part = d_act * silu
    d_gate_up = jnp.concatenate([d_gate_part, d_up_part], -1).astype(BF16)
    d_rows = jnp.einsum("etf,edf->td", d_gate_up, w_gate_up, preferred_element_type=F32)
    grad_down = jnp.einsum("td,etf->edf", cotangent_all, act_gated, preferred_element_type=F32)
    grad_gate_up = jnp.einsum("td,etf->edf", rows_all, d_gate_up, preferred_element_type=F32)

    d_expert_in = plane_scatter(d_rows.astype(BF16), tokens)
    d_gate_blocks = d_gates_local.reshape(EXP_DEV, ne, tokens)
    d_gates_dense = jnp.zeros((expert_total, tokens), F32)
    for r in range(ne):
        arrived = d_gate_blocks[:, r]
        if r:
            arrived = exchange(arrived, "expert", r)
        d_gates_dense = lax.dynamic_update_slice(d_gates_dense, arrived, ((me ^ r) * EXP_DEV, 0))
    d_gates = jnp.sum(picks * d_gates_dense.T[:, None, :], -1)
    d_chosen = gates * (d_gates - jnp.sum(gates * d_gates, -1, keepdims=True))
    d_logits = jnp.sum(picks * d_chosen[:, :, None], 1).astype(BF16)
    grad_router = dot_tn(inputs1, d_logits)

    core = lax.axis_index("dp")
    part = model_width // (nc * nd)

    def scatter_experts(grad):
        blocks = grad.reshape(EXP_DEV, nc, nd, part, -1)
        mine = cube_scatter(
            [lax.dynamic_index_in_dim(blocks, core ^ r, 2, keepdims=False) for r in range(nd)],
            "dp",
            axis_masks("dp"),
        )
        return line_scatter(
            lambda j: lax.dynamic_index_in_dim(mine, j, 1, keepdims=False), "context"
        )

    sum_gate_up = scatter_experts(grad_gate_up)
    sum_down = jnp.swapaxes(scatter_experts(grad_down), 1, 2)

    cotangent = d_out[0].astype(F32)
    scaled2 = d_expert_in * gain_second
    d_hidden = (
        cotangent
        + scale2 * scaled2
        - hidden * (scale2 * scale2 * scale2) * jnp.mean(scaled2 * hidden, -1, keepdims=True)
    )
    grad_gain_second = jnp.sum(d_expert_in * hidden * scale2, 0)
    d_attn = d_hidden.astype(BF16)
    grad_out_turned = dot_tn(d_attn, heads)
    sum_out = scatter_rows(grad_out_turned).T
    d_heads = dot_nn(d_attn, out_turned).astype(BF16)
    d_query, d_key_all, d_value_all = attend_backward(first, query, key_value, d_heads)
    d_key_value_all = jnp.concatenate([d_key_all, d_value_all], -1).reshape(nc, tokens, -1)
    d_key_value = line_scatter(
        lambda j: lax.dynamic_index_in_dim(d_key_value_all, j, 0, keepdims=False),
        "context",
        up=False,
    )
    d_rotated = rotate_back(
        jnp.concatenate([d_query, d_key_value[:, :key_width]], -1).reshape(
            tokens, -1, HEAD_DIMENSION
        ),
        cosine_values,
        sine_values,
    ).reshape(tokens, -1)
    d_qkv = jnp.concatenate([d_rotated, d_key_value[:, key_width:]], -1).astype(BF16)
    d_inputs = dot_nt(d_qkv, qkv_weight) + dot_nt(d_logits, router_weight)
    grad_gain_first = jnp.sum(d_inputs * token_rows * scale1, 0)
    grad_qkv = dot_tn(inputs1, d_qkv)
    small_grads = jnp.concatenate(
        [grad_router, grad_gain_first[:, None], grad_gain_second[:, None]], -1
    )
    small_grads = jnp.pad(small_grads, ((0, 0), (0, 128 - small_grads.shape[1])))
    sum_rows = scatter_rows(jnp.concatenate([grad_qkv, small_grads], -1))
    sum_qkv = sum_rows[:, :qkv_width]
    sum_router = sum_rows[:, qkv_width : qkv_width + expert_total]
    sum_gain_first = sum_rows[:, qkv_width + expert_total]
    sum_gain_second = sum_rows[:, qkv_width + expert_total + 1]
    scaled1 = d_inputs * gain_first
    d_input_rows = (
        d_hidden
        + scale1 * scaled1
        - token_rows
        * (scale1 * scale1 * scale1)
        * jnp.mean(scaled1 * token_rows, -1, keepdims=True)
    ).astype(BF16)
    return (
        layer_result[None],
        d_input_rows[None],
        sum_gain_first,
        sum_qkv,
        sum_out,
        sum_router,
        sum_gain_second,
        sum_gate_up,
        sum_down,
    )


def local_fused(
    layer_input,
    gain_attn,
    query_key_value_weight,
    w_out,
    w_router,
    gain_ffn,
    w_gate_up,
    w_down,
    routes,
    d_out,
):
    tokens = layer_input.shape[1]
    ne, nc, nd = sizes = tuple(lax.axis_size(a) for a in ("expert", "context", "dp"))
    expert_total = EXP_DEV * ne
    ff = w_down.shape[1]
    me = lax.axis_index("expert")
    first_row = lax.axis_index("context") * tokens
    query_width = QUERY_HEADS * HEAD_DIMENSION
    key_width = KEY_VALUE_HEADS * HEAD_DIMENSION
    qkv_width = query_width + 2 * key_width

    small = jnp.concatenate([w_router, gain_attn[:, None], gain_ffn[:, None]], -1)
    small = jnp.pad(small, ((0, 0), (0, SMALL - small.shape[1])))
    cosine_values, sine_values = rope_tables(first_row + jnp.arange(tokens), HEAD_DIMENSION)
    sign = jnp.where(jnp.arange(HEAD_DIMENSION) < HEAD_DIMENSION // 2, -1.0, 1.0)
    (
        q_all,
        o_all,
        cotangent_all,
        gate_all,
        inputs1,
        query,
        key_value,
        heads,
        hidden,
        expert_in,
        gains,
    ) = front(
        layer_input[0],
        jnp.concatenate([query_key_value_weight, small], -1),
        w_out.T,
        d_out[0],
        cosine_values,
        sine_values * sign,
        routes[0],
        sizes,
    )
    gate_local = jnp.swapaxes(
        lax.dynamic_slice_in_dim(gate_all, me * EXP_DEV, EXP_DEV, 1), 1, 2
    )
    layer_result, d_x, sum_rows, sum_out, sum_experts = back(
        (
            gate_local,
            gate_all[0],
            gains,
            cosine_values,
            sine_values * sign,
            expert_in,
            cotangent_all,
            w_gate_up,
            w_down,
            layer_input[0],
            inputs1,
            query,
            key_value,
            heads,
            hidden,
            q_all.reshape(-1, q_all.shape[-1]),
            o_all.reshape(-1, o_all.shape[-1]),
        ),
        sizes,
    )[:5]
    sum_gate_up = jnp.stack([sum_experts[:, i * 2 * ff : (i + 1) * 2 * ff] for i in range(EXP_DEV)])
    sum_down = sum_experts[:, EXP_DEV * 2 * ff :].reshape(-1, EXP_DEV, ff)
    return (
        layer_result[None],
        d_x[None],
        sum_rows[:, qkv_width + expert_total],
        sum_rows[:, :qkv_width],
        sum_out.T,
        sum_rows[:, qkv_width : qkv_width + expert_total],
        sum_rows[:, qkv_width + expert_total + 1],
        sum_gate_up,
        jnp.transpose(sum_down, (1, 2, 0)),
    )


def solution(mesh):
    in_specs = (
        P(("expert", "dp"), "context", None),
        P(("expert", "context", "dp")),
        P(("expert", "context", "dp"), None),
        P(None, ("expert", "context", "dp")),
        P(("expert", "context", "dp"), None),
        P(("expert", "context", "dp")),
        P("expert", None, None),
        P("expert", None, None),
        P(("expert", "dp"), "context", None),
        P(("expert", "dp"), "context", None),
    )
    out_specs = (
        P(("expert", "dp"), "context", None),
        P(("expert", "dp"), "context", None),
        P(("expert", "context", "dp")),
        P(("expert", "context", "dp"), None),
        P(None, ("expert", "context", "dp")),
        P(("expert", "context", "dp"), None),
        P(("expert", "context", "dp")),
        P("expert", ("context", "dp"), None),
        P("expert", None, ("context", "dp")),
    )
    sizes = tuple(mesh.shape[a] for a in ("expert", "context", "dp"))
    local = local_fused if sizes == (4, 4, 2) else local_plain
    return jax.shard_map(local, mesh=mesh, in_specs=in_specs, out_specs=out_specs, check_vma=False)
```

```python
import functools
import math

import jax
import jax.numpy as jnp
from jax import lax
from jax.experimental import pallas as pl
from jax.experimental.pallas import tpu as pltpu
from jax.sharding import PartitionSpec as P

QUERY_HEADS = 12
KEY_VALUE_HEADS = 2
HEAD_DIMENSION = 128
TOP = 4
EXP_DEV = 2

EPSILON = 1e-06
ROPE_BASE = 10000.0
MASKED = -1e30

F32 = jnp.float32
BF16 = jnp.bfloat16


def rope_tables(positions, width):
    halfway = width // 2
    fraction = jnp.arange(halfway, dtype=jnp.float32) * (2.0 / width)
    frequency = jnp.exp(-math.log(ROPE_BASE) * fraction)
    angles = positions.astype(jnp.float32)[:, None] * frequency[None, :]
    cosine_values = jnp.cos(angles)
    sine_values = jnp.sin(angles)
    return (
        jnp.concatenate([cosine_values, cosine_values], -1),
        jnp.concatenate([sine_values, sine_values], -1),
    )


def rotate_half(values, cosine_values, sine_values):
    halfway = values.shape[-1] // 2
    turned = jnp.concatenate([-values[..., halfway:], values[..., :halfway]], -1)
    return values * cosine_values[:, None, :] + turned * sine_values[:, None, :]


def rotate_back(grads, cosine_values, sine_values):
    halfway = grads.shape[-1] // 2
    scaled = grads * sine_values[:, None, :]
    turned = jnp.concatenate([scaled[..., halfway:], -scaled[..., :halfway]], -1)
    return grads * cosine_values[:, None, :] + turned


def dot_nt(a, b):
    return lax.dot_general(a, b, (((1,), (1,)), ((), ())), preferred_element_type=F32)


def dot_tn(a, b):
    return lax.dot_general(a, b, (((0,), (0,)), ((), ())), preferred_element_type=F32)


def dot_nn(a, b):
    return jnp.dot(a, b, preferred_element_type=F32)


def masked_probs(first_row, query, key):
    scores = dot_nt(query, key) * (HEAD_DIMENSION**-0.5)
    rows = first_row + lax.broadcasted_iota(jnp.int32, scores.shape, 0)
    columns = lax.broadcasted_iota(jnp.int32, scores.shape, 1)
    scores = jnp.where(columns <= rows, scores, MASKED)
    expd = jnp.exp(scores - jnp.max(scores, axis=-1, keepdims=True))
    return expd / jnp.sum(expd, axis=-1, keepdims=True)


def attend_forward_kernel(first_ref, query_ref, key_ref, value_ref, heads_ref):
    probs = masked_probs(first_ref[0], query_ref[...], key_ref[...])
    heads_ref[...] = dot_nn(probs.astype(BF16), value_ref[...]).astype(BF16)


def attend_forward(first_row, query, key_value):
    tokens, width = query.shape
    length = key_value.shape[0]
    group = QUERY_HEADS // KEY_VALUE_HEADS
    size = HEAD_DIMENSION
    return pl.pallas_call(
        attend_forward_kernel,
        grid_spec=pltpu.PrefetchScalarGridSpec(
            num_scalar_prefetch=1,
            grid=(QUERY_HEADS,),
            in_specs=[
                pl.BlockSpec((tokens, size), lambda h, s: (0, h)),
                pl.BlockSpec((length, size), lambda h, s: (0, h // group)),
                pl.BlockSpec((length, size), lambda h, s: (0, KEY_VALUE_HEADS + h // group)),
            ],
            out_specs=pl.BlockSpec((tokens, size), lambda h, s: (0, h)),
        ),
        out_shape=jax.ShapeDtypeStruct((tokens, width), BF16),
        compiler_params=pltpu.CompilerParams(vmem_limit_bytes=32 * 1024 * 1024),
        cost_estimate=pl.CostEstimate(
            flops=4 * tokens * length * width, bytes_accessed=4 * tokens * width, transcendentals=0
        ),
    )(first_row, query, key_value, key_value)


def attend_backward_kernel(
    first_ref, query_ref, key_ref, value_ref, grad_ref, d_query_ref, d_key_ref, d_value_ref
):
    query, key, value, grad = query_ref[...], key_ref[...], value_ref[...], grad_ref[...]
    probs = masked_probs(first_ref[0], query, key)
    d_probs = dot_nt(grad, value)
    inner = jnp.sum(probs * d_probs, axis=-1, keepdims=True)
    d_raw = (probs * (d_probs - inner) * (HEAD_DIMENSION**-0.5)).astype(BF16)
    d_query_ref[...] = dot_nn(d_raw, key)
    d_key = dot_tn(d_raw, query)
    d_value = dot_tn(probs.astype(BF16), grad)

    @pl.when(pl.program_id(1) == 0)
    def _():
        d_key_ref[...] = d_key
        d_value_ref[...] = d_value

    @pl.when(pl.program_id(1) > 0)
    def _():
        d_key_ref[...] += d_key
        d_value_ref[...] += d_value


def attend_backward(first_row, query, key_value, grad):
    tokens, width = query.shape
    length = key_value.shape[0]
    group = QUERY_HEADS // KEY_VALUE_HEADS
    size = HEAD_DIMENSION
    row_spec = pl.BlockSpec((tokens, size), lambda j, g, s: (0, j * group + g))
    return pl.pallas_call(
        attend_backward_kernel,
        grid_spec=pltpu.PrefetchScalarGridSpec(
            num_scalar_prefetch=1,
            grid=(KEY_VALUE_HEADS, group),
            in_specs=[
                row_spec,
                pl.BlockSpec((length, size), lambda j, g, s: (0, j)),
                pl.BlockSpec((length, size), lambda j, g, s: (0, KEY_VALUE_HEADS + j)),
                row_spec,
            ],
            out_specs=[
                row_spec,
                pl.BlockSpec((length, size), lambda j, g, s: (0, j)),
                pl.BlockSpec((length, size), lambda j, g, s: (0, j)),
            ],
        ),
        out_shape=[
            jax.ShapeDtypeStruct((tokens, width), F32),
            jax.ShapeDtypeStruct((length, KEY_VALUE_HEADS * size), F32),
            jax.ShapeDtypeStruct((length, KEY_VALUE_HEADS * size), F32),
        ],
        compiler_params=pltpu.CompilerParams(vmem_limit_bytes=32 * 1024 * 1024),
        cost_estimate=pl.CostEstimate(
            flops=10 * tokens * length * width, bytes_accessed=8 * tokens * width, transcendentals=0
        ),
    )(first_row, query, key_value, key_value, grad)


def exchange(values, axis, mask):
    size = lax.axis_size(axis)
    return lax.ppermute(values, axis, [(i, i ^ mask) for i in range(size)])


def axis_masks(axis):
    size = lax.axis_size(axis)
    masks, bit = [], 1
    while bit < size:
        masks.append(bit)
        bit *= 2
    return masks


def cube_gather(values, axis, masks):
    held = {0: values}
    for mask in masks:
        for r, block in list(held.items()):
            held[r ^ mask] = exchange(block, axis, mask)
    return [held[r] for r in range(lax.axis_size(axis))]


def cube_scatter(blocks, axis, masks):
    held = dict(enumerate(blocks))
    for mask in masks:
        kept = {}
        for r in list(held):
            if not r & mask:
                arrived = exchange(held[r ^ mask].astype(BF16), axis, mask)
                kept[r] = held[r].astype(F32) + arrived.astype(F32)
        held = kept
    return held[0]


def line_steps(values, axis, up):
    size = lax.axis_size(axis)
    pairs = [(i, i + 1) if up else (i + 1, i) for i in range(size - 1)]
    return lax.ppermute(values, axis, pairs)


def line_gather(values, axis, both=True):
    size = lax.axis_size(axis)
    me = lax.axis_index(axis)
    result = jnp.zeros((size + 1,) + values.shape, values.dtype)
    result = lax.dynamic_update_index_in_dim(result, values, me, 0)
    up = down = values
    for step in range(1, size):
        up = line_steps(up, axis, True)
        result = lax.dynamic_update_index_in_dim(
            result, up, jnp.where(me - step >= 0, me - step, size), 0
        )
        if both:
            down = line_steps(down, axis, False)
            result = lax.dynamic_update_index_in_dim(result, down, jnp.minimum(me + step, size), 0)
    return result[:size]


def line_scatter(take, axis, up=True, down=True):
    size = lax.axis_size(axis)
    me = lax.axis_index(axis)
    total = take(me).astype(F32)
    for active, sign in ((up, 1), (down, -1)):
        if not active:
            continue
        arrived = None
        for step in range(1, size):
            block = take((me + sign * (size - step)) % size).astype(F32)
            if arrived is not None:
                block = block + arrived.astype(F32)
            arrived = line_steps(block.astype(BF16), axis, sign > 0)
        total = total + arrived.astype(F32)
    return total


def gather_rows(shard):
    ne, nc, nd = (lax.axis_size(a) for a in ("expert", "context", "dp"))
    rows, width = shard.shape
    lines = line_gather(shard, "context")
    masks = axis_masks("expert")
    half = width // 256 * 128
    parts = [lines[..., :half], lines[..., half:]]
    me = lax.axis_index("expert")
    result = jnp.zeros((ne, nc, rows, width), shard.dtype)
    for start, part, order in ((0, parts[0], masks), (half, parts[1], masks[::-1])):
        for r, block in enumerate(cube_gather(part, "expert", order)):
            result = lax.dynamic_update_slice(result, block[None], (me ^ r, 0, 0, start))
    core = lax.axis_index("dp")
    whole = jnp.zeros((ne, nc, nd, rows, width), shard.dtype)
    for r, block in enumerate(cube_gather(result, "dp", axis_masks("dp"))):
        whole = lax.dynamic_update_slice(whole, block[:, :, None], (0, 0, core ^ r, 0, 0))
    return whole.reshape(-1, width)


def scatter_rows(grad):
    ne, nc, nd = (lax.axis_size(a) for a in ("expert", "context", "dp"))
    width = grad.shape[-1]
    rows = grad.shape[0] // (ne * nc * nd)
    blocks = grad.reshape(ne, nc, nd, rows, width)
    core, me = lax.axis_index("dp"), lax.axis_index("expert")
    mine = cube_scatter(
        [
            lax.dynamic_index_in_dim(blocks, core ^ r, 2, keepdims=False)
            for r in range(nd)
        ],
        "dp",
        axis_masks("dp"),
    )
    masks = axis_masks("expert")
    half = width // 256 * 128
    sums = []
    for part, order in ((mine[..., :half], masks), (mine[..., half:], masks[::-1])):
        sums.append(
            cube_scatter(
                [lax.dynamic_index_in_dim(part, me ^ r, 0, keepdims=False) for r in range(ne)],
                "expert",
                order,
            )
        )
    lines = jnp.concatenate(sums, -1)
    return line_scatter(
        lambda j: lax.dynamic_index_in_dim(lines, j, 0, keepdims=False), "context"
    )


def plane_gather(rows):
    masks = axis_masks("expert")
    half = rows.shape[-1] // 2
    left = cube_gather(rows[:, :half], "expert", masks)
    right = cube_gather(rows[:, half:], "expert", masks[::-1])
    return jnp.concatenate([jnp.concatenate(p, -1) for p in zip(left, right)], 0)


def plane_scatter(partial, tokens):
    masks = axis_masks("expert")
    size = lax.axis_size("expert")
    half = partial.shape[-1] // 2
    blocks = partial.reshape(size, tokens, -1)
    left = cube_scatter([blocks[r, :, :half] for r in range(size)], "expert", masks)
    right = cube_scatter([blocks[r, :, half:] for r in range(size)], "expert", masks[::-1])
    return jnp.concatenate([left, right], -1)


MESH = pl.DeviceIdType.MESH
MIB = 1024 * 1024
SMALL = 128
GATE_ROWS = 16


def flip(index, mask):
    bit = 1
    while bit <= mask:
        if mask & bit:
            index = index + bit - 2 * bit * lax.rem(lax.div(index, bit), 2)
        bit *= 2
    return index


class Wire:
    def __init__(self, sends, recvs):
        self.sends, self.recvs = sends, recvs
        self.n_sends = self.n_recvs = 0
        self.open = []

    def slots(self, count):
        first = self.n_recvs
        self.n_recvs += count
        return first

    def start(self, src, dst, recv, device, when=None):
        copy = pltpu.make_async_remote_copy(
            src_ref=src,
            dst_ref=dst,
            send_sem=self.sends.at[self.n_sends],
            recv_sem=self.recvs.at[recv],
            device_id=device,
            device_id_type=MESH,
        )
        self.n_sends += 1
        guard(when, copy.start)
        self.open.append((when, copy))

    def arrived(self, dst, recv, device):
        pltpu.make_async_remote_copy(
            src_ref=dst,
            dst_ref=dst,
            send_sem=self.sends.at[0],
            recv_sem=self.recvs.at[recv],
            device_id=device,
            device_id_type=MESH,
        ).wait_recv()

    def finish(self):
        for when, copy in self.open:
            guard(when, copy.wait_send)
        self.open = []


def guard(when, action):
    if when is None:
        action()
    else:
        pl.when(when)(action)


def greet(targets):
    barrier = pltpu.get_barrier_semaphore()
    for device, when in targets:
        guard(
            when,
            lambda device=device: pl.semaphore_signal(
                barrier, inc=1, device_id=device, device_id_type=MESH
            ),
        )
    count = sum(1 if when is None else when.astype(jnp.int32) for _, when in targets)
    pl.semaphore_wait(barrier, count)


def plane_ids(e):
    return {m: {"expert": flip(e, m)} for m in (1, 2, 3)}


class RowsGather:
    def __init__(self, wire, ref, e, z, c, nc, half):
        self.wire, self.ref, self.e, self.z, self.c, self.nc = wire, ref, e, z, c, nc
        self.cols = (pl.ds(0, half), pl.ds(half, ref.shape[-1] - half))
        self.line = wire.slots(nc)
        self.plane = wire.slots(nc * 6)
        self.core = wire.slots(nc)
        self.ids = plane_ids(e)

    def go(self, steps):
        for step in steps.split():
            action = {"s": self.spread, "f": self.forward, "h": self.share, "c": self.complete}
            action[step[0]](*map(int, step[1:]))

    def at(self, r, zs, half):
        return self.ref.at[flip(self.e, r), zs, self.c, :, self.cols[half]]

    def slot(self, k, r, half):
        return self.plane + k * 6 + (r - 1) * 2 + half

    def spread(self, k):
        wire, z, nc = self.wire, self.z, self.nc
        zs = flip(z, k)
        whole = self.ref.at[self.e, zs, self.c]
        if k:
            wire.arrived(whole, self.line + zs, {"context": zs})
        wire.start(
            whole, whole, self.line + zs, {"context": z + 1}, when=(zs <= z) & (z < nc - 1)
        )
        wire.start(whole, whole, self.line + zs, {"context": z - 1}, when=(zs >= z) & (z > 0))
        for half, mask in ((0, 1), (1, 2), (1, 1), (0, 2)):
            part = self.at(0, zs, half)
            wire.start(part, part, self.slot(k, mask, half), self.ids[mask])

    def forward(self, k):
        zs = flip(self.z, k)
        for half, mask in ((0, 1), (1, 2)):
            part = self.at(mask, zs, half)
            self.wire.arrived(part, self.slot(k, mask, half), self.ids[mask])
            self.wire.start(part, part, self.slot(k, 3, half), self.ids[3 - mask])

    def share(self, k):
        zs = flip(self.z, k)
        for r, half in ((1, 1), (2, 0), (3, 0), (3, 1)):
            self.wire.arrived(self.at(r, zs, half), self.slot(k, r, half), self.ids[r])
        part = self.ref.at[:, zs, self.c]
        self.wire.start(part, part, self.core + k, {"dp": 1 - self.c})

    def complete(self):
        for k in range(self.nc):
            zs = flip(self.z, k)
            self.wire.arrived(self.ref.at[:, zs, 1 - self.c], self.core + k, {"dp": 1 - self.c})


class PlaneGather:
    def __init__(self, wire, ref, e):
        self.wire, self.ref = wire, ref
        self.half = ref.shape[-1] // 2
        self.ids = plane_ids(e)
        self.first = wire.slots(6)

    def at(self, r, half):
        return self.ref.at[r, :, pl.ds(half * self.half, self.half)]

    def slot(self, r, half):
        return self.first + (r - 1) * 2 + half

    def spread(self):
        for half, mask in ((0, 1), (1, 2), (1, 1), (0, 2)):
            self.wire.start(
                self.at(0, half), self.at(mask, half), self.slot(mask, half), self.ids[mask]
            )

    def forward(self):
        for half, mask in ((0, 1), (1, 2)):
            self.wire.arrived(self.at(mask, half), self.slot(mask, half), self.ids[mask])
            self.wire.start(
                self.at(mask, half), self.at(3, half), self.slot(3, half), self.ids[3 - mask]
            )

    def near(self, r):
        half = 1 if r == 1 else 0
        self.wire.arrived(self.at(r, half), self.slot(r, half), self.ids[r])

    def far(self):
        for half in (0, 1):
            self.wire.arrived(self.at(3, half), self.slot(3, half), self.ids[3])

    def complete(self):
        self.near(1)
        self.near(2)
        self.far()


def swap_halves(values):
    return pltpu.roll(values, HEAD_DIMENSION // 2, 1)


def front_kernel(
    nc,
    experts,
    x_ref,
    qkv_shard,
    small_shard,
    wo_shard,
    cot_ref,
    cos_ref,
    sin_ref,
    routes_ref,
    wk_hbm,
    wq_hbm,
    wo_hbm,
    cot_hbm,
    gate_all,
    gate_columns,
    inputs_ref,
    query_ref,
    kv_ref,
    heads_ref,
    hidden_ref,
    expert_in_ref,
    gains_ref,
    wk_all,
    wq_all,
    wo_all,
    cot_all,
    kv_scr,
    q_scr,
    sends,
    recvs,
    out_sems,
):
    e, z, c = (lax.axis_index(a) for a in ("expert", "context", "dp"))
    size = HEAD_DIMENSION
    tokens, width = x_ref.shape
    query_width = QUERY_HEADS * size
    kv_width = 2 * KEY_VALUE_HEADS * size
    wire = Wire(sends, recvs)
    ids = plane_ids(e)
    greet(
        [(ids[m], None) for m in (1, 2, 3)]
        + [({"dp": 1 - c}, None), ({"context": z + 1}, z < nc - 1), ({"context": z - 1}, z > 0)]
    )
    wk_all[e, z, c, :, pl.ds(0, kv_width)] = qkv_shard[:, pl.ds(query_width, kv_width)]
    wk_all[e, z, c, :, pl.ds(kv_width, SMALL)] = small_shard[...]
    gather_k = RowsGather(wire, wk_all, e, z, c, nc, 256)
    gather_q = RowsGather(wire, wq_all, e, z, c, nc, 768)
    gather_o = RowsGather(wire, wo_all, e, z, c, nc, 768)
    gather_cot = PlaneGather(wire, cot_all, e)
    gather_k.go("s0")
    wq_all[e, z, c] = qkv_shard[:, pl.ds(0, query_width)]
    wo_all[e, z, c] = wo_shard[...]
    cot_all[0] = cot_ref[...]
    rows = x_ref[...].astype(F32)
    scale1 = lax.rsqrt(jnp.mean(rows * rows, -1, keepdims=True) + EPSILON)
    gather_k.go("s1 f0 s2 f1 h0 s3 f2 h1 f3")
    gather_q.go("s0")
    gather_k.go("h2 h3")
    gather_q.go("s1 f0")
    gather_k.go("c")

    small = wk_all[:, :, :, :, pl.ds(kv_width, SMALL)].reshape(width, SMALL)
    small = jnp.transpose(small.astype(F32))
    gain_first, gain_second = small[experts : experts + 1], small[experts + 1 : experts + 2]
    gains_ref[0:1] = gain_first
    gains_ref[1:2] = gain_second
    inputs_ref[...] = (rows * scale1 * gain_first).astype(BF16)
    kv_scr[...] = dot_nn(inputs_ref[...], wk_all[...].reshape(width, kv_width + SMALL))

    def turned(head):
        return (head * cos_ref[...] + swap_halves(head) * sin_ref[...]).astype(BF16)

    for j in range(KEY_VALUE_HEADS):
        columns = pl.ds(j * size, size)
        kv_ref[z, :, columns] = turned(kv_scr[:, columns])
    values = pl.ds(kv_width // 2, kv_width // 2)
    kv_ref[z, :, values] = kv_scr[:, values].astype(BF16)
    line = wire.slots(nc)
    wire.start(kv_ref.at[z], kv_ref.at[z], line, {"context": z + 1}, when=z < nc - 1)

    def pass_on(step):
        block = kv_ref.at[z - step]
        pl.when(z >= step)(lambda: wire.arrived(block, line + step - 1, {"context": z - 1}))
        wire.start(
            block, block, line + step, {"context": z + 1}, when=(z >= step) & (z < nc - 1)
        )

    outs = [
        pltpu.make_async_copy(source, dest, out_sems.at[n])
        for n, (source, dest) in enumerate(
            ((wk_all, wk_hbm), (wq_all, wq_hbm), (wo_all, wo_hbm), (cot_all, cot_hbm))
        )
    ]
    outs[0].start()
    for later in range(1, nc):

        def clear(later=later):
            kv_ref[z + later] = jnp.zeros(kv_ref.shape[1:], BF16)

        pl.when(z + later < nc)(clear)
    gather_q.go("s2 f1 s3")
    pass_on(1)
    gather_q.go("f2 h0 f3")
    pass_on(2)
    gather_q.go("h1 h2")
    gather_o.go("s0 s1")
    for step in range(3, nc):
        pass_on(step)
    gather_q.go("h3 c")
    outs[1].start()

    @pl.loop(0, query_width // 256)
    def _(n):
        columns = pl.ds(pl.multiple_of(n * 256, 256), 256)
        q_scr[:, columns] = dot_nn(
            inputs_ref[...], wq_all[:, :, :, :, columns].reshape(width, 256)
        )

    gather_o.go("f0 s2 f1 s3")

    @pl.loop(0, QUERY_HEADS)
    def _(h):
        columns = pl.ds(pl.multiple_of(h * size, size), size)
        query_ref[:, columns] = turned(q_scr[:, columns])

    logits = kv_scr[:, pl.ds(kv_width, SMALL)]
    lanes = lax.broadcasted_iota(jnp.int32, logits.shape, 1)
    named = lanes == routes_ref[:, 0:1]
    for k in range(1, TOP):
        named = named | (lanes == routes_ref[:, k : k + 1])
    logits = jnp.where(named, logits, MASKED)
    expd = jnp.exp(logits - jnp.max(logits, -1, keepdims=True))
    gates = expd / jnp.sum(expd, -1, keepdims=True)
    gate_all[0] = jnp.transpose(gates)[:GATE_ROWS]
    gate_slot = wire.slots(3)
    for r in (1, 2, 3):
        wire.start(gate_all.at[0], gate_all.at[r], gate_slot + r - 1, ids[r])
    gather_o.go("f2 h0 f3")
    gather_cot.spread()
    gather_o.go("h1")

    length = nc * tokens
    group = QUERY_HEADS // KEY_VALUE_HEADS

    def attend(first, last):
        j = first // group
        key = kv_ref[:, :, pl.ds(j * size, size)].reshape(length, size)
        value = kv_ref[:, :, pl.ds(kv_width // 2 + j * size, size)].reshape(length, size)

        @pl.loop(first, last)
        def _(h):
            column = pl.multiple_of(h * size, size)
            scores = dot_nt(query_ref[:, pl.ds(column, size)], key) * (size**-0.5)
            row = z * tokens + lax.broadcasted_iota(jnp.int32, scores.shape, 0)
            place = lax.broadcasted_iota(jnp.int32, scores.shape, 1)
            scores = jnp.where(place <= row, scores, MASKED)
            expd = jnp.exp(scores - jnp.max(scores, -1, keepdims=True))
            total = jnp.sum(expd, -1, keepdims=True)
            mixed = dot_nn(expd.astype(BF16), value) / total
            heads_ref[:, pl.ds(column, size)] = mixed.astype(BF16)

    attend(0, group)
    gather_o.go("h2 h3")
    attend(group, group + group // 2)
    gather_cot.forward()
    attend(group + group // 2, QUERY_HEADS)
    gather_o.go("c")
    outs[2].start()
    part = width // wo_all.shape[0]
    for block in range(wo_all.shape[0]):
        weight = wo_all[block].reshape(part, width)
        columns = pl.ds(block * part, part)
        hidden_ref[:, columns] = x_ref[:, columns].astype(F32) + dot_nt(heads_ref[...], weight)
    hidden = hidden_ref[...]
    scale2 = lax.rsqrt(jnp.mean(hidden * hidden, -1, keepdims=True) + EPSILON)
    expert_in_ref[...] = (hidden * scale2 * gains_ref[1:2]).astype(BF16)
    for r in (1, 2, 3):
        wire.arrived(gate_all.at[r], gate_slot + r - 1, ids[r])
    for r in range(gate_all.shape[0]):
        rest = jnp.zeros((SMALL - GATE_ROWS, tokens), F32)
        turned_gates = jnp.transpose(jnp.concatenate([gate_all[r], rest], 0))
        both = [
            jnp.sum(jnp.where(lanes == e * EXP_DEV + i, turned_gates, 0.0), -1, keepdims=True)
            for i in range(EXP_DEV)
        ]
        gate_columns[r] = jnp.where(lanes == 0, both[0], jnp.where(lanes == 1, both[1], 0.0))
    gather_cot.complete()
    outs[3].start()
    for copy in outs:
        copy.wait()
    wire.finish()


def front(operands, sizes):
    ne, nc, nd = sizes
    x, qkv_shard = operands[:2]
    tokens, width = x.shape
    rows, qkv_width = qkv_shard.shape
    query_width = QUERY_HEADS * HEAD_DIMENSION
    kv_width = qkv_width - query_width
    gathered = [
        ((ne, nc, nd, rows, kv_width + SMALL), BF16),
        ((ne, nc, nd, rows, query_width), BF16),
        ((ne, nc, nd, rows, width), BF16),
        ((ne, tokens, width), BF16),
    ]
    shapes = gathered + [
        ((ne, GATE_ROWS, tokens), F32),
        ((ne, tokens, SMALL), F32),
        ((tokens, width), BF16),
        ((tokens, query_width), BF16),
        ((nc, tokens, kv_width), BF16),
        ((tokens, query_width), BF16),
        ((tokens, width), F32),
        ((tokens, width), BF16),
        ((8, width), F32),
    ]
    copies = 160
    vmem = pl.BlockSpec(memory_space=pltpu.VMEM)
    anywhere = pl.BlockSpec(memory_space=pl.ANY)
    return pl.pallas_call(
        functools.partial(front_kernel, nc, EXP_DEV * ne),
        out_shape=[jax.ShapeDtypeStruct(*s) for s in shapes],
        in_specs=[vmem] * len(operands),
        out_specs=[anywhere] * 4 + [vmem] * (len(shapes) - 4),
        scratch_shapes=[pltpu.VMEM(*s) for s in gathered]
        + [
            pltpu.VMEM((tokens, kv_width + SMALL), F32),
            pltpu.VMEM((tokens, query_width), F32),
            pltpu.SemaphoreType.DMA((copies,)),
            pltpu.SemaphoreType.DMA((copies,)),
            pltpu.SemaphoreType.DMA((4,)),
        ],
        compiler_params=pltpu.CompilerParams(
            collective_id=0, has_side_effects=True, vmem_limit_bytes=56 * MIB
        ),
    )(*operands)


class PlaneScatter:
    def __init__(self, wire, land, ids):
        self.wire, self.part, self.land, self.ids = wire, None, land, ids
        self.half = land.shape[-1]
        self.first = wire.slots(6)

    def at(self, r, half):
        return self.part.at[r - 1, :, pl.ds(half * self.half, self.half)]

    def send(self, r, half, mask, slot):
        self.wire.start(self.at(r, half), self.land.at[slot], self.first + slot, self.ids[mask])

    def near(self, r):
        self.send(r, r - 1, r, r - 1)

    def far(self):
        self.send(3, 0, 1, 2)
        self.send(3, 1, 2, 3)

    def relay(self):
        for half, r in ((0, 2), (1, 1)):
            slot = 2 + half
            self.wire.arrived(self.land.at[slot], self.first + slot, self.ids[3 - r])
            part = self.at(r, half)
            part[...] = (part[...].astype(F32) + self.land[slot].astype(F32)).astype(BF16)
            self.send(r, half, r, 4 + half)

    def total(self, own):
        for slot, half, mask in ((0, 0, 1), (1, 1, 2), (4, 0, 2), (5, 1, 1)):
            self.wire.arrived(self.land.at[slot], self.first + slot, self.ids[mask])
            columns = pl.ds(half * self.half, self.half)
            own[:, columns] += self.land[slot].astype(F32)


class LineScatter:
    def __init__(self, wire, block, lands, z, nc, up=True):
        self.wire, self.block, self.lands, self.z, self.nc = wire, block, lands, z, nc
        self.up = up
        self.first = [wire.slots(nc - 1), wire.slots(nc - 1)]

    def arrive(self, way, index, j):
        land = self.lands[way].at[index]
        self.wire.arrived(land, self.first[way] + index, {"context": self.z})
        block = self.block(j)
        block[...] = (block[...].astype(F32) + self.lands[way][index].astype(F32)).astype(BF16)

    def move(self, way, j):
        z, nc = self.z, self.nc
        inner, index, near = ((z > 0), j - z, z + 1) if way == 0 else ((z < nc - 1), z - j, z - 1)
        wanted = (j > z) if way == 0 else (j < z)
        pl.when(wanted & inner)(lambda: self.arrive(way, index, j))
        self.wire.start(
            self.block(j),
            self.lands[way].at[index - 1],
            self.first[way] + index - 1,
            {"context": near},
            when=wanted,
        )

    def step(self, s):
        if self.up:
            self.move(0, self.nc - s)
        self.move(1, s - 1)

    def last(self):
        if self.up:
            pl.when(self.z > 0)(lambda: self.arrive(0, 0, self.z))
        pl.when(self.z < self.nc - 1)(lambda: self.arrive(1, 0, self.z))


class RowsScatter:
    def __init__(self, wire, buf, core, plane, lines, e, z, c, nc, start, width, half):
        self.wire, self.buf, self.core, self.plane = wire, buf, core, plane
        self.e, self.c = e, c
        self.all = pl.ds(start, width)
        self.cols = (pl.ds(start, half), pl.ds(start + half, width - half))
        self.ids = plane_ids(e)
        self.core_slot = wire.slots(1)
        self.first = wire.slots(6)
        rows = buf.shape[2] // nc
        self.line = LineScatter(
            wire,
            lambda j: buf.at[c, e, pl.ds(pl.multiple_of(j * rows, rows), rows), self.all],
            lines,
            z,
            nc,
        )

    def share(self):
        self.wire.start(
            self.buf.at[1 - self.c, :, :, self.all], self.core, self.core_slot, {"dp": 1 - self.c}
        )

    def at(self, r, half):
        return self.buf.at[self.c, flip(self.e, r), :, self.cols[half]]

    def send(self, r, half, mask, slot):
        self.wire.start(
            self.at(r, half), self.plane(slot, half), self.first + slot, self.ids[mask]
        )

    def merge(self, before=None):
        self.wire.arrived(self.core, self.core_slot, {"dp": 1 - self.c})
        for r in (3, 1, 2, 0):
            block = flip(self.e, r)
            part = self.buf.at[self.c, block, :, self.all]
            part[...] = (part[...].astype(F32) + self.core[block].astype(F32)).astype(BF16)
            if r == 3:
                if before is not None:
                    before()
                self.send(3, 0, 1, 2)
                self.send(3, 1, 2, 3)
            elif r:
                self.send(r, r - 1, r, r - 1)

    def add(self, r, half, slot, mask):
        land = self.plane(slot, half)
        self.wire.arrived(land, self.first + slot, self.ids[mask])
        part = self.at(r, half)
        part[...] = (part[...].astype(F32) + land[...].astype(F32)).astype(BF16)

    def relay(self):
        for half, r in ((0, 2), (1, 1)):
            self.add(r, half, 2 + half, 3 - r)
            self.send(r, half, r, 4 + half)

    def total(self):
        for slot, half, mask in ((0, 0, 1), (1, 1, 2), (4, 0, 2), (5, 1, 1)):
            self.add(0, half, slot, mask)


class ExpertLine:
    pieces = 2

    def __init__(self, wire, base, core, land, ins, outs, sems, z, nc):
        self.wire, self.base, self.core, self.land = wire, base, core, land
        self.ins, self.outs, self.sems, self.z, self.nc = ins, outs, sems, z, nc
        self.end = (z == 0) | (z == nc - 1)
        self.inner = jnp.logical_not(self.end)
        self.first = wire.slots((nc + 1) * self.pieces)
        self.sent = []

    def combine(self, sources, dest, out):
        step = self.ins.shape[2]
        count = dest.shape[0] // step

        def loads(p):
            rows = pl.ds(p * step, step)
            return [
                pltpu.make_async_copy(
                    source.at[rows], self.ins.at[k, p % 2], self.sems.at[2 * k + p % 2]
                )
                for k, source in enumerate(sources)
            ]

        def store(p):
            return pltpu.make_async_copy(
                out.at[p % 2], dest.at[pl.ds(p * step, step)], self.sems.at[8 + p % 2]
            )

        for copy in loads(0):
            copy.start()
        for p in range(count):
            if p + 1 < count:
                for copy in loads(p + 1):
                    copy.start()
            for copy in loads(p):
                copy.wait()
            if p > 1:
                store(p - 2).wait()
            total = self.ins[0, p % 2].astype(F32)
            for k in range(1, len(sources)):
                total = total + self.ins[k, p % 2].astype(F32)
            out[p % 2] = total.astype(out.dtype)
            store(p).start()
        for p in range(max(0, count - 2), count):
            store(p).wait()

    def cores(self, r):
        j = flip(self.z, r)
        self.combine([self.base.at[j], self.core.at[j]], self.base.at[j], self.outs[0])

    def rows(self, p):
        rows = self.base.shape[1] // self.pieces
        return pl.ds(p * rows, rows)

    def copy(self, r, p, number):
        target, slot = flip(self.z, r), self.z
        if r == 3:
            target = jnp.where(self.end, flip(self.z, 1), target)
            slot = jnp.where(self.end, self.nc, slot)
        return pltpu.make_async_remote_copy(
            src_ref=self.base.at[flip(self.z, r), self.rows(p)],
            dst_ref=self.land.at[slot, self.rows(p)],
            send_sem=self.wire.sends.at[number],
            recv_sem=self.wire.recvs.at[self.first + slot * self.pieces + p],
            device_id={"context": target},
            device_id_type=MESH,
        )

    def send(self, r, p, when=None):
        number = len(self.sent)
        guard(when, self.copy(r, p, number).start)
        self.sent.append((when, r, p, number))

    def finish(self):
        for when, r, p, number in self.sent:
            guard(when, self.copy(r, p, number).wait_send)

    def arrived(self, slot):
        for p in range(self.pieces):
            self.wire.arrived(
                self.land.at[slot, self.rows(p)],
                self.first + slot * self.pieces + p,
                {"context": self.z},
            )

    def relay(self):
        def add():
            self.arrived(self.nc)
            j = flip(self.z, 2)
            self.combine([self.base.at[j], self.land.at[self.nc]], self.base.at[j], self.outs[0])

        pl.when(self.inner)(add)

    def last(self, result):
        z = self.z
        near = [self.base.at[z], self.land.at[flip(z, 1)], self.land.at[flip(z, 2)]]
        self.arrived(flip(z, 1))
        self.arrived(flip(z, 2))
        pl.when(self.end)(lambda: self.combine(near, result, self.outs[1]))

        def inner():
            self.arrived(flip(z, 3))
            self.combine(near + [self.land.at[flip(z, 3)]], result, self.outs[1])

        pl.when(self.inner)(inner)


def back_kernel(
    nc,
    experts,
    gates_ref,
    gate_ref,
    gains_ref,
    cos_ref,
    sin_ref,
    expert_in_hbm,
    cot_hbm,
    w_gu_hbm,
    w_dn_hbm,
    x_hbm,
    inputs_hbm,
    query_hbm,
    kv_hbm,
    heads_hbm,
    hidden_hbm,
    wk_hbm,
    wq_hbm,
    o_hbm,
    layer_ref,
    d_x_ref,
    sum_q_ref,
    sum_o_ref,
    sum_e_hbm,
    base_hbm,
    core_hbm,
    land_hbm,
    x_all,
    y_land,
    dx_land,
    core_q,
    plane_q,
    plane_k,
    lines_o,
    lines_q,
    lines_k,
    dkv_land,
    d_in_ref,
    mixture_ref,
    dg_lanes,
    dg_part,
    dg_land,
    ins,
    out_low,
    out_wide,
    sends_1,
    recvs_1,
    sends_2,
    recvs_2,
    sends_e,
    recvs_e,
    hand_sends,
    hand_recvs,
    stage_sems,
    load_sems,
    sum_sems,
    credits,
):
    e, z, c = (lax.axis_index(a) for a in ("expert", "context", "dp"))
    size = HEAD_DIMENSION
    blocks, tokens, width = cot_hbm.shape
    ff = w_dn_hbm.shape[1]
    query_width = QUERY_HEADS * size
    key_width = KEY_VALUE_HEADS * size
    qkv_width = query_width + 2 * key_width
    rest = wk_hbm.shape[-1]
    grad_width = base_hbm.shape[-1]
    ids = plane_ids(e)
    sibling = {"dp": 1 - c}
    wire_1, wire_2, wire_e = Wire(sends_1, recvs_1), Wire(sends_2, recvs_2), Wire(sends_e, recvs_e)
    expert = ExpertLine(
        wire_e, base_hbm, core_hbm, land_hbm, ins, (out_low, out_wide), sum_sems, z, nc
    )
    gather = PlaneGather(wire_1, x_all, e)
    scatter_dx = PlaneScatter(wire_1, dx_land, ids)
    scatter_y = PlaneScatter(wire_1, y_land, ids)
    dg_slot = wire_1.slots(3)

    def token_phase(w_gu, w_dn, cot_all, a_all, dgu_all, y_part, dx_part, stage):
        scatter_dx.part, scatter_y.part = dx_part, y_part
        loads = [
            pltpu.make_async_copy(source, dest, load_sems.at[n])
            for n, (source, dest) in enumerate(
                ((expert_in_hbm, x_all.at[0]), (w_gu_hbm, w_gu), (w_dn_hbm, w_dn), (cot_hbm, cot_all))
            )
        ]
        for copy in loads:
            copy.start()
        greet(
            [(ids[m], None) for m in (1, 2, 3)]
            + [(sibling, None), ({"context": flip(z, 2)}, None)]
            + [({"context": z + 1}, z < nc - 1), ({"context": z - 1}, z > 0)]
        )
        loads[0].wait()
        gather.spread()
        for copy in loads[1:]:
            copy.wait()
        step = 256
        wide = 512

        def block(r):
            dg_lanes[...] = jnp.zeros_like(dg_lanes)
            for i in range(EXP_DEV):

                @pl.loop(0, ff // step)
                def _(f):
                    column = pl.multiple_of(f * step, step)
                    rows, grads = x_all[r], cot_all[r]
                    gate_part = dot_nn(rows, w_gu[i, :, pl.ds(column, step)])
                    up_part = dot_nn(rows, w_gu[i, :, pl.ds(ff + column, step)])
                    raw = dot_nt(grads, w_dn[i, pl.ds(column, step), :])
                    gate = gates_ref[r][:, i : i + 1]
                    sigma = jax.nn.sigmoid(gate_part)
                    silu = gate_part * sigma
                    act = silu * up_part
                    lanes = lax.broadcasted_iota(jnp.int32, dg_lanes.shape, 1)
                    dg_lanes[...] += jnp.where(
                        lanes == e * EXP_DEV + i, jnp.sum(act * raw, -1, keepdims=True), 0.0
                    )
                    a_all[r, :, pl.ds(i * ff + column, step)] = (act * gate).astype(BF16)
                    d_act = raw * gate
                    d_gate_part = d_act * up_part * sigma * (1.0 + gate_part * (1.0 - sigma))
                    first = i * 2 * ff + column
                    dgu_all[r, :, pl.ds(first, step)] = d_gate_part.astype(BF16)
                    dgu_all[r, :, pl.ds(first + ff, step)] = (d_act * silu).astype(BF16)

            @pl.loop(0, width // wide)
            def _(n):
                columns = pl.ds(pl.multiple_of(n * wide, wide), wide)
                d_rows = dot_nt(dgu_all[r, :, pl.ds(0, 2 * ff)], w_gu[0, columns, :])
                d_rows += dot_nt(dgu_all[r, :, pl.ds(2 * ff, 2 * ff)], w_gu[1, columns, :])
                weight = w_dn[:, :, columns].reshape(EXP_DEV * ff, wide)
                out = dot_nn(a_all[r], weight)
                if r == 0:
                    d_in_ref[:, columns] = d_rows
                    mixture_ref[:, columns] = out
                else:
                    dx_part[r - 1, :, columns] = d_rows.astype(BF16)
                    y_part[r - 1, :, columns] = out.astype(BF16)

            dg_part[r] = jnp.transpose(dg_lanes[...])[:GATE_ROWS]
            if r:
                wire_1.start(dg_part.at[r], dg_land.at[r - 1], dg_slot + r - 1, ids[r])

        block(0)
        gather.forward()
        gather.near(1)
        block(1)
        scatter_dx.near(1)
        scatter_y.near(1)
        gather.near(2)
        block(2)
        scatter_dx.near(2)
        scatter_y.near(2)
        gather.far()
        block(3)
        scatter_dx.far()
        scatter_y.far()

        half_rows = width // nc // 2

        def keep(r, slot):
            return pltpu.make_async_copy(
                stage.at[slot, c], base_hbm.at[flip(z, r)], stage_sems.at[slot]
            )

        def hand(r, slot):
            return pltpu.make_async_remote_copy(
                src_ref=stage.at[slot, 1 - c],
                dst_ref=core_hbm.at[flip(z, r)],
                send_sem=hand_sends.at[r],
                recv_sem=hand_recvs.at[r],
                device_id=sibling,
                device_id_type=MESH,
            )

        def weight_grads(r):
            slot = r % 2
            if r + 2 < nc:
                hand(r + 2, slot).wait_send()
            columns = pl.ds(pl.multiple_of(flip(z, r) * 2 * half_rows, 2 * half_rows), 2 * half_rows)
            for first, source, grad in ((0, x_all, dgu_all), (EXP_DEV * 2 * ff, cot_all, a_all)):
                rows = source[:, :, columns].reshape(blocks * tokens, 2 * half_rows)

                @pl.loop(0, grad.shape[-1] // ff)
                def _(i):
                    column = pl.multiple_of(i * ff, ff)
                    part = grad[:, :, pl.ds(column, ff)].reshape(blocks * tokens, ff)
                    result = dot_tn(rows, part).astype(BF16).reshape(2, half_rows, ff)
                    stage[slot, :, :, pl.ds(pl.multiple_of(first + column, ff), ff)] = result

            keep(r, slot).start()
            hand(r, slot).start()

        def settle(r):
            keep(r, r % 2).wait()
            hand(r, r % 2).wait_recv()
            expert.cores(r)

        weight_grads(3)
        scatter_dx.relay()
        weight_grads(2)
        settle(3)
        expert.send(3, 0)
        expert.send(3, 1)
        scatter_y.relay()
        weight_grads(1)
        settle(2)
        expert.send(2, 0, when=expert.end)
        weight_grads(0)
        settle(1)
        scatter_dx.total(d_in_ref)
        for r in (1, 2):
            pl.semaphore_signal(credits.at[r], inc=1, device_id=ids[r], device_id_type=MESH)
        keep(0, 0).wait()
        for r in (1, 0):
            hand(r, r % 2).wait_send()
        wire_1.finish()
        pl.semaphore_signal(credits.at[0], inc=1, device_id=sibling, device_id_type=MESH)

    def token_rows_phase(
        weight,
        grads_o,
        grads_q,
        x_ref,
        inputs_ref,
        query_ref,
        kv_ref,
        heads_ref,
        hidden_ref,
        cot_ref,
        d_hidden_ref,
        d_attn_ref,
        d_heads_ref,
        d_all_ref,
        d_inputs_ref,
        rows_ref,
        dkv_acc,
        dkv_ref,
    ):
        planes = grads_o.shape[1]
        part = width // planes
        sources = (
            (hidden_hbm, hidden_ref),
            (cot_hbm.at[0], cot_ref),
            (o_hbm, weight.at[:, pl.ds(0, width)]),
            (heads_hbm, heads_ref),
            (query_hbm, query_ref),
            (kv_hbm, kv_ref),
            (x_hbm, x_ref),
            (inputs_hbm, inputs_ref),
        )
        loads = [
            pltpu.make_async_copy(source, dest, load_sems.at[4 + n])
            for n, (source, dest) in enumerate(sources)
        ]
        for copy in loads:
            copy.start()

        def rows_scatter(buf, core, plane, lines, start, count, half):
            return RowsScatter(
                wire_2,
                buf,
                core,
                plane,
                [lines.at[0], lines.at[1]],
                e,
                z,
                c,
                nc,
                start,
                count,
                half,
            )

        rows_of = part // 2
        scatter_o = rows_scatter(
            grads_o,
            x_all.at[:, pl.ds(0, rows_of)],
            lambda slot, half: dx_land.at[slot, pl.ds(0, rows_of)],
            lines_o,
            0,
            width,
            width // 2,
        )
        scatter_q = rows_scatter(
            grads_q,
            core_q.at[:, :, pl.ds(0, query_width)],
            lambda slot, half: plane_q.at[slot],
            lines_q,
            0,
            query_width,
            query_width // 2,
        )
        rest_half = rest // 256 * 128
        scatter_k = rows_scatter(
            grads_q,
            core_q.at[:, :, pl.ds(query_width, rest)],
            lambda slot, half: plane_k.at[
                slot, :, pl.ds(0, rest - rest_half if half else rest_half)
            ],
            lines_k,
            query_width,
            rest,
            rest_half,
        )
        scatter_kv = [
            LineScatter(
                wire_2,
                lambda j, h=h: dkv_ref.at[h, j],
                [dkv_land.at[h], dkv_land.at[h]],
                z,
                nc,
                up=False,
            )
            for h in range(KEY_VALUE_HEADS)
        ]

        loads[0].wait()
        loads[1].wait()
        hidden, d_in = hidden_ref[...], d_in_ref[...]
        scale2 = lax.rsqrt(jnp.mean(hidden * hidden, -1, keepdims=True) + EPSILON)
        scaled = d_in * gains_ref[1:2]
        mean = jnp.mean(scaled * hidden, -1, keepdims=True)
        d_hidden = cot_ref[...].astype(F32) + scale2 * scaled
        d_hidden = d_hidden - hidden * (scale2 * scale2 * scale2 * mean)
        d_hidden_ref[...] = d_hidden
        d_attn_ref[...] = d_hidden.astype(BF16)
        rows_ref[...] = jnp.zeros_like(rows_ref)
        rows_ref[experts + 1 : experts + 2, :] = jnp.sum(d_in * hidden * scale2, 0, keepdims=True)

        loads[2].wait()

        @pl.loop(0, query_width // 256)
        def _(n):
            columns = pl.ds(pl.multiple_of(n * 256, 256), 256)
            d_heads_ref[:, columns] = dot_nn(d_attn_ref[...], weight[:, columns]).astype(BF16)

        load_q = [
            pltpu.make_async_copy(wq_hbm, weight.at[:, pl.ds(0, query_width)], load_sems.at[0]),
            pltpu.make_async_copy(wk_hbm, weight.at[:, pl.ds(query_width, rest)], load_sems.at[1]),
        ]
        for copy in load_q:
            copy.start()
        loads[3].wait()

        def row_grads(buf, left, right, first, count, extra=None):
            @pl.loop(0, planes)
            def _(block):
                columns = pl.ds(pl.multiple_of(block * part, part), part)
                result = dot_tn(left[:, columns], right)
                if extra is not None:
                    result = result + extra(columns)
                result = result.astype(BF16).reshape(nc, 2, part // nc // 2, count)
                for half in range(2):
                    buf[half, block, :, pl.ds(first, count)] = result[:, half].reshape(
                        part // 2, count
                    )

        row_grads(grads_o, d_attn_ref, heads_ref[...], 0, width)
        pl.semaphore_wait(credits.at[0], 1)
        scatter_o.share()

        length = nc * tokens
        group = QUERY_HEADS // KEY_VALUE_HEADS
        for copy in loads[4:6]:
            copy.wait()
        dkv_acc[...] = jnp.zeros_like(dkv_acc)

        def attend(j, first, last):
            key = kv_ref[:, :, pl.ds(j * size, size)].reshape(length, size)
            value = kv_ref[:, :, pl.ds(key_width + j * size, size)].reshape(length, size)

            @pl.loop(j * group + first, j * group + last)
            def _(h):
                columns = pl.ds(pl.multiple_of(h * size, size), size)
                query, grad = query_ref[:, columns], d_heads_ref[:, columns]
                probs = masked_probs(z * tokens, query, key)
                d_probs = dot_nt(grad, value)
                inner = jnp.sum(probs * d_probs, axis=-1, keepdims=True)
                d_raw = (probs * (d_probs - inner) * (size**-0.5)).astype(BF16)
                d_query = dot_nn(d_raw, key)
                d_query = d_query * cos_ref[...] - swap_halves(d_query) * sin_ref[...]
                d_all_ref[:, columns] = d_query.astype(BF16)
                dkv_acc[j, :, pl.ds(0, size)] += dot_tn(d_raw, query)
                dkv_acc[j, :, pl.ds(size, size)] += dot_tn(probs.astype(BF16), grad)

        def round_kv(j):
            for block in range(nc):
                rows = dkv_acc[j, pl.ds(block * tokens, tokens), :]
                dkv_ref[j, block] = rows.astype(BF16)

        def enter():
            pl.semaphore_wait(credits.at[1], 1)
            pl.semaphore_wait(credits.at[2], 1)

        attend(0, 0, group)
        round_kv(0)
        scatter_kv[0].step(1)
        scatter_o.merge(enter)
        attend(1, 0, group // 2)
        scatter_kv[0].step(2)
        attend(1, group // 2, group)
        round_kv(1)
        scatter_kv[1].step(1)
        scatter_kv[0].step(3)
        scatter_o.relay()

        for copy in loads[6:]:
            copy.wait()
        row_grads(grads_q, inputs_ref, d_all_ref[:, pl.ds(0, query_width)], 0, query_width)
        scatter_q.share()
        scatter_kv[1].step(2)
        scatter_y.total(mixture_ref)
        layer_ref[...] = (hidden_ref[...] + mixture_ref[...]).astype(BF16)
        scatter_kv[1].step(3)
        for r in (1, 2):
            scatter_kv[r - 1].last()
        expert.send(2, 1, when=expert.end)
        expert.send(1, 0)
        scatter_o.total()
        scatter_q.merge()

        for h in range(KEY_VALUE_HEADS):
            grad = dkv_ref[h, z, :, pl.ds(0, size)].astype(F32)
            grad = grad * cos_ref[...] - swap_halves(grad) * sin_ref[...]
            d_all_ref[:, pl.ds(query_width + h * size, size)] = grad.astype(BF16)
            d_all_ref[:, pl.ds(query_width + key_width + h * size, size)] = dkv_ref[
                h, z, :, pl.ds(size, size)
            ]

        total = dg_part[0]
        for r in (1, 2, 3):
            wire_1.arrived(dg_land.at[r - 1], dg_slot + r - 1, ids[r])
            total = total + dg_land[r - 1]
        gates = gate_ref[0]
        d_logits = gates * (total - jnp.sum(gates * total, 0, keepdims=True))
        d_logits = jnp.concatenate(
            [d_logits, jnp.zeros((SMALL - d_logits.shape[0], tokens), F32)], 0
        )
        d_all_ref[:, pl.ds(qkv_width, SMALL)] = jnp.transpose(d_logits).astype(BF16)

        for copy in load_q:
            copy.wait()

        @pl.loop(0, planes)
        def _(block):
            columns = pl.ds(pl.multiple_of(block * part, part), part)
            d_inputs_ref[:, columns] = dot_nt(d_all_ref[...], weight[columns, :])

        rows = x_ref[...].astype(F32)
        scale1 = lax.rsqrt(jnp.mean(rows * rows, -1, keepdims=True) + EPSILON)
        d_inputs = d_inputs_ref[...]
        rows_ref[experts : experts + 1, :] = jnp.sum(d_inputs * rows * scale1, 0, keepdims=True)

        def extra(columns):
            small = jnp.transpose(rows_ref[:, columns])
            return jnp.concatenate([jnp.zeros((part, rest - SMALL), F32), small], 1)

        row_grads(
            grads_q, inputs_ref, d_all_ref[:, pl.ds(query_width, rest)], query_width, rest, extra
        )
        scatter_k.share()
        pltpu.make_async_remote_copy(
            src_ref=core_hbm.at[z],
            dst_ref=core_hbm.at[z],
            send_sem=hand_sends.at[0],
            recv_sem=hand_recvs.at[0],
            device_id=sibling,
            device_id_type=MESH,
        ).wait_recv()
        expert.cores(0)
        expert.relay()
        expert.send(2, 0, when=expert.inner)
        expert.send(2, 1, when=expert.inner)
        expert.send(1, 1)
        scatter_q.relay()
        scatter_k.merge()
        scaled = d_inputs_ref[...] * gains_ref[0:1]
        rows = x_ref[...].astype(F32)
        scale1 = lax.rsqrt(jnp.mean(rows * rows, -1, keepdims=True) + EPSILON)
        mean = jnp.mean(scaled * rows, -1, keepdims=True)
        d_x = d_hidden_ref[...] + scale1 * scaled - rows * (scale1 * scale1 * scale1 * mean)
        d_x_ref[...] = d_x.astype(BF16)
        scatter_q.total()
        scatter_k.relay()
        scatter_o.line.step(1)
        scatter_q.line.step(1)
        scatter_k.total()
        scatter_k.line.step(1)
        for s in range(2, nc):
            for scatter in (scatter_o, scatter_q, scatter_k):
                scatter.line.step(s)
        for scatter in (scatter_o, scatter_q, scatter_k):
            scatter.line.last()
        sum_o_ref[...] = scatter_o.line.block(z)[...].astype(F32)
        sum_q_ref[...] = grads_q[c, e, pl.ds(pl.multiple_of(z * (rows_of // nc), rows_of // nc), rows_of // nc)].astype(F32)
        expert.last(sum_e_hbm)
        wire_2.finish()
        expert.finish()

    held = EXP_DEV
    pl.run_scoped(
        token_phase,
        pltpu.VMEM((held, width, 2 * ff), BF16),
        pltpu.VMEM((held, ff, width), BF16),
        pltpu.VMEM((blocks, tokens, width), BF16),
        pltpu.VMEM((blocks, tokens, held * ff), BF16),
        pltpu.VMEM((blocks, tokens, held * 2 * ff), BF16),
        pltpu.VMEM((blocks - 1, tokens, width), BF16),
        pltpu.VMEM((blocks - 1, tokens, width), BF16),
        pltpu.VMEM((2, 2, width // nc // 2, grad_width), BF16),
    )
    rows_half = width // blocks // 2
    pl.run_scoped(
        token_rows_phase,
        pltpu.VMEM((width, qkv_width + SMALL), BF16),
        pltpu.VMEM((2, blocks, rows_half, width), BF16),
        pltpu.VMEM((2, blocks, rows_half, qkv_width + SMALL), BF16),
        pltpu.VMEM((tokens, width), BF16),
        pltpu.VMEM((tokens, width), BF16),
        pltpu.VMEM((tokens, query_width), BF16),
        pltpu.VMEM((nc, tokens, 2 * key_width), BF16),
        pltpu.VMEM((tokens, query_width), BF16),
        pltpu.VMEM((tokens, width), F32),
        pltpu.VMEM((tokens, width), BF16),
        pltpu.VMEM((tokens, width), F32),
        pltpu.VMEM((tokens, width), BF16),
        pltpu.VMEM((tokens, query_width), BF16),
        pltpu.VMEM((tokens, qkv_width + SMALL), BF16),
        pltpu.VMEM((tokens, width), F32),
        pltpu.VMEM((SMALL, width), F32),
        pltpu.VMEM((KEY_VALUE_HEADS, nc * tokens, 2 * size), F32),
        pltpu.VMEM((KEY_VALUE_HEADS, nc, tokens, 2 * size), BF16),
    )


def back(operands, sizes):
    ne, nc, nd = sizes
    cot, w_gu, w_dn, x = operands[6], operands[7], operands[8], operands[9]
    tokens, width = x.shape
    held, ff = w_dn.shape[0], w_dn.shape[1]
    rest = operands[15].shape[-1]
    q_width = QUERY_HEADS * HEAD_DIMENSION + rest
    rows = width // (ne * nc * nd)
    rest_half = rest // 256 * 128
    shard, grads = width // (nc * nd), held * 3 * ff
    kv_size = 2 * HEAD_DIMENSION
    shapes = [
        ((tokens, width), BF16),
        ((tokens, width), BF16),
        ((rows, q_width), F32),
        ((rows, width), F32),
        ((shard, grads), F32),
        ((nc, shard, grads), BF16),
        ((nc, shard, grads), BF16),
        ((nc + 1, shard, grads), BF16),
    ]
    vmem = pl.BlockSpec(memory_space=pltpu.VMEM)
    anywhere = pl.BlockSpec(memory_space=pl.ANY)
    step = 16
    return pl.pallas_call(
        functools.partial(back_kernel, nc, EXP_DEV * ne),
        out_shape=[jax.ShapeDtypeStruct(*s) for s in shapes],
        in_specs=[vmem] * 5 + [anywhere] * (len(operands) - 5),
        out_specs=[vmem] * 4 + [anywhere] * 4,
        scratch_shapes=[
            pltpu.VMEM((ne, tokens, width), BF16),
            pltpu.VMEM((6, tokens, width // 2), BF16),
            pltpu.VMEM((6, tokens, width // 2), BF16),
            pltpu.VMEM((ne, nc * rows, q_width), BF16),
            pltpu.VMEM((6, nc * rows, QUERY_HEADS * HEAD_DIMENSION // 2), BF16),
            pltpu.VMEM((6, nc * rows, rest - rest_half), BF16),
            pltpu.VMEM((2, nc - 1, rows, width), BF16),
            pltpu.VMEM((2, nc - 1, rows, QUERY_HEADS * HEAD_DIMENSION), BF16),
            pltpu.VMEM((2, nc - 1, rows, rest), BF16),
            pltpu.VMEM((KEY_VALUE_HEADS, nc - 1, tokens, kv_size), BF16),
            pltpu.VMEM((tokens, width), F32),
            pltpu.VMEM((tokens, width), F32),
            pltpu.VMEM((tokens, SMALL), F32),
            pltpu.VMEM((ne, GATE_ROWS, tokens), F32),
            pltpu.VMEM((ne - 1, GATE_ROWS, tokens), F32),
            pltpu.VMEM((4, 2, step, grads), BF16),
            pltpu.VMEM((2, step, grads), BF16),
            pltpu.VMEM((2, step, grads), F32),
            pltpu.SemaphoreType.DMA((32,)),
            pltpu.SemaphoreType.DMA((32,)),
            pltpu.SemaphoreType.DMA((64,)),
            pltpu.SemaphoreType.DMA((64,)),
            pltpu.SemaphoreType.DMA((8,)),
            pltpu.SemaphoreType.DMA((2 * nc + 2,)),
            pltpu.SemaphoreType.DMA((nc,)),
            pltpu.SemaphoreType.DMA((nc,)),
            pltpu.SemaphoreType.DMA((2,)),
            pltpu.SemaphoreType.DMA((12,)),
            pltpu.SemaphoreType.DMA((10,)),
            pltpu.SemaphoreType.REGULAR((3,)),
        ],
        compiler_params=pltpu.CompilerParams(
            collective_id=1, has_side_effects=True, vmem_limit_bytes=63 * MIB
        ),
    )(*operands)


def local_plain(
    layer_input,
    gain_attn,
    query_key_value_weight,
    w_out,
    w_router,
    gain_ffn,
    w_gate_up,
    w_down,
    routes,
    d_out,
):
    tokens = layer_input.shape[1]
    model_width = layer_input.shape[2]
    ne, nc, nd = (lax.axis_size(a) for a in ("expert", "context", "dp"))
    expert_total = EXP_DEV * ne
    ff = w_down.shape[1]
    me = lax.axis_index("expert")
    first_row = lax.axis_index("context") * tokens
    query_width = QUERY_HEADS * HEAD_DIMENSION
    key_width = KEY_VALUE_HEADS * HEAD_DIMENSION
    qkv_width = query_width + 2 * key_width

    small = jnp.concatenate([w_router, gain_attn[:, None], gain_ffn[:, None]], -1)
    small = jnp.pad(small, ((0, 0), (0, 128 - small.shape[1])))
    gathered = gather_rows(jnp.concatenate([query_key_value_weight, small], -1))
    out_turned = gather_rows(w_out.T)
    qkv_weight = gathered[:, :qkv_width]
    router_weight = gathered[:, qkv_width : qkv_width + expert_total]
    gains = gathered[:, qkv_width + expert_total : qkv_width + expert_total + 2].T.astype(F32)
    gain_first, gain_second = gains[0], gains[1]
    cotangent_all = plane_gather(d_out[0])

    token_rows = layer_input[0].astype(F32)
    scale1 = lax.rsqrt(jnp.mean(token_rows * token_rows, -1, keepdims=True) + EPSILON)
    inputs1 = (token_rows * scale1 * gain_first).astype(BF16)
    query_key_value = dot_nn(inputs1, qkv_weight)
    cosine_values, sine_values = rope_tables(first_row + jnp.arange(tokens), HEAD_DIMENSION)
    rotated = rotate_half(
        query_key_value[:, : query_width + key_width].reshape(tokens, -1, HEAD_DIMENSION),
        cosine_values,
        sine_values,
    ).reshape(tokens, -1)
    query = rotated[:, :query_width].astype(BF16)
    key_value_local = jnp.concatenate(
        [rotated[:, query_width:], query_key_value[:, query_width + key_width :]], -1
    ).astype(BF16)
    key_value = line_gather(key_value_local, "context", both=False).reshape(nc * tokens, -1)
    first = first_row.astype(jnp.int32).reshape(1)
    heads = attend_forward(first, query, key_value)

    logits = dot_nn(inputs1, router_weight)
    chosen_ids = routes[0]
    picks = (chosen_ids[:, :, None] == jnp.arange(expert_total)[None, None, :]).astype(F32)
    chosen = jnp.sum(picks * logits[:, None, :], -1)
    gates = jax.nn.softmax(chosen, axis=-1)
    gate_dense = jnp.sum(picks * gates[:, :, None], 1).T
    gate_blocks = cube_gather(gate_dense, "expert", axis_masks("expert"))
    gate_local = jnp.concatenate(
        [lax.dynamic_slice_in_dim(b, me * EXP_DEV, EXP_DEV, 0) for b in gate_blocks], 1
    )

    attn = dot_nt(heads, out_turned)
    hidden = token_rows + attn
    scale2 = lax.rsqrt(jnp.mean(hidden * hidden, -1, keepdims=True) + EPSILON)
    expert_in = (hidden * scale2 * gain_second).astype(BF16)

    rows_all = plane_gather(expert_in)
    gate_up = jnp.einsum("td,edf->etf", rows_all, w_gate_up, preferred_element_type=F32)
    gate_part, up_part = gate_up[..., :ff], gate_up[..., ff:]
    sigma = jax.nn.sigmoid(gate_part)
    silu = gate_part * sigma
    act = silu * up_part
    gate_column = gate_local[:, :, None]
    act_gated = (act * gate_column).astype(BF16)
    partial_out = jnp.einsum("etf,efd->td", act_gated, w_down, preferred_element_type=F32)
    mixture = plane_scatter(partial_out.astype(BF16), tokens)
    layer_result = (hidden + mixture).astype(BF16)

    d_act_raw = jnp.einsum("td,efd->etf", cotangent_all, w_down, preferred_element_type=F32)
    d_gates_local = jnp.sum(d_act_raw * act, -1)
    d_act = d_act_raw * gate_column
    d_gate_part = d_act * up_part * sigma * (1.0 + gate_part * (1.0 - sigma))
    d_up_part = d_act * silu
    d_gate_up = jnp.concatenate([d_gate_part, d_up_part], -1).astype(BF16)
    d_rows = jnp.einsum("etf,edf->td", d_gate_up, w_gate_up, preferred_element_type=F32)
    grad_down = jnp.einsum("td,etf->edf", cotangent_all, act_gated, preferred_element_type=F32)
    grad_gate_up = jnp.einsum("td,etf->edf", rows_all, d_gate_up, preferred_element_type=F32)

    d_expert_in = plane_scatter(d_rows.astype(BF16), tokens)
    d_gate_blocks = d_gates_local.reshape(EXP_DEV, ne, tokens)
    d_gates_dense = jnp.zeros((expert_total, tokens), F32)
    for r in range(ne):
        arrived = d_gate_blocks[:, r]
        if r:
            arrived = exchange(arrived, "expert", r)
        d_gates_dense = lax.dynamic_update_slice(d_gates_dense, arrived, ((me ^ r) * EXP_DEV, 0))
    d_gates = jnp.sum(picks * d_gates_dense.T[:, None, :], -1)
    d_chosen = gates * (d_gates - jnp.sum(gates * d_gates, -1, keepdims=True))
    d_logits = jnp.sum(picks * d_chosen[:, :, None], 1).astype(BF16)
    grad_router = dot_tn(inputs1, d_logits)

    core = lax.axis_index("dp")
    part = model_width // (nc * nd)

    def scatter_experts(grad):
        blocks = grad.reshape(EXP_DEV, nc, nd, part, -1)
        mine = cube_scatter(
            [lax.dynamic_index_in_dim(blocks, core ^ r, 2, keepdims=False) for r in range(nd)],
            "dp",
            axis_masks("dp"),
        )
        return line_scatter(
            lambda j: lax.dynamic_index_in_dim(mine, j, 1, keepdims=False), "context"
        )

    sum_gate_up = scatter_experts(grad_gate_up)
    sum_down = jnp.swapaxes(scatter_experts(grad_down), 1, 2)

    cotangent = d_out[0].astype(F32)
    scaled2 = d_expert_in * gain_second
    d_hidden = (
        cotangent
        + scale2 * scaled2
        - hidden * (scale2 * scale2 * scale2) * jnp.mean(scaled2 * hidden, -1, keepdims=True)
    )
    grad_gain_second = jnp.sum(d_expert_in * hidden * scale2, 0)
    d_attn = d_hidden.astype(BF16)
    grad_out_turned = dot_tn(d_attn, heads)
    sum_out = scatter_rows(grad_out_turned).T
    d_heads = dot_nn(d_attn, out_turned).astype(BF16)
    d_query, d_key_all, d_value_all = attend_backward(first, query, key_value, d_heads)
    d_key_value_all = jnp.concatenate([d_key_all, d_value_all], -1).reshape(nc, tokens, -1)
    d_key_value = line_scatter(
        lambda j: lax.dynamic_index_in_dim(d_key_value_all, j, 0, keepdims=False),
        "context",
        up=False,
    )
    d_rotated = rotate_back(
        jnp.concatenate([d_query, d_key_value[:, :key_width]], -1).reshape(
            tokens, -1, HEAD_DIMENSION
        ),
        cosine_values,
        sine_values,
    ).reshape(tokens, -1)
    d_qkv = jnp.concatenate([d_rotated, d_key_value[:, key_width:]], -1).astype(BF16)
    d_inputs = dot_nt(d_qkv, qkv_weight) + dot_nt(d_logits, router_weight)
    grad_gain_first = jnp.sum(d_inputs * token_rows * scale1, 0)
    grad_qkv = dot_tn(inputs1, d_qkv)
    small_grads = jnp.concatenate(
        [grad_router, grad_gain_first[:, None], grad_gain_second[:, None]], -1
    )
    small_grads = jnp.pad(small_grads, ((0, 0), (0, 128 - small_grads.shape[1])))
    sum_rows = scatter_rows(jnp.concatenate([grad_qkv, small_grads], -1))
    sum_qkv = sum_rows[:, :qkv_width]
    sum_router = sum_rows[:, qkv_width : qkv_width + expert_total]
    sum_gain_first = sum_rows[:, qkv_width + expert_total]
    sum_gain_second = sum_rows[:, qkv_width + expert_total + 1]
    scaled1 = d_inputs * gain_first
    d_input_rows = (
        d_hidden
        + scale1 * scaled1
        - token_rows
        * (scale1 * scale1 * scale1)
        * jnp.mean(scaled1 * token_rows, -1, keepdims=True)
    ).astype(BF16)
    return (
        layer_result[None],
        d_input_rows[None],
        sum_gain_first,
        sum_qkv,
        sum_out,
        sum_router,
        sum_gain_second,
        sum_gate_up,
        sum_down,
    )


def local_fused(
    layer_input,
    gain_attn,
    query_key_value_weight,
    w_out,
    w_router,
    gain_ffn,
    w_gate_up,
    w_down,
    routes,
    d_out,
):
    tokens = layer_input.shape[1]
    ne, nc, nd = sizes = tuple(lax.axis_size(a) for a in ("expert", "context", "dp"))
    expert_total = EXP_DEV * ne
    ff = w_down.shape[1]
    first_row = lax.axis_index("context") * tokens
    query_width = QUERY_HEADS * HEAD_DIMENSION
    key_width = KEY_VALUE_HEADS * HEAD_DIMENSION
    qkv_width = query_width + 2 * key_width

    small = jnp.concatenate([w_router, gain_attn[:, None], gain_ffn[:, None]], -1)
    small = jnp.pad(small, ((0, 0), (0, SMALL - small.shape[1])))
    cosine_values, sine_values = rope_tables(first_row + jnp.arange(tokens), HEAD_DIMENSION)
    sine_values = sine_values * jnp.where(
        jnp.arange(HEAD_DIMENSION) < HEAD_DIMENSION // 2, -1.0, 1.0
    )
    (
        wk_all,
        wq_all,
        wo_all,
        cotangent_all,
        gate_all,
        gate_columns,
        inputs1,
        query,
        key_value,
        heads,
        hidden,
        expert_in,
        gains,
    ) = front(
        (
            layer_input[0],
            query_key_value_weight,
            small,
            w_out.T,
            d_out[0],
            cosine_values,
            sine_values,
            routes[0],
        ),
        sizes,
    )
    layer_result, d_x, sum_rows, sum_out, sum_experts = back(
        (
            gate_columns,
            gate_all,
            gains,
            cosine_values,
            sine_values,
            expert_in,
            cotangent_all,
            w_gate_up,
            w_down,
            layer_input[0],
            inputs1,
            query,
            key_value,
            heads,
            hidden,
            wk_all.reshape(-1, wk_all.shape[-1]),
            wq_all.reshape(-1, query_width),
            wo_all.reshape(-1, wo_all.shape[-1]),
        ),
        sizes,
    )[:5]
    sum_gate_up = jnp.stack([sum_experts[:, i * 2 * ff : (i + 1) * 2 * ff] for i in range(EXP_DEV)])
    sum_down = sum_experts[:, EXP_DEV * 2 * ff :].reshape(-1, EXP_DEV, ff)
    return (
        layer_result[None],
        d_x[None],
        sum_rows[:, qkv_width + expert_total],
        sum_rows[:, :qkv_width],
        sum_out.T,
        sum_rows[:, qkv_width : qkv_width + expert_total],
        sum_rows[:, qkv_width + expert_total + 1],
        sum_gate_up,
        jnp.transpose(sum_down, (1, 2, 0)),
    )


def solution(mesh):
    in_specs = (
        P(("expert", "dp"), "context", None),
        P(("expert", "context", "dp")),
        P(("expert", "context", "dp"), None),
        P(None, ("expert", "context", "dp")),
        P(("expert", "context", "dp"), None),
        P(("expert", "context", "dp")),
        P("expert", None, None),
        P("expert", None, None),
        P(("expert", "dp"), "context", None),
        P(("expert", "dp"), "context", None),
    )
    out_specs = (
        P(("expert", "dp"), "context", None),
        P(("expert", "dp"), "context", None),
        P(("expert", "context", "dp")),
        P(("expert", "context", "dp"), None),
        P(None, ("expert", "context", "dp")),
        P(("expert", "context", "dp"), None),
        P(("expert", "context", "dp")),
        P("expert", ("context", "dp"), None),
        P("expert", None, ("context", "dp")),
    )
    sizes = tuple(mesh.shape[a] for a in ("expert", "context", "dp"))
    local = local_fused if sizes == (4, 4, 2) else local_plain
    return jax.shard_map(local, mesh=mesh, in_specs=in_specs, out_specs=out_specs, check_vma=False)
```

```python
import functools
import math

import jax
import jax.numpy as jnp
from jax import lax
from jax.experimental import pallas as pl
from jax.experimental.pallas import tpu as pltpu
from jax.sharding import PartitionSpec as P

QUERY_HEADS = 12
KEY_VALUE_HEADS = 2
HEAD_DIMENSION = 128
TOP = 4
EXP_DEV = 2

EPSILON = 1e-06
ROPE_BASE = 10000.0
MASKED = -1e30

F32 = jnp.float32
BF16 = jnp.bfloat16


def rope_tables(positions, width):
    halfway = width // 2
    fraction = jnp.arange(halfway, dtype=jnp.float32) * (2.0 / width)
    frequency = jnp.exp(-math.log(ROPE_BASE) * fraction)
    angles = positions.astype(jnp.float32)[:, None] * frequency[None, :]
    cosine_values = jnp.cos(angles)
    sine_values = jnp.sin(angles)
    return (
        jnp.concatenate([cosine_values, cosine_values], -1),
        jnp.concatenate([sine_values, sine_values], -1),
    )


def rotate_half(values, cosine_values, sine_values):
    halfway = values.shape[-1] // 2
    turned = jnp.concatenate([-values[..., halfway:], values[..., :halfway]], -1)
    return values * cosine_values[:, None, :] + turned * sine_values[:, None, :]


def rotate_back(grads, cosine_values, sine_values):
    halfway = grads.shape[-1] // 2
    scaled = grads * sine_values[:, None, :]
    turned = jnp.concatenate([scaled[..., halfway:], -scaled[..., :halfway]], -1)
    return grads * cosine_values[:, None, :] + turned


def dot_nt(a, b):
    return lax.dot_general(a, b, (((1,), (1,)), ((), ())), preferred_element_type=F32)


def dot_tn(a, b):
    return lax.dot_general(a, b, (((0,), (0,)), ((), ())), preferred_element_type=F32)


def dot_nn(a, b):
    return jnp.dot(a, b, preferred_element_type=F32)


def masked_probs(first_row, query, key):
    scores = dot_nt(query, key) * (HEAD_DIMENSION**-0.5)
    rows = first_row + lax.broadcasted_iota(jnp.int32, scores.shape, 0)
    columns = lax.broadcasted_iota(jnp.int32, scores.shape, 1)
    scores = jnp.where(columns <= rows, scores, MASKED)
    expd = jnp.exp(scores - jnp.max(scores, axis=-1, keepdims=True))
    return expd / jnp.sum(expd, axis=-1, keepdims=True)


def attend_forward_kernel(first_ref, query_ref, key_ref, value_ref, heads_ref):
    probs = masked_probs(first_ref[0], query_ref[...], key_ref[...])
    heads_ref[...] = dot_nn(probs.astype(BF16), value_ref[...]).astype(BF16)


def attend_forward(first_row, query, key_value):
    tokens, width = query.shape
    length = key_value.shape[0]
    group = QUERY_HEADS // KEY_VALUE_HEADS
    size = HEAD_DIMENSION
    return pl.pallas_call(
        attend_forward_kernel,
        grid_spec=pltpu.PrefetchScalarGridSpec(
            num_scalar_prefetch=1,
            grid=(QUERY_HEADS,),
            in_specs=[
                pl.BlockSpec((tokens, size), lambda h, s: (0, h)),
                pl.BlockSpec((length, size), lambda h, s: (0, h // group)),
                pl.BlockSpec((length, size), lambda h, s: (0, KEY_VALUE_HEADS + h // group)),
            ],
            out_specs=pl.BlockSpec((tokens, size), lambda h, s: (0, h)),
        ),
        out_shape=jax.ShapeDtypeStruct((tokens, width), BF16),
        compiler_params=pltpu.CompilerParams(vmem_limit_bytes=32 * 1024 * 1024),
        cost_estimate=pl.CostEstimate(
            flops=4 * tokens * length * width, bytes_accessed=4 * tokens * width, transcendentals=0
        ),
    )(first_row, query, key_value, key_value)


def attend_backward_kernel(
    first_ref, query_ref, key_ref, value_ref, grad_ref, d_query_ref, d_key_ref, d_value_ref
):
    query, key, value, grad = query_ref[...], key_ref[...], value_ref[...], grad_ref[...]
    probs = masked_probs(first_ref[0], query, key)
    d_probs = dot_nt(grad, value)
    inner = jnp.sum(probs * d_probs, axis=-1, keepdims=True)
    d_raw = (probs * (d_probs - inner) * (HEAD_DIMENSION**-0.5)).astype(BF16)
    d_query_ref[...] = dot_nn(d_raw, key)
    d_key = dot_tn(d_raw, query)
    d_value = dot_tn(probs.astype(BF16), grad)

    @pl.when(pl.program_id(1) == 0)
    def _():
        d_key_ref[...] = d_key
        d_value_ref[...] = d_value

    @pl.when(pl.program_id(1) > 0)
    def _():
        d_key_ref[...] += d_key
        d_value_ref[...] += d_value


def attend_backward(first_row, query, key_value, grad):
    tokens, width = query.shape
    length = key_value.shape[0]
    group = QUERY_HEADS // KEY_VALUE_HEADS
    size = HEAD_DIMENSION
    row_spec = pl.BlockSpec((tokens, size), lambda j, g, s: (0, j * group + g))
    return pl.pallas_call(
        attend_backward_kernel,
        grid_spec=pltpu.PrefetchScalarGridSpec(
            num_scalar_prefetch=1,
            grid=(KEY_VALUE_HEADS, group),
            in_specs=[
                row_spec,
                pl.BlockSpec((length, size), lambda j, g, s: (0, j)),
                pl.BlockSpec((length, size), lambda j, g, s: (0, KEY_VALUE_HEADS + j)),
                row_spec,
            ],
            out_specs=[
                row_spec,
                pl.BlockSpec((length, size), lambda j, g, s: (0, j)),
                pl.BlockSpec((length, size), lambda j, g, s: (0, j)),
            ],
        ),
        out_shape=[
            jax.ShapeDtypeStruct((tokens, width), F32),
            jax.ShapeDtypeStruct((length, KEY_VALUE_HEADS * size), F32),
            jax.ShapeDtypeStruct((length, KEY_VALUE_HEADS * size), F32),
        ],
        compiler_params=pltpu.CompilerParams(vmem_limit_bytes=32 * 1024 * 1024),
        cost_estimate=pl.CostEstimate(
            flops=10 * tokens * length * width, bytes_accessed=8 * tokens * width, transcendentals=0
        ),
    )(first_row, query, key_value, key_value, grad)


def exchange(values, axis, mask):
    size = lax.axis_size(axis)
    return lax.ppermute(values, axis, [(i, i ^ mask) for i in range(size)])


def axis_masks(axis):
    size = lax.axis_size(axis)
    masks, bit = [], 1
    while bit < size:
        masks.append(bit)
        bit *= 2
    return masks


def cube_gather(values, axis, masks):
    held = {0: values}
    for mask in masks:
        for r, block in list(held.items()):
            held[r ^ mask] = exchange(block, axis, mask)
    return [held[r] for r in range(lax.axis_size(axis))]


def cube_scatter(blocks, axis, masks):
    held = dict(enumerate(blocks))
    for mask in masks:
        kept = {}
        for r in list(held):
            if not r & mask:
                arrived = exchange(held[r ^ mask].astype(BF16), axis, mask)
                kept[r] = held[r].astype(F32) + arrived.astype(F32)
        held = kept
    return held[0]


def line_steps(values, axis, up):
    size = lax.axis_size(axis)
    pairs = [(i, i + 1) if up else (i + 1, i) for i in range(size - 1)]
    return lax.ppermute(values, axis, pairs)


def line_gather(values, axis, both=True):
    size = lax.axis_size(axis)
    me = lax.axis_index(axis)
    result = jnp.zeros((size + 1,) + values.shape, values.dtype)
    result = lax.dynamic_update_index_in_dim(result, values, me, 0)
    up = down = values
    for step in range(1, size):
        up = line_steps(up, axis, True)
        result = lax.dynamic_update_index_in_dim(
            result, up, jnp.where(me - step >= 0, me - step, size), 0
        )
        if both:
            down = line_steps(down, axis, False)
            result = lax.dynamic_update_index_in_dim(result, down, jnp.minimum(me + step, size), 0)
    return result[:size]


def line_scatter(take, axis, up=True, down=True):
    size = lax.axis_size(axis)
    me = lax.axis_index(axis)
    total = take(me).astype(F32)
    for active, sign in ((up, 1), (down, -1)):
        if not active:
            continue
        arrived = None
        for step in range(1, size):
            block = take((me + sign * (size - step)) % size).astype(F32)
            if arrived is not None:
                block = block + arrived.astype(F32)
            arrived = line_steps(block.astype(BF16), axis, sign > 0)
        total = total + arrived.astype(F32)
    return total


def gather_rows(shard):
    ne, nc, nd = (lax.axis_size(a) for a in ("expert", "context", "dp"))
    rows, width = shard.shape
    lines = line_gather(shard, "context")
    masks = axis_masks("expert")
    half = width // 256 * 128
    parts = [lines[..., :half], lines[..., half:]]
    me = lax.axis_index("expert")
    result = jnp.zeros((ne, nc, rows, width), shard.dtype)
    for start, part, order in ((0, parts[0], masks), (half, parts[1], masks[::-1])):
        for r, block in enumerate(cube_gather(part, "expert", order)):
            result = lax.dynamic_update_slice(result, block[None], (me ^ r, 0, 0, start))
    core = lax.axis_index("dp")
    whole = jnp.zeros((ne, nc, nd, rows, width), shard.dtype)
    for r, block in enumerate(cube_gather(result, "dp", axis_masks("dp"))):
        whole = lax.dynamic_update_slice(whole, block[:, :, None], (0, 0, core ^ r, 0, 0))
    return whole.reshape(-1, width)


def scatter_rows(grad):
    ne, nc, nd = (lax.axis_size(a) for a in ("expert", "context", "dp"))
    width = grad.shape[-1]
    rows = grad.shape[0] // (ne * nc * nd)
    blocks = grad.reshape(ne, nc, nd, rows, width)
    core, me = lax.axis_index("dp"), lax.axis_index("expert")
    mine = cube_scatter(
        [
            lax.dynamic_index_in_dim(blocks, core ^ r, 2, keepdims=False)
            for r in range(nd)
        ],
        "dp",
        axis_masks("dp"),
    )
    masks = axis_masks("expert")
    half = width // 256 * 128
    sums = []
    for part, order in ((mine[..., :half], masks), (mine[..., half:], masks[::-1])):
        sums.append(
            cube_scatter(
                [lax.dynamic_index_in_dim(part, me ^ r, 0, keepdims=False) for r in range(ne)],
                "expert",
                order,
            )
        )
    lines = jnp.concatenate(sums, -1)
    return line_scatter(
        lambda j: lax.dynamic_index_in_dim(lines, j, 0, keepdims=False), "context"
    )


def plane_gather(rows):
    masks = axis_masks("expert")
    half = rows.shape[-1] // 2
    left = cube_gather(rows[:, :half], "expert", masks)
    right = cube_gather(rows[:, half:], "expert", masks[::-1])
    return jnp.concatenate([jnp.concatenate(p, -1) for p in zip(left, right)], 0)


def plane_scatter(partial, tokens):
    masks = axis_masks("expert")
    size = lax.axis_size("expert")
    half = partial.shape[-1] // 2
    blocks = partial.reshape(size, tokens, -1)
    left = cube_scatter([blocks[r, :, :half] for r in range(size)], "expert", masks)
    right = cube_scatter([blocks[r, :, half:] for r in range(size)], "expert", masks[::-1])
    return jnp.concatenate([left, right], -1)


MESH = pl.DeviceIdType.MESH
MIB = 1024 * 1024
SMALL = 128
GATE_ROWS = 16


def flip(index, mask):
    bit = 1
    while bit <= mask:
        if mask & bit:
            index = index + bit - 2 * bit * lax.rem(lax.div(index, bit), 2)
        bit *= 2
    return index


class Wire:
    def __init__(self, sends, recvs):
        self.sends, self.recvs = sends, recvs
        self.n_sends = self.n_recvs = 0
        self.open = []

    def slots(self, count):
        first = self.n_recvs
        self.n_recvs += count
        return first

    def start(self, src, dst, recv, device, when=None):
        copy = pltpu.make_async_remote_copy(
            src_ref=src,
            dst_ref=dst,
            send_sem=self.sends.at[self.n_sends],
            recv_sem=self.recvs.at[recv],
            device_id=device,
            device_id_type=MESH,
        )
        self.n_sends += 1
        guard(when, copy.start)
        self.open.append((when, copy))

    def arrived(self, dst, recv, device):
        pltpu.make_async_remote_copy(
            src_ref=dst,
            dst_ref=dst,
            send_sem=self.sends.at[0],
            recv_sem=self.recvs.at[recv],
            device_id=device,
            device_id_type=MESH,
        ).wait_recv()

    def finish(self):
        for when, copy in self.open:
            guard(when, copy.wait_send)
        self.open = []


def guard(when, action):
    if when is None:
        action()
    else:
        pl.when(when)(action)


def greet(targets):
    barrier = pltpu.get_barrier_semaphore()
    for device, when in targets:
        guard(
            when,
            lambda device=device: pl.semaphore_signal(
                barrier, inc=1, device_id=device, device_id_type=MESH
            ),
        )
    count = sum(1 if when is None else when.astype(jnp.int32) for _, when in targets)
    pl.semaphore_wait(barrier, count)


def plane_ids(e):
    return {m: {"expert": flip(e, m)} for m in (1, 2, 3)}


class RowsGather:
    def __init__(self, wire, ref, e, z, c, nc, half):
        self.wire, self.ref, self.e, self.z, self.c, self.nc = wire, ref, e, z, c, nc
        self.cols = (pl.ds(0, half), pl.ds(half, ref.shape[-1] - half))
        self.line = wire.slots(nc)
        self.plane = wire.slots(nc * 6)
        self.core = wire.slots(nc)
        self.ids = plane_ids(e)

    def go(self, *steps):
        for step in steps:
            action = {"s": self.spread, "f": self.forward, "h": self.share, "c": self.complete}
            action[step[0]](*map(int, step[1:]))

    def at(self, r, zs, half):
        return self.ref.at[flip(self.e, r), zs, self.c, :, self.cols[half]]

    def slot(self, k, r, half):
        return self.plane + k * 6 + (r - 1) * 2 + half

    def spread(self, k):
        wire, z, nc = self.wire, self.z, self.nc
        zs = flip(z, k)
        whole = self.ref.at[self.e, zs, self.c]
        if k:
            wire.arrived(whole, self.line + zs, {"context": zs})
        wire.start(
            whole, whole, self.line + zs, {"context": z + 1}, when=(zs <= z) & (z < nc - 1)
        )
        wire.start(whole, whole, self.line + zs, {"context": z - 1}, when=(zs >= z) & (z > 0))
        for half, mask in ((0, 1), (1, 2), (1, 1), (0, 2)):
            part = self.at(0, zs, half)
            wire.start(part, part, self.slot(k, mask, half), self.ids[mask])

    def forward(self, k):
        zs = flip(self.z, k)
        for half, mask in ((0, 1), (1, 2)):
            part = self.at(mask, zs, half)
            self.wire.arrived(part, self.slot(k, mask, half), self.ids[mask])
            self.wire.start(part, part, self.slot(k, 3, half), self.ids[3 - mask])

    def share(self, k):
        zs = flip(self.z, k)
        for r, half in ((1, 1), (2, 0), (3, 0), (3, 1)):
            self.wire.arrived(self.at(r, zs, half), self.slot(k, r, half), self.ids[r])
        part = self.ref.at[:, zs, self.c]
        self.wire.start(part, part, self.core + k, {"dp": 1 - self.c})

    def complete(self):
        for k in range(self.nc):
            zs = flip(self.z, k)
            self.wire.arrived(self.ref.at[:, zs, 1 - self.c], self.core + k, {"dp": 1 - self.c})


class PlaneGather:
    def __init__(self, wire, ref, e):
        self.wire, self.ref = wire, ref
        self.half = ref.shape[-1] // 2
        self.ids = plane_ids(e)
        self.first = wire.slots(6)

    def at(self, r, half):
        return self.ref.at[r, :, pl.ds(half * self.half, self.half)]

    def slot(self, r, half):
        return self.first + (r - 1) * 2 + half

    def spread(self):
        for half, mask in ((0, 1), (1, 2), (1, 1), (0, 2)):
            self.wire.start(
                self.at(0, half), self.at(mask, half), self.slot(mask, half), self.ids[mask]
            )

    def forward(self):
        for half, mask in ((0, 1), (1, 2)):
            self.wire.arrived(self.at(mask, half), self.slot(mask, half), self.ids[mask])
            self.wire.start(
                self.at(mask, half), self.at(3, half), self.slot(3, half), self.ids[3 - mask]
            )

    def near(self, r):
        half = 1 if r == 1 else 0
        self.wire.arrived(self.at(r, half), self.slot(r, half), self.ids[r])

    def far(self):
        for half in (0, 1):
            self.wire.arrived(self.at(3, half), self.slot(3, half), self.ids[3])

    def complete(self):
        self.near(1)
        self.near(2)
        self.far()


def swap_halves(values):
    return pltpu.roll(values, HEAD_DIMENSION // 2, 1)


def front_kernel(
    nc,
    experts,
    x_ref,
    qkv_shard,
    small_shard,
    wo_shard,
    cot_ref,
    cos_ref,
    sin_ref,
    routes_ref,
    wk_hbm,
    wq_hbm,
    wo_hbm,
    cot_hbm,
    gate_all,
    gate_columns,
    inputs_ref,
    query_ref,
    kv_ref,
    heads_ref,
    hidden_ref,
    expert_in_ref,
    gains_ref,
    wk_all,
    wq_all,
    wo_all,
    cot_all,
    kv_scr,
    q_scr,
    sends,
    recvs,
    out_sems,
):
    e, z, c = (lax.axis_index(a) for a in ("expert", "context", "dp"))
    size = HEAD_DIMENSION
    tokens, width = x_ref.shape
    query_width = QUERY_HEADS * size
    kv_width = 2 * KEY_VALUE_HEADS * size
    wire = Wire(sends, recvs)
    ids = plane_ids(e)
    greet(
        [(ids[m], None) for m in (1, 2, 3)]
        + [({"dp": 1 - c}, None), ({"context": z + 1}, z < nc - 1), ({"context": z - 1}, z > 0)]
    )
    wk_all[e, z, c, :, pl.ds(0, kv_width)] = qkv_shard[:, pl.ds(query_width, kv_width)]
    wk_all[e, z, c, :, pl.ds(kv_width, SMALL)] = small_shard[...]
    gather_k = RowsGather(wire, wk_all, e, z, c, nc, 256)
    gather_q = RowsGather(wire, wq_all, e, z, c, nc, 768)
    gather_o = RowsGather(wire, wo_all, e, z, c, nc, 768)
    gather_cot = PlaneGather(wire, cot_all, e)
    gather_k.go("s0")
    wq_all[e, z, c] = qkv_shard[:, pl.ds(0, query_width)]
    wo_all[e, z, c] = wo_shard[...]
    cot_all[0] = cot_ref[...]
    rows = x_ref[...].astype(F32)
    scale1 = lax.rsqrt(jnp.mean(rows * rows, -1, keepdims=True) + EPSILON)
    gather_k.go("s1", "f0", "s2", "f1", "h0", "s3", "f2", "h1", "f3")
    gather_q.go("s0")
    gather_k.go("h2", "h3")
    gather_q.go("s1", "f0")
    gather_k.go("c")

    small = wk_all[:, :, :, :, pl.ds(kv_width, SMALL)].reshape(width, SMALL)
    small = jnp.transpose(small.astype(F32))
    gain_first, gain_second = small[experts : experts + 1], small[experts + 1 : experts + 2]
    gains_ref[0:1] = gain_first
    gains_ref[1:2] = gain_second
    inputs_ref[...] = (rows * scale1 * gain_first).astype(BF16)
    kv_scr[...] = dot_nn(inputs_ref[...], wk_all[...].reshape(width, kv_width + SMALL))

    def turned(head):
        return (head * cos_ref[...] + swap_halves(head) * sin_ref[...]).astype(BF16)

    for j in range(KEY_VALUE_HEADS):
        columns = pl.ds(j * size, size)
        kv_ref[z, :, columns] = turned(kv_scr[:, columns])
    values = pl.ds(kv_width // 2, kv_width // 2)
    kv_ref[z, :, values] = kv_scr[:, values].astype(BF16)
    line = wire.slots(nc)
    wire.start(kv_ref.at[z], kv_ref.at[z], line, {"context": z + 1}, when=z < nc - 1)

    def pass_on(step):
        block = kv_ref.at[z - step]
        pl.when(z >= step)(lambda: wire.arrived(block, line + step - 1, {"context": z - 1}))
        wire.start(
            block, block, line + step, {"context": z + 1}, when=(z >= step) & (z < nc - 1)
        )

    outs = [
        pltpu.make_async_copy(source, dest, out_sems.at[n])
        for n, (source, dest) in enumerate(
            ((wk_all, wk_hbm), (wq_all, wq_hbm), (wo_all, wo_hbm), (cot_all, cot_hbm))
        )
    ]
    outs[0].start()
    for later in range(1, nc):

        def clear(later=later):
            kv_ref[z + later] = jnp.zeros(kv_ref.shape[1:], BF16)

        pl.when(z + later < nc)(clear)
    gather_q.go("s2", "f1", "s3")
    pass_on(1)
    gather_q.go("f2", "h0", "f3")
    pass_on(2)
    gather_q.go("h1", "h2")
    gather_o.go("s0", "s1")
    for step in range(3, nc):
        pass_on(step)
    gather_q.go("h3", "c")
    outs[1].start()

    @pl.loop(0, query_width // 256)
    def _(n):
        columns = pl.ds(pl.multiple_of(n * 256, 256), 256)
        q_scr[:, columns] = dot_nn(
            inputs_ref[...], wq_all[:, :, :, :, columns].reshape(width, 256)
        )

    gather_o.go("f0", "s2", "f1", "s3")

    @pl.loop(0, QUERY_HEADS)
    def _(h):
        columns = pl.ds(pl.multiple_of(h * size, size), size)
        query_ref[:, columns] = turned(q_scr[:, columns])

    logits = kv_scr[:, pl.ds(kv_width, SMALL)]
    lanes = lax.broadcasted_iota(jnp.int32, logits.shape, 1)
    named = lanes == routes_ref[:, 0:1]
    for k in range(1, TOP):
        named = named | (lanes == routes_ref[:, k : k + 1])
    logits = jnp.where(named, logits, MASKED)
    expd = jnp.exp(logits - jnp.max(logits, -1, keepdims=True))
    gates = expd / jnp.sum(expd, -1, keepdims=True)
    gate_all[0] = jnp.transpose(gates)[:GATE_ROWS]
    gate_slot = wire.slots(3)
    for r in (1, 2, 3):
        wire.start(gate_all.at[0], gate_all.at[r], gate_slot + r - 1, ids[r])
    gather_o.go("f2", "h0", "f3")
    gather_cot.spread()
    gather_o.go("h1")

    length = nc * tokens
    group = QUERY_HEADS // KEY_VALUE_HEADS

    def attend(first, last):
        j = first // group
        key = kv_ref[:, :, pl.ds(j * size, size)].reshape(length, size)
        value = kv_ref[:, :, pl.ds(kv_width // 2 + j * size, size)].reshape(length, size)

        @pl.loop(first, last)
        def _(h):
            column = pl.multiple_of(h * size, size)
            scores = dot_nt(query_ref[:, pl.ds(column, size)], key) * (size**-0.5)
            row = z * tokens + lax.broadcasted_iota(jnp.int32, scores.shape, 0)
            place = lax.broadcasted_iota(jnp.int32, scores.shape, 1)
            scores = jnp.where(place <= row, scores, MASKED)
            expd = jnp.exp(scores - jnp.max(scores, -1, keepdims=True))
            total = jnp.sum(expd, -1, keepdims=True)
            mixed = dot_nn(expd.astype(BF16), value) / total
            heads_ref[:, pl.ds(column, size)] = mixed.astype(BF16)

    attend(0, group)
    gather_o.go("h2", "h3")
    attend(group, group + group // 2)
    gather_cot.forward()
    attend(group + group // 2, QUERY_HEADS)
    gather_o.go("c")
    outs[2].start()
    part = width // wo_all.shape[0]
    for block in range(wo_all.shape[0]):
        weight = wo_all[block].reshape(part, width)
        columns = pl.ds(block * part, part)
        hidden_ref[:, columns] = x_ref[:, columns].astype(F32) + dot_nt(heads_ref[...], weight)
    hidden = hidden_ref[...]
    scale2 = lax.rsqrt(jnp.mean(hidden * hidden, -1, keepdims=True) + EPSILON)
    expert_in_ref[...] = (hidden * scale2 * gains_ref[1:2]).astype(BF16)
    for r in (1, 2, 3):
        wire.arrived(gate_all.at[r], gate_slot + r - 1, ids[r])
    for r in range(gate_all.shape[0]):
        rest = jnp.zeros((SMALL - GATE_ROWS, tokens), F32)
        turned_gates = jnp.transpose(jnp.concatenate([gate_all[r], rest], 0))
        both = [
            jnp.sum(jnp.where(lanes == e * EXP_DEV + i, turned_gates, 0.0), -1, keepdims=True)
            for i in range(EXP_DEV)
        ]
        gate_columns[r] = jnp.where(lanes == 0, both[0], jnp.where(lanes == 1, both[1], 0.0))
    gather_cot.complete()
    outs[3].start()
    for copy in outs:
        copy.wait()
    wire.finish()


def front(operands, sizes):
    ne, nc, nd = sizes
    x, qkv_shard = operands[:2]
    tokens, width = x.shape
    rows, qkv_width = qkv_shard.shape
    query_width = QUERY_HEADS * HEAD_DIMENSION
    kv_width = qkv_width - query_width
    gathered = [
        ((ne, nc, nd, rows, kv_width + SMALL), BF16),
        ((ne, nc, nd, rows, query_width), BF16),
        ((ne, nc, nd, rows, width), BF16),
        ((ne, tokens, width), BF16),
    ]
    shapes = gathered + [
        ((ne, GATE_ROWS, tokens), F32),
        ((ne, tokens, SMALL), F32),
        ((tokens, width), BF16),
        ((tokens, query_width), BF16),
        ((nc, tokens, kv_width), BF16),
        ((tokens, query_width), BF16),
        ((tokens, width), F32),
        ((tokens, width), BF16),
        ((8, width), F32),
    ]
    copies = 160
    vmem = pl.BlockSpec(memory_space=pltpu.VMEM)
    anywhere = pl.BlockSpec(memory_space=pl.ANY)
    return pl.pallas_call(
        functools.partial(front_kernel, nc, EXP_DEV * ne),
        out_shape=[jax.ShapeDtypeStruct(*s) for s in shapes],
        in_specs=[vmem] * len(operands),
        out_specs=[anywhere] * 4 + [vmem] * (len(shapes) - 4),
        scratch_shapes=[pltpu.VMEM(*s) for s in gathered]
        + [
            pltpu.VMEM((tokens, kv_width + SMALL), F32),
            pltpu.VMEM((tokens, query_width), F32),
            pltpu.SemaphoreType.DMA((copies,)),
            pltpu.SemaphoreType.DMA((copies,)),
            pltpu.SemaphoreType.DMA((4,)),
        ],
        compiler_params=pltpu.CompilerParams(
            collective_id=0, has_side_effects=True, vmem_limit_bytes=56 * MIB
        ),
    )(*operands)


class PlaneScatter:
    def __init__(self, wire, land, ids):
        self.wire, self.land, self.ids, self.part = wire, land, ids, None
        self.half = land.shape[-1]
        self.first = wire.slots(6)

    def send(self, source, mask, slot):
        self.wire.start(source, self.land.at[slot], self.first + slot, self.ids[mask])

    def near(self, r):
        self.send(self.part(r, r - 1), r, r - 1)

    def far(self):
        self.send(self.part(3, 0), 1, 2)
        self.send(self.part(3, 1), 2, 3)

    def relay(self, part=None):
        for half, r in ((0, 2), (1, 1)):
            slot = 2 + half
            self.wire.arrived(self.land.at[slot], self.first + slot, self.ids[3 - r])
            mine = (part or self.part)(r, half)
            mine[...] = (mine[...].astype(F32) + self.land[slot].astype(F32)).astype(BF16)
            self.send(mine, r, 4 + half)

    def total(self, own):
        for slot, half, mask in ((0, 0, 1), (1, 1, 2), (4, 0, 2), (5, 1, 1)):
            self.wire.arrived(self.land.at[slot], self.first + slot, self.ids[mask])
            columns = pl.ds(half * self.half, self.half)
            own[:, columns] += self.land[slot].astype(F32)


class LineScatter:
    def __init__(self, wire, block, lands, z, nc, up=True):
        self.wire, self.block, self.lands, self.z, self.nc = wire, block, lands, z, nc
        self.up = up
        self.first = [wire.slots(nc - 1), wire.slots(nc - 1)]

    def arrive(self, way, index, j):
        land = self.lands[way].at[index]
        self.wire.arrived(land, self.first[way] + index, {"context": self.z})
        block = self.block(j)
        block[...] = (block[...].astype(F32) + self.lands[way][index].astype(F32)).astype(BF16)

    def move(self, way, j):
        z, nc = self.z, self.nc
        inner, index, near = ((z > 0), j - z, z + 1) if way == 0 else ((z < nc - 1), z - j, z - 1)
        wanted = (j > z) if way == 0 else (j < z)
        pl.when(wanted & inner)(lambda: self.arrive(way, index, j))
        self.wire.start(
            self.block(j),
            self.lands[way].at[index - 1],
            self.first[way] + index - 1,
            {"context": near},
            when=wanted,
        )

    def step(self, s):
        if self.up:
            self.move(0, self.nc - s)
        self.move(1, s - 1)

    def last(self):
        if self.up:
            pl.when(self.z > 0)(lambda: self.arrive(0, 0, self.z))
        pl.when(self.z < self.nc - 1)(lambda: self.arrive(1, 0, self.z))


class RowsScatter:
    def __init__(self, wire, buf, core, plane, lines, e, z, c, nc, start, width, half):
        self.wire, self.buf, self.core, self.plane = wire, buf, core, plane
        self.e, self.c = e, c
        self.all = pl.ds(start, width)
        self.cols = (pl.ds(start, half), pl.ds(start + half, width - half))
        self.ids = plane_ids(e)
        self.core_slot = wire.slots(1)
        self.first = wire.slots(6)
        rows = buf.shape[2] // nc
        self.line = LineScatter(
            wire,
            lambda j: buf.at[c, e, pl.ds(pl.multiple_of(j * rows, rows), rows), self.all],
            lines,
            z,
            nc,
        )

    def share(self):
        self.wire.start(
            self.buf.at[1 - self.c, :, :, self.all], self.core, self.core_slot, {"dp": 1 - self.c}
        )

    def at(self, r, half):
        return self.buf.at[self.c, flip(self.e, r), :, self.cols[half]]

    def send(self, r, half, mask, slot):
        self.wire.start(
            self.at(r, half), self.plane(slot, half), self.first + slot, self.ids[mask]
        )

    def merge(self, before=None):
        self.wire.arrived(self.core, self.core_slot, {"dp": 1 - self.c})
        for r in (3, 1, 2, 0):
            block = flip(self.e, r)
            part = self.buf.at[self.c, block, :, self.all]
            part[...] = (part[...].astype(F32) + self.core[block].astype(F32)).astype(BF16)
            if r == 3:
                if before is not None:
                    before()
                self.send(3, 0, 1, 2)
                self.send(3, 1, 2, 3)
            elif r:
                self.send(r, r - 1, r, r - 1)

    def add(self, r, half, slot, mask):
        land = self.plane(slot, half)
        self.wire.arrived(land, self.first + slot, self.ids[mask])
        part = self.at(r, half)
        part[...] = (part[...].astype(F32) + land[...].astype(F32)).astype(BF16)

    def relay(self):
        for half, r in ((0, 2), (1, 1)):
            self.add(r, half, 2 + half, 3 - r)
            self.send(r, half, r, 4 + half)

    def total(self):
        for slot, half, mask in ((0, 0, 1), (1, 1, 2), (4, 0, 2), (5, 1, 1)):
            self.add(0, half, slot, mask)


class ExpertLine:
    def __init__(self, wire, base, land, ins, outs, sems, z, nc):
        self.wire, self.base, self.land = wire, base, land
        self.ins, self.outs, self.sems, self.z, self.nc = ins, outs, sems, z, nc
        self.end = (z == 0) | (z == nc - 1)
        self.inner = jnp.logical_not(self.end)
        self.width = base.shape[-1] // EXP_DEV
        self.first = wire.slots((nc + 1) * EXP_DEV)
        self.sent = []

    def part(self, ref, j, i):
        return ref.at[j, :, pl.ds(i * self.width, self.width)]

    def combine(self, sources, stores, out):
        step = self.ins.shape[2]
        count = sources[0].shape[0] // step

        def loads(p):
            rows = pl.ds(p * step, step)
            return [
                pltpu.make_async_copy(
                    source.at[rows], self.ins.at[k, p % 2], self.sems.at[2 * k + p % 2]
                )
                for k, source in enumerate(sources)
            ]

        def store(p):
            pairs = stores(pl.ds(p * step, step), out.at[p % 2])
            return [
                pltpu.make_async_copy(source, dest, self.sems.at[8 + 2 * n + p % 2])
                for n, (source, dest) in enumerate(pairs)
            ]

        for copy in loads(0):
            copy.start()
        for p in range(count):
            if p + 1 < count:
                for copy in loads(p + 1):
                    copy.start()
            for copy in loads(p):
                copy.wait()
            if p > 1:
                for copy in store(p - 2):
                    copy.wait()
            total = self.ins[0, p % 2].astype(F32)
            for k in range(1, len(sources)):
                total = total + self.ins[k, p % 2].astype(F32)
            out[p % 2] = total.astype(out.dtype)
            for copy in store(p):
                copy.start()
        for p in range(max(0, count - 2), count):
            for copy in store(p):
                copy.wait()

    def copy(self, i, r, number):
        target, slot = flip(self.z, r), self.z
        if r == 3:
            target = jnp.where(self.end, flip(self.z, 1), target)
            slot = jnp.where(self.end, self.nc, slot)
        return pltpu.make_async_remote_copy(
            src_ref=self.part(self.base, flip(self.z, r), i),
            dst_ref=self.part(self.land, slot, i),
            send_sem=self.wire.sends.at[number],
            recv_sem=self.wire.recvs.at[self.first + slot * EXP_DEV + i],
            device_id={"context": target},
            device_id_type=MESH,
        )

    def send(self, i, r, when=None):
        number = len(self.sent)
        guard(when, self.copy(i, r, number).start)
        self.sent.append((when, i, r, number))

    def finish(self):
        for when, i, r, number in self.sent:
            guard(when, self.copy(i, r, number).wait_send)

    def arrived(self, slot, i):
        land = self.part(self.land, slot, i)
        self.wire.arrived(land, self.first + slot * EXP_DEV + i, {"context": self.z})

    def relay(self, i):
        mine = self.part(self.base, flip(self.z, 2), i)

        def add():
            self.arrived(self.nc, i)
            self.combine(
                [mine, self.part(self.land, self.nc, i)],
                lambda rows, low: [(low, mine.at[rows])],
                self.outs[0],
            )

        pl.when(self.inner)(add)
        self.send(i, 2, when=self.inner)

    def last(self, i, results):
        z = self.z
        sources = [self.part(self.base, z, i)]
        for r in (1, 2):
            self.arrived(flip(z, r), i)
            sources.append(self.part(self.land, flip(z, r), i))

        def stores(rows, wide):
            pairs, first = [], 0
            for result in results:
                columns = pl.ds(first, result.shape[-1])
                pairs.append((wide.at[:, columns], result.at[i, rows]))
                first += result.shape[-1]
            return pairs

        pl.when(self.end)(lambda: self.combine(sources, stores, self.outs[1]))

        def inner():
            self.arrived(flip(z, 3), i)
            self.combine(sources + [self.part(self.land, flip(z, 3), i)], stores, self.outs[1])

        pl.when(self.inner)(inner)


def back_kernel(
    nc,
    experts,
    gates_ref,
    gate_ref,
    gains_ref,
    cos_ref,
    sin_ref,
    expert_in_hbm,
    cot_hbm,
    w_gu_hbm,
    w_dn_hbm,
    x_hbm,
    inputs_hbm,
    query_hbm,
    kv_hbm,
    heads_hbm,
    hidden_hbm,
    wk_hbm,
    wq_hbm,
    o_hbm,
    layer_ref,
    d_x_ref,
    sum_q_ref,
    sum_o_ref,
    sum_gu_hbm,
    sum_dn_hbm,
    base_hbm,
    land_hbm,
    y_hbm,
    x_all,
    y_land,
    dx_land,
    core_land,
    plane_q,
    plane_k,
    lines_o,
    lines_q,
    lines_k,
    dkv_land,
    d_in_ref,
    dg_lanes,
    dg_part,
    dg_land,
    ins,
    out_low,
    out_wide,
    sends_1,
    recvs_1,
    sends_2,
    recvs_2,
    sends_e,
    recvs_e,
    hand_sends,
    hand_recvs,
    stage_sems,
    load_sems,
    sum_sems,
    y_sems,
    credits,
):
    e, z, c = (lax.axis_index(a) for a in ("expert", "context", "dp"))
    size = HEAD_DIMENSION
    blocks, tokens, width = cot_hbm.shape
    ff = w_dn_hbm.shape[1]
    query_width = QUERY_HEADS * size
    key_width = KEY_VALUE_HEADS * size
    qkv_width = query_width + 2 * key_width
    rest = wk_hbm.shape[-1]
    grad_width = base_hbm.shape[-1]
    ids = plane_ids(e)
    sibling = {"dp": 1 - c}
    wire_1, wire_2, wire_e = Wire(sends_1, recvs_1), Wire(sends_2, recvs_2), Wire(sends_e, recvs_e)
    expert = ExpertLine(
        wire_e, base_hbm, land_hbm, ins, (out_low, out_wide), sum_sems, z, nc
    )
    gather = PlaneGather(wire_1, x_all, e)
    scatter_dx = PlaneScatter(wire_1, dx_land, ids)
    scatter_y = PlaneScatter(wire_2, y_land, ids)
    dg_slot = wire_1.slots(3)

    def token_phase(w_gu, w_dn, cot_all, a_all, dgu_all, y_stage, dx_part, stage):
        scatter_dx.part = lambda r, half: dx_part.at[
            r - 1, :, pl.ds(half * width // 2, width // 2)
        ]
        sources = [(expert_in_hbm, x_all.at[0])]
        for i in range(EXP_DEV):
            sources += [(w_gu_hbm.at[i], w_gu.at[i]), (w_dn_hbm.at[i], w_dn.at[i])]
            if i == 0:
                sources += [(cot_hbm.at[0], cot_all.at[0]), (cot_hbm.at[1:], cot_all.at[1:])]
        loads = [
            pltpu.make_async_copy(source, dest, load_sems.at[n])
            for n, (source, dest) in enumerate(sources)
        ]
        for copy in loads:
            copy.start()
        greet(
            [(ids[m], None) for m in (1, 2, 3)]
            + [(sibling, None), ({"context": flip(z, 2)}, None)]
            + [({"context": z + 1}, z < nc - 1), ({"context": z - 1}, z > 0)]
        )
        loads[0].wait()
        gather.spread()
        step = 256
        wide = 512
        dg_lanes[...] = jnp.zeros_like(dg_lanes)

        def hidden_units(r, i):
            @pl.loop(0, ff // step)
            def _(f):
                column = pl.multiple_of(f * step, step)
                rows, grads = x_all[r], cot_all[r]
                gate_part = dot_nn(rows, w_gu[i, :, pl.ds(column, step)])
                up_part = dot_nn(rows, w_gu[i, :, pl.ds(ff + column, step)])
                raw = dot_nt(grads, w_dn[i, pl.ds(column, step), :])
                gate = gates_ref[r][:, i : i + 1]
                sigma = jax.nn.sigmoid(gate_part)
                silu = gate_part * sigma
                act = silu * up_part
                lanes = lax.broadcasted_iota(jnp.int32, dg_lanes.shape[1:], 1)
                dg_lanes[r] += jnp.where(
                    lanes == e * EXP_DEV + i, jnp.sum(act * raw, -1, keepdims=True), 0.0
                )
                a_all[r, :, pl.ds(i * ff + column, step)] = (act * gate).astype(BF16)
                d_act = raw * gate
                d_gate_part = d_act * up_part * sigma * (1.0 + gate_part * (1.0 - sigma))
                first = i * 2 * ff + column
                dgu_all[r, :, pl.ds(first, step)] = d_gate_part.astype(BF16)
                dgu_all[r, :, pl.ds(first + ff, step)] = (d_act * silu).astype(BF16)

        def y_copy(r):
            return pltpu.make_async_copy(y_stage.at[r % 2], y_hbm.at[r], y_sems.at[r % 2])

        def outputs(r):
            @pl.loop(0, width // wide)
            def _(n):
                columns = pl.ds(pl.multiple_of(n * wide, wide), wide)
                d_rows = dot_nt(dgu_all[r, :, pl.ds(0, 2 * ff)], w_gu[0, columns, :])
                d_rows += dot_nt(dgu_all[r, :, pl.ds(2 * ff, 2 * ff)], w_gu[1, columns, :])
                weight = w_dn[:, :, columns].reshape(EXP_DEV * ff, wide)
                y_stage[r % 2, :, columns] = dot_nn(a_all[r], weight).astype(BF16)
                if r == 0:
                    d_in_ref[:, columns] = d_rows
                else:
                    dx_part[r - 1, :, columns] = d_rows.astype(BF16)

            y_copy(r).start()
            dg_part[r] = jnp.transpose(dg_lanes[r])[:GATE_ROWS]
            if r:
                wire_1.start(dg_part.at[r], dg_land.at[r - 1], dg_slot + r - 1, ids[r])

        half_rows = width // nc // 2
        units = [(i, r) for i in range(EXP_DEV) for r in (3, 2, 1, 0)]

        def keep(u):
            i, r = units[u]
            return pltpu.make_async_copy(
                stage.at[u % 2, c], expert.part(base_hbm, flip(z, r), i), stage_sems.at[u % 2]
            )

        def hand(u):
            r = units[u][1]
            return pltpu.make_async_remote_copy(
                src_ref=stage.at[u % 2, 1 - c],
                dst_ref=core_land.at[r],
                send_sem=hand_sends.at[u],
                recv_sem=hand_recvs.at[u],
                device_id=sibling,
                device_id_type=MESH,
            )

        def weight_grads(u):
            i, r = units[u]
            columns = pl.ds(pl.multiple_of(flip(z, r) * 2 * half_rows, 2 * half_rows), 2 * half_rows)
            for first, source, grad, start, count in (
                (0, x_all, dgu_all, i * 2 * ff, 2),
                (2 * ff, cot_all, a_all, i * ff, 1),
            ):
                rows = source[:, :, columns].reshape(blocks * tokens, 2 * half_rows)

                @pl.loop(0, count)
                def _(n):
                    column = pl.multiple_of(n * ff, ff)
                    part = grad[:, :, pl.ds(pl.multiple_of(start + column, ff), ff)]
                    result = dot_tn(rows, part.reshape(blocks * tokens, ff)).astype(BF16)
                    stage[u % 2, :, :, pl.ds(pl.multiple_of(first + column, ff), ff)] = (
                        result.reshape(2, half_rows, ff)
                    )

            if u == nc:
                pl.semaphore_wait(credits.at[3], 1)
            hand(u).start()

        def settle(u):
            hand(u).wait_recv()
            r = units[u][1]
            mine = stage[u % 2, c].astype(F32) + core_land[r].astype(F32)
            stage[u % 2, c] = mine.astype(BF16)
            keep(u).start()

        def clear(u):
            keep(u).wait()
            hand(u).wait_send()
            i, r = units[u]
            if i == 0 or r == 3:
                if r in (3, 1):
                    expert.send(i, r)
                elif r == 2:
                    expert.send(i, r, when=expert.end)

        for copy in loads[1:4]:
            copy.wait()
        hidden_units(0, 0)
        for copy in loads[4:]:
            copy.wait()
        gather.forward()
        hidden_units(0, 1)
        gather.near(1)
        hidden_units(1, 0)
        gather.near(2)
        hidden_units(2, 0)
        gather.far()
        hidden_units(3, 0)
        weight_grads(0)
        weight_grads(1)
        settle(0)
        clear(0)
        weight_grads(2)
        settle(1)
        clear(1)
        weight_grads(3)
        settle(2)
        hidden_units(1, 1)
        clear(2)
        settle(3)
        pl.semaphore_signal(credits.at[3], inc=1, device_id=sibling, device_id_type=MESH)
        outputs(1)
        scatter_dx.near(1)
        hidden_units(2, 1)
        outputs(2)
        scatter_dx.near(2)
        hidden_units(3, 1)
        y_copy(1).wait()
        outputs(3)
        scatter_dx.far()
        clear(3)
        y_copy(2).wait()
        outputs(0)
        weight_grads(4)
        expert.relay(0)
        weight_grads(5)
        settle(4)
        scatter_dx.relay()
        clear(4)
        weight_grads(6)
        settle(5)
        clear(5)
        weight_grads(7)
        settle(6)
        scatter_dx.total(d_in_ref)
        for r in (1, 2):
            pl.semaphore_signal(credits.at[r], inc=1, device_id=ids[r], device_id_type=MESH)
        settle(7)
        clear(6)
        clear(7)
        y_copy(3).wait()
        y_copy(0).wait()
        wire_1.finish()
        pl.semaphore_signal(credits.at[0], inc=1, device_id=sibling, device_id_type=MESH)

    def token_rows_phase(
        weight,
        grads_o,
        grads_q,
        x_ref,
        inputs_ref,
        query_ref,
        kv_ref,
        heads_ref,
        hidden_ref,
        d_hidden_ref,
        d_attn_ref,
        d_heads_ref,
        d_all_ref,
        rows_ref,
        dkv_acc,
        dkv_ref,
        y_relay,
    ):
        cot_ref, d_inputs_ref = d_heads_ref, hidden_ref
        scatter_y.part = lambda r, half: y_hbm.at[r, :, pl.ds(half * width // 2, width // 2)]
        y_loads = [
            pltpu.make_async_copy(scatter_y.part(2 - half, half), y_relay.at[half], y_sems.at[half])
            for half in range(2)
        ]
        for copy in y_loads:
            copy.start()
        planes = grads_o.shape[1]
        part = width // planes
        sources = (
            (hidden_hbm, hidden_ref),
            (cot_hbm.at[0], cot_ref),
            (o_hbm, weight.at[:, pl.ds(0, width)]),
            (heads_hbm, heads_ref),
            (query_hbm, query_ref),
            (kv_hbm, kv_ref),
            (x_hbm, x_ref),
            (inputs_hbm, inputs_ref),
        )
        loads = [
            pltpu.make_async_copy(source, dest, load_sems.at[4 + n])
            for n, (source, dest) in enumerate(sources)
        ]
        for copy in loads:
            copy.start()
        for r in (1, 2):
            scatter_y.near(r)
        scatter_y.far()

        def rows_scatter(buf, core, plane, lines, start, count, half):
            return RowsScatter(
                wire_2,
                buf,
                core,
                plane,
                [lines.at[0], lines.at[1]],
                e,
                z,
                c,
                nc,
                start,
                count,
                half,
            )

        rows_of = part // 2
        scatter_o = rows_scatter(
            grads_o,
            x_all.at[:, pl.ds(0, rows_of)],
            lambda slot, half: dx_land.at[slot, pl.ds(0, rows_of)],
            lines_o,
            0,
            width,
            width // 2,
        )
        scatter_q = rows_scatter(
            grads_q,
            core_land.at[:, :, pl.ds(0, query_width)],
            lambda slot, half: plane_q.at[slot],
            lines_q,
            0,
            query_width,
            query_width // 2,
        )
        rest_half = rest // 256 * 128
        scatter_k = rows_scatter(
            grads_q,
            core_land.at[:, :, pl.ds(query_width, rest)],
            lambda slot, half: plane_k.at[
                slot, :, pl.ds(0, rest - rest_half if half else rest_half)
            ],
            lines_k,
            query_width,
            rest,
            rest_half,
        )
        scatter_kv = [
            LineScatter(
                wire_2,
                lambda j, h=h: dkv_ref.at[h, j],
                [dkv_land.at[h], dkv_land.at[h]],
                z,
                nc,
                up=False,
            )
            for h in range(KEY_VALUE_HEADS)
        ]

        loads[0].wait()
        loads[1].wait()
        hidden, d_in = hidden_ref[...], d_in_ref[...]
        scale2 = lax.rsqrt(jnp.mean(hidden * hidden, -1, keepdims=True) + EPSILON)
        scaled = d_in * gains_ref[1:2]
        mean = jnp.mean(scaled * hidden, -1, keepdims=True)
        d_hidden = cot_ref[...].astype(F32) + scale2 * scaled
        d_hidden = d_hidden - hidden * (scale2 * scale2 * scale2 * mean)
        d_hidden_ref[...] = d_hidden
        d_attn_ref[...] = d_hidden.astype(BF16)
        rows_ref[...] = jnp.zeros_like(rows_ref)
        rows_ref[experts + 1 : experts + 2, :] = jnp.sum(d_in * hidden * scale2, 0, keepdims=True)

        loads[2].wait()

        @pl.loop(0, query_width // 256)
        def _(n):
            columns = pl.ds(pl.multiple_of(n * 256, 256), 256)
            d_heads_ref[:, columns] = dot_nn(d_attn_ref[...], weight[:, columns]).astype(BF16)

        load_q = [
            pltpu.make_async_copy(wq_hbm, weight.at[:, pl.ds(0, query_width)], load_sems.at[0]),
            pltpu.make_async_copy(wk_hbm, weight.at[:, pl.ds(query_width, rest)], load_sems.at[1]),
        ]
        for copy in load_q:
            copy.start()
        loads[3].wait()

        def row_grads(buf, left, right, first, count, extra=None):
            @pl.loop(0, planes)
            def _(block):
                columns = pl.ds(pl.multiple_of(block * part, part), part)
                result = dot_tn(left[:, columns], right)
                if extra is not None:
                    result = result + extra(columns)
                result = result.astype(BF16).reshape(nc, 2, part // nc // 2, count)
                for half in range(2):
                    buf[half, block, :, pl.ds(first, count)] = result[:, half].reshape(
                        part // 2, count
                    )

        row_grads(grads_o, d_attn_ref, heads_ref[...], 0, width)
        pl.semaphore_wait(credits.at[0], 1)
        scatter_o.share()
        y_own = pltpu.make_async_copy(y_hbm.at[0], heads_ref, load_sems.at[2])
        y_own.start()

        length = nc * tokens
        group = QUERY_HEADS // KEY_VALUE_HEADS
        for copy in loads[4:6]:
            copy.wait()
        dkv_acc[...] = jnp.zeros_like(dkv_acc)

        def attend(j, first, last):
            key = kv_ref[:, :, pl.ds(j * size, size)].reshape(length, size)
            value = kv_ref[:, :, pl.ds(key_width + j * size, size)].reshape(length, size)

            @pl.loop(j * group + first, j * group + last)
            def _(h):
                columns = pl.ds(pl.multiple_of(h * size, size), size)
                query, grad = query_ref[:, columns], d_heads_ref[:, columns]
                probs = masked_probs(z * tokens, query, key)
                d_probs = dot_nt(grad, value)
                inner = jnp.sum(probs * d_probs, axis=-1, keepdims=True)
                d_raw = (probs * (d_probs - inner) * (size**-0.5)).astype(BF16)
                d_query = dot_nn(d_raw, key)
                d_query = d_query * cos_ref[...] - swap_halves(d_query) * sin_ref[...]
                d_all_ref[:, columns] = d_query.astype(BF16)
                dkv_acc[j, :, pl.ds(0, size)] += dot_tn(d_raw, query)
                dkv_acc[j, :, pl.ds(size, size)] += dot_tn(probs.astype(BF16), grad)

        def round_kv(j):
            for block in range(nc):
                rows = dkv_acc[j, pl.ds(block * tokens, tokens), :]
                dkv_ref[j, block] = rows.astype(BF16)

        def enter():
            pl.semaphore_wait(credits.at[1], 1)
            pl.semaphore_wait(credits.at[2], 1)

        attend(0, 0, group)
        round_kv(0)
        scatter_kv[0].step(1)
        scatter_o.merge(enter)
        for copy in y_loads:
            copy.wait()
        scatter_y.relay(lambda r, half: y_relay.at[half])
        attend(1, 0, group // 2)
        scatter_kv[0].step(2)
        attend(1, group // 2, group)
        round_kv(1)
        scatter_kv[1].step(1)
        scatter_kv[0].step(3)
        scatter_o.relay()

        for copy in loads[6:]:
            copy.wait()
        row_grads(grads_q, inputs_ref, d_all_ref[:, pl.ds(0, query_width)], 0, query_width)
        scatter_q.share()
        scatter_kv[1].step(2)
        scatter_kv[1].step(3)
        expert.send(1, 2, when=expert.end)
        expert.send(1, 1)
        y_own.wait()
        hidden_ref[...] += heads_ref[...].astype(F32)
        scatter_y.total(hidden_ref)
        layer_ref[...] = hidden_ref[...].astype(BF16)
        scatter_o.total()
        scatter_q.merge()
        for h in range(KEY_VALUE_HEADS):
            scatter_kv[h].last()

        for h in range(KEY_VALUE_HEADS):
            grad = dkv_ref[h, z, :, pl.ds(0, size)].astype(F32)
            grad = grad * cos_ref[...] - swap_halves(grad) * sin_ref[...]
            d_all_ref[:, pl.ds(query_width + h * size, size)] = grad.astype(BF16)
            d_all_ref[:, pl.ds(query_width + key_width + h * size, size)] = dkv_ref[
                h, z, :, pl.ds(size, size)
            ]

        total = dg_part[0]
        for r in (1, 2, 3):
            wire_1.arrived(dg_land.at[r - 1], dg_slot + r - 1, ids[r])
            total = total + dg_land[r - 1]
        gates = gate_ref[0]
        d_logits = gates * (total - jnp.sum(gates * total, 0, keepdims=True))
        d_logits = jnp.concatenate(
            [d_logits, jnp.zeros((SMALL - d_logits.shape[0], tokens), F32)], 0
        )
        d_all_ref[:, pl.ds(qkv_width, SMALL)] = jnp.transpose(d_logits).astype(BF16)

        for copy in load_q:
            copy.wait()

        @pl.loop(0, planes)
        def _(block):
            columns = pl.ds(pl.multiple_of(block * part, part), part)
            d_inputs_ref[:, columns] = dot_nt(d_all_ref[...], weight[columns, :])

        rows = x_ref[...].astype(F32)
        scale1 = lax.rsqrt(jnp.mean(rows * rows, -1, keepdims=True) + EPSILON)
        d_inputs = d_inputs_ref[...]
        rows_ref[experts : experts + 1, :] = jnp.sum(d_inputs * rows * scale1, 0, keepdims=True)

        def extra(columns):
            small = jnp.transpose(rows_ref[:, columns])
            return jnp.concatenate([jnp.zeros((part, rest - SMALL), F32), small], 1)

        row_grads(
            grads_q, inputs_ref, d_all_ref[:, pl.ds(query_width, rest)], query_width, rest, extra
        )
        scatter_k.share()
        expert.relay(1)
        scatter_q.relay()
        scatter_k.merge()
        scaled = d_inputs_ref[...] * gains_ref[0:1]
        rows = x_ref[...].astype(F32)
        scale1 = lax.rsqrt(jnp.mean(rows * rows, -1, keepdims=True) + EPSILON)
        mean = jnp.mean(scaled * rows, -1, keepdims=True)
        d_x = d_hidden_ref[...] + scale1 * scaled - rows * (scale1 * scale1 * scale1 * mean)
        d_x_ref[...] = d_x.astype(BF16)
        scatter_q.total()
        expert.last(0, (sum_gu_hbm, sum_dn_hbm))
        scatter_k.relay()
        scatter_o.line.step(1)
        scatter_q.line.step(1)
        scatter_k.total()
        scatter_k.line.step(1)
        for s in range(2, nc):
            for scatter in (scatter_o, scatter_q, scatter_k):
                scatter.line.step(s)
        for scatter in (scatter_o, scatter_q, scatter_k):
            scatter.line.last()
        sum_o_ref[...] = scatter_o.line.block(z)[...].astype(F32)
        sum_q_ref[...] = grads_q[c, e, pl.ds(pl.multiple_of(z * (rows_of // nc), rows_of // nc), rows_of // nc)].astype(F32)
        expert.last(1, (sum_gu_hbm, sum_dn_hbm))
        wire_2.finish()
        expert.finish()

    held = EXP_DEV
    pl.run_scoped(
        token_phase,
        pltpu.VMEM((held, width, 2 * ff), BF16),
        pltpu.VMEM((held, ff, width), BF16),
        pltpu.VMEM((blocks, tokens, width), BF16),
        pltpu.VMEM((blocks, tokens, held * ff), BF16),
        pltpu.VMEM((blocks, tokens, held * 2 * ff), BF16),
        pltpu.VMEM((2, tokens, width), BF16),
        pltpu.VMEM((blocks - 1, tokens, width), BF16),
        pltpu.VMEM((2, 2, width // nc // 2, grad_width // held), BF16),
    )
    rows_half = width // blocks // 2
    pl.run_scoped(
        token_rows_phase,
        pltpu.VMEM((width, qkv_width + SMALL), BF16),
        pltpu.VMEM((2, blocks, rows_half, width), BF16),
        pltpu.VMEM((2, blocks, rows_half, qkv_width + SMALL), BF16),
        pltpu.VMEM((tokens, width), BF16),
        pltpu.VMEM((tokens, width), BF16),
        pltpu.VMEM((tokens, query_width), BF16),
        pltpu.VMEM((nc, tokens, 2 * key_width), BF16),
        pltpu.VMEM((tokens, query_width), BF16),
        pltpu.VMEM((tokens, width), F32),
        pltpu.VMEM((tokens, width), F32),
        pltpu.VMEM((tokens, width), BF16),
        pltpu.VMEM((tokens, query_width), BF16),
        pltpu.VMEM((tokens, qkv_width + SMALL), BF16),
        pltpu.VMEM((SMALL, width), F32),
        pltpu.VMEM((KEY_VALUE_HEADS, nc * tokens, 2 * size), F32),
        pltpu.VMEM((KEY_VALUE_HEADS, nc, tokens, 2 * size), BF16),
        pltpu.VMEM((2, tokens, width // 2), BF16),
    )


def back(operands, sizes):
    ne, nc, nd = sizes
    cot, w_gu, w_dn, x = operands[6], operands[7], operands[8], operands[9]
    tokens, width = x.shape
    held, ff = w_dn.shape[0], w_dn.shape[1]
    rest = operands[15].shape[-1]
    q_width = QUERY_HEADS * HEAD_DIMENSION + rest
    rows = width // (ne * nc * nd)
    rest_half = rest // 256 * 128
    shard, grads = width // (nc * nd), held * 3 * ff
    kv_size = 2 * HEAD_DIMENSION
    shapes = [
        ((tokens, width), BF16),
        ((tokens, width), BF16),
        ((rows, q_width), F32),
        ((rows, width), F32),
        ((held, shard, 2 * ff), F32),
        ((held, shard, ff), F32),
        ((nc, shard, grads), BF16),
        ((nc + 1, shard, grads), BF16),
        ((ne, tokens, width), BF16),
    ]
    vmem = pl.BlockSpec(memory_space=pltpu.VMEM)
    anywhere = pl.BlockSpec(memory_space=pl.ANY)
    step, units = 48, nc * held
    return pl.pallas_call(
        functools.partial(back_kernel, nc, EXP_DEV * ne),
        out_shape=[jax.ShapeDtypeStruct(*s) for s in shapes],
        in_specs=[vmem] * 5 + [anywhere] * (len(operands) - 5),
        out_specs=[vmem] * 4 + [anywhere] * 5,
        scratch_shapes=[
            pltpu.VMEM((ne, tokens, width), BF16),
            pltpu.VMEM((6, tokens, width // 2), BF16),
            pltpu.VMEM((6, tokens, width // 2), BF16),
            pltpu.VMEM((nc, shard, grads // held), BF16),
            pltpu.VMEM((6, nc * rows, QUERY_HEADS * HEAD_DIMENSION // 2), BF16),
            pltpu.VMEM((6, nc * rows, rest - rest_half), BF16),
            pltpu.VMEM((2, nc - 1, rows, width), BF16),
            pltpu.VMEM((2, nc - 1, rows, QUERY_HEADS * HEAD_DIMENSION), BF16),
            pltpu.VMEM((2, nc - 1, rows, rest), BF16),
            pltpu.VMEM((KEY_VALUE_HEADS, nc - 1, tokens, kv_size), BF16),
            pltpu.VMEM((tokens, width), F32),
            pltpu.VMEM((ne, tokens, SMALL), F32),
            pltpu.VMEM((ne, GATE_ROWS, tokens), F32),
            pltpu.VMEM((ne - 1, GATE_ROWS, tokens), F32),
            pltpu.VMEM((4, 2, step, grads // held), BF16),
            pltpu.VMEM((2, step, grads // held), BF16),
            pltpu.VMEM((2, step, grads // held), F32),
            pltpu.SemaphoreType.DMA((32,)),
            pltpu.SemaphoreType.DMA((32,)),
            pltpu.SemaphoreType.DMA((64,)),
            pltpu.SemaphoreType.DMA((64,)),
            pltpu.SemaphoreType.DMA((units + held,)),
            pltpu.SemaphoreType.DMA(((nc + 1) * held,)),
            pltpu.SemaphoreType.DMA((units,)),
            pltpu.SemaphoreType.DMA((units,)),
            pltpu.SemaphoreType.DMA((2,)),
            pltpu.SemaphoreType.DMA((12,)),
            pltpu.SemaphoreType.DMA((12,)),
            pltpu.SemaphoreType.DMA((2,)),
            pltpu.SemaphoreType.REGULAR((4,)),
        ],
        compiler_params=pltpu.CompilerParams(
            collective_id=1, has_side_effects=True, vmem_limit_bytes=63 * MIB
        ),
    )(*operands)


def local_plain(
    layer_input,
    gain_attn,
    query_key_value_weight,
    w_out,
    w_router,
    gain_ffn,
    w_gate_up,
    w_down,
    routes,
    d_out,
):
    tokens = layer_input.shape[1]
    model_width = layer_input.shape[2]
    ne, nc, nd = (lax.axis_size(a) for a in ("expert", "context", "dp"))
    expert_total = EXP_DEV * ne
    ff = w_down.shape[1]
    me = lax.axis_index("expert")
    first_row = lax.axis_index("context") * tokens
    query_width = QUERY_HEADS * HEAD_DIMENSION
    key_width = KEY_VALUE_HEADS * HEAD_DIMENSION
    qkv_width = query_width + 2 * key_width

    small = jnp.concatenate([w_router, gain_attn[:, None], gain_ffn[:, None]], -1)
    small = jnp.pad(small, ((0, 0), (0, 128 - small.shape[1])))
    gathered = gather_rows(jnp.concatenate([query_key_value_weight, small], -1))
    out_turned = gather_rows(w_out.T)
    qkv_weight = gathered[:, :qkv_width]
    router_weight = gathered[:, qkv_width : qkv_width + expert_total]
    gains = gathered[:, qkv_width + expert_total : qkv_width + expert_total + 2].T.astype(F32)
    gain_first, gain_second = gains[0], gains[1]
    cotangent_all = plane_gather(d_out[0])

    token_rows = layer_input[0].astype(F32)
    scale1 = lax.rsqrt(jnp.mean(token_rows * token_rows, -1, keepdims=True) + EPSILON)
    inputs1 = (token_rows * scale1 * gain_first).astype(BF16)
    query_key_value = dot_nn(inputs1, qkv_weight)
    cosine_values, sine_values = rope_tables(first_row + jnp.arange(tokens), HEAD_DIMENSION)
    rotated = rotate_half(
        query_key_value[:, : query_width + key_width].reshape(tokens, -1, HEAD_DIMENSION),
        cosine_values,
        sine_values,
    ).reshape(tokens, -1)
    query = rotated[:, :query_width].astype(BF16)
    key_value_local = jnp.concatenate(
        [rotated[:, query_width:], query_key_value[:, query_width + key_width :]], -1
    ).astype(BF16)
    key_value = line_gather(key_value_local, "context", both=False).reshape(nc * tokens, -1)
    first = first_row.astype(jnp.int32).reshape(1)
    heads = attend_forward(first, query, key_value)

    logits = dot_nn(inputs1, router_weight)
    chosen_ids = routes[0]
    picks = (chosen_ids[:, :, None] == jnp.arange(expert_total)[None, None, :]).astype(F32)
    chosen = jnp.sum(picks * logits[:, None, :], -1)
    gates = jax.nn.softmax(chosen, axis=-1)
    gate_dense = jnp.sum(picks * gates[:, :, None], 1).T
    gate_blocks = cube_gather(gate_dense, "expert", axis_masks("expert"))
    gate_local = jnp.concatenate(
        [lax.dynamic_slice_in_dim(b, me * EXP_DEV, EXP_DEV, 0) for b in gate_blocks], 1
    )

    attn = dot_nt(heads, out_turned)
    hidden = token_rows + attn
    scale2 = lax.rsqrt(jnp.mean(hidden * hidden, -1, keepdims=True) + EPSILON)
    expert_in = (hidden * scale2 * gain_second).astype(BF16)

    rows_all = plane_gather(expert_in)
    gate_up = jnp.einsum("td,edf->etf", rows_all, w_gate_up, preferred_element_type=F32)
    gate_part, up_part = gate_up[..., :ff], gate_up[..., ff:]
    sigma = jax.nn.sigmoid(gate_part)
    silu = gate_part * sigma
    act = silu * up_part
    gate_column = gate_local[:, :, None]
    act_gated = (act * gate_column).astype(BF16)
    partial_out = jnp.einsum("etf,efd->td", act_gated, w_down, preferred_element_type=F32)
    mixture = plane_scatter(partial_out.astype(BF16), tokens)
    layer_result = (hidden + mixture).astype(BF16)

    d_act_raw = jnp.einsum("td,efd->etf", cotangent_all, w_down, preferred_element_type=F32)
    d_gates_local = jnp.sum(d_act_raw * act, -1)
    d_act = d_act_raw * gate_column
    d_gate_part = d_act * up_part * sigma * (1.0 + gate_part * (1.0 - sigma))
    d_up_part = d_act * silu
    d_gate_up = jnp.concatenate([d_gate_part, d_up_part], -1).astype(BF16)
    d_rows = jnp.einsum("etf,edf->td", d_gate_up, w_gate_up, preferred_element_type=F32)
    grad_down = jnp.einsum("td,etf->edf", cotangent_all, act_gated, preferred_element_type=F32)
    grad_gate_up = jnp.einsum("td,etf->edf", rows_all, d_gate_up, preferred_element_type=F32)

    d_expert_in = plane_scatter(d_rows.astype(BF16), tokens)
    d_gate_blocks = d_gates_local.reshape(EXP_DEV, ne, tokens)
    d_gates_dense = jnp.zeros((expert_total, tokens), F32)
    for r in range(ne):
        arrived = d_gate_blocks[:, r]
        if r:
            arrived = exchange(arrived, "expert", r)
        d_gates_dense = lax.dynamic_update_slice(d_gates_dense, arrived, ((me ^ r) * EXP_DEV, 0))
    d_gates = jnp.sum(picks * d_gates_dense.T[:, None, :], -1)
    d_chosen = gates * (d_gates - jnp.sum(gates * d_gates, -1, keepdims=True))
    d_logits = jnp.sum(picks * d_chosen[:, :, None], 1).astype(BF16)
    grad_router = dot_tn(inputs1, d_logits)

    core = lax.axis_index("dp")
    part = model_width // (nc * nd)

    def scatter_experts(grad):
        blocks = grad.reshape(EXP_DEV, nc, nd, part, -1)
        mine = cube_scatter(
            [lax.dynamic_index_in_dim(blocks, core ^ r, 2, keepdims=False) for r in range(nd)],
            "dp",
            axis_masks("dp"),
        )
        return line_scatter(
            lambda j: lax.dynamic_index_in_dim(mine, j, 1, keepdims=False), "context"
        )

    sum_gate_up = scatter_experts(grad_gate_up)
    sum_down = jnp.swapaxes(scatter_experts(grad_down), 1, 2)

    cotangent = d_out[0].astype(F32)
    scaled2 = d_expert_in * gain_second
    d_hidden = (
        cotangent
        + scale2 * scaled2
        - hidden * (scale2 * scale2 * scale2) * jnp.mean(scaled2 * hidden, -1, keepdims=True)
    )
    grad_gain_second = jnp.sum(d_expert_in * hidden * scale2, 0)
    d_attn = d_hidden.astype(BF16)
    grad_out_turned = dot_tn(d_attn, heads)
    sum_out = scatter_rows(grad_out_turned).T
    d_heads = dot_nn(d_attn, out_turned).astype(BF16)
    d_query, d_key_all, d_value_all = attend_backward(first, query, key_value, d_heads)
    d_key_value_all = jnp.concatenate([d_key_all, d_value_all], -1).reshape(nc, tokens, -1)
    d_key_value = line_scatter(
        lambda j: lax.dynamic_index_in_dim(d_key_value_all, j, 0, keepdims=False),
        "context",
        up=False,
    )
    d_rotated = rotate_back(
        jnp.concatenate([d_query, d_key_value[:, :key_width]], -1).reshape(
            tokens, -1, HEAD_DIMENSION
        ),
        cosine_values,
        sine_values,
    ).reshape(tokens, -1)
    d_qkv = jnp.concatenate([d_rotated, d_key_value[:, key_width:]], -1).astype(BF16)
    d_inputs = dot_nt(d_qkv, qkv_weight) + dot_nt(d_logits, router_weight)
    grad_gain_first = jnp.sum(d_inputs * token_rows * scale1, 0)
    grad_qkv = dot_tn(inputs1, d_qkv)
    small_grads = jnp.concatenate(
        [grad_router, grad_gain_first[:, None], grad_gain_second[:, None]], -1
    )
    small_grads = jnp.pad(small_grads, ((0, 0), (0, 128 - small_grads.shape[1])))
    sum_rows = scatter_rows(jnp.concatenate([grad_qkv, small_grads], -1))
    sum_qkv = sum_rows[:, :qkv_width]
    sum_router = sum_rows[:, qkv_width : qkv_width + expert_total]
    sum_gain_first = sum_rows[:, qkv_width + expert_total]
    sum_gain_second = sum_rows[:, qkv_width + expert_total + 1]
    scaled1 = d_inputs * gain_first
    d_input_rows = (
        d_hidden
        + scale1 * scaled1
        - token_rows
        * (scale1 * scale1 * scale1)
        * jnp.mean(scaled1 * token_rows, -1, keepdims=True)
    ).astype(BF16)
    return (
        layer_result[None],
        d_input_rows[None],
        sum_gain_first,
        sum_qkv,
        sum_out,
        sum_router,
        sum_gain_second,
        sum_gate_up,
        sum_down,
    )


def local_fused(
    layer_input,
    gain_attn,
    query_key_value_weight,
    w_out,
    w_router,
    gain_ffn,
    w_gate_up,
    w_down,
    routes,
    d_out,
):
    tokens = layer_input.shape[1]
    ne, nc, nd = sizes = tuple(lax.axis_size(a) for a in ("expert", "context", "dp"))
    expert_total = EXP_DEV * ne
    first_row = lax.axis_index("context") * tokens
    query_width = QUERY_HEADS * HEAD_DIMENSION
    key_width = KEY_VALUE_HEADS * HEAD_DIMENSION
    qkv_width = query_width + 2 * key_width

    small = jnp.concatenate([w_router, gain_attn[:, None], gain_ffn[:, None]], -1)
    small = jnp.pad(small, ((0, 0), (0, SMALL - small.shape[1])))
    cosine_values, sine_values = rope_tables(first_row + jnp.arange(tokens), HEAD_DIMENSION)
    sine_values = sine_values * jnp.where(
        jnp.arange(HEAD_DIMENSION) < HEAD_DIMENSION // 2, -1.0, 1.0
    )
    (
        wk_all,
        wq_all,
        wo_all,
        cotangent_all,
        gate_all,
        gate_columns,
        inputs1,
        query,
        key_value,
        heads,
        hidden,
        expert_in,
        gains,
    ) = front(
        (
            layer_input[0],
            query_key_value_weight,
            small,
            w_out.T,
            d_out[0],
            cosine_values,
            sine_values,
            routes[0],
        ),
        sizes,
    )
    layer_result, d_x, sum_rows, sum_out, sum_gate_up, sum_down = back(
        (
            gate_columns,
            gate_all,
            gains,
            cosine_values,
            sine_values,
            expert_in,
            cotangent_all,
            w_gate_up,
            w_down,
            layer_input[0],
            inputs1,
            query,
            key_value,
            heads,
            hidden,
            wk_all.reshape(-1, wk_all.shape[-1]),
            wq_all.reshape(-1, query_width),
            wo_all.reshape(-1, wo_all.shape[-1]),
        ),
        sizes,
    )[:6]
    return (
        layer_result[None],
        d_x[None],
        sum_rows[:, qkv_width + expert_total],
        sum_rows[:, :qkv_width],
        sum_out.T,
        sum_rows[:, qkv_width : qkv_width + expert_total],
        sum_rows[:, qkv_width + expert_total + 1],
        sum_gate_up,
        jnp.swapaxes(sum_down, 1, 2),
    )


def solution(mesh):
    in_specs = (
        P(("expert", "dp"), "context", None),
        P(("expert", "context", "dp")),
        P(("expert", "context", "dp"), None),
        P(None, ("expert", "context", "dp")),
        P(("expert", "context", "dp"), None),
        P(("expert", "context", "dp")),
        P("expert", None, None),
        P("expert", None, None),
        P(("expert", "dp"), "context", None),
        P(("expert", "dp"), "context", None),
    )
    out_specs = (
        P(("expert", "dp"), "context", None),
        P(("expert", "dp"), "context", None),
        P(("expert", "context", "dp")),
        P(("expert", "context", "dp"), None),
        P(None, ("expert", "context", "dp")),
        P(("expert", "context", "dp"), None),
        P(("expert", "context", "dp")),
        P("expert", ("context", "dp"), None),
        P("expert", None, ("context", "dp")),
    )
    sizes = tuple(mesh.shape[a] for a in ("expert", "context", "dp"))
    local = local_fused if sizes == (4, 4, 2) else local_plain
    return jax.shard_map(local, mesh=mesh, in_specs=in_specs, out_specs=out_specs, check_vma=False)
```

```python
import functools
import math

import jax
import jax.numpy as jnp
from jax import lax
from jax.experimental import pallas as pl
from jax.experimental.pallas import tpu as pltpu
from jax.sharding import PartitionSpec as P

QUERY_HEADS = 12
KEY_VALUE_HEADS = 2
HEAD_DIMENSION = 128
TOP = 4
EXP_DEV = 2

EPSILON = 1e-06
ROPE_BASE = 10000.0
MASKED = -1e30

F32 = jnp.float32
BF16 = jnp.bfloat16


def rope_tables(positions, width):
    halfway = width // 2
    fraction = jnp.arange(halfway, dtype=jnp.float32) * (2.0 / width)
    frequency = jnp.exp(-math.log(ROPE_BASE) * fraction)
    angles = positions.astype(jnp.float32)[:, None] * frequency[None, :]
    cosine_values = jnp.cos(angles)
    sine_values = jnp.sin(angles)
    return (
        jnp.concatenate([cosine_values, cosine_values], -1),
        jnp.concatenate([sine_values, sine_values], -1),
    )


def rotate_half(values, cosine_values, sine_values):
    halfway = values.shape[-1] // 2
    turned = jnp.concatenate([-values[..., halfway:], values[..., :halfway]], -1)
    return values * cosine_values[:, None, :] + turned * sine_values[:, None, :]


def rotate_back(grads, cosine_values, sine_values):
    halfway = grads.shape[-1] // 2
    scaled = grads * sine_values[:, None, :]
    turned = jnp.concatenate([scaled[..., halfway:], -scaled[..., :halfway]], -1)
    return grads * cosine_values[:, None, :] + turned


def dot_nt(a, b):
    return lax.dot_general(a, b, (((1,), (1,)), ((), ())), preferred_element_type=F32)


def dot_tn(a, b):
    return lax.dot_general(a, b, (((0,), (0,)), ((), ())), preferred_element_type=F32)


def dot_nn(a, b):
    return jnp.dot(a, b, preferred_element_type=F32)


def masked_probs(first_row, query, key):
    scores = dot_nt(query, key) * (HEAD_DIMENSION**-0.5)
    rows = first_row + lax.broadcasted_iota(jnp.int32, scores.shape, 0)
    columns = lax.broadcasted_iota(jnp.int32, scores.shape, 1)
    scores = jnp.where(columns <= rows, scores, MASKED)
    expd = jnp.exp(scores - jnp.max(scores, axis=-1, keepdims=True))
    return expd / jnp.sum(expd, axis=-1, keepdims=True)


def attend_forward_kernel(first_ref, query_ref, key_ref, value_ref, heads_ref):
    probs = masked_probs(first_ref[0], query_ref[...], key_ref[...])
    heads_ref[...] = dot_nn(probs.astype(BF16), value_ref[...]).astype(BF16)


def attend_forward(first_row, query, key_value):
    tokens, width = query.shape
    length = key_value.shape[0]
    group = QUERY_HEADS // KEY_VALUE_HEADS
    size = HEAD_DIMENSION
    return pl.pallas_call(
        attend_forward_kernel,
        grid_spec=pltpu.PrefetchScalarGridSpec(
            num_scalar_prefetch=1,
            grid=(QUERY_HEADS,),
            in_specs=[
                pl.BlockSpec((tokens, size), lambda h, s: (0, h)),
                pl.BlockSpec((length, size), lambda h, s: (0, h // group)),
                pl.BlockSpec((length, size), lambda h, s: (0, KEY_VALUE_HEADS + h // group)),
            ],
            out_specs=pl.BlockSpec((tokens, size), lambda h, s: (0, h)),
        ),
        out_shape=jax.ShapeDtypeStruct((tokens, width), BF16),
        compiler_params=pltpu.CompilerParams(vmem_limit_bytes=32 * 1024 * 1024),
        cost_estimate=pl.CostEstimate(
            flops=4 * tokens * length * width, bytes_accessed=4 * tokens * width, transcendentals=0
        ),
    )(first_row, query, key_value, key_value)


def attend_backward_kernel(
    first_ref, query_ref, key_ref, value_ref, grad_ref, d_query_ref, d_key_ref, d_value_ref
):
    query, key, value, grad = query_ref[...], key_ref[...], value_ref[...], grad_ref[...]
    probs = masked_probs(first_ref[0], query, key)
    d_probs = dot_nt(grad, value)
    inner = jnp.sum(probs * d_probs, axis=-1, keepdims=True)
    d_raw = (probs * (d_probs - inner) * (HEAD_DIMENSION**-0.5)).astype(BF16)
    d_query_ref[...] = dot_nn(d_raw, key)
    d_key = dot_tn(d_raw, query)
    d_value = dot_tn(probs.astype(BF16), grad)

    @pl.when(pl.program_id(1) == 0)
    def _():
        d_key_ref[...] = d_key
        d_value_ref[...] = d_value

    @pl.when(pl.program_id(1) > 0)
    def _():
        d_key_ref[...] += d_key
        d_value_ref[...] += d_value


def attend_backward(first_row, query, key_value, grad):
    tokens, width = query.shape
    length = key_value.shape[0]
    group = QUERY_HEADS // KEY_VALUE_HEADS
    size = HEAD_DIMENSION
    row_spec = pl.BlockSpec((tokens, size), lambda j, g, s: (0, j * group + g))
    return pl.pallas_call(
        attend_backward_kernel,
        grid_spec=pltpu.PrefetchScalarGridSpec(
            num_scalar_prefetch=1,
            grid=(KEY_VALUE_HEADS, group),
            in_specs=[
                row_spec,
                pl.BlockSpec((length, size), lambda j, g, s: (0, j)),
                pl.BlockSpec((length, size), lambda j, g, s: (0, KEY_VALUE_HEADS + j)),
                row_spec,
            ],
            out_specs=[
                row_spec,
                pl.BlockSpec((length, size), lambda j, g, s: (0, j)),
                pl.BlockSpec((length, size), lambda j, g, s: (0, j)),
            ],
        ),
        out_shape=[
            jax.ShapeDtypeStruct((tokens, width), F32),
            jax.ShapeDtypeStruct((length, KEY_VALUE_HEADS * size), F32),
            jax.ShapeDtypeStruct((length, KEY_VALUE_HEADS * size), F32),
        ],
        compiler_params=pltpu.CompilerParams(vmem_limit_bytes=32 * 1024 * 1024),
        cost_estimate=pl.CostEstimate(
            flops=10 * tokens * length * width, bytes_accessed=8 * tokens * width, transcendentals=0
        ),
    )(first_row, query, key_value, key_value, grad)


def exchange(values, axis, mask):
    size = lax.axis_size(axis)
    return lax.ppermute(values, axis, [(i, i ^ mask) for i in range(size)])


def axis_masks(axis):
    size = lax.axis_size(axis)
    masks, bit = [], 1
    while bit < size:
        masks.append(bit)
        bit *= 2
    return masks


def cube_gather(values, axis, masks):
    held = {0: values}
    for mask in masks:
        for r, block in list(held.items()):
            held[r ^ mask] = exchange(block, axis, mask)
    return [held[r] for r in range(lax.axis_size(axis))]


def cube_scatter(blocks, axis, masks):
    held = dict(enumerate(blocks))
    for mask in masks:
        kept = {}
        for r in list(held):
            if not r & mask:
                arrived = exchange(held[r ^ mask].astype(BF16), axis, mask)
                kept[r] = held[r].astype(F32) + arrived.astype(F32)
        held = kept
    return held[0]


def line_steps(values, axis, up):
    size = lax.axis_size(axis)
    pairs = [(i, i + 1) if up else (i + 1, i) for i in range(size - 1)]
    return lax.ppermute(values, axis, pairs)


def line_gather(values, axis, both=True):
    size = lax.axis_size(axis)
    me = lax.axis_index(axis)
    result = jnp.zeros((size + 1,) + values.shape, values.dtype)
    result = lax.dynamic_update_index_in_dim(result, values, me, 0)
    up = down = values
    for step in range(1, size):
        up = line_steps(up, axis, True)
        result = lax.dynamic_update_index_in_dim(
            result, up, jnp.where(me - step >= 0, me - step, size), 0
        )
        if both:
            down = line_steps(down, axis, False)
            result = lax.dynamic_update_index_in_dim(result, down, jnp.minimum(me + step, size), 0)
    return result[:size]


def line_scatter(take, axis, up=True, down=True):
    size = lax.axis_size(axis)
    me = lax.axis_index(axis)
    total = take(me).astype(F32)
    for active, sign in ((up, 1), (down, -1)):
        if not active:
            continue
        arrived = None
        for step in range(1, size):
            block = take((me + sign * (size - step)) % size).astype(F32)
            if arrived is not None:
                block = block + arrived.astype(F32)
            arrived = line_steps(block.astype(BF16), axis, sign > 0)
        total = total + arrived.astype(F32)
    return total


def gather_rows(shard):
    ne, nc, nd = (lax.axis_size(a) for a in ("expert", "context", "dp"))
    rows, width = shard.shape
    lines = line_gather(shard, "context")
    masks = axis_masks("expert")
    half = width // 256 * 128
    parts = [lines[..., :half], lines[..., half:]]
    me = lax.axis_index("expert")
    result = jnp.zeros((ne, nc, rows, width), shard.dtype)
    for start, part, order in ((0, parts[0], masks), (half, parts[1], masks[::-1])):
        for r, block in enumerate(cube_gather(part, "expert", order)):
            result = lax.dynamic_update_slice(result, block[None], (me ^ r, 0, 0, start))
    core = lax.axis_index("dp")
    whole = jnp.zeros((ne, nc, nd, rows, width), shard.dtype)
    for r, block in enumerate(cube_gather(result, "dp", axis_masks("dp"))):
        whole = lax.dynamic_update_slice(whole, block[:, :, None], (0, 0, core ^ r, 0, 0))
    return whole.reshape(-1, width)


def scatter_rows(grad):
    ne, nc, nd = (lax.axis_size(a) for a in ("expert", "context", "dp"))
    width = grad.shape[-1]
    rows = grad.shape[0] // (ne * nc * nd)
    blocks = grad.reshape(ne, nc, nd, rows, width)
    core, me = lax.axis_index("dp"), lax.axis_index("expert")
    mine = cube_scatter(
        [
            lax.dynamic_index_in_dim(blocks, core ^ r, 2, keepdims=False)
            for r in range(nd)
        ],
        "dp",
        axis_masks("dp"),
    )
    masks = axis_masks("expert")
    half = width // 256 * 128
    sums = []
    for part, order in ((mine[..., :half], masks), (mine[..., half:], masks[::-1])):
        sums.append(
            cube_scatter(
                [lax.dynamic_index_in_dim(part, me ^ r, 0, keepdims=False) for r in range(ne)],
                "expert",
                order,
            )
        )
    lines = jnp.concatenate(sums, -1)
    return line_scatter(
        lambda j: lax.dynamic_index_in_dim(lines, j, 0, keepdims=False), "context"
    )


def plane_gather(rows):
    masks = axis_masks("expert")
    half = rows.shape[-1] // 2
    left = cube_gather(rows[:, :half], "expert", masks)
    right = cube_gather(rows[:, half:], "expert", masks[::-1])
    return jnp.concatenate([jnp.concatenate(p, -1) for p in zip(left, right)], 0)


def plane_scatter(partial, tokens):
    masks = axis_masks("expert")
    size = lax.axis_size("expert")
    half = partial.shape[-1] // 2
    blocks = partial.reshape(size, tokens, -1)
    left = cube_scatter([blocks[r, :, :half] for r in range(size)], "expert", masks)
    right = cube_scatter([blocks[r, :, half:] for r in range(size)], "expert", masks[::-1])
    return jnp.concatenate([left, right], -1)


MESH = pl.DeviceIdType.MESH
MIB = 1024 * 1024
SMALL = 128
GATE_ROWS = 16


def flip(index, mask):
    bit = 1
    while bit <= mask:
        if mask & bit:
            index = index + bit - 2 * bit * lax.rem(lax.div(index, bit), 2)
        bit *= 2
    return index


class Wire:
    def __init__(self, sends, recvs):
        self.sends, self.recvs = sends, recvs
        self.n_sends = self.n_recvs = 0
        self.open = []

    def slots(self, count):
        first = self.n_recvs
        self.n_recvs += count
        return first

    def start(self, src, dst, recv, device, when=None):
        copy = pltpu.make_async_remote_copy(
            src_ref=src,
            dst_ref=dst,
            send_sem=self.sends.at[self.n_sends],
            recv_sem=self.recvs.at[recv],
            device_id=device,
            device_id_type=MESH,
        )
        self.n_sends += 1
        guard(when, copy.start)
        self.open.append((when, copy))

    def arrived(self, dst, recv, device):
        pltpu.make_async_remote_copy(
            src_ref=dst,
            dst_ref=dst,
            send_sem=self.sends.at[0],
            recv_sem=self.recvs.at[recv],
            device_id=device,
            device_id_type=MESH,
        ).wait_recv()

    def finish(self):
        for when, copy in self.open:
            guard(when, copy.wait_send)
        self.open = []


def guard(when, action):
    if when is None:
        action()
    else:
        pl.when(when)(action)


def greet(targets):
    barrier = pltpu.get_barrier_semaphore()
    for device, when in targets:
        guard(
            when,
            lambda device=device: pl.semaphore_signal(
                barrier, inc=1, device_id=device, device_id_type=MESH
            ),
        )
    count = sum(1 if when is None else when.astype(jnp.int32) for _, when in targets)
    pl.semaphore_wait(barrier, count)


def plane_ids(e):
    return {m: {"expert": flip(e, m)} for m in (1, 2, 3)}


class RowsGather:
    def __init__(self, wire, ref, e, z, c, nc, half):
        self.wire, self.ref, self.e, self.z, self.c, self.nc = wire, ref, e, z, c, nc
        self.cols = (pl.ds(0, half), pl.ds(half, ref.shape[-1] - half))
        self.line = wire.slots(nc)
        self.plane = wire.slots(nc * 6)
        self.core = wire.slots(nc)
        self.ids = plane_ids(e)

    def go(self, *steps):
        for step in steps:
            action = {"l": self.pass_on, "s": self.spread, "f": self.forward, "h": self.share, "c": self.complete}
            action[step[0]](*map(int, step[1:]))

    def shard(self, k):
        if k < 2:
            return flip(self.z, k)
        inner = (self.z > 0) & (self.z < self.nc - 1)
        return jnp.where(inner, flip(self.z, 5 - k), flip(self.z, k))

    def at(self, r, zs, half):
        return self.ref.at[flip(self.e, r), zs, self.c, :, self.cols[half]]

    def slot(self, k, r, half):
        return self.plane + k * 6 + (r - 1) * 2 + half

    def pass_on(self, k):
        wire, z, nc = self.wire, self.z, self.nc
        zs = self.shard(k)
        whole = self.ref.at[self.e, zs, self.c]
        if k:
            wire.arrived(whole, self.line + zs, {"context": zs})
        wire.start(
            whole, whole, self.line + zs, {"context": z + 1}, when=(zs <= z) & (z < nc - 1)
        )
        wire.start(whole, whole, self.line + zs, {"context": z - 1}, when=(zs >= z) & (z > 0))

    def spread(self, k):
        zs = self.shard(k)
        for half, mask in ((0, 1), (1, 2), (1, 1), (0, 2)):
            part = self.at(0, zs, half)
            self.wire.start(part, part, self.slot(k, mask, half), self.ids[mask])

    def forward(self, k):
        zs = self.shard(k)
        for half, mask in ((0, 1), (1, 2)):
            part = self.at(mask, zs, half)
            self.wire.arrived(part, self.slot(k, mask, half), self.ids[mask])
            self.wire.start(part, part, self.slot(k, 3, half), self.ids[3 - mask])

    def share(self, k):
        zs = self.shard(k)
        for r, half in ((1, 1), (2, 0), (3, 0), (3, 1)):
            self.wire.arrived(self.at(r, zs, half), self.slot(k, r, half), self.ids[r])
        part = self.ref.at[:, zs, self.c]
        self.wire.start(part, part, self.core + k, {"dp": 1 - self.c})

    def complete(self):
        for k in range(self.nc):
            zs = self.shard(k)
            self.wire.arrived(self.ref.at[:, zs, 1 - self.c], self.core + k, {"dp": 1 - self.c})


class PlaneGather:
    def __init__(self, wire, ref, e):
        self.wire, self.ref = wire, ref
        self.half = ref.shape[-1] // 2
        self.ids = plane_ids(e)
        self.first = wire.slots(6)

    def at(self, r, half):
        return self.ref.at[r, :, pl.ds(half * self.half, self.half)]

    def slot(self, r, half):
        return self.first + (r - 1) * 2 + half

    def spread(self):
        for half, mask in ((0, 1), (1, 2), (1, 1), (0, 2)):
            self.wire.start(
                self.at(0, half), self.at(mask, half), self.slot(mask, half), self.ids[mask]
            )

    def forward(self):
        for half, mask in ((0, 1), (1, 2)):
            self.wire.arrived(self.at(mask, half), self.slot(mask, half), self.ids[mask])
            self.wire.start(
                self.at(mask, half), self.at(3, half), self.slot(3, half), self.ids[3 - mask]
            )

    def near(self, r):
        half = 1 if r == 1 else 0
        self.wire.arrived(self.at(r, half), self.slot(r, half), self.ids[r])

    def far(self):
        for half in (0, 1):
            self.wire.arrived(self.at(3, half), self.slot(3, half), self.ids[3])

    def complete(self):
        self.near(1)
        self.near(2)
        self.far()


def swap_halves(values):
    return pltpu.roll(values, HEAD_DIMENSION // 2, 1)


def front_kernel(
    nc,
    experts,
    x_ref,
    qkv_shard,
    small_shard,
    wo_shard,
    cot_ref,
    cos_ref,
    sin_ref,
    routes_ref,
    wk_hbm,
    wq_hbm,
    wo_hbm,
    cot_hbm,
    gate_all,
    gate_columns,
    inputs_ref,
    query_ref,
    kv_ref,
    heads_ref,
    hidden_ref,
    expert_in_ref,
    gains_ref,
    wk_all,
    wq_all,
    wo_all,
    cot_all,
    kv_scr,
    q_scr,
    sends,
    recvs,
    out_sems,
):
    e, z, c = (lax.axis_index(a) for a in ("expert", "context", "dp"))
    size = HEAD_DIMENSION
    tokens, width = x_ref.shape
    query_width = QUERY_HEADS * size
    kv_width = 2 * KEY_VALUE_HEADS * size
    wire = Wire(sends, recvs)
    ids = plane_ids(e)
    greet(
        [(ids[m], None) for m in (1, 2, 3)]
        + [({"dp": 1 - c}, None), ({"context": z + 1}, z < nc - 1), ({"context": z - 1}, z > 0)]
    )
    wk_all[e, z, c, :, pl.ds(0, kv_width)] = qkv_shard[:, pl.ds(query_width, kv_width)]
    wk_all[e, z, c, :, pl.ds(kv_width, SMALL)] = small_shard[...]
    gather_k = RowsGather(wire, wk_all, e, z, c, nc, 256)
    gather_q = RowsGather(wire, wq_all, e, z, c, nc, 768)
    gather_o = RowsGather(wire, wo_all, e, z, c, nc, 768)
    gather_cot = PlaneGather(wire, cot_all, e)
    wq_all[e, z, c] = qkv_shard[:, pl.ds(0, query_width)]
    wo_all[e, z, c] = wo_shard[...]
    gather_k.go("l0", "s0")
    gather_q.go("l0", "s0")
    gather_o.go("l0")
    cot_all[0] = cot_ref[...]
    gather_k.go("l1", "s1")
    gather_q.go("l1", "s1")
    gather_k.go("f0", "l2", "s2")
    gather_q.go("l2", "s2")
    gather_k.go("f1", "h0", "l3", "s3")
    gather_q.go("l3", "s3")
    gather_k.go("f2", "h1", "f3")
    gather_q.go("f0")
    gather_k.go("h2")
    gather_o.go("l1")
    gather_q.go("f1")
    gather_k.go("h3", "c")
    rows = x_ref[...].astype(F32)
    scale1 = lax.rsqrt(jnp.mean(rows * rows, -1, keepdims=True) + EPSILON)

    small = wk_all[:, :, :, :, pl.ds(kv_width, SMALL)].reshape(width, SMALL)
    small = jnp.transpose(small.astype(F32))
    gain_first, gain_second = small[experts : experts + 1], small[experts + 1 : experts + 2]
    gains_ref[0:1] = gain_first
    gains_ref[1:2] = gain_second
    inputs_ref[...] = (rows * scale1 * gain_first).astype(BF16)
    kv_scr[...] = dot_nn(inputs_ref[...], wk_all[...].reshape(width, kv_width + SMALL))

    def turned(head):
        return (head * cos_ref[...] + swap_halves(head) * sin_ref[...]).astype(BF16)

    for j in range(KEY_VALUE_HEADS):
        columns = pl.ds(j * size, size)
        kv_ref[z, :, columns] = turned(kv_scr[:, columns])
    values = pl.ds(kv_width // 2, kv_width // 2)
    kv_ref[z, :, values] = kv_scr[:, values].astype(BF16)
    line = wire.slots(nc)
    wire.start(kv_ref.at[z], kv_ref.at[z], line, {"context": z + 1}, when=z < nc - 1)

    def pass_on(step):
        block = kv_ref.at[z - step]
        pl.when(z >= step)(lambda: wire.arrived(block, line + step - 1, {"context": z - 1}))
        wire.start(
            block, block, line + step, {"context": z + 1}, when=(z >= step) & (z < nc - 1)
        )

    outs = [
        pltpu.make_async_copy(source, dest, out_sems.at[n])
        for n, (source, dest) in enumerate(
            ((wk_all, wk_hbm), (wq_all, wq_hbm), (wo_all, wo_hbm), (cot_all, cot_hbm))
        )
    ]
    outs[0].start()
    for later in range(1, nc):

        def clear(later=later):
            kv_ref[z + later] = jnp.zeros(kv_ref.shape[1:], BF16)

        pl.when(z + later < nc)(clear)
    gather_q.go("f2", "h0", "f3")
    gather_o.go("s0", "l2", "s1")
    pass_on(1)
    gather_q.go("h1", "h2")
    gather_o.go("l3", "s2", "s3")
    pass_on(2)
    gather_q.go("h3", "c")
    for step in range(3, nc):
        pass_on(step)
    outs[1].start()

    @pl.loop(0, query_width // 256)
    def _(n):
        columns = pl.ds(pl.multiple_of(n * 256, 256), 256)
        q_scr[:, columns] = dot_nn(
            inputs_ref[...], wq_all[:, :, :, :, columns].reshape(width, 256)
        )

    @pl.loop(0, QUERY_HEADS)
    def _(h):
        columns = pl.ds(pl.multiple_of(h * size, size), size)
        query_ref[:, columns] = turned(q_scr[:, columns])

    logits = kv_scr[:, pl.ds(kv_width, SMALL)]
    lanes = lax.broadcasted_iota(jnp.int32, logits.shape, 1)
    named = lanes == routes_ref[:, 0:1]
    for k in range(1, TOP):
        named = named | (lanes == routes_ref[:, k : k + 1])
    logits = jnp.where(named, logits, MASKED)
    expd = jnp.exp(logits - jnp.max(logits, -1, keepdims=True))
    gates = expd / jnp.sum(expd, -1, keepdims=True)
    gate_all[0] = jnp.transpose(gates)[:GATE_ROWS]
    gate_slot = wire.slots(3)
    for r in (1, 2, 3):
        wire.start(gate_all.at[0], gate_all.at[r], gate_slot + r - 1, ids[r])
    gather_o.go("f0", "f1")

    length = nc * tokens
    group = QUERY_HEADS // KEY_VALUE_HEADS

    def attend(first, last):
        j = first // group
        key = kv_ref[:, :, pl.ds(j * size, size)].reshape(length, size)
        value = kv_ref[:, :, pl.ds(kv_width // 2 + j * size, size)].reshape(length, size)

        @pl.loop(first, last)
        def _(h):
            column = pl.multiple_of(h * size, size)
            scores = dot_nt(query_ref[:, pl.ds(column, size)], key) * (size**-0.5)
            row = z * tokens + lax.broadcasted_iota(jnp.int32, scores.shape, 0)
            place = lax.broadcasted_iota(jnp.int32, scores.shape, 1)
            scores = jnp.where(place <= row, scores, MASKED)
            expd = jnp.exp(scores - jnp.max(scores, -1, keepdims=True))
            total = jnp.sum(expd, -1, keepdims=True)
            mixed = dot_nn(expd.astype(BF16), value) / total
            heads_ref[:, pl.ds(column, size)] = mixed.astype(BF16)

    half = group // 2
    attend(0, half)
    gather_o.go("f2", "f3")
    gather_cot.spread()
    attend(half, group)
    gather_o.go("h0", "h1")
    attend(group, group + half)
    gather_o.go("h2", "h3")
    attend(group + half, QUERY_HEADS)
    gather_cot.forward()
    gather_o.go("c")
    outs[2].start()
    part = width // wo_all.shape[0]
    for block in range(wo_all.shape[0]):
        weight = wo_all[block].reshape(part, width)
        columns = pl.ds(block * part, part)
        hidden_ref[:, columns] = x_ref[:, columns].astype(F32) + dot_nt(heads_ref[...], weight)
    hidden = hidden_ref[...]
    scale2 = lax.rsqrt(jnp.mean(hidden * hidden, -1, keepdims=True) + EPSILON)
    expert_in_ref[...] = (hidden * scale2 * gains_ref[1:2]).astype(BF16)
    for r in (1, 2, 3):
        wire.arrived(gate_all.at[r], gate_slot + r - 1, ids[r])
    for r in range(gate_all.shape[0]):
        rest = jnp.zeros((SMALL - GATE_ROWS, tokens), F32)
        turned_gates = jnp.transpose(jnp.concatenate([gate_all[r], rest], 0))
        both = [
            jnp.sum(jnp.where(lanes == e * EXP_DEV + i, turned_gates, 0.0), -1, keepdims=True)
            for i in range(EXP_DEV)
        ]
        gate_columns[r] = jnp.where(lanes == 0, both[0], jnp.where(lanes == 1, both[1], 0.0))
    gather_cot.complete()
    outs[3].start()
    for copy in outs:
        copy.wait()
    wire.finish()


def front(operands, sizes):
    ne, nc, nd = sizes
    x, qkv_shard = operands[:2]
    tokens, width = x.shape
    rows, qkv_width = qkv_shard.shape
    query_width = QUERY_HEADS * HEAD_DIMENSION
    kv_width = qkv_width - query_width
    gathered = [
        ((ne, nc, nd, rows, kv_width + SMALL), BF16),
        ((ne, nc, nd, rows, query_width), BF16),
        ((ne, nc, nd, rows, width), BF16),
        ((ne, tokens, width), BF16),
    ]
    shapes = gathered + [
        ((ne, GATE_ROWS, tokens), F32),
        ((ne, tokens, SMALL), F32),
        ((tokens, width), BF16),
        ((tokens, query_width), BF16),
        ((nc, tokens, kv_width), BF16),
        ((tokens, query_width), BF16),
        ((tokens, width), F32),
        ((tokens, width), BF16),
        ((8, width), F32),
    ]
    copies = 160
    vmem = pl.BlockSpec(memory_space=pltpu.VMEM)
    anywhere = pl.BlockSpec(memory_space=pl.ANY)
    return pl.pallas_call(
        functools.partial(front_kernel, nc, EXP_DEV * ne),
        out_shape=[jax.ShapeDtypeStruct(*s) for s in shapes],
        in_specs=[vmem] * len(operands),
        out_specs=[anywhere] * 4 + [vmem] * (len(shapes) - 4),
        scratch_shapes=[pltpu.VMEM(*s) for s in gathered]
        + [
            pltpu.VMEM((tokens, kv_width + SMALL), F32),
            pltpu.VMEM((tokens, query_width), F32),
            pltpu.SemaphoreType.DMA((copies,)),
            pltpu.SemaphoreType.DMA((copies,)),
            pltpu.SemaphoreType.DMA((4,)),
        ],
        compiler_params=pltpu.CompilerParams(
            collective_id=0, has_side_effects=True, vmem_limit_bytes=56 * MIB
        ),
    )(*operands)


class PlaneScatter:
    def __init__(self, wire, land, ids):
        self.wire, self.land, self.ids, self.part = wire, land, ids, None
        self.half = land.shape[-1]
        self.first = wire.slots(6)

    def send(self, source, mask, slot):
        self.wire.start(source, self.land.at[slot], self.first + slot, self.ids[mask])

    def near(self, r):
        self.send(self.part(r, r - 1), r, r - 1)

    def far(self):
        self.send(self.part(3, 0), 1, 2)
        self.send(self.part(3, 1), 2, 3)

    def relay(self, part=None):
        for half, r in ((0, 2), (1, 1)):
            slot = 2 + half
            self.wire.arrived(self.land.at[slot], self.first + slot, self.ids[3 - r])
            mine = (part or self.part)(r, half)
            mine[...] = (mine[...].astype(F32) + self.land[slot].astype(F32)).astype(BF16)
            self.send(mine, r, 4 + half)

    def total(self, own):
        for slot, half, mask in ((0, 0, 1), (1, 1, 2), (4, 0, 2), (5, 1, 1)):
            self.wire.arrived(self.land.at[slot], self.first + slot, self.ids[mask])
            columns = pl.ds(half * self.half, self.half)
            own[:, columns] += self.land[slot].astype(F32)


class LineScatter:
    def __init__(self, wire, block, lands, z, nc, up=True):
        self.wire, self.block, self.lands, self.z, self.nc = wire, block, lands, z, nc
        self.up = up
        self.first = [wire.slots(nc - 1), wire.slots(nc - 1)]

    def arrive(self, way, index, j):
        land = self.lands[way].at[index]
        self.wire.arrived(land, self.first[way] + index, {"context": self.z})
        block = self.block(j)
        block[...] = (block[...].astype(F32) + self.lands[way][index].astype(F32)).astype(BF16)

    def move(self, way, j):
        z, nc = self.z, self.nc
        inner, index, near = ((z > 0), j - z, z + 1) if way == 0 else ((z < nc - 1), z - j, z - 1)
        wanted = (j > z) if way == 0 else (j < z)
        pl.when(wanted & inner)(lambda: self.arrive(way, index, j))
        self.wire.start(
            self.block(j),
            self.lands[way].at[index - 1],
            self.first[way] + index - 1,
            {"context": near},
            when=wanted,
        )

    def step(self, s):
        if self.up:
            self.move(0, self.nc - s)
        self.move(1, s - 1)

    def last(self):
        if self.up:
            pl.when(self.z > 0)(lambda: self.arrive(0, 0, self.z))
        pl.when(self.z < self.nc - 1)(lambda: self.arrive(1, 0, self.z))


class RowsScatter:
    def __init__(self, wire, buf, core, plane, lines, e, z, c, nc, start, width, half):
        self.wire, self.buf, self.core, self.plane = wire, buf, core, plane
        self.e, self.c = e, c
        self.all = pl.ds(start, width)
        self.cols = (pl.ds(start, half), pl.ds(start + half, width - half))
        self.ids = plane_ids(e)
        self.core_slot = wire.slots(1)
        self.first = wire.slots(6)
        rows = buf.shape[2] // nc
        self.line = LineScatter(
            wire,
            lambda j: buf.at[c, e, pl.ds(pl.multiple_of(j * rows, rows), rows), self.all],
            lines,
            z,
            nc,
        )

    def share(self):
        self.wire.start(
            self.buf.at[1 - self.c, :, :, self.all], self.core, self.core_slot, {"dp": 1 - self.c}
        )

    def at(self, r, half):
        return self.buf.at[self.c, flip(self.e, r), :, self.cols[half]]

    def send(self, r, half, mask, slot):
        self.wire.start(
            self.at(r, half), self.plane(slot, half), self.first + slot, self.ids[mask]
        )

    def merge(self, before=None):
        self.wire.arrived(self.core, self.core_slot, {"dp": 1 - self.c})
        for r in (3, 1, 2, 0):
            block = flip(self.e, r)
            part = self.buf.at[self.c, block, :, self.all]
            part[...] = (part[...].astype(F32) + self.core[block].astype(F32)).astype(BF16)
            if r == 3:
                if before is not None:
                    before()
                self.send(3, 0, 1, 2)
                self.send(3, 1, 2, 3)
            elif r:
                self.send(r, r - 1, r, r - 1)

    def add(self, r, half, slot, mask):
        land = self.plane(slot, half)
        self.wire.arrived(land, self.first + slot, self.ids[mask])
        part = self.at(r, half)
        part[...] = (part[...].astype(F32) + land[...].astype(F32)).astype(BF16)

    def relay(self):
        for half, r in ((0, 2), (1, 1)):
            self.add(r, half, 2 + half, 3 - r)
            self.send(r, half, r, 4 + half)

    def total(self):
        for slot, half, mask in ((0, 0, 1), (1, 1, 2), (4, 0, 2), (5, 1, 1)):
            self.add(0, half, slot, mask)


class ExpertLine:
    def __init__(self, wire, base, land, ins, outs, sems, z, nc):
        self.wire, self.base, self.land = wire, base, land
        self.ins, self.outs, self.sems, self.z, self.nc = ins, outs, sems, z, nc
        self.end = (z == 0) | (z == nc - 1)
        self.inner = jnp.logical_not(self.end)
        self.width = base.shape[-1] // EXP_DEV
        self.first = wire.slots((nc + 1) * EXP_DEV)
        self.sent = []

    def part(self, ref, j, i):
        return ref.at[j, :, pl.ds(i * self.width, self.width)]

    def combine(self, sources, stores, out):
        step = self.ins.shape[2]
        count = sources[0].shape[0] // step

        def loads(p):
            rows = pl.ds(p * step, step)
            return [
                pltpu.make_async_copy(
                    source.at[rows], self.ins.at[k, p % 2], self.sems.at[2 * k + p % 2]
                )
                for k, source in enumerate(sources)
            ]

        def store(p):
            pairs = stores(pl.ds(p * step, step), out.at[p % 2])
            return [
                pltpu.make_async_copy(source, dest, self.sems.at[8 + 2 * n + p % 2])
                for n, (source, dest) in enumerate(pairs)
            ]

        for copy in loads(0):
            copy.start()
        for p in range(count):
            if p + 1 < count:
                for copy in loads(p + 1):
                    copy.start()
            for copy in loads(p):
                copy.wait()
            if p > 1:
                for copy in store(p - 2):
                    copy.wait()
            total = self.ins[0, p % 2].astype(F32)
            for k in range(1, len(sources)):
                total = total + self.ins[k, p % 2].astype(F32)
            out[p % 2] = total.astype(out.dtype)
            for copy in store(p):
                copy.start()
        for p in range(max(0, count - 2), count):
            for copy in store(p):
                copy.wait()

    def copy(self, i, r, number):
        target, slot = flip(self.z, r), self.z
        if r == 3:
            target = jnp.where(self.end, flip(self.z, 1), target)
            slot = jnp.where(self.end, self.nc, slot)
        return pltpu.make_async_remote_copy(
            src_ref=self.part(self.base, flip(self.z, r), i),
            dst_ref=self.part(self.land, slot, i),
            send_sem=self.wire.sends.at[number],
            recv_sem=self.wire.recvs.at[self.first + slot * EXP_DEV + i],
            device_id={"context": target},
            device_id_type=MESH,
        )

    def send(self, i, r, when=None):
        number = len(self.sent)
        guard(when, self.copy(i, r, number).start)
        self.sent.append((when, i, r, number))

    def finish(self):
        for when, i, r, number in self.sent:
            guard(when, self.copy(i, r, number).wait_send)

    def arrived(self, slot, i):
        land = self.part(self.land, slot, i)
        self.wire.arrived(land, self.first + slot * EXP_DEV + i, {"context": self.z})

    def relay(self, i):
        mine = self.part(self.base, flip(self.z, 2), i)

        def add():
            self.arrived(self.nc, i)
            self.combine(
                [mine, self.part(self.land, self.nc, i)],
                lambda rows, low: [(low, mine.at[rows])],
                self.outs[0],
            )

        pl.when(self.inner)(add)
        self.send(i, 2, when=self.inner)

    def last(self, i, results):
        z = self.z
        sources = [self.part(self.base, z, i)]
        for r in (1, 2):
            self.arrived(flip(z, r), i)
            sources.append(self.part(self.land, flip(z, r), i))

        def stores(rows, wide):
            pairs, first = [], 0
            for result in results:
                columns = pl.ds(first, result.shape[-1])
                pairs.append((wide.at[:, columns], result.at[i, rows]))
                first += result.shape[-1]
            return pairs

        pl.when(self.end)(lambda: self.combine(sources, stores, self.outs[1]))

        def inner():
            self.arrived(flip(z, 3), i)
            self.combine(sources + [self.part(self.land, flip(z, 3), i)], stores, self.outs[1])

        pl.when(self.inner)(inner)


def back_kernel(
    nc,
    experts,
    gates_ref,
    gate_ref,
    gains_ref,
    cos_ref,
    sin_ref,
    expert_in_hbm,
    cot_hbm,
    w_gu_hbm,
    w_dn_hbm,
    x_hbm,
    inputs_hbm,
    query_hbm,
    kv_hbm,
    heads_hbm,
    hidden_hbm,
    wk_hbm,
    wq_hbm,
    o_hbm,
    layer_ref,
    d_x_ref,
    sum_q_ref,
    sum_o_ref,
    sum_gu_hbm,
    sum_dn_hbm,
    base_hbm,
    land_hbm,
    y_hbm,
    x_all,
    y_land,
    dx_land,
    core_land,
    plane_q,
    plane_k,
    lines_o,
    lines_q,
    lines_k,
    dkv_land,
    d_in_ref,
    dg_lanes,
    dg_part,
    dg_land,
    ins,
    out_low,
    out_wide,
    sends_1,
    recvs_1,
    sends_2,
    recvs_2,
    sends_e,
    recvs_e,
    hand_sends,
    hand_recvs,
    stage_sems,
    load_sems,
    sum_sems,
    y_sems,
    credits,
):
    e, z, c = (lax.axis_index(a) for a in ("expert", "context", "dp"))
    size = HEAD_DIMENSION
    blocks, tokens, width = cot_hbm.shape
    ff = w_dn_hbm.shape[1]
    query_width = QUERY_HEADS * size
    key_width = KEY_VALUE_HEADS * size
    qkv_width = query_width + 2 * key_width
    rest = wk_hbm.shape[-1]
    grad_width = base_hbm.shape[-1]
    ids = plane_ids(e)
    sibling = {"dp": 1 - c}
    wire_1, wire_2, wire_e = Wire(sends_1, recvs_1), Wire(sends_2, recvs_2), Wire(sends_e, recvs_e)
    expert = ExpertLine(
        wire_e, base_hbm, land_hbm, ins, (out_low, out_wide), sum_sems, z, nc
    )
    gather = PlaneGather(wire_1, x_all, e)
    scatter_dx = PlaneScatter(wire_1, dx_land, ids)
    scatter_y = PlaneScatter(wire_2, y_land, ids)
    dg_slot = wire_1.slots(3)

    def token_phase(w_gu, w_dn, cot_all, a_all, dgu_all, y_stage, dx_part, stage):
        scatter_dx.part = lambda r, half: dx_part.at[
            r - 1, :, pl.ds(half * width // 2, width // 2)
        ]
        sources = [(expert_in_hbm, x_all.at[0])]
        for i in range(EXP_DEV):
            sources += [(w_gu_hbm.at[i], w_gu.at[i]), (w_dn_hbm.at[i], w_dn.at[i])]
            if i == 0:
                sources += [(cot_hbm.at[0], cot_all.at[0]), (cot_hbm.at[1:], cot_all.at[1:])]
        loads = [
            pltpu.make_async_copy(source, dest, load_sems.at[n])
            for n, (source, dest) in enumerate(sources)
        ]
        for copy in loads:
            copy.start()
        greet(
            [(ids[m], None) for m in (1, 2, 3)]
            + [(sibling, None), ({"context": flip(z, 2)}, None)]
            + [({"context": z + 1}, z < nc - 1), ({"context": z - 1}, z > 0)]
        )
        loads[0].wait()
        gather.spread()
        step = 256
        wide = 512
        dg_lanes[...] = jnp.zeros_like(dg_lanes)

        def hidden_units(r, i):
            @pl.loop(0, ff // step)
            def _(f):
                column = pl.multiple_of(f * step, step)
                rows, grads = x_all[r], cot_all[r]
                gate_part = dot_nn(rows, w_gu[i, :, pl.ds(column, step)])
                up_part = dot_nn(rows, w_gu[i, :, pl.ds(ff + column, step)])
                raw = dot_nt(grads, w_dn[i, pl.ds(column, step), :])
                gate = gates_ref[r][:, i : i + 1]
                sigma = jax.nn.sigmoid(gate_part)
                silu = gate_part * sigma
                act = silu * up_part
                lanes = lax.broadcasted_iota(jnp.int32, dg_lanes.shape[1:], 1)
                dg_lanes[r] += jnp.where(
                    lanes == e * EXP_DEV + i, jnp.sum(act * raw, -1, keepdims=True), 0.0
                )
                a_all[r, :, pl.ds(i * ff + column, step)] = (act * gate).astype(BF16)
                d_act = raw * gate
                d_gate_part = d_act * up_part * sigma * (1.0 + gate_part * (1.0 - sigma))
                first = i * 2 * ff + column
                dgu_all[r, :, pl.ds(first, step)] = d_gate_part.astype(BF16)
                dgu_all[r, :, pl.ds(first + ff, step)] = (d_act * silu).astype(BF16)

        def y_copy(r):
            return pltpu.make_async_copy(y_stage.at[r % 2], y_hbm.at[r], y_sems.at[r % 2])

        def outputs(r):
            @pl.loop(0, width // wide)
            def _(n):
                columns = pl.ds(pl.multiple_of(n * wide, wide), wide)
                d_rows = dot_nt(dgu_all[r, :, pl.ds(0, 2 * ff)], w_gu[0, columns, :])
                d_rows += dot_nt(dgu_all[r, :, pl.ds(2 * ff, 2 * ff)], w_gu[1, columns, :])
                weight = w_dn[:, :, columns].reshape(EXP_DEV * ff, wide)
                y_stage[r % 2, :, columns] = dot_nn(a_all[r], weight).astype(BF16)
                if r == 0:
                    d_in_ref[:, columns] = d_rows
                else:
                    dx_part[r - 1, :, columns] = d_rows.astype(BF16)

            y_copy(r).start()
            dg_part[r] = jnp.transpose(dg_lanes[r])[:GATE_ROWS]
            if r:
                wire_1.start(dg_part.at[r], dg_land.at[r - 1], dg_slot + r - 1, ids[r])

        half_rows = width // nc // 2
        units = [(i, r) for i in range(EXP_DEV) for r in (3, 2, 1, 0)]

        def keep(u):
            i, r = units[u]
            return pltpu.make_async_copy(
                stage.at[u % 2, c], expert.part(base_hbm, flip(z, r), i), stage_sems.at[u % 2]
            )

        def hand(u):
            r = units[u][1]
            return pltpu.make_async_remote_copy(
                src_ref=stage.at[u % 2, 1 - c],
                dst_ref=core_land.at[r],
                send_sem=hand_sends.at[u],
                recv_sem=hand_recvs.at[u],
                device_id=sibling,
                device_id_type=MESH,
            )

        def weight_grads(u):
            i, r = units[u]
            columns = pl.ds(pl.multiple_of(flip(z, r) * 2 * half_rows, 2 * half_rows), 2 * half_rows)
            for first, source, grad, start, count in (
                (0, x_all, dgu_all, i * 2 * ff, 2),
                (2 * ff, cot_all, a_all, i * ff, 1),
            ):
                rows = source[:, :, columns].reshape(blocks * tokens, 2 * half_rows)

                @pl.loop(0, count)
                def _(n):
                    column = pl.multiple_of(n * ff, ff)
                    part = grad[:, :, pl.ds(pl.multiple_of(start + column, ff), ff)]
                    result = dot_tn(rows, part.reshape(blocks * tokens, ff)).astype(BF16)
                    stage[u % 2, :, :, pl.ds(pl.multiple_of(first + column, ff), ff)] = (
                        result.reshape(2, half_rows, ff)
                    )

            if u == nc:
                pl.semaphore_wait(credits.at[3], 1)
            hand(u).start()

        def settle(u):
            hand(u).wait_recv()
            r = units[u][1]
            mine = stage[u % 2, c].astype(F32) + core_land[r].astype(F32)
            stage[u % 2, c] = mine.astype(BF16)
            keep(u).start()

        def clear(u):
            keep(u).wait()
            hand(u).wait_send()
            i, r = units[u]
            if i == 0 or r == 3:
                if r in (3, 1):
                    expert.send(i, r)
                elif r == 2:
                    expert.send(i, r, when=expert.end)

        for copy in loads[1:4]:
            copy.wait()
        hidden_units(0, 0)
        for copy in loads[4:]:
            copy.wait()
        gather.forward()
        hidden_units(0, 1)
        gather.near(1)
        hidden_units(1, 0)
        gather.near(2)
        hidden_units(2, 0)
        gather.far()
        hidden_units(3, 0)
        weight_grads(0)
        weight_grads(1)
        settle(0)
        clear(0)
        weight_grads(2)
        settle(1)
        clear(1)
        weight_grads(3)
        settle(2)
        hidden_units(1, 1)
        clear(2)
        settle(3)
        pl.semaphore_signal(credits.at[3], inc=1, device_id=sibling, device_id_type=MESH)
        outputs(1)
        scatter_dx.near(1)
        hidden_units(2, 1)
        outputs(2)
        scatter_dx.near(2)
        hidden_units(3, 1)
        y_copy(1).wait()
        outputs(3)
        scatter_dx.far()
        clear(3)
        y_copy(2).wait()
        outputs(0)
        weight_grads(4)
        expert.relay(0)
        weight_grads(5)
        settle(4)
        scatter_dx.relay()
        clear(4)
        weight_grads(6)
        settle(5)
        clear(5)
        weight_grads(7)
        settle(6)
        scatter_dx.total(d_in_ref)
        for r in (1, 2):
            pl.semaphore_signal(credits.at[r], inc=1, device_id=ids[r], device_id_type=MESH)
        settle(7)
        clear(6)
        clear(7)
        y_copy(3).wait()
        y_copy(0).wait()
        wire_1.finish()
        pl.semaphore_signal(credits.at[0], inc=1, device_id=sibling, device_id_type=MESH)

    def token_rows_phase(
        weight,
        grads_o,
        grads_q,
        x_ref,
        inputs_ref,
        query_ref,
        kv_ref,
        heads_ref,
        hidden_ref,
        d_hidden_ref,
        d_attn_ref,
        d_heads_ref,
        d_all_ref,
        rows_ref,
        dkv_acc,
        dkv_ref,
        y_relay,
    ):
        cot_ref, d_inputs_ref = d_heads_ref, hidden_ref
        scatter_y.part = lambda r, half: y_hbm.at[r, :, pl.ds(half * width // 2, width // 2)]
        y_loads = [
            pltpu.make_async_copy(scatter_y.part(2 - half, half), y_relay.at[half], y_sems.at[half])
            for half in range(2)
        ]
        for copy in y_loads:
            copy.start()
        planes = grads_o.shape[1]
        part = width // planes
        sources = (
            (hidden_hbm, hidden_ref),
            (cot_hbm.at[0], cot_ref),
            (o_hbm, weight.at[:, pl.ds(0, width)]),
            (heads_hbm, heads_ref),
            (query_hbm, query_ref),
            (kv_hbm, kv_ref),
            (x_hbm, x_ref),
            (inputs_hbm, inputs_ref),
        )
        loads = [
            pltpu.make_async_copy(source, dest, load_sems.at[4 + n])
            for n, (source, dest) in enumerate(sources)
        ]
        for copy in loads:
            copy.start()
        for r in (1, 2):
            scatter_y.near(r)
        scatter_y.far()

        def rows_scatter(buf, core, plane, lines, start, count, half):
            return RowsScatter(
                wire_2,
                buf,
                core,
                plane,
                [lines.at[0], lines.at[1]],
                e,
                z,
                c,
                nc,
                start,
                count,
                half,
            )

        rows_of = part // 2
        scatter_o = rows_scatter(
            grads_o,
            x_all.at[:, pl.ds(0, rows_of)],
            lambda slot, half: dx_land.at[slot, pl.ds(0, rows_of)],
            lines_o,
            0,
            width,
            width // 2,
        )
        scatter_q = rows_scatter(
            grads_q,
            core_land.at[:, :, pl.ds(0, query_width)],
            lambda slot, half: plane_q.at[slot],
            lines_q,
            0,
            query_width,
            query_width // 2,
        )
        rest_half = rest // 256 * 128
        scatter_k = rows_scatter(
            grads_q,
            core_land.at[:, :, pl.ds(query_width, rest)],
            lambda slot, half: plane_k.at[
                slot, :, pl.ds(0, rest - rest_half if half else rest_half)
            ],
            lines_k,
            query_width,
            rest,
            rest_half,
        )
        scatter_kv = [
            LineScatter(
                wire_2,
                lambda j, h=h: dkv_ref.at[h, j],
                [dkv_land.at[h], dkv_land.at[h]],
                z,
                nc,
                up=False,
            )
            for h in range(KEY_VALUE_HEADS)
        ]

        loads[0].wait()
        loads[1].wait()
        hidden, d_in = hidden_ref[...], d_in_ref[...]
        scale2 = lax.rsqrt(jnp.mean(hidden * hidden, -1, keepdims=True) + EPSILON)
        scaled = d_in * gains_ref[1:2]
        mean = jnp.mean(scaled * hidden, -1, keepdims=True)
        d_hidden = cot_ref[...].astype(F32) + scale2 * scaled
        d_hidden = d_hidden - hidden * (scale2 * scale2 * scale2 * mean)
        d_hidden_ref[...] = d_hidden
        d_attn_ref[...] = d_hidden.astype(BF16)
        rows_ref[...] = jnp.zeros_like(rows_ref)
        rows_ref[experts + 1 : experts + 2, :] = jnp.sum(d_in * hidden * scale2, 0, keepdims=True)

        loads[2].wait()

        @pl.loop(0, query_width // 256)
        def _(n):
            columns = pl.ds(pl.multiple_of(n * 256, 256), 256)
            d_heads_ref[:, columns] = dot_nn(d_attn_ref[...], weight[:, columns]).astype(BF16)

        load_q = [
            pltpu.make_async_copy(wq_hbm, weight.at[:, pl.ds(0, query_width)], load_sems.at[0]),
            pltpu.make_async_copy(wk_hbm, weight.at[:, pl.ds(query_width, rest)], load_sems.at[1]),
        ]
        for copy in load_q:
            copy.start()
        loads[3].wait()

        def row_grads(buf, left, right, first, count, extra=None):
            @pl.loop(0, planes)
            def _(block):
                columns = pl.ds(pl.multiple_of(block * part, part), part)
                result = dot_tn(left[:, columns], right)
                if extra is not None:
                    result = result + extra(columns)
                result = result.astype(BF16).reshape(nc, 2, part // nc // 2, count)
                for half in range(2):
                    buf[half, block, :, pl.ds(first, count)] = result[:, half].reshape(
                        part // 2, count
                    )

        row_grads(grads_o, d_attn_ref, heads_ref[...], 0, width)
        pl.semaphore_wait(credits.at[0], 1)
        scatter_o.share()
        y_own = pltpu.make_async_copy(y_hbm.at[0], heads_ref, load_sems.at[2])
        y_own.start()

        length = nc * tokens
        group = QUERY_HEADS // KEY_VALUE_HEADS
        for copy in loads[4:6]:
            copy.wait()
        dkv_acc[...] = jnp.zeros_like(dkv_acc)

        def attend(j, first, last):
            key = kv_ref[:, :, pl.ds(j * size, size)].reshape(length, size)
            value = kv_ref[:, :, pl.ds(key_width + j * size, size)].reshape(length, size)

            @pl.loop(j * group + first, j * group + last)
            def _(h):
                columns = pl.ds(pl.multiple_of(h * size, size), size)
                query, grad = query_ref[:, columns], d_heads_ref[:, columns]
                probs = masked_probs(z * tokens, query, key)
                d_probs = dot_nt(grad, value)
                inner = jnp.sum(probs * d_probs, axis=-1, keepdims=True)
                d_raw = (probs * (d_probs - inner) * (size**-0.5)).astype(BF16)
                d_query = dot_nn(d_raw, key)
                d_query = d_query * cos_ref[...] - swap_halves(d_query) * sin_ref[...]
                d_all_ref[:, columns] = d_query.astype(BF16)
                dkv_acc[j, :, pl.ds(0, size)] += dot_tn(d_raw, query)
                dkv_acc[j, :, pl.ds(size, size)] += dot_tn(probs.astype(BF16), grad)

        def round_kv(j):
            for block in range(nc):
                rows = dkv_acc[j, pl.ds(block * tokens, tokens), :]
                dkv_ref[j, block] = rows.astype(BF16)

        def enter():
            pl.semaphore_wait(credits.at[1], 1)
            pl.semaphore_wait(credits.at[2], 1)

        attend(0, 0, group)
        round_kv(0)
        scatter_kv[0].step(1)
        scatter_o.merge(enter)
        for copy in y_loads:
            copy.wait()
        scatter_y.relay(lambda r, half: y_relay.at[half])
        attend(1, 0, group // 2)
        scatter_kv[0].step(2)
        attend(1, group // 2, group)
        round_kv(1)
        scatter_kv[1].step(1)
        scatter_kv[0].step(3)
        scatter_o.relay()

        for copy in loads[6:]:
            copy.wait()
        row_grads(grads_q, inputs_ref, d_all_ref[:, pl.ds(0, query_width)], 0, query_width)
        scatter_q.share()
        scatter_kv[1].step(2)
        scatter_kv[1].step(3)
        expert.send(1, 2, when=expert.end)
        expert.send(1, 1)
        y_own.wait()
        hidden_ref[...] += heads_ref[...].astype(F32)
        scatter_y.total(hidden_ref)
        layer_ref[...] = hidden_ref[...].astype(BF16)
        scatter_o.total()
        scatter_q.merge()
        for h in range(KEY_VALUE_HEADS):
            scatter_kv[h].last()

        for h in range(KEY_VALUE_HEADS):
            grad = dkv_ref[h, z, :, pl.ds(0, size)].astype(F32)
            grad = grad * cos_ref[...] - swap_halves(grad) * sin_ref[...]
            d_all_ref[:, pl.ds(query_width + h * size, size)] = grad.astype(BF16)
            d_all_ref[:, pl.ds(query_width + key_width + h * size, size)] = dkv_ref[
                h, z, :, pl.ds(size, size)
            ]

        total = dg_part[0]
        for r in (1, 2, 3):
            wire_1.arrived(dg_land.at[r - 1], dg_slot + r - 1, ids[r])
            total = total + dg_land[r - 1]
        gates = gate_ref[0]
        d_logits = gates * (total - jnp.sum(gates * total, 0, keepdims=True))
        d_logits = jnp.concatenate(
            [d_logits, jnp.zeros((SMALL - d_logits.shape[0], tokens), F32)], 0
        )
        d_all_ref[:, pl.ds(qkv_width, SMALL)] = jnp.transpose(d_logits).astype(BF16)

        for copy in load_q:
            copy.wait()

        @pl.loop(0, planes)
        def _(block):
            columns = pl.ds(pl.multiple_of(block * part, part), part)
            d_inputs_ref[:, columns] = dot_nt(d_all_ref[...], weight[columns, :])

        rows = x_ref[...].astype(F32)
        scale1 = lax.rsqrt(jnp.mean(rows * rows, -1, keepdims=True) + EPSILON)
        d_inputs = d_inputs_ref[...]
        rows_ref[experts : experts + 1, :] = jnp.sum(d_inputs * rows * scale1, 0, keepdims=True)

        def extra(columns):
            small = jnp.transpose(rows_ref[:, columns])
            return jnp.concatenate([jnp.zeros((part, rest - SMALL), F32), small], 1)

        row_grads(
            grads_q, inputs_ref, d_all_ref[:, pl.ds(query_width, rest)], query_width, rest, extra
        )
        scatter_k.share()
        expert.relay(1)
        scatter_q.relay()
        scatter_k.merge()
        scaled = d_inputs_ref[...] * gains_ref[0:1]
        rows = x_ref[...].astype(F32)
        scale1 = lax.rsqrt(jnp.mean(rows * rows, -1, keepdims=True) + EPSILON)
        mean = jnp.mean(scaled * rows, -1, keepdims=True)
        d_x = d_hidden_ref[...] + scale1 * scaled - rows * (scale1 * scale1 * scale1 * mean)
        d_x_ref[...] = d_x.astype(BF16)
        scatter_q.total()
        expert.last(0, (sum_gu_hbm, sum_dn_hbm))
        scatter_k.relay()
        scatter_o.line.step(1)
        scatter_q.line.step(1)
        scatter_k.total()
        scatter_k.line.step(1)
        for s in range(2, nc):
            for scatter in (scatter_o, scatter_q, scatter_k):
                scatter.line.step(s)
        for scatter in (scatter_o, scatter_q, scatter_k):
            scatter.line.last()
        sum_o_ref[...] = scatter_o.line.block(z)[...].astype(F32)
        sum_q_ref[...] = grads_q[c, e, pl.ds(pl.multiple_of(z * (rows_of // nc), rows_of // nc), rows_of // nc)].astype(F32)
        expert.last(1, (sum_gu_hbm, sum_dn_hbm))
        wire_2.finish()
        expert.finish()

    held = EXP_DEV
    pl.run_scoped(
        token_phase,
        pltpu.VMEM((held, width, 2 * ff), BF16),
        pltpu.VMEM((held, ff, width), BF16),
        pltpu.VMEM((blocks, tokens, width), BF16),
        pltpu.VMEM((blocks, tokens, held * ff), BF16),
        pltpu.VMEM((blocks, tokens, held * 2 * ff), BF16),
        pltpu.VMEM((2, tokens, width), BF16),
        pltpu.VMEM((blocks - 1, tokens, width), BF16),
        pltpu.VMEM((2, 2, width // nc // 2, grad_width // held), BF16),
    )
    rows_half = width // blocks // 2
    pl.run_scoped(
        token_rows_phase,
        pltpu.VMEM((width, qkv_width + SMALL), BF16),
        pltpu.VMEM((2, blocks, rows_half, width), BF16),
        pltpu.VMEM((2, blocks, rows_half, qkv_width + SMALL), BF16),
        pltpu.VMEM((tokens, width), BF16),
        pltpu.VMEM((tokens, width), BF16),
        pltpu.VMEM((tokens, query_width), BF16),
        pltpu.VMEM((nc, tokens, 2 * key_width), BF16),
        pltpu.VMEM((tokens, query_width), BF16),
        pltpu.VMEM((tokens, width), F32),
        pltpu.VMEM((tokens, width), F32),
        pltpu.VMEM((tokens, width), BF16),
        pltpu.VMEM((tokens, query_width), BF16),
        pltpu.VMEM((tokens, qkv_width + SMALL), BF16),
        pltpu.VMEM((SMALL, width), F32),
        pltpu.VMEM((KEY_VALUE_HEADS, nc * tokens, 2 * size), F32),
        pltpu.VMEM((KEY_VALUE_HEADS, nc, tokens, 2 * size), BF16),
        pltpu.VMEM((2, tokens, width // 2), BF16),
    )


def back(operands, sizes):
    ne, nc, nd = sizes
    cot, w_gu, w_dn, x = operands[6], operands[7], operands[8], operands[9]
    tokens, width = x.shape
    held, ff = w_dn.shape[0], w_dn.shape[1]
    rest = operands[15].shape[-1]
    q_width = QUERY_HEADS * HEAD_DIMENSION + rest
    rows = width // (ne * nc * nd)
    rest_half = rest // 256 * 128
    shard, grads = width // (nc * nd), held * 3 * ff
    kv_size = 2 * HEAD_DIMENSION
    shapes = [
        ((tokens, width), BF16),
        ((tokens, width), BF16),
        ((rows, q_width), F32),
        ((rows, width), F32),
        ((held, shard, 2 * ff), F32),
        ((held, shard, ff), F32),
        ((nc, shard, grads), BF16),
        ((nc + 1, shard, grads), BF16),
        ((ne, tokens, width), BF16),
    ]
    vmem = pl.BlockSpec(memory_space=pltpu.VMEM)
    anywhere = pl.BlockSpec(memory_space=pl.ANY)
    step, units = 48, nc * held
    return pl.pallas_call(
        functools.partial(back_kernel, nc, EXP_DEV * ne),
        out_shape=[jax.ShapeDtypeStruct(*s) for s in shapes],
        in_specs=[vmem] * 5 + [anywhere] * (len(operands) - 5),
        out_specs=[vmem] * 4 + [anywhere] * 5,
        scratch_shapes=[
            pltpu.VMEM((ne, tokens, width), BF16),
            pltpu.VMEM((6, tokens, width // 2), BF16),
            pltpu.VMEM((6, tokens, width // 2), BF16),
            pltpu.VMEM((nc, shard, grads // held), BF16),
            pltpu.VMEM((6, nc * rows, QUERY_HEADS * HEAD_DIMENSION // 2), BF16),
            pltpu.VMEM((6, nc * rows, rest - rest_half), BF16),
            pltpu.VMEM((2, nc - 1, rows, width), BF16),
            pltpu.VMEM((2, nc - 1, rows, QUERY_HEADS * HEAD_DIMENSION), BF16),
            pltpu.VMEM((2, nc - 1, rows, rest), BF16),
            pltpu.VMEM((KEY_VALUE_HEADS, nc - 1, tokens, kv_size), BF16),
            pltpu.VMEM((tokens, width), F32),
            pltpu.VMEM((ne, tokens, SMALL), F32),
            pltpu.VMEM((ne, GATE_ROWS, tokens), F32),
            pltpu.VMEM((ne - 1, GATE_ROWS, tokens), F32),
            pltpu.VMEM((4, 2, step, grads // held), BF16),
            pltpu.VMEM((2, step, grads // held), BF16),
            pltpu.VMEM((2, step, grads // held), F32),
            pltpu.SemaphoreType.DMA((32,)),
            pltpu.SemaphoreType.DMA((32,)),
            pltpu.SemaphoreType.DMA((64,)),
            pltpu.SemaphoreType.DMA((64,)),
            pltpu.SemaphoreType.DMA((units + held,)),
            pltpu.SemaphoreType.DMA(((nc + 1) * held,)),
            pltpu.SemaphoreType.DMA((units,)),
            pltpu.SemaphoreType.DMA((units,)),
            pltpu.SemaphoreType.DMA((2,)),
            pltpu.SemaphoreType.DMA((12,)),
            pltpu.SemaphoreType.DMA((12,)),
            pltpu.SemaphoreType.DMA((2,)),
            pltpu.SemaphoreType.REGULAR((4,)),
        ],
        compiler_params=pltpu.CompilerParams(
            collective_id=1, has_side_effects=True, vmem_limit_bytes=63 * MIB
        ),
    )(*operands)


def local_plain(
    layer_input,
    gain_attn,
    query_key_value_weight,
    w_out,
    w_router,
    gain_ffn,
    w_gate_up,
    w_down,
    routes,
    d_out,
):
    tokens = layer_input.shape[1]
    model_width = layer_input.shape[2]
    ne, nc, nd = (lax.axis_size(a) for a in ("expert", "context", "dp"))
    expert_total = EXP_DEV * ne
    ff = w_down.shape[1]
    me = lax.axis_index("expert")
    first_row = lax.axis_index("context") * tokens
    query_width = QUERY_HEADS * HEAD_DIMENSION
    key_width = KEY_VALUE_HEADS * HEAD_DIMENSION
    qkv_width = query_width + 2 * key_width

    small = jnp.concatenate([w_router, gain_attn[:, None], gain_ffn[:, None]], -1)
    small = jnp.pad(small, ((0, 0), (0, 128 - small.shape[1])))
    gathered = gather_rows(jnp.concatenate([query_key_value_weight, small], -1))
    out_turned = gather_rows(w_out.T)
    qkv_weight = gathered[:, :qkv_width]
    router_weight = gathered[:, qkv_width : qkv_width + expert_total]
    gains = gathered[:, qkv_width + expert_total : qkv_width + expert_total + 2].T.astype(F32)
    gain_first, gain_second = gains[0], gains[1]
    cotangent_all = plane_gather(d_out[0])

    token_rows = layer_input[0].astype(F32)
    scale1 = lax.rsqrt(jnp.mean(token_rows * token_rows, -1, keepdims=True) + EPSILON)
    inputs1 = (token_rows * scale1 * gain_first).astype(BF16)
    query_key_value = dot_nn(inputs1, qkv_weight)
    cosine_values, sine_values = rope_tables(first_row + jnp.arange(tokens), HEAD_DIMENSION)
    rotated = rotate_half(
        query_key_value[:, : query_width + key_width].reshape(tokens, -1, HEAD_DIMENSION),
        cosine_values,
        sine_values,
    ).reshape(tokens, -1)
    query = rotated[:, :query_width].astype(BF16)
    key_value_local = jnp.concatenate(
        [rotated[:, query_width:], query_key_value[:, query_width + key_width :]], -1
    ).astype(BF16)
    key_value = line_gather(key_value_local, "context", both=False).reshape(nc * tokens, -1)
    first = first_row.astype(jnp.int32).reshape(1)
    heads = attend_forward(first, query, key_value)

    logits = dot_nn(inputs1, router_weight)
    chosen_ids = routes[0]
    picks = (chosen_ids[:, :, None] == jnp.arange(expert_total)[None, None, :]).astype(F32)
    chosen = jnp.sum(picks * logits[:, None, :], -1)
    gates = jax.nn.softmax(chosen, axis=-1)
    gate_dense = jnp.sum(picks * gates[:, :, None], 1).T
    gate_blocks = cube_gather(gate_dense, "expert", axis_masks("expert"))
    gate_local = jnp.concatenate(
        [lax.dynamic_slice_in_dim(b, me * EXP_DEV, EXP_DEV, 0) for b in gate_blocks], 1
    )

    attn = dot_nt(heads, out_turned)
    hidden = token_rows + attn
    scale2 = lax.rsqrt(jnp.mean(hidden * hidden, -1, keepdims=True) + EPSILON)
    expert_in = (hidden * scale2 * gain_second).astype(BF16)

    rows_all = plane_gather(expert_in)
    gate_up = jnp.einsum("td,edf->etf", rows_all, w_gate_up, preferred_element_type=F32)
    gate_part, up_part = gate_up[..., :ff], gate_up[..., ff:]
    sigma = jax.nn.sigmoid(gate_part)
    silu = gate_part * sigma
    act = silu * up_part
    gate_column = gate_local[:, :, None]
    act_gated = (act * gate_column).astype(BF16)
    partial_out = jnp.einsum("etf,efd->td", act_gated, w_down, preferred_element_type=F32)
    mixture = plane_scatter(partial_out.astype(BF16), tokens)
    layer_result = (hidden + mixture).astype(BF16)

    d_act_raw = jnp.einsum("td,efd->etf", cotangent_all, w_down, preferred_element_type=F32)
    d_gates_local = jnp.sum(d_act_raw * act, -1)
    d_act = d_act_raw * gate_column
    d_gate_part = d_act * up_part * sigma * (1.0 + gate_part * (1.0 - sigma))
    d_up_part = d_act * silu
    d_gate_up = jnp.concatenate([d_gate_part, d_up_part], -1).astype(BF16)
    d_rows = jnp.einsum("etf,edf->td", d_gate_up, w_gate_up, preferred_element_type=F32)
    grad_down = jnp.einsum("td,etf->edf", cotangent_all, act_gated, preferred_element_type=F32)
    grad_gate_up = jnp.einsum("td,etf->edf", rows_all, d_gate_up, preferred_element_type=F32)

    d_expert_in = plane_scatter(d_rows.astype(BF16), tokens)
    d_gate_blocks = d_gates_local.reshape(EXP_DEV, ne, tokens)
    d_gates_dense = jnp.zeros((expert_total, tokens), F32)
    for r in range(ne):
        arrived = d_gate_blocks[:, r]
        if r:
            arrived = exchange(arrived, "expert", r)
        d_gates_dense = lax.dynamic_update_slice(d_gates_dense, arrived, ((me ^ r) * EXP_DEV, 0))
    d_gates = jnp.sum(picks * d_gates_dense.T[:, None, :], -1)
    d_chosen = gates * (d_gates - jnp.sum(gates * d_gates, -1, keepdims=True))
    d_logits = jnp.sum(picks * d_chosen[:, :, None], 1).astype(BF16)
    grad_router = dot_tn(inputs1, d_logits)

    core = lax.axis_index("dp")
    part = model_width // (nc * nd)

    def scatter_experts(grad):
        blocks = grad.reshape(EXP_DEV, nc, nd, part, -1)
        mine = cube_scatter(
            [lax.dynamic_index_in_dim(blocks, core ^ r, 2, keepdims=False) for r in range(nd)],
            "dp",
            axis_masks("dp"),
        )
        return line_scatter(
            lambda j: lax.dynamic_index_in_dim(mine, j, 1, keepdims=False), "context"
        )

    sum_gate_up = scatter_experts(grad_gate_up)
    sum_down = jnp.swapaxes(scatter_experts(grad_down), 1, 2)

    cotangent = d_out[0].astype(F32)
    scaled2 = d_expert_in * gain_second
    d_hidden = (
        cotangent
        + scale2 * scaled2
        - hidden * (scale2 * scale2 * scale2) * jnp.mean(scaled2 * hidden, -1, keepdims=True)
    )
    grad_gain_second = jnp.sum(d_expert_in * hidden * scale2, 0)
    d_attn = d_hidden.astype(BF16)
    grad_out_turned = dot_tn(d_attn, heads)
    sum_out = scatter_rows(grad_out_turned).T
    d_heads = dot_nn(d_attn, out_turned).astype(BF16)
    d_query, d_key_all, d_value_all = attend_backward(first, query, key_value, d_heads)
    d_key_value_all = jnp.concatenate([d_key_all, d_value_all], -1).reshape(nc, tokens, -1)
    d_key_value = line_scatter(
        lambda j: lax.dynamic_index_in_dim(d_key_value_all, j, 0, keepdims=False),
        "context",
        up=False,
    )
    d_rotated = rotate_back(
        jnp.concatenate([d_query, d_key_value[:, :key_width]], -1).reshape(
            tokens, -1, HEAD_DIMENSION
        ),
        cosine_values,
        sine_values,
    ).reshape(tokens, -1)
    d_qkv = jnp.concatenate([d_rotated, d_key_value[:, key_width:]], -1).astype(BF16)
    d_inputs = dot_nt(d_qkv, qkv_weight) + dot_nt(d_logits, router_weight)
    grad_gain_first = jnp.sum(d_inputs * token_rows * scale1, 0)
    grad_qkv = dot_tn(inputs1, d_qkv)
    small_grads = jnp.concatenate(
        [grad_router, grad_gain_first[:, None], grad_gain_second[:, None]], -1
    )
    small_grads = jnp.pad(small_grads, ((0, 0), (0, 128 - small_grads.shape[1])))
    sum_rows = scatter_rows(jnp.concatenate([grad_qkv, small_grads], -1))
    sum_qkv = sum_rows[:, :qkv_width]
    sum_router = sum_rows[:, qkv_width : qkv_width + expert_total]
    sum_gain_first = sum_rows[:, qkv_width + expert_total]
    sum_gain_second = sum_rows[:, qkv_width + expert_total + 1]
    scaled1 = d_inputs * gain_first
    d_input_rows = (
        d_hidden
        + scale1 * scaled1
        - token_rows
        * (scale1 * scale1 * scale1)
        * jnp.mean(scaled1 * token_rows, -1, keepdims=True)
    ).astype(BF16)
    return (
        layer_result[None],
        d_input_rows[None],
        sum_gain_first,
        sum_qkv,
        sum_out,
        sum_router,
        sum_gain_second,
        sum_gate_up,
        sum_down,
    )


def local_fused(
    layer_input,
    gain_attn,
    query_key_value_weight,
    w_out,
    w_router,
    gain_ffn,
    w_gate_up,
    w_down,
    routes,
    d_out,
):
    tokens = layer_input.shape[1]
    ne, nc, nd = sizes = tuple(lax.axis_size(a) for a in ("expert", "context", "dp"))
    expert_total = EXP_DEV * ne
    first_row = lax.axis_index("context") * tokens
    query_width = QUERY_HEADS * HEAD_DIMENSION
    key_width = KEY_VALUE_HEADS * HEAD_DIMENSION
    qkv_width = query_width + 2 * key_width

    small = jnp.concatenate([w_router, gain_attn[:, None], gain_ffn[:, None]], -1)
    small = jnp.pad(small, ((0, 0), (0, SMALL - small.shape[1])))
    cosine_values, sine_values = rope_tables(first_row + jnp.arange(tokens), HEAD_DIMENSION)
    sine_values = sine_values * jnp.where(
        jnp.arange(HEAD_DIMENSION) < HEAD_DIMENSION // 2, -1.0, 1.0
    )
    (
        wk_all,
        wq_all,
        wo_all,
        cotangent_all,
        gate_all,
        gate_columns,
        inputs1,
        query,
        key_value,
        heads,
        hidden,
        expert_in,
        gains,
    ) = front(
        (
            layer_input[0],
            query_key_value_weight,
            small,
            w_out.T,
            d_out[0],
            cosine_values,
            sine_values,
            routes[0],
        ),
        sizes,
    )
    layer_result, d_x, sum_rows, sum_out, sum_gate_up, sum_down = back(
        (
            gate_columns,
            gate_all,
            gains,
            cosine_values,
            sine_values,
            expert_in,
            cotangent_all,
            w_gate_up,
            w_down,
            layer_input[0],
            inputs1,
            query,
            key_value,
            heads,
            hidden,
            wk_all.reshape(-1, wk_all.shape[-1]),
            wq_all.reshape(-1, query_width),
            wo_all.reshape(-1, wo_all.shape[-1]),
        ),
        sizes,
    )[:6]
    return (
        layer_result[None],
        d_x[None],
        sum_rows[:, qkv_width + expert_total],
        sum_rows[:, :qkv_width],
        sum_out.T,
        sum_rows[:, qkv_width : qkv_width + expert_total],
        sum_rows[:, qkv_width + expert_total + 1],
        sum_gate_up,
        jnp.swapaxes(sum_down, 1, 2),
    )


def solution(mesh):
    in_specs = (
        P(("expert", "dp"), "context", None),
        P(("expert", "context", "dp")),
        P(("expert", "context", "dp"), None),
        P(None, ("expert", "context", "dp")),
        P(("expert", "context", "dp"), None),
        P(("expert", "context", "dp")),
        P("expert", None, None),
        P("expert", None, None),
        P(("expert", "dp"), "context", None),
        P(("expert", "dp"), "context", None),
    )
    out_specs = (
        P(("expert", "dp"), "context", None),
        P(("expert", "dp"), "context", None),
        P(("expert", "context", "dp")),
        P(("expert", "context", "dp"), None),
        P(None, ("expert", "context", "dp")),
        P(("expert", "context", "dp"), None),
        P(("expert", "context", "dp")),
        P("expert", ("context", "dp"), None),
        P("expert", None, ("context", "dp")),
    )
    sizes = tuple(mesh.shape[a] for a in ("expert", "context", "dp"))
    local = local_fused if sizes == (4, 4, 2) else local_plain
    return jax.shard_map(local, mesh=mesh, in_specs=in_specs, out_specs=out_specs, check_vma=False)
```

```python
import functools
import math

import jax
import jax.numpy as jnp
from jax import lax
from jax.experimental import pallas as pl
from jax.experimental.pallas import tpu as pltpu
from jax.sharding import PartitionSpec as P

QUERY_HEADS = 12
KEY_VALUE_HEADS = 2
HEAD_DIMENSION = 128
TOP = 4
EXP_DEV = 2

EPSILON = 1e-06
ROPE_BASE = 10000.0
MASKED = -1e30

F32 = jnp.float32
BF16 = jnp.bfloat16


def rope_tables(positions, width):
    halfway = width // 2
    fraction = jnp.arange(halfway, dtype=jnp.float32) * (2.0 / width)
    frequency = jnp.exp(-math.log(ROPE_BASE) * fraction)
    angles = positions.astype(jnp.float32)[:, None] * frequency[None, :]
    cosine_values = jnp.cos(angles)
    sine_values = jnp.sin(angles)
    return (
        jnp.concatenate([cosine_values, cosine_values], -1),
        jnp.concatenate([sine_values, sine_values], -1),
    )


def rotate_half(values, cosine_values, sine_values):
    halfway = values.shape[-1] // 2
    turned = jnp.concatenate([-values[..., halfway:], values[..., :halfway]], -1)
    return values * cosine_values[:, None, :] + turned * sine_values[:, None, :]


def rotate_back(grads, cosine_values, sine_values):
    halfway = grads.shape[-1] // 2
    scaled = grads * sine_values[:, None, :]
    turned = jnp.concatenate([scaled[..., halfway:], -scaled[..., :halfway]], -1)
    return grads * cosine_values[:, None, :] + turned


def dot_nt(a, b):
    return lax.dot_general(a, b, (((1,), (1,)), ((), ())), preferred_element_type=F32)


def dot_tn(a, b):
    return lax.dot_general(a, b, (((0,), (0,)), ((), ())), preferred_element_type=F32)


def dot_nn(a, b):
    return jnp.dot(a, b, preferred_element_type=F32)


def masked_probs(first_row, query, key):
    scores = dot_nt(query, key) * (HEAD_DIMENSION**-0.5)
    rows = first_row + lax.broadcasted_iota(jnp.int32, scores.shape, 0)
    columns = lax.broadcasted_iota(jnp.int32, scores.shape, 1)
    scores = jnp.where(columns <= rows, scores, MASKED)
    expd = jnp.exp(scores - jnp.max(scores, axis=-1, keepdims=True))
    return expd / jnp.sum(expd, axis=-1, keepdims=True)


def attend_forward_kernel(first_ref, query_ref, key_ref, value_ref, heads_ref):
    probs = masked_probs(first_ref[0], query_ref[...], key_ref[...])
    heads_ref[...] = dot_nn(probs.astype(BF16), value_ref[...]).astype(BF16)


def attend_forward(first_row, query, key_value):
    tokens, width = query.shape
    length = key_value.shape[0]
    group = QUERY_HEADS // KEY_VALUE_HEADS
    size = HEAD_DIMENSION
    return pl.pallas_call(
        attend_forward_kernel,
        grid_spec=pltpu.PrefetchScalarGridSpec(
            num_scalar_prefetch=1,
            grid=(QUERY_HEADS,),
            in_specs=[
                pl.BlockSpec((tokens, size), lambda h, s: (0, h)),
                pl.BlockSpec((length, size), lambda h, s: (0, h // group)),
                pl.BlockSpec((length, size), lambda h, s: (0, KEY_VALUE_HEADS + h // group)),
            ],
            out_specs=pl.BlockSpec((tokens, size), lambda h, s: (0, h)),
        ),
        out_shape=jax.ShapeDtypeStruct((tokens, width), BF16),
        compiler_params=pltpu.CompilerParams(vmem_limit_bytes=32 * 1024 * 1024),
        cost_estimate=pl.CostEstimate(
            flops=4 * tokens * length * width, bytes_accessed=4 * tokens * width, transcendentals=0
        ),
    )(first_row, query, key_value, key_value)


def attend_backward_kernel(
    first_ref, query_ref, key_ref, value_ref, grad_ref, d_query_ref, d_key_ref, d_value_ref
):
    query, key, value, grad = query_ref[...], key_ref[...], value_ref[...], grad_ref[...]
    probs = masked_probs(first_ref[0], query, key)
    d_probs = dot_nt(grad, value)
    inner = jnp.sum(probs * d_probs, axis=-1, keepdims=True)
    d_raw = (probs * (d_probs - inner) * (HEAD_DIMENSION**-0.5)).astype(BF16)
    d_query_ref[...] = dot_nn(d_raw, key)
    d_key = dot_tn(d_raw, query)
    d_value = dot_tn(probs.astype(BF16), grad)

    @pl.when(pl.program_id(1) == 0)
    def _():
        d_key_ref[...] = d_key
        d_value_ref[...] = d_value

    @pl.when(pl.program_id(1) > 0)
    def _():
        d_key_ref[...] += d_key
        d_value_ref[...] += d_value


def attend_backward(first_row, query, key_value, grad):
    tokens, width = query.shape
    length = key_value.shape[0]
    group = QUERY_HEADS // KEY_VALUE_HEADS
    size = HEAD_DIMENSION
    row_spec = pl.BlockSpec((tokens, size), lambda j, g, s: (0, j * group + g))
    return pl.pallas_call(
        attend_backward_kernel,
        grid_spec=pltpu.PrefetchScalarGridSpec(
            num_scalar_prefetch=1,
            grid=(KEY_VALUE_HEADS, group),
            in_specs=[
                row_spec,
                pl.BlockSpec((length, size), lambda j, g, s: (0, j)),
                pl.BlockSpec((length, size), lambda j, g, s: (0, KEY_VALUE_HEADS + j)),
                row_spec,
            ],
            out_specs=[
                row_spec,
                pl.BlockSpec((length, size), lambda j, g, s: (0, j)),
                pl.BlockSpec((length, size), lambda j, g, s: (0, j)),
            ],
        ),
        out_shape=[
            jax.ShapeDtypeStruct((tokens, width), F32),
            jax.ShapeDtypeStruct((length, KEY_VALUE_HEADS * size), F32),
            jax.ShapeDtypeStruct((length, KEY_VALUE_HEADS * size), F32),
        ],
        compiler_params=pltpu.CompilerParams(vmem_limit_bytes=32 * 1024 * 1024),
        cost_estimate=pl.CostEstimate(
            flops=10 * tokens * length * width, bytes_accessed=8 * tokens * width, transcendentals=0
        ),
    )(first_row, query, key_value, key_value, grad)


def exchange(values, axis, mask):
    size = lax.axis_size(axis)
    return lax.ppermute(values, axis, [(i, i ^ mask) for i in range(size)])


def axis_masks(axis):
    size = lax.axis_size(axis)
    masks, bit = [], 1
    while bit < size:
        masks.append(bit)
        bit *= 2
    return masks


def cube_gather(values, axis, masks):
    held = {0: values}
    for mask in masks:
        for r, block in list(held.items()):
            held[r ^ mask] = exchange(block, axis, mask)
    return [held[r] for r in range(lax.axis_size(axis))]


def cube_scatter(blocks, axis, masks):
    held = dict(enumerate(blocks))
    for mask in masks:
        kept = {}
        for r in list(held):
            if not r & mask:
                arrived = exchange(held[r ^ mask].astype(BF16), axis, mask)
                kept[r] = held[r].astype(F32) + arrived.astype(F32)
        held = kept
    return held[0]


def line_steps(values, axis, up):
    size = lax.axis_size(axis)
    pairs = [(i, i + 1) if up else (i + 1, i) for i in range(size - 1)]
    return lax.ppermute(values, axis, pairs)


def line_gather(values, axis, both=True):
    size = lax.axis_size(axis)
    me = lax.axis_index(axis)
    result = jnp.zeros((size + 1,) + values.shape, values.dtype)
    result = lax.dynamic_update_index_in_dim(result, values, me, 0)
    up = down = values
    for step in range(1, size):
        up = line_steps(up, axis, True)
        result = lax.dynamic_update_index_in_dim(
            result, up, jnp.where(me - step >= 0, me - step, size), 0
        )
        if both:
            down = line_steps(down, axis, False)
            result = lax.dynamic_update_index_in_dim(result, down, jnp.minimum(me + step, size), 0)
    return result[:size]


def line_scatter(take, axis, up=True, down=True):
    size = lax.axis_size(axis)
    me = lax.axis_index(axis)
    total = take(me).astype(F32)
    for active, sign in ((up, 1), (down, -1)):
        if not active:
            continue
        arrived = None
        for step in range(1, size):
            block = take((me + sign * (size - step)) % size).astype(F32)
            if arrived is not None:
                block = block + arrived.astype(F32)
            arrived = line_steps(block.astype(BF16), axis, sign > 0)
        total = total + arrived.astype(F32)
    return total


def gather_rows(shard):
    ne, nc, nd = (lax.axis_size(a) for a in ("expert", "context", "dp"))
    rows, width = shard.shape
    lines = line_gather(shard, "context")
    masks = axis_masks("expert")
    half = width // 256 * 128
    parts = [lines[..., :half], lines[..., half:]]
    me = lax.axis_index("expert")
    result = jnp.zeros((ne, nc, rows, width), shard.dtype)
    for start, part, order in ((0, parts[0], masks), (half, parts[1], masks[::-1])):
        for r, block in enumerate(cube_gather(part, "expert", order)):
            result = lax.dynamic_update_slice(result, block[None], (me ^ r, 0, 0, start))
    core = lax.axis_index("dp")
    whole = jnp.zeros((ne, nc, nd, rows, width), shard.dtype)
    for r, block in enumerate(cube_gather(result, "dp", axis_masks("dp"))):
        whole = lax.dynamic_update_slice(whole, block[:, :, None], (0, 0, core ^ r, 0, 0))
    return whole.reshape(-1, width)


def scatter_rows(grad):
    ne, nc, nd = (lax.axis_size(a) for a in ("expert", "context", "dp"))
    width = grad.shape[-1]
    rows = grad.shape[0] // (ne * nc * nd)
    blocks = grad.reshape(ne, nc, nd, rows, width)
    core, me = lax.axis_index("dp"), lax.axis_index("expert")
    mine = cube_scatter(
        [
            lax.dynamic_index_in_dim(blocks, core ^ r, 2, keepdims=False)
            for r in range(nd)
        ],
        "dp",
        axis_masks("dp"),
    )
    masks = axis_masks("expert")
    half = width // 256 * 128
    sums = []
    for part, order in ((mine[..., :half], masks), (mine[..., half:], masks[::-1])):
        sums.append(
            cube_scatter(
                [lax.dynamic_index_in_dim(part, me ^ r, 0, keepdims=False) for r in range(ne)],
                "expert",
                order,
            )
        )
    lines = jnp.concatenate(sums, -1)
    return line_scatter(
        lambda j: lax.dynamic_index_in_dim(lines, j, 0, keepdims=False), "context"
    )


def plane_gather(rows):
    masks = axis_masks("expert")
    half = rows.shape[-1] // 2
    left = cube_gather(rows[:, :half], "expert", masks)
    right = cube_gather(rows[:, half:], "expert", masks[::-1])
    return jnp.concatenate([jnp.concatenate(p, -1) for p in zip(left, right)], 0)


def plane_scatter(partial, tokens):
    masks = axis_masks("expert")
    size = lax.axis_size("expert")
    half = partial.shape[-1] // 2
    blocks = partial.reshape(size, tokens, -1)
    left = cube_scatter([blocks[r, :, :half] for r in range(size)], "expert", masks)
    right = cube_scatter([blocks[r, :, half:] for r in range(size)], "expert", masks[::-1])
    return jnp.concatenate([left, right], -1)


MESH = pl.DeviceIdType.MESH
MIB = 1024 * 1024
SMALL = 128
GATE_ROWS = 16


def flip(index, mask):
    bit = 1
    while bit <= mask:
        if mask & bit:
            index = index + bit - 2 * bit * lax.rem(lax.div(index, bit), 2)
        bit *= 2
    return index


class Wire:
    def __init__(self, sends, recvs):
        self.sends, self.recvs = sends, recvs
        self.n_sends = self.n_recvs = 0
        self.open = []

    def slots(self, count):
        first = self.n_recvs
        self.n_recvs += count
        return first

    def start(self, src, dst, recv, device, when=None):
        copy = pltpu.make_async_remote_copy(
            src_ref=src,
            dst_ref=dst,
            send_sem=self.sends.at[self.n_sends],
            recv_sem=self.recvs.at[recv],
            device_id=device,
            device_id_type=MESH,
        )
        self.n_sends += 1
        guard(when, copy.start)
        self.open.append((when, copy))

    def arrived(self, dst, recv, device):
        pltpu.make_async_remote_copy(
            src_ref=dst,
            dst_ref=dst,
            send_sem=self.sends.at[0],
            recv_sem=self.recvs.at[recv],
            device_id=device,
            device_id_type=MESH,
        ).wait_recv()

    def finish(self):
        for when, copy in self.open:
            guard(when, copy.wait_send)
        self.open = []


def guard(when, action):
    if when is None:
        action()
    else:
        pl.when(when)(action)


def greet(targets):
    barrier = pltpu.get_barrier_semaphore()
    for device, when in targets:
        guard(
            when,
            lambda device=device: pl.semaphore_signal(
                barrier, inc=1, device_id=device, device_id_type=MESH
            ),
        )
    count = sum(1 if when is None else when.astype(jnp.int32) for _, when in targets)
    pl.semaphore_wait(barrier, count)


def plane_ids(e):
    return {m: {"expert": flip(e, m)} for m in (1, 2, 3)}


class RowsGather:
    def __init__(self, wire, ref, e, z, c, nc, half):
        self.wire, self.ref, self.e, self.z, self.c, self.nc = wire, ref, e, z, c, nc
        self.cols = (pl.ds(0, half), pl.ds(half, ref.shape[-1] - half))
        self.line = wire.slots(nc)
        self.plane = wire.slots(nc * 6)
        self.core = wire.slots(nc)
        self.ids = plane_ids(e)

    def go(self, *steps):
        for step in steps:
            action = {"l": self.pass_on, "s": self.spread, "f": self.forward, "h": self.share, "c": self.complete}
            action[step[0]](*map(int, step[1:]))

    def shard(self, k):
        if k < 2:
            return flip(self.z, k)
        inner = (self.z > 0) & (self.z < self.nc - 1)
        return jnp.where(inner, flip(self.z, 5 - k), flip(self.z, k))

    def at(self, r, zs, half):
        return self.ref.at[flip(self.e, r), zs, self.c, :, self.cols[half]]

    def slot(self, k, r, half):
        return self.plane + k * 6 + (r - 1) * 2 + half

    def pass_on(self, k):
        wire, z, nc = self.wire, self.z, self.nc
        zs = self.shard(k)
        whole = self.ref.at[self.e, zs, self.c]
        if k:
            wire.arrived(whole, self.line + zs, {"context": zs})
        wire.start(
            whole, whole, self.line + zs, {"context": z + 1}, when=(zs <= z) & (z < nc - 1)
        )
        wire.start(whole, whole, self.line + zs, {"context": z - 1}, when=(zs >= z) & (z > 0))

    def spread(self, k):
        zs = self.shard(k)
        for half, mask in ((0, 1), (1, 2), (1, 1), (0, 2)):
            part = self.at(0, zs, half)
            self.wire.start(part, part, self.slot(k, mask, half), self.ids[mask])

    def forward(self, k):
        zs = self.shard(k)
        for half, mask in ((0, 1), (1, 2)):
            part = self.at(mask, zs, half)
            self.wire.arrived(part, self.slot(k, mask, half), self.ids[mask])
            self.wire.start(part, part, self.slot(k, 3, half), self.ids[3 - mask])

    def share(self, k):
        zs = self.shard(k)
        for r, half in ((1, 1), (2, 0), (3, 0), (3, 1)):
            self.wire.arrived(self.at(r, zs, half), self.slot(k, r, half), self.ids[r])
        part = self.ref.at[:, zs, self.c]
        self.wire.start(part, part, self.core + k, {"dp": 1 - self.c})

    def complete(self):
        for k in range(self.nc):
            zs = self.shard(k)
            self.wire.arrived(self.ref.at[:, zs, 1 - self.c], self.core + k, {"dp": 1 - self.c})


class PlaneGather:
    def __init__(self, wire, ref, e):
        self.wire, self.ref = wire, ref
        self.half = ref.shape[-1] // 2
        self.ids = plane_ids(e)
        self.first = wire.slots(6)

    def at(self, r, half):
        return self.ref.at[r, :, pl.ds(half * self.half, self.half)]

    def slot(self, r, half):
        return self.first + (r - 1) * 2 + half

    def spread(self):
        for half, mask in ((0, 1), (1, 2), (1, 1), (0, 2)):
            self.wire.start(
                self.at(0, half), self.at(mask, half), self.slot(mask, half), self.ids[mask]
            )

    def forward(self):
        for half, mask in ((0, 1), (1, 2)):
            self.wire.arrived(self.at(mask, half), self.slot(mask, half), self.ids[mask])
            self.wire.start(
                self.at(mask, half), self.at(3, half), self.slot(3, half), self.ids[3 - mask]
            )

    def near(self, r):
        half = 1 if r == 1 else 0
        self.wire.arrived(self.at(r, half), self.slot(r, half), self.ids[r])

    def far(self):
        for half in (0, 1):
            self.wire.arrived(self.at(3, half), self.slot(3, half), self.ids[3])

    def complete(self):
        self.near(1)
        self.near(2)
        self.far()


def swap_halves(values):
    return pltpu.roll(values, HEAD_DIMENSION // 2, 1)


def front_kernel(
    nc,
    experts,
    x_ref,
    qkv_shard,
    small_shard,
    wo_shard,
    cot_ref,
    cos_ref,
    sin_ref,
    routes_ref,
    wk_hbm,
    wq_hbm,
    wo_hbm,
    cot_hbm,
    gate_all,
    gate_columns,
    inputs_ref,
    query_ref,
    kv_ref,
    heads_ref,
    hidden_ref,
    expert_in_ref,
    gains_ref,
    wk_all,
    wq_all,
    wo_all,
    cot_all,
    kv_scr,
    q_scr,
    sends,
    recvs,
    out_sems,
):
    e, z, c = (lax.axis_index(a) for a in ("expert", "context", "dp"))
    size = HEAD_DIMENSION
    tokens, width = x_ref.shape
    query_width = QUERY_HEADS * size
    kv_width = 2 * KEY_VALUE_HEADS * size
    wire = Wire(sends, recvs)
    ids = plane_ids(e)
    greet(
        [(ids[m], None) for m in (1, 2, 3)]
        + [({"dp": 1 - c}, None)]
        + [({"context": z + d}, z + d < nc) for d in range(1, nc)]
        + [({"context": z - d}, z >= d) for d in range(1, nc)]
    )
    wk_all[e, z, c, :, pl.ds(0, kv_width)] = qkv_shard[:, pl.ds(query_width, kv_width)]
    wk_all[e, z, c, :, pl.ds(kv_width, SMALL)] = small_shard[...]
    gather_k = RowsGather(wire, wk_all, e, z, c, nc, 256)
    gather_q = RowsGather(wire, wq_all, e, z, c, nc, 768)
    gather_o = RowsGather(wire, wo_all, e, z, c, nc, 768)
    gather_cot = PlaneGather(wire, cot_all, e)
    wq_all[e, z, c] = qkv_shard[:, pl.ds(0, query_width)]
    wo_all[e, z, c] = wo_shard[...]
    gather_k.go("l0", "s0")
    gather_q.go("l0", "s0")
    gather_o.go("l0")
    cot_all[0] = cot_ref[...]
    gather_k.go("l1", "s1")
    gather_q.go("l1", "s1")
    gather_k.go("f0", "l2", "s2")
    gather_q.go("l2", "s2")
    gather_k.go("f1", "h0", "l3", "s3")
    gather_q.go("l3", "s3")
    gather_k.go("f2", "h1", "f3")
    gather_q.go("f0")
    gather_k.go("h2")
    gather_o.go("l1")
    gather_q.go("f1")
    gather_k.go("h3", "c")
    rows = x_ref[...].astype(F32)
    scale1 = lax.rsqrt(jnp.mean(rows * rows, -1, keepdims=True) + EPSILON)

    small = wk_all[:, :, :, :, pl.ds(kv_width, SMALL)].reshape(width, SMALL)
    small = jnp.transpose(small.astype(F32))
    gain_first, gain_second = small[experts : experts + 1], small[experts + 1 : experts + 2]
    gains_ref[0:1] = gain_first
    gains_ref[1:2] = gain_second
    inputs_ref[...] = (rows * scale1 * gain_first).astype(BF16)
    kv_scr[...] = dot_nn(inputs_ref[...], wk_all[...].reshape(width, kv_width + SMALL))

    def turned(head):
        return (head * cos_ref[...] + swap_halves(head) * sin_ref[...]).astype(BF16)

    line = wire.slots(KEY_VALUE_HEADS * nc)
    for j in range(KEY_VALUE_HEADS):
        kv_ref[j, z, :, pl.ds(0, size)] = turned(kv_scr[:, pl.ds(j * size, size)])
        value = kv_scr[:, pl.ds(kv_width // 2 + j * size, size)]
        kv_ref[j, z, :, pl.ds(size, size)] = value.astype(BF16)
        mine = kv_ref.at[j, z]
        for d in range(nc - 1, 0, -1):
            wire.start(mine, mine, line + j * nc + z, {"context": z + d}, when=z + d < nc)

    def keys_here(j):
        for d in range(1, nc):

            def wait(d=d):
                wire.arrived(kv_ref.at[j, z - d], line + j * nc + z - d, {"context": z - d})

            pl.when(z >= d)(wait)

    outs = [
        pltpu.make_async_copy(source, dest, out_sems.at[n])
        for n, (source, dest) in enumerate(
            ((wk_all, wk_hbm), (wq_all, wq_hbm), (wo_all, wo_hbm), (cot_all, cot_hbm))
        )
    ]
    outs[0].start()
    for later in range(1, nc):

        def clear(later=later):
            for j in range(KEY_VALUE_HEADS):
                kv_ref[j, z + later] = jnp.zeros(kv_ref.shape[2:], BF16)

        pl.when(z + later < nc)(clear)
    gather_q.go("f2", "h0", "f3")
    gather_o.go("s0", "l2", "s1")
    gather_q.go("h1", "h2")
    gather_o.go("l3", "s2", "s3")
    gather_q.go("h3", "c")
    outs[1].start()

    @pl.loop(0, query_width // 256)
    def _(n):
        columns = pl.ds(pl.multiple_of(n * 256, 256), 256)
        q_scr[:, columns] = dot_nn(
            inputs_ref[...], wq_all[:, :, :, :, columns].reshape(width, 256)
        )

    @pl.loop(0, QUERY_HEADS)
    def _(h):
        columns = pl.ds(pl.multiple_of(h * size, size), size)
        query_ref[:, columns] = turned(q_scr[:, columns])

    logits = kv_scr[:, pl.ds(kv_width, SMALL)]
    lanes = lax.broadcasted_iota(jnp.int32, logits.shape, 1)
    routes = jnp.concatenate(
        [routes_ref[...].astype(F32), jnp.zeros((SMALL - TOP, tokens), F32)], 0
    )
    routes = jnp.transpose(routes).astype(jnp.int32)
    named = lanes == routes[:, 0:1]
    for k in range(1, TOP):
        named = named | (lanes == routes[:, k : k + 1])
    logits = jnp.where(named, logits, MASKED)
    expd = jnp.exp(logits - jnp.max(logits, -1, keepdims=True))
    gates = expd / jnp.sum(expd, -1, keepdims=True)
    gate_all[0] = jnp.transpose(gates)[:GATE_ROWS]
    gate_slot = wire.slots(3)
    for r in (1, 2, 3):
        wire.start(gate_all.at[0], gate_all.at[r], gate_slot + r - 1, ids[r])
    gather_o.go("f0", "f1")

    length = nc * tokens
    group = QUERY_HEADS // KEY_VALUE_HEADS

    def attend(first, last):
        j = first // group
        key = kv_ref[j, :, :, pl.ds(0, size)].reshape(length, size)
        value = kv_ref[j, :, :, pl.ds(size, size)].reshape(length, size)

        @pl.loop(first, last)
        def _(h):
            column = pl.multiple_of(h * size, size)
            scores = dot_nt(query_ref[:, pl.ds(column, size)], key) * (size**-0.5)
            row = z * tokens + lax.broadcasted_iota(jnp.int32, scores.shape, 0)
            place = lax.broadcasted_iota(jnp.int32, scores.shape, 1)
            scores = jnp.where(place <= row, scores, MASKED)
            expd = jnp.exp(scores - jnp.max(scores, -1, keepdims=True))
            total = jnp.sum(expd, -1, keepdims=True)
            mixed = dot_nn(expd.astype(BF16), value) / total
            heads_ref[:, pl.ds(column, size)] = mixed.astype(BF16)

    half = group // 2
    keys_here(0)
    attend(0, half)
    gather_o.go("f2", "f3")
    gather_cot.spread()
    attend(half, group)
    gather_o.go("h0", "h1")
    keys_here(1)
    attend(group, group + half)
    gather_o.go("h2", "h3")
    attend(group + half, QUERY_HEADS)
    gather_cot.forward()
    gather_o.go("c")
    outs[2].start()
    part = width // wo_all.shape[0]
    for block in range(wo_all.shape[0]):
        weight = wo_all[block].reshape(part, width)
        columns = pl.ds(block * part, part)
        hidden_ref[:, columns] = x_ref[:, columns].astype(F32) + dot_nt(heads_ref[...], weight)
    hidden = hidden_ref[...]
    scale2 = lax.rsqrt(jnp.mean(hidden * hidden, -1, keepdims=True) + EPSILON)
    expert_in_ref[...] = (hidden * scale2 * gains_ref[1:2]).astype(BF16)
    for r in (1, 2, 3):
        wire.arrived(gate_all.at[r], gate_slot + r - 1, ids[r])
    for r in range(gate_all.shape[0]):
        rest = jnp.zeros((SMALL - GATE_ROWS, tokens), F32)
        turned_gates = jnp.transpose(jnp.concatenate([gate_all[r], rest], 0))
        both = [
            jnp.sum(jnp.where(lanes == e * EXP_DEV + i, turned_gates, 0.0), -1, keepdims=True)
            for i in range(EXP_DEV)
        ]
        gate_columns[r] = jnp.where(lanes == 0, both[0], jnp.where(lanes == 1, both[1], 0.0))
    gather_cot.complete()
    outs[3].start()
    for copy in outs:
        copy.wait()
    wire.finish()


def front(operands, sizes):
    ne, nc, nd = sizes
    x, qkv_shard = operands[:2]
    tokens, width = x.shape
    rows, qkv_width = qkv_shard.shape
    query_width = QUERY_HEADS * HEAD_DIMENSION
    kv_width = qkv_width - query_width
    gathered = [
        ((ne, nc, nd, rows, kv_width + SMALL), BF16),
        ((ne, nc, nd, rows, query_width), BF16),
        ((ne, nc, nd, rows, width), BF16),
        ((ne, tokens, width), BF16),
    ]
    shapes = gathered + [
        ((ne, GATE_ROWS, tokens), F32),
        ((ne, tokens, SMALL), F32),
        ((tokens, width), BF16),
        ((tokens, query_width), BF16),
        ((KEY_VALUE_HEADS, nc, tokens, 2 * HEAD_DIMENSION), BF16),
        ((tokens, query_width), BF16),
        ((tokens, width), F32),
        ((tokens, width), BF16),
        ((8, width), F32),
    ]
    copies = 160
    vmem = pl.BlockSpec(memory_space=pltpu.VMEM)
    anywhere = pl.BlockSpec(memory_space=pl.ANY)
    return pl.pallas_call(
        functools.partial(front_kernel, nc, EXP_DEV * ne),
        out_shape=[jax.ShapeDtypeStruct(*s) for s in shapes],
        in_specs=[vmem] * len(operands),
        out_specs=[anywhere] * 4 + [vmem] * (len(shapes) - 4),
        scratch_shapes=[pltpu.VMEM(*s) for s in gathered]
        + [
            pltpu.VMEM((tokens, kv_width + SMALL), F32),
            pltpu.VMEM((tokens, query_width), F32),
            pltpu.SemaphoreType.DMA((copies,)),
            pltpu.SemaphoreType.DMA((copies,)),
            pltpu.SemaphoreType.DMA((4,)),
        ],
        compiler_params=pltpu.CompilerParams(
            collective_id=0, has_side_effects=True, vmem_limit_bytes=56 * MIB
        ),
    )(*operands)


class PlaneScatter:
    def __init__(self, wire, land, ids):
        self.wire, self.land, self.ids, self.part = wire, land, ids, None
        self.half = land.shape[-1]
        self.first = wire.slots(6)

    def send(self, source, mask, slot):
        self.wire.start(source, self.land.at[slot], self.first + slot, self.ids[mask])

    def near(self, r):
        self.send(self.part(r, r - 1), r, r - 1)

    def far(self):
        self.send(self.part(3, 0), 1, 2)
        self.send(self.part(3, 1), 2, 3)

    def relay(self, part=None):
        for half, r in ((0, 2), (1, 1)):
            slot = 2 + half
            self.wire.arrived(self.land.at[slot], self.first + slot, self.ids[3 - r])
            mine = (part or self.part)(r, half)
            mine[...] = (mine[...].astype(F32) + self.land[slot].astype(F32)).astype(BF16)
            self.send(mine, r, 4 + half)

    def total(self, own):
        for slot, half, mask in ((0, 0, 1), (1, 1, 2), (4, 0, 2), (5, 1, 1)):
            self.wire.arrived(self.land.at[slot], self.first + slot, self.ids[mask])
            columns = pl.ds(half * self.half, self.half)
            own[:, columns] += self.land[slot].astype(F32)


class LineScatter:
    def __init__(self, wire, block, lands, z, nc, up=True):
        self.wire, self.block, self.lands, self.z, self.nc = wire, block, lands, z, nc
        self.up = up
        self.first = [wire.slots(nc - 1), wire.slots(nc - 1)]

    def arrive(self, way, index, j):
        land = self.lands[way].at[index]
        self.wire.arrived(land, self.first[way] + index, {"context": self.z})
        block = self.block(j)
        block[...] = (block[...].astype(F32) + self.lands[way][index].astype(F32)).astype(BF16)

    def move(self, way, j):
        z, nc = self.z, self.nc
        inner, index, near = ((z > 0), j - z, z + 1) if way == 0 else ((z < nc - 1), z - j, z - 1)
        wanted = (j > z) if way == 0 else (j < z)
        pl.when(wanted & inner)(lambda: self.arrive(way, index, j))
        self.wire.start(
            self.block(j),
            self.lands[way].at[index - 1],
            self.first[way] + index - 1,
            {"context": near},
            when=wanted,
        )

    def step(self, s):
        if self.up:
            self.move(0, self.nc - s)
        self.move(1, s - 1)

    def last(self):
        if self.up:
            pl.when(self.z > 0)(lambda: self.arrive(0, 0, self.z))
        pl.when(self.z < self.nc - 1)(lambda: self.arrive(1, 0, self.z))


class RowsScatter:
    def __init__(self, wire, buf, core, plane, lines, e, z, c, nc, start, width, half):
        self.wire, self.buf, self.core, self.plane = wire, buf, core, plane
        self.e, self.c = e, c
        self.all = pl.ds(start, width)
        self.cols = (pl.ds(start, half), pl.ds(start + half, width - half))
        self.ids = plane_ids(e)
        self.core_slot = wire.slots(1)
        self.first = wire.slots(6)
        rows = buf.shape[2] // nc
        self.line = LineScatter(
            wire,
            lambda j: buf.at[c, e, pl.ds(pl.multiple_of(j * rows, rows), rows), self.all],
            lines,
            z,
            nc,
        )

    def share(self):
        self.wire.start(
            self.buf.at[1 - self.c, :, :, self.all], self.core, self.core_slot, {"dp": 1 - self.c}
        )

    def at(self, r, half):
        return self.buf.at[self.c, flip(self.e, r), :, self.cols[half]]

    def send(self, r, half, mask, slot):
        self.wire.start(
            self.at(r, half), self.plane(slot, half), self.first + slot, self.ids[mask]
        )

    def merge(self, before=None):
        self.wire.arrived(self.core, self.core_slot, {"dp": 1 - self.c})
        for r in (3, 1, 2, 0):
            block = flip(self.e, r)
            part = self.buf.at[self.c, block, :, self.all]
            part[...] = (part[...].astype(F32) + self.core[block].astype(F32)).astype(BF16)
            if r == 3:
                if before is not None:
                    before()
                self.send(3, 0, 1, 2)
                self.send(3, 1, 2, 3)
            elif r:
                self.send(r, r - 1, r, r - 1)

    def add(self, r, half, slot, mask):
        land = self.plane(slot, half)
        self.wire.arrived(land, self.first + slot, self.ids[mask])
        part = self.at(r, half)
        part[...] = (part[...].astype(F32) + land[...].astype(F32)).astype(BF16)

    def relay(self):
        for half, r in ((0, 2), (1, 1)):
            self.add(r, half, 2 + half, 3 - r)
            self.send(r, half, r, 4 + half)

    def total(self):
        for slot, half, mask in ((0, 0, 1), (1, 1, 2), (4, 0, 2), (5, 1, 1)):
            self.add(0, half, slot, mask)


class ExpertLine:
    def __init__(self, wire, base, land, ins, out, sems, z, nc):
        self.wire, self.base, self.land = wire, base, land
        self.ins, self.out, self.sems, self.z, self.nc = ins, out, sems, z, nc
        self.end = (z == 0) | (z == nc - 1)
        self.inner = jnp.logical_not(self.end)
        self.width = base.shape[-1] // EXP_DEV
        self.first = wire.slots((nc + 1) * EXP_DEV)
        self.sent = []

    def part(self, ref, j, i):
        return ref.at[j, :, pl.ds(i * self.width, self.width)]

    def combine(self, sources, stores):
        out, step = self.out, self.ins.shape[2]
        count = sources[0].shape[0] // step

        def loads(p):
            rows = pl.ds(p * step, step)
            return [
                pltpu.make_async_copy(
                    source.at[rows], self.ins.at[k, p % 2], self.sems.at[2 * k + p % 2]
                )
                for k, source in enumerate(sources)
            ]

        def store(p):
            pairs = stores(pl.ds(p * step, step), out.at[p % 2])
            return [
                pltpu.make_async_copy(source, dest, self.sems.at[8 + 2 * n + p % 2])
                for n, (source, dest) in enumerate(pairs)
            ]

        for copy in loads(0):
            copy.start()
        for p in range(count):
            if p + 1 < count:
                for copy in loads(p + 1):
                    copy.start()
            for copy in loads(p):
                copy.wait()
            if p > 1:
                for copy in store(p - 2):
                    copy.wait()
            total = self.ins[0, p % 2].astype(F32)
            for k in range(1, len(sources)):
                total = total + self.ins[k, p % 2].astype(F32)
            out[p % 2] = total.astype(out.dtype)
            for copy in store(p):
                copy.start()
        for p in range(max(0, count - 2), count):
            for copy in store(p):
                copy.wait()

    def copy(self, i, r, number):
        target, slot = flip(self.z, r), self.z
        if r == 3:
            target = jnp.where(self.end, flip(self.z, 1), target)
            slot = jnp.where(self.end, self.nc, slot)
        return pltpu.make_async_remote_copy(
            src_ref=self.part(self.base, flip(self.z, r), i),
            dst_ref=self.part(self.land, slot, i),
            send_sem=self.wire.sends.at[number],
            recv_sem=self.wire.recvs.at[self.first + slot * EXP_DEV + i],
            device_id={"context": target},
            device_id_type=MESH,
        )

    def send(self, i, r, when=None):
        number = len(self.sent)
        guard(when, self.copy(i, r, number).start)
        self.sent.append((when, i, r, number))

    def finish(self):
        for when, i, r, number in self.sent:
            guard(when, self.copy(i, r, number).wait_send)

    def arrived(self, slot, i):
        land = self.part(self.land, slot, i)
        self.wire.arrived(land, self.first + slot * EXP_DEV + i, {"context": self.z})

    def relay_loads(self, i, p):
        step = self.ins.shape[2]
        rows = pl.ds(p * step, step)
        sources = (self.part(self.base, flip(self.z, 2), i), self.part(self.land, self.nc, i))
        return [
            pltpu.make_async_copy(
                source.at[rows], self.ins.at[2 * k + p // 2, p % 2], self.sems.at[4 * k + p]
            )
            for k, source in enumerate(sources)
        ]

    def relay_store(self, i, p):
        step = self.ins.shape[2]
        mine = self.part(self.base, flip(self.z, 2), i).at[pl.ds(p * step, step)]
        return pltpu.make_async_copy(self.ins.at[p // 2, p % 2], mine, self.sems.at[8 + p])

    def relay_steps(self):
        return range(self.base.shape[1] // self.ins.shape[2])

    def relay_begin(self, i):
        self.relayed = i

        def begin():
            self.arrived(self.nc, i)
            for p in self.relay_steps():
                for copy in self.relay_loads(i, p):
                    copy.start()

        pl.when(self.inner)(begin)

    def relay_add(self):
        i = self.relayed

        def add():
            for p in self.relay_steps():
                for copy in self.relay_loads(i, p):
                    copy.wait()
                a, b = (self.ins[2 * k + p // 2, p % 2].astype(F32) for k in range(2))
                self.ins[p // 2, p % 2] = (a + b).astype(BF16)
                self.relay_store(i, p).start()

        pl.when(self.inner)(add)

    def relay_send(self, i):
        def wait():
            for p in self.relay_steps():
                self.relay_store(i, p).wait()

        pl.when(self.inner)(wait)
        self.send(i, 2, when=self.inner)

    def last(self, i, results):
        z = self.z
        sources = [self.part(self.base, z, i)]
        for r in (1, 2):
            self.arrived(flip(z, r), i)
            sources.append(self.part(self.land, flip(z, r), i))

        def stores(rows, wide):
            pairs, first = [], 0
            for result in results:
                columns = pl.ds(first, result.shape[-1])
                pairs.append((wide.at[:, columns], result.at[i, rows]))
                first += result.shape[-1]
            return pairs

        pl.when(self.end)(lambda: self.combine(sources, stores))

        def inner():
            self.arrived(flip(z, 3), i)
            self.combine(sources + [self.part(self.land, flip(z, 3), i)], stores)

        pl.when(self.inner)(inner)


def back_kernel(
    nc,
    experts,
    gates_ref,
    gate_ref,
    gains_ref,
    cos_ref,
    sin_ref,
    expert_in_hbm,
    cot_hbm,
    w_gu_hbm,
    w_dn_hbm,
    x_hbm,
    inputs_hbm,
    query_hbm,
    kv_hbm,
    heads_hbm,
    hidden_hbm,
    wk_hbm,
    wq_hbm,
    o_hbm,
    layer_ref,
    d_x_ref,
    sum_q_ref,
    sum_o_ref,
    sum_gu_hbm,
    sum_dn_hbm,
    base_hbm,
    land_hbm,
    y_hbm,
    x_all,
    y_land,
    dx_land,
    core_land,
    plane_q,
    plane_k,
    lines_o,
    lines_q,
    lines_k,
    dkv_land,
    d_in_ref,
    dg_lanes,
    dg_part,
    dg_land,
    ins,
    out_wide,
    sends_1,
    recvs_1,
    sends_2,
    recvs_2,
    sends_e,
    recvs_e,
    hand_sends,
    hand_recvs,
    stage_sems,
    load_sems,
    sum_sems,
    y_sems,
    credits,
):
    e, z, c = (lax.axis_index(a) for a in ("expert", "context", "dp"))
    size = HEAD_DIMENSION
    blocks, tokens, width = cot_hbm.shape
    ff = w_dn_hbm.shape[1]
    query_width = QUERY_HEADS * size
    key_width = KEY_VALUE_HEADS * size
    qkv_width = query_width + 2 * key_width
    rest = wk_hbm.shape[-1]
    grad_width = base_hbm.shape[-1]
    ids = plane_ids(e)
    sibling = {"dp": 1 - c}
    wire_1, wire_2, wire_e = Wire(sends_1, recvs_1), Wire(sends_2, recvs_2), Wire(sends_e, recvs_e)
    expert = ExpertLine(
        wire_e, base_hbm, land_hbm, ins, out_wide, sum_sems, z, nc
    )
    gather = PlaneGather(wire_1, x_all, e)
    scatter_dx = PlaneScatter(wire_1, dx_land, ids)
    scatter_y = PlaneScatter(wire_2, y_land, ids)
    dg_slot = wire_1.slots(3)

    def token_phase(w_gu, w_dn, cot_all, a_all, dgu_all, y_stage, dx_part, stage):
        scatter_dx.part = lambda r, half: dx_part.at[
            r - 1, :, pl.ds(half * width // 2, width // 2)
        ]
        sources = [(expert_in_hbm, x_all.at[0])]
        for i in range(EXP_DEV):
            sources += [(w_gu_hbm.at[i], w_gu.at[i]), (w_dn_hbm.at[i], w_dn.at[i])]
            if i == 0:
                sources += [(cot_hbm.at[0], cot_all.at[0]), (cot_hbm.at[1:], cot_all.at[1:])]
        loads = [
            pltpu.make_async_copy(source, dest, load_sems.at[n])
            for n, (source, dest) in enumerate(sources)
        ]
        for copy in loads:
            copy.start()
        greet(
            [(ids[m], None) for m in (1, 2, 3)]
            + [(sibling, None), ({"context": flip(z, 2)}, None)]
            + [({"context": z + 1}, z < nc - 1), ({"context": z - 1}, z > 0)]
        )
        loads[0].wait()
        gather.spread()
        step = 256
        wide = 512
        dg_lanes[...] = jnp.zeros_like(dg_lanes)

        def hidden_units(r, i, count=1):
            here = pl.ds(r, count)
            flat = count * tokens

            @pl.loop(0, ff // step)
            def _(f):
                column = pl.multiple_of(f * step, step)
                rows = x_all[here].reshape(flat, width)
                grads = cot_all[here].reshape(flat, width)
                gate_part = dot_nn(rows, w_gu[i, :, pl.ds(column, step)])
                up_part = dot_nn(rows, w_gu[i, :, pl.ds(ff + column, step)])
                raw = dot_nt(grads, w_dn[i, pl.ds(column, step), :])
                gate = gates_ref[here].reshape(flat, SMALL)[:, i : i + 1]
                sigma = jax.nn.sigmoid(gate_part)
                silu = gate_part * sigma
                act = silu * up_part
                lanes = lax.broadcasted_iota(jnp.int32, (flat, SMALL), 1)
                d_gate = jnp.where(
                    lanes == e * EXP_DEV + i, jnp.sum(act * raw, -1, keepdims=True), 0.0
                )
                dg_lanes[here] += d_gate.reshape(count, tokens, SMALL)

                def put(ref, first, values):
                    values = values.astype(BF16).reshape(count, tokens, step)
                    ref[here, :, pl.ds(pl.multiple_of(first, step), step)] = values

                put(a_all, i * ff + column, act * gate)
                d_act = raw * gate
                d_gate_part = d_act * up_part * sigma * (1.0 + gate_part * (1.0 - sigma))
                put(dgu_all, i * 2 * ff + column, d_gate_part)
                put(dgu_all, i * 2 * ff + ff + column, d_act * silu)

        def y_copy(r):
            return pltpu.make_async_copy(y_stage.at[r % 2], y_hbm.at[r], y_sems.at[r % 2])

        def outputs(r, count=1):
            here = pl.ds(r, count)
            flat = count * tokens

            @pl.loop(0, width // wide)
            def _(n):
                columns = pl.ds(pl.multiple_of(n * wide, wide), wide)
                low = dgu_all[here].reshape(flat, EXP_DEV * 2 * ff)
                d_rows = dot_nt(low[:, : 2 * ff], w_gu[0, columns, :])
                d_rows += dot_nt(low[:, 2 * ff :], w_gu[1, columns, :])
                weight = w_dn[:, :, columns].reshape(EXP_DEV * ff, wide)
                out = dot_nn(a_all[here].reshape(flat, EXP_DEV * ff), weight).astype(BF16)
                for k in range(count):
                    rows = slice(k * tokens, (k + 1) * tokens)
                    y_stage[(r + k) % 2, :, columns] = out[rows]
                    if r == 0:
                        d_in_ref[:, columns] = d_rows
                    else:
                        dx_part[r + k - 1, :, columns] = d_rows[rows].astype(BF16)

            for k in range(r, r + count):
                y_copy(k).start()
                dg_part[k] = jnp.transpose(dg_lanes[k])[:GATE_ROWS]
                if k:
                    wire_1.start(dg_part.at[k], dg_land.at[k - 1], dg_slot + k - 1, ids[k])

        half_rows = width // nc // 2
        units = [(i, r) for i in range(EXP_DEV) for r in (3, 2, 1, 0)]

        def keep(u):
            i, r = units[u]
            return pltpu.make_async_copy(
                stage.at[u % 2, c], expert.part(base_hbm, flip(z, r), i), stage_sems.at[u % 2]
            )

        def hand(u):
            r = units[u][1]
            return pltpu.make_async_remote_copy(
                src_ref=stage.at[u % 2, 1 - c],
                dst_ref=core_land.at[r],
                send_sem=hand_sends.at[u],
                recv_sem=hand_recvs.at[u],
                device_id=sibling,
                device_id_type=MESH,
            )

        def weight_grads(u):
            i, r = units[u]
            columns = pl.ds(pl.multiple_of(flip(z, r) * 2 * half_rows, 2 * half_rows), 2 * half_rows)
            for first, source, grad, start, count in (
                (0, x_all, dgu_all, i * 2 * ff, 2),
                (2 * ff, cot_all, a_all, i * ff, 1),
            ):
                rows = source[:, :, columns].reshape(blocks * tokens, 2 * half_rows)

                @pl.loop(0, count)
                def _(n):
                    column = pl.multiple_of(n * ff, ff)
                    part = grad[:, :, pl.ds(pl.multiple_of(start + column, ff), ff)]
                    result = dot_tn(rows, part.reshape(blocks * tokens, ff)).astype(BF16)
                    stage[u % 2, :, :, pl.ds(pl.multiple_of(first + column, ff), ff)] = (
                        result.reshape(2, half_rows, ff)
                    )

            if u == nc:
                pl.semaphore_wait(credits.at[3], 1)
            hand(u).start()

        def settle(u):
            hand(u).wait_recv()
            r = units[u][1]
            mine = stage[u % 2, c].astype(F32) + core_land[r].astype(F32)
            stage[u % 2, c] = mine.astype(BF16)
            keep(u).start()

        def clear(u):
            keep(u).wait()
            hand(u).wait_send()
            i, r = units[u]
            if i == 0 or r == 3:
                if r in (3, 1):
                    expert.send(i, r)
                elif r == 2:
                    expert.send(i, r, when=expert.end)

        for copy in loads[1:4]:
            copy.wait()
        hidden_units(0, 0)
        for copy in loads[4:]:
            copy.wait()
        hidden_units(0, 1)
        gather.forward()
        outputs(0)
        gather.near(1)
        gather.near(2)
        hidden_units(1, 0, 2)
        gather.far()
        hidden_units(3, 0)
        weight_grads(0)
        weight_grads(1)
        settle(0)
        clear(0)
        weight_grads(2)
        settle(1)
        clear(1)
        weight_grads(3)
        settle(2)
        hidden_units(1, 1, 2)
        clear(2)
        settle(3)
        pl.semaphore_signal(credits.at[3], inc=1, device_id=sibling, device_id_type=MESH)
        y_copy(0).wait()
        outputs(1, 2)
        scatter_dx.near(1)
        scatter_dx.near(2)
        hidden_units(3, 1)
        expert.relay_begin(0)
        y_copy(1).wait()
        outputs(3)
        scatter_dx.far()
        clear(3)
        expert.relay_add()
        weight_grads(4)
        expert.relay_send(0)
        weight_grads(5)
        settle(4)
        scatter_dx.relay()
        clear(4)
        weight_grads(6)
        settle(5)
        clear(5)
        weight_grads(7)
        settle(6)
        scatter_dx.total(d_in_ref)
        for r in (1, 2):
            pl.semaphore_signal(credits.at[r], inc=1, device_id=ids[r], device_id_type=MESH)
        settle(7)
        clear(6)
        clear(7)
        y_copy(3).wait()
        y_copy(2).wait()
        wire_1.finish()
        pl.semaphore_signal(credits.at[0], inc=1, device_id=sibling, device_id_type=MESH)

    def token_rows_phase(
        weight,
        grads_o,
        grads_q,
        x_ref,
        inputs_ref,
        query_ref,
        kv_ref,
        heads_ref,
        hidden_ref,
        d_hidden_ref,
        d_attn_ref,
        d_heads_ref,
        d_all_ref,
        rows_ref,
        dkv_acc,
        dkv_ref,
        y_relay,
    ):
        cot_ref, d_inputs_ref = d_heads_ref, hidden_ref
        scatter_y.part = lambda r, half: y_hbm.at[r, :, pl.ds(half * width // 2, width // 2)]
        y_loads = [
            pltpu.make_async_copy(scatter_y.part(2 - half, half), y_relay.at[half], y_sems.at[half])
            for half in range(2)
        ]
        for copy in y_loads:
            copy.start()
        planes = grads_o.shape[1]
        part = width // planes
        sources = (
            (hidden_hbm, hidden_ref),
            (cot_hbm.at[0], cot_ref),
            (o_hbm, weight.at[:, pl.ds(0, width)]),
            (heads_hbm, heads_ref),
            (query_hbm, query_ref),
            (kv_hbm, kv_ref),
            (x_hbm, x_ref),
            (inputs_hbm, inputs_ref),
        )
        loads = [
            pltpu.make_async_copy(source, dest, load_sems.at[4 + n])
            for n, (source, dest) in enumerate(sources)
        ]
        for copy in loads:
            copy.start()
        for r in (1, 2):
            scatter_y.near(r)
        scatter_y.far()

        def rows_scatter(buf, core, plane, lines, start, count, half):
            return RowsScatter(
                wire_2,
                buf,
                core,
                plane,
                [lines.at[0], lines.at[1]],
                e,
                z,
                c,
                nc,
                start,
                count,
                half,
            )

        rows_of = part // 2
        scatter_o = rows_scatter(
            grads_o,
            x_all.at[:, pl.ds(0, rows_of)],
            lambda slot, half: dx_land.at[slot, pl.ds(0, rows_of)],
            lines_o,
            0,
            width,
            width // 2,
        )
        scatter_q = rows_scatter(
            grads_q,
            core_land.at[:, :, pl.ds(0, query_width)],
            lambda slot, half: plane_q.at[slot],
            lines_q,
            0,
            query_width,
            query_width // 2,
        )
        rest_half = rest // 256 * 128
        scatter_k = rows_scatter(
            grads_q,
            core_land.at[:, :, pl.ds(query_width, rest)],
            lambda slot, half: plane_k.at[
                slot, :, pl.ds(0, rest - rest_half if half else rest_half)
            ],
            lines_k,
            query_width,
            rest,
            rest_half,
        )
        scatter_kv = [
            LineScatter(
                wire_2,
                lambda j, h=h: dkv_ref.at[h, j],
                [dkv_land.at[h], dkv_land.at[h]],
                z,
                nc,
                up=False,
            )
            for h in range(KEY_VALUE_HEADS)
        ]

        loads[0].wait()
        loads[1].wait()
        hidden, d_in = hidden_ref[...], d_in_ref[...]
        scale2 = lax.rsqrt(jnp.mean(hidden * hidden, -1, keepdims=True) + EPSILON)
        scaled = d_in * gains_ref[1:2]
        mean = jnp.mean(scaled * hidden, -1, keepdims=True)
        d_hidden = cot_ref[...].astype(F32) + scale2 * scaled
        d_hidden = d_hidden - hidden * (scale2 * scale2 * scale2 * mean)
        d_hidden_ref[...] = d_hidden
        d_attn_ref[...] = d_hidden.astype(BF16)
        rows_ref[...] = jnp.zeros_like(rows_ref)
        rows_ref[experts + 1 : experts + 2, :] = jnp.sum(d_in * hidden * scale2, 0, keepdims=True)

        loads[2].wait()

        @pl.loop(0, query_width // 256)
        def _(n):
            columns = pl.ds(pl.multiple_of(n * 256, 256), 256)
            d_heads_ref[:, columns] = dot_nn(d_attn_ref[...], weight[:, columns]).astype(BF16)

        load_q = [
            pltpu.make_async_copy(wq_hbm, weight.at[:, pl.ds(0, query_width)], load_sems.at[0]),
            pltpu.make_async_copy(wk_hbm, weight.at[:, pl.ds(query_width, rest)], load_sems.at[1]),
        ]
        for copy in load_q:
            copy.start()
        loads[3].wait()

        def row_grads(buf, left, right, first, count, extra=None):
            @pl.loop(0, planes)
            def _(block):
                columns = pl.ds(pl.multiple_of(block * part, part), part)
                result = dot_tn(left[:, columns], right)
                if extra is not None:
                    result = result + extra(columns)
                result = result.astype(BF16).reshape(nc, 2, part // nc // 2, count)
                for half in range(2):
                    buf[half, block, :, pl.ds(first, count)] = result[:, half].reshape(
                        part // 2, count
                    )

        row_grads(grads_o, d_attn_ref, heads_ref[...], 0, width)
        pl.semaphore_wait(credits.at[0], 1)
        scatter_o.share()
        y_own = pltpu.make_async_copy(y_hbm.at[0], heads_ref, load_sems.at[2])
        y_own.start()

        length = nc * tokens
        group = QUERY_HEADS // KEY_VALUE_HEADS
        for copy in loads[4:6]:
            copy.wait()
        dkv_acc[...] = jnp.zeros_like(dkv_acc)

        def attend(j, first, last):
            key = kv_ref[j, :, :, pl.ds(0, size)].reshape(length, size)
            value = kv_ref[j, :, :, pl.ds(size, size)].reshape(length, size)

            @pl.loop(j * group + first, j * group + last)
            def _(h):
                columns = pl.ds(pl.multiple_of(h * size, size), size)
                query, grad = query_ref[:, columns], d_heads_ref[:, columns]
                probs = masked_probs(z * tokens, query, key)
                d_probs = dot_nt(grad, value)
                inner = jnp.sum(probs * d_probs, axis=-1, keepdims=True)
                d_raw = (probs * (d_probs - inner) * (size**-0.5)).astype(BF16)
                d_query = dot_nn(d_raw, key)
                d_query = d_query * cos_ref[...] - swap_halves(d_query) * sin_ref[...]
                d_all_ref[:, columns] = d_query.astype(BF16)
                dkv_acc[j, :, pl.ds(0, size)] += dot_tn(d_raw, query)
                dkv_acc[j, :, pl.ds(size, size)] += dot_tn(probs.astype(BF16), grad)

        def round_kv(j):
            for block in range(nc):
                rows = dkv_acc[j, pl.ds(block * tokens, tokens), :]
                dkv_ref[j, block] = rows.astype(BF16)

        def enter():
            pl.semaphore_wait(credits.at[1], 1)
            pl.semaphore_wait(credits.at[2], 1)

        attend(0, 0, group)
        round_kv(0)
        scatter_kv[0].step(1)
        scatter_o.merge(enter)
        for copy in y_loads:
            copy.wait()
        scatter_y.relay(lambda r, half: y_relay.at[half])
        attend(1, 0, group // 2)
        scatter_kv[0].step(2)
        attend(1, group // 2, group)
        round_kv(1)
        scatter_kv[1].step(1)
        scatter_kv[0].step(3)
        scatter_o.relay()

        for copy in loads[6:]:
            copy.wait()
        row_grads(grads_q, inputs_ref, d_all_ref[:, pl.ds(0, query_width)], 0, query_width)
        scatter_q.share()
        scatter_kv[1].step(2)
        scatter_kv[1].step(3)
        expert.send(1, 2, when=expert.end)
        expert.send(1, 1)
        expert.relay_begin(1)
        y_own.wait()
        hidden_ref[...] += heads_ref[...].astype(F32)
        scatter_y.total(hidden_ref)
        layer_ref[...] = hidden_ref[...].astype(BF16)
        scatter_o.total()
        scatter_q.merge()
        for h in range(KEY_VALUE_HEADS):
            scatter_kv[h].last()
        expert.relay_add()
        expert.relay_send(1)

        for h in range(KEY_VALUE_HEADS):
            grad = dkv_ref[h, z, :, pl.ds(0, size)].astype(F32)
            grad = grad * cos_ref[...] - swap_halves(grad) * sin_ref[...]
            d_all_ref[:, pl.ds(query_width + h * size, size)] = grad.astype(BF16)
            d_all_ref[:, pl.ds(query_width + key_width + h * size, size)] = dkv_ref[
                h, z, :, pl.ds(size, size)
            ]

        total = dg_part[0]
        for r in (1, 2, 3):
            wire_1.arrived(dg_land.at[r - 1], dg_slot + r - 1, ids[r])
            total = total + dg_land[r - 1]
        gates = gate_ref[0]
        d_logits = gates * (total - jnp.sum(gates * total, 0, keepdims=True))
        d_logits = jnp.concatenate(
            [d_logits, jnp.zeros((SMALL - d_logits.shape[0], tokens), F32)], 0
        )
        d_all_ref[:, pl.ds(qkv_width, SMALL)] = jnp.transpose(d_logits).astype(BF16)

        for copy in load_q:
            copy.wait()

        @pl.loop(0, planes)
        def _(block):
            columns = pl.ds(pl.multiple_of(block * part, part), part)
            d_inputs_ref[:, columns] = dot_nt(d_all_ref[...], weight[columns, :])

        rows = x_ref[...].astype(F32)
        scale1 = lax.rsqrt(jnp.mean(rows * rows, -1, keepdims=True) + EPSILON)
        d_inputs = d_inputs_ref[...]
        rows_ref[experts : experts + 1, :] = jnp.sum(d_inputs * rows * scale1, 0, keepdims=True)

        def extra(columns):
            small = jnp.transpose(rows_ref[:, columns])
            return jnp.concatenate([jnp.zeros((part, rest - SMALL), F32), small], 1)

        row_grads(
            grads_q, inputs_ref, d_all_ref[:, pl.ds(query_width, rest)], query_width, rest, extra
        )
        scatter_k.share()
        scatter_q.relay()
        scatter_k.merge()
        scaled = d_inputs_ref[...] * gains_ref[0:1]
        rows = x_ref[...].astype(F32)
        scale1 = lax.rsqrt(jnp.mean(rows * rows, -1, keepdims=True) + EPSILON)
        mean = jnp.mean(scaled * rows, -1, keepdims=True)
        d_x = d_hidden_ref[...] + scale1 * scaled - rows * (scale1 * scale1 * scale1 * mean)
        d_x_ref[...] = d_x.astype(BF16)
        scatter_q.total()
        expert.last(0, (sum_gu_hbm, sum_dn_hbm))
        scatter_k.relay()
        scatter_o.line.step(1)
        scatter_q.line.step(1)
        scatter_k.total()
        scatter_k.line.step(1)
        for s in range(2, nc):
            for scatter in (scatter_o, scatter_q, scatter_k):
                scatter.line.step(s)
        for scatter in (scatter_o, scatter_q, scatter_k):
            scatter.line.last()
        sum_o_ref[...] = scatter_o.line.block(z)[...].astype(F32)
        sum_q_ref[...] = grads_q[c, e, pl.ds(pl.multiple_of(z * (rows_of // nc), rows_of // nc), rows_of // nc)].astype(F32)
        expert.last(1, (sum_gu_hbm, sum_dn_hbm))
        wire_2.finish()
        expert.finish()

    held = EXP_DEV
    pl.run_scoped(
        token_phase,
        pltpu.VMEM((held, width, 2 * ff), BF16),
        pltpu.VMEM((held, ff, width), BF16),
        pltpu.VMEM((blocks, tokens, width), BF16),
        pltpu.VMEM((blocks, tokens, held * ff), BF16),
        pltpu.VMEM((blocks, tokens, held * 2 * ff), BF16),
        pltpu.VMEM((2, tokens, width), BF16),
        pltpu.VMEM((blocks - 1, tokens, width), BF16),
        pltpu.VMEM((2, 2, width // nc // 2, grad_width // held), BF16),
    )
    rows_half = width // blocks // 2
    pl.run_scoped(
        token_rows_phase,
        pltpu.VMEM((width, qkv_width + SMALL), BF16),
        pltpu.VMEM((2, blocks, rows_half, width), BF16),
        pltpu.VMEM((2, blocks, rows_half, qkv_width + SMALL), BF16),
        pltpu.VMEM((tokens, width), BF16),
        pltpu.VMEM((tokens, width), BF16),
        pltpu.VMEM((tokens, query_width), BF16),
        pltpu.VMEM((KEY_VALUE_HEADS, nc, tokens, 2 * size), BF16),
        pltpu.VMEM((tokens, query_width), BF16),
        pltpu.VMEM((tokens, width), F32),
        pltpu.VMEM((tokens, width), F32),
        pltpu.VMEM((tokens, width), BF16),
        pltpu.VMEM((tokens, query_width), BF16),
        pltpu.VMEM((tokens, qkv_width + SMALL), BF16),
        pltpu.VMEM((SMALL, width), F32),
        pltpu.VMEM((KEY_VALUE_HEADS, nc * tokens, 2 * size), F32),
        pltpu.VMEM((KEY_VALUE_HEADS, nc, tokens, 2 * size), BF16),
        pltpu.VMEM((2, tokens, width // 2), BF16),
    )


def back(operands, sizes):
    ne, nc, nd = sizes
    cot, w_gu, w_dn, x = operands[6], operands[7], operands[8], operands[9]
    tokens, width = x.shape
    held, ff = w_dn.shape[0], w_dn.shape[1]
    rest = operands[15].shape[-1]
    q_width = QUERY_HEADS * HEAD_DIMENSION + rest
    rows = width // (ne * nc * nd)
    rest_half = rest // 256 * 128
    shard, grads = width // (nc * nd), held * 3 * ff
    kv_size = 2 * HEAD_DIMENSION
    shapes = [
        ((tokens, width), BF16),
        ((tokens, width), BF16),
        ((rows, q_width), F32),
        ((rows, width), F32),
        ((held, shard, 2 * ff), F32),
        ((held, shard, ff), F32),
        ((nc, shard, grads), BF16),
        ((nc + 1, shard, grads), BF16),
        ((ne, tokens, width), BF16),
    ]
    vmem = pl.BlockSpec(memory_space=pltpu.VMEM)
    anywhere = pl.BlockSpec(memory_space=pl.ANY)
    step, units = 48, nc * held
    return pl.pallas_call(
        functools.partial(back_kernel, nc, EXP_DEV * ne),
        out_shape=[jax.ShapeDtypeStruct(*s) for s in shapes],
        in_specs=[vmem] * 5 + [anywhere] * (len(operands) - 5),
        out_specs=[vmem] * 4 + [anywhere] * 5,
        scratch_shapes=[
            pltpu.VMEM((ne, tokens, width), BF16),
            pltpu.VMEM((6, tokens, width // 2), BF16),
            pltpu.VMEM((6, tokens, width // 2), BF16),
            pltpu.VMEM((nc, shard, grads // held), BF16),
            pltpu.VMEM((6, nc * rows, QUERY_HEADS * HEAD_DIMENSION // 2), BF16),
            pltpu.VMEM((6, nc * rows, rest - rest_half), BF16),
            pltpu.VMEM((2, nc - 1, rows, width), BF16),
            pltpu.VMEM((2, nc - 1, rows, QUERY_HEADS * HEAD_DIMENSION), BF16),
            pltpu.VMEM((2, nc - 1, rows, rest), BF16),
            pltpu.VMEM((KEY_VALUE_HEADS, nc - 1, tokens, kv_size), BF16),
            pltpu.VMEM((tokens, width), F32),
            pltpu.VMEM((ne, tokens, SMALL), F32),
            pltpu.VMEM((ne, GATE_ROWS, tokens), F32),
            pltpu.VMEM((ne - 1, GATE_ROWS, tokens), F32),
            pltpu.VMEM((4, 2, step, grads // held), BF16),
            pltpu.VMEM((2, step, grads // held), F32),
            pltpu.SemaphoreType.DMA((32,)),
            pltpu.SemaphoreType.DMA((32,)),
            pltpu.SemaphoreType.DMA((64,)),
            pltpu.SemaphoreType.DMA((64,)),
            pltpu.SemaphoreType.DMA((units + held,)),
            pltpu.SemaphoreType.DMA(((nc + 1) * held,)),
            pltpu.SemaphoreType.DMA((units,)),
            pltpu.SemaphoreType.DMA((units,)),
            pltpu.SemaphoreType.DMA((2,)),
            pltpu.SemaphoreType.DMA((12,)),
            pltpu.SemaphoreType.DMA((12,)),
            pltpu.SemaphoreType.DMA((2,)),
            pltpu.SemaphoreType.REGULAR((4,)),
        ],
        compiler_params=pltpu.CompilerParams(
            collective_id=1, has_side_effects=True, vmem_limit_bytes=63 * MIB
        ),
    )(*operands)


def local_plain(
    layer_input,
    gain_attn,
    query_key_value_weight,
    w_out,
    w_router,
    gain_ffn,
    w_gate_up,
    w_down,
    routes,
    d_out,
):
    tokens = layer_input.shape[1]
    model_width = layer_input.shape[2]
    ne, nc, nd = (lax.axis_size(a) for a in ("expert", "context", "dp"))
    expert_total = EXP_DEV * ne
    ff = w_down.shape[1]
    me = lax.axis_index("expert")
    first_row = lax.axis_index("context") * tokens
    query_width = QUERY_HEADS * HEAD_DIMENSION
    key_width = KEY_VALUE_HEADS * HEAD_DIMENSION
    qkv_width = query_width + 2 * key_width

    small = jnp.concatenate([w_router, gain_attn[:, None], gain_ffn[:, None]], -1)
    small = jnp.pad(small, ((0, 0), (0, 128 - small.shape[1])))
    gathered = gather_rows(jnp.concatenate([query_key_value_weight, small], -1))
    out_turned = gather_rows(w_out.T)
    qkv_weight = gathered[:, :qkv_width]
    router_weight = gathered[:, qkv_width : qkv_width + expert_total]
    gains = gathered[:, qkv_width + expert_total : qkv_width + expert_total + 2].T.astype(F32)
    gain_first, gain_second = gains[0], gains[1]
    cotangent_all = plane_gather(d_out[0])

    token_rows = layer_input[0].astype(F32)
    scale1 = lax.rsqrt(jnp.mean(token_rows * token_rows, -1, keepdims=True) + EPSILON)
    inputs1 = (token_rows * scale1 * gain_first).astype(BF16)
    query_key_value = dot_nn(inputs1, qkv_weight)
    cosine_values, sine_values = rope_tables(first_row + jnp.arange(tokens), HEAD_DIMENSION)
    rotated = rotate_half(
        query_key_value[:, : query_width + key_width].reshape(tokens, -1, HEAD_DIMENSION),
        cosine_values,
        sine_values,
    ).reshape(tokens, -1)
    query = rotated[:, :query_width].astype(BF16)
    key_value_local = jnp.concatenate(
        [rotated[:, query_width:], query_key_value[:, query_width + key_width :]], -1
    ).astype(BF16)
    key_value = line_gather(key_value_local, "context", both=False).reshape(nc * tokens, -1)
    first = first_row.astype(jnp.int32).reshape(1)
    heads = attend_forward(first, query, key_value)

    logits = dot_nn(inputs1, router_weight)
    chosen_ids = routes[0]
    picks = (chosen_ids[:, :, None] == jnp.arange(expert_total)[None, None, :]).astype(F32)
    chosen = jnp.sum(picks * logits[:, None, :], -1)
    gates = jax.nn.softmax(chosen, axis=-1)
    gate_dense = jnp.sum(picks * gates[:, :, None], 1).T
    gate_blocks = cube_gather(gate_dense, "expert", axis_masks("expert"))
    gate_local = jnp.concatenate(
        [lax.dynamic_slice_in_dim(b, me * EXP_DEV, EXP_DEV, 0) for b in gate_blocks], 1
    )

    attn = dot_nt(heads, out_turned)
    hidden = token_rows + attn
    scale2 = lax.rsqrt(jnp.mean(hidden * hidden, -1, keepdims=True) + EPSILON)
    expert_in = (hidden * scale2 * gain_second).astype(BF16)

    rows_all = plane_gather(expert_in)
    gate_up = jnp.einsum("td,edf->etf", rows_all, w_gate_up, preferred_element_type=F32)
    gate_part, up_part = gate_up[..., :ff], gate_up[..., ff:]
    sigma = jax.nn.sigmoid(gate_part)
    silu = gate_part * sigma
    act = silu * up_part
    gate_column = gate_local[:, :, None]
    act_gated = (act * gate_column).astype(BF16)
    partial_out = jnp.einsum("etf,efd->td", act_gated, w_down, preferred_element_type=F32)
    mixture = plane_scatter(partial_out.astype(BF16), tokens)
    layer_result = (hidden + mixture).astype(BF16)

    d_act_raw = jnp.einsum("td,efd->etf", cotangent_all, w_down, preferred_element_type=F32)
    d_gates_local = jnp.sum(d_act_raw * act, -1)
    d_act = d_act_raw * gate_column
    d_gate_part = d_act * up_part * sigma * (1.0 + gate_part * (1.0 - sigma))
    d_up_part = d_act * silu
    d_gate_up = jnp.concatenate([d_gate_part, d_up_part], -1).astype(BF16)
    d_rows = jnp.einsum("etf,edf->td", d_gate_up, w_gate_up, preferred_element_type=F32)
    grad_down = jnp.einsum("td,etf->edf", cotangent_all, act_gated, preferred_element_type=F32)
    grad_gate_up = jnp.einsum("td,etf->edf", rows_all, d_gate_up, preferred_element_type=F32)

    d_expert_in = plane_scatter(d_rows.astype(BF16), tokens)
    d_gate_blocks = d_gates_local.reshape(EXP_DEV, ne, tokens)
    d_gates_dense = jnp.zeros((expert_total, tokens), F32)
    for r in range(ne):
        arrived = d_gate_blocks[:, r]
        if r:
            arrived = exchange(arrived, "expert", r)
        d_gates_dense = lax.dynamic_update_slice(d_gates_dense, arrived, ((me ^ r) * EXP_DEV, 0))
    d_gates = jnp.sum(picks * d_gates_dense.T[:, None, :], -1)
    d_chosen = gates * (d_gates - jnp.sum(gates * d_gates, -1, keepdims=True))
    d_logits = jnp.sum(picks * d_chosen[:, :, None], 1).astype(BF16)
    grad_router = dot_tn(inputs1, d_logits)

    core = lax.axis_index("dp")
    part = model_width // (nc * nd)

    def scatter_experts(grad):
        blocks = grad.reshape(EXP_DEV, nc, nd, part, -1)
        mine = cube_scatter(
            [lax.dynamic_index_in_dim(blocks, core ^ r, 2, keepdims=False) for r in range(nd)],
            "dp",
            axis_masks("dp"),
        )
        return line_scatter(
            lambda j: lax.dynamic_index_in_dim(mine, j, 1, keepdims=False), "context"
        )

    sum_gate_up = scatter_experts(grad_gate_up)
    sum_down = jnp.swapaxes(scatter_experts(grad_down), 1, 2)

    cotangent = d_out[0].astype(F32)
    scaled2 = d_expert_in * gain_second
    d_hidden = (
        cotangent
        + scale2 * scaled2
        - hidden * (scale2 * scale2 * scale2) * jnp.mean(scaled2 * hidden, -1, keepdims=True)
    )
    grad_gain_second = jnp.sum(d_expert_in * hidden * scale2, 0)
    d_attn = d_hidden.astype(BF16)
    grad_out_turned = dot_tn(d_attn, heads)
    sum_out = scatter_rows(grad_out_turned).T
    d_heads = dot_nn(d_attn, out_turned).astype(BF16)
    d_query, d_key_all, d_value_all = attend_backward(first, query, key_value, d_heads)
    d_key_value_all = jnp.concatenate([d_key_all, d_value_all], -1).reshape(nc, tokens, -1)
    d_key_value = line_scatter(
        lambda j: lax.dynamic_index_in_dim(d_key_value_all, j, 0, keepdims=False),
        "context",
        up=False,
    )
    d_rotated = rotate_back(
        jnp.concatenate([d_query, d_key_value[:, :key_width]], -1).reshape(
            tokens, -1, HEAD_DIMENSION
        ),
        cosine_values,
        sine_values,
    ).reshape(tokens, -1)
    d_qkv = jnp.concatenate([d_rotated, d_key_value[:, key_width:]], -1).astype(BF16)
    d_inputs = dot_nt(d_qkv, qkv_weight) + dot_nt(d_logits, router_weight)
    grad_gain_first = jnp.sum(d_inputs * token_rows * scale1, 0)
    grad_qkv = dot_tn(inputs1, d_qkv)
    small_grads = jnp.concatenate(
        [grad_router, grad_gain_first[:, None], grad_gain_second[:, None]], -1
    )
    small_grads = jnp.pad(small_grads, ((0, 0), (0, 128 - small_grads.shape[1])))
    sum_rows = scatter_rows(jnp.concatenate([grad_qkv, small_grads], -1))
    sum_qkv = sum_rows[:, :qkv_width]
    sum_router = sum_rows[:, qkv_width : qkv_width + expert_total]
    sum_gain_first = sum_rows[:, qkv_width + expert_total]
    sum_gain_second = sum_rows[:, qkv_width + expert_total + 1]
    scaled1 = d_inputs * gain_first
    d_input_rows = (
        d_hidden
        + scale1 * scaled1
        - token_rows
        * (scale1 * scale1 * scale1)
        * jnp.mean(scaled1 * token_rows, -1, keepdims=True)
    ).astype(BF16)
    return (
        layer_result[None],
        d_input_rows[None],
        sum_gain_first,
        sum_qkv,
        sum_out,
        sum_router,
        sum_gain_second,
        sum_gate_up,
        sum_down,
    )


def local_fused(
    layer_input,
    gain_attn,
    query_key_value_weight,
    w_out,
    w_router,
    gain_ffn,
    w_gate_up,
    w_down,
    routes,
    d_out,
):
    tokens = layer_input.shape[1]
    ne, nc, nd = sizes = tuple(lax.axis_size(a) for a in ("expert", "context", "dp"))
    expert_total = EXP_DEV * ne
    first_row = lax.axis_index("context") * tokens
    query_width = QUERY_HEADS * HEAD_DIMENSION
    key_width = KEY_VALUE_HEADS * HEAD_DIMENSION
    qkv_width = query_width + 2 * key_width

    small = jnp.concatenate([w_router, gain_attn[:, None], gain_ffn[:, None]], -1)
    small = jnp.pad(small, ((0, 0), (0, SMALL - small.shape[1])))
    cosine_values, sine_values = rope_tables(first_row + jnp.arange(tokens), HEAD_DIMENSION)
    sine_values = sine_values * jnp.where(
        jnp.arange(HEAD_DIMENSION) < HEAD_DIMENSION // 2, -1.0, 1.0
    )
    (
        wk_all,
        wq_all,
        wo_all,
        cotangent_all,
        gate_all,
        gate_columns,
        inputs1,
        query,
        key_value,
        heads,
        hidden,
        expert_in,
        gains,
    ) = front(
        (
            layer_input[0],
            query_key_value_weight,
            small,
            w_out.T,
            d_out[0],
            cosine_values,
            sine_values,
            routes[0].T,
        ),
        sizes,
    )
    layer_result, d_x, sum_rows, sum_out, sum_gate_up, sum_down = back(
        (
            gate_columns,
            gate_all,
            gains,
            cosine_values,
            sine_values,
            expert_in,
            cotangent_all,
            w_gate_up,
            w_down,
            layer_input[0],
            inputs1,
            query,
            key_value,
            heads,
            hidden,
            wk_all.reshape(-1, wk_all.shape[-1]),
            wq_all.reshape(-1, query_width),
            wo_all.reshape(-1, wo_all.shape[-1]),
        ),
        sizes,
    )[:6]
    return (
        layer_result[None],
        d_x[None],
        sum_rows[:, qkv_width + expert_total],
        sum_rows[:, :qkv_width],
        sum_out.T,
        sum_rows[:, qkv_width : qkv_width + expert_total],
        sum_rows[:, qkv_width + expert_total + 1],
        sum_gate_up,
        jnp.swapaxes(sum_down, 1, 2),
    )


def solution(mesh):
    in_specs = (
        P(("expert", "dp"), "context", None),
        P(("expert", "context", "dp")),
        P(("expert", "context", "dp"), None),
        P(None, ("expert", "context", "dp")),
        P(("expert", "context", "dp"), None),
        P(("expert", "context", "dp")),
        P("expert", None, None),
        P("expert", None, None),
        P(("expert", "dp"), "context", None),
        P(("expert", "dp"), "context", None),
    )
    out_specs = (
        P(("expert", "dp"), "context", None),
        P(("expert", "dp"), "context", None),
        P(("expert", "context", "dp")),
        P(("expert", "context", "dp"), None),
        P(None, ("expert", "context", "dp")),
        P(("expert", "context", "dp"), None),
        P(("expert", "context", "dp")),
        P("expert", ("context", "dp"), None),
        P("expert", None, ("context", "dp")),
    )
    sizes = tuple(mesh.shape[a] for a in ("expert", "context", "dp"))
    local = local_fused if sizes == (4, 4, 2) else local_plain
    return jax.shard_map(local, mesh=mesh, in_specs=in_specs, out_specs=out_specs, check_vma=False)
```

```python
import functools
import math

import jax
import jax.numpy as jnp
from jax import lax
from jax.experimental import pallas as pl
from jax.experimental.pallas import tpu as pltpu
from jax.sharding import PartitionSpec as P

QUERY_HEADS = 12
KEY_VALUE_HEADS = 2
HEAD_DIMENSION = 128
TOP = 4
EXP_DEV = 2

EPSILON = 1e-06
ROPE_BASE = 10000.0
MASKED = -1e30

F32 = jnp.float32
BF16 = jnp.bfloat16


def rope_tables(positions, width):
    halfway = width // 2
    fraction = jnp.arange(halfway, dtype=jnp.float32) * (2.0 / width)
    frequency = jnp.exp(-math.log(ROPE_BASE) * fraction)
    angles = positions.astype(jnp.float32)[:, None] * frequency[None, :]
    cosine_values = jnp.cos(angles)
    sine_values = jnp.sin(angles)
    return (
        jnp.concatenate([cosine_values, cosine_values], -1),
        jnp.concatenate([sine_values, sine_values], -1),
    )


def rotate_half(values, cosine_values, sine_values):
    halfway = values.shape[-1] // 2
    turned = jnp.concatenate([-values[..., halfway:], values[..., :halfway]], -1)
    return values * cosine_values[:, None, :] + turned * sine_values[:, None, :]


def rotate_back(grads, cosine_values, sine_values):
    halfway = grads.shape[-1] // 2
    scaled = grads * sine_values[:, None, :]
    turned = jnp.concatenate([scaled[..., halfway:], -scaled[..., :halfway]], -1)
    return grads * cosine_values[:, None, :] + turned


def dot_nt(a, b):
    return lax.dot_general(a, b, (((1,), (1,)), ((), ())), preferred_element_type=F32)


def dot_tn(a, b):
    return lax.dot_general(a, b, (((0,), (0,)), ((), ())), preferred_element_type=F32)


def dot_nn(a, b):
    return jnp.dot(a, b, preferred_element_type=F32)


def masked_probs(first_row, query, key):
    scores = dot_nt(query, key) * (HEAD_DIMENSION**-0.5)
    rows = first_row + lax.broadcasted_iota(jnp.int32, scores.shape, 0)
    columns = lax.broadcasted_iota(jnp.int32, scores.shape, 1)
    scores = jnp.where(columns <= rows, scores, MASKED)
    expd = jnp.exp(scores - jnp.max(scores, axis=-1, keepdims=True))
    return expd / jnp.sum(expd, axis=-1, keepdims=True)


def attend_forward_kernel(first_ref, query_ref, key_ref, value_ref, heads_ref):
    probs = masked_probs(first_ref[0], query_ref[...], key_ref[...])
    heads_ref[...] = dot_nn(probs.astype(BF16), value_ref[...]).astype(BF16)


def attend_forward(first_row, query, key_value):
    tokens, width = query.shape
    length = key_value.shape[0]
    group = QUERY_HEADS // KEY_VALUE_HEADS
    size = HEAD_DIMENSION
    return pl.pallas_call(
        attend_forward_kernel,
        grid_spec=pltpu.PrefetchScalarGridSpec(
            num_scalar_prefetch=1,
            grid=(QUERY_HEADS,),
            in_specs=[
                pl.BlockSpec((tokens, size), lambda h, s: (0, h)),
                pl.BlockSpec((length, size), lambda h, s: (0, h // group)),
                pl.BlockSpec((length, size), lambda h, s: (0, KEY_VALUE_HEADS + h // group)),
            ],
            out_specs=pl.BlockSpec((tokens, size), lambda h, s: (0, h)),
        ),
        out_shape=jax.ShapeDtypeStruct((tokens, width), BF16),
        compiler_params=pltpu.CompilerParams(vmem_limit_bytes=32 * 1024 * 1024),
        cost_estimate=pl.CostEstimate(
            flops=4 * tokens * length * width, bytes_accessed=4 * tokens * width, transcendentals=0
        ),
    )(first_row, query, key_value, key_value)


def attend_backward_kernel(
    first_ref, query_ref, key_ref, value_ref, grad_ref, d_query_ref, d_key_ref, d_value_ref
):
    query, key, value, grad = query_ref[...], key_ref[...], value_ref[...], grad_ref[...]
    probs = masked_probs(first_ref[0], query, key)
    d_probs = dot_nt(grad, value)
    inner = jnp.sum(probs * d_probs, axis=-1, keepdims=True)
    d_raw = (probs * (d_probs - inner) * (HEAD_DIMENSION**-0.5)).astype(BF16)
    d_query_ref[...] = dot_nn(d_raw, key)
    d_key = dot_tn(d_raw, query)
    d_value = dot_tn(probs.astype(BF16), grad)

    @pl.when(pl.program_id(1) == 0)
    def _():
        d_key_ref[...] = d_key
        d_value_ref[...] = d_value

    @pl.when(pl.program_id(1) > 0)
    def _():
        d_key_ref[...] += d_key
        d_value_ref[...] += d_value


def attend_backward(first_row, query, key_value, grad):
    tokens, width = query.shape
    length = key_value.shape[0]
    group = QUERY_HEADS // KEY_VALUE_HEADS
    size = HEAD_DIMENSION
    row_spec = pl.BlockSpec((tokens, size), lambda j, g, s: (0, j * group + g))
    return pl.pallas_call(
        attend_backward_kernel,
        grid_spec=pltpu.PrefetchScalarGridSpec(
            num_scalar_prefetch=1,
            grid=(KEY_VALUE_HEADS, group),
            in_specs=[
                row_spec,
                pl.BlockSpec((length, size), lambda j, g, s: (0, j)),
                pl.BlockSpec((length, size), lambda j, g, s: (0, KEY_VALUE_HEADS + j)),
                row_spec,
            ],
            out_specs=[
                row_spec,
                pl.BlockSpec((length, size), lambda j, g, s: (0, j)),
                pl.BlockSpec((length, size), lambda j, g, s: (0, j)),
            ],
        ),
        out_shape=[
            jax.ShapeDtypeStruct((tokens, width), F32),
            jax.ShapeDtypeStruct((length, KEY_VALUE_HEADS * size), F32),
            jax.ShapeDtypeStruct((length, KEY_VALUE_HEADS * size), F32),
        ],
        compiler_params=pltpu.CompilerParams(vmem_limit_bytes=32 * 1024 * 1024),
        cost_estimate=pl.CostEstimate(
            flops=10 * tokens * length * width, bytes_accessed=8 * tokens * width, transcendentals=0
        ),
    )(first_row, query, key_value, key_value, grad)


def exchange(values, axis, mask):
    size = lax.axis_size(axis)
    return lax.ppermute(values, axis, [(i, i ^ mask) for i in range(size)])


def axis_masks(axis):
    size = lax.axis_size(axis)
    masks, bit = [], 1
    while bit < size:
        masks.append(bit)
        bit *= 2
    return masks


def cube_gather(values, axis, masks):
    held = {0: values}
    for mask in masks:
        for r, block in list(held.items()):
            held[r ^ mask] = exchange(block, axis, mask)
    return [held[r] for r in range(lax.axis_size(axis))]


def cube_scatter(blocks, axis, masks):
    held = dict(enumerate(blocks))
    for mask in masks:
        kept = {}
        for r in list(held):
            if not r & mask:
                arrived = exchange(held[r ^ mask].astype(BF16), axis, mask)
                kept[r] = held[r].astype(F32) + arrived.astype(F32)
        held = kept
    return held[0]


def line_steps(values, axis, up):
    size = lax.axis_size(axis)
    pairs = [(i, i + 1) if up else (i + 1, i) for i in range(size - 1)]
    return lax.ppermute(values, axis, pairs)


def line_gather(values, axis, both=True):
    size = lax.axis_size(axis)
    me = lax.axis_index(axis)
    result = jnp.zeros((size + 1,) + values.shape, values.dtype)
    result = lax.dynamic_update_index_in_dim(result, values, me, 0)
    up = down = values
    for step in range(1, size):
        up = line_steps(up, axis, True)
        result = lax.dynamic_update_index_in_dim(
            result, up, jnp.where(me - step >= 0, me - step, size), 0
        )
        if both:
            down = line_steps(down, axis, False)
            result = lax.dynamic_update_index_in_dim(result, down, jnp.minimum(me + step, size), 0)
    return result[:size]


def line_scatter(take, axis, up=True, down=True):
    size = lax.axis_size(axis)
    me = lax.axis_index(axis)
    total = take(me).astype(F32)
    for active, sign in ((up, 1), (down, -1)):
        if not active:
            continue
        arrived = None
        for step in range(1, size):
            block = take((me + sign * (size - step)) % size).astype(F32)
            if arrived is not None:
                block = block + arrived.astype(F32)
            arrived = line_steps(block.astype(BF16), axis, sign > 0)
        total = total + arrived.astype(F32)
    return total


def gather_rows(shard):
    ne, nc, nd = (lax.axis_size(a) for a in ("expert", "context", "dp"))
    rows, width = shard.shape
    lines = line_gather(shard, "context")
    masks = axis_masks("expert")
    half = width // 256 * 128
    parts = [lines[..., :half], lines[..., half:]]
    me = lax.axis_index("expert")
    result = jnp.zeros((ne, nc, rows, width), shard.dtype)
    for start, part, order in ((0, parts[0], masks), (half, parts[1], masks[::-1])):
        for r, block in enumerate(cube_gather(part, "expert", order)):
            result = lax.dynamic_update_slice(result, block[None], (me ^ r, 0, 0, start))
    core = lax.axis_index("dp")
    whole = jnp.zeros((ne, nc, nd, rows, width), shard.dtype)
    for r, block in enumerate(cube_gather(result, "dp", axis_masks("dp"))):
        whole = lax.dynamic_update_slice(whole, block[:, :, None], (0, 0, core ^ r, 0, 0))
    return whole.reshape(-1, width)


def scatter_rows(grad):
    ne, nc, nd = (lax.axis_size(a) for a in ("expert", "context", "dp"))
    width = grad.shape[-1]
    rows = grad.shape[0] // (ne * nc * nd)
    blocks = grad.reshape(ne, nc, nd, rows, width)
    core, me = lax.axis_index("dp"), lax.axis_index("expert")
    mine = cube_scatter(
        [
            lax.dynamic_index_in_dim(blocks, core ^ r, 2, keepdims=False)
            for r in range(nd)
        ],
        "dp",
        axis_masks("dp"),
    )
    masks = axis_masks("expert")
    half = width // 256 * 128
    sums = []
    for part, order in ((mine[..., :half], masks), (mine[..., half:], masks[::-1])):
        sums.append(
            cube_scatter(
                [lax.dynamic_index_in_dim(part, me ^ r, 0, keepdims=False) for r in range(ne)],
                "expert",
                order,
            )
        )
    lines = jnp.concatenate(sums, -1)
    return line_scatter(
        lambda j: lax.dynamic_index_in_dim(lines, j, 0, keepdims=False), "context"
    )


def plane_gather(rows):
    masks = axis_masks("expert")
    half = rows.shape[-1] // 2
    left = cube_gather(rows[:, :half], "expert", masks)
    right = cube_gather(rows[:, half:], "expert", masks[::-1])
    return jnp.concatenate([jnp.concatenate(p, -1) for p in zip(left, right)], 0)


def plane_scatter(partial, tokens):
    masks = axis_masks("expert")
    size = lax.axis_size("expert")
    half = partial.shape[-1] // 2
    blocks = partial.reshape(size, tokens, -1)
    left = cube_scatter([blocks[r, :, :half] for r in range(size)], "expert", masks)
    right = cube_scatter([blocks[r, :, half:] for r in range(size)], "expert", masks[::-1])
    return jnp.concatenate([left, right], -1)


MESH = pl.DeviceIdType.MESH
MIB = 1024 * 1024
SMALL = 128
GATE_ROWS = 16


def flip(index, mask):
    bit = 1
    while bit <= mask:
        if mask & bit:
            index = index + bit - 2 * bit * lax.rem(lax.div(index, bit), 2)
        bit *= 2
    return index


class Wire:
    def __init__(self, sends, recvs):
        self.sends, self.recvs = sends, recvs
        self.n_sends = self.n_recvs = 0
        self.open = []

    def slots(self, count):
        first = self.n_recvs
        self.n_recvs += count
        return first

    def start(self, src, dst, recv, device, when=None):
        copy = pltpu.make_async_remote_copy(
            src_ref=src,
            dst_ref=dst,
            send_sem=self.sends.at[self.n_sends],
            recv_sem=self.recvs.at[recv],
            device_id=device,
            device_id_type=MESH,
        )
        self.n_sends += 1
        guard(when, copy.start)
        self.open.append((when, copy))

    def arrived(self, dst, recv, device):
        pltpu.make_async_remote_copy(
            src_ref=dst,
            dst_ref=dst,
            send_sem=self.sends.at[0],
            recv_sem=self.recvs.at[recv],
            device_id=device,
            device_id_type=MESH,
        ).wait_recv()

    def finish(self):
        for when, copy in self.open:
            guard(when, copy.wait_send)
        self.open = []


def guard(when, action):
    if when is None:
        action()
    else:
        pl.when(when)(action)


def greet(targets):
    barrier = pltpu.get_barrier_semaphore()
    for device, when in targets:
        guard(
            when,
            lambda device=device: pl.semaphore_signal(
                barrier, inc=1, device_id=device, device_id_type=MESH
            ),
        )
    count = sum(1 if when is None else when.astype(jnp.int32) for _, when in targets)
    pl.semaphore_wait(barrier, count)


def plane_ids(e):
    return {m: {"expert": flip(e, m)} for m in (1, 2, 3)}


class RowsGather:
    def __init__(self, wire, ref, e, z, c, nc, half):
        self.wire, self.ref, self.e, self.z, self.c, self.nc = wire, ref, e, z, c, nc
        self.cols = (pl.ds(0, half), pl.ds(half, ref.shape[-1] - half))
        self.line = wire.slots(nc)
        self.plane = wire.slots(nc * 6)
        self.core = wire.slots(nc)
        self.ids = plane_ids(e)

    def go(self, *steps):
        for step in steps:
            action = {"l": self.pass_on, "s": self.spread, "f": self.forward, "h": self.share, "c": self.complete}
            action[step[0]](*map(int, step[1:]))

    def shard(self, k):
        if k < 2:
            return flip(self.z, k)
        inner = (self.z > 0) & (self.z < self.nc - 1)
        return jnp.where(inner, flip(self.z, 5 - k), flip(self.z, k))

    def at(self, r, zs, half):
        return self.ref.at[flip(self.e, r), zs, self.c, :, self.cols[half]]

    def slot(self, k, r, half):
        return self.plane + k * 6 + (r - 1) * 2 + half

    def pass_on(self, k):
        wire, z, nc = self.wire, self.z, self.nc
        zs = self.shard(k)
        whole = self.ref.at[self.e, zs, self.c]
        if k:
            wire.arrived(whole, self.line + zs, {"context": zs})
        wire.start(
            whole, whole, self.line + zs, {"context": z + 1}, when=(zs <= z) & (z < nc - 1)
        )
        wire.start(whole, whole, self.line + zs, {"context": z - 1}, when=(zs >= z) & (z > 0))

    def spread(self, k):
        zs = self.shard(k)
        for half, mask in ((0, 1), (1, 2), (1, 1), (0, 2)):
            part = self.at(0, zs, half)
            self.wire.start(part, part, self.slot(k, mask, half), self.ids[mask])

    def forward(self, k):
        zs = self.shard(k)
        for half, mask in ((0, 1), (1, 2)):
            part = self.at(mask, zs, half)
            self.wire.arrived(part, self.slot(k, mask, half), self.ids[mask])
            self.wire.start(part, part, self.slot(k, 3, half), self.ids[3 - mask])

    def share(self, k):
        zs = self.shard(k)
        for r, half in ((1, 1), (2, 0), (3, 0), (3, 1)):
            self.wire.arrived(self.at(r, zs, half), self.slot(k, r, half), self.ids[r])
        part = self.ref.at[:, zs, self.c]
        self.wire.start(part, part, self.core + k, {"dp": 1 - self.c})

    def complete(self):
        for k in range(self.nc):
            zs = self.shard(k)
            self.wire.arrived(self.ref.at[:, zs, 1 - self.c], self.core + k, {"dp": 1 - self.c})


class PlaneGather:
    def __init__(self, wire, ref, e):
        self.wire, self.ref = wire, ref
        self.half = ref.shape[-1] // 2
        self.ids = plane_ids(e)
        self.first = wire.slots(6)

    def at(self, r, half):
        return self.ref.at[r, :, pl.ds(half * self.half, self.half)]

    def slot(self, r, half):
        return self.first + (r - 1) * 2 + half

    def spread(self):
        for half, mask in ((0, 1), (1, 2), (1, 1), (0, 2)):
            self.wire.start(
                self.at(0, half), self.at(mask, half), self.slot(mask, half), self.ids[mask]
            )

    def forward(self):
        for half, mask in ((0, 1), (1, 2)):
            self.wire.arrived(self.at(mask, half), self.slot(mask, half), self.ids[mask])
            self.wire.start(
                self.at(mask, half), self.at(3, half), self.slot(3, half), self.ids[3 - mask]
            )

    def near(self, r):
        half = 1 if r == 1 else 0
        self.wire.arrived(self.at(r, half), self.slot(r, half), self.ids[r])

    def far(self):
        for half in (0, 1):
            self.wire.arrived(self.at(3, half), self.slot(3, half), self.ids[3])

    def complete(self):
        self.near(1)
        self.near(2)
        self.far()


def swap_halves(values):
    return pltpu.roll(values, HEAD_DIMENSION // 2, 1)


def front_kernel(
    nc,
    experts,
    x_ref,
    qkv_shard,
    small_shard,
    wo_shard,
    cot_ref,
    cos_ref,
    sin_ref,
    routes_ref,
    wk_hbm,
    wq_hbm,
    wo_hbm,
    cot_hbm,
    gate_all,
    gate_columns,
    inputs_ref,
    query_ref,
    kv_ref,
    heads_ref,
    hidden_ref,
    expert_in_ref,
    gains_ref,
    wk_all,
    wq_all,
    wo_all,
    cot_all,
    kv_scr,
    q_scr,
    sends,
    recvs,
    out_sems,
):
    e, z, c = (lax.axis_index(a) for a in ("expert", "context", "dp"))
    size = HEAD_DIMENSION
    tokens, width = x_ref.shape
    query_width = QUERY_HEADS * size
    kv_width = 2 * KEY_VALUE_HEADS * size
    wire = Wire(sends, recvs)
    ids = plane_ids(e)
    greet(
        [(ids[m], None) for m in (1, 2, 3)]
        + [({"dp": 1 - c}, None)]
        + [({"context": z + d}, z + d < nc) for d in range(1, nc)]
        + [({"context": z - d}, z >= d) for d in range(1, nc)]
    )
    wk_all[e, z, c, :, pl.ds(0, kv_width)] = qkv_shard[:, pl.ds(query_width, kv_width)]
    wk_all[e, z, c, :, pl.ds(kv_width, SMALL)] = small_shard[...]
    gather_k = RowsGather(wire, wk_all, e, z, c, nc, 256)
    gather_q = RowsGather(wire, wq_all, e, z, c, nc, 768)
    gather_o = RowsGather(wire, wo_all, e, z, c, nc, 768)
    gather_cot = PlaneGather(wire, cot_all, e)
    wq_all[e, z, c] = qkv_shard[:, pl.ds(0, query_width)]
    wo_all[e, z, c] = wo_shard[...]
    gather_k.go("l0", "s0")
    gather_q.go("s0")
    cot_all[0] = cot_ref[...]
    gather_k.go("l1", "s1", "f0", "l2", "s2")
    gather_q.go("l0")
    gather_k.go("f1", "h0", "l3", "s3")
    gather_q.go("l1", "s1")
    gather_o.go("l0")
    gather_k.go("f2", "h1", "f3")
    gather_q.go("l2", "s2")
    gather_k.go("h2")
    gather_o.go("l1")
    gather_q.go("f0")
    gather_k.go("h3")
    gather_q.go("l3", "s3")
    gather_k.go("c")
    rows = x_ref[...].astype(F32)
    scale1 = lax.rsqrt(jnp.mean(rows * rows, -1, keepdims=True) + EPSILON)

    small = wk_all[:, :, :, :, pl.ds(kv_width, SMALL)].reshape(width, SMALL)
    small = jnp.transpose(small.astype(F32))
    gain_first, gain_second = small[experts : experts + 1], small[experts + 1 : experts + 2]
    gains_ref[0:1] = gain_first
    gains_ref[1:2] = gain_second
    inputs_ref[...] = (rows * scale1 * gain_first).astype(BF16)
    kv_scr[...] = dot_nn(inputs_ref[...], wk_all[...].reshape(width, kv_width + SMALL))

    def turned(head):
        return (head * cos_ref[...] + swap_halves(head) * sin_ref[...]).astype(BF16)

    line = wire.slots(KEY_VALUE_HEADS * nc)
    for j in range(KEY_VALUE_HEADS):
        kv_ref[j, z, :, pl.ds(0, size)] = turned(kv_scr[:, pl.ds(j * size, size)])
        value = kv_scr[:, pl.ds(kv_width // 2 + j * size, size)]
        kv_ref[j, z, :, pl.ds(size, size)] = value.astype(BF16)
        mine = kv_ref.at[j, z]
        for d in range(nc - 1, 0, -1):
            wire.start(mine, mine, line + j * nc + z, {"context": z + d}, when=z + d < nc)

    def keys_here(j):
        for d in range(1, nc):

            def wait(d=d):
                wire.arrived(kv_ref.at[j, z - d], line + j * nc + z - d, {"context": z - d})

            pl.when(z >= d)(wait)

    outs = [
        pltpu.make_async_copy(source, dest, out_sems.at[n])
        for n, (source, dest) in enumerate(
            ((wk_all, wk_hbm), (wq_all, wq_hbm), (wo_all, wo_hbm), (cot_all, cot_hbm))
        )
    ]
    outs[0].start()
    for later in range(1, nc):

        def clear(later=later):
            for j in range(KEY_VALUE_HEADS):
                kv_ref[j, z + later] = jnp.zeros(kv_ref.shape[2:], BF16)

        pl.when(z + later < nc)(clear)
    gather_q.go("f1")
    gather_o.go("l2")
    gather_q.go("f2", "h0")
    gather_o.go("l3", "s0")
    gather_q.go("f3", "h1")
    gather_o.go("s1")
    gather_q.go("h2")
    gather_o.go("s2", "s3")
    gather_q.go("h3", "c")
    outs[1].start()

    @pl.loop(0, query_width // 256)
    def _(n):
        columns = pl.ds(pl.multiple_of(n * 256, 256), 256)
        q_scr[:, columns] = dot_nn(
            inputs_ref[...], wq_all[:, :, :, :, columns].reshape(width, 256)
        )

    @pl.loop(0, QUERY_HEADS)
    def _(h):
        columns = pl.ds(pl.multiple_of(h * size, size), size)
        query_ref[:, columns] = turned(q_scr[:, columns])

    logits = kv_scr[:, pl.ds(kv_width, SMALL)]
    lanes = lax.broadcasted_iota(jnp.int32, logits.shape, 1)
    routes = jnp.concatenate(
        [routes_ref[...].astype(F32), jnp.zeros((SMALL - TOP, tokens), F32)], 0
    )
    routes = jnp.transpose(routes).astype(jnp.int32)
    named = lanes == routes[:, 0:1]
    for k in range(1, TOP):
        named = named | (lanes == routes[:, k : k + 1])
    logits = jnp.where(named, logits, MASKED)
    expd = jnp.exp(logits - jnp.max(logits, -1, keepdims=True))
    gates = expd / jnp.sum(expd, -1, keepdims=True)
    gate_all[0] = jnp.transpose(gates)[:GATE_ROWS]
    gate_slot = wire.slots(3)
    for r in (1, 2, 3):
        wire.start(gate_all.at[0], gate_all.at[r], gate_slot + r - 1, ids[r])
    gather_o.go("f0", "f1")

    length = nc * tokens
    group = QUERY_HEADS // KEY_VALUE_HEADS

    def attend(first, last):
        j = first // group
        key = kv_ref[j, :, :, pl.ds(0, size)].reshape(length, size)
        value = kv_ref[j, :, :, pl.ds(size, size)].reshape(length, size)

        @pl.loop(first, last)
        def _(h):
            column = pl.multiple_of(h * size, size)
            scores = dot_nt(query_ref[:, pl.ds(column, size)], key) * (size**-0.5)
            row = z * tokens + lax.broadcasted_iota(jnp.int32, scores.shape, 0)
            place = lax.broadcasted_iota(jnp.int32, scores.shape, 1)
            scores = jnp.where(place <= row, scores, MASKED)
            expd = jnp.exp(scores - jnp.max(scores, -1, keepdims=True))
            total = jnp.sum(expd, -1, keepdims=True)
            mixed = dot_nn(expd.astype(BF16), value) / total
            heads_ref[:, pl.ds(column, size)] = mixed.astype(BF16)

    half = group // 2
    keys_here(0)
    attend(0, half)
    gather_o.go("f2", "f3")
    gather_cot.spread()
    attend(half, group)
    gather_o.go("h0", "h1")
    keys_here(1)
    attend(group, group + half)
    gather_o.go("h2", "h3")
    attend(group + half, QUERY_HEADS)
    gather_cot.forward()
    gather_o.go("c")
    outs[2].start()
    part = width // wo_all.shape[0]
    for block in range(wo_all.shape[0]):
        weight = wo_all[block].reshape(part, width)
        columns = pl.ds(block * part, part)
        hidden_ref[:, columns] = x_ref[:, columns].astype(F32) + dot_nt(heads_ref[...], weight)
    hidden = hidden_ref[...]
    scale2 = lax.rsqrt(jnp.mean(hidden * hidden, -1, keepdims=True) + EPSILON)
    expert_in_ref[...] = (hidden * scale2 * gains_ref[1:2]).astype(BF16)
    for r in (1, 2, 3):
        wire.arrived(gate_all.at[r], gate_slot + r - 1, ids[r])
    for r in range(gate_all.shape[0]):
        rest = jnp.zeros((SMALL - GATE_ROWS, tokens), F32)
        turned_gates = jnp.transpose(jnp.concatenate([gate_all[r], rest], 0))
        both = [
            jnp.sum(jnp.where(lanes == e * EXP_DEV + i, turned_gates, 0.0), -1, keepdims=True)
            for i in range(EXP_DEV)
        ]
        gate_columns[r] = jnp.where(lanes == 0, both[0], jnp.where(lanes == 1, both[1], 0.0))
    gather_cot.complete()
    outs[3].start()
    for copy in outs:
        copy.wait()
    wire.finish()


def front(operands, sizes):
    ne, nc, nd = sizes
    x, qkv_shard = operands[:2]
    tokens, width = x.shape
    rows, qkv_width = qkv_shard.shape
    query_width = QUERY_HEADS * HEAD_DIMENSION
    kv_width = qkv_width - query_width
    gathered = [
        ((ne, nc, nd, rows, kv_width + SMALL), BF16),
        ((ne, nc, nd, rows, query_width), BF16),
        ((ne, nc, nd, rows, width), BF16),
        ((ne, tokens, width), BF16),
    ]
    shapes = gathered + [
        ((ne, GATE_ROWS, tokens), F32),
        ((ne, tokens, SMALL), F32),
        ((tokens, width), BF16),
        ((tokens, query_width), BF16),
        ((KEY_VALUE_HEADS, nc, tokens, 2 * HEAD_DIMENSION), BF16),
        ((tokens, query_width), BF16),
        ((tokens, width), F32),
        ((tokens, width), BF16),
        ((8, width), F32),
    ]
    copies = 160
    vmem = pl.BlockSpec(memory_space=pltpu.VMEM)
    anywhere = pl.BlockSpec(memory_space=pl.ANY)
    return pl.pallas_call(
        functools.partial(front_kernel, nc, EXP_DEV * ne),
        out_shape=[jax.ShapeDtypeStruct(*s) for s in shapes],
        in_specs=[vmem] * len(operands),
        out_specs=[anywhere] * 4 + [vmem] * (len(shapes) - 4),
        scratch_shapes=[pltpu.VMEM(*s) for s in gathered]
        + [
            pltpu.VMEM((tokens, kv_width + SMALL), F32),
            pltpu.VMEM((tokens, query_width), F32),
            pltpu.SemaphoreType.DMA((copies,)),
            pltpu.SemaphoreType.DMA((copies,)),
            pltpu.SemaphoreType.DMA((4,)),
        ],
        compiler_params=pltpu.CompilerParams(
            collective_id=0, has_side_effects=True, vmem_limit_bytes=56 * MIB
        ),
    )(*operands)


class PlaneScatter:
    def __init__(self, wire, land, ids):
        self.wire, self.land, self.ids, self.part = wire, land, ids, None
        self.half = land.shape[-1]
        self.first = wire.slots(6)

    def send(self, source, mask, slot):
        self.wire.start(source, self.land.at[slot], self.first + slot, self.ids[mask])

    def near(self, r):
        self.send(self.part(r, r - 1), r, r - 1)

    def far(self):
        self.send(self.part(3, 0), 1, 2)
        self.send(self.part(3, 1), 2, 3)

    def relay(self, part=None):
        for half, r in ((0, 2), (1, 1)):
            slot = 2 + half
            self.wire.arrived(self.land.at[slot], self.first + slot, self.ids[3 - r])
            mine = (part or self.part)(r, half)
            mine[...] = (mine[...].astype(F32) + self.land[slot].astype(F32)).astype(BF16)
            self.send(mine, r, 4 + half)

    def total(self, own):
        for slot, half, mask in ((0, 0, 1), (1, 1, 2), (4, 0, 2), (5, 1, 1)):
            self.wire.arrived(self.land.at[slot], self.first + slot, self.ids[mask])
            columns = pl.ds(half * self.half, self.half)
            own[:, columns] += self.land[slot].astype(F32)


class LineScatter:
    def __init__(self, wire, block, lands, z, nc, up=True):
        self.wire, self.block, self.lands, self.z, self.nc = wire, block, lands, z, nc
        self.up = up
        self.first = [wire.slots(nc - 1), wire.slots(nc - 1)]

    def arrive(self, way, index, j):
        land = self.lands[way].at[index]
        self.wire.arrived(land, self.first[way] + index, {"context": self.z})
        block = self.block(j)
        block[...] = (block[...].astype(F32) + self.lands[way][index].astype(F32)).astype(BF16)

    def move(self, way, j):
        z, nc = self.z, self.nc
        inner, index, near = ((z > 0), j - z, z + 1) if way == 0 else ((z < nc - 1), z - j, z - 1)
        wanted = (j > z) if way == 0 else (j < z)
        pl.when(wanted & inner)(lambda: self.arrive(way, index, j))
        self.wire.start(
            self.block(j),
            self.lands[way].at[index - 1],
            self.first[way] + index - 1,
            {"context": near},
            when=wanted,
        )

    def step(self, s):
        if self.up:
            self.move(0, self.nc - s)
        self.move(1, s - 1)

    def last(self):
        if self.up:
            pl.when(self.z > 0)(lambda: self.arrive(0, 0, self.z))
        pl.when(self.z < self.nc - 1)(lambda: self.arrive(1, 0, self.z))


class RowsScatter:
    def __init__(self, wire, buf, core, plane, lines, e, z, c, nc, start, width, half):
        self.wire, self.buf, self.core, self.plane = wire, buf, core, plane
        self.e, self.c = e, c
        self.all = pl.ds(start, width)
        self.cols = (pl.ds(start, half), pl.ds(start + half, width - half))
        self.ids = plane_ids(e)
        self.core_slot = wire.slots(1)
        self.first = wire.slots(6)
        rows = buf.shape[2] // nc
        self.line = LineScatter(
            wire,
            lambda j: buf.at[c, e, pl.ds(pl.multiple_of(j * rows, rows), rows), self.all],
            lines,
            z,
            nc,
        )

    def share(self):
        self.wire.start(
            self.buf.at[1 - self.c, :, :, self.all], self.core, self.core_slot, {"dp": 1 - self.c}
        )

    def at(self, r, half):
        return self.buf.at[self.c, flip(self.e, r), :, self.cols[half]]

    def send(self, r, half, mask, slot):
        self.wire.start(
            self.at(r, half), self.plane(slot, half), self.first + slot, self.ids[mask]
        )

    def merge(self, before=None):
        self.wire.arrived(self.core, self.core_slot, {"dp": 1 - self.c})
        for r in (3, 1, 2, 0):
            block = flip(self.e, r)
            part = self.buf.at[self.c, block, :, self.all]
            part[...] = (part[...].astype(F32) + self.core[block].astype(F32)).astype(BF16)
            if r == 3:
                if before is not None:
                    before()
                self.send(3, 0, 1, 2)
                self.send(3, 1, 2, 3)
            elif r:
                self.send(r, r - 1, r, r - 1)

    def add(self, r, half, slot, mask):
        land = self.plane(slot, half)
        self.wire.arrived(land, self.first + slot, self.ids[mask])
        part = self.at(r, half)
        part[...] = (part[...].astype(F32) + land[...].astype(F32)).astype(BF16)

    def relay(self):
        for half, r in ((0, 2), (1, 1)):
            self.add(r, half, 2 + half, 3 - r)
            self.send(r, half, r, 4 + half)

    def total(self):
        for slot, half, mask in ((0, 0, 1), (1, 1, 2), (4, 0, 2), (5, 1, 1)):
            self.add(0, half, slot, mask)


class ExpertLine:
    def __init__(self, wire, base, land, ins, out, sems, z, nc):
        self.wire, self.base, self.land = wire, base, land
        self.ins, self.out, self.sems, self.z, self.nc = ins, out, sems, z, nc
        self.end = (z == 0) | (z == nc - 1)
        self.inner = jnp.logical_not(self.end)
        self.width = base.shape[-1] // EXP_DEV
        self.first = wire.slots((nc + 1) * EXP_DEV)
        self.sent = []

    def part(self, ref, j, i):
        return ref.at[j, :, pl.ds(i * self.width, self.width)]

    def combine(self, sources, stores):
        out, step = self.out, self.ins.shape[2]
        count = sources[0].shape[0] // step

        def loads(p):
            rows = pl.ds(p * step, step)
            return [
                pltpu.make_async_copy(
                    source.at[rows], self.ins.at[k, p % 2], self.sems.at[2 * k + p % 2]
                )
                for k, source in enumerate(sources)
            ]

        def store(p):
            pairs = stores(pl.ds(p * step, step), out.at[p % 2])
            return [
                pltpu.make_async_copy(source, dest, self.sems.at[8 + 2 * n + p % 2])
                for n, (source, dest) in enumerate(pairs)
            ]

        for copy in loads(0):
            copy.start()
        for p in range(count):
            if p + 1 < count:
                for copy in loads(p + 1):
                    copy.start()
            for copy in loads(p):
                copy.wait()
            if p > 1:
                for copy in store(p - 2):
                    copy.wait()
            total = self.ins[0, p % 2].astype(F32)
            for k in range(1, len(sources)):
                total = total + self.ins[k, p % 2].astype(F32)
            out[p % 2] = total.astype(out.dtype)
            for copy in store(p):
                copy.start()
        for p in range(max(0, count - 2), count):
            for copy in store(p):
                copy.wait()

    def copy(self, i, r, number):
        target, slot = flip(self.z, r), self.z
        if r == 3:
            target = jnp.where(self.end, flip(self.z, 1), target)
            slot = jnp.where(self.end, self.nc, slot)
        return pltpu.make_async_remote_copy(
            src_ref=self.part(self.base, flip(self.z, r), i),
            dst_ref=self.part(self.land, slot, i),
            send_sem=self.wire.sends.at[number],
            recv_sem=self.wire.recvs.at[self.first + slot * EXP_DEV + i],
            device_id={"context": target},
            device_id_type=MESH,
        )

    def send(self, i, r, when=None):
        number = len(self.sent)
        guard(when, self.copy(i, r, number).start)
        self.sent.append((when, i, r, number))

    def finish(self):
        for when, i, r, number in self.sent:
            guard(when, self.copy(i, r, number).wait_send)

    def arrived(self, slot, i):
        land = self.part(self.land, slot, i)
        self.wire.arrived(land, self.first + slot * EXP_DEV + i, {"context": self.z})

    def relay_loads(self, i, p):
        step = self.ins.shape[2]
        rows = pl.ds(p * step, step)
        sources = (self.part(self.base, flip(self.z, 2), i), self.part(self.land, self.nc, i))
        return [
            pltpu.make_async_copy(
                source.at[rows], self.ins.at[2 * k + p // 2, p % 2], self.sems.at[4 * k + p]
            )
            for k, source in enumerate(sources)
        ]

    def relay_store(self, i, p):
        step = self.ins.shape[2]
        mine = self.part(self.base, flip(self.z, 2), i).at[pl.ds(p * step, step)]
        return pltpu.make_async_copy(self.ins.at[p // 2, p % 2], mine, self.sems.at[8 + p])

    def relay_steps(self):
        return range(self.base.shape[1] // self.ins.shape[2])

    def relay_begin(self, i):
        self.relayed = i

        def begin():
            self.arrived(self.nc, i)
            for p in self.relay_steps():
                for copy in self.relay_loads(i, p):
                    copy.start()

        pl.when(self.inner)(begin)

    def relay_add(self):
        i = self.relayed

        def add():
            for p in self.relay_steps():
                for copy in self.relay_loads(i, p):
                    copy.wait()
                a, b = (self.ins[2 * k + p // 2, p % 2].astype(F32) for k in range(2))
                self.ins[p // 2, p % 2] = (a + b).astype(BF16)
                self.relay_store(i, p).start()

        pl.when(self.inner)(add)

    def relay_send(self, i):
        def wait():
            for p in self.relay_steps():
                self.relay_store(i, p).wait()

        pl.when(self.inner)(wait)
        self.send(i, 2, when=self.inner)

    def last(self, i, results):
        z = self.z
        sources = [self.part(self.base, z, i)]
        for r in (1, 2):
            self.arrived(flip(z, r), i)
            sources.append(self.part(self.land, flip(z, r), i))

        def stores(rows, wide):
            pairs, first = [], 0
            for result in results:
                columns = pl.ds(first, result.shape[-1])
                pairs.append((wide.at[:, columns], result.at[i, rows]))
                first += result.shape[-1]
            return pairs

        pl.when(self.end)(lambda: self.combine(sources, stores))

        def inner():
            self.arrived(flip(z, 3), i)
            self.combine(sources + [self.part(self.land, flip(z, 3), i)], stores)

        pl.when(self.inner)(inner)


def back_kernel(
    nc,
    experts,
    gates_ref,
    gate_ref,
    gains_ref,
    cos_ref,
    sin_ref,
    expert_in_hbm,
    cot_hbm,
    w_gu_hbm,
    w_dn_hbm,
    x_hbm,
    inputs_hbm,
    query_hbm,
    kv_hbm,
    heads_hbm,
    hidden_hbm,
    wk_hbm,
    wq_hbm,
    o_hbm,
    layer_ref,
    d_x_ref,
    sum_q_ref,
    sum_o_ref,
    sum_gu_hbm,
    sum_dn_hbm,
    base_hbm,
    land_hbm,
    y_hbm,
    x_all,
    y_land,
    dx_land,
    core_land,
    plane_q,
    plane_k,
    lines_o,
    lines_q,
    lines_k,
    dkv_land,
    d_in_ref,
    dg_lanes,
    dg_part,
    dg_land,
    ins,
    out_wide,
    sends_1,
    recvs_1,
    sends_2,
    recvs_2,
    sends_e,
    recvs_e,
    hand_sends,
    hand_recvs,
    stage_sems,
    load_sems,
    sum_sems,
    y_sems,
    credits,
):
    e, z, c = (lax.axis_index(a) for a in ("expert", "context", "dp"))
    size = HEAD_DIMENSION
    blocks, tokens, width = cot_hbm.shape
    ff = w_dn_hbm.shape[1]
    query_width = QUERY_HEADS * size
    key_width = KEY_VALUE_HEADS * size
    qkv_width = query_width + 2 * key_width
    rest = wk_hbm.shape[-1]
    grad_width = base_hbm.shape[-1]
    ids = plane_ids(e)
    sibling = {"dp": 1 - c}
    wire_1, wire_2, wire_e = Wire(sends_1, recvs_1), Wire(sends_2, recvs_2), Wire(sends_e, recvs_e)
    expert = ExpertLine(
        wire_e, base_hbm, land_hbm, ins, out_wide, sum_sems, z, nc
    )
    gather = PlaneGather(wire_1, x_all, e)
    scatter_dx = PlaneScatter(wire_1, dx_land, ids)
    scatter_y = PlaneScatter(wire_2, y_land, ids)
    dg_slot = wire_1.slots(3)

    def token_phase(w_gu, w_dn, cot_all, a_all, dgu_all, y_stage, dx_part, stage):
        scatter_dx.part = lambda r, half: dx_part.at[
            r - 1, :, pl.ds(half * width // 2, width // 2)
        ]
        sources = [(expert_in_hbm, x_all.at[0])]
        for i in range(EXP_DEV):
            sources += [(w_gu_hbm.at[i], w_gu.at[i]), (w_dn_hbm.at[i], w_dn.at[i])]
            if i == 0:
                sources += [(cot_hbm.at[0], cot_all.at[0]), (cot_hbm.at[1:], cot_all.at[1:])]
        loads = [
            pltpu.make_async_copy(source, dest, load_sems.at[n])
            for n, (source, dest) in enumerate(sources)
        ]
        for copy in loads:
            copy.start()
        greet(
            [(ids[m], None) for m in (1, 2, 3)]
            + [(sibling, None), ({"context": flip(z, 2)}, None)]
            + [({"context": z + 1}, z < nc - 1), ({"context": z - 1}, z > 0)]
        )
        loads[0].wait()
        gather.spread()
        step = 256
        wide = 512
        dg_lanes[...] = jnp.zeros_like(dg_lanes)

        def hidden_units(r, i, count=1):
            here = pl.ds(r, count)
            flat = count * tokens

            @pl.loop(0, ff // step)
            def _(f):
                column = pl.multiple_of(f * step, step)
                rows = x_all[here].reshape(flat, width)
                grads = cot_all[here].reshape(flat, width)
                gate_part = dot_nn(rows, w_gu[i, :, pl.ds(column, step)])
                up_part = dot_nn(rows, w_gu[i, :, pl.ds(ff + column, step)])
                raw = dot_nt(grads, w_dn[i, pl.ds(column, step), :])
                gate = gates_ref[here].reshape(flat, SMALL)[:, i : i + 1]
                sigma = jax.nn.sigmoid(gate_part)
                silu = gate_part * sigma
                act = silu * up_part
                lanes = lax.broadcasted_iota(jnp.int32, (flat, SMALL), 1)
                d_gate = jnp.where(
                    lanes == e * EXP_DEV + i, jnp.sum(act * raw, -1, keepdims=True), 0.0
                )
                dg_lanes[here] += d_gate.reshape(count, tokens, SMALL)

                def put(ref, first, values):
                    values = values.astype(BF16).reshape(count, tokens, step)
                    ref[here, :, pl.ds(pl.multiple_of(first, step), step)] = values

                put(a_all, i * ff + column, act * gate)
                d_act = raw * gate
                d_gate_part = d_act * up_part * sigma * (1.0 + gate_part * (1.0 - sigma))
                put(dgu_all, i * 2 * ff + column, d_gate_part)
                put(dgu_all, i * 2 * ff + ff + column, d_act * silu)

        def y_copy(r):
            return pltpu.make_async_copy(y_stage.at[r % 2], y_hbm.at[r], y_sems.at[r % 2])

        def outputs(r, count=1):
            here = pl.ds(r, count)
            flat = count * tokens

            @pl.loop(0, width // wide)
            def _(n):
                columns = pl.ds(pl.multiple_of(n * wide, wide), wide)
                low = dgu_all[here].reshape(flat, EXP_DEV * 2 * ff)
                d_rows = dot_nt(low[:, : 2 * ff], w_gu[0, columns, :])
                d_rows += dot_nt(low[:, 2 * ff :], w_gu[1, columns, :])
                weight = w_dn[:, :, columns].reshape(EXP_DEV * ff, wide)
                out = dot_nn(a_all[here].reshape(flat, EXP_DEV * ff), weight).astype(BF16)
                for k in range(count):
                    rows = slice(k * tokens, (k + 1) * tokens)
                    y_stage[(r + k) % 2, :, columns] = out[rows]
                    if r == 0:
                        d_in_ref[:, columns] = d_rows
                    else:
                        dx_part[r + k - 1, :, columns] = d_rows[rows].astype(BF16)

            for k in range(r, r + count):
                y_copy(k).start()
                dg_part[k] = jnp.transpose(dg_lanes[k])[:GATE_ROWS]
                if k:
                    wire_1.start(dg_part.at[k], dg_land.at[k - 1], dg_slot + k - 1, ids[k])

        half_rows = width // nc // 2
        units = [(i, r) for i in range(EXP_DEV) for r in (3, 2, 1, 0)]

        def keep(u):
            i, r = units[u]
            return pltpu.make_async_copy(
                stage.at[u % 2, c], expert.part(base_hbm, flip(z, r), i), stage_sems.at[u % 2]
            )

        def hand(u):
            r = units[u][1]
            return pltpu.make_async_remote_copy(
                src_ref=stage.at[u % 2, 1 - c],
                dst_ref=core_land.at[r],
                send_sem=hand_sends.at[u],
                recv_sem=hand_recvs.at[u],
                device_id=sibling,
                device_id_type=MESH,
            )

        def weight_grads(u):
            i, r = units[u]
            columns = pl.ds(pl.multiple_of(flip(z, r) * 2 * half_rows, 2 * half_rows), 2 * half_rows)
            for first, source, grad, start, count in (
                (0, x_all, dgu_all, i * 2 * ff, 2),
                (2 * ff, cot_all, a_all, i * ff, 1),
            ):
                rows = source[:, :, columns].reshape(blocks * tokens, 2 * half_rows)

                @pl.loop(0, count)
                def _(n):
                    column = pl.multiple_of(n * ff, ff)
                    part = grad[:, :, pl.ds(pl.multiple_of(start + column, ff), ff)]
                    result = dot_tn(rows, part.reshape(blocks * tokens, ff)).astype(BF16)
                    stage[u % 2, :, :, pl.ds(pl.multiple_of(first + column, ff), ff)] = (
                        result.reshape(2, half_rows, ff)
                    )

            if u == nc:
                pl.semaphore_wait(credits.at[3], 1)
            hand(u).start()

        def settle(u):
            hand(u).wait_recv()
            r = units[u][1]
            mine = stage[u % 2, c].astype(F32) + core_land[r].astype(F32)
            stage[u % 2, c] = mine.astype(BF16)
            keep(u).start()

        def clear(u):
            keep(u).wait()
            hand(u).wait_send()
            i, r = units[u]
            if r in (3, 1):
                expert.send(i, r)
            elif r == 2:
                expert.send(i, r, when=expert.end)

        for copy in loads[1:4]:
            copy.wait()
        hidden_units(0, 0)
        for copy in loads[4:]:
            copy.wait()
        hidden_units(0, 1)
        gather.forward()
        outputs(0)
        gather.near(1)
        gather.near(2)
        hidden_units(1, 0, 2)
        gather.far()
        hidden_units(3, 0)
        weight_grads(0)
        weight_grads(1)
        settle(0)
        clear(0)
        weight_grads(2)
        settle(1)
        clear(1)
        weight_grads(3)
        settle(2)
        hidden_units(1, 1, 2)
        clear(2)
        settle(3)
        pl.semaphore_signal(credits.at[3], inc=1, device_id=sibling, device_id_type=MESH)
        y_copy(0).wait()
        outputs(1, 2)
        scatter_dx.near(1)
        scatter_dx.near(2)
        hidden_units(3, 1)
        expert.relay_begin(0)
        y_copy(1).wait()
        outputs(3)
        scatter_dx.far()
        clear(3)
        expert.relay_add()
        weight_grads(4)
        expert.relay_send(0)
        weight_grads(5)
        settle(4)
        scatter_dx.relay()
        clear(4)
        weight_grads(6)
        settle(5)
        clear(5)
        weight_grads(7)
        settle(6)
        scatter_dx.total(d_in_ref)
        for r in (1, 2):
            pl.semaphore_signal(credits.at[r], inc=1, device_id=ids[r], device_id_type=MESH)
        settle(7)
        clear(6)
        clear(7)
        y_copy(3).wait()
        y_copy(2).wait()
        wire_1.finish()
        pl.semaphore_signal(credits.at[0], inc=1, device_id=sibling, device_id_type=MESH)

    def token_rows_phase(
        weight,
        grads_o,
        grads_q,
        x_ref,
        inputs_ref,
        query_ref,
        kv_ref,
        heads_ref,
        hidden_ref,
        d_hidden_ref,
        d_attn_ref,
        d_heads_ref,
        d_all_ref,
        rows_ref,
        dkv_acc,
        dkv_ref,
        y_relay,
    ):
        cot_ref, d_inputs_ref = d_heads_ref, hidden_ref
        scatter_y.part = lambda r, half: y_hbm.at[r, :, pl.ds(half * width // 2, width // 2)]
        y_loads = [
            pltpu.make_async_copy(scatter_y.part(2 - half, half), y_relay.at[half], y_sems.at[half])
            for half in range(2)
        ]
        for copy in y_loads:
            copy.start()
        planes = grads_o.shape[1]
        part = width // planes
        sources = (
            (hidden_hbm, hidden_ref),
            (cot_hbm.at[0], cot_ref),
            (o_hbm, weight.at[:, pl.ds(0, width)]),
            (heads_hbm, heads_ref),
            (query_hbm, query_ref),
            (kv_hbm, kv_ref),
            (x_hbm, x_ref),
            (inputs_hbm, inputs_ref),
        )
        loads = [
            pltpu.make_async_copy(source, dest, load_sems.at[4 + n])
            for n, (source, dest) in enumerate(sources)
        ]
        for copy in loads:
            copy.start()
        for r in (1, 2):
            scatter_y.near(r)
        scatter_y.far()

        def rows_scatter(buf, core, plane, lines, start, count, half):
            return RowsScatter(
                wire_2,
                buf,
                core,
                plane,
                [lines.at[0], lines.at[1]],
                e,
                z,
                c,
                nc,
                start,
                count,
                half,
            )

        rows_of = part // 2
        scatter_o = rows_scatter(
            grads_o,
            x_all.at[:, pl.ds(0, rows_of)],
            lambda slot, half: dx_land.at[slot, pl.ds(0, rows_of)],
            lines_o,
            0,
            width,
            width // 2,
        )
        scatter_q = rows_scatter(
            grads_q,
            core_land.at[:, :, pl.ds(0, query_width)],
            lambda slot, half: plane_q.at[slot],
            lines_q,
            0,
            query_width,
            query_width // 2,
        )
        rest_half = rest // 256 * 128
        scatter_k = rows_scatter(
            grads_q,
            core_land.at[:, :, pl.ds(query_width, rest)],
            lambda slot, half: plane_k.at[
                slot, :, pl.ds(0, rest - rest_half if half else rest_half)
            ],
            lines_k,
            query_width,
            rest,
            rest_half,
        )
        scatter_kv = [
            LineScatter(
                wire_2,
                lambda j, h=h: dkv_ref.at[h, j],
                [dkv_land.at[h], dkv_land.at[h]],
                z,
                nc,
                up=False,
            )
            for h in range(KEY_VALUE_HEADS)
        ]

        loads[0].wait()
        loads[1].wait()
        hidden, d_in = hidden_ref[...], d_in_ref[...]
        scale2 = lax.rsqrt(jnp.mean(hidden * hidden, -1, keepdims=True) + EPSILON)
        scaled = d_in * gains_ref[1:2]
        mean = jnp.mean(scaled * hidden, -1, keepdims=True)
        d_hidden = cot_ref[...].astype(F32) + scale2 * scaled
        d_hidden = d_hidden - hidden * (scale2 * scale2 * scale2 * mean)
        d_hidden_ref[...] = d_hidden
        d_attn_ref[...] = d_hidden.astype(BF16)
        rows_ref[...] = jnp.zeros_like(rows_ref)
        rows_ref[experts + 1 : experts + 2, :] = jnp.sum(d_in * hidden * scale2, 0, keepdims=True)

        loads[2].wait()

        @pl.loop(0, query_width // 256)
        def _(n):
            columns = pl.ds(pl.multiple_of(n * 256, 256), 256)
            d_heads_ref[:, columns] = dot_nn(d_attn_ref[...], weight[:, columns]).astype(BF16)

        load_q = [
            pltpu.make_async_copy(wq_hbm, weight.at[:, pl.ds(0, query_width)], load_sems.at[0]),
            pltpu.make_async_copy(wk_hbm, weight.at[:, pl.ds(query_width, rest)], load_sems.at[1]),
        ]
        for copy in load_q:
            copy.start()
        loads[3].wait()

        def row_grads(buf, left, right, first, count, extra=None):
            @pl.loop(0, planes)
            def _(block):
                columns = pl.ds(pl.multiple_of(block * part, part), part)
                result = dot_tn(left[:, columns], right)
                if extra is not None:
                    result = result + extra(columns)
                result = result.astype(BF16).reshape(nc, 2, part // nc // 2, count)
                for half in range(2):
                    buf[half, block, :, pl.ds(first, count)] = result[:, half].reshape(
                        part // 2, count
                    )

        row_grads(grads_o, d_attn_ref, heads_ref[...], 0, width)
        pl.semaphore_wait(credits.at[0], 1)
        scatter_o.share()
        y_own = pltpu.make_async_copy(y_hbm.at[0], heads_ref, load_sems.at[2])
        y_own.start()

        length = nc * tokens
        group = QUERY_HEADS // KEY_VALUE_HEADS
        for copy in loads[4:6]:
            copy.wait()
        dkv_acc[...] = jnp.zeros_like(dkv_acc)

        def attend(j, first, last):
            key = kv_ref[j, :, :, pl.ds(0, size)].reshape(length, size)
            value = kv_ref[j, :, :, pl.ds(size, size)].reshape(length, size)

            @pl.loop(j * group + first, j * group + last)
            def _(h):
                columns = pl.ds(pl.multiple_of(h * size, size), size)
                query, grad = query_ref[:, columns], d_heads_ref[:, columns]
                probs = masked_probs(z * tokens, query, key)
                d_probs = dot_nt(grad, value)
                inner = jnp.sum(probs * d_probs, axis=-1, keepdims=True)
                d_raw = (probs * (d_probs - inner) * (size**-0.5)).astype(BF16)
                d_query = dot_nn(d_raw, key)
                d_query = d_query * cos_ref[...] - swap_halves(d_query) * sin_ref[...]
                d_all_ref[:, columns] = d_query.astype(BF16)
                dkv_acc[j, :, pl.ds(0, size)] += dot_tn(d_raw, query)
                dkv_acc[j, :, pl.ds(size, size)] += dot_tn(probs.astype(BF16), grad)

        def round_kv(j):
            for block in range(nc):
                rows = dkv_acc[j, pl.ds(block * tokens, tokens), :]
                dkv_ref[j, block] = rows.astype(BF16)

        def enter():
            pl.semaphore_wait(credits.at[1], 1)
            pl.semaphore_wait(credits.at[2], 1)

        attend(0, 0, group)
        round_kv(0)
        scatter_kv[0].step(1)
        scatter_o.merge(enter)
        for copy in y_loads:
            copy.wait()
        scatter_y.relay(lambda r, half: y_relay.at[half])
        attend(1, 0, group // 2)
        scatter_kv[0].step(2)
        attend(1, group // 2, group)
        round_kv(1)
        scatter_kv[1].step(1)
        scatter_kv[0].step(3)
        scatter_o.relay()

        for copy in loads[6:]:
            copy.wait()
        row_grads(grads_q, inputs_ref, d_all_ref[:, pl.ds(0, query_width)], 0, query_width)
        scatter_q.share()
        scatter_kv[1].step(2)
        scatter_kv[1].step(3)
        expert.relay_begin(1)
        y_own.wait()
        hidden_ref[...] += heads_ref[...].astype(F32)
        scatter_y.total(hidden_ref)
        layer_ref[...] = hidden_ref[...].astype(BF16)
        scatter_o.total()
        scatter_q.merge()
        for h in range(KEY_VALUE_HEADS):
            scatter_kv[h].last()
        expert.relay_add()
        expert.relay_send(1)

        for h in range(KEY_VALUE_HEADS):
            grad = dkv_ref[h, z, :, pl.ds(0, size)].astype(F32)
            grad = grad * cos_ref[...] - swap_halves(grad) * sin_ref[...]
            d_all_ref[:, pl.ds(query_width + h * size, size)] = grad.astype(BF16)
            d_all_ref[:, pl.ds(query_width + key_width + h * size, size)] = dkv_ref[
                h, z, :, pl.ds(size, size)
            ]

        total = dg_part[0]
        for r in (1, 2, 3):
            wire_1.arrived(dg_land.at[r - 1], dg_slot + r - 1, ids[r])
            total = total + dg_land[r - 1]
        gates = gate_ref[0]
        d_logits = gates * (total - jnp.sum(gates * total, 0, keepdims=True))
        d_logits = jnp.concatenate(
            [d_logits, jnp.zeros((SMALL - d_logits.shape[0], tokens), F32)], 0
        )
        d_all_ref[:, pl.ds(qkv_width, SMALL)] = jnp.transpose(d_logits).astype(BF16)

        for copy in load_q:
            copy.wait()

        @pl.loop(0, planes)
        def _(block):
            columns = pl.ds(pl.multiple_of(block * part, part), part)
            d_inputs_ref[:, columns] = dot_nt(d_all_ref[...], weight[columns, :])

        rows = x_ref[...].astype(F32)
        scale1 = lax.rsqrt(jnp.mean(rows * rows, -1, keepdims=True) + EPSILON)
        d_inputs = d_inputs_ref[...]
        rows_ref[experts : experts + 1, :] = jnp.sum(d_inputs * rows * scale1, 0, keepdims=True)

        def extra(columns):
            small = jnp.transpose(rows_ref[:, columns])
            return jnp.concatenate([jnp.zeros((part, rest - SMALL), F32), small], 1)

        row_grads(
            grads_q, inputs_ref, d_all_ref[:, pl.ds(query_width, rest)], query_width, rest, extra
        )
        scatter_k.share()
        scatter_q.relay()
        scatter_k.merge()
        scaled = d_inputs_ref[...] * gains_ref[0:1]
        rows = x_ref[...].astype(F32)
        scale1 = lax.rsqrt(jnp.mean(rows * rows, -1, keepdims=True) + EPSILON)
        mean = jnp.mean(scaled * rows, -1, keepdims=True)
        d_x = d_hidden_ref[...] + scale1 * scaled - rows * (scale1 * scale1 * scale1 * mean)
        d_x_ref[...] = d_x.astype(BF16)
        scatter_q.total()
        expert.last(0, (sum_gu_hbm, sum_dn_hbm))
        scatter_k.relay()
        scatter_o.line.step(1)
        scatter_q.line.step(1)
        scatter_k.total()
        scatter_k.line.step(1)
        for s in range(2, nc):
            for scatter in (scatter_o, scatter_q, scatter_k):
                scatter.line.step(s)
        for scatter in (scatter_o, scatter_q, scatter_k):
            scatter.line.last()
        sum_o_ref[...] = scatter_o.line.block(z)[...].astype(F32)
        sum_q_ref[...] = grads_q[c, e, pl.ds(pl.multiple_of(z * (rows_of // nc), rows_of // nc), rows_of // nc)].astype(F32)
        expert.last(1, (sum_gu_hbm, sum_dn_hbm))
        wire_2.finish()
        expert.finish()

    held = EXP_DEV
    pl.run_scoped(
        token_phase,
        pltpu.VMEM((held, width, 2 * ff), BF16),
        pltpu.VMEM((held, ff, width), BF16),
        pltpu.VMEM((blocks, tokens, width), BF16),
        pltpu.VMEM((blocks, tokens, held * ff), BF16),
        pltpu.VMEM((blocks, tokens, held * 2 * ff), BF16),
        pltpu.VMEM((2, tokens, width), BF16),
        pltpu.VMEM((blocks - 1, tokens, width), BF16),
        pltpu.VMEM((2, 2, width // nc // 2, grad_width // held), BF16),
    )
    rows_half = width // blocks // 2
    pl.run_scoped(
        token_rows_phase,
        pltpu.VMEM((width, qkv_width + SMALL), BF16),
        pltpu.VMEM((2, blocks, rows_half, width), BF16),
        pltpu.VMEM((2, blocks, rows_half, qkv_width + SMALL), BF16),
        pltpu.VMEM((tokens, width), BF16),
        pltpu.VMEM((tokens, width), BF16),
        pltpu.VMEM((tokens, query_width), BF16),
        pltpu.VMEM((KEY_VALUE_HEADS, nc, tokens, 2 * size), BF16),
        pltpu.VMEM((tokens, query_width), BF16),
        pltpu.VMEM((tokens, width), F32),
        pltpu.VMEM((tokens, width), F32),
        pltpu.VMEM((tokens, width), BF16),
        pltpu.VMEM((tokens, query_width), BF16),
        pltpu.VMEM((tokens, qkv_width + SMALL), BF16),
        pltpu.VMEM((SMALL, width), F32),
        pltpu.VMEM((KEY_VALUE_HEADS, nc * tokens, 2 * size), F32),
        pltpu.VMEM((KEY_VALUE_HEADS, nc, tokens, 2 * size), BF16),
        pltpu.VMEM((2, tokens, width // 2), BF16),
    )


def back(operands, sizes):
    ne, nc, nd = sizes
    cot, w_gu, w_dn, x = operands[6], operands[7], operands[8], operands[9]
    tokens, width = x.shape
    held, ff = w_dn.shape[0], w_dn.shape[1]
    rest = operands[15].shape[-1]
    q_width = QUERY_HEADS * HEAD_DIMENSION + rest
    rows = width // (ne * nc * nd)
    rest_half = rest // 256 * 128
    shard, grads = width // (nc * nd), held * 3 * ff
    kv_size = 2 * HEAD_DIMENSION
    shapes = [
        ((tokens, width), BF16),
        ((tokens, width), BF16),
        ((rows, q_width), F32),
        ((rows, width), F32),
        ((held, shard, 2 * ff), F32),
        ((held, shard, ff), F32),
        ((nc, shard, grads), BF16),
        ((nc + 1, shard, grads), BF16),
        ((ne, tokens, width), BF16),
    ]
    vmem = pl.BlockSpec(memory_space=pltpu.VMEM)
    anywhere = pl.BlockSpec(memory_space=pl.ANY)
    step, units = 48, nc * held
    return pl.pallas_call(
        functools.partial(back_kernel, nc, EXP_DEV * ne),
        out_shape=[jax.ShapeDtypeStruct(*s) for s in shapes],
        in_specs=[vmem] * 5 + [anywhere] * (len(operands) - 5),
        out_specs=[vmem] * 4 + [anywhere] * 5,
        scratch_shapes=[
            pltpu.VMEM((ne, tokens, width), BF16),
            pltpu.VMEM((6, tokens, width // 2), BF16),
            pltpu.VMEM((6, tokens, width // 2), BF16),
            pltpu.VMEM((nc, shard, grads // held), BF16),
            pltpu.VMEM((6, nc * rows, QUERY_HEADS * HEAD_DIMENSION // 2), BF16),
            pltpu.VMEM((6, nc * rows, rest - rest_half), BF16),
            pltpu.VMEM((2, nc - 1, rows, width), BF16),
            pltpu.VMEM((2, nc - 1, rows, QUERY_HEADS * HEAD_DIMENSION), BF16),
            pltpu.VMEM((2, nc - 1, rows, rest), BF16),
            pltpu.VMEM((KEY_VALUE_HEADS, nc - 1, tokens, kv_size), BF16),
            pltpu.VMEM((tokens, width), F32),
            pltpu.VMEM((ne, tokens, SMALL), F32),
            pltpu.VMEM((ne, GATE_ROWS, tokens), F32),
            pltpu.VMEM((ne - 1, GATE_ROWS, tokens), F32),
            pltpu.VMEM((4, 2, step, grads // held), BF16),
            pltpu.VMEM((2, step, grads // held), F32),
            pltpu.SemaphoreType.DMA((32,)),
            pltpu.SemaphoreType.DMA((32,)),
            pltpu.SemaphoreType.DMA((64,)),
            pltpu.SemaphoreType.DMA((64,)),
            pltpu.SemaphoreType.DMA((units + held,)),
            pltpu.SemaphoreType.DMA(((nc + 1) * held,)),
            pltpu.SemaphoreType.DMA((units,)),
            pltpu.SemaphoreType.DMA((units,)),
            pltpu.SemaphoreType.DMA((2,)),
            pltpu.SemaphoreType.DMA((12,)),
            pltpu.SemaphoreType.DMA((12,)),
            pltpu.SemaphoreType.DMA((2,)),
            pltpu.SemaphoreType.REGULAR((4,)),
        ],
        compiler_params=pltpu.CompilerParams(
            collective_id=1, has_side_effects=True, vmem_limit_bytes=63 * MIB
        ),
    )(*operands)


def local_plain(
    layer_input,
    gain_attn,
    query_key_value_weight,
    w_out,
    w_router,
    gain_ffn,
    w_gate_up,
    w_down,
    routes,
    d_out,
):
    tokens = layer_input.shape[1]
    model_width = layer_input.shape[2]
    ne, nc, nd = (lax.axis_size(a) for a in ("expert", "context", "dp"))
    expert_total = EXP_DEV * ne
    ff = w_down.shape[1]
    me = lax.axis_index("expert")
    first_row = lax.axis_index("context") * tokens
    query_width = QUERY_HEADS * HEAD_DIMENSION
    key_width = KEY_VALUE_HEADS * HEAD_DIMENSION
    qkv_width = query_width + 2 * key_width

    small = jnp.concatenate([w_router, gain_attn[:, None], gain_ffn[:, None]], -1)
    small = jnp.pad(small, ((0, 0), (0, 128 - small.shape[1])))
    gathered = gather_rows(jnp.concatenate([query_key_value_weight, small], -1))
    out_turned = gather_rows(w_out.T)
    qkv_weight = gathered[:, :qkv_width]
    router_weight = gathered[:, qkv_width : qkv_width + expert_total]
    gains = gathered[:, qkv_width + expert_total : qkv_width + expert_total + 2].T.astype(F32)
    gain_first, gain_second = gains[0], gains[1]
    cotangent_all = plane_gather(d_out[0])

    token_rows = layer_input[0].astype(F32)
    scale1 = lax.rsqrt(jnp.mean(token_rows * token_rows, -1, keepdims=True) + EPSILON)
    inputs1 = (token_rows * scale1 * gain_first).astype(BF16)
    query_key_value = dot_nn(inputs1, qkv_weight)
    cosine_values, sine_values = rope_tables(first_row + jnp.arange(tokens), HEAD_DIMENSION)
    rotated = rotate_half(
        query_key_value[:, : query_width + key_width].reshape(tokens, -1, HEAD_DIMENSION),
        cosine_values,
        sine_values,
    ).reshape(tokens, -1)
    query = rotated[:, :query_width].astype(BF16)
    key_value_local = jnp.concatenate(
        [rotated[:, query_width:], query_key_value[:, query_width + key_width :]], -1
    ).astype(BF16)
    key_value = line_gather(key_value_local, "context", both=False).reshape(nc * tokens, -1)
    first = first_row.astype(jnp.int32).reshape(1)
    heads = attend_forward(first, query, key_value)

    logits = dot_nn(inputs1, router_weight)
    chosen_ids = routes[0]
    picks = (chosen_ids[:, :, None] == jnp.arange(expert_total)[None, None, :]).astype(F32)
    chosen = jnp.sum(picks * logits[:, None, :], -1)
    gates = jax.nn.softmax(chosen, axis=-1)
    gate_dense = jnp.sum(picks * gates[:, :, None], 1).T
    gate_blocks = cube_gather(gate_dense, "expert", axis_masks("expert"))
    gate_local = jnp.concatenate(
        [lax.dynamic_slice_in_dim(b, me * EXP_DEV, EXP_DEV, 0) for b in gate_blocks], 1
    )

    attn = dot_nt(heads, out_turned)
    hidden = token_rows + attn
    scale2 = lax.rsqrt(jnp.mean(hidden * hidden, -1, keepdims=True) + EPSILON)
    expert_in = (hidden * scale2 * gain_second).astype(BF16)

    rows_all = plane_gather(expert_in)
    gate_up = jnp.einsum("td,edf->etf", rows_all, w_gate_up, preferred_element_type=F32)
    gate_part, up_part = gate_up[..., :ff], gate_up[..., ff:]
    sigma = jax.nn.sigmoid(gate_part)
    silu = gate_part * sigma
    act = silu * up_part
    gate_column = gate_local[:, :, None]
    act_gated = (act * gate_column).astype(BF16)
    partial_out = jnp.einsum("etf,efd->td", act_gated, w_down, preferred_element_type=F32)
    mixture = plane_scatter(partial_out.astype(BF16), tokens)
    layer_result = (hidden + mixture).astype(BF16)

    d_act_raw = jnp.einsum("td,efd->etf", cotangent_all, w_down, preferred_element_type=F32)
    d_gates_local = jnp.sum(d_act_raw * act, -1)
    d_act = d_act_raw * gate_column
    d_gate_part = d_act * up_part * sigma * (1.0 + gate_part * (1.0 - sigma))
    d_up_part = d_act * silu
    d_gate_up = jnp.concatenate([d_gate_part, d_up_part], -1).astype(BF16)
    d_rows = jnp.einsum("etf,edf->td", d_gate_up, w_gate_up, preferred_element_type=F32)
    grad_down = jnp.einsum("td,etf->edf", cotangent_all, act_gated, preferred_element_type=F32)
    grad_gate_up = jnp.einsum("td,etf->edf", rows_all, d_gate_up, preferred_element_type=F32)

    d_expert_in = plane_scatter(d_rows.astype(BF16), tokens)
    d_gate_blocks = d_gates_local.reshape(EXP_DEV, ne, tokens)
    d_gates_dense = jnp.zeros((expert_total, tokens), F32)
    for r in range(ne):
        arrived = d_gate_blocks[:, r]
        if r:
            arrived = exchange(arrived, "expert", r)
        d_gates_dense = lax.dynamic_update_slice(d_gates_dense, arrived, ((me ^ r) * EXP_DEV, 0))
    d_gates = jnp.sum(picks * d_gates_dense.T[:, None, :], -1)
    d_chosen = gates * (d_gates - jnp.sum(gates * d_gates, -1, keepdims=True))
    d_logits = jnp.sum(picks * d_chosen[:, :, None], 1).astype(BF16)
    grad_router = dot_tn(inputs1, d_logits)

    core = lax.axis_index("dp")
    part = model_width // (nc * nd)

    def scatter_experts(grad):
        blocks = grad.reshape(EXP_DEV, nc, nd, part, -1)
        mine = cube_scatter(
            [lax.dynamic_index_in_dim(blocks, core ^ r, 2, keepdims=False) for r in range(nd)],
            "dp",
            axis_masks("dp"),
        )
        return line_scatter(
            lambda j: lax.dynamic_index_in_dim(mine, j, 1, keepdims=False), "context"
        )

    sum_gate_up = scatter_experts(grad_gate_up)
    sum_down = jnp.swapaxes(scatter_experts(grad_down), 1, 2)

    cotangent = d_out[0].astype(F32)
    scaled2 = d_expert_in * gain_second
    d_hidden = (
        cotangent
        + scale2 * scaled2
        - hidden * (scale2 * scale2 * scale2) * jnp.mean(scaled2 * hidden, -1, keepdims=True)
    )
    grad_gain_second = jnp.sum(d_expert_in * hidden * scale2, 0)
    d_attn = d_hidden.astype(BF16)
    grad_out_turned = dot_tn(d_attn, heads)
    sum_out = scatter_rows(grad_out_turned).T
    d_heads = dot_nn(d_attn, out_turned).astype(BF16)
    d_query, d_key_all, d_value_all = attend_backward(first, query, key_value, d_heads)
    d_key_value_all = jnp.concatenate([d_key_all, d_value_all], -1).reshape(nc, tokens, -1)
    d_key_value = line_scatter(
        lambda j: lax.dynamic_index_in_dim(d_key_value_all, j, 0, keepdims=False),
        "context",
        up=False,
    )
    d_rotated = rotate_back(
        jnp.concatenate([d_query, d_key_value[:, :key_width]], -1).reshape(
            tokens, -1, HEAD_DIMENSION
        ),
        cosine_values,
        sine_values,
    ).reshape(tokens, -1)
    d_qkv = jnp.concatenate([d_rotated, d_key_value[:, key_width:]], -1).astype(BF16)
    d_inputs = dot_nt(d_qkv, qkv_weight) + dot_nt(d_logits, router_weight)
    grad_gain_first = jnp.sum(d_inputs * token_rows * scale1, 0)
    grad_qkv = dot_tn(inputs1, d_qkv)
    small_grads = jnp.concatenate(
        [grad_router, grad_gain_first[:, None], grad_gain_second[:, None]], -1
    )
    small_grads = jnp.pad(small_grads, ((0, 0), (0, 128 - small_grads.shape[1])))
    sum_rows = scatter_rows(jnp.concatenate([grad_qkv, small_grads], -1))
    sum_qkv = sum_rows[:, :qkv_width]
    sum_router = sum_rows[:, qkv_width : qkv_width + expert_total]
    sum_gain_first = sum_rows[:, qkv_width + expert_total]
    sum_gain_second = sum_rows[:, qkv_width + expert_total + 1]
    scaled1 = d_inputs * gain_first
    d_input_rows = (
        d_hidden
        + scale1 * scaled1
        - token_rows
        * (scale1 * scale1 * scale1)
        * jnp.mean(scaled1 * token_rows, -1, keepdims=True)
    ).astype(BF16)
    return (
        layer_result[None],
        d_input_rows[None],
        sum_gain_first,
        sum_qkv,
        sum_out,
        sum_router,
        sum_gain_second,
        sum_gate_up,
        sum_down,
    )


def local_fused(
    layer_input,
    gain_attn,
    query_key_value_weight,
    w_out,
    w_router,
    gain_ffn,
    w_gate_up,
    w_down,
    routes,
    d_out,
):
    tokens = layer_input.shape[1]
    ne, nc, nd = sizes = tuple(lax.axis_size(a) for a in ("expert", "context", "dp"))
    expert_total = EXP_DEV * ne
    first_row = lax.axis_index("context") * tokens
    query_width = QUERY_HEADS * HEAD_DIMENSION
    key_width = KEY_VALUE_HEADS * HEAD_DIMENSION
    qkv_width = query_width + 2 * key_width

    small = jnp.concatenate([w_router, gain_attn[:, None], gain_ffn[:, None]], -1)
    small = jnp.pad(small, ((0, 0), (0, SMALL - small.shape[1])))
    cosine_values, sine_values = rope_tables(first_row + jnp.arange(tokens), HEAD_DIMENSION)
    sine_values = sine_values * jnp.where(
        jnp.arange(HEAD_DIMENSION) < HEAD_DIMENSION // 2, -1.0, 1.0
    )
    (
        wk_all,
        wq_all,
        wo_all,
        cotangent_all,
        gate_all,
        gate_columns,
        inputs1,
        query,
        key_value,
        heads,
        hidden,
        expert_in,
        gains,
    ) = front(
        (
            layer_input[0],
            query_key_value_weight,
            small,
            w_out.T,
            d_out[0],
            cosine_values,
            sine_values,
            routes[0].T,
        ),
        sizes,
    )
    layer_result, d_x, sum_rows, sum_out, sum_gate_up, sum_down = back(
        (
            gate_columns,
            gate_all,
            gains,
            cosine_values,
            sine_values,
            expert_in,
            cotangent_all,
            w_gate_up,
            w_down,
            layer_input[0],
            inputs1,
            query,
            key_value,
            heads,
            hidden,
            wk_all.reshape(-1, wk_all.shape[-1]),
            wq_all.reshape(-1, query_width),
            wo_all.reshape(-1, wo_all.shape[-1]),
        ),
        sizes,
    )[:6]
    return (
        layer_result[None],
        d_x[None],
        sum_rows[:, qkv_width + expert_total],
        sum_rows[:, :qkv_width],
        sum_out.T,
        sum_rows[:, qkv_width : qkv_width + expert_total],
        sum_rows[:, qkv_width + expert_total + 1],
        sum_gate_up,
        jnp.swapaxes(sum_down, 1, 2),
    )


def solution(mesh):
    in_specs = (
        P(("expert", "dp"), "context", None),
        P(("expert", "context", "dp")),
        P(("expert", "context", "dp"), None),
        P(None, ("expert", "context", "dp")),
        P(("expert", "context", "dp"), None),
        P(("expert", "context", "dp")),
        P("expert", None, None),
        P("expert", None, None),
        P(("expert", "dp"), "context", None),
        P(("expert", "dp"), "context", None),
    )
    out_specs = (
        P(("expert", "dp"), "context", None),
        P(("expert", "dp"), "context", None),
        P(("expert", "context", "dp")),
        P(("expert", "context", "dp"), None),
        P(None, ("expert", "context", "dp")),
        P(("expert", "context", "dp"), None),
        P(("expert", "context", "dp")),
        P("expert", ("context", "dp"), None),
        P("expert", None, ("context", "dp")),
    )
    sizes = tuple(mesh.shape[a] for a in ("expert", "context", "dp"))
    local = local_fused if sizes == (4, 4, 2) else local_plain
    return jax.shard_map(local, mesh=mesh, in_specs=in_specs, out_specs=out_specs, check_vma=False)
```

```python
import functools
import math

import jax
import jax.numpy as jnp
from jax import lax
from jax.experimental import pallas as pl
from jax.experimental.pallas import tpu as pltpu
from jax.sharding import PartitionSpec as P

QUERY_HEADS = 12
KEY_VALUE_HEADS = 2
HEAD_DIMENSION = 128
TOP = 4
EXP_DEV = 2

EPSILON = 1e-06
ROPE_BASE = 10000.0
MASKED = -1e30

F32 = jnp.float32
BF16 = jnp.bfloat16


def rope_tables(positions, width):
    halfway = width // 2
    fraction = jnp.arange(halfway, dtype=jnp.float32) * (2.0 / width)
    frequency = jnp.exp(-math.log(ROPE_BASE) * fraction)
    angles = positions.astype(jnp.float32)[:, None] * frequency[None, :]
    cosine_values = jnp.cos(angles)
    sine_values = jnp.sin(angles)
    return (
        jnp.concatenate([cosine_values, cosine_values], -1),
        jnp.concatenate([sine_values, sine_values], -1),
    )


def rotate_half(values, cosine_values, sine_values):
    halfway = values.shape[-1] // 2
    turned = jnp.concatenate([-values[..., halfway:], values[..., :halfway]], -1)
    return values * cosine_values[:, None, :] + turned * sine_values[:, None, :]


def rotate_back(grads, cosine_values, sine_values):
    halfway = grads.shape[-1] // 2
    scaled = grads * sine_values[:, None, :]
    turned = jnp.concatenate([scaled[..., halfway:], -scaled[..., :halfway]], -1)
    return grads * cosine_values[:, None, :] + turned


def dot_nt(a, b):
    return lax.dot_general(a, b, (((1,), (1,)), ((), ())), preferred_element_type=F32)


def dot_tn(a, b):
    return lax.dot_general(a, b, (((0,), (0,)), ((), ())), preferred_element_type=F32)


def dot_nn(a, b):
    return jnp.dot(a, b, preferred_element_type=F32)


def masked_probs(first_row, query, key):
    scores = dot_nt(query, key) * (HEAD_DIMENSION**-0.5)
    rows = first_row + lax.broadcasted_iota(jnp.int32, scores.shape, 0)
    columns = lax.broadcasted_iota(jnp.int32, scores.shape, 1)
    scores = jnp.where(columns <= rows, scores, MASKED)
    expd = jnp.exp(scores - jnp.max(scores, axis=-1, keepdims=True))
    return expd / jnp.sum(expd, axis=-1, keepdims=True)


def attend_forward_kernel(first_ref, query_ref, key_ref, value_ref, heads_ref):
    probs = masked_probs(first_ref[0], query_ref[...], key_ref[...])
    heads_ref[...] = dot_nn(probs.astype(BF16), value_ref[...]).astype(BF16)


def attend_forward(first_row, query, key_value):
    tokens, width = query.shape
    length = key_value.shape[0]
    group = QUERY_HEADS // KEY_VALUE_HEADS
    size = HEAD_DIMENSION
    return pl.pallas_call(
        attend_forward_kernel,
        grid_spec=pltpu.PrefetchScalarGridSpec(
            num_scalar_prefetch=1,
            grid=(QUERY_HEADS,),
            in_specs=[
                pl.BlockSpec((tokens, size), lambda h, s: (0, h)),
                pl.BlockSpec((length, size), lambda h, s: (0, h // group)),
                pl.BlockSpec((length, size), lambda h, s: (0, KEY_VALUE_HEADS + h // group)),
            ],
            out_specs=pl.BlockSpec((tokens, size), lambda h, s: (0, h)),
        ),
        out_shape=jax.ShapeDtypeStruct((tokens, width), BF16),
        compiler_params=pltpu.CompilerParams(vmem_limit_bytes=32 * 1024 * 1024),
        cost_estimate=pl.CostEstimate(
            flops=4 * tokens * length * width, bytes_accessed=4 * tokens * width, transcendentals=0
        ),
    )(first_row, query, key_value, key_value)


def attend_backward_kernel(
    first_ref, query_ref, key_ref, value_ref, grad_ref, d_query_ref, d_key_ref, d_value_ref
):
    query, key, value, grad = query_ref[...], key_ref[...], value_ref[...], grad_ref[...]
    probs = masked_probs(first_ref[0], query, key)
    d_probs = dot_nt(grad, value)
    inner = jnp.sum(probs * d_probs, axis=-1, keepdims=True)
    d_raw = (probs * (d_probs - inner) * (HEAD_DIMENSION**-0.5)).astype(BF16)
    d_query_ref[...] = dot_nn(d_raw, key)
    d_key = dot_tn(d_raw, query)
    d_value = dot_tn(probs.astype(BF16), grad)

    @pl.when(pl.program_id(1) == 0)
    def _():
        d_key_ref[...] = d_key
        d_value_ref[...] = d_value

    @pl.when(pl.program_id(1) > 0)
    def _():
        d_key_ref[...] += d_key
        d_value_ref[...] += d_value


def attend_backward(first_row, query, key_value, grad):
    tokens, width = query.shape
    length = key_value.shape[0]
    group = QUERY_HEADS // KEY_VALUE_HEADS
    size = HEAD_DIMENSION
    row_spec = pl.BlockSpec((tokens, size), lambda j, g, s: (0, j * group + g))
    return pl.pallas_call(
        attend_backward_kernel,
        grid_spec=pltpu.PrefetchScalarGridSpec(
            num_scalar_prefetch=1,
            grid=(KEY_VALUE_HEADS, group),
            in_specs=[
                row_spec,
                pl.BlockSpec((length, size), lambda j, g, s: (0, j)),
                pl.BlockSpec((length, size), lambda j, g, s: (0, KEY_VALUE_HEADS + j)),
                row_spec,
            ],
            out_specs=[
                row_spec,
                pl.BlockSpec((length, size), lambda j, g, s: (0, j)),
                pl.BlockSpec((length, size), lambda j, g, s: (0, j)),
            ],
        ),
        out_shape=[
            jax.ShapeDtypeStruct((tokens, width), F32),
            jax.ShapeDtypeStruct((length, KEY_VALUE_HEADS * size), F32),
            jax.ShapeDtypeStruct((length, KEY_VALUE_HEADS * size), F32),
        ],
        compiler_params=pltpu.CompilerParams(vmem_limit_bytes=32 * 1024 * 1024),
        cost_estimate=pl.CostEstimate(
            flops=10 * tokens * length * width, bytes_accessed=8 * tokens * width, transcendentals=0
        ),
    )(first_row, query, key_value, key_value, grad)


def exchange(values, axis, mask):
    size = lax.axis_size(axis)
    return lax.ppermute(values, axis, [(i, i ^ mask) for i in range(size)])


def axis_masks(axis):
    size = lax.axis_size(axis)
    masks, bit = [], 1
    while bit < size:
        masks.append(bit)
        bit *= 2
    return masks


def cube_gather(values, axis, masks):
    held = {0: values}
    for mask in masks:
        for r, block in list(held.items()):
            held[r ^ mask] = exchange(block, axis, mask)
    return [held[r] for r in range(lax.axis_size(axis))]


def cube_scatter(blocks, axis, masks):
    held = dict(enumerate(blocks))
    for mask in masks:
        kept = {}
        for r in list(held):
            if not r & mask:
                arrived = exchange(held[r ^ mask].astype(BF16), axis, mask)
                kept[r] = held[r].astype(F32) + arrived.astype(F32)
        held = kept
    return held[0]


def line_steps(values, axis, up):
    size = lax.axis_size(axis)
    pairs = [(i, i + 1) if up else (i + 1, i) for i in range(size - 1)]
    return lax.ppermute(values, axis, pairs)


def line_gather(values, axis, both=True):
    size = lax.axis_size(axis)
    me = lax.axis_index(axis)
    result = jnp.zeros((size + 1,) + values.shape, values.dtype)
    result = lax.dynamic_update_index_in_dim(result, values, me, 0)
    up = down = values
    for step in range(1, size):
        up = line_steps(up, axis, True)
        result = lax.dynamic_update_index_in_dim(
            result, up, jnp.where(me - step >= 0, me - step, size), 0
        )
        if both:
            down = line_steps(down, axis, False)
            result = lax.dynamic_update_index_in_dim(result, down, jnp.minimum(me + step, size), 0)
    return result[:size]


def line_scatter(take, axis, up=True, down=True):
    size = lax.axis_size(axis)
    me = lax.axis_index(axis)
    total = take(me).astype(F32)
    for active, sign in ((up, 1), (down, -1)):
        if not active:
            continue
        arrived = None
        for step in range(1, size):
            block = take((me + sign * (size - step)) % size).astype(F32)
            if arrived is not None:
                block = block + arrived.astype(F32)
            arrived = line_steps(block.astype(BF16), axis, sign > 0)
        total = total + arrived.astype(F32)
    return total


def gather_rows(shard):
    ne, nc, nd = (lax.axis_size(a) for a in ("expert", "context", "dp"))
    rows, width = shard.shape
    lines = line_gather(shard, "context")
    masks = axis_masks("expert")
    half = width // 256 * 128
    parts = [lines[..., :half], lines[..., half:]]
    me = lax.axis_index("expert")
    result = jnp.zeros((ne, nc, rows, width), shard.dtype)
    for start, part, order in ((0, parts[0], masks), (half, parts[1], masks[::-1])):
        for r, block in enumerate(cube_gather(part, "expert", order)):
            result = lax.dynamic_update_slice(result, block[None], (me ^ r, 0, 0, start))
    core = lax.axis_index("dp")
    whole = jnp.zeros((ne, nc, nd, rows, width), shard.dtype)
    for r, block in enumerate(cube_gather(result, "dp", axis_masks("dp"))):
        whole = lax.dynamic_update_slice(whole, block[:, :, None], (0, 0, core ^ r, 0, 0))
    return whole.reshape(-1, width)


def scatter_rows(grad):
    ne, nc, nd = (lax.axis_size(a) for a in ("expert", "context", "dp"))
    width = grad.shape[-1]
    rows = grad.shape[0] // (ne * nc * nd)
    blocks = grad.reshape(ne, nc, nd, rows, width)
    core, me = lax.axis_index("dp"), lax.axis_index("expert")
    mine = cube_scatter(
        [
            lax.dynamic_index_in_dim(blocks, core ^ r, 2, keepdims=False)
            for r in range(nd)
        ],
        "dp",
        axis_masks("dp"),
    )
    masks = axis_masks("expert")
    half = width // 256 * 128
    sums = []
    for part, order in ((mine[..., :half], masks), (mine[..., half:], masks[::-1])):
        sums.append(
            cube_scatter(
                [lax.dynamic_index_in_dim(part, me ^ r, 0, keepdims=False) for r in range(ne)],
                "expert",
                order,
            )
        )
    lines = jnp.concatenate(sums, -1)
    return line_scatter(
        lambda j: lax.dynamic_index_in_dim(lines, j, 0, keepdims=False), "context"
    )


def plane_gather(rows):
    masks = axis_masks("expert")
    half = rows.shape[-1] // 2
    left = cube_gather(rows[:, :half], "expert", masks)
    right = cube_gather(rows[:, half:], "expert", masks[::-1])
    return jnp.concatenate([jnp.concatenate(p, -1) for p in zip(left, right)], 0)


def plane_scatter(partial, tokens):
    masks = axis_masks("expert")
    size = lax.axis_size("expert")
    half = partial.shape[-1] // 2
    blocks = partial.reshape(size, tokens, -1)
    left = cube_scatter([blocks[r, :, :half] for r in range(size)], "expert", masks)
    right = cube_scatter([blocks[r, :, half:] for r in range(size)], "expert", masks[::-1])
    return jnp.concatenate([left, right], -1)


MESH = pl.DeviceIdType.MESH
MIB = 1024 * 1024
SMALL = 128
GATE_ROWS = 16


def flip(index, mask):
    bit = 1
    while bit <= mask:
        if mask & bit:
            index = index + bit - 2 * bit * lax.rem(lax.div(index, bit), 2)
        bit *= 2
    return index


class Wire:
    def __init__(self, sends, recvs):
        self.sends, self.recvs = sends, recvs
        self.n_sends = self.n_recvs = 0
        self.open = []

    def slots(self, count):
        first = self.n_recvs
        self.n_recvs += count
        return first

    def start(self, src, dst, recv, device, when=None):
        copy = pltpu.make_async_remote_copy(
            src_ref=src,
            dst_ref=dst,
            send_sem=self.sends.at[self.n_sends],
            recv_sem=self.recvs.at[recv],
            device_id=device,
            device_id_type=MESH,
        )
        self.n_sends += 1
        guard(when, copy.start)
        self.open.append((when, copy))

    def arrived(self, dst, recv, device):
        pltpu.make_async_remote_copy(
            src_ref=dst,
            dst_ref=dst,
            send_sem=self.sends.at[0],
            recv_sem=self.recvs.at[recv],
            device_id=device,
            device_id_type=MESH,
        ).wait_recv()

    def finish(self):
        for when, copy in self.open:
            guard(when, copy.wait_send)
        self.open = []


def guard(when, action):
    if when is None:
        action()
    else:
        pl.when(when)(action)


def greet(targets):
    barrier = pltpu.get_barrier_semaphore()
    for device, when in targets:
        guard(
            when,
            lambda device=device: pl.semaphore_signal(
                barrier, inc=1, device_id=device, device_id_type=MESH
            ),
        )
    count = sum(1 if when is None else when.astype(jnp.int32) for _, when in targets)
    pl.semaphore_wait(barrier, count)


def plane_ids(e):
    return {m: {"expert": flip(e, m)} for m in (1, 2, 3)}


class RowsGather:
    def __init__(self, wire, ref, e, z, c, nc, half):
        self.wire, self.ref, self.e, self.z, self.c, self.nc = wire, ref, e, z, c, nc
        self.cols = (pl.ds(0, half), pl.ds(half, ref.shape[-1] - half))
        self.line = wire.slots(nc)
        self.plane = wire.slots(nc * 6)
        self.core = wire.slots(nc)
        self.ids = plane_ids(e)

    def go(self, *steps):
        for step in steps:
            action = {"l": self.pass_on, "s": self.spread, "f": self.forward, "h": self.share, "c": self.complete}
            action[step[0]](*map(int, step[1:]))

    def shard(self, k):
        if k < 2:
            return flip(self.z, k)
        inner = (self.z > 0) & (self.z < self.nc - 1)
        return jnp.where(inner, flip(self.z, 5 - k), flip(self.z, k))

    def at(self, r, zs, half):
        return self.ref.at[flip(self.e, r), zs, self.c, :, self.cols[half]]

    def slot(self, k, r, half):
        return self.plane + k * 6 + (r - 1) * 2 + half

    def pass_on(self, k):
        wire, z, nc = self.wire, self.z, self.nc
        zs = self.shard(k)
        whole = self.ref.at[self.e, zs, self.c]
        if k:
            wire.arrived(whole, self.line + zs, {"context": zs})
        wire.start(
            whole, whole, self.line + zs, {"context": z + 1}, when=(zs <= z) & (z < nc - 1)
        )
        wire.start(whole, whole, self.line + zs, {"context": z - 1}, when=(zs >= z) & (z > 0))

    def spread(self, k):
        zs = self.shard(k)
        for half, mask in ((0, 1), (1, 2), (1, 1), (0, 2)):
            part = self.at(0, zs, half)
            self.wire.start(part, part, self.slot(k, mask, half), self.ids[mask])

    def forward(self, k):
        zs = self.shard(k)
        for half, mask in ((0, 1), (1, 2)):
            part = self.at(mask, zs, half)
            self.wire.arrived(part, self.slot(k, mask, half), self.ids[mask])
            self.wire.start(part, part, self.slot(k, 3, half), self.ids[3 - mask])

    def share(self, k):
        zs = self.shard(k)
        for r, half in ((1, 1), (2, 0), (3, 0), (3, 1)):
            self.wire.arrived(self.at(r, zs, half), self.slot(k, r, half), self.ids[r])
        part = self.ref.at[:, zs, self.c]
        self.wire.start(part, part, self.core + k, {"dp": 1 - self.c})

    def complete(self):
        for k in range(self.nc):
            zs = self.shard(k)
            self.wire.arrived(self.ref.at[:, zs, 1 - self.c], self.core + k, {"dp": 1 - self.c})


class PlaneGather:
    def __init__(self, wire, ref, e):
        self.wire, self.ref = wire, ref
        self.half = ref.shape[-1] // 2
        self.ids = plane_ids(e)
        self.first = wire.slots(6)

    def at(self, r, half):
        return self.ref.at[r, :, pl.ds(half * self.half, self.half)]

    def slot(self, r, half):
        return self.first + (r - 1) * 2 + half

    def spread(self):
        for half, mask in ((0, 1), (1, 2), (1, 1), (0, 2)):
            self.wire.start(
                self.at(0, half), self.at(mask, half), self.slot(mask, half), self.ids[mask]
            )

    def forward(self):
        for half, mask in ((0, 1), (1, 2)):
            self.wire.arrived(self.at(mask, half), self.slot(mask, half), self.ids[mask])
            self.wire.start(
                self.at(mask, half), self.at(3, half), self.slot(3, half), self.ids[3 - mask]
            )

    def near(self, r):
        half = 1 if r == 1 else 0
        self.wire.arrived(self.at(r, half), self.slot(r, half), self.ids[r])

    def far(self):
        for half in (0, 1):
            self.wire.arrived(self.at(3, half), self.slot(3, half), self.ids[3])

    def complete(self):
        self.near(1)
        self.near(2)
        self.far()


def swap_halves(values):
    return pltpu.roll(values, HEAD_DIMENSION // 2, 1)


def front_kernel(
    nc,
    experts,
    x_ref,
    qkv_shard,
    small_shard,
    wo_shard,
    cot_ref,
    cos_ref,
    sin_ref,
    routes_ref,
    wk_hbm,
    wq_hbm,
    wo_hbm,
    cot_hbm,
    gate_all,
    gate_columns,
    inputs_ref,
    query_ref,
    kv_ref,
    heads_ref,
    hidden_ref,
    expert_in_ref,
    gains_ref,
    wk_all,
    wq_all,
    wo_all,
    cot_all,
    kv_scr,
    q_scr,
    sends,
    recvs,
    out_sems,
):
    e, z, c = (lax.axis_index(a) for a in ("expert", "context", "dp"))
    size = HEAD_DIMENSION
    tokens, width = x_ref.shape
    query_width = QUERY_HEADS * size
    kv_width = 2 * KEY_VALUE_HEADS * size
    wire = Wire(sends, recvs)
    ids = plane_ids(e)
    greet(
        [(ids[m], None) for m in (1, 2, 3)]
        + [({"dp": 1 - c}, None)]
        + [({"context": z + d}, z + d < nc) for d in range(1, nc)]
        + [({"context": z - d}, z >= d) for d in range(1, nc)]
    )
    wk_all[e, z, c, :, pl.ds(0, kv_width)] = qkv_shard[:, pl.ds(query_width, kv_width)]
    wk_all[e, z, c, :, pl.ds(kv_width, SMALL)] = small_shard[...]
    gather_k = RowsGather(wire, wk_all, e, z, c, nc, 256)
    gather_q = RowsGather(wire, wq_all, e, z, c, nc, 768)
    gather_o = RowsGather(wire, wo_all, e, z, c, nc, 768)
    gather_cot = PlaneGather(wire, cot_all, e)
    wq_all[e, z, c] = qkv_shard[:, pl.ds(0, query_width)]
    wo_all[e, z, c] = wo_shard[...]
    gather_k.go("l0", "s0")
    gather_q.go("s0")
    cot_all[0] = cot_ref[...]
    gather_k.go("l1", "s1", "f0", "l2", "s2")
    gather_q.go("l0")
    gather_k.go("f1", "h0", "l3", "s3")
    gather_q.go("l1", "s1")
    gather_o.go("l0")
    gather_k.go("f2", "h1", "f3")
    gather_q.go("l2", "s2")
    gather_k.go("h2")
    gather_o.go("l1")
    gather_q.go("f0")
    gather_k.go("h3")
    gather_q.go("l3", "s3")
    gather_k.go("c")
    rows = x_ref[...].astype(F32)
    scale1 = lax.rsqrt(jnp.mean(rows * rows, -1, keepdims=True) + EPSILON)

    small = wk_all[:, :, :, :, pl.ds(kv_width, SMALL)].reshape(width, SMALL)
    small = jnp.transpose(small.astype(F32))
    gain_first, gain_second = small[experts : experts + 1], small[experts + 1 : experts + 2]
    gains_ref[0:1] = gain_first
    gains_ref[1:2] = gain_second
    inputs_ref[...] = (rows * scale1 * gain_first).astype(BF16)
    kv_scr[...] = dot_nn(inputs_ref[...], wk_all[...].reshape(width, kv_width + SMALL))

    def turned(head):
        return (head * cos_ref[...] + swap_halves(head) * sin_ref[...]).astype(BF16)

    line = wire.slots(KEY_VALUE_HEADS * nc)
    for j in range(KEY_VALUE_HEADS):
        kv_ref[j, z, :, pl.ds(0, size)] = turned(kv_scr[:, pl.ds(j * size, size)])
        value = kv_scr[:, pl.ds(kv_width // 2 + j * size, size)]
        kv_ref[j, z, :, pl.ds(size, size)] = value.astype(BF16)
        mine = kv_ref.at[j, z]
        for d in range(nc - 1, 0, -1):
            wire.start(mine, mine, line + j * nc + z, {"context": z + d}, when=z + d < nc)

    def keys_here(j):
        for d in range(1, nc):

            def wait(d=d):
                wire.arrived(kv_ref.at[j, z - d], line + j * nc + z - d, {"context": z - d})

            pl.when(z >= d)(wait)

    outs = [
        pltpu.make_async_copy(source, dest, out_sems.at[n])
        for n, (source, dest) in enumerate(
            ((wk_all, wk_hbm), (wq_all, wq_hbm), (wo_all, wo_hbm), (cot_all, cot_hbm))
        )
    ]
    outs[0].start()
    for later in range(1, nc):

        def clear(later=later):
            for j in range(KEY_VALUE_HEADS):
                kv_ref[j, z + later] = jnp.zeros(kv_ref.shape[2:], BF16)

        pl.when(z + later < nc)(clear)
    gather_q.go("f1", "f2", "h0")
    gather_o.go("s0")
    gather_q.go("f3", "h1")
    gather_o.go("s1")
    gather_q.go("h2", "h3", "c")
    outs[1].start()
    gather_o.go("f0", "f1")
    gather_cot.spread()

    @pl.loop(0, query_width // 256)
    def _(n):
        columns = pl.ds(pl.multiple_of(n * 256, 256), 256)
        q_scr[:, columns] = dot_nn(
            inputs_ref[...], wq_all[:, :, :, :, columns].reshape(width, 256)
        )

    @pl.loop(0, QUERY_HEADS)
    def _(h):
        columns = pl.ds(pl.multiple_of(h * size, size), size)
        query_ref[:, columns] = turned(q_scr[:, columns])

    logits = kv_scr[:, pl.ds(kv_width, SMALL)]
    lanes = lax.broadcasted_iota(jnp.int32, logits.shape, 1)
    routes = jnp.concatenate(
        [routes_ref[...].astype(F32), jnp.zeros((SMALL - TOP, tokens), F32)], 0
    )
    routes = jnp.transpose(routes).astype(jnp.int32)
    named = lanes == routes[:, 0:1]
    for k in range(1, TOP):
        named = named | (lanes == routes[:, k : k + 1])
    logits = jnp.where(named, logits, MASKED)
    expd = jnp.exp(logits - jnp.max(logits, -1, keepdims=True))
    gates = expd / jnp.sum(expd, -1, keepdims=True)
    gate_all[0] = jnp.transpose(gates)[:GATE_ROWS]
    gate_slot = wire.slots(3)
    for r in (1, 2, 3):
        wire.start(gate_all.at[0], gate_all.at[r], gate_slot + r - 1, ids[r])

    length = nc * tokens
    group = QUERY_HEADS // KEY_VALUE_HEADS

    def attend(first, last):
        j = first // group
        key = kv_ref[j, :, :, pl.ds(0, size)].reshape(length, size)
        value = kv_ref[j, :, :, pl.ds(size, size)].reshape(length, size)

        @pl.loop(first, last)
        def _(h):
            column = pl.multiple_of(h * size, size)
            scores = dot_nt(query_ref[:, pl.ds(column, size)], key) * (size**-0.5)
            row = z * tokens + lax.broadcasted_iota(jnp.int32, scores.shape, 0)
            place = lax.broadcasted_iota(jnp.int32, scores.shape, 1)
            scores = jnp.where(place <= row, scores, MASKED)
            expd = jnp.exp(scores - jnp.max(scores, -1, keepdims=True))
            total = jnp.sum(expd, -1, keepdims=True)
            mixed = dot_nn(expd.astype(BF16), value) / total
            heads_ref[:, pl.ds(column, size)] = mixed.astype(BF16)

    half = group // 2
    keys_here(0)
    attend(0, half)
    gather_o.go("l2", "s2")
    attend(half, group)
    gather_o.go("l3", "s3", "f2", "h0")
    keys_here(1)
    attend(group, group + half)
    gather_o.go("f3", "h1")
    attend(group + half, QUERY_HEADS)
    gather_o.go("h2")
    gather_cot.forward()
    gather_o.go("h3")
    gather_o.go("c")
    outs[2].start()
    part = width // wo_all.shape[0]
    for block in range(wo_all.shape[0]):
        weight = wo_all[block].reshape(part, width)
        columns = pl.ds(block * part, part)
        hidden_ref[:, columns] = x_ref[:, columns].astype(F32) + dot_nt(heads_ref[...], weight)
    hidden = hidden_ref[...]
    scale2 = lax.rsqrt(jnp.mean(hidden * hidden, -1, keepdims=True) + EPSILON)
    expert_in_ref[...] = (hidden * scale2 * gains_ref[1:2]).astype(BF16)
    for r in (1, 2, 3):
        wire.arrived(gate_all.at[r], gate_slot + r - 1, ids[r])
    for r in range(gate_all.shape[0]):
        rest = jnp.zeros((SMALL - GATE_ROWS, tokens), F32)
        turned_gates = jnp.transpose(jnp.concatenate([gate_all[r], rest], 0))
        both = [
            jnp.sum(jnp.where(lanes == e * EXP_DEV + i, turned_gates, 0.0), -1, keepdims=True)
            for i in range(EXP_DEV)
        ]
        gate_columns[r] = jnp.where(lanes == 0, both[0], jnp.where(lanes == 1, both[1], 0.0))
    gather_cot.complete()
    outs[3].start()
    for copy in outs:
        copy.wait()
    wire.finish()


def front(operands, sizes):
    ne, nc, nd = sizes
    x, qkv_shard = operands[:2]
    tokens, width = x.shape
    rows, qkv_width = qkv_shard.shape
    query_width = QUERY_HEADS * HEAD_DIMENSION
    kv_width = qkv_width - query_width
    gathered = [
        ((ne, nc, nd, rows, kv_width + SMALL), BF16),
        ((ne, nc, nd, rows, query_width), BF16),
        ((ne, nc, nd, rows, width), BF16),
        ((ne, tokens, width), BF16),
    ]
    shapes = gathered + [
        ((ne, GATE_ROWS, tokens), F32),
        ((ne, tokens, SMALL), F32),
        ((tokens, width), BF16),
        ((tokens, query_width), BF16),
        ((KEY_VALUE_HEADS, nc, tokens, 2 * HEAD_DIMENSION), BF16),
        ((tokens, query_width), BF16),
        ((tokens, width), F32),
        ((tokens, width), BF16),
        ((8, width), F32),
    ]
    copies = 160
    vmem = pl.BlockSpec(memory_space=pltpu.VMEM)
    anywhere = pl.BlockSpec(memory_space=pl.ANY)
    return pl.pallas_call(
        functools.partial(front_kernel, nc, EXP_DEV * ne),
        out_shape=[jax.ShapeDtypeStruct(*s) for s in shapes],
        in_specs=[vmem] * len(operands),
        out_specs=[anywhere] * 4 + [vmem] * (len(shapes) - 4),
        scratch_shapes=[pltpu.VMEM(*s) for s in gathered]
        + [
            pltpu.VMEM((tokens, kv_width + SMALL), F32),
            pltpu.VMEM((tokens, query_width), F32),
            pltpu.SemaphoreType.DMA((copies,)),
            pltpu.SemaphoreType.DMA((copies,)),
            pltpu.SemaphoreType.DMA((4,)),
        ],
        compiler_params=pltpu.CompilerParams(
            collective_id=0, has_side_effects=True, vmem_limit_bytes=56 * MIB
        ),
    )(*operands)


class PlaneScatter:
    def __init__(self, wire, land, ids):
        self.wire, self.land, self.ids, self.part = wire, land, ids, None
        self.half = land.shape[-1]
        self.first = wire.slots(6)

    def send(self, source, mask, slot):
        self.wire.start(source, self.land.at[slot], self.first + slot, self.ids[mask])

    def near(self, r):
        self.send(self.part(r, r - 1), r, r - 1)

    def far(self):
        self.send(self.part(3, 0), 1, 2)
        self.send(self.part(3, 1), 2, 3)

    def relay(self, part=None):
        for half, r in ((0, 2), (1, 1)):
            slot = 2 + half
            self.wire.arrived(self.land.at[slot], self.first + slot, self.ids[3 - r])
            mine = (part or self.part)(r, half)
            mine[...] = (mine[...].astype(F32) + self.land[slot].astype(F32)).astype(BF16)
            self.send(mine, r, 4 + half)

    def total(self, own):
        for slot, half, mask in ((0, 0, 1), (1, 1, 2), (4, 0, 2), (5, 1, 1)):
            self.wire.arrived(self.land.at[slot], self.first + slot, self.ids[mask])
            columns = pl.ds(half * self.half, self.half)
            own[:, columns] += self.land[slot].astype(F32)


class LineScatter:
    def __init__(self, wire, block, lands, z, nc, up=True):
        self.wire, self.block, self.lands, self.z, self.nc = wire, block, lands, z, nc
        self.up = up
        self.first = [wire.slots(nc - 1), wire.slots(nc - 1)]

    def arrive(self, way, index, j):
        land = self.lands[way].at[index]
        self.wire.arrived(land, self.first[way] + index, {"context": self.z})
        block = self.block(j)
        block[...] = (block[...].astype(F32) + self.lands[way][index].astype(F32)).astype(BF16)

    def move(self, way, j, only=None):
        z, nc = self.z, self.nc
        inner, index = ((z > 0), j - z) if way == 0 else ((z < nc - 1), z - j)
        wanted = (j > z) if way == 0 else (j < z)
        if only is not None:
            wanted = wanted & only
        pl.when(wanted & inner)(lambda: self.arrive(way, index, j))
        self.leave(way, j, wanted)

    def step(self, s):
        if self.up:
            self.move(0, self.nc - s)
            self.move(1, s - 1)
        else:
            top = self.z == self.nc - 1
            if s == 1:
                for j in range(self.nc - 1):
                    self.leave(1, j, top)
            self.move(1, s - 1, jnp.logical_not(top))

    def leave(self, way, j, wanted):
        z = self.z
        index, near = (j - z, z + 1) if way == 0 else (z - j, z - 1)
        self.wire.start(
            self.block(j),
            self.lands[way].at[index - 1],
            self.first[way] + index - 1,
            {"context": near},
            when=wanted,
        )

    def last(self):
        if self.up:
            pl.when(self.z > 0)(lambda: self.arrive(0, 0, self.z))
        pl.when(self.z < self.nc - 1)(lambda: self.arrive(1, 0, self.z))


class RowsScatter:
    def __init__(self, wire, buf, core, plane, lines, e, z, c, nc, start, width, half):
        self.wire, self.buf, self.core, self.plane = wire, buf, core, plane
        self.e, self.c = e, c
        self.all = pl.ds(start, width)
        self.cols = (pl.ds(start, half), pl.ds(start + half, width - half))
        self.ids = plane_ids(e)
        self.core_slot = wire.slots(1)
        self.first = wire.slots(6)
        rows = buf.shape[2] // nc
        self.line = LineScatter(
            wire,
            lambda j: buf.at[c, e, pl.ds(pl.multiple_of(j * rows, rows), rows), self.all],
            lines,
            z,
            nc,
        )

    def share(self):
        self.wire.start(
            self.buf.at[1 - self.c, :, :, self.all], self.core, self.core_slot, {"dp": 1 - self.c}
        )

    def at(self, r, half):
        return self.buf.at[self.c, flip(self.e, r), :, self.cols[half]]

    def send(self, r, half, mask, slot):
        self.wire.start(
            self.at(r, half), self.plane(slot, half), self.first + slot, self.ids[mask]
        )

    def merge(self, before=None):
        self.wire.arrived(self.core, self.core_slot, {"dp": 1 - self.c})
        for r in (3, 1, 2, 0):
            block = flip(self.e, r)
            part = self.buf.at[self.c, block, :, self.all]
            part[...] = (part[...].astype(F32) + self.core[block].astype(F32)).astype(BF16)
            if r == 3:
                if before is not None:
                    before()
                self.send(3, 0, 1, 2)
                self.send(3, 1, 2, 3)
            elif r:
                self.send(r, r - 1, r, r - 1)

    def add(self, r, half, slot, mask):
        land = self.plane(slot, half)
        self.wire.arrived(land, self.first + slot, self.ids[mask])
        part = self.at(r, half)
        part[...] = (part[...].astype(F32) + land[...].astype(F32)).astype(BF16)

    def relay(self):
        for half, r in ((0, 2), (1, 1)):
            self.add(r, half, 2 + half, 3 - r)
            self.send(r, half, r, 4 + half)

    def total(self):
        for slot, half, mask in ((0, 0, 1), (1, 1, 2), (4, 0, 2), (5, 1, 1)):
            self.add(0, half, slot, mask)


class ExpertLine:
    def __init__(self, wire, base, land, ins, out, sems, z, nc):
        self.wire, self.base, self.land = wire, base, land
        self.ins, self.out, self.sems, self.z, self.nc = ins, out, sems, z, nc
        self.end = (z == 0) | (z == nc - 1)
        self.inner = jnp.logical_not(self.end)
        self.width = base.shape[-1] // EXP_DEV
        self.first = wire.slots((nc + 1) * EXP_DEV)
        self.sent = []

    def part(self, ref, j, i):
        return ref.at[j, :, pl.ds(i * self.width, self.width)]

    def combine(self, sources, stores):
        out, step = self.out, self.ins.shape[2]
        count = sources[0].shape[0] // step

        def loads(p):
            rows = pl.ds(p * step, step)
            return [
                pltpu.make_async_copy(source.at[rows], self.ins.at[k, p], self.sems.at[4 * k + p])
                for k, source in enumerate(sources)
            ]

        def store(p):
            pairs = stores(pl.ds(p * step, step), out.at[p % 2])
            return [
                pltpu.make_async_copy(source, dest, self.sems.at[16 + 2 * n + p % 2])
                for n, (source, dest) in enumerate(pairs)
            ]

        for p in range(count):
            for copy in loads(p):
                copy.start()
        for p in range(count):
            for copy in loads(p):
                copy.wait()
            if p > 1:
                for copy in store(p - 2):
                    copy.wait()
            total = self.ins[0, p].astype(F32)
            for k in range(1, len(sources)):
                total = total + self.ins[k, p].astype(F32)
            out[p % 2] = total.astype(out.dtype)
            for copy in store(p):
                copy.start()
        for p in range(max(0, count - 2), count):
            for copy in store(p):
                copy.wait()

    def copy(self, i, r, number):
        target, slot = flip(self.z, r), self.z
        if r == 3:
            target = jnp.where(self.end, flip(self.z, 1), target)
            slot = jnp.where(self.end, self.nc, slot)
        return pltpu.make_async_remote_copy(
            src_ref=self.part(self.base, flip(self.z, r), i),
            dst_ref=self.part(self.land, slot, i),
            send_sem=self.wire.sends.at[number],
            recv_sem=self.wire.recvs.at[self.first + slot * EXP_DEV + i],
            device_id={"context": target},
            device_id_type=MESH,
        )

    def send(self, i, r, when=None):
        number = len(self.sent)
        guard(when, self.copy(i, r, number).start)
        self.sent.append((when, i, r, number))

    def finish(self):
        for when, i, r, number in self.sent:
            guard(when, self.copy(i, r, number).wait_send)

    def arrived(self, slot, i):
        land = self.part(self.land, slot, i)
        self.wire.arrived(land, self.first + slot * EXP_DEV + i, {"context": self.z})

    def relay_loads(self, i, p):
        step = self.ins.shape[2]
        rows = pl.ds(p * step, step)
        sources = (self.part(self.base, flip(self.z, 2), i), self.part(self.land, self.nc, i))
        return [
            pltpu.make_async_copy(
                source.at[rows], self.ins.at[k, p], self.sems.at[4 * k + p]
            )
            for k, source in enumerate(sources)
        ]

    def relay_store(self, i, p):
        step = self.ins.shape[2]
        mine = self.part(self.base, flip(self.z, 2), i).at[pl.ds(p * step, step)]
        return pltpu.make_async_copy(self.ins.at[0, p], mine, self.sems.at[16 + p])

    def relay_steps(self):
        return range(self.base.shape[1] // self.ins.shape[2])

    def relay_begin(self, i):
        self.relayed = i

        def begin():
            self.arrived(self.nc, i)
            for p in self.relay_steps():
                for copy in self.relay_loads(i, p):
                    copy.start()

        pl.when(self.inner)(begin)

    def relay_add(self):
        i = self.relayed

        def add():
            for p in self.relay_steps():
                for copy in self.relay_loads(i, p):
                    copy.wait()
                a, b = (self.ins[k, p].astype(F32) for k in range(2))
                self.ins[0, p] = (a + b).astype(BF16)
                self.relay_store(i, p).start()

        pl.when(self.inner)(add)

    def relay_send(self, i):
        def wait():
            for p in self.relay_steps():
                self.relay_store(i, p).wait()

        pl.when(self.inner)(wait)
        self.send(i, 2, when=self.inner)

    def last(self, i, results):
        z = self.z
        sources = [self.part(self.base, z, i)]
        for r in (1, 2):
            self.arrived(flip(z, r), i)
            sources.append(self.part(self.land, flip(z, r), i))

        def stores(rows, wide):
            pairs, first = [], 0
            for result in results:
                columns = pl.ds(first, result.shape[-1])
                pairs.append((wide.at[:, columns], result.at[i, rows]))
                first += result.shape[-1]
            return pairs

        pl.when(self.end)(lambda: self.combine(sources, stores))

        def inner():
            self.arrived(flip(z, 3), i)
            self.combine(sources + [self.part(self.land, flip(z, 3), i)], stores)

        pl.when(self.inner)(inner)


def back_kernel(
    nc,
    experts,
    gates_ref,
    gate_ref,
    gains_ref,
    cos_ref,
    sin_ref,
    expert_in_hbm,
    cot_hbm,
    w_gu_hbm,
    w_dn_hbm,
    x_hbm,
    inputs_hbm,
    query_hbm,
    kv_hbm,
    heads_hbm,
    hidden_hbm,
    wk_hbm,
    wq_hbm,
    o_hbm,
    layer_ref,
    d_x_ref,
    sum_q_ref,
    sum_o_ref,
    sum_gu_hbm,
    sum_dn_hbm,
    base_hbm,
    land_hbm,
    y_hbm,
    x_all,
    y_land,
    dx_land,
    core_land,
    plane_q,
    plane_k,
    lines_o,
    lines_q,
    lines_k,
    dkv_land,
    d_in_ref,
    dg_lanes,
    dg_part,
    dg_land,
    ins,
    out_wide,
    sends_1,
    recvs_1,
    sends_2,
    recvs_2,
    sends_e,
    recvs_e,
    hand_sends,
    hand_recvs,
    stage_sems,
    load_sems,
    sum_sems,
    y_sems,
    credits,
):
    e, z, c = (lax.axis_index(a) for a in ("expert", "context", "dp"))
    size = HEAD_DIMENSION
    blocks, tokens, width = cot_hbm.shape
    ff = w_dn_hbm.shape[1]
    query_width = QUERY_HEADS * size
    key_width = KEY_VALUE_HEADS * size
    qkv_width = query_width + 2 * key_width
    rest = wk_hbm.shape[-1]
    grad_width = base_hbm.shape[-1]
    ids = plane_ids(e)
    sibling = {"dp": 1 - c}
    bottom, even = z == 0, lax.rem(z, 2) == 0
    wire_1, wire_2, wire_e = Wire(sends_1, recvs_1), Wire(sends_2, recvs_2), Wire(sends_e, recvs_e)
    expert = ExpertLine(
        wire_e, base_hbm, land_hbm, ins, out_wide, sum_sems, z, nc
    )
    gather = PlaneGather(wire_1, x_all, e)
    scatter_dx = PlaneScatter(wire_1, dx_land, ids)
    scatter_y = PlaneScatter(wire_2, y_land, ids)
    dg_slot = wire_1.slots(3)

    def token_phase(w_gu, w_dn, cot_all, a_all, dgu_all, y_stage, dx_part, stage):
        scatter_dx.part = lambda r, half: dx_part.at[
            r - 1, :, pl.ds(half * width // 2, width // 2)
        ]
        sources = [(expert_in_hbm, x_all.at[0])]
        for i in range(EXP_DEV):
            sources += [(w_gu_hbm.at[i], w_gu.at[i]), (w_dn_hbm.at[i], w_dn.at[i])]
            if i == 0:
                sources += [(cot_hbm.at[0], cot_all.at[0]), (cot_hbm.at[1:], cot_all.at[1:])]
        loads = [
            pltpu.make_async_copy(source, dest, load_sems.at[n])
            for n, (source, dest) in enumerate(sources)
        ]
        for copy in loads:
            copy.start()
        greet(
            [(ids[m], None) for m in (1, 2, 3)]
            + [(sibling, None), ({"context": flip(z, 2)}, None)]
            + [({"context": z + 1}, z < nc - 1), ({"context": z - 1}, z > 0)]
        )
        loads[0].wait()
        gather.spread()
        step = 256
        wide = 512
        dg_lanes[...] = jnp.zeros_like(dg_lanes)

        def hidden_units(r, i, count=1):
            here = pl.ds(r, count)
            flat = count * tokens

            @pl.loop(0, ff // step)
            def _(f):
                column = pl.multiple_of(f * step, step)
                rows = x_all[here].reshape(flat, width)
                grads = cot_all[here].reshape(flat, width)
                gate_part = dot_nn(rows, w_gu[i, :, pl.ds(column, step)])
                up_part = dot_nn(rows, w_gu[i, :, pl.ds(ff + column, step)])
                raw = dot_nt(grads, w_dn[i, pl.ds(column, step), :])
                gate = gates_ref[here].reshape(flat, SMALL)[:, i : i + 1]
                sigma = jax.nn.sigmoid(gate_part)
                silu = gate_part * sigma
                act = silu * up_part
                lanes = lax.broadcasted_iota(jnp.int32, (flat, SMALL), 1)
                d_gate = jnp.where(
                    lanes == e * EXP_DEV + i, jnp.sum(act * raw, -1, keepdims=True), 0.0
                )
                dg_lanes[here] += d_gate.reshape(count, tokens, SMALL)

                def put(ref, first, values):
                    values = values.astype(BF16).reshape(count, tokens, step)
                    ref[here, :, pl.ds(pl.multiple_of(first, step), step)] = values

                put(a_all, i * ff + column, act * gate)
                d_act = raw * gate
                d_gate_part = d_act * up_part * sigma * (1.0 + gate_part * (1.0 - sigma))
                put(dgu_all, i * 2 * ff + column, d_gate_part)
                put(dgu_all, i * 2 * ff + ff + column, d_act * silu)

        def y_copy(r):
            return pltpu.make_async_copy(y_stage.at[r % 2], y_hbm.at[r], y_sems.at[r % 2])

        def outputs(r, count=1):
            here = pl.ds(r, count)
            flat = count * tokens

            @pl.loop(0, width // wide)
            def _(n):
                columns = pl.ds(pl.multiple_of(n * wide, wide), wide)
                low = dgu_all[here].reshape(flat, EXP_DEV * 2 * ff)
                d_rows = dot_nt(low[:, : 2 * ff], w_gu[0, columns, :])
                d_rows += dot_nt(low[:, 2 * ff :], w_gu[1, columns, :])
                weight = w_dn[:, :, columns].reshape(EXP_DEV * ff, wide)
                out = dot_nn(a_all[here].reshape(flat, EXP_DEV * ff), weight).astype(BF16)
                for k in range(count):
                    rows = slice(k * tokens, (k + 1) * tokens)
                    y_stage[(r + k) % 2, :, columns] = out[rows]
                    if r == 0:
                        d_in_ref[:, columns] = d_rows
                    else:
                        dx_part[r + k - 1, :, columns] = d_rows[rows].astype(BF16)

            for k in range(r, r + count):
                y_copy(k).start()
                dg_part[k] = jnp.transpose(dg_lanes[k])[:GATE_ROWS]
                if k:
                    wire_1.start(dg_part.at[k], dg_land.at[k - 1], dg_slot + k - 1, ids[k])

        half_rows = width // nc // 2
        units = [(i, r) for i in range(EXP_DEV) for r in (3, 2, 1, 0)]

        def keep(u):
            i, r = units[u]
            return pltpu.make_async_copy(
                stage.at[u % 2, c], expert.part(base_hbm, flip(z, r), i), stage_sems.at[u % 2]
            )

        def hand(u):
            r = units[u][1]
            return pltpu.make_async_remote_copy(
                src_ref=stage.at[u % 2, 1 - c],
                dst_ref=core_land.at[r],
                send_sem=hand_sends.at[u],
                recv_sem=hand_recvs.at[u],
                device_id=sibling,
                device_id_type=MESH,
            )

        def weight_grads(u):
            i, r = units[u]
            columns = pl.ds(pl.multiple_of(flip(z, r) * 2 * half_rows, 2 * half_rows), 2 * half_rows)
            for first, source, grad, start, count in (
                (0, x_all, dgu_all, i * 2 * ff, 2),
                (2 * ff, cot_all, a_all, i * ff, 1),
            ):
                rows = source[:, :, columns].reshape(blocks * tokens, 2 * half_rows)

                @pl.loop(0, count)
                def _(n):
                    column = pl.multiple_of(n * ff, ff)
                    part = grad[:, :, pl.ds(pl.multiple_of(start + column, ff), ff)]
                    result = dot_tn(rows, part.reshape(blocks * tokens, ff)).astype(BF16)
                    stage[u % 2, :, :, pl.ds(pl.multiple_of(first + column, ff), ff)] = (
                        result.reshape(2, half_rows, ff)
                    )

            if u == nc:
                pl.semaphore_wait(credits.at[3], 1)
            hand(u).start()

        def settle(u):
            hand(u).wait_recv()
            r = units[u][1]
            mine = stage[u % 2, c].astype(F32) + core_land[r].astype(F32)
            stage[u % 2, c] = mine.astype(BF16)
            keep(u).start()

        def clear(u):
            keep(u).wait()
            hand(u).wait_send()
            i, r = units[u]
            if i == 0 and r == 2:
                expert.send(i, r, when=expert.end)
            elif i == 0 and r == 1 or r == 3:
                expert.send(i, r)
            elif r == 2:
                expert.send(i, r, when=bottom)
            elif r == 1:
                expert.send(i, r, when=even)

        for copy in loads[1:4]:
            copy.wait()
        hidden_units(0, 0)
        for copy in loads[4:]:
            copy.wait()
        hidden_units(0, 1)
        gather.forward()
        outputs(0)
        gather.near(1)
        gather.near(2)
        hidden_units(1, 0, 2)
        gather.far()
        hidden_units(3, 0)
        weight_grads(0)
        weight_grads(1)
        settle(0)
        clear(0)
        weight_grads(2)
        settle(1)
        clear(1)
        weight_grads(3)
        settle(2)
        hidden_units(1, 1, 2)
        clear(2)
        settle(3)
        pl.semaphore_signal(credits.at[3], inc=1, device_id=sibling, device_id_type=MESH)
        y_copy(0).wait()
        outputs(1, 2)
        scatter_dx.near(1)
        scatter_dx.near(2)
        hidden_units(3, 1)
        expert.relay_begin(0)
        y_copy(1).wait()
        outputs(3)
        scatter_dx.far()
        clear(3)
        expert.relay_add()
        weight_grads(4)
        expert.relay_send(0)
        weight_grads(5)
        settle(4)
        scatter_dx.relay()
        clear(4)
        weight_grads(6)
        settle(5)
        clear(5)
        weight_grads(7)
        settle(6)
        scatter_dx.total(d_in_ref)
        for r in (1, 2):
            pl.semaphore_signal(credits.at[r], inc=1, device_id=ids[r], device_id_type=MESH)
        settle(7)
        clear(6)
        clear(7)
        y_copy(3).wait()
        y_copy(2).wait()
        wire_1.finish()
        pl.semaphore_signal(credits.at[0], inc=1, device_id=sibling, device_id_type=MESH)

    def token_rows_phase(
        weight,
        grads_o,
        grads_q,
        x_ref,
        inputs_ref,
        query_ref,
        kv_ref,
        heads_ref,
        hidden_ref,
        d_hidden_ref,
        d_attn_ref,
        d_heads_ref,
        d_all_ref,
        rows_ref,
        dkv_acc,
        dkv_ref,
        y_relay,
    ):
        cot_ref, d_inputs_ref = d_heads_ref, hidden_ref
        scatter_y.part = lambda r, half: y_hbm.at[r, :, pl.ds(half * width // 2, width // 2)]
        y_loads = [
            pltpu.make_async_copy(scatter_y.part(2 - half, half), y_relay.at[half], y_sems.at[half])
            for half in range(2)
        ]
        for copy in y_loads:
            copy.start()
        planes = grads_o.shape[1]
        part = width // planes
        sources = (
            (hidden_hbm, hidden_ref),
            (cot_hbm.at[0], cot_ref),
            (o_hbm, weight.at[:, pl.ds(0, width)]),
            (heads_hbm, heads_ref),
            (query_hbm, query_ref),
            (kv_hbm, kv_ref),
            (x_hbm, x_ref),
            (inputs_hbm, inputs_ref),
        )
        loads = [
            pltpu.make_async_copy(source, dest, load_sems.at[4 + n])
            for n, (source, dest) in enumerate(sources)
        ]
        for copy in loads:
            copy.start()
        for r in (1, 2):
            scatter_y.near(r)
        scatter_y.far()

        def rows_scatter(buf, core, plane, lines, start, count, half):
            return RowsScatter(
                wire_2,
                buf,
                core,
                plane,
                [lines.at[0], lines.at[1]],
                e,
                z,
                c,
                nc,
                start,
                count,
                half,
            )

        rows_of = part // 2
        scatter_o = rows_scatter(
            grads_o,
            x_all.at[:, pl.ds(0, rows_of)],
            lambda slot, half: dx_land.at[slot, pl.ds(0, rows_of)],
            lines_o,
            0,
            width,
            width // 2,
        )
        scatter_q = rows_scatter(
            grads_q,
            core_land.at[:, :, pl.ds(0, query_width)],
            lambda slot, half: plane_q.at[slot],
            lines_q,
            0,
            query_width,
            query_width // 2,
        )
        rest_half = rest // 256 * 128
        scatter_k = rows_scatter(
            grads_q,
            core_land.at[:, :, pl.ds(query_width, rest)],
            lambda slot, half: plane_k.at[
                slot, :, pl.ds(0, rest - rest_half if half else rest_half)
            ],
            lines_k,
            query_width,
            rest,
            rest_half,
        )
        scatter_kv = [
            LineScatter(
                wire_2,
                lambda j, h=h: dkv_ref.at[h, j],
                [dkv_land.at[h], dkv_land.at[h]],
                z,
                nc,
                up=False,
            )
            for h in range(KEY_VALUE_HEADS)
        ]

        loads[0].wait()
        loads[1].wait()
        hidden, d_in = hidden_ref[...], d_in_ref[...]
        scale2 = lax.rsqrt(jnp.mean(hidden * hidden, -1, keepdims=True) + EPSILON)
        scaled = d_in * gains_ref[1:2]
        mean = jnp.mean(scaled * hidden, -1, keepdims=True)
        d_hidden = cot_ref[...].astype(F32) + scale2 * scaled
        d_hidden = d_hidden - hidden * (scale2 * scale2 * scale2 * mean)
        d_hidden_ref[...] = d_hidden
        d_attn_ref[...] = d_hidden.astype(BF16)
        rows_ref[...] = jnp.zeros_like(rows_ref)
        rows_ref[experts + 1 : experts + 2, :] = jnp.sum(d_in * hidden * scale2, 0, keepdims=True)

        loads[2].wait()

        @pl.loop(0, query_width // 256)
        def _(n):
            columns = pl.ds(pl.multiple_of(n * 256, 256), 256)
            d_heads_ref[:, columns] = dot_nn(d_attn_ref[...], weight[:, columns]).astype(BF16)

        load_q = [
            pltpu.make_async_copy(wq_hbm, weight.at[:, pl.ds(0, query_width)], load_sems.at[0]),
            pltpu.make_async_copy(wk_hbm, weight.at[:, pl.ds(query_width, rest)], load_sems.at[1]),
        ]
        for copy in load_q:
            copy.start()
        loads[3].wait()

        def row_grads(buf, left, right, first, count, extra=None):
            @pl.loop(0, planes)
            def _(block):
                columns = pl.ds(pl.multiple_of(block * part, part), part)
                result = dot_tn(left[:, columns], right)
                if extra is not None:
                    result = result + extra(columns)
                result = result.astype(BF16).reshape(nc, 2, part // nc // 2, count)
                for half in range(2):
                    buf[half, block, :, pl.ds(first, count)] = result[:, half].reshape(
                        part // 2, count
                    )

        row_grads(grads_o, d_attn_ref, heads_ref[...], 0, width)
        pl.semaphore_wait(credits.at[0], 1)
        scatter_o.share()
        y_own = pltpu.make_async_copy(y_hbm.at[0], heads_ref, load_sems.at[2])
        y_own.start()

        length = nc * tokens
        group = QUERY_HEADS // KEY_VALUE_HEADS
        for copy in loads[4:6]:
            copy.wait()
        dkv_acc[...] = jnp.zeros_like(dkv_acc)

        def attend(j, first, last):
            key = kv_ref[j, :, :, pl.ds(0, size)].reshape(length, size)
            value = kv_ref[j, :, :, pl.ds(size, size)].reshape(length, size)

            @pl.loop(j * group + first, j * group + last)
            def _(h):
                columns = pl.ds(pl.multiple_of(h * size, size), size)
                query, grad = query_ref[:, columns], d_heads_ref[:, columns]
                probs = masked_probs(z * tokens, query, key)
                d_probs = dot_nt(grad, value)
                inner = jnp.sum(probs * d_probs, axis=-1, keepdims=True)
                d_raw = (probs * (d_probs - inner) * (size**-0.5)).astype(BF16)
                d_query = dot_nn(d_raw, key)
                d_query = d_query * cos_ref[...] - swap_halves(d_query) * sin_ref[...]
                d_all_ref[:, columns] = d_query.astype(BF16)
                dkv_acc[j, :, pl.ds(0, size)] += dot_tn(d_raw, query)
                dkv_acc[j, :, pl.ds(size, size)] += dot_tn(probs.astype(BF16), grad)

        def round_kv(j):
            for block in range(nc):
                rows = dkv_acc[j, pl.ds(block * tokens, tokens), :]
                dkv_ref[j, block] = rows.astype(BF16)

        def enter():
            pl.semaphore_wait(credits.at[1], 1)
            pl.semaphore_wait(credits.at[2], 1)

        attend(0, 0, group)
        round_kv(0)
        scatter_kv[0].step(1)
        scatter_o.merge(enter)
        for copy in y_loads:
            copy.wait()
        scatter_y.relay(lambda r, half: y_relay.at[half])
        attend(1, 0, group // 2)
        scatter_kv[0].step(2)
        attend(1, group // 2, group)
        round_kv(1)
        scatter_kv[1].step(1)
        for r in (2, 1):
            expert.send(1, r, when=z == nc - 1)
        scatter_kv[0].step(3)
        scatter_o.relay()

        for copy in loads[6:]:
            copy.wait()
        row_grads(grads_q, inputs_ref, d_all_ref[:, pl.ds(0, query_width)], 0, query_width)
        scatter_q.share()
        scatter_kv[1].step(2)
        scatter_kv[1].step(3)
        expert.send(1, 1, when=z == 1)
        expert.relay_begin(1)
        y_own.wait()
        hidden_ref[...] += heads_ref[...].astype(F32)
        scatter_y.total(hidden_ref)
        layer_ref[...] = hidden_ref[...].astype(BF16)
        scatter_o.total()
        scatter_q.merge()
        for h in range(KEY_VALUE_HEADS):
            scatter_kv[h].last()
        expert.relay_add()
        expert.relay_send(1)

        for h in range(KEY_VALUE_HEADS):
            grad = dkv_ref[h, z, :, pl.ds(0, size)].astype(F32)
            grad = grad * cos_ref[...] - swap_halves(grad) * sin_ref[...]
            d_all_ref[:, pl.ds(query_width + h * size, size)] = grad.astype(BF16)
            d_all_ref[:, pl.ds(query_width + key_width + h * size, size)] = dkv_ref[
                h, z, :, pl.ds(size, size)
            ]

        total = dg_part[0]
        for r in (1, 2, 3):
            wire_1.arrived(dg_land.at[r - 1], dg_slot + r - 1, ids[r])
            total = total + dg_land[r - 1]
        gates = gate_ref[0]
        d_logits = gates * (total - jnp.sum(gates * total, 0, keepdims=True))
        d_logits = jnp.concatenate(
            [d_logits, jnp.zeros((SMALL - d_logits.shape[0], tokens), F32)], 0
        )
        d_all_ref[:, pl.ds(qkv_width, SMALL)] = jnp.transpose(d_logits).astype(BF16)

        for copy in load_q:
            copy.wait()

        @pl.loop(0, planes)
        def _(block):
            columns = pl.ds(pl.multiple_of(block * part, part), part)
            d_inputs_ref[:, columns] = dot_nt(d_all_ref[...], weight[columns, :])

        rows = x_ref[...].astype(F32)
        scale1 = lax.rsqrt(jnp.mean(rows * rows, -1, keepdims=True) + EPSILON)
        d_inputs = d_inputs_ref[...]
        rows_ref[experts : experts + 1, :] = jnp.sum(d_inputs * rows * scale1, 0, keepdims=True)

        def extra(columns):
            small = jnp.transpose(rows_ref[:, columns])
            return jnp.concatenate([jnp.zeros((part, rest - SMALL), F32), small], 1)

        row_grads(
            grads_q, inputs_ref, d_all_ref[:, pl.ds(query_width, rest)], query_width, rest, extra
        )
        scatter_k.share()
        scatter_q.relay()
        scatter_k.merge()
        scaled = d_inputs_ref[...] * gains_ref[0:1]
        rows = x_ref[...].astype(F32)
        scale1 = lax.rsqrt(jnp.mean(rows * rows, -1, keepdims=True) + EPSILON)
        mean = jnp.mean(scaled * rows, -1, keepdims=True)
        d_x = d_hidden_ref[...] + scale1 * scaled - rows * (scale1 * scale1 * scale1 * mean)
        d_x_ref[...] = d_x.astype(BF16)
        scatter_q.total()
        expert.last(0, (sum_gu_hbm, sum_dn_hbm))
        scatter_k.relay()
        scatter_o.line.step(1)
        scatter_q.line.step(1)
        scatter_k.total()
        scatter_k.line.step(1)
        for s in range(2, nc):
            for scatter in (scatter_o, scatter_q, scatter_k):
                scatter.line.step(s)
        for scatter in (scatter_o, scatter_q, scatter_k):
            scatter.line.last()
        sum_o_ref[...] = scatter_o.line.block(z)[...].astype(F32)
        sum_q_ref[...] = grads_q[c, e, pl.ds(pl.multiple_of(z * (rows_of // nc), rows_of // nc), rows_of // nc)].astype(F32)
        expert.last(1, (sum_gu_hbm, sum_dn_hbm))
        wire_2.finish()
        expert.finish()

    held = EXP_DEV
    pl.run_scoped(
        token_phase,
        pltpu.VMEM((held, width, 2 * ff), BF16),
        pltpu.VMEM((held, ff, width), BF16),
        pltpu.VMEM((blocks, tokens, width), BF16),
        pltpu.VMEM((blocks, tokens, held * ff), BF16),
        pltpu.VMEM((blocks, tokens, held * 2 * ff), BF16),
        pltpu.VMEM((2, tokens, width), BF16),
        pltpu.VMEM((blocks - 1, tokens, width), BF16),
        pltpu.VMEM((2, 2, width // nc // 2, grad_width // held), BF16),
    )
    rows_half = width // blocks // 2
    pl.run_scoped(
        token_rows_phase,
        pltpu.VMEM((width, qkv_width + SMALL), BF16),
        pltpu.VMEM((2, blocks, rows_half, width), BF16),
        pltpu.VMEM((2, blocks, rows_half, qkv_width + SMALL), BF16),
        pltpu.VMEM((tokens, width), BF16),
        pltpu.VMEM((tokens, width), BF16),
        pltpu.VMEM((tokens, query_width), BF16),
        pltpu.VMEM((KEY_VALUE_HEADS, nc, tokens, 2 * size), BF16),
        pltpu.VMEM((tokens, query_width), BF16),
        pltpu.VMEM((tokens, width), F32),
        pltpu.VMEM((tokens, width), F32),
        pltpu.VMEM((tokens, width), BF16),
        pltpu.VMEM((tokens, query_width), BF16),
        pltpu.VMEM((tokens, qkv_width + SMALL), BF16),
        pltpu.VMEM((SMALL, width), F32),
        pltpu.VMEM((KEY_VALUE_HEADS, nc * tokens, 2 * size), F32),
        pltpu.VMEM((KEY_VALUE_HEADS, nc, tokens, 2 * size), BF16),
        pltpu.VMEM((2, tokens, width // 2), BF16),
    )


def back(operands, sizes):
    ne, nc, nd = sizes
    cot, w_gu, w_dn, x = operands[6], operands[7], operands[8], operands[9]
    tokens, width = x.shape
    held, ff = w_dn.shape[0], w_dn.shape[1]
    rest = operands[15].shape[-1]
    q_width = QUERY_HEADS * HEAD_DIMENSION + rest
    rows = width // (ne * nc * nd)
    rest_half = rest // 256 * 128
    shard, grads = width // (nc * nd), held * 3 * ff
    kv_size = 2 * HEAD_DIMENSION
    shapes = [
        ((tokens, width), BF16),
        ((tokens, width), BF16),
        ((rows, q_width), F32),
        ((rows, width), F32),
        ((held, shard, 2 * ff), F32),
        ((held, shard, ff), F32),
        ((nc, shard, grads), BF16),
        ((nc + 1, shard, grads), BF16),
        ((ne, tokens, width), BF16),
    ]
    vmem = pl.BlockSpec(memory_space=pltpu.VMEM)
    anywhere = pl.BlockSpec(memory_space=pl.ANY)
    step, units = 48, nc * held
    return pl.pallas_call(
        functools.partial(back_kernel, nc, EXP_DEV * ne),
        out_shape=[jax.ShapeDtypeStruct(*s) for s in shapes],
        in_specs=[vmem] * 5 + [anywhere] * (len(operands) - 5),
        out_specs=[vmem] * 4 + [anywhere] * 5,
        scratch_shapes=[
            pltpu.VMEM((ne, tokens, width), BF16),
            pltpu.VMEM((6, tokens, width // 2), BF16),
            pltpu.VMEM((6, tokens, width // 2), BF16),
            pltpu.VMEM((nc, shard, grads // held), BF16),
            pltpu.VMEM((6, nc * rows, QUERY_HEADS * HEAD_DIMENSION // 2), BF16),
            pltpu.VMEM((6, nc * rows, rest - rest_half), BF16),
            pltpu.VMEM((2, nc - 1, rows, width), BF16),
            pltpu.VMEM((2, nc - 1, rows, QUERY_HEADS * HEAD_DIMENSION), BF16),
            pltpu.VMEM((2, nc - 1, rows, rest), BF16),
            pltpu.VMEM((KEY_VALUE_HEADS, nc - 1, tokens, kv_size), BF16),
            pltpu.VMEM((tokens, width), F32),
            pltpu.VMEM((ne, tokens, SMALL), F32),
            pltpu.VMEM((ne, GATE_ROWS, tokens), F32),
            pltpu.VMEM((ne - 1, GATE_ROWS, tokens), F32),
            pltpu.VMEM((4, shard // step, step, grads // held), BF16),
            pltpu.VMEM((2, step, grads // held), F32),
            pltpu.SemaphoreType.DMA((32,)),
            pltpu.SemaphoreType.DMA((32,)),
            pltpu.SemaphoreType.DMA((64,)),
            pltpu.SemaphoreType.DMA((64,)),
            pltpu.SemaphoreType.DMA((2 * units,)),
            pltpu.SemaphoreType.DMA(((nc + 1) * held,)),
            pltpu.SemaphoreType.DMA((units,)),
            pltpu.SemaphoreType.DMA((units,)),
            pltpu.SemaphoreType.DMA((2,)),
            pltpu.SemaphoreType.DMA((12,)),
            pltpu.SemaphoreType.DMA((20,)),
            pltpu.SemaphoreType.DMA((2,)),
            pltpu.SemaphoreType.REGULAR((4,)),
        ],
        compiler_params=pltpu.CompilerParams(
            collective_id=1, has_side_effects=True, vmem_limit_bytes=63 * MIB
        ),
    )(*operands)


def local_plain(
    layer_input,
    gain_attn,
    query_key_value_weight,
    w_out,
    w_router,
    gain_ffn,
    w_gate_up,
    w_down,
    routes,
    d_out,
):
    tokens = layer_input.shape[1]
    model_width = layer_input.shape[2]
    ne, nc, nd = (lax.axis_size(a) for a in ("expert", "context", "dp"))
    expert_total = EXP_DEV * ne
    ff = w_down.shape[1]
    me = lax.axis_index("expert")
    first_row = lax.axis_index("context") * tokens
    query_width = QUERY_HEADS * HEAD_DIMENSION
    key_width = KEY_VALUE_HEADS * HEAD_DIMENSION
    qkv_width = query_width + 2 * key_width

    small = jnp.concatenate([w_router, gain_attn[:, None], gain_ffn[:, None]], -1)
    small = jnp.pad(small, ((0, 0), (0, 128 - small.shape[1])))
    gathered = gather_rows(jnp.concatenate([query_key_value_weight, small], -1))
    out_turned = gather_rows(w_out.T)
    qkv_weight = gathered[:, :qkv_width]
    router_weight = gathered[:, qkv_width : qkv_width + expert_total]
    gains = gathered[:, qkv_width + expert_total : qkv_width + expert_total + 2].T.astype(F32)
    gain_first, gain_second = gains[0], gains[1]
    cotangent_all = plane_gather(d_out[0])

    token_rows = layer_input[0].astype(F32)
    scale1 = lax.rsqrt(jnp.mean(token_rows * token_rows, -1, keepdims=True) + EPSILON)
    inputs1 = (token_rows * scale1 * gain_first).astype(BF16)
    query_key_value = dot_nn(inputs1, qkv_weight)
    cosine_values, sine_values = rope_tables(first_row + jnp.arange(tokens), HEAD_DIMENSION)
    rotated = rotate_half(
        query_key_value[:, : query_width + key_width].reshape(tokens, -1, HEAD_DIMENSION),
        cosine_values,
        sine_values,
    ).reshape(tokens, -1)
    query = rotated[:, :query_width].astype(BF16)
    key_value_local = jnp.concatenate(
        [rotated[:, query_width:], query_key_value[:, query_width + key_width :]], -1
    ).astype(BF16)
    key_value = line_gather(key_value_local, "context", both=False).reshape(nc * tokens, -1)
    first = first_row.astype(jnp.int32).reshape(1)
    heads = attend_forward(first, query, key_value)

    logits = dot_nn(inputs1, router_weight)
    chosen_ids = routes[0]
    picks = (chosen_ids[:, :, None] == jnp.arange(expert_total)[None, None, :]).astype(F32)
    chosen = jnp.sum(picks * logits[:, None, :], -1)
    gates = jax.nn.softmax(chosen, axis=-1)
    gate_dense = jnp.sum(picks * gates[:, :, None], 1).T
    gate_blocks = cube_gather(gate_dense, "expert", axis_masks("expert"))
    gate_local = jnp.concatenate(
        [lax.dynamic_slice_in_dim(b, me * EXP_DEV, EXP_DEV, 0) for b in gate_blocks], 1
    )

    attn = dot_nt(heads, out_turned)
    hidden = token_rows + attn
    scale2 = lax.rsqrt(jnp.mean(hidden * hidden, -1, keepdims=True) + EPSILON)
    expert_in = (hidden * scale2 * gain_second).astype(BF16)

    rows_all = plane_gather(expert_in)
    gate_up = jnp.einsum("td,edf->etf", rows_all, w_gate_up, preferred_element_type=F32)
    gate_part, up_part = gate_up[..., :ff], gate_up[..., ff:]
    sigma = jax.nn.sigmoid(gate_part)
    silu = gate_part * sigma
    act = silu * up_part
    gate_column = gate_local[:, :, None]
    act_gated = (act * gate_column).astype(BF16)
    partial_out = jnp.einsum("etf,efd->td", act_gated, w_down, preferred_element_type=F32)
    mixture = plane_scatter(partial_out.astype(BF16), tokens)
    layer_result = (hidden + mixture).astype(BF16)

    d_act_raw = jnp.einsum("td,efd->etf", cotangent_all, w_down, preferred_element_type=F32)
    d_gates_local = jnp.sum(d_act_raw * act, -1)
    d_act = d_act_raw * gate_column
    d_gate_part = d_act * up_part * sigma * (1.0 + gate_part * (1.0 - sigma))
    d_up_part = d_act * silu
    d_gate_up = jnp.concatenate([d_gate_part, d_up_part], -1).astype(BF16)
    d_rows = jnp.einsum("etf,edf->td", d_gate_up, w_gate_up, preferred_element_type=F32)
    grad_down = jnp.einsum("td,etf->edf", cotangent_all, act_gated, preferred_element_type=F32)
    grad_gate_up = jnp.einsum("td,etf->edf", rows_all, d_gate_up, preferred_element_type=F32)

    d_expert_in = plane_scatter(d_rows.astype(BF16), tokens)
    d_gate_blocks = d_gates_local.reshape(EXP_DEV, ne, tokens)
    d_gates_dense = jnp.zeros((expert_total, tokens), F32)
    for r in range(ne):
        arrived = d_gate_blocks[:, r]
        if r:
            arrived = exchange(arrived, "expert", r)
        d_gates_dense = lax.dynamic_update_slice(d_gates_dense, arrived, ((me ^ r) * EXP_DEV, 0))
    d_gates = jnp.sum(picks * d_gates_dense.T[:, None, :], -1)
    d_chosen = gates * (d_gates - jnp.sum(gates * d_gates, -1, keepdims=True))
    d_logits = jnp.sum(picks * d_chosen[:, :, None], 1).astype(BF16)
    grad_router = dot_tn(inputs1, d_logits)

    core = lax.axis_index("dp")
    part = model_width // (nc * nd)

    def scatter_experts(grad):
        blocks = grad.reshape(EXP_DEV, nc, nd, part, -1)
        mine = cube_scatter(
            [lax.dynamic_index_in_dim(blocks, core ^ r, 2, keepdims=False) for r in range(nd)],
            "dp",
            axis_masks("dp"),
        )
        return line_scatter(
            lambda j: lax.dynamic_index_in_dim(mine, j, 1, keepdims=False), "context"
        )

    sum_gate_up = scatter_experts(grad_gate_up)
    sum_down = jnp.swapaxes(scatter_experts(grad_down), 1, 2)

    cotangent = d_out[0].astype(F32)
    scaled2 = d_expert_in * gain_second
    d_hidden = (
        cotangent
        + scale2 * scaled2
        - hidden * (scale2 * scale2 * scale2) * jnp.mean(scaled2 * hidden, -1, keepdims=True)
    )
    grad_gain_second = jnp.sum(d_expert_in * hidden * scale2, 0)
    d_attn = d_hidden.astype(BF16)
    grad_out_turned = dot_tn(d_attn, heads)
    sum_out = scatter_rows(grad_out_turned).T
    d_heads = dot_nn(d_attn, out_turned).astype(BF16)
    d_query, d_key_all, d_value_all = attend_backward(first, query, key_value, d_heads)
    d_key_value_all = jnp.concatenate([d_key_all, d_value_all], -1).reshape(nc, tokens, -1)
    d_key_value = line_scatter(
        lambda j: lax.dynamic_index_in_dim(d_key_value_all, j, 0, keepdims=False),
        "context",
        up=False,
    )
    d_rotated = rotate_back(
        jnp.concatenate([d_query, d_key_value[:, :key_width]], -1).reshape(
            tokens, -1, HEAD_DIMENSION
        ),
        cosine_values,
        sine_values,
    ).reshape(tokens, -1)
    d_qkv = jnp.concatenate([d_rotated, d_key_value[:, key_width:]], -1).astype(BF16)
    d_inputs = dot_nt(d_qkv, qkv_weight) + dot_nt(d_logits, router_weight)
    grad_gain_first = jnp.sum(d_inputs * token_rows * scale1, 0)
    grad_qkv = dot_tn(inputs1, d_qkv)
    small_grads = jnp.concatenate(
        [grad_router, grad_gain_first[:, None], grad_gain_second[:, None]], -1
    )
    small_grads = jnp.pad(small_grads, ((0, 0), (0, 128 - small_grads.shape[1])))
    sum_rows = scatter_rows(jnp.concatenate([grad_qkv, small_grads], -1))
    sum_qkv = sum_rows[:, :qkv_width]
    sum_router = sum_rows[:, qkv_width : qkv_width + expert_total]
    sum_gain_first = sum_rows[:, qkv_width + expert_total]
    sum_gain_second = sum_rows[:, qkv_width + expert_total + 1]
    scaled1 = d_inputs * gain_first
    d_input_rows = (
        d_hidden
        + scale1 * scaled1
        - token_rows
        * (scale1 * scale1 * scale1)
        * jnp.mean(scaled1 * token_rows, -1, keepdims=True)
    ).astype(BF16)
    return (
        layer_result[None],
        d_input_rows[None],
        sum_gain_first,
        sum_qkv,
        sum_out,
        sum_router,
        sum_gain_second,
        sum_gate_up,
        sum_down,
    )


def local_fused(
    layer_input,
    gain_attn,
    query_key_value_weight,
    w_out,
    w_router,
    gain_ffn,
    w_gate_up,
    w_down,
    routes,
    d_out,
):
    tokens = layer_input.shape[1]
    ne, nc, nd = sizes = tuple(lax.axis_size(a) for a in ("expert", "context", "dp"))
    expert_total = EXP_DEV * ne
    first_row = lax.axis_index("context") * tokens
    query_width = QUERY_HEADS * HEAD_DIMENSION
    key_width = KEY_VALUE_HEADS * HEAD_DIMENSION
    qkv_width = query_width + 2 * key_width

    small = jnp.concatenate([w_router, gain_attn[:, None], gain_ffn[:, None]], -1)
    small = jnp.pad(small, ((0, 0), (0, SMALL - small.shape[1])))
    cosine_values, sine_values = rope_tables(first_row + jnp.arange(tokens), HEAD_DIMENSION)
    sine_values = sine_values * jnp.where(
        jnp.arange(HEAD_DIMENSION) < HEAD_DIMENSION // 2, -1.0, 1.0
    )
    (
        wk_all,
        wq_all,
        wo_all,
        cotangent_all,
        gate_all,
        gate_columns,
        inputs1,
        query,
        key_value,
        heads,
        hidden,
        expert_in,
        gains,
    ) = front(
        (
            layer_input[0],
            query_key_value_weight,
            small,
            w_out.T,
            d_out[0],
            cosine_values,
            sine_values,
            routes[0].T,
        ),
        sizes,
    )
    layer_result, d_x, sum_rows, sum_out, sum_gate_up, sum_down = back(
        (
            gate_columns,
            gate_all,
            gains,
            cosine_values,
            sine_values,
            expert_in,
            cotangent_all,
            w_gate_up,
            w_down,
            layer_input[0],
            inputs1,
            query,
            key_value,
            heads,
            hidden,
            wk_all.reshape(-1, wk_all.shape[-1]),
            wq_all.reshape(-1, query_width),
            wo_all.reshape(-1, wo_all.shape[-1]),
        ),
        sizes,
    )[:6]
    return (
        layer_result[None],
        d_x[None],
        sum_rows[:, qkv_width + expert_total],
        sum_rows[:, :qkv_width],
        sum_out.T,
        sum_rows[:, qkv_width : qkv_width + expert_total],
        sum_rows[:, qkv_width + expert_total + 1],
        sum_gate_up,
        jnp.swapaxes(sum_down, 1, 2),
    )


def solution(mesh):
    in_specs = (
        P(("expert", "dp"), "context", None),
        P(("expert", "context", "dp")),
        P(("expert", "context", "dp"), None),
        P(None, ("expert", "context", "dp")),
        P(("expert", "context", "dp"), None),
        P(("expert", "context", "dp")),
        P("expert", None, None),
        P("expert", None, None),
        P(("expert", "dp"), "context", None),
        P(("expert", "dp"), "context", None),
    )
    out_specs = (
        P(("expert", "dp"), "context", None),
        P(("expert", "dp"), "context", None),
        P(("expert", "context", "dp")),
        P(("expert", "context", "dp"), None),
        P(None, ("expert", "context", "dp")),
        P(("expert", "context", "dp"), None),
        P(("expert", "context", "dp")),
        P("expert", ("context", "dp"), None),
        P("expert", None, ("context", "dp")),
    )
    sizes = tuple(mesh.shape[a] for a in ("expert", "context", "dp"))
    local = local_fused if sizes == (4, 4, 2) else local_plain
    return jax.shard_map(local, mesh=mesh, in_specs=in_specs, out_specs=out_specs, check_vma=False)
```

```python
import functools
import math

import jax
import jax.numpy as jnp
from jax import lax
from jax.experimental import pallas as pl
from jax.experimental.pallas import tpu as pltpu
from jax.sharding import PartitionSpec as P

QUERY_HEADS = 12
KEY_VALUE_HEADS = 2
HEAD_DIMENSION = 128
TOP = 4
EXP_DEV = 2

EPSILON = 1e-06
ROPE_BASE = 10000.0
MASKED = -1e30

F32 = jnp.float32
BF16 = jnp.bfloat16


def rope_tables(positions, width):
    halfway = width // 2
    fraction = jnp.arange(halfway, dtype=jnp.float32) * (2.0 / width)
    frequency = jnp.exp(-math.log(ROPE_BASE) * fraction)
    angles = positions.astype(jnp.float32)[:, None] * frequency[None, :]
    cosine_values = jnp.cos(angles)
    sine_values = jnp.sin(angles)
    return (
        jnp.concatenate([cosine_values, cosine_values], -1),
        jnp.concatenate([sine_values, sine_values], -1),
    )


def rotate_half(values, cosine_values, sine_values):
    halfway = values.shape[-1] // 2
    turned = jnp.concatenate([-values[..., halfway:], values[..., :halfway]], -1)
    return values * cosine_values[:, None, :] + turned * sine_values[:, None, :]


def rotate_back(grads, cosine_values, sine_values):
    halfway = grads.shape[-1] // 2
    scaled = grads * sine_values[:, None, :]
    turned = jnp.concatenate([scaled[..., halfway:], -scaled[..., :halfway]], -1)
    return grads * cosine_values[:, None, :] + turned


def dot_nt(a, b):
    return lax.dot_general(a, b, (((1,), (1,)), ((), ())), preferred_element_type=F32)


def dot_tn(a, b):
    return lax.dot_general(a, b, (((0,), (0,)), ((), ())), preferred_element_type=F32)


def dot_nn(a, b):
    return jnp.dot(a, b, preferred_element_type=F32)


def masked_probs(first_row, query, key):
    scores = dot_nt(query, key) * (HEAD_DIMENSION**-0.5)
    rows = first_row + lax.broadcasted_iota(jnp.int32, scores.shape, 0)
    columns = lax.broadcasted_iota(jnp.int32, scores.shape, 1)
    scores = jnp.where(columns <= rows, scores, MASKED)
    expd = jnp.exp(scores - jnp.max(scores, axis=-1, keepdims=True))
    return expd / jnp.sum(expd, axis=-1, keepdims=True)


def attend_forward_kernel(first_ref, query_ref, key_ref, value_ref, heads_ref):
    probs = masked_probs(first_ref[0], query_ref[...], key_ref[...])
    heads_ref[...] = dot_nn(probs.astype(BF16), value_ref[...]).astype(BF16)


def attend_forward(first_row, query, key_value):
    tokens, width = query.shape
    length = key_value.shape[0]
    group = QUERY_HEADS // KEY_VALUE_HEADS
    size = HEAD_DIMENSION
    return pl.pallas_call(
        attend_forward_kernel,
        grid_spec=pltpu.PrefetchScalarGridSpec(
            num_scalar_prefetch=1,
            grid=(QUERY_HEADS,),
            in_specs=[
                pl.BlockSpec((tokens, size), lambda h, s: (0, h)),
                pl.BlockSpec((length, size), lambda h, s: (0, h // group)),
                pl.BlockSpec((length, size), lambda h, s: (0, KEY_VALUE_HEADS + h // group)),
            ],
            out_specs=pl.BlockSpec((tokens, size), lambda h, s: (0, h)),
        ),
        out_shape=jax.ShapeDtypeStruct((tokens, width), BF16),
        compiler_params=pltpu.CompilerParams(vmem_limit_bytes=32 * 1024 * 1024),
        cost_estimate=pl.CostEstimate(
            flops=4 * tokens * length * width, bytes_accessed=4 * tokens * width, transcendentals=0
        ),
    )(first_row, query, key_value, key_value)


def attend_backward_kernel(
    first_ref, query_ref, key_ref, value_ref, grad_ref, d_query_ref, d_key_ref, d_value_ref
):
    query, key, value, grad = query_ref[...], key_ref[...], value_ref[...], grad_ref[...]
    probs = masked_probs(first_ref[0], query, key)
    d_probs = dot_nt(grad, value)
    inner = jnp.sum(probs * d_probs, axis=-1, keepdims=True)
    d_raw = (probs * (d_probs - inner) * (HEAD_DIMENSION**-0.5)).astype(BF16)
    d_query_ref[...] = dot_nn(d_raw, key)
    d_key = dot_tn(d_raw, query)
    d_value = dot_tn(probs.astype(BF16), grad)

    @pl.when(pl.program_id(1) == 0)
    def _():
        d_key_ref[...] = d_key
        d_value_ref[...] = d_value

    @pl.when(pl.program_id(1) > 0)
    def _():
        d_key_ref[...] += d_key
        d_value_ref[...] += d_value


def attend_backward(first_row, query, key_value, grad):
    tokens, width = query.shape
    length = key_value.shape[0]
    group = QUERY_HEADS // KEY_VALUE_HEADS
    size = HEAD_DIMENSION
    row_spec = pl.BlockSpec((tokens, size), lambda j, g, s: (0, j * group + g))
    return pl.pallas_call(
        attend_backward_kernel,
        grid_spec=pltpu.PrefetchScalarGridSpec(
            num_scalar_prefetch=1,
            grid=(KEY_VALUE_HEADS, group),
            in_specs=[
                row_spec,
                pl.BlockSpec((length, size), lambda j, g, s: (0, j)),
                pl.BlockSpec((length, size), lambda j, g, s: (0, KEY_VALUE_HEADS + j)),
                row_spec,
            ],
            out_specs=[
                row_spec,
                pl.BlockSpec((length, size), lambda j, g, s: (0, j)),
                pl.BlockSpec((length, size), lambda j, g, s: (0, j)),
            ],
        ),
        out_shape=[
            jax.ShapeDtypeStruct((tokens, width), F32),
            jax.ShapeDtypeStruct((length, KEY_VALUE_HEADS * size), F32),
            jax.ShapeDtypeStruct((length, KEY_VALUE_HEADS * size), F32),
        ],
        compiler_params=pltpu.CompilerParams(vmem_limit_bytes=32 * 1024 * 1024),
        cost_estimate=pl.CostEstimate(
            flops=10 * tokens * length * width, bytes_accessed=8 * tokens * width, transcendentals=0
        ),
    )(first_row, query, key_value, key_value, grad)


def exchange(values, axis, mask):
    size = lax.axis_size(axis)
    return lax.ppermute(values, axis, [(i, i ^ mask) for i in range(size)])


def axis_masks(axis):
    size = lax.axis_size(axis)
    masks, bit = [], 1
    while bit < size:
        masks.append(bit)
        bit *= 2
    return masks


def cube_gather(values, axis, masks):
    held = {0: values}
    for mask in masks:
        for r, block in list(held.items()):
            held[r ^ mask] = exchange(block, axis, mask)
    return [held[r] for r in range(lax.axis_size(axis))]


def cube_scatter(blocks, axis, masks):
    held = dict(enumerate(blocks))
    for mask in masks:
        kept = {}
        for r in list(held):
            if not r & mask:
                arrived = exchange(held[r ^ mask].astype(BF16), axis, mask)
                kept[r] = held[r].astype(F32) + arrived.astype(F32)
        held = kept
    return held[0]


def line_steps(values, axis, up):
    size = lax.axis_size(axis)
    pairs = [(i, i + 1) if up else (i + 1, i) for i in range(size - 1)]
    return lax.ppermute(values, axis, pairs)


def line_gather(values, axis, both=True):
    size = lax.axis_size(axis)
    me = lax.axis_index(axis)
    result = jnp.zeros((size + 1,) + values.shape, values.dtype)
    result = lax.dynamic_update_index_in_dim(result, values, me, 0)
    up = down = values
    for step in range(1, size):
        up = line_steps(up, axis, True)
        result = lax.dynamic_update_index_in_dim(
            result, up, jnp.where(me - step >= 0, me - step, size), 0
        )
        if both:
            down = line_steps(down, axis, False)
            result = lax.dynamic_update_index_in_dim(result, down, jnp.minimum(me + step, size), 0)
    return result[:size]


def line_scatter(take, axis, up=True, down=True):
    size = lax.axis_size(axis)
    me = lax.axis_index(axis)
    total = take(me).astype(F32)
    for active, sign in ((up, 1), (down, -1)):
        if not active:
            continue
        arrived = None
        for step in range(1, size):
            block = take((me + sign * (size - step)) % size).astype(F32)
            if arrived is not None:
                block = block + arrived.astype(F32)
            arrived = line_steps(block.astype(BF16), axis, sign > 0)
        total = total + arrived.astype(F32)
    return total


def gather_rows(shard):
    ne, nc, nd = (lax.axis_size(a) for a in ("expert", "context", "dp"))
    rows, width = shard.shape
    lines = line_gather(shard, "context")
    masks = axis_masks("expert")
    half = width // 256 * 128
    parts = [lines[..., :half], lines[..., half:]]
    me = lax.axis_index("expert")
    result = jnp.zeros((ne, nc, rows, width), shard.dtype)
    for start, part, order in ((0, parts[0], masks), (half, parts[1], masks[::-1])):
        for r, block in enumerate(cube_gather(part, "expert", order)):
            result = lax.dynamic_update_slice(result, block[None], (me ^ r, 0, 0, start))
    core = lax.axis_index("dp")
    whole = jnp.zeros((ne, nc, nd, rows, width), shard.dtype)
    for r, block in enumerate(cube_gather(result, "dp", axis_masks("dp"))):
        whole = lax.dynamic_update_slice(whole, block[:, :, None], (0, 0, core ^ r, 0, 0))
    return whole.reshape(-1, width)


def scatter_rows(grad):
    ne, nc, nd = (lax.axis_size(a) for a in ("expert", "context", "dp"))
    width = grad.shape[-1]
    rows = grad.shape[0] // (ne * nc * nd)
    blocks = grad.reshape(ne, nc, nd, rows, width)
    core, me = lax.axis_index("dp"), lax.axis_index("expert")
    mine = cube_scatter(
        [
            lax.dynamic_index_in_dim(blocks, core ^ r, 2, keepdims=False)
            for r in range(nd)
        ],
        "dp",
        axis_masks("dp"),
    )
    masks = axis_masks("expert")
    half = width // 256 * 128
    sums = []
    for part, order in ((mine[..., :half], masks), (mine[..., half:], masks[::-1])):
        sums.append(
            cube_scatter(
                [lax.dynamic_index_in_dim(part, me ^ r, 0, keepdims=False) for r in range(ne)],
                "expert",
                order,
            )
        )
    lines = jnp.concatenate(sums, -1)
    return line_scatter(
        lambda j: lax.dynamic_index_in_dim(lines, j, 0, keepdims=False), "context"
    )


def plane_gather(rows):
    masks = axis_masks("expert")
    half = rows.shape[-1] // 2
    left = cube_gather(rows[:, :half], "expert", masks)
    right = cube_gather(rows[:, half:], "expert", masks[::-1])
    return jnp.concatenate([jnp.concatenate(p, -1) for p in zip(left, right)], 0)


def plane_scatter(partial, tokens):
    masks = axis_masks("expert")
    size = lax.axis_size("expert")
    half = partial.shape[-1] // 2
    blocks = partial.reshape(size, tokens, -1)
    left = cube_scatter([blocks[r, :, :half] for r in range(size)], "expert", masks)
    right = cube_scatter([blocks[r, :, half:] for r in range(size)], "expert", masks[::-1])
    return jnp.concatenate([left, right], -1)


MESH = pl.DeviceIdType.MESH
MIB = 1024 * 1024
SMALL = 128
GATE_ROWS = 16


def flip(index, mask):
    bit = 1
    while bit <= mask:
        if mask & bit:
            index = index + bit - 2 * bit * lax.rem(lax.div(index, bit), 2)
        bit *= 2
    return index


class Wire:
    def __init__(self, sends, recvs):
        self.sends, self.recvs = sends, recvs
        self.n_sends = self.n_recvs = 0
        self.open = []

    def slots(self, count):
        first = self.n_recvs
        self.n_recvs += count
        return first

    def start(self, src, dst, recv, device, when=None):
        number = self.n_sends
        self.n_sends += 1

        def copy():
            return pltpu.make_async_remote_copy(
                src_ref=src() if callable(src) else src,
                dst_ref=dst() if callable(dst) else dst,
                send_sem=self.sends.at[number],
                recv_sem=self.recvs.at[recv],
                device_id=device,
                device_id_type=MESH,
            )

        guard(when, lambda: copy().start())
        self.open.append((when, copy))

    def arrived(self, dst, recv, device):
        pltpu.make_async_remote_copy(
            src_ref=dst,
            dst_ref=dst,
            send_sem=self.sends.at[0],
            recv_sem=self.recvs.at[recv],
            device_id=device,
            device_id_type=MESH,
        ).wait_recv()

    def finish(self):
        for when, copy in self.open:
            guard(when, lambda copy=copy: copy().wait_send())
        self.open = []


def guard(when, action):
    if when is None:
        action()
    else:
        pl.when(when)(action)


def add_into(dest, source, steps=4):
    rows = dest.shape[0] // steps

    @pl.loop(0, steps)
    def _(n):
        here = pl.ds(pl.multiple_of(n * rows, rows), rows)
        dest[here] = (dest[here].astype(F32) + source[here].astype(F32)).astype(BF16)


def greet(targets):
    barrier = pltpu.get_barrier_semaphore()
    for device, when in targets:
        guard(
            when,
            lambda device=device: pl.semaphore_signal(
                barrier, inc=1, device_id=device, device_id_type=MESH
            ),
        )
    count = sum(1 if when is None else when.astype(jnp.int32) for _, when in targets)
    pl.semaphore_wait(barrier, count)


def plane_ids(e):
    return {m: {"expert": flip(e, m)} for m in (1, 2, 3)}


class RowsGather:
    def __init__(self, wire, ref, e, z, c, nc, half, into=None, sems=None):
        self.into, self.sems = into, sems
        self.wire, self.ref, self.e, self.z, self.c, self.nc = wire, ref, e, z, c, nc
        self.cols = (pl.ds(0, half), pl.ds(half, ref.shape[-1] - half))
        self.line = wire.slots(nc)
        self.plane = wire.slots(nc * 6)
        self.core = wire.slots(nc)
        self.ids = plane_ids(e)

    def go(self, *steps):
        for step in steps:
            action = {"l": self.pass_on, "s": self.spread, "f": self.forward, "h": self.share, "c": self.complete}
            action[step[0]](*map(int, step[1:]))

    def shard(self, k):
        if k < 2:
            return flip(self.z, k)
        inner = (self.z > 0) & (self.z < self.nc - 1)
        return jnp.where(inner, flip(self.z, 5 - k), flip(self.z, k))

    def at(self, r, zs, half):
        return self.ref.at[flip(self.e, r), zs, self.c, :, self.cols[half]]

    def slot(self, k, r, half):
        return self.plane + k * 6 + (r - 1) * 2 + half

    def pass_on(self, k):
        wire, z, nc = self.wire, self.z, self.nc
        zs = self.shard(k)
        whole = self.ref.at[self.e, zs, self.c]
        if k:
            wire.arrived(whole, self.line + zs, {"context": zs})
        wire.start(
            whole, whole, self.line + zs, {"context": z + 1}, when=(zs <= z) & (z < nc - 1)
        )
        wire.start(whole, whole, self.line + zs, {"context": z - 1}, when=(zs >= z) & (z > 0))

    def spread(self, k):
        zs = self.shard(k)
        for half, mask in ((0, 1), (1, 2), (1, 1), (0, 2)):
            part = self.at(0, zs, half)
            self.wire.start(part, part, self.slot(k, mask, half), self.ids[mask])

    def forward(self, k):
        zs = self.shard(k)
        for half, mask in ((0, 1), (1, 2)):
            part = self.at(mask, zs, half)
            self.wire.arrived(part, self.slot(k, mask, half), self.ids[mask])
            self.wire.start(part, part, self.slot(k, 3, half), self.ids[3 - mask])

    def share(self, k):
        zs = self.shard(k)
        for r, half in ((1, 1), (2, 0), (3, 0), (3, 1)):
            self.wire.arrived(self.at(r, zs, half), self.slot(k, r, half), self.ids[r])
        part = self.ref.at[:, zs, self.c]
        self.wire.start(part, part, self.core + k, {"dp": 1 - self.c})
        if self.into is not None:
            self.load(k, self.c, 0).start()

    def load(self, k, core, number):
        zs = self.shard(k)
        return pltpu.make_async_copy(
            self.ref.at[:, zs, core], self.into.at[:, zs, core], self.sems.at[2 * k + number]
        )

    def complete(self):
        for k in range(self.nc):
            zs = self.shard(k)
            self.wire.arrived(self.ref.at[:, zs, 1 - self.c], self.core + k, {"dp": 1 - self.c})
            if self.into is not None:
                self.load(k, 1 - self.c, 1).start()
        if self.into is not None:
            for k in range(self.nc):
                self.load(k, self.c, 0).wait()
                self.load(k, 1 - self.c, 1).wait()


class PlaneGather:
    def __init__(self, wire, ref, e):
        self.wire, self.ref = wire, ref
        self.half = ref.shape[-1] // 2
        self.ids = plane_ids(e)
        self.first = wire.slots(6)

    def at(self, r, half):
        return self.ref.at[r, :, pl.ds(half * self.half, self.half)]

    def slot(self, r, half):
        return self.first + (r - 1) * 2 + half

    def send(self, r, half, to, mask):
        self.wire.start(
            lambda: self.at(r, half), lambda: self.at(to, half), self.slot(to, half), self.ids[mask]
        )

    def spread(self):
        for half, mask in ((0, 1), (1, 2), (1, 1), (0, 2)):
            self.send(0, half, mask, mask)

    def forward(self):
        for half, mask in ((0, 1), (1, 2)):
            self.wire.arrived(self.at(mask, half), self.slot(mask, half), self.ids[mask])
            self.send(mask, half, 3, 3 - mask)

    def near(self, r):
        half = 1 if r == 1 else 0
        self.wire.arrived(self.at(r, half), self.slot(r, half), self.ids[r])

    def far(self):
        for half in (0, 1):
            self.wire.arrived(self.at(3, half), self.slot(3, half), self.ids[3])

    def complete(self):
        self.near(1)
        self.near(2)
        self.far()


def swap_halves(values):
    return pltpu.roll(values, HEAD_DIMENSION // 2, 1)


class PlaneScatter:
    def __init__(self, wire, land, ids):
        self.wire, self.land, self.ids, self.part = wire, land, ids, None
        self.half = land.shape[-1]
        self.first = wire.slots(6)

    def send(self, source, mask, slot):
        self.wire.start(source, lambda: self.land.at[slot], self.first + slot, self.ids[mask])

    def near(self, r):
        self.send(self.part(r, r - 1), r, r - 1)

    def far(self):
        self.send(self.part(3, 0), 1, 2)
        self.send(self.part(3, 1), 2, 3)

    def relay(self, part=None):
        for half, r in ((0, 2), (1, 1)):
            slot = 2 + half
            self.wire.arrived(self.land.at[slot], self.first + slot, self.ids[3 - r])
            take = part or self.part
            mine = take(r, half)
            add_into(mine, self.land.at[slot])
            self.send(lambda r=r, half=half, take=take: take(r, half), r, 4 + half)

    def total(self, own):
        for slot, half, mask in ((0, 0, 1), (1, 1, 2), (4, 0, 2), (5, 1, 1)):
            self.wire.arrived(self.land.at[slot], self.first + slot, self.ids[mask])
            columns = pl.ds(half * self.half, self.half)
            rows = own.shape[0] // 4

            @pl.loop(0, 4)
            def _(n):
                here = pl.ds(pl.multiple_of(n * rows, rows), rows)
                own[here, columns] += self.land[slot, here].astype(F32)


class LineScatter:
    def __init__(self, wire, block, lands, z, nc, up=True):
        self.wire, self.block, self.lands, self.z, self.nc = wire, block, lands, z, nc
        self.up = up
        self.first = [wire.slots(nc - 1), wire.slots(nc - 1)]

    def arrive(self, way, index, j):
        land = self.lands[way].at[index]
        self.wire.arrived(land, self.first[way] + index, {"context": self.z})
        add_into(self.block(j), land, 1)

    def move(self, way, j, only=None):
        z, nc = self.z, self.nc
        inner, index = ((z > 0), j - z) if way == 0 else ((z < nc - 1), z - j)
        wanted = (j > z) if way == 0 else (j < z)
        if only is not None:
            wanted = wanted & only
        pl.when(wanted & inner)(lambda: self.arrive(way, index, j))
        self.leave(way, j, wanted)

    def step(self, s):
        if self.up:
            self.move(0, self.nc - s)
            self.move(1, s - 1)
        else:
            top = self.z == self.nc - 1
            if s == 1:
                for j in range(self.nc - 1):
                    self.leave(1, j, top)
            self.move(1, s - 1, jnp.logical_not(top))

    def leave(self, way, j, wanted):
        z = self.z
        index, near = (j - z, z + 1) if way == 0 else (z - j, z - 1)
        self.wire.start(
            self.block(j),
            self.lands[way].at[index - 1],
            self.first[way] + index - 1,
            {"context": near},
            when=wanted,
        )

    def last(self):
        if self.up:
            pl.when(self.z > 0)(lambda: self.arrive(0, 0, self.z))
        pl.when(self.z < self.nc - 1)(lambda: self.arrive(1, 0, self.z))


class RowsScatter:
    def __init__(self, wire, buf, core, plane, lines, e, z, c, nc, start, width, half):
        self.wire, self.buf, self.core, self.plane = wire, buf, core, plane
        self.e, self.c = e, c
        self.all = pl.ds(start, width)
        self.cols = (pl.ds(start, half), pl.ds(start + half, width - half))
        self.ids = plane_ids(e)
        self.core_slot = wire.slots(1)
        self.first = wire.slots(6)
        rows = buf.shape[2] // nc
        self.line = LineScatter(
            wire,
            lambda j: buf.at[c, e, pl.ds(pl.multiple_of(j * rows, rows), rows), self.all],
            lines,
            z,
            nc,
        )

    def share(self):
        self.wire.start(
            self.buf.at[1 - self.c, :, :, self.all], self.core, self.core_slot, {"dp": 1 - self.c}
        )

    def at(self, r, half):
        return self.buf.at[self.c, flip(self.e, r), :, self.cols[half]]

    def send(self, r, half, mask, slot):
        self.wire.start(
            self.at(r, half), self.plane(slot, half), self.first + slot, self.ids[mask]
        )

    def merge(self, before=None):
        self.wire.arrived(self.core, self.core_slot, {"dp": 1 - self.c})
        for r in (3, 1, 2, 0):
            block = flip(self.e, r)
            part = self.buf.at[self.c, block, :, self.all]
            add_into(part, self.core.at[block])
            if r == 3:
                if before is not None:
                    before()
                self.send(3, 0, 1, 2)
                self.send(3, 1, 2, 3)
            elif r:
                self.send(r, r - 1, r, r - 1)

    def add(self, r, half, slot, mask):
        land = self.plane(slot, half)
        self.wire.arrived(land, self.first + slot, self.ids[mask])
        add_into(self.at(r, half), land)

    def relay(self):
        for half, r in ((0, 2), (1, 1)):
            self.add(r, half, 2 + half, 3 - r)
            self.send(r, half, r, 4 + half)

    def total(self):
        for slot, half, mask in ((0, 0, 1), (1, 1, 2), (4, 0, 2), (5, 1, 1)):
            self.add(0, half, slot, mask)


class ExpertLine:
    def __init__(self, wire, base, land, sems, z, nc):
        self.wire, self.base, self.land = wire, base, land
        self.ins, self.out, self.sems, self.z, self.nc = None, None, sems, z, nc
        self.end = (z == 0) | (z == nc - 1)
        self.inner = jnp.logical_not(self.end)
        self.width = base.shape[-1] // EXP_DEV
        self.first = wire.slots((nc + 1) * EXP_DEV)
        self.sent = []

    def part(self, ref, j, i):
        return ref.at[j, :, pl.ds(i * self.width, self.width)]

    def combine(self, sources, stores):
        out, step = self.out, self.ins.shape[2]
        count = sources[0].shape[0] // step

        def loads(p):
            rows = pl.ds(p * step, step)
            return [
                pltpu.make_async_copy(source.at[rows], self.ins.at[k, p], self.sems.at[4 * k + p])
                for k, source in enumerate(sources)
            ]

        def store(p):
            pairs = stores(pl.ds(p * step, step), out.at[p % 2])
            return [
                pltpu.make_async_copy(source, dest, self.sems.at[16 + 2 * n + p % 2])
                for n, (source, dest) in enumerate(pairs)
            ]

        for p in range(count):
            for copy in loads(p):
                copy.start()
        for p in range(count):
            for copy in loads(p):
                copy.wait()
            if p > 1:
                for copy in store(p - 2):
                    copy.wait()
            total = self.ins[0, p].astype(F32)
            for k in range(1, len(sources)):
                total = total + self.ins[k, p].astype(F32)
            out[p % 2] = total.astype(out.dtype)
            for copy in store(p):
                copy.start()
        for p in range(max(0, count - 2), count):
            for copy in store(p):
                copy.wait()

    def copy(self, i, r, number):
        target, slot = flip(self.z, r), self.z
        if r == 3:
            target = jnp.where(self.end, flip(self.z, 1), target)
            slot = jnp.where(self.end, self.nc, slot)
        return pltpu.make_async_remote_copy(
            src_ref=self.part(self.base, flip(self.z, r), i),
            dst_ref=self.part(self.land, slot, i),
            send_sem=self.wire.sends.at[number],
            recv_sem=self.wire.recvs.at[self.first + slot * EXP_DEV + i],
            device_id={"context": target},
            device_id_type=MESH,
        )

    def send(self, i, r, when=None):
        number = len(self.sent)
        guard(when, self.copy(i, r, number).start)
        self.sent.append((when, i, r, number))

    def finish(self):
        for when, i, r, number in self.sent:
            guard(when, self.copy(i, r, number).wait_send)

    def arrived(self, slot, i):
        land = self.part(self.land, slot, i)
        self.wire.arrived(land, self.first + slot * EXP_DEV + i, {"context": self.z})

    def relay_loads(self, i, p):
        step = self.ins.shape[2]
        rows = pl.ds(p * step, step)
        sources = (self.part(self.base, flip(self.z, 2), i), self.part(self.land, self.nc, i))
        return [
            pltpu.make_async_copy(
                source.at[rows], self.ins.at[k, p], self.sems.at[4 * k + p]
            )
            for k, source in enumerate(sources)
        ]

    def relay_store(self, i, p):
        step = self.ins.shape[2]
        mine = self.part(self.base, flip(self.z, 2), i).at[pl.ds(p * step, step)]
        return pltpu.make_async_copy(self.ins.at[0, p], mine, self.sems.at[16 + p])

    def relay_steps(self):
        return range(self.base.shape[1] // self.ins.shape[2])

    def relay_begin(self, i):
        self.relayed = i

        def begin():
            self.arrived(self.nc, i)
            for p in self.relay_steps():
                for copy in self.relay_loads(i, p):
                    copy.start()

        pl.when(self.inner)(begin)

    def relay_add(self):
        i = self.relayed

        def add():
            for p in self.relay_steps():
                for copy in self.relay_loads(i, p):
                    copy.wait()
                a, b = (self.ins[k, p].astype(F32) for k in range(2))
                self.ins[0, p] = (a + b).astype(BF16)
                self.relay_store(i, p).start()

        pl.when(self.inner)(add)

    def relay_send(self, i):
        def wait():
            for p in self.relay_steps():
                self.relay_store(i, p).wait()

        pl.when(self.inner)(wait)
        self.send(i, 2, when=self.inner)

    def last(self, i, results):
        z = self.z
        sources = [self.part(self.base, z, i)]
        for r in (1, 2):
            self.arrived(flip(z, r), i)
            sources.append(self.part(self.land, flip(z, r), i))

        def stores(rows, wide):
            pairs, first = [], 0
            for result in results:
                columns = pl.ds(first, result.shape[-1])
                pairs.append((wide.at[:, columns], result.at[i, rows]))
                first += result.shape[-1]
            return pairs

        pl.when(self.end)(lambda: self.combine(sources, stores))

        def inner():
            self.arrived(flip(z, 3), i)
            self.combine(sources + [self.part(self.land, flip(z, 3), i)], stores)

        pl.when(self.inner)(inner)


def layer_kernel(
    nc,
    experts,
    cos_ref,
    sin_ref,
    routes_ref,
    x_hbm,
    qkv_hbm,
    small_hbm,
    wo_shard_hbm,
    d_out_hbm,
    w_gu_hbm,
    w_dn_hbm,
    layer_ref,
    d_x_ref,
    sum_q_ref,
    sum_o_ref,
    sum_gu_hbm,
    sum_dn_hbm,
    base_hbm,
    land_hbm,
    y_hbm,
    wq_hbm,
    wo_hbm,
    cot_hbm,
    inputs_hbm,
    query_hbm,
    heads_hbm,
    hidden_hbm,
    wk_all,
    kv_ref,
    gate_all,
    gates_ref,
    gains_ref,
    x_all,
    y_land,
    dx_land,
    core_land,
    plane_q,
    plane_k,
    lines_o,
    lines_q,
    lines_k,
    dkv_land,
    d_in_ref,
    dg_lanes,
    dg_part,
    dg_land,
    sends_f,
    recvs_f,
    sends_c,
    recvs_c,
    sends_1,
    recvs_1,
    sends_2,
    recvs_2,
    sends_e,
    recvs_e,
    hand_sends,
    hand_recvs,
    stage_sems,
    load_sems,
    out_sems,
    weight_sems,
    sum_sems,
    y_sems,
    credits,
):
    e, z, c = (lax.axis_index(a) for a in ("expert", "context", "dp"))
    size = HEAD_DIMENSION
    blocks, tokens, width = cot_hbm.shape
    ff = w_dn_hbm.shape[1]
    query_width = QUERY_HEADS * size
    key_width = KEY_VALUE_HEADS * size
    qkv_width = query_width + 2 * key_width
    rest = wk_all.shape[-1]
    grad_width = base_hbm.shape[-1]
    ids = plane_ids(e)
    sibling = {"dp": 1 - c}
    bottom, even = z == 0, lax.rem(z, 2) == 0
    wire_1, wire_2, wire_e = Wire(sends_1, recvs_1), Wire(sends_2, recvs_2), Wire(sends_e, recvs_e)
    expert = ExpertLine(wire_e, base_hbm, land_hbm, sum_sems, z, nc)
    wire_c = Wire(sends_c, recvs_c)
    gather_cot = PlaneGather(wire_c, cot_hbm, e)
    gather = PlaneGather(wire_1, x_all, e)
    scatter_dx = PlaneScatter(wire_1, dx_land, ids)
    scatter_y = PlaneScatter(wire_2, y_land, ids)
    dg_slot = wire_1.slots(3)

    def front_phase(wq_ref, wo_ref, x_ref, inputs_ref, query_ref, heads_ref, hidden_ref, kv_scr, q_scr):
        wire = Wire(sends_f, recvs_f)
        kv_width = 2 * key_width
        own = (
            (qkv_hbm.at[:, pl.ds(query_width, kv_width)], wk_all.at[e, z, c, :, pl.ds(0, kv_width)]),
            (small_hbm, wk_all.at[e, z, c, :, pl.ds(kv_width, SMALL)]),
            (qkv_hbm.at[:, pl.ds(0, query_width)], wq_hbm.at[e, z, c]),
            (wo_shard_hbm, wo_hbm.at[e, z, c]),
            (d_out_hbm, cot_hbm.at[0]),
            (x_hbm, x_ref),
        )
        copies = [
            pltpu.make_async_copy(source, dest, load_sems.at[n])
            for n, (source, dest) in enumerate(own)
        ]
        load_x = copies.pop()
        for copy in copies + [load_x]:
            copy.start()
        greet(
            [(ids[m], None) for m in (1, 2, 3)]
            + [(sibling, None)]
            + [({"context": z + d}, z + d < nc) for d in range(1, nc)]
            + [({"context": z - d}, z >= d) for d in range(1, nc)]
        )
        gather_k = RowsGather(wire, wk_all, e, z, c, nc, 256)
        gather_q = RowsGather(wire, wq_hbm, e, z, c, nc, 768, wq_ref, weight_sems.at[0])
        gather_o = RowsGather(wire, wo_hbm, e, z, c, nc, 768, wo_ref, weight_sems.at[1])
        for copy in copies:
            copy.wait()
        gather_k.go("l0", "s0")
        gather_q.go("s0")
        gather_k.go("l1", "s1", "f0", "l2", "s2")
        gather_q.go("l0")
        gather_k.go("f1", "h0", "l3", "s3")
        gather_q.go("l1", "s1")
        gather_o.go("l0")
        gather_k.go("f2", "h1", "f3")
        gather_q.go("l2", "s2")
        gather_k.go("h2")
        gather_o.go("l1")
        gather_q.go("f0")
        gather_k.go("h3")
        gather_q.go("l3", "s3")
        gather_k.go("c")
        load_x.wait()
        rows = x_ref[...].astype(F32)
        scale1 = lax.rsqrt(jnp.mean(rows * rows, -1, keepdims=True) + EPSILON)

        small = wk_all[:, :, :, :, pl.ds(kv_width, SMALL)].reshape(width, SMALL)
        small = jnp.transpose(small.astype(F32))
        gain_first, gain_second = small[experts : experts + 1], small[experts + 1 : experts + 2]
        gains_ref[0:1] = gain_first
        gains_ref[1:2] = gain_second
        inputs_ref[...] = (rows * scale1 * gain_first).astype(BF16)
        kv_scr[...] = dot_nn(inputs_ref[...], wk_all[...].reshape(width, kv_width + SMALL))

        def turned(head):
            return (head * cos_ref[...] + swap_halves(head) * sin_ref[...]).astype(BF16)

        line = wire.slots(KEY_VALUE_HEADS * nc)
        for j in range(KEY_VALUE_HEADS):
            kv_ref[j, z, :, pl.ds(0, size)] = turned(kv_scr[:, pl.ds(j * size, size)])
            value = kv_scr[:, pl.ds(kv_width // 2 + j * size, size)]
            kv_ref[j, z, :, pl.ds(size, size)] = value.astype(BF16)
            mine = kv_ref.at[j, z]
            for d in range(nc - 1, 0, -1):
                wire.start(mine, mine, line + j * nc + z, {"context": z + d}, when=z + d < nc)

        def keys_here(j):
            for d in range(1, nc):

                def wait(d=d):
                    wire.arrived(kv_ref.at[j, z - d], line + j * nc + z - d, {"context": z - d})

                pl.when(z >= d)(wait)

        outs = [
            pltpu.make_async_copy(source, dest, out_sems.at[n])
            for n, (source, dest) in enumerate(
                (
                    (inputs_ref, inputs_hbm),
                    (query_ref, query_hbm),
                    (heads_ref, heads_hbm),
                    (hidden_ref, hidden_hbm),
                )
            )
        ]
        outs[0].start()
        for later in range(1, nc):

            def clear(later=later):
                for j in range(KEY_VALUE_HEADS):
                    kv_ref[j, z + later] = jnp.zeros(kv_ref.shape[2:], BF16)

            pl.when(z + later < nc)(clear)
        gather_q.go("f1", "f2", "h0")
        gather_o.go("s0")
        gather_q.go("f3", "h1")
        gather_o.go("s1")
        gather_q.go("h2", "h3", "c")
        gather_o.go("f0", "f1")
        gather_cot.spread()

        @pl.loop(0, query_width // 256)
        def _(n):
            columns = pl.ds(pl.multiple_of(n * 256, 256), 256)
            q_scr[:, columns] = dot_nn(
                inputs_ref[...], wq_ref[:, :, :, :, columns].reshape(width, 256)
            )

        @pl.loop(0, QUERY_HEADS)
        def _(h):
            columns = pl.ds(pl.multiple_of(h * size, size), size)
            query_ref[:, columns] = turned(q_scr[:, columns])

        outs[1].start()

        logits = kv_scr[:, pl.ds(kv_width, SMALL)]
        lanes = lax.broadcasted_iota(jnp.int32, logits.shape, 1)
        routes = jnp.concatenate(
            [routes_ref[...].astype(F32), jnp.zeros((SMALL - TOP, tokens), F32)], 0
        )
        routes = jnp.transpose(routes).astype(jnp.int32)
        named = lanes == routes[:, 0:1]
        for k in range(1, TOP):
            named = named | (lanes == routes[:, k : k + 1])
        logits = jnp.where(named, logits, MASKED)
        expd = jnp.exp(logits - jnp.max(logits, -1, keepdims=True))
        gates = expd / jnp.sum(expd, -1, keepdims=True)
        gate_all[0] = jnp.transpose(gates)[:GATE_ROWS]
        gate_slot = wire.slots(3)
        for r in (1, 2, 3):
            wire.start(gate_all.at[0], gate_all.at[r], gate_slot + r - 1, ids[r])

        length = nc * tokens
        group = QUERY_HEADS // KEY_VALUE_HEADS

        def attend(first, last):
            j = first // group
            key = kv_ref[j, :, :, pl.ds(0, size)].reshape(length, size)
            value = kv_ref[j, :, :, pl.ds(size, size)].reshape(length, size)

            @pl.loop(first, last)
            def _(h):
                column = pl.multiple_of(h * size, size)
                scores = dot_nt(query_ref[:, pl.ds(column, size)], key) * (size**-0.5)
                row = z * tokens + lax.broadcasted_iota(jnp.int32, scores.shape, 0)
                place = lax.broadcasted_iota(jnp.int32, scores.shape, 1)
                scores = jnp.where(place <= row, scores, MASKED)
                expd = jnp.exp(scores - jnp.max(scores, -1, keepdims=True))
                total = jnp.sum(expd, -1, keepdims=True)
                mixed = dot_nn(expd.astype(BF16), value) / total
                heads_ref[:, pl.ds(column, size)] = mixed.astype(BF16)

        half = group // 2
        keys_here(0)
        attend(0, half)
        gather_o.go("l2", "s2")
        attend(half, group)
        gather_o.go("l3", "s3", "f2", "h0")
        keys_here(1)
        attend(group, group + half)
        gather_o.go("f3", "h1")
        attend(group + half, QUERY_HEADS)
        gather_o.go("h2")
        gather_cot.forward()
        gather_o.go("h3", "c")
        outs[2].start()
        part = width // wo_ref.shape[0]
        for block in range(wo_ref.shape[0]):
            weight = wo_ref[block].reshape(part, width)
            columns = pl.ds(block * part, part)
            hidden_ref[:, columns] = x_ref[:, columns].astype(F32) + dot_nt(heads_ref[...], weight)
        hidden = hidden_ref[...]
        scale2 = lax.rsqrt(jnp.mean(hidden * hidden, -1, keepdims=True) + EPSILON)
        x_all[0] = (hidden * scale2 * gains_ref[1:2]).astype(BF16)
        gather.spread()
        outs[3].start()
        for r in (1, 2, 3):
            wire.arrived(gate_all.at[r], gate_slot + r - 1, ids[r])
        for r in range(gate_all.shape[0]):
            zeros = jnp.zeros((SMALL - GATE_ROWS, tokens), F32)
            turned_gates = jnp.transpose(jnp.concatenate([gate_all[r], zeros], 0))
            both = [
                jnp.sum(jnp.where(lanes == e * EXP_DEV + i, turned_gates, 0.0), -1, keepdims=True)
                for i in range(EXP_DEV)
            ]
            gates_ref[r] = jnp.where(lanes == 0, both[0], jnp.where(lanes == 1, both[1], 0.0))
        for copy in outs:
            copy.wait()
        wire.finish()

    def token_phase(w_gu, w_dn, cot_all, a_all, dgu_all, y_stage, dx_part, stage, ins):
        expert.ins = ins
        scatter_dx.part = lambda r, half: dx_part.at[
            r - 1, :, pl.ds(half * width // 2, width // 2)
        ]
        sources = [
            (w_gu_hbm.at[0], w_gu.at[0]),
            (w_dn_hbm.at[0], w_dn.at[0]),
            (cot_hbm.at[0], cot_all.at[0]),
            (w_gu_hbm.at[1], w_gu.at[1]),
            (w_dn_hbm.at[1], w_dn.at[1]),
            (cot_hbm.at[1:], cot_all.at[1:]),
        ]
        loads = [
            pltpu.make_async_copy(source, dest, load_sems.at[n])
            for n, (source, dest) in enumerate(sources)
        ]
        for copy in loads[:5]:
            copy.start()
        step = 256
        wide = 512
        dg_lanes[...] = jnp.zeros_like(dg_lanes)

        def hidden_units(r, i, count=1):
            lane = lax.broadcasted_iota(jnp.int32, (1, SMALL), 1)
            here = pl.ds(r, count)
            flat = count * tokens

            @pl.loop(0, ff // step)
            def _(f):
                column = pl.multiple_of(f * step, step)
                rows = x_all[here].reshape(flat, width)
                grads = cot_all[here].reshape(flat, width)
                gate_part = dot_nn(rows, w_gu[i, :, pl.ds(column, step)])
                up_part = dot_nn(rows, w_gu[i, :, pl.ds(ff + column, step)])
                raw = dot_nt(grads, w_dn[i, pl.ds(column, step), :])
                gate = gates_ref[here].reshape(flat, SMALL)
                gate = jnp.sum(jnp.where(lane == i, gate, 0.0), -1, keepdims=True)
                sigma = jax.nn.sigmoid(gate_part)
                silu = gate_part * sigma
                act = silu * up_part
                lanes = lax.broadcasted_iota(jnp.int32, (flat, SMALL), 1)
                d_gate = jnp.where(
                    lanes == e * EXP_DEV + i, jnp.sum(act * raw, -1, keepdims=True), 0.0
                )
                dg_lanes[here] += d_gate.reshape(count, tokens, SMALL)

                def put(ref, first, values):
                    values = values.astype(BF16).reshape(count, tokens, step)
                    ref[here, :, pl.ds(pl.multiple_of(first, step), step)] = values

                put(a_all, i * ff + column, act * gate)
                d_act = raw * gate
                d_gate_part = d_act * up_part * sigma * (1.0 + gate_part * (1.0 - sigma))
                put(dgu_all, i * 2 * ff + column, d_gate_part)
                put(dgu_all, i * 2 * ff + ff + column, d_act * silu)

        def y_copy(r):
            return pltpu.make_async_copy(y_stage.at[r % 2], y_hbm.at[r], y_sems.at[r % 2])

        def outputs(r, count=1):
            here = pl.ds(r, count)
            flat = count * tokens

            @pl.loop(0, width // wide)
            def _(n):
                columns = pl.ds(pl.multiple_of(n * wide, wide), wide)
                low = dgu_all[here].reshape(flat, EXP_DEV * 2 * ff)
                d_rows = dot_nt(low[:, : 2 * ff], w_gu[0, columns, :])
                d_rows += dot_nt(low[:, 2 * ff :], w_gu[1, columns, :])
                weight = w_dn[:, :, columns].reshape(EXP_DEV * ff, wide)
                out = dot_nn(a_all[here].reshape(flat, EXP_DEV * ff), weight).astype(BF16)
                for k in range(count):
                    rows = slice(k * tokens, (k + 1) * tokens)
                    y_stage[(r + k) % 2, :, columns] = out[rows]
                    if r == 0:
                        d_in_ref[:, columns] = d_rows
                    else:
                        dx_part[r + k - 1, :, columns] = d_rows[rows].astype(BF16)

            for k in range(r, r + count):
                y_copy(k).start()
                dg_part[k] = jnp.transpose(dg_lanes[k])[:GATE_ROWS]
                if k:
                    wire_1.start(dg_part.at[k], dg_land.at[k - 1], dg_slot + k - 1, ids[k])

        half_rows = width // nc // 2
        def where(k):
            high = lax.rem(lax.div(z, 2) + 1 + lax.div(k, 2), 2)
            return 2 * high + lax.rem(z + 1 + k, 2)

        def keep(i, k):
            slot = lax.rem(k, 2)
            return pltpu.make_async_copy(
                stage.at[slot, c], expert.part(base_hbm, where(k), i), stage_sems.at[slot]
            )

        def hand(i, k):
            return pltpu.make_async_remote_copy(
                src_ref=stage.at[lax.rem(k, 2), 1 - c],
                dst_ref=core_land.at[k],
                send_sem=hand_sends.at[i * nc + k],
                recv_sem=hand_recvs.at[i * nc + k],
                device_id=sibling,
                device_id_type=MESH,
            )

        def settle(i, k):
            hand(i, k).wait_recv()
            add_into(stage.at[lax.rem(k, 2), c], core_land.at[k])
            keep(i, k).start()

        def clear(i, k):
            keep(i, k).wait()
            hand(i, k).wait_send()

        def leave(i, r):
            if i == 0 and r == 2:
                expert.send(i, r, when=expert.end)
            elif i == 0 and r == 1 or r == 3:
                expert.send(i, r)
            elif r == 2:
                expert.send(i, r, when=bottom)
            elif r == 1:
                expert.send(i, r, when=even)

        def weight_grads(i, between=lambda k: None):
            @pl.loop(0, nc)
            def _(k):
                @pl.when(k >= 2)
                def _():
                    clear(i, k - 2)

                for n in (2, 3):

                    @pl.when(k == n)
                    def _(n=n):
                        leave(i, 5 - n)

                rows_at = pl.ds(pl.multiple_of(where(k) * 2 * half_rows, 2 * half_rows), 2 * half_rows)
                for first, source, grad, start, count in (
                    (0, x_all, dgu_all, i * 2 * ff, 2),
                    (2 * ff, cot_all, a_all, i * ff, 1),
                ):
                    rows = source[:, :, rows_at].reshape(blocks * tokens, 2 * half_rows)

                    @pl.loop(0, count)
                    def _(n):
                        column = pl.multiple_of(n * ff, ff)
                        part = grad[:, :, pl.ds(pl.multiple_of(start + column, ff), ff)]
                        result = dot_tn(rows, part.reshape(blocks * tokens, ff)).astype(BF16)
                        stage[lax.rem(k, 2), :, :, pl.ds(pl.multiple_of(first + column, ff), ff)] = (
                            result.reshape(2, half_rows, ff)
                        )

                if i:

                    @pl.when(k == 0)
                    def _():
                        pl.semaphore_wait(credits.at[3], 1)

                hand(i, k).start()

                @pl.when(k >= 1)
                def _():
                    settle(i, k - 1)

                between(k)

        for copy in loads[:3]:
            copy.wait()
        gather_cot.complete()
        loads[5].start()
        for copy in loads[3:5]:
            copy.wait()

        @pl.loop(0, EXP_DEV)
        def _(i):
            hidden_units(0, i)

        gather.forward()
        outputs(0)
        loads[5].wait()
        gather.near(1)
        gather.near(2)
        hidden_units(1, 0, 2)
        gather.far()
        hidden_units(3, 0)
        weight_grads(0)
        hidden_units(1, 1, 2)
        clear(0, nc - 2)
        leave(0, 1)
        settle(0, nc - 1)
        pl.semaphore_signal(credits.at[3], inc=1, device_id=sibling, device_id_type=MESH)
        y_copy(0).wait()
        outputs(1, 2)
        scatter_dx.near(1)
        scatter_dx.near(2)
        hidden_units(3, 1)
        expert.relay_begin(0)
        y_copy(1).wait()
        outputs(3)
        scatter_dx.far()
        clear(0, nc - 1)
        expert.relay_add()

        def between(k):
            @pl.when(k == 0)
            def _():
                expert.relay_send(0)

            @pl.when(k == 1)
            def _():
                scatter_dx.relay()

        weight_grads(1, between)
        scatter_dx.total(d_in_ref)
        for r in (1, 2):
            pl.semaphore_signal(credits.at[r], inc=1, device_id=ids[r], device_id_type=MESH)
        settle(1, nc - 1)
        for k in (nc - 2, nc - 1):
            clear(1, k)
        leave(1, 1)
        y_copy(3).wait()
        y_copy(2).wait()
        wire_1.finish()
        wire_c.finish()
        pl.semaphore_signal(credits.at[0], inc=1, device_id=sibling, device_id_type=MESH)

    def token_rows_phase(
        weight,
        grads_o,
        grads_q,
        x_ref,
        inputs_ref,
        query_ref,
        heads_ref,
        hidden_ref,
        d_hidden_ref,
        d_attn_ref,
        d_heads_ref,
        d_all_ref,
        rows_ref,
        dkv_acc,
        dkv_ref,
        y_relay,
        ins,
        out_wide,
    ):
        expert.ins, expert.out = ins, out_wide
        cot_ref, d_inputs_ref = d_heads_ref, hidden_ref
        scatter_y.part = lambda r, half: y_hbm.at[r, :, pl.ds(half * width // 2, width // 2)]
        y_loads = [
            pltpu.make_async_copy(scatter_y.part(2 - half, half), y_relay.at[half], y_sems.at[half])
            for half in range(2)
        ]
        for copy in y_loads:
            copy.start()
        planes = grads_o.shape[1]
        part = width // planes
        sources = (
            (hidden_hbm, hidden_ref),
            (cot_hbm.at[0], cot_ref),
            (wo_hbm, weight),
            (heads_hbm, heads_ref),
            (query_hbm, query_ref),
            (x_hbm, x_ref),
            (inputs_hbm, inputs_ref),
        )
        loads = [
            pltpu.make_async_copy(source, dest, load_sems.at[4 + n])
            for n, (source, dest) in enumerate(sources)
        ]
        for copy in loads:
            copy.start()
        for r in (1, 2):
            scatter_y.near(r)
        scatter_y.far()

        def rows_scatter(buf, core, plane, lines, start, count, half):
            return RowsScatter(
                wire_2,
                buf,
                core,
                plane,
                [lines.at[0], lines.at[1]],
                e,
                z,
                c,
                nc,
                start,
                count,
                half,
            )

        rows_of = part // 2
        scatter_o = rows_scatter(
            grads_o,
            x_all.at[:, pl.ds(0, rows_of)],
            lambda slot, half: dx_land.at[slot, pl.ds(0, rows_of)],
            lines_o,
            0,
            width,
            width // 2,
        )
        scatter_q = rows_scatter(
            grads_q,
            core_land.at[:, :, pl.ds(0, query_width)],
            lambda slot, half: plane_q.at[slot],
            lines_q,
            0,
            query_width,
            query_width // 2,
        )
        rest_half = rest // 256 * 128
        scatter_k = rows_scatter(
            grads_q,
            core_land.at[:, :, pl.ds(query_width, rest)],
            lambda slot, half: plane_k.at[
                slot, :, pl.ds(0, rest - rest_half if half else rest_half)
            ],
            lines_k,
            query_width,
            rest,
            rest_half,
        )
        scatter_kv = [
            LineScatter(
                wire_2,
                lambda j, h=h: dkv_ref.at[h, j],
                [dkv_land.at[h], dkv_land.at[h]],
                z,
                nc,
                up=False,
            )
            for h in range(KEY_VALUE_HEADS)
        ]

        loads[0].wait()
        loads[1].wait()
        hidden, d_in = hidden_ref[...], d_in_ref[...]
        scale2 = lax.rsqrt(jnp.mean(hidden * hidden, -1, keepdims=True) + EPSILON)
        scaled = d_in * gains_ref[1:2]
        mean = jnp.mean(scaled * hidden, -1, keepdims=True)
        d_hidden = cot_ref[...].astype(F32) + scale2 * scaled
        d_hidden = d_hidden - hidden * (scale2 * scale2 * scale2 * mean)
        d_hidden_ref[...] = d_hidden
        d_attn_ref[...] = d_hidden.astype(BF16)
        rows_ref[...] = jnp.zeros_like(rows_ref)
        rows_ref[experts + 1 : experts + 2, :] = jnp.sum(d_in * hidden * scale2, 0, keepdims=True)

        loads[2].wait()

        @pl.loop(0, query_width // 256)
        def _(n):
            columns = pl.ds(pl.multiple_of(n * 256, 256), 256)
            out = weight[:, :, :, :, columns].reshape(width, 256)
            d_heads_ref[:, columns] = dot_nn(d_attn_ref[...], out).astype(BF16)

        load_q = pltpu.make_async_copy(wq_hbm, weight, load_sems.at[0])
        load_q.start()
        loads[3].wait()

        def row_grads(buf, left, right, first, count, extra=None):
            @pl.loop(0, planes)
            def _(block):
                columns = pl.ds(pl.multiple_of(block * part, part), part)
                result = dot_tn(left[:, columns], right)
                if extra is not None:
                    result = result + extra(columns)
                result = result.astype(BF16).reshape(nc, 2, part // nc // 2, count)
                for half in range(2):
                    buf[half, block, :, pl.ds(first, count)] = result[:, half].reshape(
                        part // 2, count
                    )

        row_grads(grads_o, d_attn_ref, heads_ref[...], 0, width)
        pl.semaphore_wait(credits.at[0], 1)
        scatter_o.share()
        y_own = pltpu.make_async_copy(y_hbm.at[0], heads_ref, load_sems.at[2])
        y_own.start()

        length = nc * tokens
        group = QUERY_HEADS // KEY_VALUE_HEADS
        loads[4].wait()
        dkv_acc[...] = jnp.zeros_like(dkv_acc)

        def attend(j, first, last):
            key = kv_ref[j, :, :, pl.ds(0, size)].reshape(length, size)
            value = kv_ref[j, :, :, pl.ds(size, size)].reshape(length, size)

            @pl.loop(j * group + first, j * group + last)
            def _(h):
                columns = pl.ds(pl.multiple_of(h * size, size), size)
                query, grad = query_ref[:, columns], d_heads_ref[:, columns]
                probs = masked_probs(z * tokens, query, key)
                d_probs = dot_nt(grad, value)
                inner = jnp.sum(probs * d_probs, axis=-1, keepdims=True)
                d_raw = (probs * (d_probs - inner) * (size**-0.5)).astype(BF16)
                d_query = dot_nn(d_raw, key)
                d_query = d_query * cos_ref[...] - swap_halves(d_query) * sin_ref[...]
                d_all_ref[:, columns] = d_query.astype(BF16)
                dkv_acc[j, :, pl.ds(0, size)] += dot_tn(d_raw, query)
                dkv_acc[j, :, pl.ds(size, size)] += dot_tn(probs.astype(BF16), grad)

        def round_kv(j):
            for block in range(nc):
                rows = dkv_acc[j, pl.ds(block * tokens, tokens), :]
                dkv_ref[j, block] = rows.astype(BF16)

        def enter():
            pl.semaphore_wait(credits.at[1], 1)
            pl.semaphore_wait(credits.at[2], 1)

        attend(0, 0, group)
        round_kv(0)
        scatter_kv[0].step(1)
        scatter_o.merge(enter)
        for copy in y_loads:
            copy.wait()
        scatter_y.relay(lambda r, half: y_relay.at[half])
        attend(1, 0, group // 2)
        scatter_kv[0].step(2)
        attend(1, group // 2, group)
        round_kv(1)
        scatter_kv[1].step(1)
        for r in (2, 1):
            expert.send(1, r, when=z == nc - 1)
        scatter_kv[0].step(3)
        scatter_o.relay()

        for copy in loads[5:]:
            copy.wait()
        row_grads(grads_q, inputs_ref, d_all_ref[:, pl.ds(0, query_width)], 0, query_width)
        scatter_q.share()
        scatter_kv[1].step(2)
        scatter_kv[1].step(3)
        expert.send(1, 1, when=z == 1)
        expert.relay_begin(1)
        y_own.wait()
        hidden_ref[...] += heads_ref[...].astype(F32)
        scatter_y.total(hidden_ref)
        layer_ref[...] = hidden_ref[...].astype(BF16)
        scatter_o.total()
        scatter_q.merge()
        for h in range(KEY_VALUE_HEADS):
            scatter_kv[h].last()
        expert.relay_add()
        expert.relay_send(1)

        for h in range(KEY_VALUE_HEADS):
            grad = dkv_ref[h, z, :, pl.ds(0, size)].astype(F32)
            grad = grad * cos_ref[...] - swap_halves(grad) * sin_ref[...]
            d_all_ref[:, pl.ds(query_width + h * size, size)] = grad.astype(BF16)
            d_all_ref[:, pl.ds(query_width + key_width + h * size, size)] = dkv_ref[
                h, z, :, pl.ds(size, size)
            ]

        total = dg_part[0]
        for r in (1, 2, 3):
            wire_1.arrived(dg_land.at[r - 1], dg_slot + r - 1, ids[r])
            total = total + dg_land[r - 1]
        gates = gate_all[0]
        d_logits = gates * (total - jnp.sum(gates * total, 0, keepdims=True))
        d_logits = jnp.concatenate(
            [d_logits, jnp.zeros((SMALL - d_logits.shape[0], tokens), F32)], 0
        )
        d_all_ref[:, pl.ds(qkv_width, SMALL)] = jnp.transpose(d_logits).astype(BF16)

        load_q.wait()

        @pl.loop(0, planes)
        def _(block):
            columns = pl.ds(pl.multiple_of(block * part, part), part)
            rows_q = weight[block].reshape(part, query_width)
            rows_k = wk_all[block].reshape(part, rest)
            d_inputs_ref[:, columns] = dot_nt(
                d_all_ref[:, pl.ds(0, query_width)], rows_q
            ) + dot_nt(d_all_ref[:, pl.ds(query_width, rest)], rows_k)

        rows = x_ref[...].astype(F32)
        scale1 = lax.rsqrt(jnp.mean(rows * rows, -1, keepdims=True) + EPSILON)
        d_inputs = d_inputs_ref[...]
        rows_ref[experts : experts + 1, :] = jnp.sum(d_inputs * rows * scale1, 0, keepdims=True)

        def extra(columns):
            small = jnp.transpose(rows_ref[:, columns])
            return jnp.concatenate([jnp.zeros((part, rest - SMALL), F32), small], 1)

        row_grads(
            grads_q, inputs_ref, d_all_ref[:, pl.ds(query_width, rest)], query_width, rest, extra
        )
        scatter_k.share()
        scatter_q.relay()
        scatter_k.merge()
        scaled = d_inputs_ref[...] * gains_ref[0:1]
        rows = x_ref[...].astype(F32)
        scale1 = lax.rsqrt(jnp.mean(rows * rows, -1, keepdims=True) + EPSILON)
        mean = jnp.mean(scaled * rows, -1, keepdims=True)
        d_x = d_hidden_ref[...] + scale1 * scaled - rows * (scale1 * scale1 * scale1 * mean)
        d_x_ref[...] = d_x.astype(BF16)
        scatter_q.total()
        expert.last(0, (sum_gu_hbm, sum_dn_hbm))
        scatter_k.relay()
        scatter_o.line.step(1)
        scatter_q.line.step(1)
        scatter_k.total()
        scatter_k.line.step(1)
        for s in range(2, nc):
            for scatter in (scatter_o, scatter_q, scatter_k):
                scatter.line.step(s)
        for scatter in (scatter_o, scatter_q, scatter_k):
            scatter.line.last()
        sum_o_ref[...] = scatter_o.line.block(z)[...].astype(F32)
        sum_q_ref[...] = grads_q[c, e, pl.ds(pl.multiple_of(z * (rows_of // nc), rows_of // nc), rows_of // nc)].astype(F32)
        expert.last(1, (sum_gu_hbm, sum_dn_hbm))
        wire_2.finish()
        expert.finish()

    held = EXP_DEV
    weight_shape = wq_hbm.shape
    pl.run_scoped(
        front_phase,
        pltpu.VMEM(weight_shape, BF16),
        pltpu.VMEM(weight_shape, BF16),
        pltpu.VMEM((tokens, width), BF16),
        pltpu.VMEM((tokens, width), BF16),
        pltpu.VMEM((tokens, query_width), BF16),
        pltpu.VMEM((tokens, query_width), BF16),
        pltpu.VMEM((tokens, width), F32),
        pltpu.VMEM((tokens, rest), F32),
        pltpu.VMEM((tokens, query_width), F32),
    )
    shard, step = width // nc // 2, 48
    pl.run_scoped(
        token_phase,
        pltpu.VMEM((held, width, 2 * ff), BF16),
        pltpu.VMEM((held, ff, width), BF16),
        pltpu.VMEM((blocks, tokens, width), BF16),
        pltpu.VMEM((blocks, tokens, held * ff), BF16),
        pltpu.VMEM((blocks, tokens, held * 2 * ff), BF16),
        pltpu.VMEM((2, tokens, width), BF16),
        pltpu.VMEM((blocks - 1, tokens, width), BF16),
        pltpu.VMEM((2, 2, shard, grad_width // held), BF16),
        pltpu.VMEM((2, shard // step, step, grad_width // held), BF16),
    )
    rows_half = width // blocks // 2
    pl.run_scoped(
        token_rows_phase,
        pltpu.VMEM(weight_shape, BF16),
        pltpu.VMEM((2, blocks, rows_half, width), BF16),
        pltpu.VMEM((2, blocks, rows_half, qkv_width + SMALL), BF16),
        pltpu.VMEM((tokens, width), BF16),
        pltpu.VMEM((tokens, width), BF16),
        pltpu.VMEM((tokens, query_width), BF16),
        pltpu.VMEM((tokens, query_width), BF16),
        pltpu.VMEM((tokens, width), F32),
        pltpu.VMEM((tokens, width), F32),
        pltpu.VMEM((tokens, width), BF16),
        pltpu.VMEM((tokens, query_width), BF16),
        pltpu.VMEM((tokens, qkv_width + SMALL), BF16),
        pltpu.VMEM((SMALL, width), F32),
        pltpu.VMEM((KEY_VALUE_HEADS, nc * tokens, 2 * size), F32),
        pltpu.VMEM((KEY_VALUE_HEADS, nc, tokens, 2 * size), BF16),
        pltpu.VMEM((2, tokens, width // 2), BF16),
        pltpu.VMEM((4, shard // step, step, grad_width // held), BF16),
        pltpu.VMEM((2, step, grad_width // held), F32),
    )


def layer(operands, sizes):
    ne, nc, nd = sizes
    x, qkv_shard, small = operands[3:6]
    w_dn = operands[9]
    tokens, width = x.shape
    held, ff = w_dn.shape[0], w_dn.shape[1]
    query_width = QUERY_HEADS * HEAD_DIMENSION
    rows, qkv_width = qkv_shard.shape
    rest = qkv_width - query_width + SMALL
    rest_half = rest // 256 * 128
    shard, grads = width // (nc * nd), held * 3 * ff
    kv_size = 2 * HEAD_DIMENSION
    weight = (ne, nc, nd, rows, query_width)
    shapes = [
        ((tokens, width), BF16),
        ((tokens, width), BF16),
        ((rows, qkv_width + SMALL), F32),
        ((rows, width), F32),
        ((held, shard, 2 * ff), F32),
        ((held, shard, ff), F32),
        ((nc, shard, grads), BF16),
        ((nc + 1, shard, grads), BF16),
        ((ne, tokens, width), BF16),
        (weight, BF16),
        (weight, BF16),
        ((ne, tokens, width), BF16),
        ((tokens, width), BF16),
        ((tokens, query_width), BF16),
        ((tokens, query_width), BF16),
        ((tokens, width), F32),
    ]
    vmem = pl.BlockSpec(memory_space=pltpu.VMEM)
    anywhere = pl.BlockSpec(memory_space=pl.ANY)
    units = nc * held
    sems = [120, 110, 6, 6, 16, 16, 64, 64, 2 * units, (nc + 1) * held, units, units, 2, 12, 4]
    return pl.pallas_call(
        functools.partial(layer_kernel, nc, EXP_DEV * ne),
        out_shape=[jax.ShapeDtypeStruct(*s) for s in shapes],
        in_specs=[vmem] * 3 + [anywhere] * (len(operands) - 3),
        out_specs=[vmem] * 4 + [anywhere] * (len(shapes) - 4),
        scratch_shapes=[
            pltpu.VMEM((ne, nc, nd, rows, rest), BF16),
            pltpu.VMEM((KEY_VALUE_HEADS, nc, tokens, kv_size), BF16),
            pltpu.VMEM((ne, GATE_ROWS, tokens), F32),
            pltpu.VMEM((ne, tokens, SMALL), F32),
            pltpu.VMEM((8, width), F32),
            pltpu.VMEM((ne, tokens, width), BF16),
            pltpu.VMEM((6, tokens, width // 2), BF16),
            pltpu.VMEM((6, tokens, width // 2), BF16),
            pltpu.VMEM((nc, shard, grads // held), BF16),
            pltpu.VMEM((6, nc * rows, query_width // 2), BF16),
            pltpu.VMEM((6, nc * rows, rest - rest_half), BF16),
            pltpu.VMEM((2, nc - 1, rows, width), BF16),
            pltpu.VMEM((2, nc - 1, rows, query_width), BF16),
            pltpu.VMEM((2, nc - 1, rows, rest), BF16),
            pltpu.VMEM((KEY_VALUE_HEADS, nc - 1, tokens, kv_size), BF16),
            pltpu.VMEM((tokens, width), F32),
            pltpu.VMEM((ne, tokens, SMALL), F32),
            pltpu.VMEM((ne, GATE_ROWS, tokens), F32),
            pltpu.VMEM((ne - 1, GATE_ROWS, tokens), F32),
        ]
        + [pltpu.SemaphoreType.DMA((count,)) for count in sems]
        + [
            pltpu.SemaphoreType.DMA((2, 2 * nc)),
            pltpu.SemaphoreType.DMA((20,)),
            pltpu.SemaphoreType.DMA((2,)),
            pltpu.SemaphoreType.REGULAR((4,)),
        ],
        compiler_params=pltpu.CompilerParams(
            collective_id=0, has_side_effects=True, vmem_limit_bytes=63 * MIB
        ),
    )(*operands)


def local_plain(
    layer_input,
    gain_attn,
    query_key_value_weight,
    w_out,
    w_router,
    gain_ffn,
    w_gate_up,
    w_down,
    routes,
    d_out,
):
    tokens = layer_input.shape[1]
    model_width = layer_input.shape[2]
    ne, nc, nd = (lax.axis_size(a) for a in ("expert", "context", "dp"))
    expert_total = EXP_DEV * ne
    ff = w_down.shape[1]
    me = lax.axis_index("expert")
    first_row = lax.axis_index("context") * tokens
    query_width = QUERY_HEADS * HEAD_DIMENSION
    key_width = KEY_VALUE_HEADS * HEAD_DIMENSION
    qkv_width = query_width + 2 * key_width

    small = jnp.concatenate([w_router, gain_attn[:, None], gain_ffn[:, None]], -1)
    small = jnp.pad(small, ((0, 0), (0, 128 - small.shape[1])))
    gathered = gather_rows(jnp.concatenate([query_key_value_weight, small], -1))
    out_turned = gather_rows(w_out.T)
    qkv_weight = gathered[:, :qkv_width]
    router_weight = gathered[:, qkv_width : qkv_width + expert_total]
    gains = gathered[:, qkv_width + expert_total : qkv_width + expert_total + 2].T.astype(F32)
    gain_first, gain_second = gains[0], gains[1]
    cotangent_all = plane_gather(d_out[0])

    token_rows = layer_input[0].astype(F32)
    scale1 = lax.rsqrt(jnp.mean(token_rows * token_rows, -1, keepdims=True) + EPSILON)
    inputs1 = (token_rows * scale1 * gain_first).astype(BF16)
    query_key_value = dot_nn(inputs1, qkv_weight)
    cosine_values, sine_values = rope_tables(first_row + jnp.arange(tokens), HEAD_DIMENSION)
    rotated = rotate_half(
        query_key_value[:, : query_width + key_width].reshape(tokens, -1, HEAD_DIMENSION),
        cosine_values,
        sine_values,
    ).reshape(tokens, -1)
    query = rotated[:, :query_width].astype(BF16)
    key_value_local = jnp.concatenate(
        [rotated[:, query_width:], query_key_value[:, query_width + key_width :]], -1
    ).astype(BF16)
    key_value = line_gather(key_value_local, "context", both=False).reshape(nc * tokens, -1)
    first = first_row.astype(jnp.int32).reshape(1)
    heads = attend_forward(first, query, key_value)

    logits = dot_nn(inputs1, router_weight)
    chosen_ids = routes[0]
    picks = (chosen_ids[:, :, None] == jnp.arange(expert_total)[None, None, :]).astype(F32)
    chosen = jnp.sum(picks * logits[:, None, :], -1)
    gates = jax.nn.softmax(chosen, axis=-1)
    gate_dense = jnp.sum(picks * gates[:, :, None], 1).T
    gate_blocks = cube_gather(gate_dense, "expert", axis_masks("expert"))
    gate_local = jnp.concatenate(
        [lax.dynamic_slice_in_dim(b, me * EXP_DEV, EXP_DEV, 0) for b in gate_blocks], 1
    )

    attn = dot_nt(heads, out_turned)
    hidden = token_rows + attn
    scale2 = lax.rsqrt(jnp.mean(hidden * hidden, -1, keepdims=True) + EPSILON)
    expert_in = (hidden * scale2 * gain_second).astype(BF16)

    rows_all = plane_gather(expert_in)
    gate_up = jnp.einsum("td,edf->etf", rows_all, w_gate_up, preferred_element_type=F32)
    gate_part, up_part = gate_up[..., :ff], gate_up[..., ff:]
    sigma = jax.nn.sigmoid(gate_part)
    silu = gate_part * sigma
    act = silu * up_part
    gate_column = gate_local[:, :, None]
    act_gated = (act * gate_column).astype(BF16)
    partial_out = jnp.einsum("etf,efd->td", act_gated, w_down, preferred_element_type=F32)
    mixture = plane_scatter(partial_out.astype(BF16), tokens)
    layer_result = (hidden + mixture).astype(BF16)

    d_act_raw = jnp.einsum("td,efd->etf", cotangent_all, w_down, preferred_element_type=F32)
    d_gates_local = jnp.sum(d_act_raw * act, -1)
    d_act = d_act_raw * gate_column
    d_gate_part = d_act * up_part * sigma * (1.0 + gate_part * (1.0 - sigma))
    d_up_part = d_act * silu
    d_gate_up = jnp.concatenate([d_gate_part, d_up_part], -1).astype(BF16)
    d_rows = jnp.einsum("etf,edf->td", d_gate_up, w_gate_up, preferred_element_type=F32)
    grad_down = jnp.einsum("td,etf->edf", cotangent_all, act_gated, preferred_element_type=F32)
    grad_gate_up = jnp.einsum("td,etf->edf", rows_all, d_gate_up, preferred_element_type=F32)

    d_expert_in = plane_scatter(d_rows.astype(BF16), tokens)
    d_gate_blocks = d_gates_local.reshape(EXP_DEV, ne, tokens)
    d_gates_dense = jnp.zeros((expert_total, tokens), F32)
    for r in range(ne):
        arrived = d_gate_blocks[:, r]
        if r:
            arrived = exchange(arrived, "expert", r)
        d_gates_dense = lax.dynamic_update_slice(d_gates_dense, arrived, ((me ^ r) * EXP_DEV, 0))
    d_gates = jnp.sum(picks * d_gates_dense.T[:, None, :], -1)
    d_chosen = gates * (d_gates - jnp.sum(gates * d_gates, -1, keepdims=True))
    d_logits = jnp.sum(picks * d_chosen[:, :, None], 1).astype(BF16)
    grad_router = dot_tn(inputs1, d_logits)

    core = lax.axis_index("dp")
    part = model_width // (nc * nd)

    def scatter_experts(grad):
        blocks = grad.reshape(EXP_DEV, nc, nd, part, -1)
        mine = cube_scatter(
            [lax.dynamic_index_in_dim(blocks, core ^ r, 2, keepdims=False) for r in range(nd)],
            "dp",
            axis_masks("dp"),
        )
        return line_scatter(
            lambda j: lax.dynamic_index_in_dim(mine, j, 1, keepdims=False), "context"
        )

    sum_gate_up = scatter_experts(grad_gate_up)
    sum_down = jnp.swapaxes(scatter_experts(grad_down), 1, 2)

    cotangent = d_out[0].astype(F32)
    scaled2 = d_expert_in * gain_second
    d_hidden = (
        cotangent
        + scale2 * scaled2
        - hidden * (scale2 * scale2 * scale2) * jnp.mean(scaled2 * hidden, -1, keepdims=True)
    )
    grad_gain_second = jnp.sum(d_expert_in * hidden * scale2, 0)
    d_attn = d_hidden.astype(BF16)
    grad_out_turned = dot_tn(d_attn, heads)
    sum_out = scatter_rows(grad_out_turned).T
    d_heads = dot_nn(d_attn, out_turned).astype(BF16)
    d_query, d_key_all, d_value_all = attend_backward(first, query, key_value, d_heads)
    d_key_value_all = jnp.concatenate([d_key_all, d_value_all], -1).reshape(nc, tokens, -1)
    d_key_value = line_scatter(
        lambda j: lax.dynamic_index_in_dim(d_key_value_all, j, 0, keepdims=False),
        "context",
        up=False,
    )
    d_rotated = rotate_back(
        jnp.concatenate([d_query, d_key_value[:, :key_width]], -1).reshape(
            tokens, -1, HEAD_DIMENSION
        ),
        cosine_values,
        sine_values,
    ).reshape(tokens, -1)
    d_qkv = jnp.concatenate([d_rotated, d_key_value[:, key_width:]], -1).astype(BF16)
    d_inputs = dot_nt(d_qkv, qkv_weight) + dot_nt(d_logits, router_weight)
    grad_gain_first = jnp.sum(d_inputs * token_rows * scale1, 0)
    grad_qkv = dot_tn(inputs1, d_qkv)
    small_grads = jnp.concatenate(
        [grad_router, grad_gain_first[:, None], grad_gain_second[:, None]], -1
    )
    small_grads = jnp.pad(small_grads, ((0, 0), (0, 128 - small_grads.shape[1])))
    sum_rows = scatter_rows(jnp.concatenate([grad_qkv, small_grads], -1))
    sum_qkv = sum_rows[:, :qkv_width]
    sum_router = sum_rows[:, qkv_width : qkv_width + expert_total]
    sum_gain_first = sum_rows[:, qkv_width + expert_total]
    sum_gain_second = sum_rows[:, qkv_width + expert_total + 1]
    scaled1 = d_inputs * gain_first
    d_input_rows = (
        d_hidden
        + scale1 * scaled1
        - token_rows
        * (scale1 * scale1 * scale1)
        * jnp.mean(scaled1 * token_rows, -1, keepdims=True)
    ).astype(BF16)
    return (
        layer_result[None],
        d_input_rows[None],
        sum_gain_first,
        sum_qkv,
        sum_out,
        sum_router,
        sum_gain_second,
        sum_gate_up,
        sum_down,
    )


def local_fused(
    layer_input,
    gain_attn,
    query_key_value_weight,
    w_out,
    w_router,
    gain_ffn,
    w_gate_up,
    w_down,
    routes,
    d_out,
):
    tokens = layer_input.shape[1]
    ne, nc, nd = sizes = tuple(lax.axis_size(a) for a in ("expert", "context", "dp"))
    expert_total = EXP_DEV * ne
    first_row = lax.axis_index("context") * tokens
    query_width = QUERY_HEADS * HEAD_DIMENSION
    key_width = KEY_VALUE_HEADS * HEAD_DIMENSION
    qkv_width = query_width + 2 * key_width

    small = jnp.concatenate([w_router, gain_attn[:, None], gain_ffn[:, None]], -1)
    small = jnp.pad(small, ((0, 0), (0, SMALL - small.shape[1])))
    cosine_values, sine_values = rope_tables(first_row + jnp.arange(tokens), HEAD_DIMENSION)
    sine_values = sine_values * jnp.where(
        jnp.arange(HEAD_DIMENSION) < HEAD_DIMENSION // 2, -1.0, 1.0
    )
    layer_result, d_x, sum_rows, sum_out, sum_gate_up, sum_down = layer(
        (
            cosine_values,
            sine_values,
            routes[0].T,
            layer_input[0],
            query_key_value_weight,
            small,
            w_out.T,
            d_out[0],
            w_gate_up,
            w_down,
        ),
        sizes,
    )[:6]
    return (
        layer_result[None],
        d_x[None],
        sum_rows[:, qkv_width + expert_total],
        sum_rows[:, :qkv_width],
        sum_out.T,
        sum_rows[:, qkv_width : qkv_width + expert_total],
        sum_rows[:, qkv_width + expert_total + 1],
        sum_gate_up,
        jnp.swapaxes(sum_down, 1, 2),
    )


def solution(mesh):
    in_specs = (
        P(("expert", "dp"), "context", None),
        P(("expert", "context", "dp")),
        P(("expert", "context", "dp"), None),
        P(None, ("expert", "context", "dp")),
        P(("expert", "context", "dp"), None),
        P(("expert", "context", "dp")),
        P("expert", None, None),
        P("expert", None, None),
        P(("expert", "dp"), "context", None),
        P(("expert", "dp"), "context", None),
    )
    out_specs = (
        P(("expert", "dp"), "context", None),
        P(("expert", "dp"), "context", None),
        P(("expert", "context", "dp")),
        P(("expert", "context", "dp"), None),
        P(None, ("expert", "context", "dp")),
        P(("expert", "context", "dp"), None),
        P(("expert", "context", "dp")),
        P("expert", ("context", "dp"), None),
        P("expert", None, ("context", "dp")),
    )
    sizes = tuple(mesh.shape[a] for a in ("expert", "context", "dp"))
    local = local_fused if sizes == (4, 4, 2) else local_plain
    return jax.shard_map(local, mesh=mesh, in_specs=in_specs, out_specs=out_specs, check_vma=False)
```

```python
import functools
import math

import jax
import jax.numpy as jnp
from jax import lax
from jax.experimental import pallas as pl
from jax.experimental.pallas import tpu as pltpu
from jax.sharding import PartitionSpec as P

QUERY_HEADS = 12
KEY_VALUE_HEADS = 2
HEAD_DIMENSION = 128
TOP = 4
EXP_DEV = 2

EPSILON = 1e-06
ROPE_BASE = 10000.0
MASKED = -1e30

F32 = jnp.float32
BF16 = jnp.bfloat16


def rope_tables(positions, width):
    halfway = width // 2
    fraction = jnp.arange(halfway, dtype=jnp.float32) * (2.0 / width)
    frequency = jnp.exp(-math.log(ROPE_BASE) * fraction)
    angles = positions.astype(jnp.float32)[:, None] * frequency[None, :]
    cosine_values = jnp.cos(angles)
    sine_values = jnp.sin(angles)
    return (
        jnp.concatenate([cosine_values, cosine_values], -1),
        jnp.concatenate([sine_values, sine_values], -1),
    )


def rotate_half(values, cosine_values, sine_values):
    halfway = values.shape[-1] // 2
    turned = jnp.concatenate([-values[..., halfway:], values[..., :halfway]], -1)
    return values * cosine_values[:, None, :] + turned * sine_values[:, None, :]


def rotate_back(grads, cosine_values, sine_values):
    halfway = grads.shape[-1] // 2
    scaled = grads * sine_values[:, None, :]
    turned = jnp.concatenate([scaled[..., halfway:], -scaled[..., :halfway]], -1)
    return grads * cosine_values[:, None, :] + turned


def dot_nt(a, b):
    return lax.dot_general(a, b, (((1,), (1,)), ((), ())), preferred_element_type=F32)


def dot_tn(a, b):
    return lax.dot_general(a, b, (((0,), (0,)), ((), ())), preferred_element_type=F32)


def dot_nn(a, b):
    return jnp.dot(a, b, preferred_element_type=F32)


def masked_probs(first_row, query, key):
    scores = dot_nt(query, key) * (HEAD_DIMENSION**-0.5)
    rows = first_row + lax.broadcasted_iota(jnp.int32, scores.shape, 0)
    columns = lax.broadcasted_iota(jnp.int32, scores.shape, 1)
    scores = jnp.where(columns <= rows, scores, MASKED)
    expd = jnp.exp(scores - jnp.max(scores, axis=-1, keepdims=True))
    return expd / jnp.sum(expd, axis=-1, keepdims=True)


def attend_forward_kernel(first_ref, query_ref, key_ref, value_ref, heads_ref):
    probs = masked_probs(first_ref[0], query_ref[...], key_ref[...])
    heads_ref[...] = dot_nn(probs.astype(BF16), value_ref[...]).astype(BF16)


def attend_forward(first_row, query, key_value):
    tokens, width = query.shape
    length = key_value.shape[0]
    group = QUERY_HEADS // KEY_VALUE_HEADS
    size = HEAD_DIMENSION
    return pl.pallas_call(
        attend_forward_kernel,
        grid_spec=pltpu.PrefetchScalarGridSpec(
            num_scalar_prefetch=1,
            grid=(QUERY_HEADS,),
            in_specs=[
                pl.BlockSpec((tokens, size), lambda h, s: (0, h)),
                pl.BlockSpec((length, size), lambda h, s: (0, h // group)),
                pl.BlockSpec((length, size), lambda h, s: (0, KEY_VALUE_HEADS + h // group)),
            ],
            out_specs=pl.BlockSpec((tokens, size), lambda h, s: (0, h)),
        ),
        out_shape=jax.ShapeDtypeStruct((tokens, width), BF16),
        compiler_params=pltpu.CompilerParams(vmem_limit_bytes=32 * 1024 * 1024),
        cost_estimate=pl.CostEstimate(
            flops=4 * tokens * length * width, bytes_accessed=4 * tokens * width, transcendentals=0
        ),
    )(first_row, query, key_value, key_value)


def attend_backward_kernel(
    first_ref, query_ref, key_ref, value_ref, grad_ref, d_query_ref, d_key_ref, d_value_ref
):
    query, key, value, grad = query_ref[...], key_ref[...], value_ref[...], grad_ref[...]
    probs = masked_probs(first_ref[0], query, key)
    d_probs = dot_nt(grad, value)
    inner = jnp.sum(probs * d_probs, axis=-1, keepdims=True)
    d_raw = (probs * (d_probs - inner) * (HEAD_DIMENSION**-0.5)).astype(BF16)
    d_query_ref[...] = dot_nn(d_raw, key)
    d_key = dot_tn(d_raw, query)
    d_value = dot_tn(probs.astype(BF16), grad)

    @pl.when(pl.program_id(1) == 0)
    def _():
        d_key_ref[...] = d_key
        d_value_ref[...] = d_value

    @pl.when(pl.program_id(1) > 0)
    def _():
        d_key_ref[...] += d_key
        d_value_ref[...] += d_value


def attend_backward(first_row, query, key_value, grad):
    tokens, width = query.shape
    length = key_value.shape[0]
    group = QUERY_HEADS // KEY_VALUE_HEADS
    size = HEAD_DIMENSION
    row_spec = pl.BlockSpec((tokens, size), lambda j, g, s: (0, j * group + g))
    return pl.pallas_call(
        attend_backward_kernel,
        grid_spec=pltpu.PrefetchScalarGridSpec(
            num_scalar_prefetch=1,
            grid=(KEY_VALUE_HEADS, group),
            in_specs=[
                row_spec,
                pl.BlockSpec((length, size), lambda j, g, s: (0, j)),
                pl.BlockSpec((length, size), lambda j, g, s: (0, KEY_VALUE_HEADS + j)),
                row_spec,
            ],
            out_specs=[
                row_spec,
                pl.BlockSpec((length, size), lambda j, g, s: (0, j)),
                pl.BlockSpec((length, size), lambda j, g, s: (0, j)),
            ],
        ),
        out_shape=[
            jax.ShapeDtypeStruct((tokens, width), F32),
            jax.ShapeDtypeStruct((length, KEY_VALUE_HEADS * size), F32),
            jax.ShapeDtypeStruct((length, KEY_VALUE_HEADS * size), F32),
        ],
        compiler_params=pltpu.CompilerParams(vmem_limit_bytes=32 * 1024 * 1024),
        cost_estimate=pl.CostEstimate(
            flops=10 * tokens * length * width, bytes_accessed=8 * tokens * width, transcendentals=0
        ),
    )(first_row, query, key_value, key_value, grad)


def exchange(values, axis, mask):
    size = lax.axis_size(axis)
    return lax.ppermute(values, axis, [(i, i ^ mask) for i in range(size)])


def axis_masks(axis):
    size = lax.axis_size(axis)
    masks, bit = [], 1
    while bit < size:
        masks.append(bit)
        bit *= 2
    return masks


def cube_gather(values, axis, masks):
    held = {0: values}
    for mask in masks:
        for r, block in list(held.items()):
            held[r ^ mask] = exchange(block, axis, mask)
    return [held[r] for r in range(lax.axis_size(axis))]


def cube_scatter(blocks, axis, masks):
    held = dict(enumerate(blocks))
    for mask in masks:
        kept = {}
        for r in list(held):
            if not r & mask:
                arrived = exchange(held[r ^ mask].astype(BF16), axis, mask)
                kept[r] = held[r].astype(F32) + arrived.astype(F32)
        held = kept
    return held[0]


def line_steps(values, axis, up):
    size = lax.axis_size(axis)
    pairs = [(i, i + 1) if up else (i + 1, i) for i in range(size - 1)]
    return lax.ppermute(values, axis, pairs)


def line_gather(values, axis, both=True):
    size = lax.axis_size(axis)
    me = lax.axis_index(axis)
    result = jnp.zeros((size + 1,) + values.shape, values.dtype)
    result = lax.dynamic_update_index_in_dim(result, values, me, 0)
    up = down = values
    for step in range(1, size):
        up = line_steps(up, axis, True)
        result = lax.dynamic_update_index_in_dim(
            result, up, jnp.where(me - step >= 0, me - step, size), 0
        )
        if both:
            down = line_steps(down, axis, False)
            result = lax.dynamic_update_index_in_dim(result, down, jnp.minimum(me + step, size), 0)
    return result[:size]


def line_scatter(take, axis, up=True, down=True):
    size = lax.axis_size(axis)
    me = lax.axis_index(axis)
    total = take(me).astype(F32)
    for active, sign in ((up, 1), (down, -1)):
        if not active:
            continue
        arrived = None
        for step in range(1, size):
            block = take((me + sign * (size - step)) % size).astype(F32)
            if arrived is not None:
                block = block + arrived.astype(F32)
            arrived = line_steps(block.astype(BF16), axis, sign > 0)
        total = total + arrived.astype(F32)
    return total


def gather_rows(shard):
    ne, nc, nd = (lax.axis_size(a) for a in ("expert", "context", "dp"))
    rows, width = shard.shape
    lines = line_gather(shard, "context")
    masks = axis_masks("expert")
    half = width // 256 * 128
    parts = [lines[..., :half], lines[..., half:]]
    me = lax.axis_index("expert")
    result = jnp.zeros((ne, nc, rows, width), shard.dtype)
    for start, part, order in ((0, parts[0], masks), (half, parts[1], masks[::-1])):
        for r, block in enumerate(cube_gather(part, "expert", order)):
            result = lax.dynamic_update_slice(result, block[None], (me ^ r, 0, 0, start))
    core = lax.axis_index("dp")
    whole = jnp.zeros((ne, nc, nd, rows, width), shard.dtype)
    for r, block in enumerate(cube_gather(result, "dp", axis_masks("dp"))):
        whole = lax.dynamic_update_slice(whole, block[:, :, None], (0, 0, core ^ r, 0, 0))
    return whole.reshape(-1, width)


def scatter_rows(grad):
    ne, nc, nd = (lax.axis_size(a) for a in ("expert", "context", "dp"))
    width = grad.shape[-1]
    rows = grad.shape[0] // (ne * nc * nd)
    blocks = grad.reshape(ne, nc, nd, rows, width)
    core, me = lax.axis_index("dp"), lax.axis_index("expert")
    mine = cube_scatter(
        [
            lax.dynamic_index_in_dim(blocks, core ^ r, 2, keepdims=False)
            for r in range(nd)
        ],
        "dp",
        axis_masks("dp"),
    )
    masks = axis_masks("expert")
    half = width // 256 * 128
    sums = []
    for part, order in ((mine[..., :half], masks), (mine[..., half:], masks[::-1])):
        sums.append(
            cube_scatter(
                [lax.dynamic_index_in_dim(part, me ^ r, 0, keepdims=False) for r in range(ne)],
                "expert",
                order,
            )
        )
    lines = jnp.concatenate(sums, -1)
    return line_scatter(
        lambda j: lax.dynamic_index_in_dim(lines, j, 0, keepdims=False), "context"
    )


def plane_gather(rows):
    masks = axis_masks("expert")
    half = rows.shape[-1] // 2
    left = cube_gather(rows[:, :half], "expert", masks)
    right = cube_gather(rows[:, half:], "expert", masks[::-1])
    return jnp.concatenate([jnp.concatenate(p, -1) for p in zip(left, right)], 0)


def plane_scatter(partial, tokens):
    masks = axis_masks("expert")
    size = lax.axis_size("expert")
    half = partial.shape[-1] // 2
    blocks = partial.reshape(size, tokens, -1)
    left = cube_scatter([blocks[r, :, :half] for r in range(size)], "expert", masks)
    right = cube_scatter([blocks[r, :, half:] for r in range(size)], "expert", masks[::-1])
    return jnp.concatenate([left, right], -1)


MESH = pl.DeviceIdType.MESH
MIB = 1024 * 1024
SMALL = 128
GATE_ROWS = 16


def flip(index, mask):
    bit = 1
    while bit <= mask:
        if mask & bit:
            index = index + bit - 2 * bit * lax.rem(lax.div(index, bit), 2)
        bit *= 2
    return index


class Wire:
    def __init__(self, sends, recvs):
        self.sends, self.recvs = sends, recvs
        self.n_sends = self.n_recvs = 0
        self.open = []

    def slots(self, count):
        first = self.n_recvs
        self.n_recvs += count
        return first

    def start(self, src, dst, recv, device, when=None):
        copy = pltpu.make_async_remote_copy(
            src_ref=src,
            dst_ref=dst,
            send_sem=self.sends.at[self.n_sends],
            recv_sem=self.recvs.at[recv],
            device_id=device,
            device_id_type=MESH,
        )
        self.n_sends += 1
        guard(when, copy.start)
        self.open.append((when, copy))

    def arrived(self, dst, recv, device):
        pltpu.make_async_remote_copy(
            src_ref=dst,
            dst_ref=dst,
            send_sem=self.sends.at[0],
            recv_sem=self.recvs.at[recv],
            device_id=device,
            device_id_type=MESH,
        ).wait_recv()

    def finish(self):
        for when, copy in self.open:
            guard(when, copy.wait_send)
        self.open = []


def guard(when, action):
    if when is None:
        action()
    else:
        pl.when(when)(action)


def greet(targets):
    barrier = pltpu.get_barrier_semaphore()
    for device, when in targets:
        guard(
            when,
            lambda device=device: pl.semaphore_signal(
                barrier, inc=1, device_id=device, device_id_type=MESH
            ),
        )
    count = sum(1 if when is None else when.astype(jnp.int32) for _, when in targets)
    pl.semaphore_wait(barrier, count)


def plane_ids(e):
    return {m: {"expert": flip(e, m)} for m in (1, 2, 3)}


class RowsGather:
    def __init__(self, wire, ref, e, z, c, nc, half):
        self.wire, self.ref, self.e, self.z, self.c, self.nc = wire, ref, e, z, c, nc
        self.cols = (pl.ds(0, half), pl.ds(half, ref.shape[-1] - half))
        self.line = wire.slots(nc)
        self.plane = wire.slots(nc * 6)
        self.core = wire.slots(nc)
        self.ids = plane_ids(e)

    def go(self, *steps):
        for step in steps:
            action = {"l": self.pass_on, "s": self.spread, "f": self.forward, "h": self.share, "c": self.complete}
            action[step[0]](*map(int, step[1:]))

    def shard(self, k):
        if k < 2:
            return flip(self.z, k)
        inner = (self.z > 0) & (self.z < self.nc - 1)
        return jnp.where(inner, flip(self.z, 5 - k), flip(self.z, k))

    def at(self, r, zs, half):
        return self.ref.at[flip(self.e, r), zs, self.c, :, self.cols[half]]

    def slot(self, k, r, half):
        return self.plane + k * 6 + (r - 1) * 2 + half

    def pass_on(self, k):
        wire, z, nc = self.wire, self.z, self.nc
        zs = self.shard(k)
        whole = self.ref.at[self.e, zs, self.c]
        if k:
            wire.arrived(whole, self.line + zs, {"context": zs})
        wire.start(
            whole, whole, self.line + zs, {"context": z + 1}, when=(zs <= z) & (z < nc - 1)
        )
        wire.start(whole, whole, self.line + zs, {"context": z - 1}, when=(zs >= z) & (z > 0))

    def spread(self, k):
        zs = self.shard(k)
        for half, mask in ((0, 1), (1, 2), (1, 1), (0, 2)):
            part = self.at(0, zs, half)
            self.wire.start(part, part, self.slot(k, mask, half), self.ids[mask])

    def forward(self, k):
        zs = self.shard(k)
        for half, mask in ((0, 1), (1, 2)):
            part = self.at(mask, zs, half)
            self.wire.arrived(part, self.slot(k, mask, half), self.ids[mask])
            self.wire.start(part, part, self.slot(k, 3, half), self.ids[3 - mask])

    def share(self, k):
        zs = self.shard(k)
        for r, half in ((1, 1), (2, 0), (3, 0), (3, 1)):
            self.wire.arrived(self.at(r, zs, half), self.slot(k, r, half), self.ids[r])
        part = self.ref.at[:, zs, self.c]
        self.wire.start(part, part, self.core + k, {"dp": 1 - self.c})

    def complete(self):
        for k in range(self.nc):
            zs = self.shard(k)
            self.wire.arrived(self.ref.at[:, zs, 1 - self.c], self.core + k, {"dp": 1 - self.c})


class PlaneGather:
    def __init__(self, wire, ref, e):
        self.wire, self.ref = wire, ref
        self.half = ref.shape[-1] // 2
        self.ids = plane_ids(e)
        self.first = wire.slots(6)

    def at(self, r, half):
        return self.ref.at[r, :, pl.ds(half * self.half, self.half)]

    def slot(self, r, half):
        return self.first + (r - 1) * 2 + half

    def spread(self):
        for half, mask in ((0, 1), (1, 2), (1, 1), (0, 2)):
            self.wire.start(
                self.at(0, half), self.at(mask, half), self.slot(mask, half), self.ids[mask]
            )

    def forward(self):
        for half, mask in ((0, 1), (1, 2)):
            self.wire.arrived(self.at(mask, half), self.slot(mask, half), self.ids[mask])
            self.wire.start(
                self.at(mask, half), self.at(3, half), self.slot(3, half), self.ids[3 - mask]
            )

    def near(self, r):
        half = 1 if r == 1 else 0
        self.wire.arrived(self.at(r, half), self.slot(r, half), self.ids[r])

    def far(self):
        for half in (0, 1):
            self.wire.arrived(self.at(3, half), self.slot(3, half), self.ids[3])

    def complete(self):
        self.near(1)
        self.near(2)
        self.far()


def swap_halves(values):
    return pltpu.roll(values, HEAD_DIMENSION // 2, 1)


def front_kernel(
    nc,
    experts,
    x_ref,
    qkv_shard,
    small_shard,
    wo_shard,
    cot_ref,
    cos_ref,
    sin_ref,
    routes_ref,
    wk_hbm,
    wq_hbm,
    wo_hbm,
    cot_hbm,
    gate_all,
    gate_columns,
    inputs_ref,
    query_ref,
    kv_ref,
    heads_ref,
    hidden_ref,
    expert_in_ref,
    gains_ref,
    wk_all,
    wq_all,
    wo_all,
    cot_all,
    kv_scr,
    q_scr,
    sends,
    recvs,
    out_sems,
):
    e, z, c = (lax.axis_index(a) for a in ("expert", "context", "dp"))
    size = HEAD_DIMENSION
    tokens, width = x_ref.shape
    query_width = QUERY_HEADS * size
    kv_width = 2 * KEY_VALUE_HEADS * size
    wire = Wire(sends, recvs)
    ids = plane_ids(e)
    greet(
        [(ids[m], None) for m in (1, 2, 3)]
        + [({"dp": 1 - c}, None)]
        + [({"context": z + d}, z + d < nc) for d in range(1, nc)]
        + [({"context": z - d}, z >= d) for d in range(1, nc)]
    )
    wk_all[e, z, c, :, pl.ds(0, kv_width)] = qkv_shard[:, pl.ds(query_width, kv_width)]
    wk_all[e, z, c, :, pl.ds(kv_width, SMALL)] = small_shard[...]
    gather_k = RowsGather(wire, wk_all, e, z, c, nc, 256)
    gather_q = RowsGather(wire, wq_all, e, z, c, nc, 768)
    gather_o = RowsGather(wire, wo_all, e, z, c, nc, 768)
    gather_cot = PlaneGather(wire, cot_all, e)
    wq_all[e, z, c] = qkv_shard[:, pl.ds(0, query_width)]
    wo_all[e, z, c] = wo_shard[...]
    gather_k.go("l0", "s0")
    gather_q.go("s0")
    cot_all[0] = cot_ref[...]
    gather_k.go("l1", "s1", "f0", "l2", "s2")
    gather_q.go("l0")
    gather_k.go("f1", "h0", "l3", "s3")
    gather_q.go("l1", "s1")
    gather_o.go("l0")
    gather_k.go("f2", "h1", "f3")
    gather_q.go("l2", "s2")
    gather_k.go("h2")
    gather_o.go("l1")
    gather_q.go("f0")
    gather_k.go("h3")
    gather_q.go("l3", "s3")
    gather_k.go("c")
    rows = x_ref[...].astype(F32)
    scale1 = lax.rsqrt(jnp.mean(rows * rows, -1, keepdims=True) + EPSILON)

    small = wk_all[:, :, :, :, pl.ds(kv_width, SMALL)].reshape(width, SMALL)
    small = jnp.transpose(small.astype(F32))
    gain_first, gain_second = small[experts : experts + 1], small[experts + 1 : experts + 2]
    gains_ref[0:1] = gain_first
    gains_ref[1:2] = gain_second
    inputs_ref[...] = (rows * scale1 * gain_first).astype(BF16)
    kv_scr[...] = dot_nn(inputs_ref[...], wk_all[...].reshape(width, kv_width + SMALL))

    def turned(head):
        return (head * cos_ref[...] + swap_halves(head) * sin_ref[...]).astype(BF16)

    line = wire.slots(KEY_VALUE_HEADS * nc)
    for j in range(KEY_VALUE_HEADS):
        kv_ref[j, z, :, pl.ds(0, size)] = turned(kv_scr[:, pl.ds(j * size, size)])
        value = kv_scr[:, pl.ds(kv_width // 2 + j * size, size)]
        kv_ref[j, z, :, pl.ds(size, size)] = value.astype(BF16)
        mine = kv_ref.at[j, z]
        for d in range(nc - 1, 0, -1):
            wire.start(mine, mine, line + j * nc + z, {"context": z + d}, when=z + d < nc)

    def keys_here(j):
        for d in range(1, nc):

            def wait(d=d):
                wire.arrived(kv_ref.at[j, z - d], line + j * nc + z - d, {"context": z - d})

            pl.when(z >= d)(wait)

    outs = [
        pltpu.make_async_copy(source, dest, out_sems.at[n])
        for n, (source, dest) in enumerate(
            ((wk_all, wk_hbm), (wq_all, wq_hbm), (wo_all, wo_hbm), (cot_all, cot_hbm))
        )
    ]
    outs[0].start()
    for later in range(1, nc):

        def clear(later=later):
            for j in range(KEY_VALUE_HEADS):
                kv_ref[j, z + later] = jnp.zeros(kv_ref.shape[2:], BF16)

        pl.when(z + later < nc)(clear)
    gather_q.go("f1", "f2", "h0")
    gather_o.go("s0")
    gather_q.go("f3", "h1")
    gather_o.go("s1")
    gather_q.go("h2", "h3", "c")
    outs[1].start()
    gather_o.go("f0", "f1")
    gather_cot.spread()

    @pl.loop(0, query_width // 256)
    def _(n):
        columns = pl.ds(pl.multiple_of(n * 256, 256), 256)
        q_scr[:, columns] = dot_nn(
            inputs_ref[...], wq_all[:, :, :, :, columns].reshape(width, 256)
        )

    @pl.loop(0, QUERY_HEADS)
    def _(h):
        columns = pl.ds(pl.multiple_of(h * size, size), size)
        query_ref[:, columns] = turned(q_scr[:, columns])

    logits = kv_scr[:, pl.ds(kv_width, SMALL)]
    lanes = lax.broadcasted_iota(jnp.int32, logits.shape, 1)
    routes = jnp.concatenate(
        [routes_ref[...].astype(F32), jnp.zeros((SMALL - TOP, tokens), F32)], 0
    )
    routes = jnp.transpose(routes).astype(jnp.int32)
    named = lanes == routes[:, 0:1]
    for k in range(1, TOP):
        named = named | (lanes == routes[:, k : k + 1])
    logits = jnp.where(named, logits, MASKED)
    expd = jnp.exp(logits - jnp.max(logits, -1, keepdims=True))
    gates = expd / jnp.sum(expd, -1, keepdims=True)
    gate_all[0] = jnp.transpose(gates)[:GATE_ROWS]
    gate_slot = wire.slots(3)
    for r in (1, 2, 3):
        wire.start(gate_all.at[0], gate_all.at[r], gate_slot + r - 1, ids[r])

    length = nc * tokens
    group = QUERY_HEADS // KEY_VALUE_HEADS

    def attend(first, last):
        j = first // group
        key = kv_ref[j, :, :, pl.ds(0, size)].reshape(length, size)
        value = kv_ref[j, :, :, pl.ds(size, size)].reshape(length, size)

        @pl.loop(first, last)
        def _(h):
            column = pl.multiple_of(h * size, size)
            scores = dot_nt(query_ref[:, pl.ds(column, size)], key)
            row = z * tokens + lax.broadcasted_iota(jnp.int32, scores.shape, 0)
            place = lax.broadcasted_iota(jnp.int32, scores.shape, 1)
            scores = jnp.where(place <= row, scores, MASKED)
            expd = jnp.exp((scores - jnp.max(scores, -1, keepdims=True)) * (size**-0.5))
            total = jnp.sum(expd, -1, keepdims=True)
            mixed = dot_nn(expd.astype(BF16), value) / total
            heads_ref[:, pl.ds(column, size)] = mixed.astype(BF16)

    half = group // 2
    keys_here(0)
    attend(0, half)
    gather_o.go("l2", "s2")
    attend(half, group)
    gather_o.go("l3", "s3", "f2", "h0")
    keys_here(1)
    attend(group, group + half)
    gather_o.go("f3", "h1")
    attend(group + half, QUERY_HEADS)
    gather_o.go("h2")
    gather_cot.forward()
    gather_o.go("h3")
    gather_o.go("c")
    outs[2].start()
    part = width // wo_all.shape[0]
    for block in range(wo_all.shape[0]):
        weight = wo_all[block].reshape(part, width)
        columns = pl.ds(block * part, part)
        hidden_ref[:, columns] = x_ref[:, columns].astype(F32) + dot_nt(heads_ref[...], weight)
    hidden = hidden_ref[...]
    scale2 = lax.rsqrt(jnp.mean(hidden * hidden, -1, keepdims=True) + EPSILON)
    expert_in_ref[...] = (hidden * scale2 * gains_ref[1:2]).astype(BF16)
    for r in (1, 2, 3):
        wire.arrived(gate_all.at[r], gate_slot + r - 1, ids[r])
    for r in range(gate_all.shape[0]):
        rest = jnp.zeros((SMALL - GATE_ROWS, tokens), F32)
        turned_gates = jnp.transpose(jnp.concatenate([gate_all[r], rest], 0))
        both = [
            jnp.sum(jnp.where(lanes == e * EXP_DEV + i, turned_gates, 0.0), -1, keepdims=True)
            for i in range(EXP_DEV)
        ]
        gate_columns[r] = jnp.where(lanes == 0, both[0], jnp.where(lanes == 1, both[1], 0.0))
    gather_cot.complete()
    outs[3].start()
    for copy in outs:
        copy.wait()
    wire.finish()


def front(operands, sizes):
    ne, nc, nd = sizes
    x, qkv_shard = operands[:2]
    tokens, width = x.shape
    rows, qkv_width = qkv_shard.shape
    query_width = QUERY_HEADS * HEAD_DIMENSION
    kv_width = qkv_width - query_width
    gathered = [
        ((ne, nc, nd, rows, kv_width + SMALL), BF16),
        ((ne, nc, nd, rows, query_width), BF16),
        ((ne, nc, nd, rows, width), BF16),
        ((ne, tokens, width), BF16),
    ]
    shapes = gathered + [
        ((ne, GATE_ROWS, tokens), F32),
        ((ne, tokens, SMALL), F32),
        ((tokens, width), BF16),
        ((tokens, query_width), BF16),
        ((KEY_VALUE_HEADS, nc, tokens, 2 * HEAD_DIMENSION), BF16),
        ((tokens, query_width), BF16),
        ((tokens, width), F32),
        ((tokens, width), BF16),
        ((8, width), F32),
    ]
    copies = 160
    vmem = pl.BlockSpec(memory_space=pltpu.VMEM)
    anywhere = pl.BlockSpec(memory_space=pl.ANY)
    return pl.pallas_call(
        functools.partial(front_kernel, nc, EXP_DEV * ne),
        out_shape=[jax.ShapeDtypeStruct(*s) for s in shapes],
        in_specs=[vmem] * len(operands),
        out_specs=[anywhere] * 4 + [vmem] * (len(shapes) - 4),
        scratch_shapes=[pltpu.VMEM(*s) for s in gathered]
        + [
            pltpu.VMEM((tokens, kv_width + SMALL), F32),
            pltpu.VMEM((tokens, query_width), F32),
            pltpu.SemaphoreType.DMA((copies,)),
            pltpu.SemaphoreType.DMA((copies,)),
            pltpu.SemaphoreType.DMA((4,)),
        ],
        compiler_params=pltpu.CompilerParams(
            collective_id=0, has_side_effects=True, vmem_limit_bytes=56 * MIB
        ),
    )(*operands)


class PlaneScatter:
    def __init__(self, wire, land, ids):
        self.wire, self.land, self.ids, self.part = wire, land, ids, None
        self.half = land.shape[-1]
        self.first = wire.slots(6)

    def send(self, source, mask, slot):
        self.wire.start(source, self.land.at[slot], self.first + slot, self.ids[mask])

    def near(self, r):
        self.send(self.part(r, r - 1), r, r - 1)

    def far(self):
        self.send(self.part(3, 0), 1, 2)
        self.send(self.part(3, 1), 2, 3)

    def relay(self, part=None):
        for half, r in ((0, 2), (1, 1)):
            slot = 2 + half
            self.wire.arrived(self.land.at[slot], self.first + slot, self.ids[3 - r])
            mine = (part or self.part)(r, half)
            mine[...] = (mine[...].astype(F32) + self.land[slot].astype(F32)).astype(BF16)
            self.send(mine, r, 4 + half)

    def total(self, own):
        for slot, half, mask in ((0, 0, 1), (1, 1, 2), (4, 0, 2), (5, 1, 1)):
            self.wire.arrived(self.land.at[slot], self.first + slot, self.ids[mask])
            columns = pl.ds(half * self.half, self.half)
            own[:, columns] += self.land[slot].astype(F32)


class LineScatter:
    def __init__(self, wire, block, lands, z, nc, up=True):
        self.wire, self.block, self.lands, self.z, self.nc = wire, block, lands, z, nc
        self.up = up
        self.first = [wire.slots(nc - 1), wire.slots(nc - 1)]

    def arrive(self, way, index, j):
        land = self.lands[way].at[index]
        self.wire.arrived(land, self.first[way] + index, {"context": self.z})
        block = self.block(j)
        block[...] = (block[...].astype(F32) + self.lands[way][index].astype(F32)).astype(BF16)

    def move(self, way, j, only=None):
        z, nc = self.z, self.nc
        inner, index = ((z > 0), j - z) if way == 0 else ((z < nc - 1), z - j)
        wanted = (j > z) if way == 0 else (j < z)
        if only is not None:
            wanted = wanted & only
        pl.when(wanted & inner)(lambda: self.arrive(way, index, j))
        self.leave(way, j, wanted)

    def step(self, s):
        if self.up:
            self.move(0, self.nc - s)
            self.move(1, s - 1)
        else:
            top = self.z == self.nc - 1
            if s == 1:
                for j in range(self.nc - 1):
                    self.leave(1, j, top)
            self.move(1, s - 1, jnp.logical_not(top))

    def leave(self, way, j, wanted):
        z = self.z
        index, near = (j - z, z + 1) if way == 0 else (z - j, z - 1)
        self.wire.start(
            self.block(j),
            self.lands[way].at[index - 1],
            self.first[way] + index - 1,
            {"context": near},
            when=wanted,
        )

    def last(self):
        if self.up:
            pl.when(self.z > 0)(lambda: self.arrive(0, 0, self.z))
        pl.when(self.z < self.nc - 1)(lambda: self.arrive(1, 0, self.z))


class RowsScatter:
    def __init__(self, wire, buf, core, plane, lines, e, z, c, nc, start, width, half):
        self.wire, self.buf, self.core, self.plane = wire, buf, core, plane
        self.e, self.c = e, c
        self.all = pl.ds(start, width)
        self.cols = (pl.ds(start, half), pl.ds(start + half, width - half))
        self.ids = plane_ids(e)
        self.core_slot = wire.slots(1)
        self.first = wire.slots(6)
        rows = buf.shape[2] // nc
        self.line = LineScatter(
            wire,
            lambda j: buf.at[c, e, pl.ds(pl.multiple_of(j * rows, rows), rows), self.all],
            lines,
            z,
            nc,
        )

    def share(self):
        self.wire.start(
            self.buf.at[1 - self.c, :, :, self.all], self.core, self.core_slot, {"dp": 1 - self.c}
        )

    def at(self, r, half):
        return self.buf.at[self.c, flip(self.e, r), :, self.cols[half]]

    def send(self, r, half, mask, slot):
        self.wire.start(
            self.at(r, half), self.plane(slot, half), self.first + slot, self.ids[mask]
        )

    def merge(self, before=None):
        self.wire.arrived(self.core, self.core_slot, {"dp": 1 - self.c})
        for r in (3, 1, 2, 0):
            block = flip(self.e, r)
            part = self.buf.at[self.c, block, :, self.all]
            part[...] = (part[...].astype(F32) + self.core[block].astype(F32)).astype(BF16)
            if r == 3:
                if before is not None:
                    before()
                self.send(3, 0, 1, 2)
                self.send(3, 1, 2, 3)
            elif r:
                self.send(r, r - 1, r, r - 1)

    def add(self, r, half, slot, mask):
        land = self.plane(slot, half)
        self.wire.arrived(land, self.first + slot, self.ids[mask])
        part = self.at(r, half)
        part[...] = (part[...].astype(F32) + land[...].astype(F32)).astype(BF16)

    def relay(self):
        for half, r in ((0, 2), (1, 1)):
            self.add(r, half, 2 + half, 3 - r)
            self.send(r, half, r, 4 + half)

    def total(self):
        for slot, half, mask in ((0, 0, 1), (1, 1, 2), (4, 0, 2), (5, 1, 1)):
            self.add(0, half, slot, mask)


class ExpertLine:
    def __init__(self, wire, base, land, ins, out, sems, z, nc):
        self.wire, self.base, self.land = wire, base, land
        self.ins, self.out, self.sems, self.z, self.nc = ins, out, sems, z, nc
        self.end = (z == 0) | (z == nc - 1)
        self.inner = jnp.logical_not(self.end)
        self.width = base.shape[-1] // EXP_DEV
        self.first = wire.slots((nc + 1) * EXP_DEV)
        self.sent = []

    def part(self, ref, j, i):
        return ref.at[j, :, pl.ds(i * self.width, self.width)]

    def combine(self, sources, stores):
        out, step = self.out, self.ins.shape[2]
        count = sources[0].shape[0] // step

        def loads(p):
            rows = pl.ds(p * step, step)
            return [
                pltpu.make_async_copy(source.at[rows], self.ins.at[k, p], self.sems.at[4 * k + p])
                for k, source in enumerate(sources)
            ]

        def store(p):
            pairs = stores(pl.ds(p * step, step), out.at[p % 2])
            return [
                pltpu.make_async_copy(source, dest, self.sems.at[16 + 2 * n + p % 2])
                for n, (source, dest) in enumerate(pairs)
            ]

        for p in range(count):
            for copy in loads(p):
                copy.start()
        for p in range(count):
            for copy in loads(p):
                copy.wait()
            if p > 1:
                for copy in store(p - 2):
                    copy.wait()
            total = self.ins[0, p].astype(F32)
            for k in range(1, len(sources)):
                total = total + self.ins[k, p].astype(F32)
            out[p % 2] = total.astype(out.dtype)
            for copy in store(p):
                copy.start()
        for p in range(max(0, count - 2), count):
            for copy in store(p):
                copy.wait()

    def copy(self, i, r, number):
        target, slot = flip(self.z, r), self.z
        if r == 3:
            target = jnp.where(self.end, flip(self.z, 1), target)
            slot = jnp.where(self.end, self.nc, slot)
        return pltpu.make_async_remote_copy(
            src_ref=self.part(self.base, flip(self.z, r), i),
            dst_ref=self.part(self.land, slot, i),
            send_sem=self.wire.sends.at[number],
            recv_sem=self.wire.recvs.at[self.first + slot * EXP_DEV + i],
            device_id={"context": target},
            device_id_type=MESH,
        )

    def send(self, i, r, when=None):
        number = len(self.sent)
        guard(when, self.copy(i, r, number).start)
        self.sent.append((when, i, r, number))

    def finish(self):
        for when, i, r, number in self.sent:
            guard(when, self.copy(i, r, number).wait_send)

    def arrived(self, slot, i):
        land = self.part(self.land, slot, i)
        self.wire.arrived(land, self.first + slot * EXP_DEV + i, {"context": self.z})

    def relay_loads(self, i, p):
        step = self.ins.shape[2]
        rows = pl.ds(p * step, step)
        sources = (self.part(self.base, flip(self.z, 2), i), self.part(self.land, self.nc, i))
        return [
            pltpu.make_async_copy(
                source.at[rows], self.ins.at[k, p], self.sems.at[4 * k + p]
            )
            for k, source in enumerate(sources)
        ]

    def relay_store(self, i, p):
        step = self.ins.shape[2]
        mine = self.part(self.base, flip(self.z, 2), i).at[pl.ds(p * step, step)]
        return pltpu.make_async_copy(self.ins.at[0, p], mine, self.sems.at[16 + p])

    def relay_steps(self):
        return range(self.base.shape[1] // self.ins.shape[2])

    def relay_begin(self, i):
        self.relayed = i

        def begin():
            self.arrived(self.nc, i)
            for p in self.relay_steps():
                for copy in self.relay_loads(i, p):
                    copy.start()

        pl.when(self.inner)(begin)

    def relay_add(self):
        i = self.relayed

        def add():
            for p in self.relay_steps():
                for copy in self.relay_loads(i, p):
                    copy.wait()
                a, b = (self.ins[k, p].astype(F32) for k in range(2))
                self.ins[0, p] = (a + b).astype(BF16)
                self.relay_store(i, p).start()

        pl.when(self.inner)(add)

    def relay_send(self, i):
        def wait():
            for p in self.relay_steps():
                self.relay_store(i, p).wait()

        pl.when(self.inner)(wait)
        self.send(i, 2, when=self.inner)

    def last(self, i, results):
        z = self.z
        sources = [self.part(self.base, z, i)]
        for r in (1, 2):
            self.arrived(flip(z, r), i)
            sources.append(self.part(self.land, flip(z, r), i))

        def stores(rows, wide):
            pairs, first = [], 0
            for result in results:
                columns = pl.ds(first, result.shape[-1])
                pairs.append((wide.at[:, columns], result.at[i, rows]))
                first += result.shape[-1]
            return pairs

        pl.when(self.end)(lambda: self.combine(sources, stores))

        def inner():
            self.arrived(flip(z, 3), i)
            self.combine(sources + [self.part(self.land, flip(z, 3), i)], stores)

        pl.when(self.inner)(inner)


def back_kernel(
    nc,
    experts,
    gates_ref,
    gate_ref,
    gains_ref,
    cos_ref,
    sin_ref,
    expert_in_hbm,
    cot_hbm,
    w_gu_hbm,
    w_dn_hbm,
    x_hbm,
    inputs_hbm,
    query_hbm,
    kv_hbm,
    heads_hbm,
    hidden_hbm,
    wk_hbm,
    wq_hbm,
    o_hbm,
    layer_ref,
    d_x_ref,
    sum_q_ref,
    sum_o_ref,
    sum_gu_hbm,
    sum_dn_hbm,
    base_hbm,
    land_hbm,
    y_hbm,
    x_all,
    y_land,
    dx_land,
    core_land,
    plane_q,
    plane_k,
    lines_o,
    lines_q,
    lines_k,
    dkv_land,
    d_in_ref,
    dg_lanes,
    dg_part,
    dg_land,
    ins,
    out_wide,
    sends_1,
    recvs_1,
    sends_2,
    recvs_2,
    sends_e,
    recvs_e,
    hand_sends,
    hand_recvs,
    stage_sems,
    load_sems,
    sum_sems,
    y_sems,
    credits,
):
    e, z, c = (lax.axis_index(a) for a in ("expert", "context", "dp"))
    size = HEAD_DIMENSION
    blocks, tokens, width = cot_hbm.shape
    ff = w_dn_hbm.shape[1]
    query_width = QUERY_HEADS * size
    key_width = KEY_VALUE_HEADS * size
    qkv_width = query_width + 2 * key_width
    rest = wk_hbm.shape[-1]
    grad_width = base_hbm.shape[-1]
    ids = plane_ids(e)
    sibling = {"dp": 1 - c}
    bottom, even = z == 0, lax.rem(z, 2) == 0
    wire_1, wire_2, wire_e = Wire(sends_1, recvs_1), Wire(sends_2, recvs_2), Wire(sends_e, recvs_e)
    expert = ExpertLine(
        wire_e, base_hbm, land_hbm, ins, out_wide, sum_sems, z, nc
    )
    gather = PlaneGather(wire_1, x_all, e)
    scatter_dx = PlaneScatter(wire_1, dx_land, ids)
    scatter_y = PlaneScatter(wire_2, y_land, ids)
    dg_slot = wire_1.slots(3)

    def token_phase(w_gu, w_dn, cot_all, a_all, dgu_all, y_stage, dx_part, stage):
        scatter_dx.part = lambda r, half: dx_part.at[
            r - 1, :, pl.ds(half * width // 2, width // 2)
        ]
        sources = [(expert_in_hbm, x_all.at[0])]
        for i in range(EXP_DEV):
            sources += [(w_gu_hbm.at[i], w_gu.at[i]), (w_dn_hbm.at[i], w_dn.at[i])]
            if i == 0:
                sources += [(cot_hbm.at[0], cot_all.at[0]), (cot_hbm.at[1:], cot_all.at[1:])]
        loads = [
            pltpu.make_async_copy(source, dest, load_sems.at[n])
            for n, (source, dest) in enumerate(sources)
        ]
        for copy in loads:
            copy.start()
        greet(
            [(ids[m], None) for m in (1, 2, 3)]
            + [(sibling, None), ({"context": flip(z, 2)}, None)]
            + [({"context": z + 1}, z < nc - 1), ({"context": z - 1}, z > 0)]
        )
        loads[0].wait()
        gather.spread()
        step = 256
        wide = 512
        dg_lanes[...] = jnp.zeros_like(dg_lanes)

        def hidden_units(r, i, count=1):
            here = pl.ds(r, count)
            flat = count * tokens

            @pl.loop(0, ff // step)
            def _(f):
                column = pl.multiple_of(f * step, step)
                rows = x_all[here].reshape(flat, width)
                grads = cot_all[here].reshape(flat, width)
                gate_part = dot_nn(rows, w_gu[i, :, pl.ds(column, step)])
                up_part = dot_nn(rows, w_gu[i, :, pl.ds(ff + column, step)])
                raw = dot_nt(grads, w_dn[i, pl.ds(column, step), :])
                gate = gates_ref[here].reshape(flat, SMALL)[:, i : i + 1]
                sigma = jax.nn.sigmoid(gate_part)
                silu = gate_part * sigma
                act = silu * up_part
                lanes = lax.broadcasted_iota(jnp.int32, (flat, SMALL), 1)
                d_gate = jnp.where(
                    lanes == e * EXP_DEV + i, jnp.sum(act * raw, -1, keepdims=True), 0.0
                )
                dg_lanes[here] += d_gate.reshape(count, tokens, SMALL)

                def put(ref, first, values):
                    values = values.astype(BF16).reshape(count, tokens, step)
                    ref[here, :, pl.ds(pl.multiple_of(first, step), step)] = values

                put(a_all, i * ff + column, act * gate)
                d_act = raw * gate
                d_gate_part = d_act * up_part * sigma * (1.0 + gate_part * (1.0 - sigma))
                put(dgu_all, i * 2 * ff + column, d_gate_part)
                put(dgu_all, i * 2 * ff + ff + column, d_act * silu)

        def y_copy(r):
            return pltpu.make_async_copy(y_stage.at[r % 2], y_hbm.at[r], y_sems.at[r % 2])

        def outputs(r, count=1):
            here = pl.ds(r, count)
            flat = count * tokens

            @pl.loop(0, width // wide)
            def _(n):
                columns = pl.ds(pl.multiple_of(n * wide, wide), wide)
                low = dgu_all[here].reshape(flat, EXP_DEV * 2 * ff)
                d_rows = dot_nt(low[:, : 2 * ff], w_gu[0, columns, :])
                d_rows += dot_nt(low[:, 2 * ff :], w_gu[1, columns, :])
                weight = w_dn[:, :, columns].reshape(EXP_DEV * ff, wide)
                out = dot_nn(a_all[here].reshape(flat, EXP_DEV * ff), weight).astype(BF16)
                for k in range(count):
                    rows = slice(k * tokens, (k + 1) * tokens)
                    y_stage[(r + k) % 2, :, columns] = out[rows]
                    if r == 0:
                        d_in_ref[:, columns] = d_rows
                    else:
                        dx_part[r + k - 1, :, columns] = d_rows[rows].astype(BF16)

            for k in range(r, r + count):
                y_copy(k).start()
                dg_part[k] = jnp.transpose(dg_lanes[k])[:GATE_ROWS]
                if k:
                    wire_1.start(dg_part.at[k], dg_land.at[k - 1], dg_slot + k - 1, ids[k])

        half_rows = width // nc // 2
        units = [(i, r) for i in range(EXP_DEV) for r in (3, 2, 1, 0)]

        def keep(u):
            i, r = units[u]
            return pltpu.make_async_copy(
                stage.at[u % 2, c], expert.part(base_hbm, flip(z, r), i), stage_sems.at[u % 2]
            )

        def hand(u):
            r = units[u][1]
            return pltpu.make_async_remote_copy(
                src_ref=stage.at[u % 2, 1 - c],
                dst_ref=core_land.at[r],
                send_sem=hand_sends.at[u],
                recv_sem=hand_recvs.at[u],
                device_id=sibling,
                device_id_type=MESH,
            )

        def weight_grads(u):
            i, r = units[u]
            columns = pl.ds(pl.multiple_of(flip(z, r) * 2 * half_rows, 2 * half_rows), 2 * half_rows)
            for first, source, grad, start, count in (
                (0, x_all, dgu_all, i * 2 * ff, 2),
                (2 * ff, cot_all, a_all, i * ff, 1),
            ):
                rows = source[:, :, columns].reshape(blocks * tokens, 2 * half_rows)

                @pl.loop(0, count)
                def _(n):
                    column = pl.multiple_of(n * ff, ff)
                    part = grad[:, :, pl.ds(pl.multiple_of(start + column, ff), ff)]
                    result = dot_tn(rows, part.reshape(blocks * tokens, ff)).astype(BF16)
                    stage[u % 2, :, :, pl.ds(pl.multiple_of(first + column, ff), ff)] = (
                        result.reshape(2, half_rows, ff)
                    )

            if u == nc:
                pl.semaphore_wait(credits.at[3], 1)
            hand(u).start()

        def settle(u):
            hand(u).wait_recv()
            r = units[u][1]
            mine = stage[u % 2, c].astype(F32) + core_land[r].astype(F32)
            stage[u % 2, c] = mine.astype(BF16)
            keep(u).start()

        def clear(u):
            keep(u).wait()
            hand(u).wait_send()
            i, r = units[u]
            if i == 0 and r == 2:
                expert.send(i, r, when=expert.end)
            elif i == 0 and r == 1 or r == 3:
                expert.send(i, r)
            elif r == 2:
                expert.send(i, r, when=bottom)
            elif r == 1:
                expert.send(i, r, when=even)

        for copy in loads[1:4]:
            copy.wait()
        hidden_units(0, 0)
        for copy in loads[4:]:
            copy.wait()
        hidden_units(0, 1)
        gather.forward()
        outputs(0)
        gather.near(1)
        gather.near(2)
        hidden_units(1, 0, 2)
        gather.far()
        hidden_units(3, 0)
        weight_grads(0)
        weight_grads(1)
        settle(0)
        clear(0)
        weight_grads(2)
        settle(1)
        clear(1)
        weight_grads(3)
        settle(2)
        hidden_units(1, 1, 2)
        clear(2)
        settle(3)
        pl.semaphore_signal(credits.at[3], inc=1, device_id=sibling, device_id_type=MESH)
        y_copy(0).wait()
        outputs(1, 2)
        scatter_dx.near(1)
        scatter_dx.near(2)
        hidden_units(3, 1)
        expert.relay_begin(0)
        y_copy(1).wait()
        outputs(3)
        scatter_dx.far()
        clear(3)
        expert.relay_add()
        weight_grads(4)
        expert.relay_send(0)
        weight_grads(5)
        settle(4)
        scatter_dx.relay()
        clear(4)
        weight_grads(6)
        settle(5)
        clear(5)
        weight_grads(7)
        settle(6)
        scatter_dx.total(d_in_ref)
        for r in (1, 2):
            pl.semaphore_signal(credits.at[r], inc=1, device_id=ids[r], device_id_type=MESH)
        settle(7)
        clear(6)
        clear(7)
        y_copy(3).wait()
        y_copy(2).wait()
        wire_1.finish()
        pl.semaphore_signal(credits.at[0], inc=1, device_id=sibling, device_id_type=MESH)

    def token_rows_phase(
        weight,
        grads_o,
        grads_q,
        x_ref,
        inputs_ref,
        query_ref,
        kv_ref,
        heads_ref,
        hidden_ref,
        d_hidden_ref,
        d_attn_ref,
        d_heads_ref,
        d_all_ref,
        rows_ref,
        dkv_acc,
        dkv_ref,
        y_relay,
    ):
        cot_ref, d_inputs_ref = d_heads_ref, hidden_ref
        scatter_y.part = lambda r, half: y_hbm.at[r, :, pl.ds(half * width // 2, width // 2)]
        y_loads = [
            pltpu.make_async_copy(scatter_y.part(2 - half, half), y_relay.at[half], y_sems.at[half])
            for half in range(2)
        ]
        for copy in y_loads:
            copy.start()
        planes = grads_o.shape[1]
        part = width // planes
        sources = (
            (hidden_hbm, hidden_ref),
            (cot_hbm.at[0], cot_ref),
            (o_hbm, weight.at[:, pl.ds(0, width)]),
            (heads_hbm, heads_ref),
            (query_hbm, query_ref),
            (kv_hbm, kv_ref),
            (x_hbm, x_ref),
            (inputs_hbm, inputs_ref),
        )
        loads = [
            pltpu.make_async_copy(source, dest, load_sems.at[4 + n])
            for n, (source, dest) in enumerate(sources)
        ]
        for copy in loads:
            copy.start()
        for r in (1, 2):
            scatter_y.near(r)
        scatter_y.far()

        def rows_scatter(buf, core, plane, lines, start, count, half):
            return RowsScatter(
                wire_2,
                buf,
                core,
                plane,
                [lines.at[0], lines.at[1]],
                e,
                z,
                c,
                nc,
                start,
                count,
                half,
            )

        rows_of = part // 2
        scatter_o = rows_scatter(
            grads_o,
            x_all.at[:, pl.ds(0, rows_of)],
            lambda slot, half: dx_land.at[slot, pl.ds(0, rows_of)],
            lines_o,
            0,
            width,
            width // 2,
        )
        scatter_q = rows_scatter(
            grads_q,
            core_land.at[:, :, pl.ds(0, query_width)],
            lambda slot, half: plane_q.at[slot],
            lines_q,
            0,
            query_width,
            query_width // 2,
        )
        rest_half = rest // 256 * 128
        scatter_k = rows_scatter(
            grads_q,
            core_land.at[:, :, pl.ds(query_width, rest)],
            lambda slot, half: plane_k.at[
                slot, :, pl.ds(0, rest - rest_half if half else rest_half)
            ],
            lines_k,
            query_width,
            rest,
            rest_half,
        )
        scatter_kv = [
            LineScatter(
                wire_2,
                lambda j, h=h: dkv_ref.at[h, j],
                [dkv_land.at[h], dkv_land.at[h]],
                z,
                nc,
                up=False,
            )
            for h in range(KEY_VALUE_HEADS)
        ]

        loads[0].wait()
        loads[1].wait()
        hidden, d_in = hidden_ref[...], d_in_ref[...]
        scale2 = lax.rsqrt(jnp.mean(hidden * hidden, -1, keepdims=True) + EPSILON)
        scaled = d_in * gains_ref[1:2]
        mean = jnp.mean(scaled * hidden, -1, keepdims=True)
        d_hidden = cot_ref[...].astype(F32) + scale2 * scaled
        d_hidden = d_hidden - hidden * (scale2 * scale2 * scale2 * mean)
        d_hidden_ref[...] = d_hidden
        d_attn_ref[...] = d_hidden.astype(BF16)
        rows_ref[...] = jnp.zeros_like(rows_ref)
        rows_ref[experts + 1 : experts + 2, :] = jnp.sum(d_in * hidden * scale2, 0, keepdims=True)

        loads[2].wait()

        @pl.loop(0, query_width // 256)
        def _(n):
            columns = pl.ds(pl.multiple_of(n * 256, 256), 256)
            d_heads_ref[:, columns] = dot_nn(d_attn_ref[...], weight[:, columns]).astype(BF16)

        load_q = [
            pltpu.make_async_copy(wq_hbm, weight.at[:, pl.ds(0, query_width)], load_sems.at[0]),
            pltpu.make_async_copy(wk_hbm, weight.at[:, pl.ds(query_width, rest)], load_sems.at[1]),
        ]
        for copy in load_q:
            copy.start()
        loads[3].wait()

        def row_grads(buf, left, right, first, count, extra=None):
            @pl.loop(0, planes)
            def _(block):
                columns = pl.ds(pl.multiple_of(block * part, part), part)
                result = dot_tn(left[:, columns], right)
                if extra is not None:
                    result = result + extra(columns)
                result = result.astype(BF16).reshape(nc, 2, part // nc // 2, count)
                for half in range(2):
                    buf[half, block, :, pl.ds(first, count)] = result[:, half].reshape(
                        part // 2, count
                    )

        row_grads(grads_o, d_attn_ref, heads_ref[...], 0, width)
        pl.semaphore_wait(credits.at[0], 1)
        scatter_o.share()
        y_own = pltpu.make_async_copy(y_hbm.at[0], heads_ref, load_sems.at[2])
        y_own.start()

        length = nc * tokens
        group = QUERY_HEADS // KEY_VALUE_HEADS
        for copy in loads[4:6]:
            copy.wait()
        dkv_acc[...] = jnp.zeros_like(dkv_acc)

        def attend(j, first, last):
            key = kv_ref[j, :, :, pl.ds(0, size)].reshape(length, size)
            value = kv_ref[j, :, :, pl.ds(size, size)].reshape(length, size)

            @pl.loop(j * group + first, j * group + last)
            def _(h):
                columns = pl.ds(pl.multiple_of(h * size, size), size)
                query, grad = query_ref[:, columns], d_heads_ref[:, columns]
                scores = dot_nt(query, key)
                row = z * tokens + lax.broadcasted_iota(jnp.int32, (tokens, 1), 0)
                place = lax.broadcasted_iota(jnp.int32, scores.shape, 1)
                scores = jnp.where(place <= row, scores, MASKED)
                largest = jnp.max(scores, -1, keepdims=True)
                expd = jnp.exp((scores - largest) * (size**-0.5))
                share = 1.0 / jnp.sum(expd, -1, keepdims=True)
                probs = expd * share
                d_probs = dot_nt(grad, value)
                inner = jnp.sum(probs * d_probs, axis=-1, keepdims=True)
                d_raw = (probs * ((d_probs - inner) * (size**-0.5))).astype(BF16)
                d_query = dot_nn(d_raw, key)
                d_query = d_query * cos_ref[...] - swap_halves(d_query) * sin_ref[...]
                d_all_ref[:, columns] = d_query.astype(BF16)
                dkv_acc[j, :, pl.ds(0, size)] += dot_tn(d_raw, query)
                dkv_acc[j, :, pl.ds(size, size)] += dot_tn(probs.astype(BF16), grad)

        def round_kv(j):
            for block in range(nc):
                rows = dkv_acc[j, pl.ds(block * tokens, tokens), :]
                dkv_ref[j, block] = rows.astype(BF16)

        def enter():
            pl.semaphore_wait(credits.at[1], 1)
            pl.semaphore_wait(credits.at[2], 1)

        attend(0, 0, group)
        round_kv(0)
        scatter_kv[0].step(1)
        scatter_o.merge(enter)
        for copy in y_loads:
            copy.wait()
        scatter_y.relay(lambda r, half: y_relay.at[half])
        attend(1, 0, group // 2)
        scatter_kv[0].step(2)
        attend(1, group // 2, group)
        round_kv(1)
        scatter_kv[1].step(1)
        for r in (2, 1):
            expert.send(1, r, when=z == nc - 1)
        scatter_kv[0].step(3)
        scatter_o.relay()

        for copy in loads[6:]:
            copy.wait()
        row_grads(grads_q, inputs_ref, d_all_ref[:, pl.ds(0, query_width)], 0, query_width)
        scatter_q.share()
        scatter_kv[1].step(2)
        scatter_kv[1].step(3)
        expert.send(1, 1, when=z == 1)
        expert.relay_begin(1)
        y_own.wait()
        hidden_ref[...] += heads_ref[...].astype(F32)
        scatter_y.total(hidden_ref)
        layer_ref[...] = hidden_ref[...].astype(BF16)
        scatter_o.total()
        scatter_q.merge()
        for h in range(KEY_VALUE_HEADS):
            scatter_kv[h].last()
        expert.relay_add()
        expert.relay_send(1)

        for h in range(KEY_VALUE_HEADS):
            grad = dkv_ref[h, z, :, pl.ds(0, size)].astype(F32)
            grad = grad * cos_ref[...] - swap_halves(grad) * sin_ref[...]
            d_all_ref[:, pl.ds(query_width + h * size, size)] = grad.astype(BF16)
            d_all_ref[:, pl.ds(query_width + key_width + h * size, size)] = dkv_ref[
                h, z, :, pl.ds(size, size)
            ]

        total = dg_part[0]
        for r in (1, 2, 3):
            wire_1.arrived(dg_land.at[r - 1], dg_slot + r - 1, ids[r])
            total = total + dg_land[r - 1]
        gates = gate_ref[0]
        d_logits = gates * (total - jnp.sum(gates * total, 0, keepdims=True))
        d_logits = jnp.concatenate(
            [d_logits, jnp.zeros((SMALL - d_logits.shape[0], tokens), F32)], 0
        )
        d_all_ref[:, pl.ds(qkv_width, SMALL)] = jnp.transpose(d_logits).astype(BF16)

        for copy in load_q:
            copy.wait()

        @pl.loop(0, planes)
        def _(block):
            columns = pl.ds(pl.multiple_of(block * part, part), part)
            d_inputs_ref[:, columns] = dot_nt(d_all_ref[...], weight[columns, :])

        rows = x_ref[...].astype(F32)
        scale1 = lax.rsqrt(jnp.mean(rows * rows, -1, keepdims=True) + EPSILON)
        d_inputs = d_inputs_ref[...]
        rows_ref[experts : experts + 1, :] = jnp.sum(d_inputs * rows * scale1, 0, keepdims=True)

        def extra(columns):
            small = jnp.transpose(rows_ref[:, columns])
            return jnp.concatenate([jnp.zeros((part, rest - SMALL), F32), small], 1)

        row_grads(
            grads_q, inputs_ref, d_all_ref[:, pl.ds(query_width, rest)], query_width, rest, extra
        )
        scatter_k.share()
        scatter_q.relay()
        scatter_k.merge()
        scaled = d_inputs_ref[...] * gains_ref[0:1]
        rows = x_ref[...].astype(F32)
        scale1 = lax.rsqrt(jnp.mean(rows * rows, -1, keepdims=True) + EPSILON)
        mean = jnp.mean(scaled * rows, -1, keepdims=True)
        d_x = d_hidden_ref[...] + scale1 * scaled - rows * (scale1 * scale1 * scale1 * mean)
        d_x_ref[...] = d_x.astype(BF16)
        scatter_q.total()
        expert.last(0, (sum_gu_hbm, sum_dn_hbm))
        scatter_k.relay()
        scatter_o.line.step(1)
        scatter_q.line.step(1)
        scatter_k.total()
        scatter_k.line.step(1)
        for s in range(2, nc):
            for scatter in (scatter_o, scatter_q, scatter_k):
                scatter.line.step(s)
        for scatter in (scatter_o, scatter_q, scatter_k):
            scatter.line.last()
        sum_o_ref[...] = scatter_o.line.block(z)[...].astype(F32)
        sum_q_ref[...] = grads_q[c, e, pl.ds(pl.multiple_of(z * (rows_of // nc), rows_of // nc), rows_of // nc)].astype(F32)
        expert.last(1, (sum_gu_hbm, sum_dn_hbm))
        wire_2.finish()
        expert.finish()

    held = EXP_DEV
    pl.run_scoped(
        token_phase,
        pltpu.VMEM((held, width, 2 * ff), BF16),
        pltpu.VMEM((held, ff, width), BF16),
        pltpu.VMEM((blocks, tokens, width), BF16),
        pltpu.VMEM((blocks, tokens, held * ff), BF16),
        pltpu.VMEM((blocks, tokens, held * 2 * ff), BF16),
        pltpu.VMEM((2, tokens, width), BF16),
        pltpu.VMEM((blocks - 1, tokens, width), BF16),
        pltpu.VMEM((2, 2, width // nc // 2, grad_width // held), BF16),
    )
    rows_half = width // blocks // 2
    pl.run_scoped(
        token_rows_phase,
        pltpu.VMEM((width, qkv_width + SMALL), BF16),
        pltpu.VMEM((2, blocks, rows_half, width), BF16),
        pltpu.VMEM((2, blocks, rows_half, qkv_width + SMALL), BF16),
        pltpu.VMEM((tokens, width), BF16),
        pltpu.VMEM((tokens, width), BF16),
        pltpu.VMEM((tokens, query_width), BF16),
        pltpu.VMEM((KEY_VALUE_HEADS, nc, tokens, 2 * size), BF16),
        pltpu.VMEM((tokens, query_width), BF16),
        pltpu.VMEM((tokens, width), F32),
        pltpu.VMEM((tokens, width), F32),
        pltpu.VMEM((tokens, width), BF16),
        pltpu.VMEM((tokens, query_width), BF16),
        pltpu.VMEM((tokens, qkv_width + SMALL), BF16),
        pltpu.VMEM((SMALL, width), F32),
        pltpu.VMEM((KEY_VALUE_HEADS, nc * tokens, 2 * size), F32),
        pltpu.VMEM((KEY_VALUE_HEADS, nc, tokens, 2 * size), BF16),
        pltpu.VMEM((2, tokens, width // 2), BF16),
    )


def back(operands, sizes):
    ne, nc, nd = sizes
    cot, w_gu, w_dn, x = operands[6], operands[7], operands[8], operands[9]
    tokens, width = x.shape
    held, ff = w_dn.shape[0], w_dn.shape[1]
    rest = operands[15].shape[-1]
    q_width = QUERY_HEADS * HEAD_DIMENSION + rest
    rows = width // (ne * nc * nd)
    rest_half = rest // 256 * 128
    shard, grads = width // (nc * nd), held * 3 * ff
    kv_size = 2 * HEAD_DIMENSION
    shapes = [
        ((tokens, width), BF16),
        ((tokens, width), BF16),
        ((rows, q_width), F32),
        ((rows, width), F32),
        ((held, shard, 2 * ff), F32),
        ((held, shard, ff), F32),
        ((nc, shard, grads), BF16),
        ((nc + 1, shard, grads), BF16),
        ((ne, tokens, width), BF16),
    ]
    vmem = pl.BlockSpec(memory_space=pltpu.VMEM)
    anywhere = pl.BlockSpec(memory_space=pl.ANY)
    step, units = 48, nc * held
    return pl.pallas_call(
        functools.partial(back_kernel, nc, EXP_DEV * ne),
        out_shape=[jax.ShapeDtypeStruct(*s) for s in shapes],
        in_specs=[vmem] * 5 + [anywhere] * (len(operands) - 5),
        out_specs=[vmem] * 4 + [anywhere] * 5,
        scratch_shapes=[
            pltpu.VMEM((ne, tokens, width), BF16),
            pltpu.VMEM((6, tokens, width // 2), BF16),
            pltpu.VMEM((6, tokens, width // 2), BF16),
            pltpu.VMEM((nc, shard, grads // held), BF16),
            pltpu.VMEM((6, nc * rows, QUERY_HEADS * HEAD_DIMENSION // 2), BF16),
            pltpu.VMEM((6, nc * rows, rest - rest_half), BF16),
            pltpu.VMEM((2, nc - 1, rows, width), BF16),
            pltpu.VMEM((2, nc - 1, rows, QUERY_HEADS * HEAD_DIMENSION), BF16),
            pltpu.VMEM((2, nc - 1, rows, rest), BF16),
            pltpu.VMEM((KEY_VALUE_HEADS, nc - 1, tokens, kv_size), BF16),
            pltpu.VMEM((tokens, width), F32),
            pltpu.VMEM((ne, tokens, SMALL), F32),
            pltpu.VMEM((ne, GATE_ROWS, tokens), F32),
            pltpu.VMEM((ne - 1, GATE_ROWS, tokens), F32),
            pltpu.VMEM((4, shard // step, step, grads // held), BF16),
            pltpu.VMEM((2, step, grads // held), F32),
            pltpu.SemaphoreType.DMA((32,)),
            pltpu.SemaphoreType.DMA((32,)),
            pltpu.SemaphoreType.DMA((64,)),
            pltpu.SemaphoreType.DMA((64,)),
            pltpu.SemaphoreType.DMA((2 * units,)),
            pltpu.SemaphoreType.DMA(((nc + 1) * held,)),
            pltpu.SemaphoreType.DMA((units,)),
            pltpu.SemaphoreType.DMA((units,)),
            pltpu.SemaphoreType.DMA((2,)),
            pltpu.SemaphoreType.DMA((12,)),
            pltpu.SemaphoreType.DMA((20,)),
            pltpu.SemaphoreType.DMA((2,)),
            pltpu.SemaphoreType.REGULAR((4,)),
        ],
        compiler_params=pltpu.CompilerParams(
            collective_id=1, has_side_effects=True, vmem_limit_bytes=63 * MIB
        ),
    )(*operands)


def finish_kernel(experts, *refs):
    sources, dests = refs[:6], refs[6:12]
    router_ref, gains_ref, small_ref, sems = refs[12:]
    sum_q = sources[0]
    qkv_width = dests[0].shape[-1]
    copies = [
        pltpu.make_async_copy(sum_q.at[:, pl.ds(qkv_width, SMALL)], small_ref, sems.at[6]),
        pltpu.make_async_copy(sum_q.at[:, pl.ds(0, qkv_width)], dests[0], sems.at[0]),
    ]
    copies += [
        pltpu.make_async_copy(sources[n], dests[n], sems.at[n]) for n in range(1, len(sources))
    ]
    for copy in copies:
        copy.start()
    copies[0].wait()
    small = small_ref[...]
    rows = small.shape[0]
    filled = jnp.concatenate([small, jnp.zeros((SMALL - rows, SMALL), F32)], 0)
    turned = jnp.transpose(filled)[:, :rows]
    router_ref[...] = turned[:experts]
    gains_ref[...] = turned[experts : experts + 2]
    for copy in copies[1:]:
        copy.wait()


def finish(sum_q, others, experts):
    rows, q_width = sum_q.shape
    anywhere = pl.BlockSpec(memory_space=pl.ANY)
    vmem = pl.BlockSpec(memory_space=pltpu.VMEM)
    shapes = [jax.ShapeDtypeStruct((rows, q_width - SMALL), F32)]
    shapes += [jax.ShapeDtypeStruct(o.shape, o.dtype) for o in others]
    shapes += [jax.ShapeDtypeStruct((experts, rows), F32), jax.ShapeDtypeStruct((2, rows), F32)]
    return pl.pallas_call(
        functools.partial(finish_kernel, experts),
        out_shape=shapes,
        in_specs=[anywhere] * 6,
        out_specs=[anywhere] * 6 + [vmem] * 2,
        scratch_shapes=[pltpu.VMEM((rows, SMALL), F32), pltpu.SemaphoreType.DMA((7,))],
        compiler_params=pltpu.CompilerParams(vmem_limit_bytes=60 * MIB),
    )(sum_q, *others)


def local_plain(
    layer_input,
    gain_attn,
    query_key_value_weight,
    w_out,
    w_router,
    gain_ffn,
    w_gate_up,
    w_down,
    routes,
    d_out,
):
    tokens = layer_input.shape[1]
    model_width = layer_input.shape[2]
    ne, nc, nd = (lax.axis_size(a) for a in ("expert", "context", "dp"))
    expert_total = EXP_DEV * ne
    ff = w_down.shape[1]
    me = lax.axis_index("expert")
    first_row = lax.axis_index("context") * tokens
    query_width = QUERY_HEADS * HEAD_DIMENSION
    key_width = KEY_VALUE_HEADS * HEAD_DIMENSION
    qkv_width = query_width + 2 * key_width

    small = jnp.concatenate([w_router, gain_attn[:, None], gain_ffn[:, None]], -1)
    small = jnp.pad(small, ((0, 0), (0, 128 - small.shape[1])))
    gathered = gather_rows(jnp.concatenate([query_key_value_weight, small], -1))
    out_turned = gather_rows(w_out.T)
    qkv_weight = gathered[:, :qkv_width]
    router_weight = gathered[:, qkv_width : qkv_width + expert_total]
    gains = gathered[:, qkv_width + expert_total : qkv_width + expert_total + 2].T.astype(F32)
    gain_first, gain_second = gains[0], gains[1]
    cotangent_all = plane_gather(d_out[0])

    token_rows = layer_input[0].astype(F32)
    scale1 = lax.rsqrt(jnp.mean(token_rows * token_rows, -1, keepdims=True) + EPSILON)
    inputs1 = (token_rows * scale1 * gain_first).astype(BF16)
    query_key_value = dot_nn(inputs1, qkv_weight)
    cosine_values, sine_values = rope_tables(first_row + jnp.arange(tokens), HEAD_DIMENSION)
    rotated = rotate_half(
        query_key_value[:, : query_width + key_width].reshape(tokens, -1, HEAD_DIMENSION),
        cosine_values,
        sine_values,
    ).reshape(tokens, -1)
    query = rotated[:, :query_width].astype(BF16)
    key_value_local = jnp.concatenate(
        [rotated[:, query_width:], query_key_value[:, query_width + key_width :]], -1
    ).astype(BF16)
    key_value = line_gather(key_value_local, "context", both=False).reshape(nc * tokens, -1)
    first = first_row.astype(jnp.int32).reshape(1)
    heads = attend_forward(first, query, key_value)

    logits = dot_nn(inputs1, router_weight)
    chosen_ids = routes[0]
    picks = (chosen_ids[:, :, None] == jnp.arange(expert_total)[None, None, :]).astype(F32)
    chosen = jnp.sum(picks * logits[:, None, :], -1)
    gates = jax.nn.softmax(chosen, axis=-1)
    gate_dense = jnp.sum(picks * gates[:, :, None], 1).T
    gate_blocks = cube_gather(gate_dense, "expert", axis_masks("expert"))
    gate_local = jnp.concatenate(
        [lax.dynamic_slice_in_dim(b, me * EXP_DEV, EXP_DEV, 0) for b in gate_blocks], 1
    )

    attn = dot_nt(heads, out_turned)
    hidden = token_rows + attn
    scale2 = lax.rsqrt(jnp.mean(hidden * hidden, -1, keepdims=True) + EPSILON)
    expert_in = (hidden * scale2 * gain_second).astype(BF16)

    rows_all = plane_gather(expert_in)
    gate_up = jnp.einsum("td,edf->etf", rows_all, w_gate_up, preferred_element_type=F32)
    gate_part, up_part = gate_up[..., :ff], gate_up[..., ff:]
    sigma = jax.nn.sigmoid(gate_part)
    silu = gate_part * sigma
    act = silu * up_part
    gate_column = gate_local[:, :, None]
    act_gated = (act * gate_column).astype(BF16)
    partial_out = jnp.einsum("etf,efd->td", act_gated, w_down, preferred_element_type=F32)
    mixture = plane_scatter(partial_out.astype(BF16), tokens)
    layer_result = (hidden + mixture).astype(BF16)

    d_act_raw = jnp.einsum("td,efd->etf", cotangent_all, w_down, preferred_element_type=F32)
    d_gates_local = jnp.sum(d_act_raw * act, -1)
    d_act = d_act_raw * gate_column
    d_gate_part = d_act * up_part * sigma * (1.0 + gate_part * (1.0 - sigma))
    d_up_part = d_act * silu
    d_gate_up = jnp.concatenate([d_gate_part, d_up_part], -1).astype(BF16)
    d_rows = jnp.einsum("etf,edf->td", d_gate_up, w_gate_up, preferred_element_type=F32)
    grad_down = jnp.einsum("td,etf->edf", cotangent_all, act_gated, preferred_element_type=F32)
    grad_gate_up = jnp.einsum("td,etf->edf", rows_all, d_gate_up, preferred_element_type=F32)

    d_expert_in = plane_scatter(d_rows.astype(BF16), tokens)
    d_gate_blocks = d_gates_local.reshape(EXP_DEV, ne, tokens)
    d_gates_dense = jnp.zeros((expert_total, tokens), F32)
    for r in range(ne):
        arrived = d_gate_blocks[:, r]
        if r:
            arrived = exchange(arrived, "expert", r)
        d_gates_dense = lax.dynamic_update_slice(d_gates_dense, arrived, ((me ^ r) * EXP_DEV, 0))
    d_gates = jnp.sum(picks * d_gates_dense.T[:, None, :], -1)
    d_chosen = gates * (d_gates - jnp.sum(gates * d_gates, -1, keepdims=True))
    d_logits = jnp.sum(picks * d_chosen[:, :, None], 1).astype(BF16)
    grad_router = dot_tn(inputs1, d_logits)

    core = lax.axis_index("dp")
    part = model_width // (nc * nd)

    def scatter_experts(grad):
        blocks = grad.reshape(EXP_DEV, nc, nd, part, -1)
        mine = cube_scatter(
            [lax.dynamic_index_in_dim(blocks, core ^ r, 2, keepdims=False) for r in range(nd)],
            "dp",
            axis_masks("dp"),
        )
        return line_scatter(
            lambda j: lax.dynamic_index_in_dim(mine, j, 1, keepdims=False), "context"
        )

    sum_gate_up = scatter_experts(grad_gate_up)
    sum_down = jnp.swapaxes(scatter_experts(grad_down), 1, 2)

    cotangent = d_out[0].astype(F32)
    scaled2 = d_expert_in * gain_second
    d_hidden = (
        cotangent
        + scale2 * scaled2
        - hidden * (scale2 * scale2 * scale2) * jnp.mean(scaled2 * hidden, -1, keepdims=True)
    )
    grad_gain_second = jnp.sum(d_expert_in * hidden * scale2, 0)
    d_attn = d_hidden.astype(BF16)
    grad_out_turned = dot_tn(d_attn, heads)
    sum_out = scatter_rows(grad_out_turned).T
    d_heads = dot_nn(d_attn, out_turned).astype(BF16)
    d_query, d_key_all, d_value_all = attend_backward(first, query, key_value, d_heads)
    d_key_value_all = jnp.concatenate([d_key_all, d_value_all], -1).reshape(nc, tokens, -1)
    d_key_value = line_scatter(
        lambda j: lax.dynamic_index_in_dim(d_key_value_all, j, 0, keepdims=False),
        "context",
        up=False,
    )
    d_rotated = rotate_back(
        jnp.concatenate([d_query, d_key_value[:, :key_width]], -1).reshape(
            tokens, -1, HEAD_DIMENSION
        ),
        cosine_values,
        sine_values,
    ).reshape(tokens, -1)
    d_qkv = jnp.concatenate([d_rotated, d_key_value[:, key_width:]], -1).astype(BF16)
    d_inputs = dot_nt(d_qkv, qkv_weight) + dot_nt(d_logits, router_weight)
    grad_gain_first = jnp.sum(d_inputs * token_rows * scale1, 0)
    grad_qkv = dot_tn(inputs1, d_qkv)
    small_grads = jnp.concatenate(
        [grad_router, grad_gain_first[:, None], grad_gain_second[:, None]], -1
    )
    small_grads = jnp.pad(small_grads, ((0, 0), (0, 128 - small_grads.shape[1])))
    sum_rows = scatter_rows(jnp.concatenate([grad_qkv, small_grads], -1))
    sum_qkv = sum_rows[:, :qkv_width]
    sum_router = sum_rows[:, qkv_width : qkv_width + expert_total]
    sum_gain_first = sum_rows[:, qkv_width + expert_total]
    sum_gain_second = sum_rows[:, qkv_width + expert_total + 1]
    scaled1 = d_inputs * gain_first
    d_input_rows = (
        d_hidden
        + scale1 * scaled1
        - token_rows
        * (scale1 * scale1 * scale1)
        * jnp.mean(scaled1 * token_rows, -1, keepdims=True)
    ).astype(BF16)
    return (
        layer_result[None],
        d_input_rows[None],
        sum_gain_first,
        sum_qkv,
        sum_out,
        sum_router,
        sum_gain_second,
        sum_gate_up,
        sum_down,
    )


def local_fused(
    layer_input,
    gain_attn,
    query_key_value_weight,
    w_out,
    w_router,
    gain_ffn,
    w_gate_up,
    w_down,
    routes,
    d_out,
):
    tokens = layer_input.shape[1]
    ne, nc, nd = sizes = tuple(lax.axis_size(a) for a in ("expert", "context", "dp"))
    expert_total = EXP_DEV * ne
    first_row = lax.axis_index("context") * tokens
    query_width = QUERY_HEADS * HEAD_DIMENSION
    key_width = KEY_VALUE_HEADS * HEAD_DIMENSION
    qkv_width = query_width + 2 * key_width

    small = jnp.concatenate([w_router, gain_attn[:, None], gain_ffn[:, None]], -1)
    small = jnp.pad(small, ((0, 0), (0, SMALL - small.shape[1])))
    cosine_values, sine_values = rope_tables(first_row + jnp.arange(tokens), HEAD_DIMENSION)
    sine_values = sine_values * jnp.where(
        jnp.arange(HEAD_DIMENSION) < HEAD_DIMENSION // 2, -1.0, 1.0
    )
    (
        wk_all,
        wq_all,
        wo_all,
        cotangent_all,
        gate_all,
        gate_columns,
        inputs1,
        query,
        key_value,
        heads,
        hidden,
        expert_in,
        gains,
    ) = front(
        (
            layer_input[0],
            query_key_value_weight,
            small,
            w_out.T,
            d_out[0],
            cosine_values,
            sine_values,
            routes[0].T,
        ),
        sizes,
    )
    layer_result, d_x, sum_rows, sum_out, sum_gate_up, sum_down = back(
        (
            gate_columns,
            gate_all,
            gains,
            cosine_values,
            sine_values,
            expert_in,
            cotangent_all,
            w_gate_up,
            w_down,
            layer_input[0],
            inputs1,
            query,
            key_value,
            heads,
            hidden,
            wk_all.reshape(-1, wk_all.shape[-1]),
            wq_all.reshape(-1, query_width),
            wo_all.reshape(-1, wo_all.shape[-1]),
        ),
        sizes,
    )[:6]
    sum_qkv, layer_result, d_x, sum_gate_up, sum_down, sum_out, sum_router, sum_gains = finish(
        sum_rows, (layer_result, d_x, sum_gate_up, sum_down, sum_out), expert_total
    )
    return (
        layer_result[None],
        d_x[None],
        sum_gains[0],
        sum_qkv,
        sum_out.T,
        sum_router.T,
        sum_gains[1],
        sum_gate_up,
        jnp.swapaxes(sum_down, 1, 2),
    )


def solution(mesh):
    in_specs = (
        P(("expert", "dp"), "context", None),
        P(("expert", "context", "dp")),
        P(("expert", "context", "dp"), None),
        P(None, ("expert", "context", "dp")),
        P(("expert", "context", "dp"), None),
        P(("expert", "context", "dp")),
        P("expert", None, None),
        P("expert", None, None),
        P(("expert", "dp"), "context", None),
        P(("expert", "dp"), "context", None),
    )
    out_specs = (
        P(("expert", "dp"), "context", None),
        P(("expert", "dp"), "context", None),
        P(("expert", "context", "dp")),
        P(("expert", "context", "dp"), None),
        P(None, ("expert", "context", "dp")),
        P(("expert", "context", "dp"), None),
        P(("expert", "context", "dp")),
        P("expert", ("context", "dp"), None),
        P("expert", None, ("context", "dp")),
    )
    sizes = tuple(mesh.shape[a] for a in ("expert", "context", "dp"))
    local = local_fused if sizes == (4, 4, 2) else local_plain
    return jax.shard_map(local, mesh=mesh, in_specs=in_specs, out_specs=out_specs, check_vma=False)
```

```python
import functools
import math

import jax
import jax.numpy as jnp
from jax import lax
from jax.experimental import pallas as pl
from jax.experimental.pallas import tpu as pltpu
from jax.sharding import PartitionSpec as P

QUERY_HEADS = 12
KEY_VALUE_HEADS = 2
HEAD_DIMENSION = 128
TOP = 4
EXP_DEV = 2

EPSILON = 1e-06
ROPE_BASE = 10000.0
MASKED = -1e30

F32 = jnp.float32
BF16 = jnp.bfloat16


def rope_tables(positions, width):
    halfway = width // 2
    fraction = jnp.arange(halfway, dtype=jnp.float32) * (2.0 / width)
    frequency = jnp.exp(-math.log(ROPE_BASE) * fraction)
    angles = positions.astype(jnp.float32)[:, None] * frequency[None, :]
    cosine_values = jnp.cos(angles)
    sine_values = jnp.sin(angles)
    return (
        jnp.concatenate([cosine_values, cosine_values], -1),
        jnp.concatenate([sine_values, sine_values], -1),
    )


def rotate_half(values, cosine_values, sine_values):
    halfway = values.shape[-1] // 2
    turned = jnp.concatenate([-values[..., halfway:], values[..., :halfway]], -1)
    return values * cosine_values[:, None, :] + turned * sine_values[:, None, :]


def rotate_back(grads, cosine_values, sine_values):
    halfway = grads.shape[-1] // 2
    scaled = grads * sine_values[:, None, :]
    turned = jnp.concatenate([scaled[..., halfway:], -scaled[..., :halfway]], -1)
    return grads * cosine_values[:, None, :] + turned


def dot_nt(a, b):
    return lax.dot_general(a, b, (((1,), (1,)), ((), ())), preferred_element_type=F32)


def dot_tn(a, b):
    return lax.dot_general(a, b, (((0,), (0,)), ((), ())), preferred_element_type=F32)


def dot_nn(a, b):
    return jnp.dot(a, b, preferred_element_type=F32)


def masked_probs(first_row, query, key):
    scores = dot_nt(query, key) * (HEAD_DIMENSION**-0.5)
    rows = first_row + lax.broadcasted_iota(jnp.int32, scores.shape, 0)
    columns = lax.broadcasted_iota(jnp.int32, scores.shape, 1)
    scores = jnp.where(columns <= rows, scores, MASKED)
    expd = jnp.exp(scores - jnp.max(scores, axis=-1, keepdims=True))
    return expd / jnp.sum(expd, axis=-1, keepdims=True)


def attend_forward_kernel(first_ref, query_ref, key_ref, value_ref, heads_ref):
    probs = masked_probs(first_ref[0], query_ref[...], key_ref[...])
    heads_ref[...] = dot_nn(probs.astype(BF16), value_ref[...]).astype(BF16)


def attend_forward(first_row, query, key_value):
    tokens, width = query.shape
    length = key_value.shape[0]
    group = QUERY_HEADS // KEY_VALUE_HEADS
    size = HEAD_DIMENSION
    return pl.pallas_call(
        attend_forward_kernel,
        grid_spec=pltpu.PrefetchScalarGridSpec(
            num_scalar_prefetch=1,
            grid=(QUERY_HEADS,),
            in_specs=[
                pl.BlockSpec((tokens, size), lambda h, s: (0, h)),
                pl.BlockSpec((length, size), lambda h, s: (0, h // group)),
                pl.BlockSpec((length, size), lambda h, s: (0, KEY_VALUE_HEADS + h // group)),
            ],
            out_specs=pl.BlockSpec((tokens, size), lambda h, s: (0, h)),
        ),
        out_shape=jax.ShapeDtypeStruct((tokens, width), BF16),
        compiler_params=pltpu.CompilerParams(vmem_limit_bytes=32 * 1024 * 1024),
        cost_estimate=pl.CostEstimate(
            flops=4 * tokens * length * width, bytes_accessed=4 * tokens * width, transcendentals=0
        ),
    )(first_row, query, key_value, key_value)


def attend_backward_kernel(
    first_ref, query_ref, key_ref, value_ref, grad_ref, d_query_ref, d_key_ref, d_value_ref
):
    query, key, value, grad = query_ref[...], key_ref[...], value_ref[...], grad_ref[...]
    probs = masked_probs(first_ref[0], query, key)
    d_probs = dot_nt(grad, value)
    inner = jnp.sum(probs * d_probs, axis=-1, keepdims=True)
    d_raw = (probs * (d_probs - inner) * (HEAD_DIMENSION**-0.5)).astype(BF16)
    d_query_ref[...] = dot_nn(d_raw, key)
    d_key = dot_tn(d_raw, query)
    d_value = dot_tn(probs.astype(BF16), grad)

    @pl.when(pl.program_id(1) == 0)
    def _():
        d_key_ref[...] = d_key
        d_value_ref[...] = d_value

    @pl.when(pl.program_id(1) > 0)
    def _():
        d_key_ref[...] += d_key
        d_value_ref[...] += d_value


def attend_backward(first_row, query, key_value, grad):
    tokens, width = query.shape
    length = key_value.shape[0]
    group = QUERY_HEADS // KEY_VALUE_HEADS
    size = HEAD_DIMENSION
    row_spec = pl.BlockSpec((tokens, size), lambda j, g, s: (0, j * group + g))
    return pl.pallas_call(
        attend_backward_kernel,
        grid_spec=pltpu.PrefetchScalarGridSpec(
            num_scalar_prefetch=1,
            grid=(KEY_VALUE_HEADS, group),
            in_specs=[
                row_spec,
                pl.BlockSpec((length, size), lambda j, g, s: (0, j)),
                pl.BlockSpec((length, size), lambda j, g, s: (0, KEY_VALUE_HEADS + j)),
                row_spec,
            ],
            out_specs=[
                row_spec,
                pl.BlockSpec((length, size), lambda j, g, s: (0, j)),
                pl.BlockSpec((length, size), lambda j, g, s: (0, j)),
            ],
        ),
        out_shape=[
            jax.ShapeDtypeStruct((tokens, width), F32),
            jax.ShapeDtypeStruct((length, KEY_VALUE_HEADS * size), F32),
            jax.ShapeDtypeStruct((length, KEY_VALUE_HEADS * size), F32),
        ],
        compiler_params=pltpu.CompilerParams(vmem_limit_bytes=32 * 1024 * 1024),
        cost_estimate=pl.CostEstimate(
            flops=10 * tokens * length * width, bytes_accessed=8 * tokens * width, transcendentals=0
        ),
    )(first_row, query, key_value, key_value, grad)


def exchange(values, axis, mask):
    size = lax.axis_size(axis)
    return lax.ppermute(values, axis, [(i, i ^ mask) for i in range(size)])


def axis_masks(axis):
    size = lax.axis_size(axis)
    masks, bit = [], 1
    while bit < size:
        masks.append(bit)
        bit *= 2
    return masks


def cube_gather(values, axis, masks):
    held = {0: values}
    for mask in masks:
        for r, block in list(held.items()):
            held[r ^ mask] = exchange(block, axis, mask)
    return [held[r] for r in range(lax.axis_size(axis))]


def cube_scatter(blocks, axis, masks):
    held = dict(enumerate(blocks))
    for mask in masks:
        kept = {}
        for r in list(held):
            if not r & mask:
                arrived = exchange(held[r ^ mask].astype(BF16), axis, mask)
                kept[r] = held[r].astype(F32) + arrived.astype(F32)
        held = kept
    return held[0]


def line_steps(values, axis, up):
    size = lax.axis_size(axis)
    pairs = [(i, i + 1) if up else (i + 1, i) for i in range(size - 1)]
    return lax.ppermute(values, axis, pairs)


def line_gather(values, axis, both=True):
    size = lax.axis_size(axis)
    me = lax.axis_index(axis)
    result = jnp.zeros((size + 1,) + values.shape, values.dtype)
    result = lax.dynamic_update_index_in_dim(result, values, me, 0)
    up = down = values
    for step in range(1, size):
        up = line_steps(up, axis, True)
        result = lax.dynamic_update_index_in_dim(
            result, up, jnp.where(me - step >= 0, me - step, size), 0
        )
        if both:
            down = line_steps(down, axis, False)
            result = lax.dynamic_update_index_in_dim(result, down, jnp.minimum(me + step, size), 0)
    return result[:size]


def line_scatter(take, axis, up=True, down=True):
    size = lax.axis_size(axis)
    me = lax.axis_index(axis)
    total = take(me).astype(F32)
    for active, sign in ((up, 1), (down, -1)):
        if not active:
            continue
        arrived = None
        for step in range(1, size):
            block = take((me + sign * (size - step)) % size).astype(F32)
            if arrived is not None:
                block = block + arrived.astype(F32)
            arrived = line_steps(block.astype(BF16), axis, sign > 0)
        total = total + arrived.astype(F32)
    return total


def gather_rows(shard):
    ne, nc, nd = (lax.axis_size(a) for a in ("expert", "context", "dp"))
    rows, width = shard.shape
    lines = line_gather(shard, "context")
    masks = axis_masks("expert")
    half = width // 256 * 128
    parts = [lines[..., :half], lines[..., half:]]
    me = lax.axis_index("expert")
    result = jnp.zeros((ne, nc, rows, width), shard.dtype)
    for start, part, order in ((0, parts[0], masks), (half, parts[1], masks[::-1])):
        for r, block in enumerate(cube_gather(part, "expert", order)):
            result = lax.dynamic_update_slice(result, block[None], (me ^ r, 0, 0, start))
    core = lax.axis_index("dp")
    whole = jnp.zeros((ne, nc, nd, rows, width), shard.dtype)
    for r, block in enumerate(cube_gather(result, "dp", axis_masks("dp"))):
        whole = lax.dynamic_update_slice(whole, block[:, :, None], (0, 0, core ^ r, 0, 0))
    return whole.reshape(-1, width)


def scatter_rows(grad):
    ne, nc, nd = (lax.axis_size(a) for a in ("expert", "context", "dp"))
    width = grad.shape[-1]
    rows = grad.shape[0] // (ne * nc * nd)
    blocks = grad.reshape(ne, nc, nd, rows, width)
    core, me = lax.axis_index("dp"), lax.axis_index("expert")
    mine = cube_scatter(
        [
            lax.dynamic_index_in_dim(blocks, core ^ r, 2, keepdims=False)
            for r in range(nd)
        ],
        "dp",
        axis_masks("dp"),
    )
    masks = axis_masks("expert")
    half = width // 256 * 128
    sums = []
    for part, order in ((mine[..., :half], masks), (mine[..., half:], masks[::-1])):
        sums.append(
            cube_scatter(
                [lax.dynamic_index_in_dim(part, me ^ r, 0, keepdims=False) for r in range(ne)],
                "expert",
                order,
            )
        )
    lines = jnp.concatenate(sums, -1)
    return line_scatter(
        lambda j: lax.dynamic_index_in_dim(lines, j, 0, keepdims=False), "context"
    )


def plane_gather(rows):
    masks = axis_masks("expert")
    half = rows.shape[-1] // 2
    left = cube_gather(rows[:, :half], "expert", masks)
    right = cube_gather(rows[:, half:], "expert", masks[::-1])
    return jnp.concatenate([jnp.concatenate(p, -1) for p in zip(left, right)], 0)


def plane_scatter(partial, tokens):
    masks = axis_masks("expert")
    size = lax.axis_size("expert")
    half = partial.shape[-1] // 2
    blocks = partial.reshape(size, tokens, -1)
    left = cube_scatter([blocks[r, :, :half] for r in range(size)], "expert", masks)
    right = cube_scatter([blocks[r, :, half:] for r in range(size)], "expert", masks[::-1])
    return jnp.concatenate([left, right], -1)


MESH = pl.DeviceIdType.MESH
MIB = 1024 * 1024
SMALL = 128
GATE_ROWS = 16


def flip(index, mask):
    bit = 1
    while bit <= mask:
        if mask & bit:
            index = index + bit - 2 * bit * lax.rem(lax.div(index, bit), 2)
        bit *= 2
    return index


class Wire:
    def __init__(self, sends, recvs):
        self.sends, self.recvs = sends, recvs
        self.n_sends = self.n_recvs = 0
        self.open = []

    def slots(self, count):
        first = self.n_recvs
        self.n_recvs += count
        return first

    def start(self, src, dst, recv, device, when=None):
        number = self.n_sends
        self.n_sends += 1

        def copy():
            return pltpu.make_async_remote_copy(
                src_ref=src() if callable(src) else src,
                dst_ref=dst() if callable(dst) else dst,
                send_sem=self.sends.at[number],
                recv_sem=self.recvs.at[recv],
                device_id=device,
                device_id_type=MESH,
            )

        guard(when, lambda: copy().start())
        self.open.append((when, copy))

    def arrived(self, dst, recv, device):
        pltpu.make_async_remote_copy(
            src_ref=dst,
            dst_ref=dst,
            send_sem=self.sends.at[0],
            recv_sem=self.recvs.at[recv],
            device_id=device,
            device_id_type=MESH,
        ).wait_recv()

    def finish(self):
        for when, copy in self.open:
            guard(when, lambda copy=copy: copy().wait_send())
        self.open = []


def guard(when, action):
    if when is None:
        action()
    else:
        pl.when(when)(action)


def add_into(dest, source, steps=4):
    rows = dest.shape[0] // steps

    @pl.loop(0, steps)
    def _(n):
        here = pl.ds(pl.multiple_of(n * rows, rows), rows)
        dest[here] = (dest[here].astype(F32) + source[here].astype(F32)).astype(BF16)


def greet(targets):
    barrier = pltpu.get_barrier_semaphore()
    for device, when in targets:
        guard(
            when,
            lambda device=device: pl.semaphore_signal(
                barrier, inc=1, device_id=device, device_id_type=MESH
            ),
        )
    count = sum(1 if when is None else when.astype(jnp.int32) for _, when in targets)
    pl.semaphore_wait(barrier, count)


def plane_ids(e):
    return {m: {"expert": flip(e, m)} for m in (1, 2, 3)}


class RowsGather:
    def __init__(self, wire, ref, e, z, c, nc, half, into=None, sems=None):
        self.into, self.sems = into, sems
        self.wire, self.ref, self.e, self.z, self.c, self.nc = wire, ref, e, z, c, nc
        self.cols = (pl.ds(0, half), pl.ds(half, ref.shape[-1] - half))
        self.line = wire.slots(nc)
        self.plane = wire.slots(nc * 6)
        self.core = wire.slots(nc)
        self.ids = plane_ids(e)

    def go(self, *steps):
        for step in steps:
            action = {"l": self.pass_on, "s": self.spread, "f": self.forward, "h": self.share, "c": self.complete}
            action[step[0]](*map(int, step[1:]))

    def shard(self, k):
        if k < 2:
            return flip(self.z, k)
        inner = (self.z > 0) & (self.z < self.nc - 1)
        return jnp.where(inner, flip(self.z, 5 - k), flip(self.z, k))

    def at(self, r, zs, half):
        return self.ref.at[flip(self.e, r), zs, self.c, :, self.cols[half]]

    def slot(self, k, r, half):
        return self.plane + k * 6 + (r - 1) * 2 + half

    def pass_on(self, k):
        wire, z, nc = self.wire, self.z, self.nc
        zs = self.shard(k)
        whole = self.ref.at[self.e, zs, self.c]
        if k:
            wire.arrived(whole, self.line + zs, {"context": zs})
        wire.start(
            whole, whole, self.line + zs, {"context": z + 1}, when=(zs <= z) & (z < nc - 1)
        )
        wire.start(whole, whole, self.line + zs, {"context": z - 1}, when=(zs >= z) & (z > 0))

    def spread(self, k):
        zs = self.shard(k)
        for half, mask in ((0, 1), (1, 2), (1, 1), (0, 2)):
            part = self.at(0, zs, half)
            self.wire.start(part, part, self.slot(k, mask, half), self.ids[mask])

    def forward(self, k):
        zs = self.shard(k)
        for half, mask in ((0, 1), (1, 2)):
            part = self.at(mask, zs, half)
            self.wire.arrived(part, self.slot(k, mask, half), self.ids[mask])
            self.wire.start(part, part, self.slot(k, 3, half), self.ids[3 - mask])

    def share(self, k):
        zs = self.shard(k)
        for r, half in ((1, 1), (2, 0), (3, 0), (3, 1)):
            self.wire.arrived(self.at(r, zs, half), self.slot(k, r, half), self.ids[r])
        part = self.ref.at[:, zs, self.c]
        self.wire.start(part, part, self.core + k, {"dp": 1 - self.c})
        if self.into is not None:
            self.load(k, self.c, 0).start()

    def load(self, k, core, number):
        zs = self.shard(k)
        return pltpu.make_async_copy(
            self.ref.at[:, zs, core], self.into.at[:, zs, core], self.sems.at[2 * k + number]
        )

    def complete(self):
        for k in range(self.nc):
            zs = self.shard(k)
            self.wire.arrived(self.ref.at[:, zs, 1 - self.c], self.core + k, {"dp": 1 - self.c})
            if self.into is not None:
                self.load(k, 1 - self.c, 1).start()
        if self.into is not None:
            for k in range(self.nc):
                self.load(k, self.c, 0).wait()
                self.load(k, 1 - self.c, 1).wait()


class PlaneGather:
    def __init__(self, wire, ref, e, own=None):
        self.wire, self.ref, self.own = wire, ref, own
        self.half = ref.shape[-1] // 2
        self.ids = plane_ids(e)
        self.first = wire.slots(6)

    def at(self, r, half):
        columns = pl.ds(half * self.half, self.half)
        if r == 0 and self.own is not None:
            return self.own.at[:, columns]
        return self.ref.at[r, :, columns]

    def slot(self, r, half):
        return self.first + (r - 1) * 2 + half

    def send(self, r, half, to, mask):
        self.wire.start(
            lambda: self.at(r, half), lambda: self.at(to, half), self.slot(to, half), self.ids[mask]
        )

    def spread(self):
        for half, mask in ((0, 1), (1, 2), (1, 1), (0, 2)):
            self.send(0, half, mask, mask)

    def forward(self):
        for half, mask in ((0, 1), (1, 2)):
            self.wire.arrived(self.at(mask, half), self.slot(mask, half), self.ids[mask])
            self.send(mask, half, 3, 3 - mask)

    def near(self, r):
        half = 1 if r == 1 else 0
        self.wire.arrived(self.at(r, half), self.slot(r, half), self.ids[r])

    def far(self):
        for half in (0, 1):
            self.wire.arrived(self.at(3, half), self.slot(3, half), self.ids[3])

    def complete(self):
        self.near(1)
        self.near(2)
        self.far()


def swap_halves(values):
    return pltpu.roll(values, HEAD_DIMENSION // 2, 1)


class PlaneScatter:
    def __init__(self, wire, land, ids):
        self.wire, self.land, self.ids, self.part = wire, land, ids, None
        self.half = land.shape[-1]
        self.first = wire.slots(6)

    def send(self, source, mask, slot):
        self.wire.start(source, lambda: self.land.at[slot], self.first + slot, self.ids[mask])

    def near(self, r):
        self.send(self.part(r, r - 1), r, r - 1)

    def far(self):
        self.send(self.part(3, 0), 1, 2)
        self.send(self.part(3, 1), 2, 3)

    def relay(self, part=None):
        for half, r in ((0, 2), (1, 1)):
            slot = 2 + half
            self.wire.arrived(self.land.at[slot], self.first + slot, self.ids[3 - r])
            take = part or self.part
            mine = take(r, half)
            add_into(mine, self.land.at[slot])
            self.send(lambda r=r, half=half, take=take: take(r, half), r, 4 + half)

    def total(self, own):
        for slot, half, mask in ((0, 0, 1), (1, 1, 2), (4, 0, 2), (5, 1, 1)):
            self.wire.arrived(self.land.at[slot], self.first + slot, self.ids[mask])
            columns = pl.ds(half * self.half, self.half)
            rows = own.shape[0] // 4

            @pl.loop(0, 4)
            def _(n):
                here = pl.ds(pl.multiple_of(n * rows, rows), rows)
                own[here, columns] += self.land[slot, here].astype(F32)


class LineScatter:
    def __init__(self, wire, block, lands, z, nc, up=True):
        self.wire, self.block, self.lands, self.z, self.nc = wire, block, lands, z, nc
        self.up = up
        self.first = [wire.slots(nc - 1), wire.slots(nc - 1)]

    def arrive(self, way, index, j):
        land = self.lands[way].at[index]
        self.wire.arrived(land, self.first[way] + index, {"context": self.z})
        add_into(self.block(j), land, 1)

    def move(self, way, j, only=None):
        z, nc = self.z, self.nc
        inner, index = ((z > 0), j - z) if way == 0 else ((z < nc - 1), z - j)
        wanted = (j > z) if way == 0 else (j < z)
        if only is not None:
            wanted = wanted & only
        pl.when(wanted & inner)(lambda: self.arrive(way, index, j))
        self.leave(way, j, wanted)

    def step(self, s):
        if self.up:
            self.move(0, self.nc - s)
            self.move(1, s - 1)
        else:
            top = self.z == self.nc - 1
            if s == 1:
                for j in range(self.nc - 1):
                    self.leave(1, j, top)
            self.move(1, s - 1, jnp.logical_not(top))

    def leave(self, way, j, wanted):
        z = self.z
        index, near = (j - z, z + 1) if way == 0 else (z - j, z - 1)
        self.wire.start(
            self.block(j),
            self.lands[way].at[index - 1],
            self.first[way] + index - 1,
            {"context": near},
            when=wanted,
        )

    def last(self):
        if self.up:
            pl.when(self.z > 0)(lambda: self.arrive(0, 0, self.z))
        pl.when(self.z < self.nc - 1)(lambda: self.arrive(1, 0, self.z))


class RowsScatter:
    def __init__(self, wire, buf, core, plane, lines, e, z, c, nc, start, width, half):
        self.wire, self.buf, self.core, self.plane = wire, buf, core, plane
        self.e, self.c = e, c
        self.all = pl.ds(start, width)
        self.cols = (pl.ds(start, half), pl.ds(start + half, width - half))
        self.ids = plane_ids(e)
        self.core_slot = wire.slots(1)
        self.first = wire.slots(6)
        rows = buf.shape[2] // nc
        self.line = LineScatter(
            wire,
            lambda j: buf.at[c, e, pl.ds(pl.multiple_of(j * rows, rows), rows), self.all],
            lines,
            z,
            nc,
        )

    def share(self):
        self.wire.start(
            self.buf.at[1 - self.c, :, :, self.all], self.core, self.core_slot, {"dp": 1 - self.c}
        )

    def at(self, r, half):
        return self.buf.at[self.c, flip(self.e, r), :, self.cols[half]]

    def send(self, r, half, mask, slot):
        self.wire.start(
            self.at(r, half), self.plane(slot, half), self.first + slot, self.ids[mask]
        )

    def merge(self, before=None):
        self.wire.arrived(self.core, self.core_slot, {"dp": 1 - self.c})
        for r in (3, 1, 2, 0):
            block = flip(self.e, r)
            part = self.buf.at[self.c, block, :, self.all]
            add_into(part, self.core.at[block])
            if r == 3:
                if before is not None:
                    before()
                self.send(3, 0, 1, 2)
                self.send(3, 1, 2, 3)
            elif r:
                self.send(r, r - 1, r, r - 1)

    def add(self, r, half, slot, mask):
        land = self.plane(slot, half)
        self.wire.arrived(land, self.first + slot, self.ids[mask])
        add_into(self.at(r, half), land)

    def relay(self):
        for half, r in ((0, 2), (1, 1)):
            self.add(r, half, 2 + half, 3 - r)
            self.send(r, half, r, 4 + half)

    def total(self):
        for slot, half, mask in ((0, 0, 1), (1, 1, 2), (4, 0, 2), (5, 1, 1)):
            self.add(0, half, slot, mask)


class ExpertLine:
    def __init__(self, wire, base, land, sems, z, nc):
        self.wire, self.base, self.land = wire, base, land
        self.ins, self.out, self.sems, self.z, self.nc = None, None, sems, z, nc
        self.end = (z == 0) | (z == nc - 1)
        self.inner = jnp.logical_not(self.end)
        self.width = base.shape[-1] // EXP_DEV
        self.first = wire.slots((nc + 1) * EXP_DEV)
        self.sent = []

    def part(self, ref, j, i):
        return ref.at[j, :, pl.ds(i * self.width, self.width)]

    def combine(self, sources, stores):
        out, step = self.out, self.ins.shape[2]
        count = sources[0].shape[0] // step

        def loads(p):
            rows = pl.ds(p * step, step)
            return [
                pltpu.make_async_copy(source.at[rows], self.ins.at[k, p], self.sems.at[4 * k + p])
                for k, source in enumerate(sources)
            ]

        def store(p):
            pairs = stores(pl.ds(p * step, step), out.at[p % 2])
            return [
                pltpu.make_async_copy(source, dest, self.sems.at[16 + 2 * n + p % 2])
                for n, (source, dest) in enumerate(pairs)
            ]

        for p in range(count):
            for copy in loads(p):
                copy.start()
        for p in range(count):
            for copy in loads(p):
                copy.wait()
            if p > 1:
                for copy in store(p - 2):
                    copy.wait()
            total = self.ins[0, p].astype(F32)
            for k in range(1, len(sources)):
                total = total + self.ins[k, p].astype(F32)
            out[p % 2] = total.astype(out.dtype)
            for copy in store(p):
                copy.start()
        for p in range(max(0, count - 2), count):
            for copy in store(p):
                copy.wait()

    def copy(self, i, r, number):
        target, slot = flip(self.z, r), self.z
        if r == 3:
            target = jnp.where(self.end, flip(self.z, 1), target)
            slot = jnp.where(self.end, self.nc, slot)
        return pltpu.make_async_remote_copy(
            src_ref=self.part(self.base, flip(self.z, r), i),
            dst_ref=self.part(self.land, slot, i),
            send_sem=self.wire.sends.at[number],
            recv_sem=self.wire.recvs.at[self.first + slot * EXP_DEV + i],
            device_id={"context": target},
            device_id_type=MESH,
        )

    def send(self, i, r, when=None):
        number = len(self.sent)
        guard(when, self.copy(i, r, number).start)
        self.sent.append((when, i, r, number))

    def finish(self):
        for when, i, r, number in self.sent:
            guard(when, self.copy(i, r, number).wait_send)

    def arrived(self, slot, i):
        land = self.part(self.land, slot, i)
        self.wire.arrived(land, self.first + slot * EXP_DEV + i, {"context": self.z})

    def relay_loads(self, i, p):
        step = self.ins.shape[2]
        rows = pl.ds(p * step, step)
        sources = (self.part(self.base, flip(self.z, 2), i), self.part(self.land, self.nc, i))
        return [
            pltpu.make_async_copy(
                source.at[rows], self.ins.at[k, p], self.sems.at[4 * k + p]
            )
            for k, source in enumerate(sources)
        ]

    def relay_store(self, i, p):
        step = self.ins.shape[2]
        mine = self.part(self.base, flip(self.z, 2), i).at[pl.ds(p * step, step)]
        return pltpu.make_async_copy(self.ins.at[0, p], mine, self.sems.at[16 + p])

    def relay_steps(self):
        return range(self.base.shape[1] // self.ins.shape[2])

    def relay_begin(self, i):
        self.relayed = i

        def begin():
            self.arrived(self.nc, i)
            for p in self.relay_steps():
                for copy in self.relay_loads(i, p):
                    copy.start()

        pl.when(self.inner)(begin)

    def relay_add(self):
        i = self.relayed

        def add():
            for p in self.relay_steps():
                for copy in self.relay_loads(i, p):
                    copy.wait()
                a, b = (self.ins[k, p].astype(F32) for k in range(2))
                self.ins[0, p] = (a + b).astype(BF16)
                self.relay_store(i, p).start()

        pl.when(self.inner)(add)

    def relay_send(self, i):
        def wait():
            for p in self.relay_steps():
                self.relay_store(i, p).wait()

        pl.when(self.inner)(wait)
        self.send(i, 2, when=self.inner)

    def last(self, i, results):
        z = self.z
        sources = [self.part(self.base, z, i)]
        for r in (1, 2):
            self.arrived(flip(z, r), i)
            sources.append(self.part(self.land, flip(z, r), i))

        def stores(rows, wide):
            pairs, first = [], 0
            for result in results:
                columns = pl.ds(first, result.shape[-1])
                pairs.append((wide.at[:, columns], result.at[i, rows]))
                first += result.shape[-1]
            return pairs

        pl.when(self.end)(lambda: self.combine(sources, stores))

        def inner():
            self.arrived(flip(z, 3), i)
            self.combine(sources + [self.part(self.land, flip(z, 3), i)], stores)

        pl.when(self.inner)(inner)


def layer_kernel(
    nc,
    experts,
    cos_ref,
    sin_ref,
    routes_ref,
    qkv_ref,
    small_ref,
    wo_shard_ref,
    x_hbm,
    d_out_hbm,
    w_gu_hbm,
    w_dn_hbm,
    layer_hbm,
    d_x_hbm,
    sum_q_ref,
    sum_o_ref,
    sum_gu_hbm,
    sum_dn_hbm,
    base_hbm,
    land_hbm,
    y_hbm,
    wq_hbm,
    wo_hbm,
    cot_hbm,
    inputs_hbm,
    query_hbm,
    heads_hbm,
    hidden_hbm,
    wk_all,
    kv_ref,
    gate_all,
    gates_ref,
    gains_ref,
    x_all,
    y_land,
    dx_land,
    core_land,
    plane_q,
    plane_k,
    lines_o,
    lines_q,
    lines_k,
    dkv_land,
    d_in_ref,
    dg_lanes,
    dg_part,
    dg_land,
    sends_f,
    recvs_f,
    sends_c,
    recvs_c,
    sends_1,
    recvs_1,
    sends_2,
    recvs_2,
    sends_e,
    recvs_e,
    hand_sends,
    hand_recvs,
    stage_sems,
    load_sems,
    out_sems,
    weight_sems,
    sum_sems,
    y_sems,
    credits,
):
    e, z, c = (lax.axis_index(a) for a in ("expert", "context", "dp"))
    size = HEAD_DIMENSION
    blocks, tokens, width = cot_hbm.shape
    ff = w_dn_hbm.shape[1]
    query_width = QUERY_HEADS * size
    key_width = KEY_VALUE_HEADS * size
    qkv_width = query_width + 2 * key_width
    rest = wk_all.shape[-1]
    grad_width = base_hbm.shape[-1]
    ids = plane_ids(e)
    sibling = {"dp": 1 - c}
    bottom, even = z == 0, lax.rem(z, 2) == 0
    wire_1, wire_2, wire_e = Wire(sends_1, recvs_1), Wire(sends_2, recvs_2), Wire(sends_e, recvs_e)
    expert = ExpertLine(wire_e, base_hbm, land_hbm, sum_sems, z, nc)
    wire_c = Wire(sends_c, recvs_c)
    gather_cot = PlaneGather(wire_c, cot_hbm, e, d_out_hbm)
    gather = PlaneGather(wire_1, x_all, e)
    scatter_dx = PlaneScatter(wire_1, dx_land, ids)
    scatter_y = PlaneScatter(wire_2, y_land, ids)
    dg_slot = wire_1.slots(3)

    def front_phase(wq_ref, wo_ref, x_ref, inputs_ref, query_ref, heads_ref, hidden_ref, kv_scr, q_scr):
        wire = Wire(sends_f, recvs_f)
        kv_width = 2 * key_width
        own = (
            (qkv_ref.at[:, pl.ds(0, query_width)], wq_hbm.at[e, z, c]),
            (wo_shard_ref, wo_hbm.at[e, z, c]),
            (x_hbm, x_ref),
        )
        copies = [
            pltpu.make_async_copy(source, dest, load_sems.at[n])
            for n, (source, dest) in enumerate(own)
        ]
        for copy in copies:
            copy.start()
        load_x = copies.pop()
        wk_all[e, z, c, :, pl.ds(0, kv_width)] = qkv_ref[:, pl.ds(query_width, kv_width)]
        wk_all[e, z, c, :, pl.ds(kv_width, SMALL)] = small_ref[...]
        greet(
            [(ids[m], None) for m in (1, 2, 3)]
            + [(sibling, None)]
            + [({"context": z + d}, z + d < nc) for d in range(1, nc)]
            + [({"context": z - d}, z >= d) for d in range(1, nc)]
        )
        gather_k = RowsGather(wire, wk_all, e, z, c, nc, 256)
        gather_q = RowsGather(wire, wq_hbm, e, z, c, nc, 768, wq_ref, weight_sems.at[0])
        gather_o = RowsGather(wire, wo_hbm, e, z, c, nc, 768, wo_ref, weight_sems.at[1])
        for copy in copies:
            copy.wait()
        gather_k.go("l0", "s0")
        gather_q.go("s0")
        gather_k.go("l1", "s1", "f0", "l2", "s2")
        gather_q.go("l0")
        gather_k.go("f1", "h0", "l3", "s3")
        gather_q.go("l1", "s1")
        gather_o.go("l0")
        gather_k.go("f2", "h1", "f3")
        gather_q.go("l2", "s2")
        gather_k.go("h2")
        gather_o.go("l1")
        gather_q.go("f0")
        gather_k.go("h3")
        gather_q.go("l3", "s3")
        gather_k.go("c")
        load_x.wait()
        rows = x_ref[...].astype(F32)
        scale1 = lax.rsqrt(jnp.mean(rows * rows, -1, keepdims=True) + EPSILON)

        small = wk_all[:, :, :, :, pl.ds(kv_width, SMALL)].reshape(width, SMALL)
        small = jnp.transpose(small.astype(F32))
        gain_first, gain_second = small[experts : experts + 1], small[experts + 1 : experts + 2]
        gains_ref[0:1] = gain_first
        gains_ref[1:2] = gain_second
        inputs_ref[...] = (rows * scale1 * gain_first).astype(BF16)
        kv_scr[...] = dot_nn(inputs_ref[...], wk_all[...].reshape(width, kv_width + SMALL))

        def turned(head):
            return (head * cos_ref[...] + swap_halves(head) * sin_ref[...]).astype(BF16)

        line = wire.slots(KEY_VALUE_HEADS * nc)
        for j in range(KEY_VALUE_HEADS):
            kv_ref[j, z, :, pl.ds(0, size)] = turned(kv_scr[:, pl.ds(j * size, size)])
            value = kv_scr[:, pl.ds(kv_width // 2 + j * size, size)]
            kv_ref[j, z, :, pl.ds(size, size)] = value.astype(BF16)
            mine = kv_ref.at[j, z]
            for d in range(nc - 1, 0, -1):
                wire.start(mine, mine, line + j * nc + z, {"context": z + d}, when=z + d < nc)

        def keys_here(j):
            for d in range(1, nc):

                def wait(d=d):
                    wire.arrived(kv_ref.at[j, z - d], line + j * nc + z - d, {"context": z - d})

                pl.when(z >= d)(wait)

        outs = [
            pltpu.make_async_copy(source, dest, out_sems.at[n])
            for n, (source, dest) in enumerate(
                (
                    (inputs_ref, inputs_hbm),
                    (query_ref, query_hbm),
                    (heads_ref, heads_hbm),
                    (hidden_ref, hidden_hbm),
                )
            )
        ]
        outs[0].start()
        for later in range(1, nc):

            def clear(later=later):
                for j in range(KEY_VALUE_HEADS):
                    kv_ref[j, z + later] = jnp.zeros(kv_ref.shape[2:], BF16)

            pl.when(z + later < nc)(clear)
        gather_q.go("f1", "f2", "h0")
        gather_o.go("s0")
        gather_q.go("f3", "h1")
        gather_o.go("s1")
        gather_q.go("h2", "h3", "c")
        gather_o.go("f0", "f1")
        gather_cot.spread()

        @pl.loop(0, query_width // 256)
        def _(n):
            columns = pl.ds(pl.multiple_of(n * 256, 256), 256)
            q_scr[:, columns] = dot_nn(
                inputs_ref[...], wq_ref[:, :, :, :, columns].reshape(width, 256)
            )

        @pl.loop(0, QUERY_HEADS)
        def _(h):
            columns = pl.ds(pl.multiple_of(h * size, size), size)
            query_ref[:, columns] = turned(q_scr[:, columns])

        outs[1].start()

        logits = kv_scr[:, pl.ds(kv_width, SMALL)]
        lanes = lax.broadcasted_iota(jnp.int32, logits.shape, 1)
        routes = jnp.concatenate(
            [routes_ref[...].astype(F32), jnp.zeros((SMALL - TOP, tokens), F32)], 0
        )
        routes = jnp.transpose(routes).astype(jnp.int32)
        named = lanes == routes[:, 0:1]
        for k in range(1, TOP):
            named = named | (lanes == routes[:, k : k + 1])
        logits = jnp.where(named, logits, MASKED)
        expd = jnp.exp(logits - jnp.max(logits, -1, keepdims=True))
        gates = expd / jnp.sum(expd, -1, keepdims=True)
        gate_all[0] = jnp.transpose(gates)[:GATE_ROWS]
        gate_slot = wire.slots(3)
        for r in (1, 2, 3):
            wire.start(gate_all.at[0], gate_all.at[r], gate_slot + r - 1, ids[r])

        length = nc * tokens
        group = QUERY_HEADS // KEY_VALUE_HEADS

        def attend(first, last):
            j = first // group
            key = kv_ref[j, :, :, pl.ds(0, size)].reshape(length, size)
            value = kv_ref[j, :, :, pl.ds(size, size)].reshape(length, size)

            @pl.loop(first, last)
            def _(h):
                column = pl.multiple_of(h * size, size)
                scores = dot_nt(query_ref[:, pl.ds(column, size)], key) * (size**-0.5)
                row = z * tokens + lax.broadcasted_iota(jnp.int32, scores.shape, 0)
                place = lax.broadcasted_iota(jnp.int32, scores.shape, 1)
                scores = jnp.where(place <= row, scores, MASKED)
                expd = jnp.exp(scores - jnp.max(scores, -1, keepdims=True))
                total = jnp.sum(expd, -1, keepdims=True)
                mixed = dot_nn(expd.astype(BF16), value) / total
                heads_ref[:, pl.ds(column, size)] = mixed.astype(BF16)

        half = group // 2
        keys_here(0)
        attend(0, half)
        gather_o.go("l2", "s2")
        attend(half, group)
        gather_o.go("l3", "s3", "f2", "h0")
        keys_here(1)
        attend(group, group + half)
        gather_o.go("f3", "h1")
        attend(group + half, QUERY_HEADS)
        gather_o.go("h2")
        gather_cot.forward()
        gather_o.go("h3", "c")
        outs[2].start()
        part = width // wo_ref.shape[0]
        for block in range(wo_ref.shape[0]):
            weight = wo_ref[block].reshape(part, width)
            columns = pl.ds(block * part, part)
            hidden_ref[:, columns] = x_ref[:, columns].astype(F32) + dot_nt(heads_ref[...], weight)
        hidden = hidden_ref[...]
        scale2 = lax.rsqrt(jnp.mean(hidden * hidden, -1, keepdims=True) + EPSILON)
        x_all[0] = (hidden * scale2 * gains_ref[1:2]).astype(BF16)
        gather.spread()
        outs[3].start()
        for r in (1, 2, 3):
            wire.arrived(gate_all.at[r], gate_slot + r - 1, ids[r])
        for r in range(gate_all.shape[0]):
            zeros = jnp.zeros((SMALL - GATE_ROWS, tokens), F32)
            turned_gates = jnp.transpose(jnp.concatenate([gate_all[r], zeros], 0))
            both = [
                jnp.sum(jnp.where(lanes == e * EXP_DEV + i, turned_gates, 0.0), -1, keepdims=True)
                for i in range(EXP_DEV)
            ]
            gates_ref[r] = jnp.where(lanes == 0, both[0], jnp.where(lanes == 1, both[1], 0.0))
        for copy in outs:
            copy.wait()
        wire.finish()

    def token_phase(w_gu, w_dn, cot_all, a_all, dgu_all, y_stage, dx_part, stage, ins):
        expert.ins = ins
        scatter_dx.part = lambda r, half: dx_part.at[
            r - 1, :, pl.ds(half * width // 2, width // 2)
        ]
        sources = [
            (w_gu_hbm.at[0], w_gu.at[0]),
            (w_dn_hbm.at[0], w_dn.at[0]),
            (d_out_hbm, cot_all.at[0]),
            (w_gu_hbm.at[1], w_gu.at[1]),
            (w_dn_hbm.at[1], w_dn.at[1]),
            (cot_hbm.at[1:], cot_all.at[1:]),
        ]
        loads = [
            pltpu.make_async_copy(source, dest, load_sems.at[n])
            for n, (source, dest) in enumerate(sources)
        ]
        for copy in loads[:5]:
            copy.start()
        step = 256
        wide = 512
        dg_lanes[...] = jnp.zeros_like(dg_lanes)

        def hidden_units(r, i, count=1):
            lane = lax.broadcasted_iota(jnp.int32, (1, SMALL), 1)
            here = pl.ds(r, count)
            flat = count * tokens

            @pl.loop(0, ff // step)
            def _(f):
                column = pl.multiple_of(f * step, step)
                rows = x_all[here].reshape(flat, width)
                grads = cot_all[here].reshape(flat, width)
                gate_part = dot_nn(rows, w_gu[i, :, pl.ds(column, step)])
                up_part = dot_nn(rows, w_gu[i, :, pl.ds(ff + column, step)])
                raw = dot_nt(grads, w_dn[i, pl.ds(column, step), :])
                gate = gates_ref[here].reshape(flat, SMALL)
                gate = jnp.sum(jnp.where(lane == i, gate, 0.0), -1, keepdims=True)
                sigma = jax.nn.sigmoid(gate_part)
                silu = gate_part * sigma
                act = silu * up_part
                lanes = lax.broadcasted_iota(jnp.int32, (flat, SMALL), 1)
                d_gate = jnp.where(
                    lanes == e * EXP_DEV + i, jnp.sum(act * raw, -1, keepdims=True), 0.0
                )
                dg_lanes[here] += d_gate.reshape(count, tokens, SMALL)

                def put(ref, first, values):
                    values = values.astype(BF16).reshape(count, tokens, step)
                    ref[here, :, pl.ds(pl.multiple_of(first, step), step)] = values

                put(a_all, i * ff + column, act * gate)
                d_act = raw * gate
                d_gate_part = d_act * up_part * sigma * (1.0 + gate_part * (1.0 - sigma))
                put(dgu_all, i * 2 * ff + column, d_gate_part)
                put(dgu_all, i * 2 * ff + ff + column, d_act * silu)

        def y_copy(r):
            return pltpu.make_async_copy(y_stage.at[r % 2], y_hbm.at[r], y_sems.at[r % 2])

        def outputs(r, count=1):
            here = pl.ds(r, count)
            flat = count * tokens

            @pl.loop(0, width // wide)
            def _(n):
                columns = pl.ds(pl.multiple_of(n * wide, wide), wide)
                low = dgu_all[here].reshape(flat, EXP_DEV * 2 * ff)
                d_rows = dot_nt(low[:, : 2 * ff], w_gu[0, columns, :])
                d_rows += dot_nt(low[:, 2 * ff :], w_gu[1, columns, :])
                weight = w_dn[:, :, columns].reshape(EXP_DEV * ff, wide)
                out = dot_nn(a_all[here].reshape(flat, EXP_DEV * ff), weight).astype(BF16)
                for k in range(count):
                    rows = slice(k * tokens, (k + 1) * tokens)
                    y_stage[(r + k) % 2, :, columns] = out[rows]
                    if r == 0:
                        d_in_ref[:, columns] = d_rows
                    else:
                        dx_part[r + k - 1, :, columns] = d_rows[rows].astype(BF16)

            for k in range(r, r + count):
                y_copy(k).start()
                dg_part[k] = jnp.transpose(dg_lanes[k])[:GATE_ROWS]
                if k:
                    wire_1.start(dg_part.at[k], dg_land.at[k - 1], dg_slot + k - 1, ids[k])

        half_rows = width // nc // 2
        def where(k):
            high = lax.rem(lax.div(z, 2) + 1 + lax.div(k, 2), 2)
            return 2 * high + lax.rem(z + 1 + k, 2)

        def keep(i, k):
            slot = lax.rem(k, 2)
            return pltpu.make_async_copy(
                stage.at[slot, c], expert.part(base_hbm, where(k), i), stage_sems.at[slot]
            )

        def hand(i, k):
            return pltpu.make_async_remote_copy(
                src_ref=stage.at[lax.rem(k, 2), 1 - c],
                dst_ref=core_land.at[k],
                send_sem=hand_sends.at[i * nc + k],
                recv_sem=hand_recvs.at[i * nc + k],
                device_id=sibling,
                device_id_type=MESH,
            )

        def settle(i, k):
            hand(i, k).wait_recv()
            add_into(stage.at[lax.rem(k, 2), c], core_land.at[k])
            keep(i, k).start()

        def clear(i, k):
            keep(i, k).wait()
            hand(i, k).wait_send()

        def leave(i, r):
            if i == 0 and r == 2:
                expert.send(i, r, when=expert.end)
            elif i == 0 and r == 1 or r == 3:
                expert.send(i, r)
            elif r == 2:
                expert.send(i, r, when=bottom)
            elif r == 1:
                expert.send(i, r, when=even)

        def weight_grads(i, between=lambda k: None):
            @pl.loop(0, nc)
            def _(k):
                @pl.when(k >= 2)
                def _():
                    clear(i, k - 2)

                for n in (2, 3):

                    @pl.when(k == n)
                    def _(n=n):
                        leave(i, 5 - n)

                rows_at = pl.ds(pl.multiple_of(where(k) * 2 * half_rows, 2 * half_rows), 2 * half_rows)
                for first, source, grad, start, count in (
                    (0, x_all, dgu_all, i * 2 * ff, 2),
                    (2 * ff, cot_all, a_all, i * ff, 1),
                ):
                    rows = source[:, :, rows_at].reshape(blocks * tokens, 2 * half_rows)

                    @pl.loop(0, count)
                    def _(n):
                        column = pl.multiple_of(n * ff, ff)
                        part = grad[:, :, pl.ds(pl.multiple_of(start + column, ff), ff)]
                        result = dot_tn(rows, part.reshape(blocks * tokens, ff)).astype(BF16)
                        stage[lax.rem(k, 2), :, :, pl.ds(pl.multiple_of(first + column, ff), ff)] = (
                            result.reshape(2, half_rows, ff)
                        )

                if i:

                    @pl.when(k == 0)
                    def _():
                        pl.semaphore_wait(credits.at[3], 1)

                hand(i, k).start()

                @pl.when(k >= 1)
                def _():
                    settle(i, k - 1)

                between(k)

        for copy in loads[:3]:
            copy.wait()
        gather_cot.complete()
        loads[5].start()
        for copy in loads[3:5]:
            copy.wait()

        @pl.loop(0, EXP_DEV)
        def _(i):
            hidden_units(0, i)

        gather.forward()
        outputs(0)
        loads[5].wait()
        gather.near(1)
        gather.near(2)
        hidden_units(1, 0, 2)
        gather.far()
        hidden_units(3, 0)
        weight_grads(0)
        hidden_units(1, 1, 2)
        clear(0, nc - 2)
        leave(0, 1)
        settle(0, nc - 1)
        pl.semaphore_signal(credits.at[3], inc=1, device_id=sibling, device_id_type=MESH)
        y_copy(0).wait()
        outputs(1, 2)
        scatter_dx.near(1)
        scatter_dx.near(2)
        hidden_units(3, 1)
        expert.relay_begin(0)
        y_copy(1).wait()
        outputs(3)
        scatter_dx.far()
        clear(0, nc - 1)
        expert.relay_add()

        def between(k):
            @pl.when(k == 0)
            def _():
                expert.relay_send(0)

            @pl.when(k == 1)
            def _():
                scatter_dx.relay()

        weight_grads(1, between)
        scatter_dx.total(d_in_ref)
        for r in (1, 2):
            pl.semaphore_signal(credits.at[r], inc=1, device_id=ids[r], device_id_type=MESH)
        settle(1, nc - 1)
        for k in (nc - 2, nc - 1):
            clear(1, k)
        leave(1, 1)
        y_copy(3).wait()
        y_copy(2).wait()
        wire_1.finish()
        wire_c.finish()
        pl.semaphore_signal(credits.at[0], inc=1, device_id=sibling, device_id_type=MESH)

    def token_rows_phase(
        weight,
        grads_o,
        grads_q,
        x_ref,
        inputs_ref,
        query_ref,
        heads_ref,
        hidden_ref,
        d_hidden_ref,
        d_attn_ref,
        d_heads_ref,
        d_all_ref,
        rows_ref,
        dkv_acc,
        dkv_ref,
        y_relay,
        ins,
        out_wide,
    ):
        expert.ins, expert.out = ins, out_wide
        cot_ref, d_inputs_ref = d_heads_ref, hidden_ref
        scatter_y.part = lambda r, half: y_hbm.at[r, :, pl.ds(half * width // 2, width // 2)]
        y_loads = [
            pltpu.make_async_copy(scatter_y.part(2 - half, half), y_relay.at[half], y_sems.at[half])
            for half in range(2)
        ]
        for copy in y_loads:
            copy.start()
        planes = grads_o.shape[1]
        part = width // planes
        sources = (
            (hidden_hbm, hidden_ref),
            (d_out_hbm, cot_ref),
            (wo_hbm, weight),
            (heads_hbm, heads_ref),
            (query_hbm, query_ref),
            (x_hbm, x_ref),
            (inputs_hbm, inputs_ref),
        )
        loads = [
            pltpu.make_async_copy(source, dest, load_sems.at[4 + n])
            for n, (source, dest) in enumerate(sources)
        ]
        for copy in loads:
            copy.start()
        for r in (1, 2):
            scatter_y.near(r)
        scatter_y.far()

        def rows_scatter(buf, core, plane, lines, start, count, half):
            return RowsScatter(
                wire_2,
                buf,
                core,
                plane,
                [lines.at[0], lines.at[1]],
                e,
                z,
                c,
                nc,
                start,
                count,
                half,
            )

        rows_of = part // 2
        scatter_o = rows_scatter(
            grads_o,
            x_all.at[:, pl.ds(0, rows_of)],
            lambda slot, half: dx_land.at[slot, pl.ds(0, rows_of)],
            lines_o,
            0,
            width,
            width // 2,
        )
        scatter_q = rows_scatter(
            grads_q,
            core_land.at[:, :, pl.ds(0, query_width)],
            lambda slot, half: plane_q.at[slot],
            lines_q,
            0,
            query_width,
            query_width // 2,
        )
        rest_half = rest // 256 * 128
        scatter_k = rows_scatter(
            grads_q,
            core_land.at[:, :, pl.ds(query_width, rest)],
            lambda slot, half: plane_k.at[
                slot, :, pl.ds(0, rest - rest_half if half else rest_half)
            ],
            lines_k,
            query_width,
            rest,
            rest_half,
        )
        scatter_kv = [
            LineScatter(
                wire_2,
                lambda j, h=h: dkv_ref.at[h, j],
                [dkv_land.at[h], dkv_land.at[h]],
                z,
                nc,
                up=False,
            )
            for h in range(KEY_VALUE_HEADS)
        ]

        loads[0].wait()
        loads[1].wait()
        hidden, d_in = hidden_ref[...], d_in_ref[...]
        scale2 = lax.rsqrt(jnp.mean(hidden * hidden, -1, keepdims=True) + EPSILON)
        scaled = d_in * gains_ref[1:2]
        mean = jnp.mean(scaled * hidden, -1, keepdims=True)
        d_hidden = cot_ref[...].astype(F32) + scale2 * scaled
        d_hidden = d_hidden - hidden * (scale2 * scale2 * scale2 * mean)
        d_hidden_ref[...] = d_hidden
        d_attn_ref[...] = d_hidden.astype(BF16)
        rows_ref[...] = jnp.zeros_like(rows_ref)
        rows_ref[experts + 1 : experts + 2, :] = jnp.sum(d_in * hidden * scale2, 0, keepdims=True)

        loads[2].wait()

        @pl.loop(0, query_width // 256)
        def _(n):
            columns = pl.ds(pl.multiple_of(n * 256, 256), 256)
            out = weight[:, :, :, :, columns].reshape(width, 256)
            d_heads_ref[:, columns] = dot_nn(d_attn_ref[...], out).astype(BF16)

        load_q = pltpu.make_async_copy(wq_hbm, weight, load_sems.at[0])
        load_q.start()
        loads[3].wait()

        def row_grads(buf, left, right, first, count, extra=None):
            @pl.loop(0, planes)
            def _(block):
                columns = pl.ds(pl.multiple_of(block * part, part), part)
                result = dot_tn(left[:, columns], right)
                if extra is not None:
                    result = result + extra(columns)
                result = result.astype(BF16).reshape(nc, 2, part // nc // 2, count)
                for half in range(2):
                    buf[half, block, :, pl.ds(first, count)] = result[:, half].reshape(
                        part // 2, count
                    )

        row_grads(grads_o, d_attn_ref, heads_ref[...], 0, width)
        pl.semaphore_wait(credits.at[0], 1)
        scatter_o.share()
        y_own = pltpu.make_async_copy(y_hbm.at[0], heads_ref, load_sems.at[2])
        y_own.start()

        length = nc * tokens
        group = QUERY_HEADS // KEY_VALUE_HEADS
        loads[4].wait()
        dkv_acc[...] = jnp.zeros_like(dkv_acc)

        def attend(j, first, last):
            key = kv_ref[j, :, :, pl.ds(0, size)].reshape(length, size)
            value = kv_ref[j, :, :, pl.ds(size, size)].reshape(length, size)

            @pl.loop(j * group + first, j * group + last)
            def _(h):
                columns = pl.ds(pl.multiple_of(h * size, size), size)
                query, grad = query_ref[:, columns], d_heads_ref[:, columns]
                probs = masked_probs(z * tokens, query, key)
                d_probs = dot_nt(grad, value)
                inner = jnp.sum(probs * d_probs, axis=-1, keepdims=True)
                d_raw = (probs * (d_probs - inner) * (size**-0.5)).astype(BF16)
                d_query = dot_nn(d_raw, key)
                d_query = d_query * cos_ref[...] - swap_halves(d_query) * sin_ref[...]
                d_all_ref[:, columns] = d_query.astype(BF16)
                dkv_acc[j, :, pl.ds(0, size)] += dot_tn(d_raw, query)
                dkv_acc[j, :, pl.ds(size, size)] += dot_tn(probs.astype(BF16), grad)

        def round_kv(j):
            for block in range(nc):
                rows = dkv_acc[j, pl.ds(block * tokens, tokens), :]
                dkv_ref[j, block] = rows.astype(BF16)

        def enter():
            pl.semaphore_wait(credits.at[1], 1)
            pl.semaphore_wait(credits.at[2], 1)

        attend(0, 0, group)
        round_kv(0)
        scatter_kv[0].step(1)
        scatter_o.merge(enter)
        for copy in y_loads:
            copy.wait()
        scatter_y.relay(lambda r, half: y_relay.at[half])
        attend(1, 0, group // 2)
        scatter_kv[0].step(2)
        attend(1, group // 2, group)
        round_kv(1)
        scatter_kv[1].step(1)
        for r in (2, 1):
            expert.send(1, r, when=z == nc - 1)
        scatter_kv[0].step(3)
        scatter_o.relay()

        for copy in loads[5:]:
            copy.wait()
        row_grads(grads_q, inputs_ref, d_all_ref[:, pl.ds(0, query_width)], 0, query_width)
        scatter_q.share()
        scatter_kv[1].step(2)
        scatter_kv[1].step(3)
        expert.send(1, 1, when=z == 1)
        expert.relay_begin(1)
        y_own.wait()
        hidden_ref[...] += heads_ref[...].astype(F32)
        scatter_y.total(hidden_ref)
        heads_ref[...] = hidden_ref[...].astype(BF16)
        layer_out = pltpu.make_async_copy(heads_ref, layer_hbm, out_sems.at[0])
        layer_out.start()
        scatter_o.total()
        scatter_q.merge()
        for h in range(KEY_VALUE_HEADS):
            scatter_kv[h].last()
        expert.relay_add()
        expert.relay_send(1)

        for h in range(KEY_VALUE_HEADS):
            grad = dkv_ref[h, z, :, pl.ds(0, size)].astype(F32)
            grad = grad * cos_ref[...] - swap_halves(grad) * sin_ref[...]
            d_all_ref[:, pl.ds(query_width + h * size, size)] = grad.astype(BF16)
            d_all_ref[:, pl.ds(query_width + key_width + h * size, size)] = dkv_ref[
                h, z, :, pl.ds(size, size)
            ]

        total = dg_part[0]
        for r in (1, 2, 3):
            wire_1.arrived(dg_land.at[r - 1], dg_slot + r - 1, ids[r])
            total = total + dg_land[r - 1]
        gates = gate_all[0]
        d_logits = gates * (total - jnp.sum(gates * total, 0, keepdims=True))
        d_logits = jnp.concatenate(
            [d_logits, jnp.zeros((SMALL - d_logits.shape[0], tokens), F32)], 0
        )
        d_all_ref[:, pl.ds(qkv_width, SMALL)] = jnp.transpose(d_logits).astype(BF16)

        load_q.wait()

        @pl.loop(0, planes)
        def _(block):
            columns = pl.ds(pl.multiple_of(block * part, part), part)
            rows_q = weight[block].reshape(part, query_width)
            rows_k = wk_all[block].reshape(part, rest)
            d_inputs_ref[:, columns] = dot_nt(
                d_all_ref[:, pl.ds(0, query_width)], rows_q
            ) + dot_nt(d_all_ref[:, pl.ds(query_width, rest)], rows_k)

        rows = x_ref[...].astype(F32)
        scale1 = lax.rsqrt(jnp.mean(rows * rows, -1, keepdims=True) + EPSILON)
        d_inputs = d_inputs_ref[...]
        rows_ref[experts : experts + 1, :] = jnp.sum(d_inputs * rows * scale1, 0, keepdims=True)

        def extra(columns):
            small = jnp.transpose(rows_ref[:, columns])
            return jnp.concatenate([jnp.zeros((part, rest - SMALL), F32), small], 1)

        row_grads(
            grads_q, inputs_ref, d_all_ref[:, pl.ds(query_width, rest)], query_width, rest, extra
        )
        scatter_k.share()
        scatter_q.relay()
        scatter_k.merge()
        scaled = d_inputs_ref[...] * gains_ref[0:1]
        rows = x_ref[...].astype(F32)
        scale1 = lax.rsqrt(jnp.mean(rows * rows, -1, keepdims=True) + EPSILON)
        mean = jnp.mean(scaled * rows, -1, keepdims=True)
        d_x = d_hidden_ref[...] + scale1 * scaled - rows * (scale1 * scale1 * scale1 * mean)
        inputs_ref[...] = d_x.astype(BF16)
        d_x_out = pltpu.make_async_copy(inputs_ref, d_x_hbm, out_sems.at[1])
        d_x_out.start()
        scatter_q.total()
        expert.last(0, (sum_gu_hbm, sum_dn_hbm))
        scatter_k.relay()
        scatter_o.line.step(1)
        scatter_q.line.step(1)
        scatter_k.total()
        scatter_k.line.step(1)
        for s in range(2, nc):
            for scatter in (scatter_o, scatter_q, scatter_k):
                scatter.line.step(s)
        for scatter in (scatter_o, scatter_q, scatter_k):
            scatter.line.last()
        sum_o_ref[...] = scatter_o.line.block(z)[...].astype(F32)
        sum_q_ref[...] = grads_q[c, e, pl.ds(pl.multiple_of(z * (rows_of // nc), rows_of // nc), rows_of // nc)].astype(F32)
        expert.last(1, (sum_gu_hbm, sum_dn_hbm))
        layer_out.wait()
        d_x_out.wait()
        wire_2.finish()
        expert.finish()

    held = EXP_DEV
    weight_shape = wq_hbm.shape
    pl.run_scoped(
        front_phase,
        pltpu.VMEM(weight_shape, BF16),
        pltpu.VMEM(weight_shape, BF16),
        pltpu.VMEM((tokens, width), BF16),
        pltpu.VMEM((tokens, width), BF16),
        pltpu.VMEM((tokens, query_width), BF16),
        pltpu.VMEM((tokens, query_width), BF16),
        pltpu.VMEM((tokens, width), F32),
        pltpu.VMEM((tokens, rest), F32),
        pltpu.VMEM((tokens, query_width), F32),
    )
    shard, step = width // nc // 2, 48
    pl.run_scoped(
        token_phase,
        pltpu.VMEM((held, width, 2 * ff), BF16),
        pltpu.VMEM((held, ff, width), BF16),
        pltpu.VMEM((blocks, tokens, width), BF16),
        pltpu.VMEM((blocks, tokens, held * ff), BF16),
        pltpu.VMEM((blocks, tokens, held * 2 * ff), BF16),
        pltpu.VMEM((2, tokens, width), BF16),
        pltpu.VMEM((blocks - 1, tokens, width), BF16),
        pltpu.VMEM((2, 2, shard, grad_width // held), BF16),
        pltpu.VMEM((2, shard // step, step, grad_width // held), BF16),
    )
    rows_half = width // blocks // 2
    pl.run_scoped(
        token_rows_phase,
        pltpu.VMEM(weight_shape, BF16),
        pltpu.VMEM((2, blocks, rows_half, width), BF16),
        pltpu.VMEM((2, blocks, rows_half, qkv_width + SMALL), BF16),
        pltpu.VMEM((tokens, width), BF16),
        pltpu.VMEM((tokens, width), BF16),
        pltpu.VMEM((tokens, query_width), BF16),
        pltpu.VMEM((tokens, query_width), BF16),
        pltpu.VMEM((tokens, width), F32),
        pltpu.VMEM((tokens, width), F32),
        pltpu.VMEM((tokens, width), BF16),
        pltpu.VMEM((tokens, query_width), BF16),
        pltpu.VMEM((tokens, qkv_width + SMALL), BF16),
        pltpu.VMEM((SMALL, width), F32),
        pltpu.VMEM((KEY_VALUE_HEADS, nc * tokens, 2 * size), F32),
        pltpu.VMEM((KEY_VALUE_HEADS, nc, tokens, 2 * size), BF16),
        pltpu.VMEM((2, tokens, width // 2), BF16),
        pltpu.VMEM((4, shard // step, step, grad_width // held), BF16),
        pltpu.VMEM((2, step, grad_width // held), F32),
    )


def layer(operands, sizes):
    ne, nc, nd = sizes
    qkv_shard, x = operands[3], operands[6]
    w_dn = operands[9]
    tokens, width = x.shape
    held, ff = w_dn.shape[0], w_dn.shape[1]
    query_width = QUERY_HEADS * HEAD_DIMENSION
    rows, qkv_width = qkv_shard.shape
    rest = qkv_width - query_width + SMALL
    rest_half = rest // 256 * 128
    shard, grads = width // (nc * nd), held * 3 * ff
    kv_size = 2 * HEAD_DIMENSION
    weight = (ne, nc, nd, rows, query_width)
    shapes = [
        ((tokens, width), BF16),
        ((tokens, width), BF16),
        ((rows, qkv_width + SMALL), F32),
        ((rows, width), F32),
        ((held, shard, 2 * ff), F32),
        ((held, shard, ff), F32),
        ((nc, shard, grads), BF16),
        ((nc + 1, shard, grads), BF16),
        ((ne, tokens, width), BF16),
        (weight, BF16),
        (weight, BF16),
        ((ne, tokens, width), BF16),
        ((tokens, width), BF16),
        ((tokens, query_width), BF16),
        ((tokens, query_width), BF16),
        ((tokens, width), F32),
    ]
    vmem = pl.BlockSpec(memory_space=pltpu.VMEM)
    anywhere = pl.BlockSpec(memory_space=pl.ANY)
    units = nc * held
    sems = [120, 110, 6, 6, 16, 16, 64, 64, 2 * units, (nc + 1) * held, units, units, 2, 12, 4]
    return pl.pallas_call(
        functools.partial(layer_kernel, nc, EXP_DEV * ne),
        out_shape=[jax.ShapeDtypeStruct(*s) for s in shapes],
        in_specs=[vmem] * 6 + [anywhere] * (len(operands) - 6),
        out_specs=[anywhere] * 2 + [vmem] * 2 + [anywhere] * (len(shapes) - 4),
        scratch_shapes=[
            pltpu.VMEM((ne, nc, nd, rows, rest), BF16),
            pltpu.VMEM((KEY_VALUE_HEADS, nc, tokens, kv_size), BF16),
            pltpu.VMEM((ne, GATE_ROWS, tokens), F32),
            pltpu.VMEM((ne, tokens, SMALL), F32),
            pltpu.VMEM((8, width), F32),
            pltpu.VMEM((ne, tokens, width), BF16),
            pltpu.VMEM((6, tokens, width // 2), BF16),
            pltpu.VMEM((6, tokens, width // 2), BF16),
            pltpu.VMEM((nc, shard, grads // held), BF16),
            pltpu.VMEM((6, nc * rows, query_width // 2), BF16),
            pltpu.VMEM((6, nc * rows, rest - rest_half), BF16),
            pltpu.VMEM((2, nc - 1, rows, width), BF16),
            pltpu.VMEM((2, nc - 1, rows, query_width), BF16),
            pltpu.VMEM((2, nc - 1, rows, rest), BF16),
            pltpu.VMEM((KEY_VALUE_HEADS, nc - 1, tokens, kv_size), BF16),
            pltpu.VMEM((tokens, width), F32),
            pltpu.VMEM((ne, tokens, SMALL), F32),
            pltpu.VMEM((ne, GATE_ROWS, tokens), F32),
            pltpu.VMEM((ne - 1, GATE_ROWS, tokens), F32),
        ]
        + [pltpu.SemaphoreType.DMA((count,)) for count in sems]
        + [
            pltpu.SemaphoreType.DMA((2, 2 * nc)),
            pltpu.SemaphoreType.DMA((20,)),
            pltpu.SemaphoreType.DMA((2,)),
            pltpu.SemaphoreType.REGULAR((4,)),
        ],
        compiler_params=pltpu.CompilerParams(
            collective_id=0, has_side_effects=True, vmem_limit_bytes=63 * MIB
        ),
    )(*operands)


def finish_kernel(experts, *refs):
    sources, dests = refs[:6], refs[6:12]
    router_ref, gains_ref = refs[12:]
    sum_q = sources[0]
    qkv_width = dests[0].shape[-1]
    dests[0][...] = sum_q[:, pl.ds(0, qkv_width)]
    for source, dest in zip(sources[1:], dests[1:]):
        dest[...] = source[...]
    small = sum_q[:, pl.ds(qkv_width, SMALL)]
    rows = small.shape[0]
    filled = jnp.concatenate([small, jnp.zeros((SMALL - rows, SMALL), F32)], 0)
    turned = jnp.transpose(filled)[:, :rows]
    router_ref[...] = turned[:experts]
    gains_ref[...] = turned[experts : experts + 2]


def finish(sum_q, others, experts):
    rows, q_width = sum_q.shape
    vmem = pl.BlockSpec(memory_space=pltpu.VMEM)
    shapes = [jax.ShapeDtypeStruct((rows, q_width - SMALL), F32)]
    shapes += [jax.ShapeDtypeStruct(o.shape, o.dtype) for o in others]
    shapes += [jax.ShapeDtypeStruct((experts, rows), F32), jax.ShapeDtypeStruct((2, rows), F32)]
    return pl.pallas_call(
        functools.partial(finish_kernel, experts),
        out_shape=shapes,
        in_specs=[vmem] * 6,
        out_specs=[vmem] * 8,
        compiler_params=pltpu.CompilerParams(vmem_limit_bytes=60 * MIB),
    )(sum_q, *others)


def local_plain(
    layer_input,
    gain_attn,
    query_key_value_weight,
    w_out,
    w_router,
    gain_ffn,
    w_gate_up,
    w_down,
    routes,
    d_out,
):
    tokens = layer_input.shape[1]
    model_width = layer_input.shape[2]
    ne, nc, nd = (lax.axis_size(a) for a in ("expert", "context", "dp"))
    expert_total = EXP_DEV * ne
    ff = w_down.shape[1]
    me = lax.axis_index("expert")
    first_row = lax.axis_index("context") * tokens
    query_width = QUERY_HEADS * HEAD_DIMENSION
    key_width = KEY_VALUE_HEADS * HEAD_DIMENSION
    qkv_width = query_width + 2 * key_width

    small = jnp.concatenate([w_router, gain_attn[:, None], gain_ffn[:, None]], -1)
    small = jnp.pad(small, ((0, 0), (0, 128 - small.shape[1])))
    gathered = gather_rows(jnp.concatenate([query_key_value_weight, small], -1))
    out_turned = gather_rows(w_out.T)
    qkv_weight = gathered[:, :qkv_width]
    router_weight = gathered[:, qkv_width : qkv_width + expert_total]
    gains = gathered[:, qkv_width + expert_total : qkv_width + expert_total + 2].T.astype(F32)
    gain_first, gain_second = gains[0], gains[1]
    cotangent_all = plane_gather(d_out[0])

    token_rows = layer_input[0].astype(F32)
    scale1 = lax.rsqrt(jnp.mean(token_rows * token_rows, -1, keepdims=True) + EPSILON)
    inputs1 = (token_rows * scale1 * gain_first).astype(BF16)
    query_key_value = dot_nn(inputs1, qkv_weight)
    cosine_values, sine_values = rope_tables(first_row + jnp.arange(tokens), HEAD_DIMENSION)
    rotated = rotate_half(
        query_key_value[:, : query_width + key_width].reshape(tokens, -1, HEAD_DIMENSION),
        cosine_values,
        sine_values,
    ).reshape(tokens, -1)
    query = rotated[:, :query_width].astype(BF16)
    key_value_local = jnp.concatenate(
        [rotated[:, query_width:], query_key_value[:, query_width + key_width :]], -1
    ).astype(BF16)
    key_value = line_gather(key_value_local, "context", both=False).reshape(nc * tokens, -1)
    first = first_row.astype(jnp.int32).reshape(1)
    heads = attend_forward(first, query, key_value)

    logits = dot_nn(inputs1, router_weight)
    chosen_ids = routes[0]
    picks = (chosen_ids[:, :, None] == jnp.arange(expert_total)[None, None, :]).astype(F32)
    chosen = jnp.sum(picks * logits[:, None, :], -1)
    gates = jax.nn.softmax(chosen, axis=-1)
    gate_dense = jnp.sum(picks * gates[:, :, None], 1).T
    gate_blocks = cube_gather(gate_dense, "expert", axis_masks("expert"))
    gate_local = jnp.concatenate(
        [lax.dynamic_slice_in_dim(b, me * EXP_DEV, EXP_DEV, 0) for b in gate_blocks], 1
    )

    attn = dot_nt(heads, out_turned)
    hidden = token_rows + attn
    scale2 = lax.rsqrt(jnp.mean(hidden * hidden, -1, keepdims=True) + EPSILON)
    expert_in = (hidden * scale2 * gain_second).astype(BF16)

    rows_all = plane_gather(expert_in)
    gate_up = jnp.einsum("td,edf->etf", rows_all, w_gate_up, preferred_element_type=F32)
    gate_part, up_part = gate_up[..., :ff], gate_up[..., ff:]
    sigma = jax.nn.sigmoid(gate_part)
    silu = gate_part * sigma
    act = silu * up_part
    gate_column = gate_local[:, :, None]
    act_gated = (act * gate_column).astype(BF16)
    partial_out = jnp.einsum("etf,efd->td", act_gated, w_down, preferred_element_type=F32)
    mixture = plane_scatter(partial_out.astype(BF16), tokens)
    layer_result = (hidden + mixture).astype(BF16)

    d_act_raw = jnp.einsum("td,efd->etf", cotangent_all, w_down, preferred_element_type=F32)
    d_gates_local = jnp.sum(d_act_raw * act, -1)
    d_act = d_act_raw * gate_column
    d_gate_part = d_act * up_part * sigma * (1.0 + gate_part * (1.0 - sigma))
    d_up_part = d_act * silu
    d_gate_up = jnp.concatenate([d_gate_part, d_up_part], -1).astype(BF16)
    d_rows = jnp.einsum("etf,edf->td", d_gate_up, w_gate_up, preferred_element_type=F32)
    grad_down = jnp.einsum("td,etf->edf", cotangent_all, act_gated, preferred_element_type=F32)
    grad_gate_up = jnp.einsum("td,etf->edf", rows_all, d_gate_up, preferred_element_type=F32)

    d_expert_in = plane_scatter(d_rows.astype(BF16), tokens)
    d_gate_blocks = d_gates_local.reshape(EXP_DEV, ne, tokens)
    d_gates_dense = jnp.zeros((expert_total, tokens), F32)
    for r in range(ne):
        arrived = d_gate_blocks[:, r]
        if r:
            arrived = exchange(arrived, "expert", r)
        d_gates_dense = lax.dynamic_update_slice(d_gates_dense, arrived, ((me ^ r) * EXP_DEV, 0))
    d_gates = jnp.sum(picks * d_gates_dense.T[:, None, :], -1)
    d_chosen = gates * (d_gates - jnp.sum(gates * d_gates, -1, keepdims=True))
    d_logits = jnp.sum(picks * d_chosen[:, :, None], 1).astype(BF16)
    grad_router = dot_tn(inputs1, d_logits)

    core = lax.axis_index("dp")
    part = model_width // (nc * nd)

    def scatter_experts(grad):
        blocks = grad.reshape(EXP_DEV, nc, nd, part, -1)
        mine = cube_scatter(
            [lax.dynamic_index_in_dim(blocks, core ^ r, 2, keepdims=False) for r in range(nd)],
            "dp",
            axis_masks("dp"),
        )
        return line_scatter(
            lambda j: lax.dynamic_index_in_dim(mine, j, 1, keepdims=False), "context"
        )

    sum_gate_up = scatter_experts(grad_gate_up)
    sum_down = jnp.swapaxes(scatter_experts(grad_down), 1, 2)

    cotangent = d_out[0].astype(F32)
    scaled2 = d_expert_in * gain_second
    d_hidden = (
        cotangent
        + scale2 * scaled2
        - hidden * (scale2 * scale2 * scale2) * jnp.mean(scaled2 * hidden, -1, keepdims=True)
    )
    grad_gain_second = jnp.sum(d_expert_in * hidden * scale2, 0)
    d_attn = d_hidden.astype(BF16)
    grad_out_turned = dot_tn(d_attn, heads)
    sum_out = scatter_rows(grad_out_turned).T
    d_heads = dot_nn(d_attn, out_turned).astype(BF16)
    d_query, d_key_all, d_value_all = attend_backward(first, query, key_value, d_heads)
    d_key_value_all = jnp.concatenate([d_key_all, d_value_all], -1).reshape(nc, tokens, -1)
    d_key_value = line_scatter(
        lambda j: lax.dynamic_index_in_dim(d_key_value_all, j, 0, keepdims=False),
        "context",
        up=False,
    )
    d_rotated = rotate_back(
        jnp.concatenate([d_query, d_key_value[:, :key_width]], -1).reshape(
            tokens, -1, HEAD_DIMENSION
        ),
        cosine_values,
        sine_values,
    ).reshape(tokens, -1)
    d_qkv = jnp.concatenate([d_rotated, d_key_value[:, key_width:]], -1).astype(BF16)
    d_inputs = dot_nt(d_qkv, qkv_weight) + dot_nt(d_logits, router_weight)
    grad_gain_first = jnp.sum(d_inputs * token_rows * scale1, 0)
    grad_qkv = dot_tn(inputs1, d_qkv)
    small_grads = jnp.concatenate(
        [grad_router, grad_gain_first[:, None], grad_gain_second[:, None]], -1
    )
    small_grads = jnp.pad(small_grads, ((0, 0), (0, 128 - small_grads.shape[1])))
    sum_rows = scatter_rows(jnp.concatenate([grad_qkv, small_grads], -1))
    sum_qkv = sum_rows[:, :qkv_width]
    sum_router = sum_rows[:, qkv_width : qkv_width + expert_total]
    sum_gain_first = sum_rows[:, qkv_width + expert_total]
    sum_gain_second = sum_rows[:, qkv_width + expert_total + 1]
    scaled1 = d_inputs * gain_first
    d_input_rows = (
        d_hidden
        + scale1 * scaled1
        - token_rows
        * (scale1 * scale1 * scale1)
        * jnp.mean(scaled1 * token_rows, -1, keepdims=True)
    ).astype(BF16)
    return (
        layer_result[None],
        d_input_rows[None],
        sum_gain_first,
        sum_qkv,
        sum_out,
        sum_router,
        sum_gain_second,
        sum_gate_up,
        sum_down,
    )


def local_fused(
    layer_input,
    gain_attn,
    query_key_value_weight,
    w_out,
    w_router,
    gain_ffn,
    w_gate_up,
    w_down,
    routes,
    d_out,
):
    tokens = layer_input.shape[1]
    ne, nc, nd = sizes = tuple(lax.axis_size(a) for a in ("expert", "context", "dp"))
    expert_total = EXP_DEV * ne
    first_row = lax.axis_index("context") * tokens
    query_width = QUERY_HEADS * HEAD_DIMENSION
    key_width = KEY_VALUE_HEADS * HEAD_DIMENSION
    qkv_width = query_width + 2 * key_width

    small = jnp.concatenate([w_router, gain_attn[:, None], gain_ffn[:, None]], -1)
    small = jnp.pad(small, ((0, 0), (0, SMALL - small.shape[1])))
    cosine_values, sine_values = rope_tables(first_row + jnp.arange(tokens), HEAD_DIMENSION)
    sine_values = sine_values * jnp.where(
        jnp.arange(HEAD_DIMENSION) < HEAD_DIMENSION // 2, -1.0, 1.0
    )
    layer_result, d_x, sum_rows, sum_out, sum_gate_up, sum_down = layer(
        (
            cosine_values,
            sine_values,
            routes[0].T,
            query_key_value_weight,
            small,
            w_out.T,
            layer_input[0],
            d_out[0],
            w_gate_up,
            w_down,
        ),
        sizes,
    )[:6]
    sum_qkv, layer_result, d_x, sum_gate_up, sum_down, sum_out, sum_router, sum_gains = finish(
        sum_rows, (layer_result, d_x, sum_gate_up, sum_down, sum_out), expert_total
    )
    return (
        layer_result[None],
        d_x[None],
        sum_gains[0],
        sum_qkv,
        sum_out.T,
        sum_router.T,
        sum_gains[1],
        sum_gate_up,
        jnp.swapaxes(sum_down, 1, 2),
    )


def solution(mesh):
    in_specs = (
        P(("expert", "dp"), "context", None),
        P(("expert", "context", "dp")),
        P(("expert", "context", "dp"), None),
        P(None, ("expert", "context", "dp")),
        P(("expert", "context", "dp"), None),
        P(("expert", "context", "dp")),
        P("expert", None, None),
        P("expert", None, None),
        P(("expert", "dp"), "context", None),
        P(("expert", "dp"), "context", None),
    )
    out_specs = (
        P(("expert", "dp"), "context", None),
        P(("expert", "dp"), "context", None),
        P(("expert", "context", "dp")),
        P(("expert", "context", "dp"), None),
        P(None, ("expert", "context", "dp")),
        P(("expert", "context", "dp"), None),
        P(("expert", "context", "dp")),
        P("expert", ("context", "dp"), None),
        P("expert", None, ("context", "dp")),
    )
    sizes = tuple(mesh.shape[a] for a in ("expert", "context", "dp"))
    local = local_fused if sizes == (4, 4, 2) else local_plain
    return jax.shard_map(local, mesh=mesh, in_specs=in_specs, out_specs=out_specs, check_vma=False)
```

```python
import functools
import math

import jax
import jax.numpy as jnp
from jax import lax
from jax.experimental import pallas as pl
from jax.experimental.pallas import tpu as pltpu
from jax.sharding import PartitionSpec as P

QUERY_HEADS = 12
KEY_VALUE_HEADS = 2
HEAD_DIMENSION = 128
TOP = 4
EXP_DEV = 2

EPSILON = 1e-06
ROPE_BASE = 10000.0
MASKED = -1e30

F32 = jnp.float32
BF16 = jnp.bfloat16


def rope_tables(positions, width):
    halfway = width // 2
    fraction = jnp.arange(halfway, dtype=jnp.float32) * (2.0 / width)
    frequency = jnp.exp(-math.log(ROPE_BASE) * fraction)
    angles = positions.astype(jnp.float32)[:, None] * frequency[None, :]
    cosine_values = jnp.cos(angles)
    sine_values = jnp.sin(angles)
    return (
        jnp.concatenate([cosine_values, cosine_values], -1),
        jnp.concatenate([sine_values, sine_values], -1),
    )


def rotate_half(values, cosine_values, sine_values):
    halfway = values.shape[-1] // 2
    turned = jnp.concatenate([-values[..., halfway:], values[..., :halfway]], -1)
    return values * cosine_values[:, None, :] + turned * sine_values[:, None, :]


def rotate_back(grads, cosine_values, sine_values):
    halfway = grads.shape[-1] // 2
    scaled = grads * sine_values[:, None, :]
    turned = jnp.concatenate([scaled[..., halfway:], -scaled[..., :halfway]], -1)
    return grads * cosine_values[:, None, :] + turned


def dot_nt(a, b):
    return lax.dot_general(a, b, (((1,), (1,)), ((), ())), preferred_element_type=F32)


def dot_tn(a, b):
    return lax.dot_general(a, b, (((0,), (0,)), ((), ())), preferred_element_type=F32)


def dot_nn(a, b):
    return jnp.dot(a, b, preferred_element_type=F32)


def masked_probs(first_row, query, key):
    scores = dot_nt(query, key) * (HEAD_DIMENSION**-0.5)
    rows = first_row + lax.broadcasted_iota(jnp.int32, scores.shape, 0)
    columns = lax.broadcasted_iota(jnp.int32, scores.shape, 1)
    scores = jnp.where(columns <= rows, scores, MASKED)
    expd = jnp.exp(scores - jnp.max(scores, axis=-1, keepdims=True))
    return expd / jnp.sum(expd, axis=-1, keepdims=True)


def attend_forward_kernel(first_ref, query_ref, key_ref, value_ref, heads_ref):
    probs = masked_probs(first_ref[0], query_ref[...], key_ref[...])
    heads_ref[...] = dot_nn(probs.astype(BF16), value_ref[...]).astype(BF16)


def attend_forward(first_row, query, key_value):
    tokens, width = query.shape
    length = key_value.shape[0]
    group = QUERY_HEADS // KEY_VALUE_HEADS
    size = HEAD_DIMENSION
    return pl.pallas_call(
        attend_forward_kernel,
        grid_spec=pltpu.PrefetchScalarGridSpec(
            num_scalar_prefetch=1,
            grid=(QUERY_HEADS,),
            in_specs=[
                pl.BlockSpec((tokens, size), lambda h, s: (0, h)),
                pl.BlockSpec((length, size), lambda h, s: (0, h // group)),
                pl.BlockSpec((length, size), lambda h, s: (0, KEY_VALUE_HEADS + h // group)),
            ],
            out_specs=pl.BlockSpec((tokens, size), lambda h, s: (0, h)),
        ),
        out_shape=jax.ShapeDtypeStruct((tokens, width), BF16),
        compiler_params=pltpu.CompilerParams(vmem_limit_bytes=32 * 1024 * 1024),
        cost_estimate=pl.CostEstimate(
            flops=4 * tokens * length * width, bytes_accessed=4 * tokens * width, transcendentals=0
        ),
    )(first_row, query, key_value, key_value)


def attend_backward_kernel(
    first_ref, query_ref, key_ref, value_ref, grad_ref, d_query_ref, d_key_ref, d_value_ref
):
    query, key, value, grad = query_ref[...], key_ref[...], value_ref[...], grad_ref[...]
    probs = masked_probs(first_ref[0], query, key)
    d_probs = dot_nt(grad, value)
    inner = jnp.sum(probs * d_probs, axis=-1, keepdims=True)
    d_raw = (probs * (d_probs - inner) * (HEAD_DIMENSION**-0.5)).astype(BF16)
    d_query_ref[...] = dot_nn(d_raw, key)
    d_key = dot_tn(d_raw, query)
    d_value = dot_tn(probs.astype(BF16), grad)

    @pl.when(pl.program_id(1) == 0)
    def _():
        d_key_ref[...] = d_key
        d_value_ref[...] = d_value

    @pl.when(pl.program_id(1) > 0)
    def _():
        d_key_ref[...] += d_key
        d_value_ref[...] += d_value


def attend_backward(first_row, query, key_value, grad):
    tokens, width = query.shape
    length = key_value.shape[0]
    group = QUERY_HEADS // KEY_VALUE_HEADS
    size = HEAD_DIMENSION
    row_spec = pl.BlockSpec((tokens, size), lambda j, g, s: (0, j * group + g))
    return pl.pallas_call(
        attend_backward_kernel,
        grid_spec=pltpu.PrefetchScalarGridSpec(
            num_scalar_prefetch=1,
            grid=(KEY_VALUE_HEADS, group),
            in_specs=[
                row_spec,
                pl.BlockSpec((length, size), lambda j, g, s: (0, j)),
                pl.BlockSpec((length, size), lambda j, g, s: (0, KEY_VALUE_HEADS + j)),
                row_spec,
            ],
            out_specs=[
                row_spec,
                pl.BlockSpec((length, size), lambda j, g, s: (0, j)),
                pl.BlockSpec((length, size), lambda j, g, s: (0, j)),
            ],
        ),
        out_shape=[
            jax.ShapeDtypeStruct((tokens, width), F32),
            jax.ShapeDtypeStruct((length, KEY_VALUE_HEADS * size), F32),
            jax.ShapeDtypeStruct((length, KEY_VALUE_HEADS * size), F32),
        ],
        compiler_params=pltpu.CompilerParams(vmem_limit_bytes=32 * 1024 * 1024),
        cost_estimate=pl.CostEstimate(
            flops=10 * tokens * length * width, bytes_accessed=8 * tokens * width, transcendentals=0
        ),
    )(first_row, query, key_value, key_value, grad)


def exchange(values, axis, mask):
    size = lax.axis_size(axis)
    return lax.ppermute(values, axis, [(i, i ^ mask) for i in range(size)])


def axis_masks(axis):
    size = lax.axis_size(axis)
    masks, bit = [], 1
    while bit < size:
        masks.append(bit)
        bit *= 2
    return masks


def cube_gather(values, axis, masks):
    held = {0: values}
    for mask in masks:
        for r, block in list(held.items()):
            held[r ^ mask] = exchange(block, axis, mask)
    return [held[r] for r in range(lax.axis_size(axis))]


def cube_scatter(blocks, axis, masks):
    held = dict(enumerate(blocks))
    for mask in masks:
        kept = {}
        for r in list(held):
            if not r & mask:
                arrived = exchange(held[r ^ mask].astype(BF16), axis, mask)
                kept[r] = held[r].astype(F32) + arrived.astype(F32)
        held = kept
    return held[0]


def line_steps(values, axis, up):
    size = lax.axis_size(axis)
    pairs = [(i, i + 1) if up else (i + 1, i) for i in range(size - 1)]
    return lax.ppermute(values, axis, pairs)


def line_gather(values, axis, both=True):
    size = lax.axis_size(axis)
    me = lax.axis_index(axis)
    result = jnp.zeros((size + 1,) + values.shape, values.dtype)
    result = lax.dynamic_update_index_in_dim(result, values, me, 0)
    up = down = values
    for step in range(1, size):
        up = line_steps(up, axis, True)
        result = lax.dynamic_update_index_in_dim(
            result, up, jnp.where(me - step >= 0, me - step, size), 0
        )
        if both:
            down = line_steps(down, axis, False)
            result = lax.dynamic_update_index_in_dim(result, down, jnp.minimum(me + step, size), 0)
    return result[:size]


def line_scatter(take, axis, up=True, down=True):
    size = lax.axis_size(axis)
    me = lax.axis_index(axis)
    total = take(me).astype(F32)
    for active, sign in ((up, 1), (down, -1)):
        if not active:
            continue
        arrived = None
        for step in range(1, size):
            block = take((me + sign * (size - step)) % size).astype(F32)
            if arrived is not None:
                block = block + arrived.astype(F32)
            arrived = line_steps(block.astype(BF16), axis, sign > 0)
        total = total + arrived.astype(F32)
    return total


def gather_rows(shard):
    ne, nc, nd = (lax.axis_size(a) for a in ("expert", "context", "dp"))
    rows, width = shard.shape
    lines = line_gather(shard, "context")
    masks = axis_masks("expert")
    half = width // 256 * 128
    parts = [lines[..., :half], lines[..., half:]]
    me = lax.axis_index("expert")
    result = jnp.zeros((ne, nc, rows, width), shard.dtype)
    for start, part, order in ((0, parts[0], masks), (half, parts[1], masks[::-1])):
        for r, block in enumerate(cube_gather(part, "expert", order)):
            result = lax.dynamic_update_slice(result, block[None], (me ^ r, 0, 0, start))
    core = lax.axis_index("dp")
    whole = jnp.zeros((ne, nc, nd, rows, width), shard.dtype)
    for r, block in enumerate(cube_gather(result, "dp", axis_masks("dp"))):
        whole = lax.dynamic_update_slice(whole, block[:, :, None], (0, 0, core ^ r, 0, 0))
    return whole.reshape(-1, width)


def scatter_rows(grad):
    ne, nc, nd = (lax.axis_size(a) for a in ("expert", "context", "dp"))
    width = grad.shape[-1]
    rows = grad.shape[0] // (ne * nc * nd)
    blocks = grad.reshape(ne, nc, nd, rows, width)
    core, me = lax.axis_index("dp"), lax.axis_index("expert")
    mine = cube_scatter(
        [
            lax.dynamic_index_in_dim(blocks, core ^ r, 2, keepdims=False)
            for r in range(nd)
        ],
        "dp",
        axis_masks("dp"),
    )
    masks = axis_masks("expert")
    half = width // 256 * 128
    sums = []
    for part, order in ((mine[..., :half], masks), (mine[..., half:], masks[::-1])):
        sums.append(
            cube_scatter(
                [lax.dynamic_index_in_dim(part, me ^ r, 0, keepdims=False) for r in range(ne)],
                "expert",
                order,
            )
        )
    lines = jnp.concatenate(sums, -1)
    return line_scatter(
        lambda j: lax.dynamic_index_in_dim(lines, j, 0, keepdims=False), "context"
    )


def plane_gather(rows):
    masks = axis_masks("expert")
    half = rows.shape[-1] // 2
    left = cube_gather(rows[:, :half], "expert", masks)
    right = cube_gather(rows[:, half:], "expert", masks[::-1])
    return jnp.concatenate([jnp.concatenate(p, -1) for p in zip(left, right)], 0)


def plane_scatter(partial, tokens):
    masks = axis_masks("expert")
    size = lax.axis_size("expert")
    half = partial.shape[-1] // 2
    blocks = partial.reshape(size, tokens, -1)
    left = cube_scatter([blocks[r, :, :half] for r in range(size)], "expert", masks)
    right = cube_scatter([blocks[r, :, half:] for r in range(size)], "expert", masks[::-1])
    return jnp.concatenate([left, right], -1)


MESH = pl.DeviceIdType.MESH
MIB = 1024 * 1024
SMALL = 128
GATE_ROWS = 16


def flip(index, mask):
    bit = 1
    while bit <= mask:
        if mask & bit:
            index = index + bit - 2 * bit * lax.rem(lax.div(index, bit), 2)
        bit *= 2
    return index


class Wire:
    def __init__(self, sends, recvs):
        self.sends, self.recvs = sends, recvs
        self.n_sends = self.n_recvs = 0
        self.open = []

    def slots(self, count):
        first = self.n_recvs
        self.n_recvs += count
        return first

    def start(self, src, dst, recv, device, when=None):
        number = self.n_sends
        self.n_sends += 1

        def copy():
            return pltpu.make_async_remote_copy(
                src_ref=src() if callable(src) else src,
                dst_ref=dst() if callable(dst) else dst,
                send_sem=self.sends.at[number],
                recv_sem=self.recvs.at[recv],
                device_id=device,
                device_id_type=MESH,
            )

        guard(when, lambda: copy().start())
        self.open.append((when, copy))

    def arrived(self, dst, recv, device):
        pltpu.make_async_remote_copy(
            src_ref=dst,
            dst_ref=dst,
            send_sem=self.sends.at[0],
            recv_sem=self.recvs.at[recv],
            device_id=device,
            device_id_type=MESH,
        ).wait_recv()

    def finish(self):
        for when, copy in self.open:
            guard(when, lambda copy=copy: copy().wait_send())
        self.open = []


def guard(when, action):
    if when is None:
        action()
    else:
        pl.when(when)(action)


def add_into(dest, source, steps=4):
    rows = dest.shape[0] // steps

    @pl.loop(0, steps)
    def _(n):
        here = pl.ds(pl.multiple_of(n * rows, rows), rows)
        dest[here] = (dest[here].astype(F32) + source[here].astype(F32)).astype(BF16)


def greet(targets):
    barrier = pltpu.get_barrier_semaphore()
    for device, when in targets:
        guard(
            when,
            lambda device=device: pl.semaphore_signal(
                barrier, inc=1, device_id=device, device_id_type=MESH
            ),
        )
    count = sum(1 if when is None else when.astype(jnp.int32) for _, when in targets)
    pl.semaphore_wait(barrier, count)


def plane_ids(e):
    return {m: {"expert": flip(e, m)} for m in (1, 2, 3)}


class RowsGather:
    def __init__(self, wire, ref, e, z, c, nc, half):
        self.wire, self.ref, self.e, self.z, self.c, self.nc = wire, ref, e, z, c, nc
        self.cols = (pl.ds(0, half), pl.ds(half, ref.shape[-1] - half))
        self.line = wire.slots(nc)
        self.plane = wire.slots(nc * 6)
        self.core = wire.slots(nc)
        self.ids = plane_ids(e)

    def go(self, *steps):
        for step in steps:
            action = {"l": self.pass_on, "s": self.spread, "f": self.forward, "h": self.share, "c": self.complete}
            action[step[0]](*map(int, step[1:]))

    def shard(self, k):
        if k < 2:
            return flip(self.z, k)
        inner = (self.z > 0) & (self.z < self.nc - 1)
        return jnp.where(inner, flip(self.z, 5 - k), flip(self.z, k))

    def at(self, r, zs, half):
        return self.ref.at[flip(self.e, r), zs, self.c, :, self.cols[half]]

    def slot(self, k, r, half):
        return self.plane + k * 6 + (r - 1) * 2 + half

    def pass_on(self, k):
        wire, z, nc = self.wire, self.z, self.nc
        zs = self.shard(k)
        whole = self.ref.at[self.e, zs, self.c]
        if k:
            wire.arrived(whole, self.line + zs, {"context": zs})
        wire.start(
            whole, whole, self.line + zs, {"context": z + 1}, when=(zs <= z) & (z < nc - 1)
        )
        wire.start(whole, whole, self.line + zs, {"context": z - 1}, when=(zs >= z) & (z > 0))

    def spread(self, k):
        zs = self.shard(k)
        for half, mask in ((0, 1), (1, 2), (1, 1), (0, 2)):
            part = self.at(0, zs, half)
            self.wire.start(part, part, self.slot(k, mask, half), self.ids[mask])

    def forward(self, k):
        zs = self.shard(k)
        for half, mask in ((0, 1), (1, 2)):
            part = self.at(mask, zs, half)
            self.wire.arrived(part, self.slot(k, mask, half), self.ids[mask])
            self.wire.start(part, part, self.slot(k, 3, half), self.ids[3 - mask])

    def share(self, k):
        zs = self.shard(k)
        for r, half in ((1, 1), (2, 0), (3, 0), (3, 1)):
            self.wire.arrived(self.at(r, zs, half), self.slot(k, r, half), self.ids[r])
        part = self.ref.at[:, zs, self.c]
        self.wire.start(part, part, self.core + k, {"dp": 1 - self.c})

    def complete(self):
        for k in range(self.nc):
            zs = self.shard(k)
            self.wire.arrived(self.ref.at[:, zs, 1 - self.c], self.core + k, {"dp": 1 - self.c})


class PlaneGather:
    def __init__(self, wire, ref, e, own=None):
        self.wire, self.ref, self.own = wire, ref, own
        self.half = ref.shape[-1] // 2
        self.ids = plane_ids(e)
        self.first = wire.slots(6)

    def at(self, r, half):
        columns = pl.ds(half * self.half, self.half)
        if r == 0 and self.own is not None:
            return self.own.at[:, columns]
        return self.ref.at[r, :, columns]

    def slot(self, r, half):
        return self.first + (r - 1) * 2 + half

    def send(self, r, half, to, mask):
        self.wire.start(
            lambda: self.at(r, half), lambda: self.at(to, half), self.slot(to, half), self.ids[mask]
        )

    def spread(self):
        for half, mask in ((0, 1), (1, 2), (1, 1), (0, 2)):
            self.send(0, half, mask, mask)

    def forward(self):
        for half, mask in ((0, 1), (1, 2)):
            self.wire.arrived(self.at(mask, half), self.slot(mask, half), self.ids[mask])
            self.send(mask, half, 3, 3 - mask)

    def near(self, r):
        half = 1 if r == 1 else 0
        self.wire.arrived(self.at(r, half), self.slot(r, half), self.ids[r])

    def far(self):
        for half in (0, 1):
            self.wire.arrived(self.at(3, half), self.slot(3, half), self.ids[3])

    def complete(self):
        self.near(1)
        self.near(2)
        self.far()


def swap_halves(values):
    return pltpu.roll(values, HEAD_DIMENSION // 2, 1)


class PlaneScatter:
    def __init__(self, wire, land, ids):
        self.wire, self.land, self.ids, self.part = wire, land, ids, None
        self.half = land.shape[-1]
        self.first = wire.slots(6)

    def send(self, source, mask, slot):
        self.wire.start(source, lambda: self.land.at[slot], self.first + slot, self.ids[mask])

    def near(self, r):
        self.send(self.part(r, r - 1), r, r - 1)

    def far(self):
        self.send(self.part(3, 0), 1, 2)
        self.send(self.part(3, 1), 2, 3)

    def relay(self, part=None):
        for half, r in ((0, 2), (1, 1)):
            slot = 2 + half
            self.wire.arrived(self.land.at[slot], self.first + slot, self.ids[3 - r])
            take = part or self.part
            mine = take(r, half)
            add_into(mine, self.land.at[slot])
            self.send(lambda r=r, half=half, take=take: take(r, half), r, 4 + half)

    def total(self, own):
        for slot, half, mask in ((0, 0, 1), (1, 1, 2), (4, 0, 2), (5, 1, 1)):
            self.wire.arrived(self.land.at[slot], self.first + slot, self.ids[mask])
            columns = pl.ds(half * self.half, self.half)
            rows = own.shape[0] // 4

            @pl.loop(0, 4)
            def _(n):
                here = pl.ds(pl.multiple_of(n * rows, rows), rows)
                own[here, columns] += self.land[slot, here].astype(F32)


class LineScatter:
    def __init__(self, wire, block, lands, z, nc, up=True):
        self.wire, self.block, self.lands, self.z, self.nc = wire, block, lands, z, nc
        self.up = up
        self.first = [wire.slots(nc - 1), wire.slots(nc - 1)]

    def arrive(self, way, index, j):
        land = self.lands[way].at[index]
        self.wire.arrived(land, self.first[way] + index, {"context": self.z})
        add_into(self.block(j), land, 1)

    def move(self, way, j, only=None):
        z, nc = self.z, self.nc
        inner, index = ((z > 0), j - z) if way == 0 else ((z < nc - 1), z - j)
        wanted = (j > z) if way == 0 else (j < z)
        if only is not None:
            wanted = wanted & only
        pl.when(wanted & inner)(lambda: self.arrive(way, index, j))
        self.leave(way, j, wanted)

    def step(self, s):
        if self.up:
            self.move(0, self.nc - s)
            self.move(1, s - 1)
        else:
            top = self.z == self.nc - 1
            if s == 1:
                for j in range(self.nc - 1):
                    self.leave(1, j, top)
            self.move(1, s - 1, jnp.logical_not(top))

    def leave(self, way, j, wanted):
        z = self.z
        index, near = (j - z, z + 1) if way == 0 else (z - j, z - 1)
        self.wire.start(
            self.block(j),
            self.lands[way].at[index - 1],
            self.first[way] + index - 1,
            {"context": near},
            when=wanted,
        )

    def last(self):
        if self.up:
            pl.when(self.z > 0)(lambda: self.arrive(0, 0, self.z))
        pl.when(self.z < self.nc - 1)(lambda: self.arrive(1, 0, self.z))


class RowsScatter:
    def __init__(self, wire, buf, core, plane, lines, e, z, c, nc, start, width, half):
        self.wire, self.buf, self.core, self.plane = wire, buf, core, plane
        self.e, self.c = e, c
        self.all = pl.ds(start, width)
        self.cols = (pl.ds(start, half), pl.ds(start + half, width - half))
        self.ids = plane_ids(e)
        self.core_slot = wire.slots(1)
        self.first = wire.slots(6)
        rows = buf.shape[2] // nc
        self.line = LineScatter(
            wire,
            lambda j: buf.at[c, e, pl.ds(pl.multiple_of(j * rows, rows), rows), self.all],
            lines,
            z,
            nc,
        )

    def share(self):
        self.wire.start(
            self.buf.at[1 - self.c, :, :, self.all], self.core, self.core_slot, {"dp": 1 - self.c}
        )

    def at(self, r, half):
        return self.buf.at[self.c, flip(self.e, r), :, self.cols[half]]

    def send(self, r, half, mask, slot):
        self.wire.start(
            self.at(r, half), self.plane(slot, half), self.first + slot, self.ids[mask]
        )

    def merge(self, before=None):
        self.wire.arrived(self.core, self.core_slot, {"dp": 1 - self.c})
        for r in (3, 1, 2, 0):
            block = flip(self.e, r)
            part = self.buf.at[self.c, block, :, self.all]
            add_into(part, self.core.at[block])
            if r == 3:
                if before is not None:
                    before()
                self.send(3, 0, 1, 2)
                self.send(3, 1, 2, 3)
            elif r:
                self.send(r, r - 1, r, r - 1)

    def add(self, r, half, slot, mask):
        land = self.plane(slot, half)
        self.wire.arrived(land, self.first + slot, self.ids[mask])
        add_into(self.at(r, half), land)

    def relay(self):
        for half, r in ((0, 2), (1, 1)):
            self.add(r, half, 2 + half, 3 - r)
            self.send(r, half, r, 4 + half)

    def total(self):
        for slot, half, mask in ((0, 0, 1), (1, 1, 2), (4, 0, 2), (5, 1, 1)):
            self.add(0, half, slot, mask)


class ExpertLine:
    def __init__(self, wire, base, land, sems, z, nc):
        self.wire, self.base, self.land = wire, base, land
        self.ins, self.out, self.sems, self.z, self.nc = None, None, sems, z, nc
        self.end = (z == 0) | (z == nc - 1)
        self.inner = jnp.logical_not(self.end)
        self.width = base.shape[-1] // EXP_DEV
        self.first = wire.slots((nc + 1) * EXP_DEV)
        self.sent = []

    def part(self, ref, j, i):
        return ref.at[j, :, pl.ds(i * self.width, self.width)]

    def combine(self, sources, stores):
        out, step = self.out, self.ins.shape[2]
        count = sources[0].shape[0] // step

        def loads(p):
            rows = pl.ds(p * step, step)
            return [
                pltpu.make_async_copy(source.at[rows], self.ins.at[k, p], self.sems.at[4 * k + p])
                for k, source in enumerate(sources)
            ]

        def store(p):
            pairs = stores(pl.ds(p * step, step), out.at[p % 2])
            return [
                pltpu.make_async_copy(source, dest, self.sems.at[16 + 2 * n + p % 2])
                for n, (source, dest) in enumerate(pairs)
            ]

        for p in range(count):
            for copy in loads(p):
                copy.start()
        for p in range(count):
            for copy in loads(p):
                copy.wait()
            if p > 1:
                for copy in store(p - 2):
                    copy.wait()
            total = self.ins[0, p].astype(F32)
            for k in range(1, len(sources)):
                total = total + self.ins[k, p].astype(F32)
            out[p % 2] = total.astype(out.dtype)
            for copy in store(p):
                copy.start()
        for p in range(max(0, count - 2), count):
            for copy in store(p):
                copy.wait()

    def copy(self, i, r, number):
        target, slot = flip(self.z, r), self.z
        if r == 3:
            target = jnp.where(self.end, flip(self.z, 1), target)
            slot = jnp.where(self.end, self.nc, slot)
        return pltpu.make_async_remote_copy(
            src_ref=self.part(self.base, flip(self.z, r), i),
            dst_ref=self.part(self.land, slot, i),
            send_sem=self.wire.sends.at[number],
            recv_sem=self.wire.recvs.at[self.first + slot * EXP_DEV + i],
            device_id={"context": target},
            device_id_type=MESH,
        )

    def send(self, i, r, when=None):
        number = len(self.sent)
        guard(when, self.copy(i, r, number).start)
        self.sent.append((when, i, r, number))

    def finish(self):
        for when, i, r, number in self.sent:
            guard(when, self.copy(i, r, number).wait_send)

    def arrived(self, slot, i):
        land = self.part(self.land, slot, i)
        self.wire.arrived(land, self.first + slot * EXP_DEV + i, {"context": self.z})

    def relay_loads(self, i, p):
        step = self.ins.shape[2]
        rows = pl.ds(p * step, step)
        sources = (self.part(self.base, flip(self.z, 2), i), self.part(self.land, self.nc, i))
        return [
            pltpu.make_async_copy(
                source.at[rows], self.ins.at[k, p], self.sems.at[4 * k + p]
            )
            for k, source in enumerate(sources)
        ]

    def relay_store(self, i, p):
        step = self.ins.shape[2]
        mine = self.part(self.base, flip(self.z, 2), i).at[pl.ds(p * step, step)]
        return pltpu.make_async_copy(self.ins.at[0, p], mine, self.sems.at[16 + p])

    def relay_steps(self):
        return range(self.base.shape[1] // self.ins.shape[2])

    def relay_begin(self, i):
        self.relayed = i

        def begin():
            self.arrived(self.nc, i)
            for p in self.relay_steps():
                for copy in self.relay_loads(i, p):
                    copy.start()

        pl.when(self.inner)(begin)

    def relay_add(self):
        i = self.relayed

        def add():
            for p in self.relay_steps():
                for copy in self.relay_loads(i, p):
                    copy.wait()
                a, b = (self.ins[k, p].astype(F32) for k in range(2))
                self.ins[0, p] = (a + b).astype(BF16)
                self.relay_store(i, p).start()

        pl.when(self.inner)(add)

    def relay_send(self, i):
        def wait():
            for p in self.relay_steps():
                self.relay_store(i, p).wait()

        pl.when(self.inner)(wait)
        self.send(i, 2, when=self.inner)

    def last(self, i, results):
        z = self.z
        sources = [self.part(self.base, z, i)]
        for r in (1, 2):
            self.arrived(flip(z, r), i)
            sources.append(self.part(self.land, flip(z, r), i))

        def stores(rows, wide):
            pairs, first = [], 0
            for result in results:
                columns = pl.ds(first, result.shape[-1])
                pairs.append((wide.at[:, columns], result.at[i, rows]))
                first += result.shape[-1]
            return pairs

        pl.when(self.end)(lambda: self.combine(sources, stores))

        def inner():
            self.arrived(flip(z, 3), i)
            self.combine(sources + [self.part(self.land, flip(z, 3), i)], stores)

        pl.when(self.inner)(inner)


def layer_kernel(
    nc,
    experts,
    cos_ref,
    sin_ref,
    routes_ref,
    qkv_ref,
    small_ref,
    wo_shard_ref,
    x_hbm,
    d_out_hbm,
    w_gu_hbm,
    w_dn_hbm,
    layer_hbm,
    d_x_hbm,
    sum_q_ref,
    sum_o_ref,
    sum_gu_hbm,
    sum_dn_hbm,
    base_hbm,
    land_hbm,
    y_hbm,
    wq_hbm,
    wo_hbm,
    cot_hbm,
    inputs_hbm,
    query_hbm,
    heads_hbm,
    hidden_hbm,
    wk_all,
    kv_ref,
    gate_all,
    gates_ref,
    gains_ref,
    x_all,
    y_land,
    dx_land,
    core_land,
    plane_q,
    plane_k,
    lines_o,
    lines_q,
    lines_k,
    dkv_land,
    d_in_ref,
    dg_lanes,
    dg_part,
    dg_land,
    sends_f,
    recvs_f,
    sends_c,
    recvs_c,
    sends_1,
    recvs_1,
    sends_2,
    recvs_2,
    sends_e,
    recvs_e,
    hand_sends,
    hand_recvs,
    stage_sems,
    load_sems,
    out_sems,
    sum_sems,
    y_sems,
    credits,
):
    e, z, c = (lax.axis_index(a) for a in ("expert", "context", "dp"))
    size = HEAD_DIMENSION
    blocks, tokens, width = cot_hbm.shape
    ff = w_dn_hbm.shape[1]
    query_width = QUERY_HEADS * size
    key_width = KEY_VALUE_HEADS * size
    qkv_width = query_width + 2 * key_width
    rest = wk_all.shape[-1]
    grad_width = base_hbm.shape[-1]
    ids = plane_ids(e)
    sibling = {"dp": 1 - c}
    bottom, even, top = z == 0, lax.rem(z, 2) == 0, z == nc - 1
    wire_1, wire_2, wire_e = Wire(sends_1, recvs_1), Wire(sends_2, recvs_2), Wire(sends_e, recvs_e)
    expert = ExpertLine(wire_e, base_hbm, land_hbm, sum_sems, z, nc)
    wire_c = Wire(sends_c, recvs_c)
    gather_cot = PlaneGather(wire_c, cot_hbm, e, d_out_hbm)
    gather = PlaneGather(wire_1, x_all, e)
    scatter_dx = PlaneScatter(wire_1, dx_land, ids)
    scatter_y = PlaneScatter(wire_2, y_land, ids)
    dg_slot = wire_1.slots(3)

    def front_phase(wq_ref, wo_ref, x_ref, inputs_ref, query_ref, heads_ref, hidden_ref, kv_scr, q_scr):
        wire = Wire(sends_f, recvs_f)
        kv_width = 2 * key_width
        load_x = pltpu.make_async_copy(x_hbm, x_ref, load_sems.at[0])
        load_x.start()
        wq_ref[e, z, c] = qkv_ref[:, pl.ds(0, query_width)]
        wo_ref[e, z, c] = wo_shard_ref[...]
        wk_all[e, z, c, :, pl.ds(0, kv_width)] = qkv_ref[:, pl.ds(query_width, kv_width)]
        wk_all[e, z, c, :, pl.ds(kv_width, SMALL)] = small_ref[...]
        greet(
            [(ids[m], None) for m in (1, 2, 3)]
            + [(sibling, None)]
            + [({"context": z + d}, z + d < nc) for d in range(1, nc)]
            + [({"context": z - d}, z >= d) for d in range(1, nc)]
        )
        gather_k = RowsGather(wire, wk_all, e, z, c, nc, 256)
        gather_q = RowsGather(wire, wq_ref, e, z, c, nc, 768)
        gather_o = RowsGather(wire, wo_ref, e, z, c, nc, 768)
        gather_k.go("l0", "s0")
        gather_q.go("s0")
        gather_k.go("l1", "s1", "f0", "l2", "s2")
        gather_q.go("l0")
        gather_k.go("f1", "h0", "l3", "s3")
        gather_q.go("l1", "s1")
        gather_o.go("l0")
        gather_k.go("f2", "h1", "f3")
        gather_q.go("l2", "s2")
        gather_k.go("h2")
        gather_o.go("l1")
        gather_q.go("f0")
        gather_k.go("h3")
        gather_q.go("l3", "s3")
        gather_k.go("c")
        load_x.wait()
        rows = x_ref[...].astype(F32)
        scale1 = lax.rsqrt(jnp.mean(rows * rows, -1, keepdims=True) + EPSILON)

        small = wk_all[:, :, :, :, pl.ds(kv_width, SMALL)].reshape(width, SMALL)
        small = jnp.transpose(small.astype(F32))
        gain_first, gain_second = small[experts : experts + 1], small[experts + 1 : experts + 2]
        gains_ref[0:1] = gain_first
        gains_ref[1:2] = gain_second
        inputs_ref[...] = (rows * scale1 * gain_first).astype(BF16)
        kv_scr[...] = dot_nn(inputs_ref[...], wk_all[...].reshape(width, kv_width + SMALL))

        def turned(head):
            return (head * cos_ref[...] + swap_halves(head) * sin_ref[...]).astype(BF16)

        line = wire.slots(KEY_VALUE_HEADS * nc)
        for j in range(KEY_VALUE_HEADS):
            kv_ref[j, z, :, pl.ds(0, size)] = turned(kv_scr[:, pl.ds(j * size, size)])
            value = kv_scr[:, pl.ds(kv_width // 2 + j * size, size)]
            kv_ref[j, z, :, pl.ds(size, size)] = value.astype(BF16)
            mine = kv_ref.at[j, z]
            for d in range(nc - 1, 0, -1):
                wire.start(mine, mine, line + j * nc + z, {"context": z + d}, when=z + d < nc)

        def keys_here(j):
            for d in range(1, nc):

                def wait(d=d):
                    wire.arrived(kv_ref.at[j, z - d], line + j * nc + z - d, {"context": z - d})

                pl.when(z >= d)(wait)

        outs = [
            pltpu.make_async_copy(source, dest, out_sems.at[n])
            for n, (source, dest) in enumerate(
                (
                    (inputs_ref, inputs_hbm),
                    (query_ref, query_hbm),
                    (heads_ref, heads_hbm),
                    (hidden_ref, hidden_hbm),
                    (wq_ref, wq_hbm),
                    (wo_ref, wo_hbm),
                )
            )
        ]
        outs[0].start()
        for later in range(1, nc):

            def clear(later=later):
                for j in range(KEY_VALUE_HEADS):
                    kv_ref[j, z + later] = jnp.zeros(kv_ref.shape[2:], BF16)

            pl.when(z + later < nc)(clear)
        gather_q.go("f1", "f2", "h0")
        gather_o.go("s0")
        gather_q.go("f3", "h1")
        gather_o.go("s1")
        gather_q.go("h2", "h3", "c")
        outs[4].start()
        gather_o.go("f0", "f1")
        gather_cot.spread()

        @pl.loop(0, query_width // 256)
        def _(n):
            columns = pl.ds(pl.multiple_of(n * 256, 256), 256)
            q_scr[:, columns] = dot_nn(
                inputs_ref[...], wq_ref[:, :, :, :, columns].reshape(width, 256)
            )

        @pl.loop(0, QUERY_HEADS)
        def _(h):
            columns = pl.ds(pl.multiple_of(h * size, size), size)
            query_ref[:, columns] = turned(q_scr[:, columns])

        outs[1].start()

        logits = kv_scr[:, pl.ds(kv_width, SMALL)]
        lanes = lax.broadcasted_iota(jnp.int32, logits.shape, 1)
        routes = jnp.concatenate(
            [routes_ref[...].astype(F32), jnp.zeros((SMALL - TOP, tokens), F32)], 0
        )
        routes = jnp.transpose(routes).astype(jnp.int32)
        named = lanes == routes[:, 0:1]
        for k in range(1, TOP):
            named = named | (lanes == routes[:, k : k + 1])
        logits = jnp.where(named, logits, MASKED)
        expd = jnp.exp(logits - jnp.max(logits, -1, keepdims=True))
        gates = expd / jnp.sum(expd, -1, keepdims=True)
        gate_all[0] = jnp.transpose(gates)[:GATE_ROWS]
        gate_slot = wire.slots(3)
        for r in (1, 2, 3):
            wire.start(gate_all.at[0], gate_all.at[r], gate_slot + r - 1, ids[r])

        length = nc * tokens
        group = QUERY_HEADS // KEY_VALUE_HEADS

        def attend(first, last):
            j = first // group
            key = kv_ref[j, :, :, pl.ds(0, size)].reshape(length, size)
            value = kv_ref[j, :, :, pl.ds(size, size)].reshape(length, size)

            @pl.loop(first, last)
            def _(h):
                column = pl.multiple_of(h * size, size)
                scores = dot_nt(query_ref[:, pl.ds(column, size)], key) * (size**-0.5)
                row = z * tokens + lax.broadcasted_iota(jnp.int32, scores.shape, 0)
                place = lax.broadcasted_iota(jnp.int32, scores.shape, 1)
                scores = jnp.where(place <= row, scores, MASKED)
                expd = jnp.exp(scores - jnp.max(scores, -1, keepdims=True))
                total = jnp.sum(expd, -1, keepdims=True)
                mixed = dot_nn(expd.astype(BF16), value) / total
                heads_ref[:, pl.ds(column, size)] = mixed.astype(BF16)

        half = group // 2
        keys_here(0)
        attend(0, half)
        gather_o.go("l2", "s2")
        attend(half, group)
        gather_o.go("l3", "s3", "f2", "h0")
        keys_here(1)
        attend(group, group + half)
        gather_o.go("f3", "h1")
        attend(group + half, QUERY_HEADS)
        gather_o.go("h2")
        gather_cot.forward()
        gather_o.go("h3", "c")
        outs[5].start()
        outs[2].start()
        part = width // wo_ref.shape[0]
        for block in range(wo_ref.shape[0]):
            weight = wo_ref[block].reshape(part, width)
            columns = pl.ds(block * part, part)
            hidden_ref[:, columns] = x_ref[:, columns].astype(F32) + dot_nt(heads_ref[...], weight)
        hidden = hidden_ref[...]
        scale2 = lax.rsqrt(jnp.mean(hidden * hidden, -1, keepdims=True) + EPSILON)
        x_all[0] = (hidden * scale2 * gains_ref[1:2]).astype(BF16)
        gather.spread()
        outs[3].start()
        for r in (1, 2, 3):
            wire.arrived(gate_all.at[r], gate_slot + r - 1, ids[r])
        for r in range(gate_all.shape[0]):
            zeros = jnp.zeros((SMALL - GATE_ROWS, tokens), F32)
            turned_gates = jnp.transpose(jnp.concatenate([gate_all[r], zeros], 0))
            both = [
                jnp.sum(jnp.where(lanes == e * EXP_DEV + i, turned_gates, 0.0), -1, keepdims=True)
                for i in range(EXP_DEV)
            ]
            gates_ref[r] = jnp.where(lanes == 0, both[0], jnp.where(lanes == 1, both[1], 0.0))
        for copy in outs:
            copy.wait()
        wire.finish()

    def token_phase(w_gu, w_dn, cot_all, a_all, dgu_all, y_stage, dx_part, stage, ins):
        expert.ins = ins
        scatter_dx.part = lambda r, half: dx_part.at[
            r - 1, :, pl.ds(half * width // 2, width // 2)
        ]
        sources = [
            (w_gu_hbm.at[0], w_gu.at[0]),
            (w_dn_hbm.at[0], w_dn.at[0]),
            (d_out_hbm, cot_all.at[0]),
            (w_gu_hbm.at[1], w_gu.at[1]),
            (w_dn_hbm.at[1], w_dn.at[1]),
            (cot_hbm.at[1:], cot_all.at[1:]),
        ]
        loads = [
            pltpu.make_async_copy(source, dest, load_sems.at[n])
            for n, (source, dest) in enumerate(sources)
        ]
        for copy in loads[:5]:
            copy.start()
        step = 256
        wide = 512
        dg_lanes[...] = jnp.zeros_like(dg_lanes)

        def hidden_units(r, i, count=1):
            lane = lax.broadcasted_iota(jnp.int32, (1, SMALL), 1)
            here = pl.ds(r, count)
            flat = count * tokens

            @pl.loop(0, ff // step)
            def _(f):
                column = pl.multiple_of(f * step, step)
                rows = x_all[here].reshape(flat, width)
                grads = cot_all[here].reshape(flat, width)
                gate_part = dot_nn(rows, w_gu[i, :, pl.ds(column, step)])
                up_part = dot_nn(rows, w_gu[i, :, pl.ds(ff + column, step)])
                raw = dot_nt(grads, w_dn[i, pl.ds(column, step), :])
                gate = gates_ref[here].reshape(flat, SMALL)
                gate = jnp.sum(jnp.where(lane == i, gate, 0.0), -1, keepdims=True)
                sigma = jax.nn.sigmoid(gate_part)
                silu = gate_part * sigma
                act = silu * up_part
                lanes = lax.broadcasted_iota(jnp.int32, (flat, SMALL), 1)
                d_gate = jnp.where(
                    lanes == e * EXP_DEV + i, jnp.sum(act * raw, -1, keepdims=True), 0.0
                )
                dg_lanes[here] += d_gate.reshape(count, tokens, SMALL)

                def put(ref, first, values):
                    values = values.astype(BF16).reshape(count, tokens, step)
                    ref[here, :, pl.ds(pl.multiple_of(first, step), step)] = values

                put(a_all, i * ff + column, act * gate)
                d_act = raw * gate
                d_gate_part = d_act * up_part * sigma * (1.0 + gate_part * (1.0 - sigma))
                put(dgu_all, i * 2 * ff + column, d_gate_part)
                put(dgu_all, i * 2 * ff + ff + column, d_act * silu)

        def y_copy(r):
            return pltpu.make_async_copy(y_stage.at[r % 2], y_hbm.at[r], y_sems.at[r % 2])

        def outputs(r, count=1):
            here = pl.ds(r, count)
            flat = count * tokens

            @pl.loop(0, width // wide)
            def _(n):
                columns = pl.ds(pl.multiple_of(n * wide, wide), wide)
                low = dgu_all[here].reshape(flat, EXP_DEV * 2 * ff)
                d_rows = dot_nt(low[:, : 2 * ff], w_gu[0, columns, :])
                d_rows += dot_nt(low[:, 2 * ff :], w_gu[1, columns, :])
                weight = w_dn[:, :, columns].reshape(EXP_DEV * ff, wide)
                out = dot_nn(a_all[here].reshape(flat, EXP_DEV * ff), weight).astype(BF16)
                for k in range(count):
                    rows = slice(k * tokens, (k + 1) * tokens)
                    y_stage[(r + k) % 2, :, columns] = out[rows]
                    if r == 0:
                        d_in_ref[:, columns] = d_rows
                    else:
                        dx_part[r + k - 1, :, columns] = d_rows[rows].astype(BF16)

            for k in range(r, r + count):
                y_copy(k).start()
                dg_part[k] = jnp.transpose(dg_lanes[k])[:GATE_ROWS]
                if k:
                    wire_1.start(dg_part.at[k], dg_land.at[k - 1], dg_slot + k - 1, ids[k])

        half_rows = width // nc // 2
        def where(k):
            high = lax.rem(lax.div(z, 2) + 1 + lax.div(k, 2), 2)
            return 2 * high + lax.rem(z + 1 + k, 2)

        def keep(i, k):
            slot = lax.rem(k, 2)
            return pltpu.make_async_copy(
                stage.at[slot, c], expert.part(base_hbm, where(k), i), stage_sems.at[slot]
            )

        def hand(i, k):
            return pltpu.make_async_remote_copy(
                src_ref=stage.at[lax.rem(k, 2), 1 - c],
                dst_ref=core_land.at[k],
                send_sem=hand_sends.at[i * nc + k],
                recv_sem=hand_recvs.at[i * nc + k],
                device_id=sibling,
                device_id_type=MESH,
            )

        def settle(i, k):
            hand(i, k).wait_recv()
            add_into(stage.at[lax.rem(k, 2), c], core_land.at[k])
            keep(i, k).start()

        def clear(i, k):
            keep(i, k).wait()
            hand(i, k).wait_send()

        def leave(i, r):
            if i == 0 and r == 2:
                expert.send(i, r, when=expert.end)
            elif i == 0 and r == 1 or r == 3:
                expert.send(i, r)
            elif r == 2:
                expert.send(i, r, when=bottom)
            elif r == 1:
                expert.send(i, r, when=even)

        def weight_grads(i, between=lambda k: None):
            @pl.loop(0, nc)
            def _(k):
                @pl.when(k >= 2)
                def _():
                    clear(i, k - 2)

                for n in (2, 3):

                    @pl.when(k == n)
                    def _(n=n):
                        leave(i, 5 - n)

                rows_at = pl.ds(pl.multiple_of(where(k) * 2 * half_rows, 2 * half_rows), 2 * half_rows)
                for first, source, grad, start, count in (
                    (0, x_all, dgu_all, i * 2 * ff, 2),
                    (2 * ff, cot_all, a_all, i * ff, 1),
                ):
                    rows = source[:, :, rows_at].reshape(blocks * tokens, 2 * half_rows)

                    @pl.loop(0, count)
                    def _(n):
                        column = pl.multiple_of(n * ff, ff)
                        part = grad[:, :, pl.ds(pl.multiple_of(start + column, ff), ff)]
                        result = dot_tn(rows, part.reshape(blocks * tokens, ff)).astype(BF16)
                        stage[lax.rem(k, 2), :, :, pl.ds(pl.multiple_of(first + column, ff), ff)] = (
                            result.reshape(2, half_rows, ff)
                        )

                if i:

                    @pl.when(k == 0)
                    def _():
                        pl.semaphore_wait(credits.at[3], 1)

                hand(i, k).start()

                @pl.when(k >= 1)
                def _():
                    settle(i, k - 1)

                between(k)

        for copy in loads[:3]:
            copy.wait()
        gather_cot.complete()
        loads[5].start()
        for copy in loads[3:5]:
            copy.wait()

        @pl.loop(0, EXP_DEV)
        def _(i):
            hidden_units(0, i)

        gather.forward()
        outputs(0)
        loads[5].wait()
        gather.near(1)
        gather.near(2)
        hidden_units(1, 0, 2)
        gather.far()
        hidden_units(3, 0)
        weight_grads(0)
        hidden_units(1, 1, 2)
        clear(0, nc - 2)
        leave(0, 1)
        settle(0, nc - 1)
        pl.semaphore_signal(credits.at[3], inc=1, device_id=sibling, device_id_type=MESH)
        y_copy(0).wait()
        outputs(1, 2)
        scatter_dx.near(1)
        scatter_dx.near(2)
        hidden_units(3, 1)
        expert.relay_begin(0)
        y_copy(1).wait()
        outputs(3)
        scatter_dx.far()
        clear(0, nc - 1)
        expert.relay_add()

        def between(k):
            @pl.when(k == 0)
            def _():
                expert.relay_send(0)

            @pl.when(k == 1)
            def _():
                scatter_dx.relay()

        weight_grads(1, between)
        scatter_dx.total(d_in_ref)
        for r in (1, 2):
            pl.semaphore_signal(credits.at[r], inc=1, device_id=ids[r], device_id_type=MESH)
        settle(1, nc - 1)
        for k in (nc - 2, nc - 1):
            clear(1, k)
        leave(1, 1)
        y_copy(3).wait()
        y_copy(2).wait()
        wire_1.finish()
        wire_c.finish()
        pl.semaphore_signal(credits.at[0], inc=1, device_id=sibling, device_id_type=MESH)

    def token_rows_phase(
        weight,
        grads_o,
        grads_q,
        x_ref,
        inputs_ref,
        query_ref,
        heads_ref,
        hidden_ref,
        d_hidden_ref,
        d_attn_ref,
        d_heads_ref,
        d_all_ref,
        rows_ref,
        dkv_acc,
        dkv_ref,
        y_relay,
        ins,
        out_wide,
    ):
        expert.ins, expert.out = ins, out_wide
        cot_ref, d_inputs_ref = d_heads_ref, hidden_ref
        scatter_y.part = lambda r, half: y_hbm.at[r, :, pl.ds(half * width // 2, width // 2)]
        y_loads = [
            pltpu.make_async_copy(scatter_y.part(2 - half, half), y_relay.at[half], y_sems.at[half])
            for half in range(2)
        ]
        for copy in y_loads:
            copy.start()
        planes = grads_o.shape[1]
        part = width // planes
        sources = (
            (hidden_hbm, hidden_ref),
            (d_out_hbm, cot_ref),
            (wo_hbm, weight),
            (heads_hbm, heads_ref),
            (query_hbm, query_ref),
            (x_hbm, x_ref),
            (inputs_hbm, inputs_ref),
        )
        loads = [
            pltpu.make_async_copy(source, dest, load_sems.at[4 + n])
            for n, (source, dest) in enumerate(sources)
        ]
        for copy in loads:
            copy.start()
        for r in (1, 2):
            scatter_y.near(r)
        scatter_y.far()

        def rows_scatter(buf, core, plane, lines, start, count, half):
            return RowsScatter(
                wire_2,
                buf,
                core,
                plane,
                [lines.at[0], lines.at[1]],
                e,
                z,
                c,
                nc,
                start,
                count,
                half,
            )

        rows_of = part // 2
        scatter_o = rows_scatter(
            grads_o,
            x_all.at[:, pl.ds(0, rows_of)],
            lambda slot, half: dx_land.at[slot, pl.ds(0, rows_of)],
            lines_o,
            0,
            width,
            width // 2,
        )
        scatter_q = rows_scatter(
            grads_q,
            core_land.at[:, :, pl.ds(0, query_width)],
            lambda slot, half: plane_q.at[slot],
            lines_q,
            0,
            query_width,
            query_width // 2,
        )
        rest_half = rest // 256 * 128
        scatter_k = rows_scatter(
            grads_q,
            core_land.at[:, :, pl.ds(query_width, rest)],
            lambda slot, half: plane_k.at[
                slot, :, pl.ds(0, rest - rest_half if half else rest_half)
            ],
            lines_k,
            query_width,
            rest,
            rest_half,
        )
        scatter_kv = [
            LineScatter(
                wire_2,
                lambda j, h=h: dkv_ref.at[h, j],
                [dkv_land.at[h], dkv_land.at[h]],
                z,
                nc,
                up=False,
            )
            for h in range(KEY_VALUE_HEADS)
        ]

        loads[0].wait()
        loads[1].wait()
        hidden, d_in = hidden_ref[...], d_in_ref[...]
        scale2 = lax.rsqrt(jnp.mean(hidden * hidden, -1, keepdims=True) + EPSILON)
        scaled = d_in * gains_ref[1:2]
        mean = jnp.mean(scaled * hidden, -1, keepdims=True)
        d_hidden = cot_ref[...].astype(F32) + scale2 * scaled
        d_hidden = d_hidden - hidden * (scale2 * scale2 * scale2 * mean)
        d_hidden_ref[...] = d_hidden
        d_attn_ref[...] = d_hidden.astype(BF16)
        rows_ref[...] = jnp.zeros_like(rows_ref)
        rows_ref[experts + 1 : experts + 2, :] = jnp.sum(d_in * hidden * scale2, 0, keepdims=True)

        loads[2].wait()

        @pl.loop(0, query_width // 256)
        def _(n):
            columns = pl.ds(pl.multiple_of(n * 256, 256), 256)
            out = weight[:, :, :, :, columns].reshape(width, 256)
            d_heads_ref[:, columns] = dot_nn(d_attn_ref[...], out).astype(BF16)

        load_q = pltpu.make_async_copy(wq_hbm, weight, load_sems.at[0])
        load_q.start()
        loads[3].wait()

        def row_grads(buf, left, right, first, count, extra=None):
            @pl.loop(0, planes)
            def _(block):
                columns = pl.ds(pl.multiple_of(block * part, part), part)
                result = dot_tn(left[:, columns], right)
                if extra is not None:
                    result = result + extra(columns)
                result = result.astype(BF16).reshape(nc, 2, part // nc // 2, count)
                for half in range(2):
                    buf[half, block, :, pl.ds(first, count)] = result[:, half].reshape(
                        part // 2, count
                    )

        row_grads(grads_o, d_attn_ref, heads_ref[...], 0, width)
        pl.semaphore_wait(credits.at[0], 1)
        scatter_o.share()
        y_own = pltpu.make_async_copy(y_hbm.at[0], heads_ref, load_sems.at[2])
        y_own.start()

        length = nc * tokens
        group = QUERY_HEADS // KEY_VALUE_HEADS
        loads[4].wait()
        dkv_acc[...] = jnp.zeros_like(dkv_acc)

        def attend(j, first, last):
            key = kv_ref[j, :, :, pl.ds(0, size)].reshape(length, size)
            value = kv_ref[j, :, :, pl.ds(size, size)].reshape(length, size)

            @pl.loop(j * group + first, j * group + last)
            def _(h):
                columns = pl.ds(pl.multiple_of(h * size, size), size)
                query, grad = query_ref[:, columns], d_heads_ref[:, columns]
                probs = masked_probs(z * tokens, query, key)
                d_probs = dot_nt(grad, value)
                inner = jnp.sum(probs * d_probs, axis=-1, keepdims=True)
                d_raw = (probs * (d_probs - inner) * (size**-0.5)).astype(BF16)
                d_query = dot_nn(d_raw, key)
                d_query = d_query * cos_ref[...] - swap_halves(d_query) * sin_ref[...]
                d_all_ref[:, columns] = d_query.astype(BF16)
                dkv_acc[j, :, pl.ds(0, size)] += dot_tn(d_raw, query)
                dkv_acc[j, :, pl.ds(size, size)] += dot_tn(probs.astype(BF16), grad)

        def round_kv(j):
            for block in range(nc):
                rows = dkv_acc[j, pl.ds(block * tokens, tokens), :]
                dkv_ref[j, block] = rows.astype(BF16)

        def enter():
            pl.semaphore_wait(credits.at[1], 1)
            pl.semaphore_wait(credits.at[2], 1)

        attend(0, 0, group)
        round_kv(0)
        scatter_kv[0].step(1)
        scatter_o.merge(enter)
        for copy in y_loads:
            copy.wait()
        scatter_y.relay(lambda r, half: y_relay.at[half])
        attend(1, 0, group // 2)
        scatter_kv[0].step(2)
        attend(1, group // 2, group)
        round_kv(1)
        scatter_kv[1].step(1)
        expert.send(1, 2, when=top)
        scatter_kv[0].step(3)
        scatter_o.relay()

        for copy in loads[5:]:
            copy.wait()
        row_grads(grads_q, inputs_ref, d_all_ref[:, pl.ds(0, query_width)], 0, query_width)
        scatter_q.share()
        scatter_kv[1].step(2)
        scatter_kv[1].step(3)
        scatter_o.total()
        scatter_o.line.step(1)
        expert.send(1, 1, when=jnp.logical_not(even))
        expert.relay_begin(1)
        scatter_q.merge()
        for h in range(KEY_VALUE_HEADS):
            scatter_kv[h].last()
        y_own.wait()
        hidden_ref[...] += heads_ref[...].astype(F32)
        scatter_y.total(hidden_ref)
        heads_ref[...] = hidden_ref[...].astype(BF16)
        layer_out = pltpu.make_async_copy(heads_ref, layer_hbm, out_sems.at[0])
        layer_out.start()
        expert.relay_add()
        expert.relay_send(1)

        for h in range(KEY_VALUE_HEADS):
            grad = dkv_ref[h, z, :, pl.ds(0, size)].astype(F32)
            grad = grad * cos_ref[...] - swap_halves(grad) * sin_ref[...]
            d_all_ref[:, pl.ds(query_width + h * size, size)] = grad.astype(BF16)
            d_all_ref[:, pl.ds(query_width + key_width + h * size, size)] = dkv_ref[
                h, z, :, pl.ds(size, size)
            ]

        total = dg_part[0]
        for r in (1, 2, 3):
            wire_1.arrived(dg_land.at[r - 1], dg_slot + r - 1, ids[r])
            total = total + dg_land[r - 1]
        gates = gate_all[0]
        d_logits = gates * (total - jnp.sum(gates * total, 0, keepdims=True))
        d_logits = jnp.concatenate(
            [d_logits, jnp.zeros((SMALL - d_logits.shape[0], tokens), F32)], 0
        )
        d_all_ref[:, pl.ds(qkv_width, SMALL)] = jnp.transpose(d_logits).astype(BF16)

        load_q.wait()

        @pl.loop(0, planes)
        def _(block):
            columns = pl.ds(pl.multiple_of(block * part, part), part)
            rows_q = weight[block].reshape(part, query_width)
            rows_k = wk_all[block].reshape(part, rest)
            d_inputs_ref[:, columns] = dot_nt(
                d_all_ref[:, pl.ds(0, query_width)], rows_q
            ) + dot_nt(d_all_ref[:, pl.ds(query_width, rest)], rows_k)

        rows = x_ref[...].astype(F32)
        scale1 = lax.rsqrt(jnp.mean(rows * rows, -1, keepdims=True) + EPSILON)
        d_inputs = d_inputs_ref[...]
        rows_ref[experts : experts + 1, :] = jnp.sum(d_inputs * rows * scale1, 0, keepdims=True)

        def extra(columns):
            small = jnp.transpose(rows_ref[:, columns])
            return jnp.concatenate([jnp.zeros((part, rest - SMALL), F32), small], 1)

        row_grads(
            grads_q, inputs_ref, d_all_ref[:, pl.ds(query_width, rest)], query_width, rest, extra
        )
        scatter_k.share()
        scatter_q.relay()
        scatter_k.merge()
        scaled = d_inputs_ref[...] * gains_ref[0:1]
        rows = x_ref[...].astype(F32)
        scale1 = lax.rsqrt(jnp.mean(rows * rows, -1, keepdims=True) + EPSILON)
        mean = jnp.mean(scaled * rows, -1, keepdims=True)
        d_x = d_hidden_ref[...] + scale1 * scaled - rows * (scale1 * scale1 * scale1 * mean)
        inputs_ref[...] = d_x.astype(BF16)
        d_x_out = pltpu.make_async_copy(inputs_ref, d_x_hbm, out_sems.at[1])
        d_x_out.start()
        scatter_q.total()
        expert.last(0, (sum_gu_hbm, sum_dn_hbm))
        scatter_k.relay()
        scatter_q.line.step(1)
        scatter_o.line.step(2)
        scatter_k.total()
        scatter_k.line.step(1)
        for s in range(2, nc):
            if s > 2:
                scatter_o.line.step(s)
            scatter_q.line.step(s)
            scatter_k.line.step(s)
        for scatter in (scatter_o, scatter_q, scatter_k):
            scatter.line.last()
        sum_o_ref[...] = scatter_o.line.block(z)[...].astype(F32)
        sum_q_ref[...] = grads_q[c, e, pl.ds(pl.multiple_of(z * (rows_of // nc), rows_of // nc), rows_of // nc)].astype(F32)
        expert.last(1, (sum_gu_hbm, sum_dn_hbm))
        layer_out.wait()
        d_x_out.wait()
        wire_2.finish()
        expert.finish()

    held = EXP_DEV
    weight_shape = wq_hbm.shape
    pl.run_scoped(
        front_phase,
        pltpu.VMEM(weight_shape, BF16),
        pltpu.VMEM(weight_shape, BF16),
        pltpu.VMEM((tokens, width), BF16),
        pltpu.VMEM((tokens, width), BF16),
        pltpu.VMEM((tokens, query_width), BF16),
        pltpu.VMEM((tokens, query_width), BF16),
        pltpu.VMEM((tokens, width), F32),
        pltpu.VMEM((tokens, rest), F32),
        pltpu.VMEM((tokens, query_width), F32),
    )
    shard, step = width // nc // 2, 48
    pl.run_scoped(
        token_phase,
        pltpu.VMEM((held, width, 2 * ff), BF16),
        pltpu.VMEM((held, ff, width), BF16),
        pltpu.VMEM((blocks, tokens, width), BF16),
        pltpu.VMEM((blocks, tokens, held * ff), BF16),
        pltpu.VMEM((blocks, tokens, held * 2 * ff), BF16),
        pltpu.VMEM((2, tokens, width), BF16),
        pltpu.VMEM((blocks - 1, tokens, width), BF16),
        pltpu.VMEM((2, 2, shard, grad_width // held), BF16),
        pltpu.VMEM((2, shard // step, step, grad_width // held), BF16),
    )
    rows_half = width // blocks // 2
    pl.run_scoped(
        token_rows_phase,
        pltpu.VMEM(weight_shape, BF16),
        pltpu.VMEM((2, blocks, rows_half, width), BF16),
        pltpu.VMEM((2, blocks, rows_half, qkv_width + SMALL), BF16),
        pltpu.VMEM((tokens, width), BF16),
        pltpu.VMEM((tokens, width), BF16),
        pltpu.VMEM((tokens, query_width), BF16),
        pltpu.VMEM((tokens, query_width), BF16),
        pltpu.VMEM((tokens, width), F32),
        pltpu.VMEM((tokens, width), F32),
        pltpu.VMEM((tokens, width), BF16),
        pltpu.VMEM((tokens, query_width), BF16),
        pltpu.VMEM((tokens, qkv_width + SMALL), BF16),
        pltpu.VMEM((SMALL, width), F32),
        pltpu.VMEM((KEY_VALUE_HEADS, nc * tokens, 2 * size), F32),
        pltpu.VMEM((KEY_VALUE_HEADS, nc, tokens, 2 * size), BF16),
        pltpu.VMEM((2, tokens, width // 2), BF16),
        pltpu.VMEM((4, shard // step, step, grad_width // held), BF16),
        pltpu.VMEM((2, step, grad_width // held), F32),
    )


def layer(operands, sizes):
    ne, nc, nd = sizes
    qkv_shard, x = operands[3], operands[6]
    w_dn = operands[9]
    tokens, width = x.shape
    held, ff = w_dn.shape[0], w_dn.shape[1]
    query_width = QUERY_HEADS * HEAD_DIMENSION
    rows, qkv_width = qkv_shard.shape
    rest = qkv_width - query_width + SMALL
    rest_half = rest // 256 * 128
    shard, grads = width // (nc * nd), held * 3 * ff
    kv_size = 2 * HEAD_DIMENSION
    weight = (ne, nc, nd, rows, query_width)
    shapes = [
        ((tokens, width), BF16),
        ((tokens, width), BF16),
        ((rows, qkv_width + SMALL), F32),
        ((rows, width), F32),
        ((held, shard, 2 * ff), F32),
        ((held, shard, ff), F32),
        ((nc, shard, grads), BF16),
        ((nc + 1, shard, grads), BF16),
        ((ne, tokens, width), BF16),
        (weight, BF16),
        (weight, BF16),
        ((ne, tokens, width), BF16),
        ((tokens, width), BF16),
        ((tokens, query_width), BF16),
        ((tokens, query_width), BF16),
        ((tokens, width), F32),
    ]
    vmem = pl.BlockSpec(memory_space=pltpu.VMEM)
    anywhere = pl.BlockSpec(memory_space=pl.ANY)
    units = nc * held
    sems = [120, 110, 6, 6, 16, 16, 64, 64, 2 * units, (nc + 1) * held, units, units, 2, 12, 6]
    return pl.pallas_call(
        functools.partial(layer_kernel, nc, EXP_DEV * ne),
        out_shape=[jax.ShapeDtypeStruct(*s) for s in shapes],
        in_specs=[vmem] * 6 + [anywhere] * (len(operands) - 6),
        out_specs=[anywhere] * 2 + [vmem] * 2 + [anywhere] * (len(shapes) - 4),
        scratch_shapes=[
            pltpu.VMEM((ne, nc, nd, rows, rest), BF16),
            pltpu.VMEM((KEY_VALUE_HEADS, nc, tokens, kv_size), BF16),
            pltpu.VMEM((ne, GATE_ROWS, tokens), F32),
            pltpu.VMEM((ne, tokens, SMALL), F32),
            pltpu.VMEM((8, width), F32),
            pltpu.VMEM((ne, tokens, width), BF16),
            pltpu.VMEM((6, tokens, width // 2), BF16),
            pltpu.VMEM((6, tokens, width // 2), BF16),
            pltpu.VMEM((nc, shard, grads // held), BF16),
            pltpu.VMEM((6, nc * rows, query_width // 2), BF16),
            pltpu.VMEM((6, nc * rows, rest - rest_half), BF16),
            pltpu.VMEM((2, nc - 1, rows, width), BF16),
            pltpu.VMEM((2, nc - 1, rows, query_width), BF16),
            pltpu.VMEM((2, nc - 1, rows, rest), BF16),
            pltpu.VMEM((KEY_VALUE_HEADS, nc - 1, tokens, kv_size), BF16),
            pltpu.VMEM((tokens, width), F32),
            pltpu.VMEM((ne, tokens, SMALL), F32),
            pltpu.VMEM((ne, GATE_ROWS, tokens), F32),
            pltpu.VMEM((ne - 1, GATE_ROWS, tokens), F32),
        ]
        + [pltpu.SemaphoreType.DMA((count,)) for count in sems]
        + [
            pltpu.SemaphoreType.DMA((20,)),
            pltpu.SemaphoreType.DMA((2,)),
            pltpu.SemaphoreType.REGULAR((4,)),
        ],
        compiler_params=pltpu.CompilerParams(
            collective_id=0, has_side_effects=True, vmem_limit_bytes=63 * MIB
        ),
    )(*operands)


def finish_kernel(experts, *refs):
    sources, dests = refs[:6], refs[6:12]
    router_ref, first_ref, second_ref = refs[12:]
    sum_q = sources[0]
    qkv_width = dests[0].shape[-1]
    dests[0][...] = sum_q[:, pl.ds(0, qkv_width)]
    for source, dest in zip(sources[1:], dests[1:]):
        dest[...] = source[...]
    small = sum_q[:, pl.ds(qkv_width, SMALL)]
    rows = small.shape[0]
    filled = jnp.concatenate([small, jnp.zeros((SMALL - rows, SMALL), F32)], 0)
    turned = jnp.transpose(filled)[:, :rows]
    router_ref[...] = turned[:experts]
    first_ref[...] = turned[experts : experts + 1]
    second_ref[...] = turned[experts + 1 : experts + 2]


def finish(sum_q, others, experts):
    rows, q_width = sum_q.shape
    vmem = pl.BlockSpec(memory_space=pltpu.VMEM)
    shapes = [jax.ShapeDtypeStruct((rows, q_width - SMALL), F32)]
    shapes += [jax.ShapeDtypeStruct(o.shape, o.dtype) for o in others]
    shapes += [jax.ShapeDtypeStruct((count, rows), F32) for count in (experts, 1, 1)]
    return pl.pallas_call(
        functools.partial(finish_kernel, experts),
        out_shape=shapes,
        in_specs=[vmem] * 6,
        out_specs=[vmem] * 9,
        compiler_params=pltpu.CompilerParams(vmem_limit_bytes=60 * MIB),
    )(sum_q, *others)


def local_plain(
    layer_input,
    gain_attn,
    query_key_value_weight,
    w_out,
    w_router,
    gain_ffn,
    w_gate_up,
    w_down,
    routes,
    d_out,
):
    tokens = layer_input.shape[1]
    model_width = layer_input.shape[2]
    ne, nc, nd = (lax.axis_size(a) for a in ("expert", "context", "dp"))
    expert_total = EXP_DEV * ne
    ff = w_down.shape[1]
    me = lax.axis_index("expert")
    first_row = lax.axis_index("context") * tokens
    query_width = QUERY_HEADS * HEAD_DIMENSION
    key_width = KEY_VALUE_HEADS * HEAD_DIMENSION
    qkv_width = query_width + 2 * key_width

    small = jnp.concatenate([w_router, gain_attn[:, None], gain_ffn[:, None]], -1)
    small = jnp.pad(small, ((0, 0), (0, 128 - small.shape[1])))
    gathered = gather_rows(jnp.concatenate([query_key_value_weight, small], -1))
    out_turned = gather_rows(w_out.T)
    qkv_weight = gathered[:, :qkv_width]
    router_weight = gathered[:, qkv_width : qkv_width + expert_total]
    gains = gathered[:, qkv_width + expert_total : qkv_width + expert_total + 2].T.astype(F32)
    gain_first, gain_second = gains[0], gains[1]
    cotangent_all = plane_gather(d_out[0])

    token_rows = layer_input[0].astype(F32)
    scale1 = lax.rsqrt(jnp.mean(token_rows * token_rows, -1, keepdims=True) + EPSILON)
    inputs1 = (token_rows * scale1 * gain_first).astype(BF16)
    query_key_value = dot_nn(inputs1, qkv_weight)
    cosine_values, sine_values = rope_tables(first_row + jnp.arange(tokens), HEAD_DIMENSION)
    rotated = rotate_half(
        query_key_value[:, : query_width + key_width].reshape(tokens, -1, HEAD_DIMENSION),
        cosine_values,
        sine_values,
    ).reshape(tokens, -1)
    query = rotated[:, :query_width].astype(BF16)
    key_value_local = jnp.concatenate(
        [rotated[:, query_width:], query_key_value[:, query_width + key_width :]], -1
    ).astype(BF16)
    key_value = line_gather(key_value_local, "context", both=False).reshape(nc * tokens, -1)
    first = first_row.astype(jnp.int32).reshape(1)
    heads = attend_forward(first, query, key_value)

    logits = dot_nn(inputs1, router_weight)
    chosen_ids = routes[0]
    picks = (chosen_ids[:, :, None] == jnp.arange(expert_total)[None, None, :]).astype(F32)
    chosen = jnp.sum(picks * logits[:, None, :], -1)
    gates = jax.nn.softmax(chosen, axis=-1)
    gate_dense = jnp.sum(picks * gates[:, :, None], 1).T
    gate_blocks = cube_gather(gate_dense, "expert", axis_masks("expert"))
    gate_local = jnp.concatenate(
        [lax.dynamic_slice_in_dim(b, me * EXP_DEV, EXP_DEV, 0) for b in gate_blocks], 1
    )

    attn = dot_nt(heads, out_turned)
    hidden = token_rows + attn
    scale2 = lax.rsqrt(jnp.mean(hidden * hidden, -1, keepdims=True) + EPSILON)
    expert_in = (hidden * scale2 * gain_second).astype(BF16)

    rows_all = plane_gather(expert_in)
    gate_up = jnp.einsum("td,edf->etf", rows_all, w_gate_up, preferred_element_type=F32)
    gate_part, up_part = gate_up[..., :ff], gate_up[..., ff:]
    sigma = jax.nn.sigmoid(gate_part)
    silu = gate_part * sigma
    act = silu * up_part
    gate_column = gate_local[:, :, None]
    act_gated = (act * gate_column).astype(BF16)
    partial_out = jnp.einsum("etf,efd->td", act_gated, w_down, preferred_element_type=F32)
    mixture = plane_scatter(partial_out.astype(BF16), tokens)
    layer_result = (hidden + mixture).astype(BF16)

    d_act_raw = jnp.einsum("td,efd->etf", cotangent_all, w_down, preferred_element_type=F32)
    d_gates_local = jnp.sum(d_act_raw * act, -1)
    d_act = d_act_raw * gate_column
    d_gate_part = d_act * up_part * sigma * (1.0 + gate_part * (1.0 - sigma))
    d_up_part = d_act * silu
    d_gate_up = jnp.concatenate([d_gate_part, d_up_part], -1).astype(BF16)
    d_rows = jnp.einsum("etf,edf->td", d_gate_up, w_gate_up, preferred_element_type=F32)
    grad_down = jnp.einsum("td,etf->edf", cotangent_all, act_gated, preferred_element_type=F32)
    grad_gate_up = jnp.einsum("td,etf->edf", rows_all, d_gate_up, preferred_element_type=F32)

    d_expert_in = plane_scatter(d_rows.astype(BF16), tokens)
    d_gate_blocks = d_gates_local.reshape(EXP_DEV, ne, tokens)
    d_gates_dense = jnp.zeros((expert_total, tokens), F32)
    for r in range(ne):
        arrived = d_gate_blocks[:, r]
        if r:
            arrived = exchange(arrived, "expert", r)
        d_gates_dense = lax.dynamic_update_slice(d_gates_dense, arrived, ((me ^ r) * EXP_DEV, 0))
    d_gates = jnp.sum(picks * d_gates_dense.T[:, None, :], -1)
    d_chosen = gates * (d_gates - jnp.sum(gates * d_gates, -1, keepdims=True))
    d_logits = jnp.sum(picks * d_chosen[:, :, None], 1).astype(BF16)
    grad_router = dot_tn(inputs1, d_logits)

    core = lax.axis_index("dp")
    part = model_width // (nc * nd)

    def scatter_experts(grad):
        blocks = grad.reshape(EXP_DEV, nc, nd, part, -1)
        mine = cube_scatter(
            [lax.dynamic_index_in_dim(blocks, core ^ r, 2, keepdims=False) for r in range(nd)],
            "dp",
            axis_masks("dp"),
        )
        return line_scatter(
            lambda j: lax.dynamic_index_in_dim(mine, j, 1, keepdims=False), "context"
        )

    sum_gate_up = scatter_experts(grad_gate_up)
    sum_down = jnp.swapaxes(scatter_experts(grad_down), 1, 2)

    cotangent = d_out[0].astype(F32)
    scaled2 = d_expert_in * gain_second
    d_hidden = (
        cotangent
        + scale2 * scaled2
        - hidden * (scale2 * scale2 * scale2) * jnp.mean(scaled2 * hidden, -1, keepdims=True)
    )
    grad_gain_second = jnp.sum(d_expert_in * hidden * scale2, 0)
    d_attn = d_hidden.astype(BF16)
    grad_out_turned = dot_tn(d_attn, heads)
    sum_out = scatter_rows(grad_out_turned).T
    d_heads = dot_nn(d_attn, out_turned).astype(BF16)
    d_query, d_key_all, d_value_all = attend_backward(first, query, key_value, d_heads)
    d_key_value_all = jnp.concatenate([d_key_all, d_value_all], -1).reshape(nc, tokens, -1)
    d_key_value = line_scatter(
        lambda j: lax.dynamic_index_in_dim(d_key_value_all, j, 0, keepdims=False),
        "context",
        up=False,
    )
    d_rotated = rotate_back(
        jnp.concatenate([d_query, d_key_value[:, :key_width]], -1).reshape(
            tokens, -1, HEAD_DIMENSION
        ),
        cosine_values,
        sine_values,
    ).reshape(tokens, -1)
    d_qkv = jnp.concatenate([d_rotated, d_key_value[:, key_width:]], -1).astype(BF16)
    d_inputs = dot_nt(d_qkv, qkv_weight) + dot_nt(d_logits, router_weight)
    grad_gain_first = jnp.sum(d_inputs * token_rows * scale1, 0)
    grad_qkv = dot_tn(inputs1, d_qkv)
    small_grads = jnp.concatenate(
        [grad_router, grad_gain_first[:, None], grad_gain_second[:, None]], -1
    )
    small_grads = jnp.pad(small_grads, ((0, 0), (0, 128 - small_grads.shape[1])))
    sum_rows = scatter_rows(jnp.concatenate([grad_qkv, small_grads], -1))
    sum_qkv = sum_rows[:, :qkv_width]
    sum_router = sum_rows[:, qkv_width : qkv_width + expert_total]
    sum_gain_first = sum_rows[:, qkv_width + expert_total]
    sum_gain_second = sum_rows[:, qkv_width + expert_total + 1]
    scaled1 = d_inputs * gain_first
    d_input_rows = (
        d_hidden
        + scale1 * scaled1
        - token_rows
        * (scale1 * scale1 * scale1)
        * jnp.mean(scaled1 * token_rows, -1, keepdims=True)
    ).astype(BF16)
    return (
        layer_result[None],
        d_input_rows[None],
        sum_gain_first,
        sum_qkv,
        sum_out,
        sum_router,
        sum_gain_second,
        sum_gate_up,
        sum_down,
    )


def local_fused(
    layer_input,
    gain_attn,
    query_key_value_weight,
    w_out,
    w_router,
    gain_ffn,
    w_gate_up,
    w_down,
    routes,
    d_out,
):
    tokens = layer_input.shape[1]
    ne, nc, nd = sizes = tuple(lax.axis_size(a) for a in ("expert", "context", "dp"))
    expert_total = EXP_DEV * ne
    first_row = lax.axis_index("context") * tokens
    query_width = QUERY_HEADS * HEAD_DIMENSION
    key_width = KEY_VALUE_HEADS * HEAD_DIMENSION
    qkv_width = query_width + 2 * key_width

    small = jnp.concatenate([w_router, gain_attn[:, None], gain_ffn[:, None]], -1)
    small = jnp.pad(small, ((0, 0), (0, SMALL - small.shape[1])))
    cosine_values, sine_values = rope_tables(first_row + jnp.arange(tokens), HEAD_DIMENSION)
    sine_values = sine_values * jnp.where(
        jnp.arange(HEAD_DIMENSION) < HEAD_DIMENSION // 2, -1.0, 1.0
    )
    layer_result, d_x, sum_rows, sum_out, sum_gate_up, sum_down = layer(
        (
            cosine_values,
            sine_values,
            routes[0].T,
            query_key_value_weight,
            small,
            w_out.T,
            layer_input[0],
            d_out[0],
            w_gate_up,
            w_down,
        ),
        sizes,
    )[:6]
    sum_qkv, layer_result, d_x, sum_gate_up, sum_down, sum_out, sum_router, *sum_gains = finish(
        sum_rows, (layer_result, d_x, sum_gate_up, sum_down, sum_out), expert_total
    )
    return (
        layer_result[None],
        d_x[None],
        sum_gains[0][0],
        sum_qkv,
        sum_out.T,
        sum_router.T,
        sum_gains[1][0],
        sum_gate_up,
        jnp.swapaxes(sum_down, 1, 2),
    )


def solution(mesh):
    in_specs = (
        P(("expert", "dp"), "context", None),
        P(("expert", "context", "dp")),
        P(("expert", "context", "dp"), None),
        P(None, ("expert", "context", "dp")),
        P(("expert", "context", "dp"), None),
        P(("expert", "context", "dp")),
        P("expert", None, None),
        P("expert", None, None),
        P(("expert", "dp"), "context", None),
        P(("expert", "dp"), "context", None),
    )
    out_specs = (
        P(("expert", "dp"), "context", None),
        P(("expert", "dp"), "context", None),
        P(("expert", "context", "dp")),
        P(("expert", "context", "dp"), None),
        P(None, ("expert", "context", "dp")),
        P(("expert", "context", "dp"), None),
        P(("expert", "context", "dp")),
        P("expert", ("context", "dp"), None),
        P("expert", None, ("context", "dp")),
    )
    sizes = tuple(mesh.shape[a] for a in ("expert", "context", "dp"))
    local = local_fused if sizes == (4, 4, 2) else local_plain
    return jax.shard_map(local, mesh=mesh, in_specs=in_specs, out_specs=out_specs, check_vma=False)
```

```python
import functools
import math

import jax
import jax.numpy as jnp
from jax import lax
from jax.experimental import pallas as pl
from jax.experimental.pallas import tpu as pltpu
from jax.sharding import PartitionSpec as P

QUERY_HEADS = 12
KEY_VALUE_HEADS = 2
HEAD_DIMENSION = 128
TOP = 4
EXP_DEV = 2

EPSILON = 1e-06
ROPE_BASE = 10000.0
MASKED = -1e30

F32 = jnp.float32
BF16 = jnp.bfloat16


def rope_tables(positions, width):
    halfway = width // 2
    fraction = jnp.arange(halfway, dtype=jnp.float32) * (2.0 / width)
    frequency = jnp.exp(-math.log(ROPE_BASE) * fraction)
    angles = positions.astype(jnp.float32)[:, None] * frequency[None, :]
    cosine_values = jnp.cos(angles)
    sine_values = jnp.sin(angles)
    return (
        jnp.concatenate([cosine_values, cosine_values], -1),
        jnp.concatenate([sine_values, sine_values], -1),
    )


def rotate_half(values, cosine_values, sine_values):
    halfway = values.shape[-1] // 2
    turned = jnp.concatenate([-values[..., halfway:], values[..., :halfway]], -1)
    return values * cosine_values[:, None, :] + turned * sine_values[:, None, :]


def rotate_back(grads, cosine_values, sine_values):
    halfway = grads.shape[-1] // 2
    scaled = grads * sine_values[:, None, :]
    turned = jnp.concatenate([scaled[..., halfway:], -scaled[..., :halfway]], -1)
    return grads * cosine_values[:, None, :] + turned


def dot_nt(a, b):
    return lax.dot_general(a, b, (((1,), (1,)), ((), ())), preferred_element_type=F32)


def dot_tn(a, b):
    return lax.dot_general(a, b, (((0,), (0,)), ((), ())), preferred_element_type=F32)


def dot_nn(a, b):
    return jnp.dot(a, b, preferred_element_type=F32)


def masked_probs(first_row, query, key):
    scores = dot_nt(query, key) * (HEAD_DIMENSION**-0.5)
    rows = first_row + lax.broadcasted_iota(jnp.int32, scores.shape, 0)
    columns = lax.broadcasted_iota(jnp.int32, scores.shape, 1)
    scores = jnp.where(columns <= rows, scores, MASKED)
    expd = jnp.exp(scores - jnp.max(scores, axis=-1, keepdims=True))
    return expd / jnp.sum(expd, axis=-1, keepdims=True)


def attend_forward_kernel(first_ref, query_ref, key_ref, value_ref, heads_ref):
    probs = masked_probs(first_ref[0], query_ref[...], key_ref[...])
    heads_ref[...] = dot_nn(probs.astype(BF16), value_ref[...]).astype(BF16)


def attend_forward(first_row, query, key_value):
    tokens, width = query.shape
    length = key_value.shape[0]
    group = QUERY_HEADS // KEY_VALUE_HEADS
    size = HEAD_DIMENSION
    return pl.pallas_call(
        attend_forward_kernel,
        grid_spec=pltpu.PrefetchScalarGridSpec(
            num_scalar_prefetch=1,
            grid=(QUERY_HEADS,),
            in_specs=[
                pl.BlockSpec((tokens, size), lambda h, s: (0, h)),
                pl.BlockSpec((length, size), lambda h, s: (0, h // group)),
                pl.BlockSpec((length, size), lambda h, s: (0, KEY_VALUE_HEADS + h // group)),
            ],
            out_specs=pl.BlockSpec((tokens, size), lambda h, s: (0, h)),
        ),
        out_shape=jax.ShapeDtypeStruct((tokens, width), BF16),
        compiler_params=pltpu.CompilerParams(vmem_limit_bytes=32 * 1024 * 1024),
        cost_estimate=pl.CostEstimate(
            flops=4 * tokens * length * width, bytes_accessed=4 * tokens * width, transcendentals=0
        ),
    )(first_row, query, key_value, key_value)


def attend_backward_kernel(
    first_ref, query_ref, key_ref, value_ref, grad_ref, d_query_ref, d_key_ref, d_value_ref
):
    query, key, value, grad = query_ref[...], key_ref[...], value_ref[...], grad_ref[...]
    probs = masked_probs(first_ref[0], query, key)
    d_probs = dot_nt(grad, value)
    inner = jnp.sum(probs * d_probs, axis=-1, keepdims=True)
    d_raw = (probs * (d_probs - inner) * (HEAD_DIMENSION**-0.5)).astype(BF16)
    d_query_ref[...] = dot_nn(d_raw, key)
    d_key = dot_tn(d_raw, query)
    d_value = dot_tn(probs.astype(BF16), grad)

    @pl.when(pl.program_id(1) == 0)
    def _():
        d_key_ref[...] = d_key
        d_value_ref[...] = d_value

    @pl.when(pl.program_id(1) > 0)
    def _():
        d_key_ref[...] += d_key
        d_value_ref[...] += d_value


def attend_backward(first_row, query, key_value, grad):
    tokens, width = query.shape
    length = key_value.shape[0]
    group = QUERY_HEADS // KEY_VALUE_HEADS
    size = HEAD_DIMENSION
    row_spec = pl.BlockSpec((tokens, size), lambda j, g, s: (0, j * group + g))
    return pl.pallas_call(
        attend_backward_kernel,
        grid_spec=pltpu.PrefetchScalarGridSpec(
            num_scalar_prefetch=1,
            grid=(KEY_VALUE_HEADS, group),
            in_specs=[
                row_spec,
                pl.BlockSpec((length, size), lambda j, g, s: (0, j)),
                pl.BlockSpec((length, size), lambda j, g, s: (0, KEY_VALUE_HEADS + j)),
                row_spec,
            ],
            out_specs=[
                row_spec,
                pl.BlockSpec((length, size), lambda j, g, s: (0, j)),
                pl.BlockSpec((length, size), lambda j, g, s: (0, j)),
            ],
        ),
        out_shape=[
            jax.ShapeDtypeStruct((tokens, width), F32),
            jax.ShapeDtypeStruct((length, KEY_VALUE_HEADS * size), F32),
            jax.ShapeDtypeStruct((length, KEY_VALUE_HEADS * size), F32),
        ],
        compiler_params=pltpu.CompilerParams(vmem_limit_bytes=32 * 1024 * 1024),
        cost_estimate=pl.CostEstimate(
            flops=10 * tokens * length * width, bytes_accessed=8 * tokens * width, transcendentals=0
        ),
    )(first_row, query, key_value, key_value, grad)


def exchange(values, axis, mask):
    size = lax.axis_size(axis)
    return lax.ppermute(values, axis, [(i, i ^ mask) for i in range(size)])


def axis_masks(axis):
    size = lax.axis_size(axis)
    masks, bit = [], 1
    while bit < size:
        masks.append(bit)
        bit *= 2
    return masks


def cube_gather(values, axis, masks):
    held = {0: values}
    for mask in masks:
        for r, block in list(held.items()):
            held[r ^ mask] = exchange(block, axis, mask)
    return [held[r] for r in range(lax.axis_size(axis))]


def cube_scatter(blocks, axis, masks):
    held = dict(enumerate(blocks))
    for mask in masks:
        kept = {}
        for r in list(held):
            if not r & mask:
                arrived = exchange(held[r ^ mask].astype(BF16), axis, mask)
                kept[r] = held[r].astype(F32) + arrived.astype(F32)
        held = kept
    return held[0]


def line_steps(values, axis, up):
    size = lax.axis_size(axis)
    pairs = [(i, i + 1) if up else (i + 1, i) for i in range(size - 1)]
    return lax.ppermute(values, axis, pairs)


def line_gather(values, axis, both=True):
    size = lax.axis_size(axis)
    me = lax.axis_index(axis)
    result = jnp.zeros((size + 1,) + values.shape, values.dtype)
    result = lax.dynamic_update_index_in_dim(result, values, me, 0)
    up = down = values
    for step in range(1, size):
        up = line_steps(up, axis, True)
        result = lax.dynamic_update_index_in_dim(
            result, up, jnp.where(me - step >= 0, me - step, size), 0
        )
        if both:
            down = line_steps(down, axis, False)
            result = lax.dynamic_update_index_in_dim(result, down, jnp.minimum(me + step, size), 0)
    return result[:size]


def line_scatter(take, axis, up=True, down=True):
    size = lax.axis_size(axis)
    me = lax.axis_index(axis)
    total = take(me).astype(F32)
    for active, sign in ((up, 1), (down, -1)):
        if not active:
            continue
        arrived = None
        for step in range(1, size):
            block = take((me + sign * (size - step)) % size).astype(F32)
            if arrived is not None:
                block = block + arrived.astype(F32)
            arrived = line_steps(block.astype(BF16), axis, sign > 0)
        total = total + arrived.astype(F32)
    return total


def gather_rows(shard):
    ne, nc, nd = (lax.axis_size(a) for a in ("expert", "context", "dp"))
    rows, width = shard.shape
    lines = line_gather(shard, "context")
    masks = axis_masks("expert")
    half = width // 256 * 128
    parts = [lines[..., :half], lines[..., half:]]
    me = lax.axis_index("expert")
    result = jnp.zeros((ne, nc, rows, width), shard.dtype)
    for start, part, order in ((0, parts[0], masks), (half, parts[1], masks[::-1])):
        for r, block in enumerate(cube_gather(part, "expert", order)):
            result = lax.dynamic_update_slice(result, block[None], (me ^ r, 0, 0, start))
    core = lax.axis_index("dp")
    whole = jnp.zeros((ne, nc, nd, rows, width), shard.dtype)
    for r, block in enumerate(cube_gather(result, "dp", axis_masks("dp"))):
        whole = lax.dynamic_update_slice(whole, block[:, :, None], (0, 0, core ^ r, 0, 0))
    return whole.reshape(-1, width)


def scatter_rows(grad):
    ne, nc, nd = (lax.axis_size(a) for a in ("expert", "context", "dp"))
    width = grad.shape[-1]
    rows = grad.shape[0] // (ne * nc * nd)
    blocks = grad.reshape(ne, nc, nd, rows, width)
    core, me = lax.axis_index("dp"), lax.axis_index("expert")
    mine = cube_scatter(
        [
            lax.dynamic_index_in_dim(blocks, core ^ r, 2, keepdims=False)
            for r in range(nd)
        ],
        "dp",
        axis_masks("dp"),
    )
    masks = axis_masks("expert")
    half = width // 256 * 128
    sums = []
    for part, order in ((mine[..., :half], masks), (mine[..., half:], masks[::-1])):
        sums.append(
            cube_scatter(
                [lax.dynamic_index_in_dim(part, me ^ r, 0, keepdims=False) for r in range(ne)],
                "expert",
                order,
            )
        )
    lines = jnp.concatenate(sums, -1)
    return line_scatter(
        lambda j: lax.dynamic_index_in_dim(lines, j, 0, keepdims=False), "context"
    )


def plane_gather(rows):
    masks = axis_masks("expert")
    half = rows.shape[-1] // 2
    left = cube_gather(rows[:, :half], "expert", masks)
    right = cube_gather(rows[:, half:], "expert", masks[::-1])
    return jnp.concatenate([jnp.concatenate(p, -1) for p in zip(left, right)], 0)


def plane_scatter(partial, tokens):
    masks = axis_masks("expert")
    size = lax.axis_size("expert")
    half = partial.shape[-1] // 2
    blocks = partial.reshape(size, tokens, -1)
    left = cube_scatter([blocks[r, :, :half] for r in range(size)], "expert", masks)
    right = cube_scatter([blocks[r, :, half:] for r in range(size)], "expert", masks[::-1])
    return jnp.concatenate([left, right], -1)


MESH = pl.DeviceIdType.MESH
MIB = 1024 * 1024
SMALL = 128
GATE_ROWS = 16


def flip(index, mask):
    bit = 1
    while bit <= mask:
        if mask & bit:
            index = index + bit - 2 * bit * lax.rem(lax.div(index, bit), 2)
        bit *= 2
    return index


class Wire:
    def __init__(self, sends, recvs):
        self.sends, self.recvs = sends, recvs
        self.n_sends = self.n_recvs = 0
        self.open = []

    def slots(self, count):
        first = self.n_recvs
        self.n_recvs += count
        return first

    def start(self, src, dst, recv, device, when=None):
        number = self.n_sends
        self.n_sends += 1

        def copy():
            return pltpu.make_async_remote_copy(
                src_ref=src() if callable(src) else src,
                dst_ref=dst() if callable(dst) else dst,
                send_sem=self.sends.at[number],
                recv_sem=self.recvs.at[recv],
                device_id=device,
                device_id_type=MESH,
            )

        guard(when, lambda: copy().start())
        self.open.append((when, copy))

    def arrived(self, dst, recv, device):
        pltpu.make_async_remote_copy(
            src_ref=dst,
            dst_ref=dst,
            send_sem=self.sends.at[0],
            recv_sem=self.recvs.at[recv],
            device_id=device,
            device_id_type=MESH,
        ).wait_recv()

    def finish(self):
        for when, copy in self.open:
            guard(when, lambda copy=copy: copy().wait_send())
        self.open = []


def guard(when, action):
    if when is None:
        action()
    else:
        pl.when(when)(action)


def add_into(dest, source, steps=4):
    rows = dest.shape[0] // steps

    @pl.loop(0, steps)
    def _(n):
        here = pl.ds(pl.multiple_of(n * rows, rows), rows)
        dest[here] = (dest[here].astype(F32) + source[here].astype(F32)).astype(BF16)


def greet(targets):
    barrier = pltpu.get_barrier_semaphore()
    for device, when in targets:
        guard(
            when,
            lambda device=device: pl.semaphore_signal(
                barrier, inc=1, device_id=device, device_id_type=MESH
            ),
        )
    count = sum(1 if when is None else when.astype(jnp.int32) for _, when in targets)
    pl.semaphore_wait(barrier, count)


def plane_ids(e):
    return {m: {"expert": flip(e, m)} for m in (1, 2, 3)}


class RowsGather:
    def __init__(self, wire, ref, e, z, c, nc, half):
        self.wire, self.ref, self.e, self.z, self.c, self.nc = wire, ref, e, z, c, nc
        self.cols = (pl.ds(0, half), pl.ds(half, ref.shape[-1] - half))
        self.line = wire.slots(nc)
        self.plane = wire.slots(nc * 6)
        self.core = wire.slots(nc)
        self.ids = plane_ids(e)

    def go(self, *steps):
        for step in steps:
            action = {"l": self.pass_on, "s": self.spread, "f": self.forward, "h": self.share, "c": self.complete}
            action[step[0]](*map(int, step[1:]))

    def shard(self, k):
        if k < 2:
            return flip(self.z, k)
        inner = (self.z > 0) & (self.z < self.nc - 1)
        return jnp.where(inner, flip(self.z, 5 - k), flip(self.z, k))

    def at(self, r, zs, half):
        return self.ref.at[flip(self.e, r), zs, self.c, :, self.cols[half]]

    def slot(self, k, r, half):
        return self.plane + k * 6 + (r - 1) * 2 + half

    def pass_on(self, k):
        wire, z, nc = self.wire, self.z, self.nc
        zs = self.shard(k)
        whole = self.ref.at[self.e, zs, self.c]
        if k:
            wire.arrived(whole, self.line + zs, {"context": zs})
        wire.start(
            whole, whole, self.line + zs, {"context": z + 1}, when=(zs <= z) & (z < nc - 1)
        )
        wire.start(whole, whole, self.line + zs, {"context": z - 1}, when=(zs >= z) & (z > 0))

    def spread(self, k):
        zs = self.shard(k)
        for half, mask in ((0, 1), (1, 2), (1, 1), (0, 2)):
            part = self.at(0, zs, half)
            self.wire.start(part, part, self.slot(k, mask, half), self.ids[mask])

    def forward(self, k):
        zs = self.shard(k)
        for half, mask in ((0, 1), (1, 2)):
            part = self.at(mask, zs, half)
            self.wire.arrived(part, self.slot(k, mask, half), self.ids[mask])
            self.wire.start(part, part, self.slot(k, 3, half), self.ids[3 - mask])

    def share(self, k):
        zs = self.shard(k)
        for r, half in ((1, 1), (2, 0), (3, 0), (3, 1)):
            self.wire.arrived(self.at(r, zs, half), self.slot(k, r, half), self.ids[r])
        part = self.ref.at[:, zs, self.c]
        self.wire.start(part, part, self.core + k, {"dp": 1 - self.c})

    def complete(self):
        for k in range(self.nc):
            zs = self.shard(k)
            self.wire.arrived(self.ref.at[:, zs, 1 - self.c], self.core + k, {"dp": 1 - self.c})


class PlaneGather:
    def __init__(self, wire, ref, e, own=None):
        self.wire, self.ref, self.own = wire, ref, own
        self.half = ref.shape[-1] // 2
        self.ids = plane_ids(e)
        self.first = wire.slots(6)

    def at(self, r, half):
        columns = pl.ds(half * self.half, self.half)
        if r == 0 and self.own is not None:
            return self.own.at[:, columns]
        return self.ref.at[r, :, columns]

    def slot(self, r, half):
        return self.first + (r - 1) * 2 + half

    def send(self, r, half, to, mask):
        self.wire.start(
            lambda: self.at(r, half), lambda: self.at(to, half), self.slot(to, half), self.ids[mask]
        )

    def spread(self):
        for half, mask in ((0, 1), (1, 2), (1, 1), (0, 2)):
            self.send(0, half, mask, mask)

    def forward(self):
        for half, mask in ((0, 1), (1, 2)):
            self.wire.arrived(self.at(mask, half), self.slot(mask, half), self.ids[mask])
            self.send(mask, half, 3, 3 - mask)

    def near(self, r):
        half = 1 if r == 1 else 0
        self.wire.arrived(self.at(r, half), self.slot(r, half), self.ids[r])

    def far(self):
        for half in (0, 1):
            self.wire.arrived(self.at(3, half), self.slot(3, half), self.ids[3])

    def complete(self):
        self.near(1)
        self.near(2)
        self.far()


def causal(scores, first_row):
    place = lax.broadcasted_iota(jnp.int32, scores.shape, 0)
    row = first_row + lax.broadcasted_iota(jnp.int32, scores.shape, 1)
    return jnp.where(place <= row, scores, MASKED)


def swap_halves(values):
    return pltpu.roll(values, HEAD_DIMENSION // 2, 1)


class PlaneScatter:
    def __init__(self, wire, land, ids):
        self.wire, self.land, self.ids, self.part = wire, land, ids, None
        self.half = land.shape[-1]
        self.first = wire.slots(6)

    def send(self, source, mask, slot):
        self.wire.start(source, lambda: self.land.at[slot], self.first + slot, self.ids[mask])

    def near(self, r):
        self.send(self.part(r, r - 1), r, r - 1)

    def far(self):
        self.send(self.part(3, 0), 1, 2)
        self.send(self.part(3, 1), 2, 3)

    def relay(self, part=None):
        for half, r in ((0, 2), (1, 1)):
            slot = 2 + half
            self.wire.arrived(self.land.at[slot], self.first + slot, self.ids[3 - r])
            take = part or self.part
            mine = take(r, half)
            add_into(mine, self.land.at[slot])
            self.send(lambda r=r, half=half, take=take: take(r, half), r, 4 + half)

    def total(self, own):
        for slot, half, mask in ((0, 0, 1), (1, 1, 2), (4, 0, 2), (5, 1, 1)):
            self.wire.arrived(self.land.at[slot], self.first + slot, self.ids[mask])
            columns = pl.ds(half * self.half, self.half)
            rows = own.shape[0] // 4

            @pl.loop(0, 4)
            def _(n):
                here = pl.ds(pl.multiple_of(n * rows, rows), rows)
                own[here, columns] += self.land[slot, here].astype(F32)


class LineSum:
    def __init__(self, wire, block, land, z, nc, up=True):
        self.wire, self.block, self.land, self.z, self.nc, self.up = wire, block, land, z, nc, up
        self.first = wire.slots(nc)

    def clear(self):
        for slot in range(self.nc):

            def zero(slot=slot):
                self.land[slot] = jnp.zeros(self.land.shape[1:], BF16)

            pl.when(slot == self.z if self.up else slot <= self.z)(zero)

    def send(self):
        z = self.z
        for d in range(self.nc - 1, 0, -1):
            self.leave(z - d, z >= d)
            if self.up:
                self.leave(z + d, z + d < self.nc)

    def leave(self, j, wanted):
        self.wire.start(
            self.block(j), self.land.at[self.z], self.first + self.z, {"context": j}, when=wanted
        )

    def total(self):
        z = self.z
        for d in range(1, self.nc):
            for source, wanted in ((z + d, z + d < self.nc), (z - d, z >= d))[: 1 + self.up]:

                def wait(source=source):
                    self.wire.arrived(
                        self.land.at[source], self.first + source, {"context": source}
                    )

                pl.when(wanted)(wait)
        total = self.block(z)[...].astype(F32)
        for slot in range(self.nc):
            total = total + self.land[slot].astype(F32)
        return total


class RowsScatter:
    def __init__(self, wire, buf, core, plane, lines, e, z, c, nc, start, width, half):
        self.wire, self.buf, self.core, self.plane = wire, buf, core, plane
        self.e, self.c = e, c
        self.all = pl.ds(start, width)
        self.cols = (pl.ds(start, half), pl.ds(start + half, width - half))
        self.ids = plane_ids(e)
        self.core_slot = wire.slots(1)
        self.first = wire.slots(6)
        rows = buf.shape[2] // nc
        self.line = LineSum(
            wire,
            lambda j: buf.at[c, e, pl.ds(pl.multiple_of(j * rows, rows), rows), self.all],
            lines,
            z,
            nc,
        )

    def share(self):
        self.wire.start(
            self.buf.at[1 - self.c, :, :, self.all], self.core, self.core_slot, {"dp": 1 - self.c}
        )

    def at(self, r, half):
        return self.buf.at[self.c, flip(self.e, r), :, self.cols[half]]

    def send(self, r, half, mask, slot):
        self.wire.start(
            self.at(r, half), self.plane(slot, half), self.first + slot, self.ids[mask]
        )

    def merge(self, before=None):
        self.wire.arrived(self.core, self.core_slot, {"dp": 1 - self.c})
        for r in (3, 1, 2, 0):
            block = flip(self.e, r)
            part = self.buf.at[self.c, block, :, self.all]
            add_into(part, self.core.at[block])
            if r == 3:
                if before is not None:
                    before()
                self.send(3, 0, 1, 2)
                self.send(3, 1, 2, 3)
            elif r:
                self.send(r, r - 1, r, r - 1)

    def add(self, r, half, slot, mask):
        land = self.plane(slot, half)
        self.wire.arrived(land, self.first + slot, self.ids[mask])
        add_into(self.at(r, half), land)

    def relay(self):
        for half, r in ((0, 2), (1, 1)):
            self.add(r, half, 2 + half, 3 - r)
            self.send(r, half, r, 4 + half)

    def total(self):
        for slot, half, mask in ((0, 0, 1), (1, 1, 2), (4, 0, 2), (5, 1, 1)):
            self.add(0, half, slot, mask)


class ExpertLine:
    def __init__(self, wire, base, land, sems, z, nc):
        self.wire, self.base, self.land = wire, base, land
        self.ins, self.out, self.sems, self.z, self.nc = None, None, sems, z, nc
        self.end = (z == 0) | (z == nc - 1)
        self.inner = jnp.logical_not(self.end)
        self.width = base.shape[-1] // EXP_DEV
        self.first = wire.slots((nc + 1) * EXP_DEV)
        self.sent = []

    def part(self, ref, j, i):
        return ref.at[j, :, pl.ds(i * self.width, self.width)]

    def combine(self, sources, stores):
        out, step = self.out, self.ins.shape[2]
        count = sources[0].shape[0] // step

        def loads(p):
            rows = pl.ds(p * step, step)
            return [
                pltpu.make_async_copy(source.at[rows], self.ins.at[k, p], self.sems.at[4 * k + p])
                for k, source in enumerate(sources)
            ]

        def store(p):
            pairs = stores(pl.ds(p * step, step), out.at[p % 2])
            return [
                pltpu.make_async_copy(source, dest, self.sems.at[16 + 2 * n + p % 2])
                for n, (source, dest) in enumerate(pairs)
            ]

        for p in range(count):
            for copy in loads(p):
                copy.start()
        for p in range(count):
            for copy in loads(p):
                copy.wait()
            if p > 1:
                for copy in store(p - 2):
                    copy.wait()
            total = self.ins[0, p].astype(F32)
            for k in range(1, len(sources)):
                total = total + self.ins[k, p].astype(F32)
            out[p % 2] = total.astype(out.dtype)
            for copy in store(p):
                copy.start()
        for p in range(max(0, count - 2), count):
            for copy in store(p):
                copy.wait()

    def copy(self, i, r, number):
        target, slot = flip(self.z, r), self.z
        if r == 3:
            target = jnp.where(self.end, flip(self.z, 1), target)
            slot = jnp.where(self.end, self.nc, slot)
        return pltpu.make_async_remote_copy(
            src_ref=self.part(self.base, flip(self.z, r), i),
            dst_ref=self.part(self.land, slot, i),
            send_sem=self.wire.sends.at[number],
            recv_sem=self.wire.recvs.at[self.first + slot * EXP_DEV + i],
            device_id={"context": target},
            device_id_type=MESH,
        )

    def send(self, i, r, when=None):
        number = len(self.sent)
        guard(when, self.copy(i, r, number).start)
        self.sent.append((when, i, r, number))

    def finish(self):
        for when, i, r, number in self.sent:
            guard(when, self.copy(i, r, number).wait_send)

    def arrived(self, slot, i):
        land = self.part(self.land, slot, i)
        self.wire.arrived(land, self.first + slot * EXP_DEV + i, {"context": self.z})

    def relay_loads(self, i, p):
        step = self.ins.shape[2]
        rows = pl.ds(p * step, step)
        sources = (self.part(self.base, flip(self.z, 2), i), self.part(self.land, self.nc, i))
        return [
            pltpu.make_async_copy(
                source.at[rows], self.ins.at[k, p], self.sems.at[4 * k + p]
            )
            for k, source in enumerate(sources)
        ]

    def relay_store(self, i, p):
        step = self.ins.shape[2]
        mine = self.part(self.base, flip(self.z, 2), i).at[pl.ds(p * step, step)]
        return pltpu.make_async_copy(self.ins.at[0, p], mine, self.sems.at[16 + p])

    def relay_steps(self):
        return range(self.base.shape[1] // self.ins.shape[2])

    def relay_begin(self, i):
        self.relayed = i

        def begin():
            self.arrived(self.nc, i)
            for p in self.relay_steps():
                for copy in self.relay_loads(i, p):
                    copy.start()

        pl.when(self.inner)(begin)

    def relay_add(self):
        i = self.relayed

        def add():
            for p in self.relay_steps():
                for copy in self.relay_loads(i, p):
                    copy.wait()
                a, b = (self.ins[k, p].astype(F32) for k in range(2))
                self.ins[0, p] = (a + b).astype(BF16)
                self.relay_store(i, p).start()

        pl.when(self.inner)(add)

    def relay_send(self, i):
        def wait():
            for p in self.relay_steps():
                self.relay_store(i, p).wait()

        pl.when(self.inner)(wait)
        self.send(i, 2, when=self.inner)

    def last(self, i, results):
        z = self.z
        sources = [self.part(self.base, z, i)]
        for r in (1, 2):
            self.arrived(flip(z, r), i)
            sources.append(self.part(self.land, flip(z, r), i))

        def stores(rows, wide):
            pairs, first = [], 0
            for result in results:
                columns = pl.ds(first, result.shape[-1])
                pairs.append((wide.at[:, columns], result.at[i, rows]))
                first += result.shape[-1]
            return pairs

        pl.when(self.end)(lambda: self.combine(sources, stores))

        def inner():
            self.arrived(flip(z, 3), i)
            self.combine(sources + [self.part(self.land, flip(z, 3), i)], stores)

        pl.when(self.inner)(inner)


def layer_kernel(
    nc,
    experts,
    cos_ref,
    sin_ref,
    routes_ref,
    qkv_ref,
    small_ref,
    wo_shard_ref,
    x_hbm,
    d_out_hbm,
    w_gu_hbm,
    w_dn_hbm,
    layer_hbm,
    d_x_hbm,
    sum_q_ref,
    sum_o_ref,
    sum_gu_hbm,
    sum_dn_hbm,
    base_hbm,
    land_hbm,
    y_hbm,
    wq_hbm,
    wo_hbm,
    cot_hbm,
    inputs_hbm,
    query_hbm,
    heads_hbm,
    hidden_hbm,
    wk_all,
    kv_ref,
    gate_all,
    gates_ref,
    gains_ref,
    x_all,
    y_land,
    dx_land,
    core_land,
    plane_q,
    plane_k,
    lines_o,
    lines_q,
    lines_k,
    dkv_land,
    d_in_ref,
    dg_lanes,
    dg_part,
    dg_land,
    sends_f,
    recvs_f,
    sends_c,
    recvs_c,
    sends_x,
    recvs_x,
    sends_1,
    recvs_1,
    sends_2,
    recvs_2,
    sends_e,
    recvs_e,
    hand_sends,
    hand_recvs,
    stage_sems,
    load_sems,
    out_sems,
    sum_sems,
    y_sems,
    credits,
):
    e, z, c = (lax.axis_index(a) for a in ("expert", "context", "dp"))
    size = HEAD_DIMENSION
    blocks, tokens, width = cot_hbm.shape
    ff = w_dn_hbm.shape[1]
    query_width = QUERY_HEADS * size
    key_width = KEY_VALUE_HEADS * size
    qkv_width = query_width + 2 * key_width
    rest = wk_all.shape[-1]
    grad_width = base_hbm.shape[-1]
    ids = plane_ids(e)
    sibling = {"dp": 1 - c}
    bottom, even, odd, top = z == 0, lax.rem(z, 2) == 0, lax.rem(z, 2) == 1, z == nc - 1
    wire_1, wire_2, wire_e = Wire(sends_1, recvs_1), Wire(sends_2, recvs_2), Wire(sends_e, recvs_e)
    expert = ExpertLine(wire_e, base_hbm, land_hbm, sum_sems, z, nc)
    wire_c = Wire(sends_c, recvs_c)
    gather_cot = PlaneGather(wire_c, cot_hbm, e, d_out_hbm)
    wire_x = Wire(sends_x, recvs_x)
    gather = PlaneGather(wire_x, x_all, e)
    scatter_dx = PlaneScatter(wire_1, dx_land, ids)
    scatter_y = PlaneScatter(wire_2, y_land, ids)
    dg_slot = wire_1.slots(3)

    def front_phase(wq_ref, wo_ref, x_ref, inputs_ref, query_ref, heads_ref, hidden_ref, kv_scr, q_scr):
        wire = Wire(sends_f, recvs_f)
        kv_width = 2 * key_width
        load_x = pltpu.make_async_copy(x_hbm, x_ref, load_sems.at[0])
        load_x.start()
        wq_ref[e, z, c] = qkv_ref[:, pl.ds(0, query_width)]
        wo_ref[e, z, c] = wo_shard_ref[...]
        wk_all[e, z, c, :, pl.ds(0, kv_width)] = qkv_ref[:, pl.ds(query_width, kv_width)]
        wk_all[e, z, c, :, pl.ds(kv_width, SMALL)] = small_ref[...]
        greet(
            [(ids[m], None) for m in (1, 2, 3)]
            + [(sibling, None)]
            + [({"context": z + d}, z + d < nc) for d in range(1, nc)]
            + [({"context": z - d}, z >= d) for d in range(1, nc)]
        )
        gather_k = RowsGather(wire, wk_all, e, z, c, nc, 256)
        gather_q = RowsGather(wire, wq_ref, e, z, c, nc, 768)
        gather_o = RowsGather(wire, wo_ref, e, z, c, nc, 768)
        gather_k.go("l0", "s0")
        gather_q.go("s0")
        gather_k.go("l1", "s1", "f0", "l2", "s2")
        gather_q.go("l0")
        gather_k.go("f1", "h0", "l3", "s3")
        gather_q.go("l1", "s1")
        gather_o.go("l0")
        gather_k.go("f2", "h1", "f3")
        gather_q.go("l2", "s2")
        gather_k.go("h2")
        gather_o.go("l1")
        gather_q.go("f0")
        gather_k.go("h3")
        gather_q.go("l3", "s3")
        gather_k.go("c")
        load_x.wait()
        rows = x_ref[...].astype(F32)
        scale1 = lax.rsqrt(jnp.mean(rows * rows, -1, keepdims=True) + EPSILON)

        small = wk_all[:, :, :, :, pl.ds(kv_width, SMALL)].reshape(width, SMALL)
        small = jnp.transpose(small.astype(F32))
        gain_first, gain_second = small[experts : experts + 1], small[experts + 1 : experts + 2]
        gains_ref[0:1] = gain_first
        gains_ref[1:2] = gain_second
        inputs_ref[...] = (rows * scale1 * gain_first).astype(BF16)
        kv_scr[...] = dot_nn(inputs_ref[...], wk_all[...].reshape(width, kv_width + SMALL))

        def turned(head):
            return (head * cos_ref[...] + swap_halves(head) * sin_ref[...]).astype(BF16)

        line = wire.slots(KEY_VALUE_HEADS * nc)
        for j in range(KEY_VALUE_HEADS):
            kv_ref[j, z, :, pl.ds(0, size)] = turned(kv_scr[:, pl.ds(j * size, size)])
            value = kv_scr[:, pl.ds(kv_width // 2 + j * size, size)]
            kv_ref[j, z, :, pl.ds(size, size)] = value.astype(BF16)
            mine = kv_ref.at[j, z]
            for d in range(nc - 1, 0, -1):
                wire.start(mine, mine, line + j * nc + z, {"context": z + d}, when=z + d < nc)

        def keys_here(j):
            for d in range(1, nc):

                def wait(d=d):
                    wire.arrived(kv_ref.at[j, z - d], line + j * nc + z - d, {"context": z - d})

                pl.when(z >= d)(wait)

        outs = [
            pltpu.make_async_copy(source, dest, out_sems.at[n])
            for n, (source, dest) in enumerate(
                (
                    (inputs_ref, inputs_hbm),
                    (query_ref, query_hbm),
                    (heads_ref, heads_hbm),
                    (hidden_ref, hidden_hbm),
                    (wq_ref, wq_hbm),
                    (wo_ref, wo_hbm),
                )
            )
        ]
        outs[0].start()
        for later in range(1, nc):

            def clear(later=later):
                for j in range(KEY_VALUE_HEADS):
                    kv_ref[j, z + later] = jnp.zeros(kv_ref.shape[2:], BF16)

            pl.when(z + later < nc)(clear)
        gather_q.go("f1", "f2", "h0")
        gather_o.go("s0")
        gather_q.go("f3", "h1")
        gather_o.go("s1")
        gather_q.go("h2", "h3", "c")
        outs[4].start()
        gather_o.go("f0", "f1")
        gather_cot.spread()

        @pl.loop(0, query_width // 256)
        def _(n):
            columns = pl.ds(pl.multiple_of(n * 256, 256), 256)
            q_scr[:, columns] = dot_nn(
                inputs_ref[...], wq_ref[:, :, :, :, columns].reshape(width, 256)
            )

        @pl.loop(0, QUERY_HEADS)
        def _(h):
            columns = pl.ds(pl.multiple_of(h * size, size), size)
            query_ref[:, columns] = turned(q_scr[:, columns])

        outs[1].start()

        logits = kv_scr[:, pl.ds(kv_width, SMALL)]
        lanes = lax.broadcasted_iota(jnp.int32, logits.shape, 1)
        routes = jnp.concatenate(
            [routes_ref[...].astype(F32), jnp.zeros((SMALL - TOP, tokens), F32)], 0
        )
        routes = jnp.transpose(routes).astype(jnp.int32)
        named = lanes == routes[:, 0:1]
        for k in range(1, TOP):
            named = named | (lanes == routes[:, k : k + 1])
        logits = jnp.where(named, logits, MASKED)
        expd = jnp.exp(logits - jnp.max(logits, -1, keepdims=True))
        gates = expd / jnp.sum(expd, -1, keepdims=True)
        gate_all[0] = jnp.transpose(gates)[:GATE_ROWS]
        gate_slot = wire.slots(3)
        for r in (1, 2, 3):
            wire.start(gate_all.at[0], gate_all.at[r], gate_slot + r - 1, ids[r])

        length = nc * tokens
        group = QUERY_HEADS // KEY_VALUE_HEADS

        def attend(first, last):
            j = first // group
            key = kv_ref[j, :, :, pl.ds(0, size)].reshape(length, size)
            value = kv_ref[j, :, :, pl.ds(size, size)].reshape(length, size)
            value_turned = jnp.transpose(value)

            @pl.loop(first, last)
            def _(h):
                column = pl.multiple_of(h * size, size)
                scores = causal(dot_nt(key, query_ref[:, pl.ds(column, size)]), z * tokens)
                largest = jnp.max(scores, 0, keepdims=True)
                expd = jnp.exp((scores - largest) * (size**-0.5))
                total = jnp.sum(expd, 0, keepdims=True)
                mixed = dot_nn(value_turned, expd.astype(BF16)) / total
                heads_ref[:, pl.ds(column, size)] = jnp.transpose(mixed).astype(BF16)

        half = group // 2
        keys_here(0)
        attend(0, half)
        gather_o.go("l2", "s2")
        attend(half, group)
        gather_o.go("l3", "s3", "f2", "h0")
        keys_here(1)
        attend(group, group + half)
        gather_o.go("f3", "h1")
        attend(group + half, QUERY_HEADS)
        gather_o.go("h2")
        gather_cot.forward()
        gather_o.go("h3", "c")
        outs[5].start()
        outs[2].start()
        part = width // wo_ref.shape[0]
        for block in range(wo_ref.shape[0]):
            weight = wo_ref[block].reshape(part, width)
            columns = pl.ds(block * part, part)
            hidden_ref[:, columns] = x_ref[:, columns].astype(F32) + dot_nt(heads_ref[...], weight)
        hidden = hidden_ref[...]
        scale2 = lax.rsqrt(jnp.mean(hidden * hidden, -1, keepdims=True) + EPSILON)
        x_all[0] = (hidden * scale2 * gains_ref[1:2]).astype(BF16)
        gather.spread()
        outs[3].start()
        for r in (1, 2, 3):
            wire.arrived(gate_all.at[r], gate_slot + r - 1, ids[r])
        for r in range(gate_all.shape[0]):
            zeros = jnp.zeros((SMALL - GATE_ROWS, tokens), F32)
            turned_gates = jnp.transpose(jnp.concatenate([gate_all[r], zeros], 0))
            both = [
                jnp.sum(jnp.where(lanes == e * EXP_DEV + i, turned_gates, 0.0), -1, keepdims=True)
                for i in range(EXP_DEV)
            ]
            gates_ref[r] = jnp.where(lanes == 0, both[0], jnp.where(lanes == 1, both[1], 0.0))
        for copy in outs:
            copy.wait()
        wire.finish()

    def token_phase(w_gu, w_dn, cot_all, a_all, dgu_all, y_stage, stage, ins, x_turned):
        expert.ins = ins
        scatter_dx.part = lambda r, half: x_all.at[r, :, pl.ds(half * width // 2, width // 2)]
        sources = [
            (w_gu_hbm.at[0], w_gu.at[0]),
            (w_dn_hbm.at[0], w_dn.at[0]),
            (d_out_hbm, cot_all.at[0]),
            (w_gu_hbm.at[1], w_gu.at[1]),
            (w_dn_hbm.at[1], w_dn.at[1]),
            (cot_hbm.at[1:], cot_all.at[1:]),
        ]
        loads = [
            pltpu.make_async_copy(source, dest, load_sems.at[n])
            for n, (source, dest) in enumerate(sources)
        ]
        for copy in loads[:5]:
            copy.start()
        step = 256
        wide = 512
        dg_lanes[...] = jnp.zeros_like(dg_lanes)

        def hidden_units(r, i, count=1):
            lane = lax.broadcasted_iota(jnp.int32, (1, SMALL), 1)
            here = pl.ds(r, count)
            flat = count * tokens

            @pl.loop(0, ff // step)
            def _(f):
                column = pl.multiple_of(f * step, step)
                rows = x_all[here].reshape(flat, width)
                grads = cot_all[here].reshape(flat, width)
                gate_part = dot_nn(rows, w_gu[i, :, pl.ds(column, step)])
                up_part = dot_nn(rows, w_gu[i, :, pl.ds(ff + column, step)])
                raw = dot_nt(grads, w_dn[i, pl.ds(column, step), :])
                gate = gates_ref[here].reshape(flat, SMALL)
                gate = jnp.sum(jnp.where(lane == i, gate, 0.0), -1, keepdims=True)
                sigma = jax.nn.sigmoid(gate_part)
                silu = gate_part * sigma
                act = silu * up_part
                lanes = lax.broadcasted_iota(jnp.int32, (flat, SMALL), 1)
                d_gate = jnp.where(
                    lanes == e * EXP_DEV + i, jnp.sum(act * raw, -1, keepdims=True), 0.0
                )
                dg_lanes[here] += d_gate.reshape(count, tokens, SMALL)

                def put(ref, first, values):
                    values = values.astype(BF16).reshape(count, tokens, step)
                    ref[here, :, pl.ds(pl.multiple_of(first, step), step)] = values

                put(a_all, i * ff + column, act * gate)
                d_act = raw * gate
                d_gate_part = d_act * up_part * sigma * (1.0 + gate_part * (1.0 - sigma))
                put(dgu_all, i * 2 * ff + column, d_gate_part)
                put(dgu_all, i * 2 * ff + ff + column, d_act * silu)

        def turn(r):
            @pl.loop(0, width // wide)
            def _(n):
                columns = pl.ds(pl.multiple_of(n * wide, wide), wide)
                x_turned[columns, pl.ds(r * tokens, tokens)] = jnp.transpose(x_all[r, :, columns])

        def y_copy(r):
            return pltpu.make_async_copy(y_stage.at[r % 2], y_hbm.at[r], y_sems.at[r % 2])

        def outputs(r, count=1):
            here = pl.ds(r, count)
            flat = count * tokens

            @pl.loop(0, width // wide)
            def _(n):
                columns = pl.ds(pl.multiple_of(n * wide, wide), wide)
                low = dgu_all[here].reshape(flat, EXP_DEV * 2 * ff)
                d_rows = dot_nt(low[:, : 2 * ff], w_gu[0, columns, :])
                d_rows += dot_nt(low[:, 2 * ff :], w_gu[1, columns, :])
                weight = w_dn[:, :, columns].reshape(EXP_DEV * ff, wide)
                out = dot_nn(a_all[here].reshape(flat, EXP_DEV * ff), weight).astype(BF16)
                for k in range(count):
                    rows = slice(k * tokens, (k + 1) * tokens)
                    y_stage[(r + k) % 2, :, columns] = out[rows]
                    if r == 0:
                        d_in_ref[:, columns] = d_rows
                    else:
                        x_all[r + k, :, columns] = d_rows[rows].astype(BF16)

            for k in range(r, r + count):
                y_copy(k).start()
                dg_part[k] = jnp.transpose(dg_lanes[k])[:GATE_ROWS]
                if k:
                    wire_1.start(dg_part.at[k], dg_land.at[k - 1], dg_slot + k - 1, ids[k])

        half_rows = width // nc // 2
        def where(k):
            high = lax.rem(lax.div(z, 2) + 1 + lax.div(k, 2), 2)
            return 2 * high + lax.rem(z + 1 + k, 2)

        def keep(i, k):
            slot = lax.rem(k, 2)
            return pltpu.make_async_copy(
                stage.at[slot, c], expert.part(base_hbm, where(k), i), stage_sems.at[slot]
            )

        def hand(i, k):
            return pltpu.make_async_remote_copy(
                src_ref=stage.at[lax.rem(k, 2), 1 - c],
                dst_ref=core_land.at[k],
                send_sem=hand_sends.at[i * nc + k],
                recv_sem=hand_recvs.at[i * nc + k],
                device_id=sibling,
                device_id_type=MESH,
            )

        def settle(i, k):
            hand(i, k).wait_recv()
            add_into(stage.at[lax.rem(k, 2), c], core_land.at[k])
            keep(i, k).start()

        def clear(i, k):
            keep(i, k).wait()
            hand(i, k).wait_send()

        def leave(i, r):
            if i == 0 and r == 2:
                expert.send(i, r, when=expert.end)
            elif i == 0 and r == 1 or r == 3:
                expert.send(i, r)
            elif r == 2:
                expert.send(i, r, when=bottom)
            elif r == 1:
                expert.send(i, r, when=even)

        def weight_grads(i, between=lambda k: None):
            @pl.loop(0, nc)
            def _(k):
                @pl.when(k >= 2)
                def _():
                    clear(i, k - 2)

                for n in (2, 3):

                    @pl.when(k == n)
                    def _(n=n):
                        leave(i, 5 - n)

                rows_at = pl.ds(pl.multiple_of(where(k) * 2 * half_rows, 2 * half_rows), 2 * half_rows)
                grads = cot_all[:, :, rows_at].reshape(blocks * tokens, 2 * half_rows)
                for first, rows, grad, start, count in (
                    (0, x_turned[rows_at, :], dgu_all, i * 2 * ff, 2),
                    (2 * ff, jnp.transpose(grads), a_all, i * ff, 1),
                ):

                    @pl.loop(0, count)
                    def _(n):
                        column = pl.multiple_of(n * ff, ff)
                        part = grad[:, :, pl.ds(pl.multiple_of(start + column, ff), ff)]
                        result = dot_nn(rows, part.reshape(blocks * tokens, ff)).astype(BF16)
                        stage[lax.rem(k, 2), :, :, pl.ds(pl.multiple_of(first + column, ff), ff)] = (
                            result.reshape(2, half_rows, ff)
                        )

                if i:

                    @pl.when(k == 0)
                    def _():
                        pl.semaphore_wait(credits.at[3], 1)

                hand(i, k).start()

                @pl.when(k >= 1)
                def _():
                    settle(i, k - 1)

                between(k)

        for copy in loads[:3]:
            copy.wait()
        gather_cot.complete()
        loads[5].start()
        for copy in loads[3:5]:
            copy.wait()

        @pl.loop(0, EXP_DEV)
        def _(i):
            hidden_units(0, i)

        gather.forward()
        outputs(0)
        loads[5].wait()
        turn(0)
        gather.near(1)
        gather.near(2)
        turn(1)
        turn(2)
        hidden_units(1, 0, 2)
        gather.far()
        turn(3)
        hidden_units(3, 0)
        weight_grads(0)
        hidden_units(1, 1, 2)
        clear(0, nc - 2)
        leave(0, 1)
        settle(0, nc - 1)
        pl.semaphore_signal(credits.at[3], inc=1, device_id=sibling, device_id_type=MESH)
        y_copy(0).wait()
        wire_x.finish()
        outputs(1, 2)
        scatter_dx.near(1)
        scatter_dx.near(2)
        hidden_units(3, 1)
        expert.relay_begin(0)
        y_copy(1).wait()
        outputs(3)
        scatter_dx.far()
        clear(0, nc - 1)
        expert.relay_add()

        def between(k):
            @pl.when(k == 0)
            def _():
                expert.relay_send(0)

            @pl.when(k == 1)
            def _():
                scatter_dx.relay()

        weight_grads(1, between)
        scatter_dx.total(d_in_ref)
        for r in (1, 2):
            pl.semaphore_signal(credits.at[r], inc=1, device_id=ids[r], device_id_type=MESH)
        settle(1, nc - 1)
        for k in (nc - 2, nc - 1):
            clear(1, k)
        leave(1, 1)
        y_copy(3).wait()
        y_copy(2).wait()
        wire_1.finish()
        wire_c.finish()
        pl.semaphore_signal(credits.at[0], inc=1, device_id=sibling, device_id_type=MESH)

    def token_rows_phase(
        weight,
        grads_o,
        grads_q,
        x_ref,
        inputs_ref,
        query_ref,
        heads_ref,
        hidden_ref,
        d_hidden_ref,
        d_attn_ref,
        d_heads_ref,
        d_all_ref,
        rows_ref,
        dkv_acc,
        dkv_ref,
        y_relay,
        ins,
        out_wide,
    ):
        expert.ins, expert.out = ins, out_wide
        cot_ref, d_inputs_ref = d_heads_ref, hidden_ref
        scatter_y.part = lambda r, half: y_hbm.at[r, :, pl.ds(half * width // 2, width // 2)]
        y_loads = [
            pltpu.make_async_copy(scatter_y.part(2 - half, half), y_relay.at[half], y_sems.at[half])
            for half in range(2)
        ]
        for copy in y_loads:
            copy.start()
        planes = grads_o.shape[1]
        part = width // planes
        sources = (
            (hidden_hbm, hidden_ref),
            (d_out_hbm, cot_ref),
            (wo_hbm, weight),
            (heads_hbm, heads_ref),
            (query_hbm, query_ref),
            (x_hbm, x_ref),
            (inputs_hbm, inputs_ref),
        )
        loads = [
            pltpu.make_async_copy(source, dest, load_sems.at[4 + n])
            for n, (source, dest) in enumerate(sources)
        ]
        for copy in loads:
            copy.start()
        for r in (1, 2):
            scatter_y.near(r)
        scatter_y.far()

        def rows_scatter(buf, core, plane, lines, start, count, half):
            return RowsScatter(
                wire_2,
                buf,
                core,
                plane,
                lines,
                e,
                z,
                c,
                nc,
                start,
                count,
                half,
            )

        rows_of = part // 2
        scatter_o = rows_scatter(
            grads_o,
            x_all.at[:, pl.ds(0, rows_of)],
            lambda slot, half: dx_land.at[slot, pl.ds(0, rows_of)],
            lines_o,
            0,
            width,
            width // 2,
        )
        scatter_q = rows_scatter(
            grads_q,
            core_land.at[:, :, pl.ds(0, query_width)],
            lambda slot, half: plane_q.at[slot],
            lines_q,
            0,
            query_width,
            query_width // 2,
        )
        rest_half = rest // 256 * 128
        scatter_k = rows_scatter(
            grads_q,
            core_land.at[:, :, pl.ds(query_width, rest)],
            lambda slot, half: plane_k.at[
                slot, :, pl.ds(0, rest - rest_half if half else rest_half)
            ],
            lines_k,
            query_width,
            rest,
            rest_half,
        )
        scatter_kv = [
            LineSum(wire_2, lambda j, h=h: dkv_ref.at[h, j], dkv_land.at[h], z, nc, up=False)
            for h in range(KEY_VALUE_HEADS)
        ]

        for scatter in (scatter_o, scatter_q, scatter_k):
            scatter.line.clear()
        for line in scatter_kv:
            line.clear()

        loads[0].wait()
        loads[1].wait()
        hidden, d_in = hidden_ref[...], d_in_ref[...]
        scale2 = lax.rsqrt(jnp.mean(hidden * hidden, -1, keepdims=True) + EPSILON)
        scaled = d_in * gains_ref[1:2]
        mean = jnp.mean(scaled * hidden, -1, keepdims=True)
        d_hidden = cot_ref[...].astype(F32) + scale2 * scaled
        d_hidden = d_hidden - hidden * (scale2 * scale2 * scale2 * mean)
        d_hidden_ref[...] = d_hidden
        d_attn_ref[...] = d_hidden.astype(BF16)
        rows_ref[...] = jnp.zeros_like(rows_ref)
        rows_ref[experts + 1 : experts + 2, :] = jnp.sum(d_in * hidden * scale2, 0, keepdims=True)

        loads[2].wait()

        @pl.loop(0, query_width // 256)
        def _(n):
            columns = pl.ds(pl.multiple_of(n * 256, 256), 256)
            out = weight[:, :, :, :, columns].reshape(width, 256)
            d_heads_ref[:, columns] = dot_nn(d_attn_ref[...], out).astype(BF16)

        load_q = pltpu.make_async_copy(wq_hbm, weight, load_sems.at[0])
        load_q.start()
        loads[3].wait()

        def row_grads(buf, left, right, first, count, extra=None):
            @pl.loop(0, planes)
            def _(block):
                columns = pl.ds(pl.multiple_of(block * part, part), part)
                result = dot_tn(left[:, columns], right)
                if extra is not None:
                    result = result + extra(columns)
                result = result.astype(BF16).reshape(nc, 2, part // nc // 2, count)
                for half in range(2):
                    buf[half, block, :, pl.ds(first, count)] = result[:, half].reshape(
                        part // 2, count
                    )

        length = nc * tokens
        group = QUERY_HEADS // KEY_VALUE_HEADS
        loads[4].wait()
        dkv_acc[...] = jnp.zeros_like(dkv_acc)

        def attend(j, first, last):
            key = kv_ref[j, :, :, pl.ds(0, size)].reshape(length, size)
            value = kv_ref[j, :, :, pl.ds(size, size)].reshape(length, size)
            key_turned = jnp.transpose(key)

            @pl.loop(j * group + first, j * group + last)
            def _(h):
                columns = pl.ds(pl.multiple_of(h * size, size), size)
                query, grad = query_ref[:, columns], d_heads_ref[:, columns]
                scores = causal(dot_nt(key, query), z * tokens)
                largest = jnp.max(scores, 0, keepdims=True)
                expd = jnp.exp((scores - largest) * (size**-0.5))
                probs = expd * (1.0 / jnp.sum(expd, 0, keepdims=True))
                d_probs = dot_nt(value, grad)
                inner = jnp.sum(probs * d_probs, 0, keepdims=True)
                d_raw = (probs * (d_probs - inner) * (size**-0.5)).astype(BF16)
                d_query = jnp.transpose(dot_nn(key_turned, d_raw))
                d_query = d_query * cos_ref[...] - swap_halves(d_query) * sin_ref[...]
                d_all_ref[:, columns] = d_query.astype(BF16)
                dkv_acc[j, :, pl.ds(0, size)] += dot_nn(d_raw, query)
                dkv_acc[j, :, pl.ds(size, size)] += dot_nn(probs.astype(BF16), grad)

        def round_kv(j):
            for block in range(nc):
                rows = dkv_acc[j, pl.ds(block * tokens, tokens), :]
                dkv_ref[j, block] = rows.astype(BF16)

        def enter():
            pl.semaphore_wait(credits.at[1], 1)
            pl.semaphore_wait(credits.at[2], 1)

        attend(0, 0, group)
        round_kv(0)
        scatter_kv[0].send()
        attend(1, 0, group)
        round_kv(1)
        scatter_kv[1].send()
        expert.send(1, 2, when=top)
        expert.send(1, 1, when=odd)
        row_grads(grads_o, d_attn_ref, heads_ref[...], 0, width)
        pl.semaphore_wait(credits.at[0], 1)
        scatter_o.share()
        y_own = pltpu.make_async_copy(y_hbm.at[0], heads_ref, load_sems.at[2])
        y_own.start()
        for copy in y_loads:
            copy.wait()
        scatter_y.relay(lambda r, half: y_relay.at[half])
        scatter_o.merge(enter)

        for copy in loads[5:]:
            copy.wait()
        row_grads(grads_q, inputs_ref, d_all_ref[:, pl.ds(0, query_width)], 0, query_width)
        scatter_q.share()
        expert.relay_begin(1)
        scatter_o.relay()
        scatter_q.merge()
        for h in range(KEY_VALUE_HEADS):
            grad = scatter_kv[h].total()
            d_key = grad[:, :size]
            d_key = d_key * cos_ref[...] - swap_halves(d_key) * sin_ref[...]
            d_all_ref[:, pl.ds(query_width + h * size, size)] = d_key.astype(BF16)
            d_all_ref[:, pl.ds(query_width + key_width + h * size, size)] = grad[:, size:].astype(
                BF16
            )
        y_own.wait()
        hidden_ref[...] += heads_ref[...].astype(F32)
        scatter_y.total(hidden_ref)
        heads_ref[...] = hidden_ref[...].astype(BF16)
        layer_out = pltpu.make_async_copy(heads_ref, layer_hbm, out_sems.at[0])
        layer_out.start()

        total = dg_part[0]
        for r in (1, 2, 3):
            wire_1.arrived(dg_land.at[r - 1], dg_slot + r - 1, ids[r])
            total = total + dg_land[r - 1]
        gates = gate_all[0]
        d_logits = gates * (total - jnp.sum(gates * total, 0, keepdims=True))
        d_logits = jnp.concatenate(
            [d_logits, jnp.zeros((SMALL - d_logits.shape[0], tokens), F32)], 0
        )
        d_all_ref[:, pl.ds(qkv_width, SMALL)] = jnp.transpose(d_logits).astype(BF16)

        load_q.wait()

        @pl.loop(0, planes)
        def _(block):
            columns = pl.ds(pl.multiple_of(block * part, part), part)
            rows_q = weight[block].reshape(part, query_width)
            rows_k = wk_all[block].reshape(part, rest)
            d_inputs_ref[:, columns] = dot_nt(
                d_all_ref[:, pl.ds(0, query_width)], rows_q
            ) + dot_nt(d_all_ref[:, pl.ds(query_width, rest)], rows_k)

        rows = x_ref[...].astype(F32)
        scale1 = lax.rsqrt(jnp.mean(rows * rows, -1, keepdims=True) + EPSILON)
        d_inputs = d_inputs_ref[...]
        rows_ref[experts : experts + 1, :] = jnp.sum(d_inputs * rows * scale1, 0, keepdims=True)

        def extra(columns):
            small = jnp.transpose(rows_ref[:, columns])
            return jnp.concatenate([jnp.zeros((part, rest - SMALL), F32), small], 1)

        row_grads(
            grads_q, inputs_ref, d_all_ref[:, pl.ds(query_width, rest)], query_width, rest, extra
        )
        scatter_k.share()
        scatter_o.total()
        scatter_o.line.send()
        expert.relay_add()
        scatter_q.relay()
        expert.relay_send(1)
        scatter_k.merge()
        scaled = d_inputs_ref[...] * gains_ref[0:1]
        rows = x_ref[...].astype(F32)
        scale1 = lax.rsqrt(jnp.mean(rows * rows, -1, keepdims=True) + EPSILON)
        mean = jnp.mean(scaled * rows, -1, keepdims=True)
        d_x = d_hidden_ref[...] + scale1 * scaled - rows * (scale1 * scale1 * scale1 * mean)
        inputs_ref[...] = d_x.astype(BF16)
        d_x_out = pltpu.make_async_copy(inputs_ref, d_x_hbm, out_sems.at[1])
        d_x_out.start()
        scatter_q.total()
        scatter_q.line.send()
        scatter_k.relay()
        expert.last(0, (sum_gu_hbm, sum_dn_hbm))
        scatter_k.total()
        scatter_k.line.send()
        sum_o_ref[...] = scatter_o.line.total()
        expert.last(1, (sum_gu_hbm, sum_dn_hbm))
        sum_q_ref[:, pl.ds(0, query_width)] = scatter_q.line.total()
        sum_q_ref[:, pl.ds(query_width, rest)] = scatter_k.line.total()
        layer_out.wait()
        d_x_out.wait()
        wire_2.finish()
        expert.finish()

    held = EXP_DEV
    weight_shape = wq_hbm.shape
    pl.run_scoped(
        front_phase,
        pltpu.VMEM(weight_shape, BF16),
        pltpu.VMEM(weight_shape, BF16),
        pltpu.VMEM((tokens, width), BF16),
        pltpu.VMEM((tokens, width), BF16),
        pltpu.VMEM((tokens, query_width), BF16),
        pltpu.VMEM((tokens, query_width), BF16),
        pltpu.VMEM((tokens, width), F32),
        pltpu.VMEM((tokens, rest), F32),
        pltpu.VMEM((tokens, query_width), F32),
    )
    shard, step = width // nc // 2, 48
    pl.run_scoped(
        token_phase,
        pltpu.VMEM((held, width, 2 * ff), BF16),
        pltpu.VMEM((held, ff, width), BF16),
        pltpu.VMEM((blocks, tokens, width), BF16),
        pltpu.VMEM((blocks, tokens, held * ff), BF16),
        pltpu.VMEM((blocks, tokens, held * 2 * ff), BF16),
        pltpu.VMEM((2, tokens, width), BF16),
        pltpu.VMEM((2, 2, shard, grad_width // held), BF16),
        pltpu.VMEM((2, shard // step, step, grad_width // held), BF16),
        pltpu.VMEM((width, blocks * tokens), BF16),
    )
    rows_half = width // blocks // 2
    pl.run_scoped(
        token_rows_phase,
        pltpu.VMEM(weight_shape, BF16),
        pltpu.VMEM((2, blocks, rows_half, width), BF16),
        pltpu.VMEM((2, blocks, rows_half, qkv_width + SMALL), BF16),
        pltpu.VMEM((tokens, width), BF16),
        pltpu.VMEM((tokens, width), BF16),
        pltpu.VMEM((tokens, query_width), BF16),
        pltpu.VMEM((tokens, query_width), BF16),
        pltpu.VMEM((tokens, width), F32),
        pltpu.VMEM((tokens, width), F32),
        pltpu.VMEM((tokens, width), BF16),
        pltpu.VMEM((tokens, query_width), BF16),
        pltpu.VMEM((tokens, qkv_width + SMALL), BF16),
        pltpu.VMEM((SMALL, width), F32),
        pltpu.VMEM((KEY_VALUE_HEADS, nc * tokens, 2 * size), F32),
        pltpu.VMEM((KEY_VALUE_HEADS, nc, tokens, 2 * size), BF16),
        pltpu.VMEM((2, tokens, width // 2), BF16),
        pltpu.VMEM((4, shard // step, step, grad_width // held), BF16),
        pltpu.VMEM((2, step, grad_width // held), F32),
    )


def layer(operands, sizes):
    ne, nc, nd = sizes
    qkv_shard, x = operands[3], operands[6]
    w_dn = operands[9]
    tokens, width = x.shape
    held, ff = w_dn.shape[0], w_dn.shape[1]
    query_width = QUERY_HEADS * HEAD_DIMENSION
    rows, qkv_width = qkv_shard.shape
    rest = qkv_width - query_width + SMALL
    rest_half = rest // 256 * 128
    shard, grads = width // (nc * nd), held * 3 * ff
    kv_size = 2 * HEAD_DIMENSION
    weight = (ne, nc, nd, rows, query_width)
    shapes = [
        ((tokens, width), BF16),
        ((tokens, width), BF16),
        ((rows, qkv_width + SMALL), F32),
        ((rows, width), F32),
        ((held, shard, 2 * ff), F32),
        ((held, shard, ff), F32),
        ((nc, shard, grads), BF16),
        ((nc + 1, shard, grads), BF16),
        ((ne, tokens, width), BF16),
        (weight, BF16),
        (weight, BF16),
        ((ne, tokens, width), BF16),
        ((tokens, width), BF16),
        ((tokens, query_width), BF16),
        ((tokens, query_width), BF16),
        ((tokens, width), F32),
    ]
    vmem = pl.BlockSpec(memory_space=pltpu.VMEM)
    anywhere = pl.BlockSpec(memory_space=pl.ANY)
    units = nc * held
    sems = [120, 110, 6, 6, 6, 6, 10, 10, 64, 64, 2 * units, (nc + 1) * held, units, units, 2, 12, 6]
    return pl.pallas_call(
        functools.partial(layer_kernel, nc, EXP_DEV * ne),
        out_shape=[jax.ShapeDtypeStruct(*s) for s in shapes],
        in_specs=[vmem] * 6 + [anywhere] * (len(operands) - 6),
        out_specs=[anywhere] * 2 + [vmem] * 2 + [anywhere] * (len(shapes) - 4),
        scratch_shapes=[
            pltpu.VMEM((ne, nc, nd, rows, rest), BF16),
            pltpu.VMEM((KEY_VALUE_HEADS, nc, tokens, kv_size), BF16),
            pltpu.VMEM((ne, GATE_ROWS, tokens), F32),
            pltpu.VMEM((ne, tokens, SMALL), F32),
            pltpu.VMEM((8, width), F32),
            pltpu.VMEM((ne, tokens, width), BF16),
            pltpu.VMEM((6, tokens, width // 2), BF16),
            pltpu.VMEM((6, tokens, width // 2), BF16),
            pltpu.VMEM((nc, shard, grads // held), BF16),
            pltpu.VMEM((6, nc * rows, query_width // 2), BF16),
            pltpu.VMEM((6, nc * rows, rest - rest_half), BF16),
            pltpu.VMEM((nc, rows, width), BF16),
            pltpu.VMEM((nc, rows, query_width), BF16),
            pltpu.VMEM((nc, rows, rest), BF16),
            pltpu.VMEM((KEY_VALUE_HEADS, nc, tokens, kv_size), BF16),
            pltpu.VMEM((tokens, width), F32),
            pltpu.VMEM((ne, tokens, SMALL), F32),
            pltpu.VMEM((ne, GATE_ROWS, tokens), F32),
            pltpu.VMEM((ne - 1, GATE_ROWS, tokens), F32),
        ]
        + [pltpu.SemaphoreType.DMA((count,)) for count in sems]
        + [
            pltpu.SemaphoreType.DMA((20,)),
            pltpu.SemaphoreType.DMA((2,)),
            pltpu.SemaphoreType.REGULAR((4,)),
        ],
        compiler_params=pltpu.CompilerParams(
            collective_id=0, has_side_effects=True, vmem_limit_bytes=63 * MIB
        ),
    )(*operands)


def finish_kernel(experts, *refs):
    sources, dests = refs[:6], refs[6:12]
    router_ref, first_ref, second_ref = refs[12:]
    sum_q = sources[0]
    qkv_width = dests[0].shape[-1]
    dests[0][...] = sum_q[:, pl.ds(0, qkv_width)]
    for source, dest in zip(sources[1:], dests[1:]):
        dest[...] = source[...]
    small = sum_q[:, pl.ds(qkv_width, SMALL)]
    rows = small.shape[0]
    filled = jnp.concatenate([small, jnp.zeros((SMALL - rows, SMALL), F32)], 0)
    turned = jnp.transpose(filled)[:, :rows]
    router_ref[...] = turned[:experts]
    first_ref[...] = turned[experts : experts + 1]
    second_ref[...] = turned[experts + 1 : experts + 2]


def finish(sum_q, others, experts):
    rows, q_width = sum_q.shape
    vmem = pl.BlockSpec(memory_space=pltpu.VMEM)
    shapes = [jax.ShapeDtypeStruct((rows, q_width - SMALL), F32)]
    shapes += [jax.ShapeDtypeStruct(o.shape, o.dtype) for o in others]
    shapes += [jax.ShapeDtypeStruct((count, rows), F32) for count in (experts, 1, 1)]
    return pl.pallas_call(
        functools.partial(finish_kernel, experts),
        out_shape=shapes,
        in_specs=[vmem] * 6,
        out_specs=[vmem] * 9,
        compiler_params=pltpu.CompilerParams(vmem_limit_bytes=60 * MIB),
    )(sum_q, *others)


def local_plain(
    layer_input,
    gain_attn,
    query_key_value_weight,
    w_out,
    w_router,
    gain_ffn,
    w_gate_up,
    w_down,
    routes,
    d_out,
):
    tokens = layer_input.shape[1]
    model_width = layer_input.shape[2]
    ne, nc, nd = (lax.axis_size(a) for a in ("expert", "context", "dp"))
    expert_total = EXP_DEV * ne
    ff = w_down.shape[1]
    me = lax.axis_index("expert")
    first_row = lax.axis_index("context") * tokens
    query_width = QUERY_HEADS * HEAD_DIMENSION
    key_width = KEY_VALUE_HEADS * HEAD_DIMENSION
    qkv_width = query_width + 2 * key_width

    small = jnp.concatenate([w_router, gain_attn[:, None], gain_ffn[:, None]], -1)
    small = jnp.pad(small, ((0, 0), (0, 128 - small.shape[1])))
    gathered = gather_rows(jnp.concatenate([query_key_value_weight, small], -1))
    out_turned = gather_rows(w_out.T)
    qkv_weight = gathered[:, :qkv_width]
    router_weight = gathered[:, qkv_width : qkv_width + expert_total]
    gains = gathered[:, qkv_width + expert_total : qkv_width + expert_total + 2].T.astype(F32)
    gain_first, gain_second = gains[0], gains[1]
    cotangent_all = plane_gather(d_out[0])

    token_rows = layer_input[0].astype(F32)
    scale1 = lax.rsqrt(jnp.mean(token_rows * token_rows, -1, keepdims=True) + EPSILON)
    inputs1 = (token_rows * scale1 * gain_first).astype(BF16)
    query_key_value = dot_nn(inputs1, qkv_weight)
    cosine_values, sine_values = rope_tables(first_row + jnp.arange(tokens), HEAD_DIMENSION)
    rotated = rotate_half(
        query_key_value[:, : query_width + key_width].reshape(tokens, -1, HEAD_DIMENSION),
        cosine_values,
        sine_values,
    ).reshape(tokens, -1)
    query = rotated[:, :query_width].astype(BF16)
    key_value_local = jnp.concatenate(
        [rotated[:, query_width:], query_key_value[:, query_width + key_width :]], -1
    ).astype(BF16)
    key_value = line_gather(key_value_local, "context", both=False).reshape(nc * tokens, -1)
    first = first_row.astype(jnp.int32).reshape(1)
    heads = attend_forward(first, query, key_value)

    logits = dot_nn(inputs1, router_weight)
    chosen_ids = routes[0]
    picks = (chosen_ids[:, :, None] == jnp.arange(expert_total)[None, None, :]).astype(F32)
    chosen = jnp.sum(picks * logits[:, None, :], -1)
    gates = jax.nn.softmax(chosen, axis=-1)
    gate_dense = jnp.sum(picks * gates[:, :, None], 1).T
    gate_blocks = cube_gather(gate_dense, "expert", axis_masks("expert"))
    gate_local = jnp.concatenate(
        [lax.dynamic_slice_in_dim(b, me * EXP_DEV, EXP_DEV, 0) for b in gate_blocks], 1
    )

    attn = dot_nt(heads, out_turned)
    hidden = token_rows + attn
    scale2 = lax.rsqrt(jnp.mean(hidden * hidden, -1, keepdims=True) + EPSILON)
    expert_in = (hidden * scale2 * gain_second).astype(BF16)

    rows_all = plane_gather(expert_in)
    gate_up = jnp.einsum("td,edf->etf", rows_all, w_gate_up, preferred_element_type=F32)
    gate_part, up_part = gate_up[..., :ff], gate_up[..., ff:]
    sigma = jax.nn.sigmoid(gate_part)
    silu = gate_part * sigma
    act = silu * up_part
    gate_column = gate_local[:, :, None]
    act_gated = (act * gate_column).astype(BF16)
    partial_out = jnp.einsum("etf,efd->td", act_gated, w_down, preferred_element_type=F32)
    mixture = plane_scatter(partial_out.astype(BF16), tokens)
    layer_result = (hidden + mixture).astype(BF16)

    d_act_raw = jnp.einsum("td,efd->etf", cotangent_all, w_down, preferred_element_type=F32)
    d_gates_local = jnp.sum(d_act_raw * act, -1)
    d_act = d_act_raw * gate_column
    d_gate_part = d_act * up_part * sigma * (1.0 + gate_part * (1.0 - sigma))
    d_up_part = d_act * silu
    d_gate_up = jnp.concatenate([d_gate_part, d_up_part], -1).astype(BF16)
    d_rows = jnp.einsum("etf,edf->td", d_gate_up, w_gate_up, preferred_element_type=F32)
    grad_down = jnp.einsum("td,etf->edf", cotangent_all, act_gated, preferred_element_type=F32)
    grad_gate_up = jnp.einsum("td,etf->edf", rows_all, d_gate_up, preferred_element_type=F32)

    d_expert_in = plane_scatter(d_rows.astype(BF16), tokens)
    d_gate_blocks = d_gates_local.reshape(EXP_DEV, ne, tokens)
    d_gates_dense = jnp.zeros((expert_total, tokens), F32)
    for r in range(ne):
        arrived = d_gate_blocks[:, r]
        if r:
            arrived = exchange(arrived, "expert", r)
        d_gates_dense = lax.dynamic_update_slice(d_gates_dense, arrived, ((me ^ r) * EXP_DEV, 0))
    d_gates = jnp.sum(picks * d_gates_dense.T[:, None, :], -1)
    d_chosen = gates * (d_gates - jnp.sum(gates * d_gates, -1, keepdims=True))
    d_logits = jnp.sum(picks * d_chosen[:, :, None], 1).astype(BF16)
    grad_router = dot_tn(inputs1, d_logits)

    core = lax.axis_index("dp")
    part = model_width // (nc * nd)

    def scatter_experts(grad):
        blocks = grad.reshape(EXP_DEV, nc, nd, part, -1)
        mine = cube_scatter(
            [lax.dynamic_index_in_dim(blocks, core ^ r, 2, keepdims=False) for r in range(nd)],
            "dp",
            axis_masks("dp"),
        )
        return line_scatter(
            lambda j: lax.dynamic_index_in_dim(mine, j, 1, keepdims=False), "context"
        )

    sum_gate_up = scatter_experts(grad_gate_up)
    sum_down = jnp.swapaxes(scatter_experts(grad_down), 1, 2)

    cotangent = d_out[0].astype(F32)
    scaled2 = d_expert_in * gain_second
    d_hidden = (
        cotangent
        + scale2 * scaled2
        - hidden * (scale2 * scale2 * scale2) * jnp.mean(scaled2 * hidden, -1, keepdims=True)
    )
    grad_gain_second = jnp.sum(d_expert_in * hidden * scale2, 0)
    d_attn = d_hidden.astype(BF16)
    grad_out_turned = dot_tn(d_attn, heads)
    sum_out = scatter_rows(grad_out_turned).T
    d_heads = dot_nn(d_attn, out_turned).astype(BF16)
    d_query, d_key_all, d_value_all = attend_backward(first, query, key_value, d_heads)
    d_key_value_all = jnp.concatenate([d_key_all, d_value_all], -1).reshape(nc, tokens, -1)
    d_key_value = line_scatter(
        lambda j: lax.dynamic_index_in_dim(d_key_value_all, j, 0, keepdims=False),
        "context",
        up=False,
    )
    d_rotated = rotate_back(
        jnp.concatenate([d_query, d_key_value[:, :key_width]], -1).reshape(
            tokens, -1, HEAD_DIMENSION
        ),
        cosine_values,
        sine_values,
    ).reshape(tokens, -1)
    d_qkv = jnp.concatenate([d_rotated, d_key_value[:, key_width:]], -1).astype(BF16)
    d_inputs = dot_nt(d_qkv, qkv_weight) + dot_nt(d_logits, router_weight)
    grad_gain_first = jnp.sum(d_inputs * token_rows * scale1, 0)
    grad_qkv = dot_tn(inputs1, d_qkv)
    small_grads = jnp.concatenate(
        [grad_router, grad_gain_first[:, None], grad_gain_second[:, None]], -1
    )
    small_grads = jnp.pad(small_grads, ((0, 0), (0, 128 - small_grads.shape[1])))
    sum_rows = scatter_rows(jnp.concatenate([grad_qkv, small_grads], -1))
    sum_qkv = sum_rows[:, :qkv_width]
    sum_router = sum_rows[:, qkv_width : qkv_width + expert_total]
    sum_gain_first = sum_rows[:, qkv_width + expert_total]
    sum_gain_second = sum_rows[:, qkv_width + expert_total + 1]
    scaled1 = d_inputs * gain_first
    d_input_rows = (
        d_hidden
        + scale1 * scaled1
        - token_rows
        * (scale1 * scale1 * scale1)
        * jnp.mean(scaled1 * token_rows, -1, keepdims=True)
    ).astype(BF16)
    return (
        layer_result[None],
        d_input_rows[None],
        sum_gain_first,
        sum_qkv,
        sum_out,
        sum_router,
        sum_gain_second,
        sum_gate_up,
        sum_down,
    )


def local_fused(
    layer_input,
    gain_attn,
    query_key_value_weight,
    w_out,
    w_router,
    gain_ffn,
    w_gate_up,
    w_down,
    routes,
    d_out,
):
    tokens = layer_input.shape[1]
    ne, nc, nd = sizes = tuple(lax.axis_size(a) for a in ("expert", "context", "dp"))
    expert_total = EXP_DEV * ne
    first_row = lax.axis_index("context") * tokens
    query_width = QUERY_HEADS * HEAD_DIMENSION
    key_width = KEY_VALUE_HEADS * HEAD_DIMENSION
    qkv_width = query_width + 2 * key_width

    small = jnp.concatenate([w_router, gain_attn[:, None], gain_ffn[:, None]], -1)
    small = jnp.pad(small, ((0, 0), (0, SMALL - small.shape[1])))
    cosine_values, sine_values = rope_tables(first_row + jnp.arange(tokens), HEAD_DIMENSION)
    sine_values = sine_values * jnp.where(
        jnp.arange(HEAD_DIMENSION) < HEAD_DIMENSION // 2, -1.0, 1.0
    )
    layer_result, d_x, sum_rows, sum_out, sum_gate_up, sum_down = layer(
        (
            cosine_values,
            sine_values,
            routes[0].T,
            query_key_value_weight,
            small,
            w_out.T,
            layer_input[0],
            d_out[0],
            w_gate_up,
            w_down,
        ),
        sizes,
    )[:6]
    sum_qkv, layer_result, d_x, sum_gate_up, sum_down, sum_out, sum_router, *sum_gains = finish(
        sum_rows, (layer_result, d_x, sum_gate_up, sum_down, sum_out), expert_total
    )
    return (
        layer_result[None],
        d_x[None],
        sum_gains[0][0],
        sum_qkv,
        sum_out.T,
        sum_router.T,
        sum_gains[1][0],
        sum_gate_up,
        jnp.swapaxes(sum_down, 1, 2),
    )


def solution(mesh):
    in_specs = (
        P(("expert", "dp"), "context", None),
        P(("expert", "context", "dp")),
        P(("expert", "context", "dp"), None),
        P(None, ("expert", "context", "dp")),
        P(("expert", "context", "dp"), None),
        P(("expert", "context", "dp")),
        P("expert", None, None),
        P("expert", None, None),
        P(("expert", "dp"), "context", None),
        P(("expert", "dp"), "context", None),
    )
    out_specs = (
        P(("expert", "dp"), "context", None),
        P(("expert", "dp"), "context", None),
        P(("expert", "context", "dp")),
        P(("expert", "context", "dp"), None),
        P(None, ("expert", "context", "dp")),
        P(("expert", "context", "dp"), None),
        P(("expert", "context", "dp")),
        P("expert", ("context", "dp"), None),
        P("expert", None, ("context", "dp")),
    )
    sizes = tuple(mesh.shape[a] for a in ("expert", "context", "dp"))
    local = local_fused if sizes == (4, 4, 2) else local_plain
    return jax.shard_map(local, mesh=mesh, in_specs=in_specs, out_specs=out_specs, check_vma=False)
```

```python
import functools
import math

import jax
import jax.numpy as jnp
from jax import lax
from jax.experimental import pallas as pl
from jax.experimental.pallas import tpu as pltpu
from jax.sharding import PartitionSpec as P

QUERY_HEADS = 12
KEY_VALUE_HEADS = 2
HEAD_DIMENSION = 128
TOP = 4
EXP_DEV = 2

EPSILON = 1e-06
ROPE_BASE = 10000.0
MASKED = -1e30

F32 = jnp.float32
BF16 = jnp.bfloat16


def rope_tables(positions, width):
    halfway = width // 2
    fraction = jnp.arange(halfway, dtype=jnp.float32) * (2.0 / width)
    frequency = jnp.exp(-math.log(ROPE_BASE) * fraction)
    angles = positions.astype(jnp.float32)[:, None] * frequency[None, :]
    cosine_values = jnp.cos(angles)
    sine_values = jnp.sin(angles)
    return (
        jnp.concatenate([cosine_values, cosine_values], -1),
        jnp.concatenate([sine_values, sine_values], -1),
    )


def rotate_half(values, cosine_values, sine_values):
    halfway = values.shape[-1] // 2
    turned = jnp.concatenate([-values[..., halfway:], values[..., :halfway]], -1)
    return values * cosine_values[:, None, :] + turned * sine_values[:, None, :]


def rotate_back(grads, cosine_values, sine_values):
    halfway = grads.shape[-1] // 2
    scaled = grads * sine_values[:, None, :]
    turned = jnp.concatenate([scaled[..., halfway:], -scaled[..., :halfway]], -1)
    return grads * cosine_values[:, None, :] + turned


def dot_nt(a, b):
    return lax.dot_general(a, b, (((1,), (1,)), ((), ())), preferred_element_type=F32)


def dot_tn(a, b):
    return lax.dot_general(a, b, (((0,), (0,)), ((), ())), preferred_element_type=F32)


def dot_nn(a, b):
    return jnp.dot(a, b, preferred_element_type=F32)


def masked_probs(first_row, query, key):
    scores = dot_nt(query, key) * (HEAD_DIMENSION**-0.5)
    rows = first_row + lax.broadcasted_iota(jnp.int32, scores.shape, 0)
    columns = lax.broadcasted_iota(jnp.int32, scores.shape, 1)
    scores = jnp.where(columns <= rows, scores, MASKED)
    expd = jnp.exp(scores - jnp.max(scores, axis=-1, keepdims=True))
    return expd / jnp.sum(expd, axis=-1, keepdims=True)


def attend_forward_kernel(first_ref, query_ref, key_ref, value_ref, heads_ref):
    probs = masked_probs(first_ref[0], query_ref[...], key_ref[...])
    heads_ref[...] = dot_nn(probs.astype(BF16), value_ref[...]).astype(BF16)


def attend_forward(first_row, query, key_value):
    tokens, width = query.shape
    length = key_value.shape[0]
    group = QUERY_HEADS // KEY_VALUE_HEADS
    size = HEAD_DIMENSION
    return pl.pallas_call(
        attend_forward_kernel,
        grid_spec=pltpu.PrefetchScalarGridSpec(
            num_scalar_prefetch=1,
            grid=(QUERY_HEADS,),
            in_specs=[
                pl.BlockSpec((tokens, size), lambda h, s: (0, h)),
                pl.BlockSpec((length, size), lambda h, s: (0, h // group)),
                pl.BlockSpec((length, size), lambda h, s: (0, KEY_VALUE_HEADS + h // group)),
            ],
            out_specs=pl.BlockSpec((tokens, size), lambda h, s: (0, h)),
        ),
        out_shape=jax.ShapeDtypeStruct((tokens, width), BF16),
        compiler_params=pltpu.CompilerParams(vmem_limit_bytes=32 * 1024 * 1024),
        cost_estimate=pl.CostEstimate(
            flops=4 * tokens * length * width, bytes_accessed=4 * tokens * width, transcendentals=0
        ),
    )(first_row, query, key_value, key_value)


def attend_backward_kernel(
    first_ref, query_ref, key_ref, value_ref, grad_ref, d_query_ref, d_key_ref, d_value_ref
):
    query, key, value, grad = query_ref[...], key_ref[...], value_ref[...], grad_ref[...]
    probs = masked_probs(first_ref[0], query, key)
    d_probs = dot_nt(grad, value)
    inner = jnp.sum(probs * d_probs, axis=-1, keepdims=True)
    d_raw = (probs * (d_probs - inner) * (HEAD_DIMENSION**-0.5)).astype(BF16)
    d_query_ref[...] = dot_nn(d_raw, key)
    d_key = dot_tn(d_raw, query)
    d_value = dot_tn(probs.astype(BF16), grad)

    @pl.when(pl.program_id(1) == 0)
    def _():
        d_key_ref[...] = d_key
        d_value_ref[...] = d_value

    @pl.when(pl.program_id(1) > 0)
    def _():
        d_key_ref[...] += d_key
        d_value_ref[...] += d_value


def attend_backward(first_row, query, key_value, grad):
    tokens, width = query.shape
    length = key_value.shape[0]
    group = QUERY_HEADS // KEY_VALUE_HEADS
    size = HEAD_DIMENSION
    row_spec = pl.BlockSpec((tokens, size), lambda j, g, s: (0, j * group + g))
    return pl.pallas_call(
        attend_backward_kernel,
        grid_spec=pltpu.PrefetchScalarGridSpec(
            num_scalar_prefetch=1,
            grid=(KEY_VALUE_HEADS, group),
            in_specs=[
                row_spec,
                pl.BlockSpec((length, size), lambda j, g, s: (0, j)),
                pl.BlockSpec((length, size), lambda j, g, s: (0, KEY_VALUE_HEADS + j)),
                row_spec,
            ],
            out_specs=[
                row_spec,
                pl.BlockSpec((length, size), lambda j, g, s: (0, j)),
                pl.BlockSpec((length, size), lambda j, g, s: (0, j)),
            ],
        ),
        out_shape=[
            jax.ShapeDtypeStruct((tokens, width), F32),
            jax.ShapeDtypeStruct((length, KEY_VALUE_HEADS * size), F32),
            jax.ShapeDtypeStruct((length, KEY_VALUE_HEADS * size), F32),
        ],
        compiler_params=pltpu.CompilerParams(vmem_limit_bytes=32 * 1024 * 1024),
        cost_estimate=pl.CostEstimate(
            flops=10 * tokens * length * width, bytes_accessed=8 * tokens * width, transcendentals=0
        ),
    )(first_row, query, key_value, key_value, grad)


def exchange(values, axis, mask):
    size = lax.axis_size(axis)
    return lax.ppermute(values, axis, [(i, i ^ mask) for i in range(size)])


def axis_masks(axis):
    size = lax.axis_size(axis)
    masks, bit = [], 1
    while bit < size:
        masks.append(bit)
        bit *= 2
    return masks


def cube_gather(values, axis, masks):
    held = {0: values}
    for mask in masks:
        for r, block in list(held.items()):
            held[r ^ mask] = exchange(block, axis, mask)
    return [held[r] for r in range(lax.axis_size(axis))]


def cube_scatter(blocks, axis, masks):
    held = dict(enumerate(blocks))
    for mask in masks:
        kept = {}
        for r in list(held):
            if not r & mask:
                arrived = exchange(held[r ^ mask].astype(BF16), axis, mask)
                kept[r] = held[r].astype(F32) + arrived.astype(F32)
        held = kept
    return held[0]


def line_steps(values, axis, up):
    size = lax.axis_size(axis)
    pairs = [(i, i + 1) if up else (i + 1, i) for i in range(size - 1)]
    return lax.ppermute(values, axis, pairs)


def line_gather(values, axis, both=True):
    size = lax.axis_size(axis)
    me = lax.axis_index(axis)
    result = jnp.zeros((size + 1,) + values.shape, values.dtype)
    result = lax.dynamic_update_index_in_dim(result, values, me, 0)
    up = down = values
    for step in range(1, size):
        up = line_steps(up, axis, True)
        result = lax.dynamic_update_index_in_dim(
            result, up, jnp.where(me - step >= 0, me - step, size), 0
        )
        if both:
            down = line_steps(down, axis, False)
            result = lax.dynamic_update_index_in_dim(result, down, jnp.minimum(me + step, size), 0)
    return result[:size]


def line_scatter(take, axis, up=True, down=True):
    size = lax.axis_size(axis)
    me = lax.axis_index(axis)
    total = take(me).astype(F32)
    for active, sign in ((up, 1), (down, -1)):
        if not active:
            continue
        arrived = None
        for step in range(1, size):
            block = take((me + sign * (size - step)) % size).astype(F32)
            if arrived is not None:
                block = block + arrived.astype(F32)
            arrived = line_steps(block.astype(BF16), axis, sign > 0)
        total = total + arrived.astype(F32)
    return total


def gather_rows(shard):
    ne, nc, nd = (lax.axis_size(a) for a in ("expert", "context", "dp"))
    rows, width = shard.shape
    lines = line_gather(shard, "context")
    masks = axis_masks("expert")
    half = width // 256 * 128
    parts = [lines[..., :half], lines[..., half:]]
    me = lax.axis_index("expert")
    result = jnp.zeros((ne, nc, rows, width), shard.dtype)
    for start, part, order in ((0, parts[0], masks), (half, parts[1], masks[::-1])):
        for r, block in enumerate(cube_gather(part, "expert", order)):
            result = lax.dynamic_update_slice(result, block[None], (me ^ r, 0, 0, start))
    core = lax.axis_index("dp")
    whole = jnp.zeros((ne, nc, nd, rows, width), shard.dtype)
    for r, block in enumerate(cube_gather(result, "dp", axis_masks("dp"))):
        whole = lax.dynamic_update_slice(whole, block[:, :, None], (0, 0, core ^ r, 0, 0))
    return whole.reshape(-1, width)


def scatter_rows(grad):
    ne, nc, nd = (lax.axis_size(a) for a in ("expert", "context", "dp"))
    width = grad.shape[-1]
    rows = grad.shape[0] // (ne * nc * nd)
    blocks = grad.reshape(ne, nc, nd, rows, width)
    core, me = lax.axis_index("dp"), lax.axis_index("expert")
    mine = cube_scatter(
        [
            lax.dynamic_index_in_dim(blocks, core ^ r, 2, keepdims=False)
            for r in range(nd)
        ],
        "dp",
        axis_masks("dp"),
    )
    masks = axis_masks("expert")
    half = width // 256 * 128
    sums = []
    for part, order in ((mine[..., :half], masks), (mine[..., half:], masks[::-1])):
        sums.append(
            cube_scatter(
                [lax.dynamic_index_in_dim(part, me ^ r, 0, keepdims=False) for r in range(ne)],
                "expert",
                order,
            )
        )
    lines = jnp.concatenate(sums, -1)
    return line_scatter(
        lambda j: lax.dynamic_index_in_dim(lines, j, 0, keepdims=False), "context"
    )


def plane_gather(rows):
    masks = axis_masks("expert")
    half = rows.shape[-1] // 2
    left = cube_gather(rows[:, :half], "expert", masks)
    right = cube_gather(rows[:, half:], "expert", masks[::-1])
    return jnp.concatenate([jnp.concatenate(p, -1) for p in zip(left, right)], 0)


def plane_scatter(partial, tokens):
    masks = axis_masks("expert")
    size = lax.axis_size("expert")
    half = partial.shape[-1] // 2
    blocks = partial.reshape(size, tokens, -1)
    left = cube_scatter([blocks[r, :, :half] for r in range(size)], "expert", masks)
    right = cube_scatter([blocks[r, :, half:] for r in range(size)], "expert", masks[::-1])
    return jnp.concatenate([left, right], -1)


MESH = pl.DeviceIdType.MESH
MIB = 1024 * 1024
SMALL = 128
GATE_ROWS = 16


def flip(index, mask):
    bit = 1
    while bit <= mask:
        if mask & bit:
            index = index + bit - 2 * bit * lax.rem(lax.div(index, bit), 2)
        bit *= 2
    return index


class Wire:
    def __init__(self, sends, recvs):
        self.sends, self.recvs = sends, recvs
        self.n_sends = self.n_recvs = 0
        self.open = []

    def slots(self, count):
        first = self.n_recvs
        self.n_recvs += count
        return first

    def start(self, src, dst, recv, device, when=None):
        number = self.n_sends
        self.n_sends += 1

        def copy():
            return pltpu.make_async_remote_copy(
                src_ref=src() if callable(src) else src,
                dst_ref=dst() if callable(dst) else dst,
                send_sem=self.sends.at[number],
                recv_sem=self.recvs.at[recv],
                device_id=device,
                device_id_type=MESH,
            )

        guard(when, lambda: copy().start())
        self.open.append((when, copy))

    def arrived(self, dst, recv, device):
        pltpu.make_async_remote_copy(
            src_ref=dst,
            dst_ref=dst,
            send_sem=self.sends.at[0],
            recv_sem=self.recvs.at[recv],
            device_id=device,
            device_id_type=MESH,
        ).wait_recv()

    def finish(self):
        for when, copy in self.open:
            guard(when, lambda copy=copy: copy().wait_send())
        self.open = []


def guard(when, action):
    if when is None:
        action()
    else:
        pl.when(when)(action)


def add_into(dest, source, steps=4):
    rows = dest.shape[0] // steps

    @pl.loop(0, steps)
    def _(n):
        here = pl.ds(pl.multiple_of(n * rows, rows), rows)
        dest[here] = (dest[here].astype(F32) + source[here].astype(F32)).astype(BF16)


def greet(targets):
    barrier = pltpu.get_barrier_semaphore()
    for device, when in targets:
        guard(
            when,
            lambda device=device: pl.semaphore_signal(
                barrier, inc=1, device_id=device, device_id_type=MESH
            ),
        )
    count = sum(1 if when is None else when.astype(jnp.int32) for _, when in targets)
    pl.semaphore_wait(barrier, count)


def plane_ids(e):
    return {m: {"expert": flip(e, m)} for m in (1, 2, 3)}


class RowsGather:
    def __init__(self, wire, ref, e, z, c, nc, half):
        self.wire, self.ref, self.e, self.z, self.c, self.nc = wire, ref, e, z, c, nc
        self.cols = (pl.ds(0, half), pl.ds(half, ref.shape[-1] - half))
        self.line = wire.slots(nc)
        self.plane = wire.slots(nc * 6)
        self.core = wire.slots(nc)
        self.ids = plane_ids(e)

    def go(self, *steps):
        for step in steps:
            action = {"l": self.pass_on, "s": self.spread, "f": self.forward, "h": self.share, "c": self.complete}
            action[step[0]](*map(int, step[1:]))

    def shard(self, k):
        if k < 2:
            return flip(self.z, k)
        inner = (self.z > 0) & (self.z < self.nc - 1)
        return jnp.where(inner, flip(self.z, 5 - k), flip(self.z, k))

    def at(self, r, zs, half):
        return self.ref.at[flip(self.e, r), zs, self.c, :, self.cols[half]]

    def slot(self, k, r, half):
        return self.plane + k * 6 + (r - 1) * 2 + half

    def pass_on(self, k):
        wire, z, nc = self.wire, self.z, self.nc
        zs = self.shard(k)
        whole = self.ref.at[self.e, zs, self.c]
        if k:
            wire.arrived(whole, self.line + zs, {"context": zs})
        wire.start(
            whole, whole, self.line + zs, {"context": z + 1}, when=(zs <= z) & (z < nc - 1)
        )
        wire.start(whole, whole, self.line + zs, {"context": z - 1}, when=(zs >= z) & (z > 0))

    def spread(self, k):
        zs = self.shard(k)
        for half, mask in ((0, 1), (1, 2), (1, 1), (0, 2)):
            part = self.at(0, zs, half)
            self.wire.start(part, part, self.slot(k, mask, half), self.ids[mask])

    def forward(self, k):
        zs = self.shard(k)
        for half, mask in ((0, 1), (1, 2)):
            part = self.at(mask, zs, half)
            self.wire.arrived(part, self.slot(k, mask, half), self.ids[mask])
            self.wire.start(part, part, self.slot(k, 3, half), self.ids[3 - mask])

    def share(self, k):
        zs = self.shard(k)
        for r, half in ((1, 1), (2, 0), (3, 0), (3, 1)):
            self.wire.arrived(self.at(r, zs, half), self.slot(k, r, half), self.ids[r])
        part = self.ref.at[:, zs, self.c]
        self.wire.start(part, part, self.core + k, {"dp": 1 - self.c})

    def complete(self):
        for k in range(self.nc):
            zs = self.shard(k)
            self.wire.arrived(self.ref.at[:, zs, 1 - self.c], self.core + k, {"dp": 1 - self.c})


class PlaneGather:
    def __init__(self, wire, ref, e, own=None):
        self.wire, self.ref, self.own = wire, ref, own
        self.half = ref.shape[-1] // 2
        self.ids = plane_ids(e)
        self.first = wire.slots(6)

    def at(self, r, half):
        columns = pl.ds(half * self.half, self.half)
        if r == 0 and self.own is not None:
            return self.own.at[:, columns]
        return self.ref.at[r, :, columns]

    def slot(self, r, half):
        return self.first + (r - 1) * 2 + half

    def send(self, r, half, to, mask):
        self.wire.start(
            lambda: self.at(r, half), lambda: self.at(to, half), self.slot(to, half), self.ids[mask]
        )

    def spread(self):
        for half, mask in ((0, 1), (1, 2), (1, 1), (0, 2)):
            self.send(0, half, mask, mask)

    def forward(self):
        for half, mask in ((0, 1), (1, 2)):
            self.wire.arrived(self.at(mask, half), self.slot(mask, half), self.ids[mask])
            self.send(mask, half, 3, 3 - mask)

    def near(self, r):
        half = 1 if r == 1 else 0
        self.wire.arrived(self.at(r, half), self.slot(r, half), self.ids[r])

    def far(self):
        for half in (0, 1):
            self.wire.arrived(self.at(3, half), self.slot(3, half), self.ids[3])

    def complete(self):
        self.near(1)
        self.near(2)
        self.far()


def causal(scores, first_row):
    place = lax.broadcasted_iota(jnp.int32, scores.shape, 0)
    row = first_row + lax.broadcasted_iota(jnp.int32, scores.shape, 1)
    return jnp.where(place <= row, scores, MASKED)


def swap_halves(values):
    return pltpu.roll(values, HEAD_DIMENSION // 2, 1)


class PlaneScatter:
    def __init__(self, wire, land, ids):
        self.wire, self.land, self.ids, self.part = wire, land, ids, None
        self.half = land.shape[-1]
        self.first = wire.slots(6)

    def send(self, source, mask, slot):
        self.wire.start(source, lambda: self.land.at[slot], self.first + slot, self.ids[mask])

    def near(self, r):
        self.send(self.part(r, r - 1), r, r - 1)

    def far(self):
        self.send(self.part(3, 0), 1, 2)
        self.send(self.part(3, 1), 2, 3)

    def relay(self, part=None):
        for half, r in ((0, 2), (1, 1)):
            slot = 2 + half
            self.wire.arrived(self.land.at[slot], self.first + slot, self.ids[3 - r])
            take = part or self.part
            mine = take(r, half)
            add_into(mine, self.land.at[slot])
            self.send(lambda r=r, half=half, take=take: take(r, half), r, 4 + half)

    def total(self, own):
        for slot, half, mask in ((0, 0, 1), (1, 1, 2), (4, 0, 2), (5, 1, 1)):
            self.wire.arrived(self.land.at[slot], self.first + slot, self.ids[mask])
            columns = pl.ds(half * self.half, self.half)
            rows = own.shape[0] // 4

            @pl.loop(0, 4)
            def _(n):
                here = pl.ds(pl.multiple_of(n * rows, rows), rows)
                own[here, columns] += self.land[slot, here].astype(F32)


class LineSum:
    def __init__(self, wire, block, land, z, nc, up=True):
        self.wire, self.block, self.land, self.z, self.nc, self.up = wire, block, land, z, nc, up
        self.first = wire.slots(nc)

    def clear(self):
        for slot in range(self.nc):

            def zero(slot=slot):
                self.land[slot] = jnp.zeros(self.land.shape[1:], BF16)

            pl.when(slot == self.z if self.up else slot <= self.z)(zero)

    def send(self):
        z = self.z
        for d in range(self.nc - 1, 0, -1):
            self.leave(z - d, z >= d)
            if self.up:
                self.leave(z + d, z + d < self.nc)

    def leave(self, j, wanted):
        self.wire.start(
            self.block(j), self.land.at[self.z], self.first + self.z, {"context": j}, when=wanted
        )

    def total(self):
        z = self.z
        for d in range(1, self.nc):
            for source, wanted in ((z + d, z + d < self.nc), (z - d, z >= d))[: 1 + self.up]:

                def wait(source=source):
                    self.wire.arrived(
                        self.land.at[source], self.first + source, {"context": source}
                    )

                pl.when(wanted)(wait)
        total = self.block(z)[...].astype(F32)
        for slot in range(self.nc):
            total = total + self.land[slot].astype(F32)
        return total


class RowsScatter:
    def __init__(self, wire, buf, core, plane, lines, e, z, c, nc, start, width, half):
        self.wire, self.buf, self.core, self.plane = wire, buf, core, plane
        self.e, self.c = e, c
        self.all = pl.ds(start, width)
        self.cols = (pl.ds(start, half), pl.ds(start + half, width - half))
        self.ids = plane_ids(e)
        self.core_slot = wire.slots(1)
        self.first = wire.slots(6)
        rows = buf.shape[2] // nc
        self.line = LineSum(
            wire,
            lambda j: buf.at[c, e, pl.ds(pl.multiple_of(j * rows, rows), rows), self.all],
            lines,
            z,
            nc,
        )

    def share(self):
        self.wire.start(
            self.buf.at[1 - self.c, :, :, self.all], self.core, self.core_slot, {"dp": 1 - self.c}
        )

    def at(self, r, half):
        return self.buf.at[self.c, flip(self.e, r), :, self.cols[half]]

    def send(self, r, half, mask, slot):
        self.wire.start(
            self.at(r, half), self.plane(slot, half), self.first + slot, self.ids[mask]
        )

    def merge(self, before=None):
        self.wire.arrived(self.core, self.core_slot, {"dp": 1 - self.c})
        for r in (3, 1, 2, 0):
            block = flip(self.e, r)
            part = self.buf.at[self.c, block, :, self.all]
            add_into(part, self.core.at[block])
            if r == 3:
                if before is not None:
                    before()
                self.send(3, 0, 1, 2)
                self.send(3, 1, 2, 3)
            elif r:
                self.send(r, r - 1, r, r - 1)

    def add(self, r, half, slot, mask):
        land = self.plane(slot, half)
        self.wire.arrived(land, self.first + slot, self.ids[mask])
        add_into(self.at(r, half), land)

    def relay(self):
        for half, r in ((0, 2), (1, 1)):
            self.add(r, half, 2 + half, 3 - r)
            self.send(r, half, r, 4 + half)

    def total(self):
        for slot, half, mask in ((0, 0, 1), (1, 1, 2), (4, 0, 2), (5, 1, 1)):
            self.add(0, half, slot, mask)


class ExpertLine:
    def __init__(self, wire, base, land, sems, z, nc):
        self.wire, self.base, self.land = wire, base, land
        self.ins, self.out, self.sems, self.z, self.nc = None, None, sems, z, nc
        self.end = (z == 0) | (z == nc - 1)
        self.inner = jnp.logical_not(self.end)
        self.width = base.shape[-1] // EXP_DEV
        self.first = wire.slots((nc + 1) * EXP_DEV)
        self.sent = []

    def part(self, ref, j, i):
        return ref.at[j, :, pl.ds(i * self.width, self.width)]

    def combine(self, sources, stores):
        out, step = self.out, self.ins.shape[2]
        count = sources[0].shape[0] // step

        def loads(p):
            rows = pl.ds(p * step, step)
            return [
                pltpu.make_async_copy(source.at[rows], self.ins.at[k, p], self.sems.at[4 * k + p])
                for k, source in enumerate(sources)
            ]

        def store(p):
            pairs = stores(pl.ds(p * step, step), out.at[p % 2])
            return [
                pltpu.make_async_copy(source, dest, self.sems.at[16 + 2 * n + p % 2])
                for n, (source, dest) in enumerate(pairs)
            ]

        for p in range(count):
            for copy in loads(p):
                copy.start()
        for p in range(count):
            for copy in loads(p):
                copy.wait()
            if p > 1:
                for copy in store(p - 2):
                    copy.wait()
            total = self.ins[0, p].astype(F32)
            for k in range(1, len(sources)):
                total = total + self.ins[k, p].astype(F32)
            out[p % 2] = total.astype(out.dtype)
            for copy in store(p):
                copy.start()
        for p in range(max(0, count - 2), count):
            for copy in store(p):
                copy.wait()

    def copy(self, i, r, number):
        target, slot = flip(self.z, r), self.z
        if r == 3:
            target = jnp.where(self.end, flip(self.z, 1), target)
            slot = jnp.where(self.end, self.nc, slot)
        return pltpu.make_async_remote_copy(
            src_ref=self.part(self.base, flip(self.z, r), i),
            dst_ref=self.part(self.land, slot, i),
            send_sem=self.wire.sends.at[number],
            recv_sem=self.wire.recvs.at[self.first + slot * EXP_DEV + i],
            device_id={"context": target},
            device_id_type=MESH,
        )

    def send(self, i, r, when=None):
        number = len(self.sent)
        guard(when, self.copy(i, r, number).start)
        self.sent.append((when, i, r, number))

    def finish(self):
        for when, i, r, number in self.sent:
            guard(when, self.copy(i, r, number).wait_send)

    def arrived(self, slot, i):
        land = self.part(self.land, slot, i)
        self.wire.arrived(land, self.first + slot * EXP_DEV + i, {"context": self.z})

    def relay_loads(self, i, p):
        step = self.ins.shape[2]
        rows = pl.ds(p * step, step)
        sources = (self.part(self.base, flip(self.z, 2), i), self.part(self.land, self.nc, i))
        return [
            pltpu.make_async_copy(
                source.at[rows], self.ins.at[k, p], self.sems.at[4 * k + p]
            )
            for k, source in enumerate(sources)
        ]

    def relay_store(self, i, p):
        step = self.ins.shape[2]
        mine = self.part(self.base, flip(self.z, 2), i).at[pl.ds(p * step, step)]
        return pltpu.make_async_copy(self.ins.at[0, p], mine, self.sems.at[16 + p])

    def relay_steps(self):
        return range(self.base.shape[1] // self.ins.shape[2])

    def relay_begin(self, i):
        self.relayed = i

        def begin():
            self.arrived(self.nc, i)
            for p in self.relay_steps():
                for copy in self.relay_loads(i, p):
                    copy.start()

        pl.when(self.inner)(begin)

    def relay_add(self):
        i = self.relayed

        def add():
            for p in self.relay_steps():
                for copy in self.relay_loads(i, p):
                    copy.wait()
                a, b = (self.ins[k, p].astype(F32) for k in range(2))
                self.ins[0, p] = (a + b).astype(BF16)
                self.relay_store(i, p).start()

        pl.when(self.inner)(add)

    def relay_send(self, i):
        def wait():
            for p in self.relay_steps():
                self.relay_store(i, p).wait()

        pl.when(self.inner)(wait)
        self.send(i, 2, when=self.inner)

    def last(self, i, results):
        z = self.z
        sources = [self.part(self.base, z, i)]
        for r in (1, 2):
            self.arrived(flip(z, r), i)
            sources.append(self.part(self.land, flip(z, r), i))

        def stores(rows, wide):
            pairs, first = [], 0
            for result in results:
                columns = pl.ds(first, result.shape[-1])
                pairs.append((wide.at[:, columns], result.at[i, rows]))
                first += result.shape[-1]
            return pairs

        pl.when(self.end)(lambda: self.combine(sources, stores))

        def inner():
            self.arrived(flip(z, 3), i)
            self.combine(sources + [self.part(self.land, flip(z, 3), i)], stores)

        pl.when(self.inner)(inner)


def layer_kernel(
    nc,
    experts,
    cos_ref,
    sin_ref,
    routes_ref,
    qkv_ref,
    small_ref,
    wo_shard_ref,
    x_hbm,
    d_out_hbm,
    w_gu_hbm,
    w_dn_hbm,
    layer_hbm,
    d_x_hbm,
    sum_q_ref,
    sum_o_ref,
    sum_gu_hbm,
    sum_dn_hbm,
    base_hbm,
    land_hbm,
    y_hbm,
    wq_hbm,
    wo_hbm,
    cot_hbm,
    inputs_hbm,
    query_hbm,
    heads_hbm,
    hidden_hbm,
    wk_all,
    kv_ref,
    gate_all,
    gates_ref,
    gains_ref,
    x_all,
    y_land,
    dx_land,
    core_land,
    plane_q,
    plane_k,
    lines_o,
    lines_q,
    lines_k,
    dkv_land,
    d_in_ref,
    dg_lanes,
    dg_part,
    dg_land,
    sends_f,
    recvs_f,
    sends_c,
    recvs_c,
    sends_x,
    recvs_x,
    sends_1,
    recvs_1,
    sends_2,
    recvs_2,
    sends_e,
    recvs_e,
    hand_sends,
    hand_recvs,
    stage_sems,
    load_sems,
    out_sems,
    sum_sems,
    y_sems,
    credits,
):
    e, z, c = (lax.axis_index(a) for a in ("expert", "context", "dp"))
    size = HEAD_DIMENSION
    blocks, tokens, width = cot_hbm.shape
    ff = w_dn_hbm.shape[1]
    query_width = QUERY_HEADS * size
    key_width = KEY_VALUE_HEADS * size
    qkv_width = query_width + 2 * key_width
    rest = wk_all.shape[-1]
    grad_width = base_hbm.shape[-1]
    ids = plane_ids(e)
    sibling = {"dp": 1 - c}
    bottom, even, odd, top = z == 0, lax.rem(z, 2) == 0, lax.rem(z, 2) == 1, z == nc - 1
    wire_1, wire_2, wire_e = Wire(sends_1, recvs_1), Wire(sends_2, recvs_2), Wire(sends_e, recvs_e)
    expert = ExpertLine(wire_e, base_hbm, land_hbm, sum_sems, z, nc)
    wire_c = Wire(sends_c, recvs_c)
    gather_cot = PlaneGather(wire_c, cot_hbm, e, d_out_hbm)
    wire_x = Wire(sends_x, recvs_x)
    gather = PlaneGather(wire_x, x_all, e)
    scatter_dx = PlaneScatter(wire_1, dx_land, ids)
    scatter_y = PlaneScatter(wire_2, y_land, ids)
    dg_slot = wire_1.slots(3)

    def front_phase(wq_ref, wo_ref, x_ref, inputs_ref, query_ref, heads_ref, hidden_ref, kv_scr, q_scr):
        wire = Wire(sends_f, recvs_f)
        kv_width = 2 * key_width
        load_x = pltpu.make_async_copy(x_hbm, x_ref, load_sems.at[0])
        load_x.start()
        wq_ref[e, z, c] = qkv_ref[:, pl.ds(0, query_width)]
        wo_ref[e, z, c] = wo_shard_ref[...]
        wk_all[e, z, c, :, pl.ds(0, kv_width)] = qkv_ref[:, pl.ds(query_width, kv_width)]
        wk_all[e, z, c, :, pl.ds(kv_width, SMALL)] = small_ref[...]
        greet(
            [(ids[m], None) for m in (1, 2, 3)]
            + [(sibling, None)]
            + [({"context": z + d}, z + d < nc) for d in range(1, nc)]
            + [({"context": z - d}, z >= d) for d in range(1, nc)]
        )
        gather_k = RowsGather(wire, wk_all, e, z, c, nc, 256)
        gather_q = RowsGather(wire, wq_ref, e, z, c, nc, 768)
        gather_o = RowsGather(wire, wo_ref, e, z, c, nc, 768)
        gather_k.go("l0", "s0")
        gather_q.go("s0")
        gather_k.go("l1", "s1", "f0", "l2", "s2")
        gather_q.go("l0")
        gather_k.go("f1", "h0", "l3", "s3")
        gather_q.go("l1", "s1")
        gather_o.go("l0")
        gather_k.go("f2", "h1", "f3")
        gather_q.go("l2", "s2")
        gather_k.go("h2")
        gather_o.go("l1")
        gather_q.go("f0")
        gather_k.go("h3")
        gather_q.go("l3", "s3")
        gather_k.go("c")
        load_x.wait()
        rows = x_ref[...].astype(F32)
        scale1 = lax.rsqrt(jnp.mean(rows * rows, -1, keepdims=True) + EPSILON)

        small = wk_all[:, :, :, :, pl.ds(kv_width, SMALL)].reshape(width, SMALL)
        small = jnp.transpose(small.astype(F32))
        gain_first, gain_second = small[experts : experts + 1], small[experts + 1 : experts + 2]
        gains_ref[0:1] = gain_first
        gains_ref[1:2] = gain_second
        inputs_ref[...] = (rows * scale1 * gain_first).astype(BF16)
        kv_scr[...] = dot_nn(inputs_ref[...], wk_all[...].reshape(width, kv_width + SMALL))

        def turned(head):
            return (head * cos_ref[...] + swap_halves(head) * sin_ref[...]).astype(BF16)

        line = wire.slots(KEY_VALUE_HEADS * nc)
        for j in range(KEY_VALUE_HEADS):
            kv_ref[j, z, :, pl.ds(0, size)] = turned(kv_scr[:, pl.ds(j * size, size)])
            value = kv_scr[:, pl.ds(kv_width // 2 + j * size, size)]
            kv_ref[j, z, :, pl.ds(size, size)] = value.astype(BF16)
            mine = kv_ref.at[j, z]
            for d in range(nc - 1, 0, -1):
                wire.start(mine, mine, line + j * nc + z, {"context": z + d}, when=z + d < nc)

        def keys_here(j):
            for d in range(1, nc):

                def wait(d=d):
                    wire.arrived(kv_ref.at[j, z - d], line + j * nc + z - d, {"context": z - d})

                pl.when(z >= d)(wait)

        outs = [
            pltpu.make_async_copy(source, dest, out_sems.at[n])
            for n, (source, dest) in enumerate(
                (
                    (inputs_ref, inputs_hbm),
                    (query_ref, query_hbm),
                    (heads_ref, heads_hbm),
                    (hidden_ref, hidden_hbm),
                    (wq_ref, wq_hbm),
                    (wo_ref, wo_hbm),
                )
            )
        ]
        outs[0].start()
        for later in range(1, nc):

            def clear(later=later):
                for j in range(KEY_VALUE_HEADS):
                    kv_ref[j, z + later] = jnp.zeros(kv_ref.shape[2:], BF16)

            pl.when(z + later < nc)(clear)
        gather_q.go("f1", "f2", "h0")
        gather_o.go("s0")
        gather_q.go("f3", "h1")
        gather_o.go("s1")
        gather_q.go("h2", "h3", "c")
        outs[4].start()
        gather_o.go("f0", "f1")
        gather_cot.spread()

        @pl.loop(0, query_width // 256)
        def _(n):
            columns = pl.ds(pl.multiple_of(n * 256, 256), 256)
            q_scr[:, columns] = dot_nn(
                inputs_ref[...], wq_ref[:, :, :, :, columns].reshape(width, 256)
            )

        @pl.loop(0, QUERY_HEADS)
        def _(h):
            columns = pl.ds(pl.multiple_of(h * size, size), size)
            query_ref[:, columns] = turned(q_scr[:, columns])

        outs[1].start()

        logits = kv_scr[:, pl.ds(kv_width, SMALL)]
        lanes = lax.broadcasted_iota(jnp.int32, logits.shape, 1)
        routes = jnp.concatenate(
            [routes_ref[...].astype(F32), jnp.zeros((SMALL - TOP, tokens), F32)], 0
        )
        routes = jnp.transpose(routes).astype(jnp.int32)
        named = lanes == routes[:, 0:1]
        for k in range(1, TOP):
            named = named | (lanes == routes[:, k : k + 1])
        logits = jnp.where(named, logits, MASKED)
        expd = jnp.exp(logits - jnp.max(logits, -1, keepdims=True))
        gates = expd / jnp.sum(expd, -1, keepdims=True)
        gate_all[0] = jnp.transpose(gates)[:GATE_ROWS]
        gate_slot = wire.slots(3)
        for r in (1, 2, 3):
            wire.start(gate_all.at[0], gate_all.at[r], gate_slot + r - 1, ids[r])

        length = nc * tokens
        group = QUERY_HEADS // KEY_VALUE_HEADS

        def attend(first, last):
            j = first // group
            key = kv_ref[j, :, :, pl.ds(0, size)].reshape(length, size)
            value = kv_ref[j, :, :, pl.ds(size, size)].reshape(length, size)
            value_turned = jnp.transpose(value)

            @pl.loop(first, last)
            def _(h):
                column = pl.multiple_of(h * size, size)
                scores = causal(dot_nt(key, query_ref[:, pl.ds(column, size)]), z * tokens)
                largest = jnp.max(scores, 0, keepdims=True)
                expd = jnp.exp((scores - largest) * (size**-0.5))
                total = jnp.sum(expd, 0, keepdims=True)
                mixed = dot_nn(value_turned, expd.astype(BF16)) / total
                heads_ref[:, pl.ds(column, size)] = jnp.transpose(mixed).astype(BF16)

        half = group // 2
        keys_here(0)
        attend(0, half)
        gather_o.go("l2", "s2")
        attend(half, group)
        gather_o.go("l3", "s3", "f2", "h0")
        keys_here(1)
        attend(group, group + half)
        gather_o.go("f3", "h1")
        attend(group + half, QUERY_HEADS)
        gather_o.go("h2")
        gather_cot.forward()
        gather_o.go("h3", "c")
        outs[5].start()
        outs[2].start()
        part = width // wo_ref.shape[0]
        for block in range(wo_ref.shape[0]):
            weight = wo_ref[block].reshape(part, width)
            columns = pl.ds(block * part, part)
            hidden_ref[:, columns] = x_ref[:, columns].astype(F32) + dot_nt(heads_ref[...], weight)
        hidden = hidden_ref[...]
        scale2 = lax.rsqrt(jnp.mean(hidden * hidden, -1, keepdims=True) + EPSILON)
        x_all[0] = (hidden * scale2 * gains_ref[1:2]).astype(BF16)
        gather.spread()
        outs[3].start()
        for r in (1, 2, 3):
            wire.arrived(gate_all.at[r], gate_slot + r - 1, ids[r])
        for r in range(gate_all.shape[0]):
            zeros = jnp.zeros((SMALL - GATE_ROWS, tokens), F32)
            turned_gates = jnp.transpose(jnp.concatenate([gate_all[r], zeros], 0))
            both = [
                jnp.sum(jnp.where(lanes == e * EXP_DEV + i, turned_gates, 0.0), -1, keepdims=True)
                for i in range(EXP_DEV)
            ]
            gates_ref[r] = jnp.where(lanes == 0, both[0], jnp.where(lanes == 1, both[1], 0.0))
        for copy in outs:
            copy.wait()
        wire.finish()

    def token_phase(w_gu, w_dn, cot_all, a_all, dgu_all, stage, ins, x_turned, cot_turned):
        expert.ins = ins
        scatter_dx.part = lambda r, half: x_all.at[r, :, pl.ds(half * width // 2, width // 2)]
        sources = [
            (w_gu_hbm.at[0], w_gu.at[0]),
            (w_dn_hbm.at[0], w_dn.at[0]),
            (d_out_hbm, cot_all.at[0]),
            (w_gu_hbm.at[1], w_gu.at[1]),
            (w_dn_hbm.at[1], w_dn.at[1]),
            (cot_hbm.at[1:], cot_all.at[1:]),
        ]
        loads = [
            pltpu.make_async_copy(source, dest, load_sems.at[n])
            for n, (source, dest) in enumerate(sources)
        ]
        for copy in loads[:5]:
            copy.start()
        step = 256
        wide = 512
        dg_lanes[...] = jnp.zeros_like(dg_lanes)

        def hidden_units(r, i, count=1):
            lane = lax.broadcasted_iota(jnp.int32, (1, SMALL), 1)
            here = pl.ds(r, count)
            flat = count * tokens

            @pl.loop(0, ff // step)
            def _(f):
                column = pl.multiple_of(f * step, step)
                rows = x_all[here].reshape(flat, width)
                grads = cot_all[here].reshape(flat, width)
                gate_part = dot_nn(rows, w_gu[i, :, pl.ds(column, step)])
                up_part = dot_nn(rows, w_gu[i, :, pl.ds(ff + column, step)])
                raw = dot_nt(grads, w_dn[i, pl.ds(column, step), :])
                gate = gates_ref[here].reshape(flat, SMALL)
                gate = jnp.sum(jnp.where(lane == i, gate, 0.0), -1, keepdims=True)
                sigma = jax.nn.sigmoid(gate_part)
                silu = gate_part * sigma
                act = silu * up_part
                lanes = lax.broadcasted_iota(jnp.int32, (flat, SMALL), 1)
                d_gate = jnp.where(
                    lanes == e * EXP_DEV + i, jnp.sum(act * raw, -1, keepdims=True), 0.0
                )
                dg_lanes[here] += d_gate.reshape(count, tokens, SMALL)

                def put(ref, first, values):
                    values = values.astype(BF16).reshape(count, tokens, step)
                    ref[here, :, pl.ds(pl.multiple_of(first, step), step)] = values

                put(a_all, i * ff + column, act * gate)
                d_act = raw * gate
                d_gate_part = d_act * up_part * sigma * (1.0 + gate_part * (1.0 - sigma))
                put(dgu_all, i * 2 * ff + column, d_gate_part)
                put(dgu_all, i * 2 * ff + ff + column, d_act * silu)

        def turn(rows, turned, r):
            @pl.loop(0, width // wide)
            def _(n):
                columns = pl.ds(pl.multiple_of(n * wide, wide), wide)
                turned[columns, pl.ds(r * tokens, tokens)] = jnp.transpose(rows[r, :, columns])

        def y_copy(r):
            return pltpu.make_async_copy(cot_all.at[r], y_hbm.at[r], out_sems.at[r])

        def outputs(r, count=1):
            here = pl.ds(r, count)
            flat = count * tokens

            @pl.loop(0, width // wide)
            def _(n):
                columns = pl.ds(pl.multiple_of(n * wide, wide), wide)
                low = dgu_all[here].reshape(flat, EXP_DEV * 2 * ff)
                d_rows = dot_nt(low[:, : 2 * ff], w_gu[0, columns, :])
                d_rows += dot_nt(low[:, 2 * ff :], w_gu[1, columns, :])
                weight = w_dn[:, :, columns].reshape(EXP_DEV * ff, wide)
                out = dot_nn(a_all[here].reshape(flat, EXP_DEV * ff), weight).astype(BF16)
                for k in range(count):
                    rows = slice(k * tokens, (k + 1) * tokens)
                    cot_all[r + k, :, columns] = out[rows]
                    if r == 0:
                        d_in_ref[:, columns] = d_rows
                    else:
                        x_all[r + k, :, columns] = d_rows[rows].astype(BF16)

            for k in range(r, r + count):
                y_copy(k).start()
                dg_part[k] = jnp.transpose(dg_lanes[k])[:GATE_ROWS]
                if k:
                    wire_1.start(dg_part.at[k], dg_land.at[k - 1], dg_slot + k - 1, ids[k])

        half_rows = width // nc // 2
        def where(k):
            high = lax.rem(lax.div(z, 2) + 1 + lax.div(k, 2), 2)
            return 2 * high + lax.rem(z + 1 + k, 2)

        def keep(i, k):
            slot = lax.rem(k, 2)
            return pltpu.make_async_copy(
                stage.at[slot, c], expert.part(base_hbm, where(k), i), stage_sems.at[slot]
            )

        def hand(i, k):
            return pltpu.make_async_remote_copy(
                src_ref=stage.at[lax.rem(k, 2), 1 - c],
                dst_ref=core_land.at[k],
                send_sem=hand_sends.at[i * nc + k],
                recv_sem=hand_recvs.at[i * nc + k],
                device_id=sibling,
                device_id_type=MESH,
            )

        def settle(i, k):
            hand(i, k).wait_recv()
            add_into(stage.at[lax.rem(k, 2), c], core_land.at[k])
            keep(i, k).start()

        def clear(i, k):
            keep(i, k).wait()
            hand(i, k).wait_send()

        def leave(i, r):
            if i == 0 and r == 2:
                expert.send(i, r, when=expert.end)
            elif i == 0 and r == 1 or r == 3:
                expert.send(i, r)
            elif r == 2:
                expert.send(i, r, when=bottom)
            elif r == 1:
                expert.send(i, r, when=even)

        def weight_grads(i, between=lambda k: None):
            @pl.loop(0, nc)
            def _(k):
                @pl.when(k >= 2)
                def _():
                    clear(i, k - 2)

                for n in (2, 3):

                    @pl.when(k == n)
                    def _(n=n):
                        leave(i, 5 - n)

                rows_at = pl.ds(pl.multiple_of(where(k) * 2 * half_rows, 2 * half_rows), 2 * half_rows)
                for first, rows, grad, start, count in (
                    (0, x_turned[rows_at, :], dgu_all, i * 2 * ff, 2),
                    (2 * ff, cot_turned[rows_at, :], a_all, i * ff, 1),
                ):

                    @pl.loop(0, count)
                    def _(n):
                        column = pl.multiple_of(n * ff, ff)
                        part = grad[:, :, pl.ds(pl.multiple_of(start + column, ff), ff)]
                        result = dot_nn(rows, part.reshape(blocks * tokens, ff)).astype(BF16)
                        stage[lax.rem(k, 2), :, :, pl.ds(pl.multiple_of(first + column, ff), ff)] = (
                            result.reshape(2, half_rows, ff)
                        )

                if i:

                    @pl.when(k == 0)
                    def _():
                        pl.semaphore_wait(credits.at[3], 1)

                hand(i, k).start()

                @pl.when(k >= 1)
                def _():
                    settle(i, k - 1)

                between(k)

        for copy in loads[:3]:
            copy.wait()
        gather_cot.complete()
        loads[5].start()
        for copy in loads[3:5]:
            copy.wait()

        @pl.loop(0, EXP_DEV)
        def _(i):
            hidden_units(0, i)

        gather.forward()
        turn(x_all, x_turned, 0)
        turn(cot_all, cot_turned, 0)
        outputs(0)
        loads[5].wait()
        for r in range(1, blocks):
            turn(cot_all, cot_turned, r)
        gather.near(1)
        gather.near(2)
        turn(x_all, x_turned, 1)
        turn(x_all, x_turned, 2)
        hidden_units(1, 0, 2)
        gather.far()
        turn(x_all, x_turned, 3)
        hidden_units(3, 0)
        weight_grads(0)
        hidden_units(1, 1, 2)
        clear(0, nc - 2)
        leave(0, 1)
        settle(0, nc - 1)
        pl.semaphore_signal(credits.at[3], inc=1, device_id=sibling, device_id_type=MESH)
        wire_x.finish()
        outputs(1, 2)
        scatter_dx.near(1)
        scatter_dx.near(2)
        hidden_units(3, 1)
        expert.relay_begin(0)
        outputs(3)
        scatter_dx.far()
        clear(0, nc - 1)
        expert.relay_add()

        def between(k):
            @pl.when(k == 0)
            def _():
                expert.relay_send(0)

            @pl.when(k == 1)
            def _():
                scatter_dx.relay()

        weight_grads(1, between)
        scatter_dx.total(d_in_ref)
        for r in (1, 2):
            pl.semaphore_signal(credits.at[r], inc=1, device_id=ids[r], device_id_type=MESH)
        settle(1, nc - 1)
        for k in (nc - 2, nc - 1):
            clear(1, k)
        leave(1, 1)
        for r in range(blocks):
            y_copy(r).wait()
        wire_1.finish()
        wire_c.finish()
        pl.semaphore_signal(credits.at[0], inc=1, device_id=sibling, device_id_type=MESH)

    def token_rows_phase(
        weight,
        grads_o,
        grads_q,
        x_ref,
        inputs_ref,
        query_ref,
        heads_ref,
        hidden_ref,
        d_hidden_ref,
        d_attn_ref,
        d_heads_ref,
        d_all_ref,
        rows_ref,
        dkv_acc,
        dkv_ref,
        y_relay,
        ins,
        out_wide,
    ):
        expert.ins, expert.out = ins, out_wide
        cot_ref, d_inputs_ref = d_heads_ref, hidden_ref
        scatter_y.part = lambda r, half: y_hbm.at[r, :, pl.ds(half * width // 2, width // 2)]
        y_loads = [
            pltpu.make_async_copy(scatter_y.part(2 - half, half), y_relay.at[half], y_sems.at[half])
            for half in range(2)
        ]
        for copy in y_loads:
            copy.start()
        planes = grads_o.shape[1]
        part = width // planes
        sources = (
            (hidden_hbm, hidden_ref),
            (d_out_hbm, cot_ref),
            (wo_hbm, weight),
            (heads_hbm, heads_ref),
            (query_hbm, query_ref),
            (x_hbm, x_ref),
            (inputs_hbm, inputs_ref),
        )
        loads = [
            pltpu.make_async_copy(source, dest, load_sems.at[4 + n])
            for n, (source, dest) in enumerate(sources)
        ]
        for copy in loads:
            copy.start()
        for r in (1, 2):
            scatter_y.near(r)
        scatter_y.far()

        def rows_scatter(buf, core, plane, lines, start, count, half):
            return RowsScatter(
                wire_2,
                buf,
                core,
                plane,
                lines,
                e,
                z,
                c,
                nc,
                start,
                count,
                half,
            )

        rows_of = part // 2
        scatter_o = rows_scatter(
            grads_o,
            x_all.at[:, pl.ds(0, rows_of)],
            lambda slot, half: dx_land.at[slot, pl.ds(0, rows_of)],
            lines_o,
            0,
            width,
            width // 2,
        )
        scatter_q = rows_scatter(
            grads_q,
            core_land.at[:, :, pl.ds(0, query_width)],
            lambda slot, half: plane_q.at[slot],
            lines_q,
            0,
            query_width,
            query_width // 2,
        )
        rest_half = rest // 256 * 128
        scatter_k = rows_scatter(
            grads_q,
            core_land.at[:, :, pl.ds(query_width, rest)],
            lambda slot, half: plane_k.at[
                slot, :, pl.ds(0, rest - rest_half if half else rest_half)
            ],
            lines_k,
            query_width,
            rest,
            rest_half,
        )
        scatter_kv = [
            LineSum(wire_2, lambda j, h=h: dkv_ref.at[h, j], dkv_land.at[h], z, nc, up=False)
            for h in range(KEY_VALUE_HEADS)
        ]

        for scatter in (scatter_o, scatter_q, scatter_k):
            scatter.line.clear()
        for line in scatter_kv:
            line.clear()

        loads[0].wait()
        loads[1].wait()
        hidden, d_in = hidden_ref[...], d_in_ref[...]
        scale2 = lax.rsqrt(jnp.mean(hidden * hidden, -1, keepdims=True) + EPSILON)
        scaled = d_in * gains_ref[1:2]
        mean = jnp.mean(scaled * hidden, -1, keepdims=True)
        d_hidden = cot_ref[...].astype(F32) + scale2 * scaled
        d_hidden = d_hidden - hidden * (scale2 * scale2 * scale2 * mean)
        d_hidden_ref[...] = d_hidden
        d_attn_ref[...] = d_hidden.astype(BF16)
        rows_ref[...] = jnp.zeros_like(rows_ref)
        rows_ref[experts + 1 : experts + 2, :] = jnp.sum(d_in * hidden * scale2, 0, keepdims=True)

        loads[2].wait()

        @pl.loop(0, query_width // 256)
        def _(n):
            columns = pl.ds(pl.multiple_of(n * 256, 256), 256)
            out = weight[:, :, :, :, columns].reshape(width, 256)
            d_heads_ref[:, columns] = dot_nn(d_attn_ref[...], out).astype(BF16)

        load_q = pltpu.make_async_copy(wq_hbm, weight, load_sems.at[0])
        load_q.start()
        loads[3].wait()

        def row_grads(buf, left, right, first, count, extra=None):
            @pl.loop(0, planes)
            def _(block):
                columns = pl.ds(pl.multiple_of(block * part, part), part)
                result = dot_tn(left[:, columns], right)
                if extra is not None:
                    result = result + extra(columns)
                result = result.astype(BF16).reshape(nc, 2, part // nc // 2, count)
                for half in range(2):
                    buf[half, block, :, pl.ds(first, count)] = result[:, half].reshape(
                        part // 2, count
                    )

        length = nc * tokens
        group = QUERY_HEADS // KEY_VALUE_HEADS
        loads[4].wait()
        dkv_acc[...] = jnp.zeros_like(dkv_acc)

        def attend(j, first, last):
            key = kv_ref[j, :, :, pl.ds(0, size)].reshape(length, size)
            value = kv_ref[j, :, :, pl.ds(size, size)].reshape(length, size)
            key_turned = jnp.transpose(key)

            @pl.loop(j * group + first, j * group + last)
            def _(h):
                columns = pl.ds(pl.multiple_of(h * size, size), size)
                query, grad = query_ref[:, columns], d_heads_ref[:, columns]
                scores = causal(dot_nt(key, query), z * tokens)
                largest = jnp.max(scores, 0, keepdims=True)
                expd = jnp.exp((scores - largest) * (size**-0.5))
                probs = expd * (1.0 / jnp.sum(expd, 0, keepdims=True))
                d_probs = dot_nt(value, grad)
                inner = jnp.sum(probs * d_probs, 0, keepdims=True)
                d_raw = (probs * (d_probs - inner) * (size**-0.5)).astype(BF16)
                d_query = jnp.transpose(dot_nn(key_turned, d_raw))
                d_query = d_query * cos_ref[...] - swap_halves(d_query) * sin_ref[...]
                d_all_ref[:, columns] = d_query.astype(BF16)
                dkv_acc[j, :, pl.ds(0, size)] += dot_nn(d_raw, query)
                dkv_acc[j, :, pl.ds(size, size)] += dot_nn(probs.astype(BF16), grad)

        def round_kv(j):
            for block in range(nc):
                rows = dkv_acc[j, pl.ds(block * tokens, tokens), :]
                dkv_ref[j, block] = rows.astype(BF16)

        def enter():
            pl.semaphore_wait(credits.at[1], 1)
            pl.semaphore_wait(credits.at[2], 1)

        attend(0, 0, group)
        round_kv(0)
        scatter_kv[0].send()
        attend(1, 0, group)
        round_kv(1)
        scatter_kv[1].send()
        expert.send(1, 2, when=top)
        expert.send(1, 1, when=odd)
        row_grads(grads_o, d_attn_ref, heads_ref[...], 0, width)
        pl.semaphore_wait(credits.at[0], 1)
        scatter_o.share()
        y_own = pltpu.make_async_copy(y_hbm.at[0], heads_ref, load_sems.at[2])
        y_own.start()
        for copy in y_loads:
            copy.wait()
        scatter_y.relay(lambda r, half: y_relay.at[half])
        scatter_o.merge(enter)

        for copy in loads[5:]:
            copy.wait()
        row_grads(grads_q, inputs_ref, d_all_ref[:, pl.ds(0, query_width)], 0, query_width)
        scatter_q.share()
        scatter_o.relay()
        expert.last(0, (sum_gu_hbm, sum_dn_hbm))
        expert.relay_begin(1)
        scatter_q.merge()
        expert.relay_add()
        for h in range(KEY_VALUE_HEADS):
            grad = scatter_kv[h].total()
            d_key = grad[:, :size]
            d_key = d_key * cos_ref[...] - swap_halves(d_key) * sin_ref[...]
            d_all_ref[:, pl.ds(query_width + h * size, size)] = d_key.astype(BF16)
            d_all_ref[:, pl.ds(query_width + key_width + h * size, size)] = grad[:, size:].astype(
                BF16
            )
        expert.relay_send(1)
        y_own.wait()
        hidden_ref[...] += heads_ref[...].astype(F32)
        scatter_y.total(hidden_ref)
        heads_ref[...] = hidden_ref[...].astype(BF16)
        layer_out = pltpu.make_async_copy(heads_ref, layer_hbm, out_sems.at[0])
        layer_out.start()

        total = dg_part[0]
        for r in (1, 2, 3):
            wire_1.arrived(dg_land.at[r - 1], dg_slot + r - 1, ids[r])
            total = total + dg_land[r - 1]
        gates = gate_all[0]
        d_logits = gates * (total - jnp.sum(gates * total, 0, keepdims=True))
        d_logits = jnp.concatenate(
            [d_logits, jnp.zeros((SMALL - d_logits.shape[0], tokens), F32)], 0
        )
        d_all_ref[:, pl.ds(qkv_width, SMALL)] = jnp.transpose(d_logits).astype(BF16)

        load_q.wait()

        @pl.loop(0, planes)
        def _(block):
            columns = pl.ds(pl.multiple_of(block * part, part), part)
            rows_q = weight[block].reshape(part, query_width)
            rows_k = wk_all[block].reshape(part, rest)
            d_inputs_ref[:, columns] = dot_nt(
                d_all_ref[:, pl.ds(0, query_width)], rows_q
            ) + dot_nt(d_all_ref[:, pl.ds(query_width, rest)], rows_k)

        rows = x_ref[...].astype(F32)
        scale1 = lax.rsqrt(jnp.mean(rows * rows, -1, keepdims=True) + EPSILON)
        d_inputs = d_inputs_ref[...]
        rows_ref[experts : experts + 1, :] = jnp.sum(d_inputs * rows * scale1, 0, keepdims=True)

        def extra(columns):
            small = jnp.transpose(rows_ref[:, columns])
            return jnp.concatenate([jnp.zeros((part, rest - SMALL), F32), small], 1)

        row_grads(
            grads_q, inputs_ref, d_all_ref[:, pl.ds(query_width, rest)], query_width, rest, extra
        )
        scatter_k.share()
        scatter_o.total()
        scatter_o.line.send()
        scatter_q.relay()
        scatter_k.merge()
        scaled = d_inputs_ref[...] * gains_ref[0:1]
        rows = x_ref[...].astype(F32)
        scale1 = lax.rsqrt(jnp.mean(rows * rows, -1, keepdims=True) + EPSILON)
        mean = jnp.mean(scaled * rows, -1, keepdims=True)
        d_x = d_hidden_ref[...] + scale1 * scaled - rows * (scale1 * scale1 * scale1 * mean)
        inputs_ref[...] = d_x.astype(BF16)
        d_x_out = pltpu.make_async_copy(inputs_ref, d_x_hbm, out_sems.at[1])
        d_x_out.start()
        scatter_q.total()
        scatter_q.line.send()
        scatter_k.relay()
        scatter_k.total()
        scatter_k.line.send()
        sum_o_ref[...] = scatter_o.line.total()
        expert.last(1, (sum_gu_hbm, sum_dn_hbm))
        sum_q_ref[:, pl.ds(0, query_width)] = scatter_q.line.total()
        sum_q_ref[:, pl.ds(query_width, rest)] = scatter_k.line.total()
        layer_out.wait()
        d_x_out.wait()
        wire_2.finish()
        expert.finish()

    held = EXP_DEV
    weight_shape = wq_hbm.shape
    pl.run_scoped(
        front_phase,
        pltpu.VMEM(weight_shape, BF16),
        pltpu.VMEM(weight_shape, BF16),
        pltpu.VMEM((tokens, width), BF16),
        pltpu.VMEM((tokens, width), BF16),
        pltpu.VMEM((tokens, query_width), BF16),
        pltpu.VMEM((tokens, query_width), BF16),
        pltpu.VMEM((tokens, width), F32),
        pltpu.VMEM((tokens, rest), F32),
        pltpu.VMEM((tokens, query_width), F32),
    )
    shard, step = width // nc // 2, 48
    pl.run_scoped(
        token_phase,
        pltpu.VMEM((held, width, 2 * ff), BF16),
        pltpu.VMEM((held, ff, width), BF16),
        pltpu.VMEM((blocks, tokens, width), BF16),
        pltpu.VMEM((blocks, tokens, held * ff), BF16),
        pltpu.VMEM((blocks, tokens, held * 2 * ff), BF16),
        pltpu.VMEM((2, 2, shard, grad_width // held), BF16),
        pltpu.VMEM((2, shard // step, step, grad_width // held), BF16),
        pltpu.VMEM((width, blocks * tokens), BF16),
        pltpu.VMEM((width, blocks * tokens), BF16),
    )
    rows_half = width // blocks // 2
    pl.run_scoped(
        token_rows_phase,
        pltpu.VMEM(weight_shape, BF16),
        pltpu.VMEM((2, blocks, rows_half, width), BF16),
        pltpu.VMEM((2, blocks, rows_half, qkv_width + SMALL), BF16),
        pltpu.VMEM((tokens, width), BF16),
        pltpu.VMEM((tokens, width), BF16),
        pltpu.VMEM((tokens, query_width), BF16),
        pltpu.VMEM((tokens, query_width), BF16),
        pltpu.VMEM((tokens, width), F32),
        pltpu.VMEM((tokens, width), F32),
        pltpu.VMEM((tokens, width), BF16),
        pltpu.VMEM((tokens, query_width), BF16),
        pltpu.VMEM((tokens, qkv_width + SMALL), BF16),
        pltpu.VMEM((SMALL, width), F32),
        pltpu.VMEM((KEY_VALUE_HEADS, nc * tokens, 2 * size), F32),
        pltpu.VMEM((KEY_VALUE_HEADS, nc, tokens, 2 * size), BF16),
        pltpu.VMEM((2, tokens, width // 2), BF16),
        pltpu.VMEM((4, shard // step, step, grad_width // held), BF16),
        pltpu.VMEM((2, step, grad_width // held), F32),
    )


def layer(operands, sizes):
    ne, nc, nd = sizes
    qkv_shard, x = operands[3], operands[6]
    w_dn = operands[9]
    tokens, width = x.shape
    held, ff = w_dn.shape[0], w_dn.shape[1]
    query_width = QUERY_HEADS * HEAD_DIMENSION
    rows, qkv_width = qkv_shard.shape
    rest = qkv_width - query_width + SMALL
    rest_half = rest // 256 * 128
    shard, grads = width // (nc * nd), held * 3 * ff
    kv_size = 2 * HEAD_DIMENSION
    weight = (ne, nc, nd, rows, query_width)
    shapes = [
        ((tokens, width), BF16),
        ((tokens, width), BF16),
        ((rows, qkv_width + SMALL), F32),
        ((rows, width), F32),
        ((held, shard, 2 * ff), F32),
        ((held, shard, ff), F32),
        ((nc, shard, grads), BF16),
        ((nc + 1, shard, grads), BF16),
        ((ne, tokens, width), BF16),
        (weight, BF16),
        (weight, BF16),
        ((ne, tokens, width), BF16),
        ((tokens, width), BF16),
        ((tokens, query_width), BF16),
        ((tokens, query_width), BF16),
        ((tokens, width), F32),
    ]
    vmem = pl.BlockSpec(memory_space=pltpu.VMEM)
    anywhere = pl.BlockSpec(memory_space=pl.ANY)
    units = nc * held
    sems = [120, 110, 6, 6, 6, 6, 10, 10, 64, 64, 2 * units, (nc + 1) * held, units, units, 2, 12, 6]
    return pl.pallas_call(
        functools.partial(layer_kernel, nc, EXP_DEV * ne),
        out_shape=[jax.ShapeDtypeStruct(*s) for s in shapes],
        in_specs=[vmem] * 6 + [anywhere] * (len(operands) - 6),
        out_specs=[anywhere] * 2 + [vmem] * 2 + [anywhere] * (len(shapes) - 4),
        scratch_shapes=[
            pltpu.VMEM((ne, nc, nd, rows, rest), BF16),
            pltpu.VMEM((KEY_VALUE_HEADS, nc, tokens, kv_size), BF16),
            pltpu.VMEM((ne, GATE_ROWS, tokens), F32),
            pltpu.VMEM((ne, tokens, SMALL), F32),
            pltpu.VMEM((8, width), F32),
            pltpu.VMEM((ne, tokens, width), BF16),
            pltpu.VMEM((6, tokens, width // 2), BF16),
            pltpu.VMEM((6, tokens, width // 2), BF16),
            pltpu.VMEM((nc, shard, grads // held), BF16),
            pltpu.VMEM((6, nc * rows, query_width // 2), BF16),
            pltpu.VMEM((6, nc * rows, rest - rest_half), BF16),
            pltpu.VMEM((nc, rows, width), BF16),
            pltpu.VMEM((nc, rows, query_width), BF16),
            pltpu.VMEM((nc, rows, rest), BF16),
            pltpu.VMEM((KEY_VALUE_HEADS, nc, tokens, kv_size), BF16),
            pltpu.VMEM((tokens, width), F32),
            pltpu.VMEM((ne, tokens, SMALL), F32),
            pltpu.VMEM((ne, GATE_ROWS, tokens), F32),
            pltpu.VMEM((ne - 1, GATE_ROWS, tokens), F32),
        ]
        + [pltpu.SemaphoreType.DMA((count,)) for count in sems]
        + [
            pltpu.SemaphoreType.DMA((20,)),
            pltpu.SemaphoreType.DMA((2,)),
            pltpu.SemaphoreType.REGULAR((4,)),
        ],
        compiler_params=pltpu.CompilerParams(
            collective_id=0, has_side_effects=True, vmem_limit_bytes=63 * MIB
        ),
    )(*operands)


def finish_kernel(experts, *refs):
    sources, dests = refs[:6], refs[6:12]
    router_ref, first_ref, second_ref = refs[12:]
    sum_q = sources[0]
    qkv_width = dests[0].shape[-1]
    dests[0][...] = sum_q[:, pl.ds(0, qkv_width)]
    for source, dest in zip(sources[1:], dests[1:]):
        dest[...] = source[...]
    small = sum_q[:, pl.ds(qkv_width, SMALL)]
    rows = small.shape[0]
    filled = jnp.concatenate([small, jnp.zeros((SMALL - rows, SMALL), F32)], 0)
    turned = jnp.transpose(filled)[:, :rows]
    router_ref[...] = turned[:experts]
    first_ref[...] = turned[experts : experts + 1]
    second_ref[...] = turned[experts + 1 : experts + 2]


def finish(sum_q, others, experts):
    rows, q_width = sum_q.shape
    vmem = pl.BlockSpec(memory_space=pltpu.VMEM)
    shapes = [jax.ShapeDtypeStruct((rows, q_width - SMALL), F32)]
    shapes += [jax.ShapeDtypeStruct(o.shape, o.dtype) for o in others]
    shapes += [jax.ShapeDtypeStruct((count, rows), F32) for count in (experts, 1, 1)]
    return pl.pallas_call(
        functools.partial(finish_kernel, experts),
        out_shape=shapes,
        in_specs=[vmem] * 6,
        out_specs=[vmem] * 9,
        compiler_params=pltpu.CompilerParams(vmem_limit_bytes=60 * MIB),
    )(sum_q, *others)


def local_plain(
    layer_input,
    gain_attn,
    query_key_value_weight,
    w_out,
    w_router,
    gain_ffn,
    w_gate_up,
    w_down,
    routes,
    d_out,
):
    tokens = layer_input.shape[1]
    model_width = layer_input.shape[2]
    ne, nc, nd = (lax.axis_size(a) for a in ("expert", "context", "dp"))
    expert_total = EXP_DEV * ne
    ff = w_down.shape[1]
    me = lax.axis_index("expert")
    first_row = lax.axis_index("context") * tokens
    query_width = QUERY_HEADS * HEAD_DIMENSION
    key_width = KEY_VALUE_HEADS * HEAD_DIMENSION
    qkv_width = query_width + 2 * key_width

    small = jnp.concatenate([w_router, gain_attn[:, None], gain_ffn[:, None]], -1)
    small = jnp.pad(small, ((0, 0), (0, 128 - small.shape[1])))
    gathered = gather_rows(jnp.concatenate([query_key_value_weight, small], -1))
    out_turned = gather_rows(w_out.T)
    qkv_weight = gathered[:, :qkv_width]
    router_weight = gathered[:, qkv_width : qkv_width + expert_total]
    gains = gathered[:, qkv_width + expert_total : qkv_width + expert_total + 2].T.astype(F32)
    gain_first, gain_second = gains[0], gains[1]
    cotangent_all = plane_gather(d_out[0])

    token_rows = layer_input[0].astype(F32)
    scale1 = lax.rsqrt(jnp.mean(token_rows * token_rows, -1, keepdims=True) + EPSILON)
    inputs1 = (token_rows * scale1 * gain_first).astype(BF16)
    query_key_value = dot_nn(inputs1, qkv_weight)
    cosine_values, sine_values = rope_tables(first_row + jnp.arange(tokens), HEAD_DIMENSION)
    rotated = rotate_half(
        query_key_value[:, : query_width + key_width].reshape(tokens, -1, HEAD_DIMENSION),
        cosine_values,
        sine_values,
    ).reshape(tokens, -1)
    query = rotated[:, :query_width].astype(BF16)
    key_value_local = jnp.concatenate(
        [rotated[:, query_width:], query_key_value[:, query_width + key_width :]], -1
    ).astype(BF16)
    key_value = line_gather(key_value_local, "context", both=False).reshape(nc * tokens, -1)
    first = first_row.astype(jnp.int32).reshape(1)
    heads = attend_forward(first, query, key_value)

    logits = dot_nn(inputs1, router_weight)
    chosen_ids = routes[0]
    picks = (chosen_ids[:, :, None] == jnp.arange(expert_total)[None, None, :]).astype(F32)
    chosen = jnp.sum(picks * logits[:, None, :], -1)
    gates = jax.nn.softmax(chosen, axis=-1)
    gate_dense = jnp.sum(picks * gates[:, :, None], 1).T
    gate_blocks = cube_gather(gate_dense, "expert", axis_masks("expert"))
    gate_local = jnp.concatenate(
        [lax.dynamic_slice_in_dim(b, me * EXP_DEV, EXP_DEV, 0) for b in gate_blocks], 1
    )

    attn = dot_nt(heads, out_turned)
    hidden = token_rows + attn
    scale2 = lax.rsqrt(jnp.mean(hidden * hidden, -1, keepdims=True) + EPSILON)
    expert_in = (hidden * scale2 * gain_second).astype(BF16)

    rows_all = plane_gather(expert_in)
    gate_up = jnp.einsum("td,edf->etf", rows_all, w_gate_up, preferred_element_type=F32)
    gate_part, up_part = gate_up[..., :ff], gate_up[..., ff:]
    sigma = jax.nn.sigmoid(gate_part)
    silu = gate_part * sigma
    act = silu * up_part
    gate_column = gate_local[:, :, None]
    act_gated = (act * gate_column).astype(BF16)
    partial_out = jnp.einsum("etf,efd->td", act_gated, w_down, preferred_element_type=F32)
    mixture = plane_scatter(partial_out.astype(BF16), tokens)
    layer_result = (hidden + mixture).astype(BF16)

    d_act_raw = jnp.einsum("td,efd->etf", cotangent_all, w_down, preferred_element_type=F32)
    d_gates_local = jnp.sum(d_act_raw * act, -1)
    d_act = d_act_raw * gate_column
    d_gate_part = d_act * up_part * sigma * (1.0 + gate_part * (1.0 - sigma))
    d_up_part = d_act * silu
    d_gate_up = jnp.concatenate([d_gate_part, d_up_part], -1).astype(BF16)
    d_rows = jnp.einsum("etf,edf->td", d_gate_up, w_gate_up, preferred_element_type=F32)
    grad_down = jnp.einsum("td,etf->edf", cotangent_all, act_gated, preferred_element_type=F32)
    grad_gate_up = jnp.einsum("td,etf->edf", rows_all, d_gate_up, preferred_element_type=F32)

    d_expert_in = plane_scatter(d_rows.astype(BF16), tokens)
    d_gate_blocks = d_gates_local.reshape(EXP_DEV, ne, tokens)
    d_gates_dense = jnp.zeros((expert_total, tokens), F32)
    for r in range(ne):
        arrived = d_gate_blocks[:, r]
        if r:
            arrived = exchange(arrived, "expert", r)
        d_gates_dense = lax.dynamic_update_slice(d_gates_dense, arrived, ((me ^ r) * EXP_DEV, 0))
    d_gates = jnp.sum(picks * d_gates_dense.T[:, None, :], -1)
    d_chosen = gates * (d_gates - jnp.sum(gates * d_gates, -1, keepdims=True))
    d_logits = jnp.sum(picks * d_chosen[:, :, None], 1).astype(BF16)
    grad_router = dot_tn(inputs1, d_logits)

    core = lax.axis_index("dp")
    part = model_width // (nc * nd)

    def scatter_experts(grad):
        blocks = grad.reshape(EXP_DEV, nc, nd, part, -1)
        mine = cube_scatter(
            [lax.dynamic_index_in_dim(blocks, core ^ r, 2, keepdims=False) for r in range(nd)],
            "dp",
            axis_masks("dp"),
        )
        return line_scatter(
            lambda j: lax.dynamic_index_in_dim(mine, j, 1, keepdims=False), "context"
        )

    sum_gate_up = scatter_experts(grad_gate_up)
    sum_down = jnp.swapaxes(scatter_experts(grad_down), 1, 2)

    cotangent = d_out[0].astype(F32)
    scaled2 = d_expert_in * gain_second
    d_hidden = (
        cotangent
        + scale2 * scaled2
        - hidden * (scale2 * scale2 * scale2) * jnp.mean(scaled2 * hidden, -1, keepdims=True)
    )
    grad_gain_second = jnp.sum(d_expert_in * hidden * scale2, 0)
    d_attn = d_hidden.astype(BF16)
    grad_out_turned = dot_tn(d_attn, heads)
    sum_out = scatter_rows(grad_out_turned).T
    d_heads = dot_nn(d_attn, out_turned).astype(BF16)
    d_query, d_key_all, d_value_all = attend_backward(first, query, key_value, d_heads)
    d_key_value_all = jnp.concatenate([d_key_all, d_value_all], -1).reshape(nc, tokens, -1)
    d_key_value = line_scatter(
        lambda j: lax.dynamic_index_in_dim(d_key_value_all, j, 0, keepdims=False),
        "context",
        up=False,
    )
    d_rotated = rotate_back(
        jnp.concatenate([d_query, d_key_value[:, :key_width]], -1).reshape(
            tokens, -1, HEAD_DIMENSION
        ),
        cosine_values,
        sine_values,
    ).reshape(tokens, -1)
    d_qkv = jnp.concatenate([d_rotated, d_key_value[:, key_width:]], -1).astype(BF16)
    d_inputs = dot_nt(d_qkv, qkv_weight) + dot_nt(d_logits, router_weight)
    grad_gain_first = jnp.sum(d_inputs * token_rows * scale1, 0)
    grad_qkv = dot_tn(inputs1, d_qkv)
    small_grads = jnp.concatenate(
        [grad_router, grad_gain_first[:, None], grad_gain_second[:, None]], -1
    )
    small_grads = jnp.pad(small_grads, ((0, 0), (0, 128 - small_grads.shape[1])))
    sum_rows = scatter_rows(jnp.concatenate([grad_qkv, small_grads], -1))
    sum_qkv = sum_rows[:, :qkv_width]
    sum_router = sum_rows[:, qkv_width : qkv_width + expert_total]
    sum_gain_first = sum_rows[:, qkv_width + expert_total]
    sum_gain_second = sum_rows[:, qkv_width + expert_total + 1]
    scaled1 = d_inputs * gain_first
    d_input_rows = (
        d_hidden
        + scale1 * scaled1
        - token_rows
        * (scale1 * scale1 * scale1)
        * jnp.mean(scaled1 * token_rows, -1, keepdims=True)
    ).astype(BF16)
    return (
        layer_result[None],
        d_input_rows[None],
        sum_gain_first,
        sum_qkv,
        sum_out,
        sum_router,
        sum_gain_second,
        sum_gate_up,
        sum_down,
    )


def local_fused(
    layer_input,
    gain_attn,
    query_key_value_weight,
    w_out,
    w_router,
    gain_ffn,
    w_gate_up,
    w_down,
    routes,
    d_out,
):
    tokens = layer_input.shape[1]
    ne, nc, nd = sizes = tuple(lax.axis_size(a) for a in ("expert", "context", "dp"))
    expert_total = EXP_DEV * ne
    first_row = lax.axis_index("context") * tokens
    query_width = QUERY_HEADS * HEAD_DIMENSION
    key_width = KEY_VALUE_HEADS * HEAD_DIMENSION
    qkv_width = query_width + 2 * key_width

    small = jnp.concatenate([w_router, gain_attn[:, None], gain_ffn[:, None]], -1)
    small = jnp.pad(small, ((0, 0), (0, SMALL - small.shape[1])))
    cosine_values, sine_values = rope_tables(first_row + jnp.arange(tokens), HEAD_DIMENSION)
    sine_values = sine_values * jnp.where(
        jnp.arange(HEAD_DIMENSION) < HEAD_DIMENSION // 2, -1.0, 1.0
    )
    layer_result, d_x, sum_rows, sum_out, sum_gate_up, sum_down = layer(
        (
            cosine_values,
            sine_values,
            routes[0].T,
            query_key_value_weight,
            small,
            w_out.T,
            layer_input[0],
            d_out[0],
            w_gate_up,
            w_down,
        ),
        sizes,
    )[:6]
    sum_qkv, layer_result, d_x, sum_gate_up, sum_down, sum_out, sum_router, *sum_gains = finish(
        sum_rows, (layer_result, d_x, sum_gate_up, sum_down, sum_out), expert_total
    )
    return (
        layer_result[None],
        d_x[None],
        sum_gains[0][0],
        sum_qkv,
        sum_out.T,
        sum_router.T,
        sum_gains[1][0],
        sum_gate_up,
        jnp.swapaxes(sum_down, 1, 2),
    )


def solution(mesh):
    in_specs = (
        P(("expert", "dp"), "context", None),
        P(("expert", "context", "dp")),
        P(("expert", "context", "dp"), None),
        P(None, ("expert", "context", "dp")),
        P(("expert", "context", "dp"), None),
        P(("expert", "context", "dp")),
        P("expert", None, None),
        P("expert", None, None),
        P(("expert", "dp"), "context", None),
        P(("expert", "dp"), "context", None),
    )
    out_specs = (
        P(("expert", "dp"), "context", None),
        P(("expert", "dp"), "context", None),
        P(("expert", "context", "dp")),
        P(("expert", "context", "dp"), None),
        P(None, ("expert", "context", "dp")),
        P(("expert", "context", "dp"), None),
        P(("expert", "context", "dp")),
        P("expert", ("context", "dp"), None),
        P("expert", None, ("context", "dp")),
    )
    sizes = tuple(mesh.shape[a] for a in ("expert", "context", "dp"))
    local = local_fused if sizes == (4, 4, 2) else local_plain
    return jax.shard_map(local, mesh=mesh, in_specs=in_specs, out_specs=out_specs, check_vma=False)
```

```python
import functools
import math

import jax
import jax.numpy as jnp
from jax import lax
from jax.experimental import pallas as pl
from jax.experimental.pallas import tpu as pltpu
from jax.sharding import PartitionSpec as P

QUERY_HEADS = 12
KEY_VALUE_HEADS = 2
HEAD_DIMENSION = 128
TOP = 4
EXP_DEV = 2

EPSILON = 1e-06
ROPE_BASE = 10000.0
MASKED = -1e30

F32 = jnp.float32
BF16 = jnp.bfloat16


def rope_tables(positions, width):
    halfway = width // 2
    fraction = jnp.arange(halfway, dtype=jnp.float32) * (2.0 / width)
    frequency = jnp.exp(-math.log(ROPE_BASE) * fraction)
    angles = positions.astype(jnp.float32)[:, None] * frequency[None, :]
    cosine_values = jnp.cos(angles)
    sine_values = jnp.sin(angles)
    return (
        jnp.concatenate([cosine_values, cosine_values], -1),
        jnp.concatenate([sine_values, sine_values], -1),
    )


def rotate_half(values, cosine_values, sine_values):
    halfway = values.shape[-1] // 2
    turned = jnp.concatenate([-values[..., halfway:], values[..., :halfway]], -1)
    return values * cosine_values[:, None, :] + turned * sine_values[:, None, :]


def rotate_back(grads, cosine_values, sine_values):
    halfway = grads.shape[-1] // 2
    scaled = grads * sine_values[:, None, :]
    turned = jnp.concatenate([scaled[..., halfway:], -scaled[..., :halfway]], -1)
    return grads * cosine_values[:, None, :] + turned


def dot_nt(a, b):
    return lax.dot_general(a, b, (((1,), (1,)), ((), ())), preferred_element_type=F32)


def dot_tn(a, b):
    return lax.dot_general(a, b, (((0,), (0,)), ((), ())), preferred_element_type=F32)


def dot_nn(a, b):
    return jnp.dot(a, b, preferred_element_type=F32)


def masked_probs(first_row, query, key):
    scores = dot_nt(query, key) * (HEAD_DIMENSION**-0.5)
    rows = first_row + lax.broadcasted_iota(jnp.int32, scores.shape, 0)
    columns = lax.broadcasted_iota(jnp.int32, scores.shape, 1)
    scores = jnp.where(columns <= rows, scores, MASKED)
    expd = jnp.exp(scores - jnp.max(scores, axis=-1, keepdims=True))
    return expd / jnp.sum(expd, axis=-1, keepdims=True)


def attend_forward_kernel(first_ref, query_ref, key_ref, value_ref, heads_ref):
    probs = masked_probs(first_ref[0], query_ref[...], key_ref[...])
    heads_ref[...] = dot_nn(probs.astype(BF16), value_ref[...]).astype(BF16)


def attend_forward(first_row, query, key_value):
    tokens, width = query.shape
    length = key_value.shape[0]
    group = QUERY_HEADS // KEY_VALUE_HEADS
    size = HEAD_DIMENSION
    return pl.pallas_call(
        attend_forward_kernel,
        grid_spec=pltpu.PrefetchScalarGridSpec(
            num_scalar_prefetch=1,
            grid=(QUERY_HEADS,),
            in_specs=[
                pl.BlockSpec((tokens, size), lambda h, s: (0, h)),
                pl.BlockSpec((length, size), lambda h, s: (0, h // group)),
                pl.BlockSpec((length, size), lambda h, s: (0, KEY_VALUE_HEADS + h // group)),
            ],
            out_specs=pl.BlockSpec((tokens, size), lambda h, s: (0, h)),
        ),
        out_shape=jax.ShapeDtypeStruct((tokens, width), BF16),
        compiler_params=pltpu.CompilerParams(vmem_limit_bytes=32 * 1024 * 1024),
        cost_estimate=pl.CostEstimate(
            flops=4 * tokens * length * width, bytes_accessed=4 * tokens * width, transcendentals=0
        ),
    )(first_row, query, key_value, key_value)


def attend_backward_kernel(
    first_ref, query_ref, key_ref, value_ref, grad_ref, d_query_ref, d_key_ref, d_value_ref
):
    query, key, value, grad = query_ref[...], key_ref[...], value_ref[...], grad_ref[...]
    probs = masked_probs(first_ref[0], query, key)
    d_probs = dot_nt(grad, value)
    inner = jnp.sum(probs * d_probs, axis=-1, keepdims=True)
    d_raw = (probs * (d_probs - inner) * (HEAD_DIMENSION**-0.5)).astype(BF16)
    d_query_ref[...] = dot_nn(d_raw, key)
    d_key = dot_tn(d_raw, query)
    d_value = dot_tn(probs.astype(BF16), grad)

    @pl.when(pl.program_id(1) == 0)
    def _():
        d_key_ref[...] = d_key
        d_value_ref[...] = d_value

    @pl.when(pl.program_id(1) > 0)
    def _():
        d_key_ref[...] += d_key
        d_value_ref[...] += d_value


def attend_backward(first_row, query, key_value, grad):
    tokens, width = query.shape
    length = key_value.shape[0]
    group = QUERY_HEADS // KEY_VALUE_HEADS
    size = HEAD_DIMENSION
    row_spec = pl.BlockSpec((tokens, size), lambda j, g, s: (0, j * group + g))
    return pl.pallas_call(
        attend_backward_kernel,
        grid_spec=pltpu.PrefetchScalarGridSpec(
            num_scalar_prefetch=1,
            grid=(KEY_VALUE_HEADS, group),
            in_specs=[
                row_spec,
                pl.BlockSpec((length, size), lambda j, g, s: (0, j)),
                pl.BlockSpec((length, size), lambda j, g, s: (0, KEY_VALUE_HEADS + j)),
                row_spec,
            ],
            out_specs=[
                row_spec,
                pl.BlockSpec((length, size), lambda j, g, s: (0, j)),
                pl.BlockSpec((length, size), lambda j, g, s: (0, j)),
            ],
        ),
        out_shape=[
            jax.ShapeDtypeStruct((tokens, width), F32),
            jax.ShapeDtypeStruct((length, KEY_VALUE_HEADS * size), F32),
            jax.ShapeDtypeStruct((length, KEY_VALUE_HEADS * size), F32),
        ],
        compiler_params=pltpu.CompilerParams(vmem_limit_bytes=32 * 1024 * 1024),
        cost_estimate=pl.CostEstimate(
            flops=10 * tokens * length * width, bytes_accessed=8 * tokens * width, transcendentals=0
        ),
    )(first_row, query, key_value, key_value, grad)


def exchange(values, axis, mask):
    size = lax.axis_size(axis)
    return lax.ppermute(values, axis, [(i, i ^ mask) for i in range(size)])


def axis_masks(axis):
    size = lax.axis_size(axis)
    masks, bit = [], 1
    while bit < size:
        masks.append(bit)
        bit *= 2
    return masks


def cube_gather(values, axis, masks):
    held = {0: values}
    for mask in masks:
        for r, block in list(held.items()):
            held[r ^ mask] = exchange(block, axis, mask)
    return [held[r] for r in range(lax.axis_size(axis))]


def cube_scatter(blocks, axis, masks):
    held = dict(enumerate(blocks))
    for mask in masks:
        kept = {}
        for r in list(held):
            if not r & mask:
                arrived = exchange(held[r ^ mask].astype(BF16), axis, mask)
                kept[r] = held[r].astype(F32) + arrived.astype(F32)
        held = kept
    return held[0]


def line_steps(values, axis, up):
    size = lax.axis_size(axis)
    pairs = [(i, i + 1) if up else (i + 1, i) for i in range(size - 1)]
    return lax.ppermute(values, axis, pairs)


def line_gather(values, axis, both=True):
    size = lax.axis_size(axis)
    me = lax.axis_index(axis)
    result = jnp.zeros((size + 1,) + values.shape, values.dtype)
    result = lax.dynamic_update_index_in_dim(result, values, me, 0)
    up = down = values
    for step in range(1, size):
        up = line_steps(up, axis, True)
        result = lax.dynamic_update_index_in_dim(
            result, up, jnp.where(me - step >= 0, me - step, size), 0
        )
        if both:
            down = line_steps(down, axis, False)
            result = lax.dynamic_update_index_in_dim(result, down, jnp.minimum(me + step, size), 0)
    return result[:size]


def line_scatter(take, axis, up=True, down=True):
    size = lax.axis_size(axis)
    me = lax.axis_index(axis)
    total = take(me).astype(F32)
    for active, sign in ((up, 1), (down, -1)):
        if not active:
            continue
        arrived = None
        for step in range(1, size):
            block = take((me + sign * (size - step)) % size).astype(F32)
            if arrived is not None:
                block = block + arrived.astype(F32)
            arrived = line_steps(block.astype(BF16), axis, sign > 0)
        total = total + arrived.astype(F32)
    return total


def gather_rows(shard):
    ne, nc, nd = (lax.axis_size(a) for a in ("expert", "context", "dp"))
    rows, width = shard.shape
    lines = line_gather(shard, "context")
    masks = axis_masks("expert")
    half = width // 256 * 128
    parts = [lines[..., :half], lines[..., half:]]
    me = lax.axis_index("expert")
    result = jnp.zeros((ne, nc, rows, width), shard.dtype)
    for start, part, order in ((0, parts[0], masks), (half, parts[1], masks[::-1])):
        for r, block in enumerate(cube_gather(part, "expert", order)):
            result = lax.dynamic_update_slice(result, block[None], (me ^ r, 0, 0, start))
    core = lax.axis_index("dp")
    whole = jnp.zeros((ne, nc, nd, rows, width), shard.dtype)
    for r, block in enumerate(cube_gather(result, "dp", axis_masks("dp"))):
        whole = lax.dynamic_update_slice(whole, block[:, :, None], (0, 0, core ^ r, 0, 0))
    return whole.reshape(-1, width)


def scatter_rows(grad):
    ne, nc, nd = (lax.axis_size(a) for a in ("expert", "context", "dp"))
    width = grad.shape[-1]
    rows = grad.shape[0] // (ne * nc * nd)
    blocks = grad.reshape(ne, nc, nd, rows, width)
    core, me = lax.axis_index("dp"), lax.axis_index("expert")
    mine = cube_scatter(
        [
            lax.dynamic_index_in_dim(blocks, core ^ r, 2, keepdims=False)
            for r in range(nd)
        ],
        "dp",
        axis_masks("dp"),
    )
    masks = axis_masks("expert")
    half = width // 256 * 128
    sums = []
    for part, order in ((mine[..., :half], masks), (mine[..., half:], masks[::-1])):
        sums.append(
            cube_scatter(
                [lax.dynamic_index_in_dim(part, me ^ r, 0, keepdims=False) for r in range(ne)],
                "expert",
                order,
            )
        )
    lines = jnp.concatenate(sums, -1)
    return line_scatter(
        lambda j: lax.dynamic_index_in_dim(lines, j, 0, keepdims=False), "context"
    )


def plane_gather(rows):
    masks = axis_masks("expert")
    half = rows.shape[-1] // 2
    left = cube_gather(rows[:, :half], "expert", masks)
    right = cube_gather(rows[:, half:], "expert", masks[::-1])
    return jnp.concatenate([jnp.concatenate(p, -1) for p in zip(left, right)], 0)


def plane_scatter(partial, tokens):
    masks = axis_masks("expert")
    size = lax.axis_size("expert")
    half = partial.shape[-1] // 2
    blocks = partial.reshape(size, tokens, -1)
    left = cube_scatter([blocks[r, :, :half] for r in range(size)], "expert", masks)
    right = cube_scatter([blocks[r, :, half:] for r in range(size)], "expert", masks[::-1])
    return jnp.concatenate([left, right], -1)


MESH = pl.DeviceIdType.MESH
MIB = 1024 * 1024
SMALL = 128
GATE_ROWS = 16


def flip(index, mask):
    bit = 1
    while bit <= mask:
        if mask & bit:
            index = index + bit - 2 * bit * lax.rem(lax.div(index, bit), 2)
        bit *= 2
    return index


class Wire:
    def __init__(self, sends, recvs):
        self.sends, self.recvs = sends, recvs
        self.n_sends = self.n_recvs = 0
        self.open = []

    def slots(self, count):
        first = self.n_recvs
        self.n_recvs += count
        return first

    def start(self, src, dst, recv, device, when=None):
        number = self.n_sends
        self.n_sends += 1

        def copy():
            return pltpu.make_async_remote_copy(
                src_ref=src() if callable(src) else src,
                dst_ref=dst() if callable(dst) else dst,
                send_sem=self.sends.at[number],
                recv_sem=self.recvs.at[recv],
                device_id=device,
                device_id_type=MESH,
            )

        guard(when, lambda: copy().start())
        self.open.append((when, copy))

    def arrived(self, dst, recv, device):
        pltpu.make_async_remote_copy(
            src_ref=dst,
            dst_ref=dst,
            send_sem=self.sends.at[0],
            recv_sem=self.recvs.at[recv],
            device_id=device,
            device_id_type=MESH,
        ).wait_recv()

    def finish(self):
        for when, copy in self.open:
            guard(when, lambda copy=copy: copy().wait_send())
        self.open = []


def guard(when, action):
    if when is None:
        action()
    else:
        pl.when(when)(action)


def add_into(dest, source, steps=4):
    rows = dest.shape[0] // steps

    @pl.loop(0, steps)
    def _(n):
        here = pl.ds(pl.multiple_of(n * rows, rows), rows)
        dest[here] = (dest[here].astype(F32) + source[here].astype(F32)).astype(BF16)


def greet(targets):
    barrier = pltpu.get_barrier_semaphore()
    for device, when in targets:
        guard(
            when,
            lambda device=device: pl.semaphore_signal(
                barrier, inc=1, device_id=device, device_id_type=MESH
            ),
        )
    count = sum(1 if when is None else when.astype(jnp.int32) for _, when in targets)
    pl.semaphore_wait(barrier, count)


def plane_ids(e):
    return {m: {"expert": flip(e, m)} for m in (1, 2, 3)}


class RowsGather:
    def __init__(self, wire, ref, e, z, c, nc, half):
        self.wire, self.ref, self.e, self.z, self.c, self.nc = wire, ref, e, z, c, nc
        self.cols = (pl.ds(0, half), pl.ds(half, ref.shape[-1] - half))
        self.line = wire.slots(nc)
        self.plane = wire.slots(nc * 6)
        self.core = wire.slots(nc)
        self.ids = plane_ids(e)

    def go(self, *steps):
        for step in steps:
            action = {"l": self.pass_on, "s": self.spread, "f": self.forward, "h": self.share, "c": self.complete}
            action[step[0]](*map(int, step[1:]))

    def shard(self, k):
        if k < 2:
            return flip(self.z, k)
        inner = (self.z > 0) & (self.z < self.nc - 1)
        return jnp.where(inner, flip(self.z, 5 - k), flip(self.z, k))

    def at(self, r, zs, half):
        return self.ref.at[flip(self.e, r), zs, self.c, :, self.cols[half]]

    def slot(self, k, r, half):
        return self.plane + k * 6 + (r - 1) * 2 + half

    def pass_on(self, k):
        wire, z, nc = self.wire, self.z, self.nc
        zs = self.shard(k)
        whole = self.ref.at[self.e, zs, self.c]
        if k:
            wire.arrived(whole, self.line + zs, {"context": zs})
        wire.start(
            whole, whole, self.line + zs, {"context": z + 1}, when=(zs <= z) & (z < nc - 1)
        )
        wire.start(whole, whole, self.line + zs, {"context": z - 1}, when=(zs >= z) & (z > 0))

    def spread(self, k):
        zs = self.shard(k)
        for half, mask in ((0, 1), (1, 2), (1, 1), (0, 2)):
            part = self.at(0, zs, half)
            self.wire.start(part, part, self.slot(k, mask, half), self.ids[mask])

    def forward(self, k):
        zs = self.shard(k)
        for half, mask in ((0, 1), (1, 2)):
            part = self.at(mask, zs, half)
            self.wire.arrived(part, self.slot(k, mask, half), self.ids[mask])
            self.wire.start(part, part, self.slot(k, 3, half), self.ids[3 - mask])

    def share(self, k):
        zs = self.shard(k)
        for r, half in ((1, 1), (2, 0), (3, 0), (3, 1)):
            self.wire.arrived(self.at(r, zs, half), self.slot(k, r, half), self.ids[r])
        part = self.ref.at[:, zs, self.c]
        self.wire.start(part, part, self.core + k, {"dp": 1 - self.c})

    def complete(self):
        for k in range(self.nc):
            zs = self.shard(k)
            self.wire.arrived(self.ref.at[:, zs, 1 - self.c], self.core + k, {"dp": 1 - self.c})


class PlaneGather:
    def __init__(self, wire, ref, e, own=None):
        self.wire, self.ref, self.own = wire, ref, own
        self.half = ref.shape[-1] // 2
        self.ids = plane_ids(e)
        self.first = wire.slots(6)

    def at(self, r, half):
        columns = pl.ds(half * self.half, self.half)
        if r == 0 and self.own is not None:
            return self.own.at[:, columns]
        return self.ref.at[r, :, columns]

    def slot(self, r, half):
        return self.first + (r - 1) * 2 + half

    def send(self, r, half, to, mask):
        self.wire.start(
            lambda: self.at(r, half), lambda: self.at(to, half), self.slot(to, half), self.ids[mask]
        )

    def spread(self):
        for half, mask in ((0, 1), (1, 2), (1, 1), (0, 2)):
            self.send(0, half, mask, mask)

    def forward(self):
        for half, mask in ((0, 1), (1, 2)):
            self.wire.arrived(self.at(mask, half), self.slot(mask, half), self.ids[mask])
            self.send(mask, half, 3, 3 - mask)

    def near(self, r):
        half = 1 if r == 1 else 0
        self.wire.arrived(self.at(r, half), self.slot(r, half), self.ids[r])

    def far(self):
        for half in (0, 1):
            self.wire.arrived(self.at(3, half), self.slot(3, half), self.ids[3])

    def complete(self):
        self.near(1)
        self.near(2)
        self.far()


def causal(scores, first_row):
    place = lax.broadcasted_iota(jnp.int32, scores.shape, 0)
    row = first_row + lax.broadcasted_iota(jnp.int32, scores.shape, 1)
    return jnp.where(place <= row, scores, MASKED)


def swap_halves(values):
    return pltpu.roll(values, HEAD_DIMENSION // 2, 1)


class PlaneScatter:
    def __init__(self, wire, land, ids):
        self.wire, self.land, self.ids, self.part = wire, land, ids, None
        self.half = land.shape[-1]
        self.first = wire.slots(6)

    def send(self, source, mask, slot):
        self.wire.start(source, lambda: self.land.at[slot], self.first + slot, self.ids[mask])

    def near(self, r):
        self.send(self.part(r, r - 1), r, r - 1)

    def far(self):
        self.send(self.part(3, 0), 1, 2)
        self.send(self.part(3, 1), 2, 3)

    def relay(self, part=None):
        for half, r in ((0, 2), (1, 1)):
            slot = 2 + half
            self.wire.arrived(self.land.at[slot], self.first + slot, self.ids[3 - r])
            take = part or self.part
            mine = take(r, half)
            add_into(mine, self.land.at[slot])
            self.send(lambda r=r, half=half, take=take: take(r, half), r, 4 + half)

    def total(self, own):
        for slot, half, mask in ((0, 0, 1), (1, 1, 2), (4, 0, 2), (5, 1, 1)):
            self.wire.arrived(self.land.at[slot], self.first + slot, self.ids[mask])
            columns = pl.ds(half * self.half, self.half)
            rows = own.shape[0] // 4

            @pl.loop(0, 4)
            def _(n):
                here = pl.ds(pl.multiple_of(n * rows, rows), rows)
                own[here, columns] += self.land[slot, here].astype(F32)


class LineSum:
    def __init__(self, wire, block, land, z, nc, up=True):
        self.wire, self.block, self.land, self.z, self.nc, self.up = wire, block, land, z, nc, up
        self.first = wire.slots(nc)

    def clear(self):
        for slot in range(self.nc):

            def zero(slot=slot):
                self.land[slot] = jnp.zeros(self.land.shape[1:], BF16)

            pl.when(slot == self.z if self.up else slot <= self.z)(zero)

    def send(self):
        z = self.z
        for d in range(self.nc - 1, 0, -1):
            self.leave(z - d, z >= d)
            if self.up:
                self.leave(z + d, z + d < self.nc)

    def leave(self, j, wanted):
        self.wire.start(
            self.block(j), self.land.at[self.z], self.first + self.z, {"context": j}, when=wanted
        )

    def total(self):
        z = self.z
        for d in range(1, self.nc):
            for source, wanted in ((z + d, z + d < self.nc), (z - d, z >= d))[: 1 + self.up]:

                def wait(source=source):
                    self.wire.arrived(
                        self.land.at[source], self.first + source, {"context": source}
                    )

                pl.when(wanted)(wait)
        total = self.block(z)[...].astype(F32)
        for slot in range(self.nc):
            total = total + self.land[slot].astype(F32)
        return total


class RowsScatter:
    def __init__(self, wire, buf, core, plane, lines, e, z, c, nc, start, width, half):
        self.wire, self.buf, self.core, self.plane = wire, buf, core, plane
        self.e, self.c = e, c
        self.all = pl.ds(start, width)
        self.cols = (pl.ds(start, half), pl.ds(start + half, width - half))
        self.ids = plane_ids(e)
        self.core_slot = wire.slots(1)
        self.first = wire.slots(6)
        rows = buf.shape[2] // nc
        self.line = LineSum(
            wire,
            lambda j: buf.at[c, e, pl.ds(pl.multiple_of(j * rows, rows), rows), self.all],
            lines,
            z,
            nc,
        )

    def share(self):
        self.wire.start(
            self.buf.at[1 - self.c, :, :, self.all], self.core, self.core_slot, {"dp": 1 - self.c}
        )

    def at(self, r, half):
        return self.buf.at[self.c, flip(self.e, r), :, self.cols[half]]

    def send(self, r, half, mask, slot):
        self.wire.start(
            self.at(r, half), self.plane(slot, half), self.first + slot, self.ids[mask]
        )

    def merge(self, before=None):
        self.wire.arrived(self.core, self.core_slot, {"dp": 1 - self.c})
        for r in (3, 1, 2, 0):
            block = flip(self.e, r)
            part = self.buf.at[self.c, block, :, self.all]
            add_into(part, self.core.at[block])
            if r == 3:
                if before is not None:
                    before()
                self.send(3, 0, 1, 2)
                self.send(3, 1, 2, 3)
            elif r:
                self.send(r, r - 1, r, r - 1)

    def add(self, r, half, slot, mask):
        land = self.plane(slot, half)
        self.wire.arrived(land, self.first + slot, self.ids[mask])
        add_into(self.at(r, half), land)

    def relay(self):
        for half, r in ((0, 2), (1, 1)):
            self.add(r, half, 2 + half, 3 - r)
            self.send(r, half, r, 4 + half)

    def total(self):
        for slot, half, mask in ((0, 0, 1), (1, 1, 2), (4, 0, 2), (5, 1, 1)):
            self.add(0, half, slot, mask)


class ExpertLine:
    def __init__(self, wire, base, land, sems, z, nc):
        self.wire, self.base, self.land = wire, base, land
        self.ins, self.out, self.sems, self.z, self.nc = None, None, sems, z, nc
        self.end = (z == 0) | (z == nc - 1)
        self.inner = jnp.logical_not(self.end)
        self.width = base.shape[-1] // EXP_DEV
        self.first = wire.slots((nc + 2) * EXP_DEV)
        self.sent = []

    def part(self, ref, j, i):
        return ref.at[j, :, pl.ds(i * self.width, self.width)]

    def combine(self, sources, stores):
        out, step = self.out, self.ins.shape[2]
        count = sources[0].shape[0] // step

        def loads(p):
            rows = pl.ds(p * step, step)
            return [
                pltpu.make_async_copy(source.at[rows], self.ins.at[k, p], self.sems.at[4 * k + p])
                for k, source in enumerate(sources)
            ]

        def store(p):
            pairs = stores(pl.ds(p * step, step), out.at[p % 2])
            return [
                pltpu.make_async_copy(source, dest, self.sems.at[16 + 2 * n + p % 2])
                for n, (source, dest) in enumerate(pairs)
            ]

        for p in range(count):
            for copy in loads(p):
                copy.start()
        for p in range(count):
            for copy in loads(p):
                copy.wait()
            if p > 1:
                for copy in store(p - 2):
                    copy.wait()
            total = self.ins[0, p].astype(F32)
            for k in range(1, len(sources)):
                total = total + self.ins[k, p].astype(F32)
            out[p % 2] = total.astype(out.dtype)
            for copy in store(p):
                copy.start()
        for p in range(max(0, count - 2), count):
            for copy in store(p):
                copy.wait()

    def copy(self, i, r, number):
        target, slot = flip(self.z, r), self.z
        if r > 1:
            target = jnp.where(self.end, flip(self.z, 1), target)
            slot = jnp.where(self.end, self.nc + 3 - r, slot)
        return pltpu.make_async_remote_copy(
            src_ref=self.part(self.base, flip(self.z, r), i),
            dst_ref=self.part(self.land, slot, i),
            send_sem=self.wire.sends.at[number],
            recv_sem=self.wire.recvs.at[self.first + slot * EXP_DEV + i],
            device_id={"context": target},
            device_id_type=MESH,
        )

    def send(self, i, r, when=None):
        number = len(self.sent)
        guard(when, self.copy(i, r, number).start)
        self.sent.append((when, i, r, number))

    def finish(self):
        for when, i, r, number in self.sent:
            guard(when, self.copy(i, r, number).wait_send)

    def arrived(self, slot, i):
        land = self.part(self.land, slot, i)
        self.wire.arrived(land, self.first + slot * EXP_DEV + i, {"context": self.z})

    def relay_loads(self, i, r, p):
        step = self.ins.shape[2]
        rows = pl.ds(p * step, step)
        far = self.nc + r - 2
        sources = (self.part(self.base, flip(self.z, r), i), self.part(self.land, far, i))
        return [
            pltpu.make_async_copy(source.at[rows], self.ins.at[k, p], self.sems.at[4 * k + p])
            for k, source in enumerate(sources)
        ]

    def relay_store(self, i, r, p):
        step = self.ins.shape[2]
        mine = self.part(self.base, flip(self.z, r), i).at[pl.ds(p * step, step)]
        return pltpu.make_async_copy(self.ins.at[0, p], mine, self.sems.at[16 + p])

    def relay_steps(self):
        return range(self.base.shape[1] // self.ins.shape[2])

    def relay_begin(self, i, r):
        def begin():
            self.arrived(self.nc + r - 2, i)
            for p in self.relay_steps():
                for copy in self.relay_loads(i, r, p):
                    copy.start()

        pl.when(self.inner)(begin)

    def relay_add(self, i, r):
        def add():
            for p in self.relay_steps():
                for copy in self.relay_loads(i, r, p):
                    copy.wait()
                a, b = (self.ins[k, p].astype(F32) for k in range(2))
                self.ins[0, p] = (a + b).astype(BF16)
                self.relay_store(i, r, p).start()

        pl.when(self.inner)(add)

    def relay_send(self, i, r):
        def wait():
            for p in self.relay_steps():
                self.relay_store(i, r, p).wait()

        pl.when(self.inner)(wait)
        self.send(i, r, when=self.inner)

    def last(self, i, results):
        z = self.z
        other = jnp.where(self.inner, flip(z, 3), flip(z, 2))
        sources = [self.part(self.base, z, i)]
        for source in (flip(z, 1), other):
            self.arrived(source, i)
            sources.append(self.part(self.land, source, i))

        def stores(rows, wide):
            pairs, first = [], 0
            for result in results:
                columns = pl.ds(first, result.shape[-1])
                pairs.append((wide.at[:, columns], result.at[i, rows]))
                first += result.shape[-1]
            return pairs

        self.combine(sources, stores)


def layer_kernel(
    nc,
    experts,
    cos_ref,
    sin_ref,
    routes_ref,
    qkv_ref,
    small_ref,
    wo_shard_ref,
    x_hbm,
    d_out_hbm,
    w_gu_hbm,
    w_dn_hbm,
    layer_hbm,
    d_x_hbm,
    sum_q_ref,
    sum_o_ref,
    sum_gu_hbm,
    sum_dn_hbm,
    base_hbm,
    land_hbm,
    y_hbm,
    wq_hbm,
    wo_hbm,
    cot_hbm,
    inputs_hbm,
    query_hbm,
    heads_hbm,
    hidden_hbm,
    wk_all,
    kv_ref,
    gate_all,
    gates_ref,
    gains_ref,
    x_all,
    y_land,
    dx_land,
    core_land,
    plane_q,
    plane_k,
    lines_o,
    lines_q,
    lines_k,
    dkv_land,
    d_in_ref,
    dg_lanes,
    dg_part,
    dg_land,
    sends_f,
    recvs_f,
    sends_c,
    recvs_c,
    sends_x,
    recvs_x,
    sends_1,
    recvs_1,
    sends_2,
    recvs_2,
    sends_e,
    recvs_e,
    hand_sends,
    hand_recvs,
    stage_sems,
    load_sems,
    out_sems,
    sum_sems,
    y_sems,
    credits,
):
    e, z, c = (lax.axis_index(a) for a in ("expert", "context", "dp"))
    size = HEAD_DIMENSION
    blocks, tokens, width = cot_hbm.shape
    ff = w_dn_hbm.shape[1]
    query_width = QUERY_HEADS * size
    key_width = KEY_VALUE_HEADS * size
    qkv_width = query_width + 2 * key_width
    rest = wk_all.shape[-1]
    grad_width = base_hbm.shape[-1]
    ids = plane_ids(e)
    sibling = {"dp": 1 - c}
    bottom, even, odd, top = z == 0, lax.rem(z, 2) == 0, lax.rem(z, 2) == 1, z == nc - 1
    wire_1, wire_2, wire_e = Wire(sends_1, recvs_1), Wire(sends_2, recvs_2), Wire(sends_e, recvs_e)
    expert = ExpertLine(wire_e, base_hbm, land_hbm, sum_sems, z, nc)
    wire_c = Wire(sends_c, recvs_c)
    gather_cot = PlaneGather(wire_c, cot_hbm, e, d_out_hbm)
    wire_x = Wire(sends_x, recvs_x)
    gather = PlaneGather(wire_x, x_all, e)
    scatter_dx = PlaneScatter(wire_1, dx_land, ids)
    scatter_y = PlaneScatter(wire_2, y_land, ids)
    dg_slot = wire_1.slots(3)

    def front_phase(wq_ref, wo_ref, x_ref, inputs_ref, query_ref, heads_ref, hidden_ref, kv_scr, q_scr):
        wire = Wire(sends_f, recvs_f)
        kv_width = 2 * key_width
        load_x = pltpu.make_async_copy(x_hbm, x_ref, load_sems.at[0])
        load_x.start()
        wq_ref[e, z, c] = qkv_ref[:, pl.ds(0, query_width)]
        wo_ref[e, z, c] = wo_shard_ref[...]
        wk_all[e, z, c, :, pl.ds(0, kv_width)] = qkv_ref[:, pl.ds(query_width, kv_width)]
        wk_all[e, z, c, :, pl.ds(kv_width, SMALL)] = small_ref[...]
        greet(
            [(ids[m], None) for m in (1, 2, 3)]
            + [(sibling, None)]
            + [({"context": z + d}, z + d < nc) for d in range(1, nc)]
            + [({"context": z - d}, z >= d) for d in range(1, nc)]
        )
        gather_k = RowsGather(wire, wk_all, e, z, c, nc, 256)
        gather_q = RowsGather(wire, wq_ref, e, z, c, nc, 768)
        gather_o = RowsGather(wire, wo_ref, e, z, c, nc, 768)
        gather_k.go("l0", "s0")
        gather_q.go("s0")
        gather_k.go("l1", "s1", "f0", "l2", "s2")
        gather_q.go("l0")
        gather_k.go("f1", "h0", "l3", "s3")
        gather_q.go("l1", "s1")
        gather_o.go("l0")
        gather_k.go("f2", "h1", "f3")
        gather_q.go("l2", "s2")
        gather_k.go("h2")
        gather_o.go("l1")
        gather_q.go("f0")
        gather_k.go("h3")
        gather_q.go("l3", "s3")
        gather_k.go("c")
        load_x.wait()
        rows = x_ref[...].astype(F32)
        scale1 = lax.rsqrt(jnp.mean(rows * rows, -1, keepdims=True) + EPSILON)

        small = wk_all[:, :, :, :, pl.ds(kv_width, SMALL)].reshape(width, SMALL)
        small = jnp.transpose(small.astype(F32))
        gain_first, gain_second = small[experts : experts + 1], small[experts + 1 : experts + 2]
        gains_ref[0:1] = gain_first
        gains_ref[1:2] = gain_second
        inputs_ref[...] = (rows * scale1 * gain_first).astype(BF16)
        kv_scr[...] = dot_nn(inputs_ref[...], wk_all[...].reshape(width, kv_width + SMALL))

        def turned(head):
            return (head * cos_ref[...] + swap_halves(head) * sin_ref[...]).astype(BF16)

        line = wire.slots(KEY_VALUE_HEADS * nc)
        for j in range(KEY_VALUE_HEADS):
            kv_ref[j, z, :, pl.ds(0, size)] = turned(kv_scr[:, pl.ds(j * size, size)])
            value = kv_scr[:, pl.ds(kv_width // 2 + j * size, size)]
            kv_ref[j, z, :, pl.ds(size, size)] = value.astype(BF16)
            mine = kv_ref.at[j, z]
            for d in range(nc - 1, 0, -1):
                wire.start(mine, mine, line + j * nc + z, {"context": z + d}, when=z + d < nc)

        def keys_here(j):
            for d in range(1, nc):

                def wait(d=d):
                    wire.arrived(kv_ref.at[j, z - d], line + j * nc + z - d, {"context": z - d})

                pl.when(z >= d)(wait)

        outs = [
            pltpu.make_async_copy(source, dest, out_sems.at[n])
            for n, (source, dest) in enumerate(
                (
                    (inputs_ref, inputs_hbm),
                    (query_ref, query_hbm),
                    (heads_ref, heads_hbm),
                    (hidden_ref, hidden_hbm),
                    (wq_ref, wq_hbm),
                    (wo_ref, wo_hbm),
                )
            )
        ]
        outs[0].start()
        for later in range(1, nc):

            def clear(later=later):
                for j in range(KEY_VALUE_HEADS):
                    kv_ref[j, z + later] = jnp.zeros(kv_ref.shape[2:], BF16)

            pl.when(z + later < nc)(clear)
        gather_q.go("f1", "f2", "h0")
        gather_o.go("s0")
        gather_q.go("f3", "h1")
        gather_o.go("s1")
        gather_q.go("h2", "h3", "c")
        outs[4].start()
        gather_o.go("f0", "f1")
        gather_cot.spread()

        @pl.loop(0, query_width // 256)
        def _(n):
            columns = pl.ds(pl.multiple_of(n * 256, 256), 256)
            q_scr[:, columns] = dot_nn(
                inputs_ref[...], wq_ref[:, :, :, :, columns].reshape(width, 256)
            )

        @pl.loop(0, QUERY_HEADS)
        def _(h):
            columns = pl.ds(pl.multiple_of(h * size, size), size)
            query_ref[:, columns] = turned(q_scr[:, columns])

        outs[1].start()

        logits = kv_scr[:, pl.ds(kv_width, SMALL)]
        lanes = lax.broadcasted_iota(jnp.int32, logits.shape, 1)
        routes = jnp.concatenate(
            [routes_ref[...].astype(F32), jnp.zeros((SMALL - TOP, tokens), F32)], 0
        )
        routes = jnp.transpose(routes).astype(jnp.int32)
        named = lanes == routes[:, 0:1]
        for k in range(1, TOP):
            named = named | (lanes == routes[:, k : k + 1])
        logits = jnp.where(named, logits, MASKED)
        expd = jnp.exp(logits - jnp.max(logits, -1, keepdims=True))
        gates = expd / jnp.sum(expd, -1, keepdims=True)
        gate_all[0] = jnp.transpose(gates)[:GATE_ROWS]
        gate_slot = wire.slots(3)
        for r in (1, 2, 3):
            wire.start(gate_all.at[0], gate_all.at[r], gate_slot + r - 1, ids[r])

        length = nc * tokens
        group = QUERY_HEADS // KEY_VALUE_HEADS

        def attend(first, last):
            j = first // group
            key = kv_ref[j, :, :, pl.ds(0, size)].reshape(length, size)
            value = kv_ref[j, :, :, pl.ds(size, size)].reshape(length, size)
            value_turned = jnp.transpose(value)

            @pl.loop(first, last)
            def _(h):
                column = pl.multiple_of(h * size, size)
                scores = causal(dot_nt(key, query_ref[:, pl.ds(column, size)]), z * tokens)
                largest = jnp.max(scores, 0, keepdims=True)
                expd = jnp.exp((scores - largest) * (size**-0.5))
                total = jnp.sum(expd, 0, keepdims=True)
                mixed = dot_nn(value_turned, expd.astype(BF16)) / total
                heads_ref[:, pl.ds(column, size)] = jnp.transpose(mixed).astype(BF16)

        half = group // 2
        keys_here(0)
        attend(0, half)
        gather_o.go("l2", "s2")
        attend(half, group)
        gather_o.go("l3", "s3", "f2", "h0")
        keys_here(1)
        attend(group, group + half)
        gather_o.go("f3", "h1")
        attend(group + half, QUERY_HEADS)
        gather_o.go("h2")
        gather_cot.forward()
        gather_o.go("h3", "c")
        outs[5].start()
        outs[2].start()
        part = width // wo_ref.shape[0]
        for block in range(wo_ref.shape[0]):
            weight = wo_ref[block].reshape(part, width)
            columns = pl.ds(block * part, part)
            hidden_ref[:, columns] = x_ref[:, columns].astype(F32) + dot_nt(heads_ref[...], weight)
        hidden = hidden_ref[...]
        scale2 = lax.rsqrt(jnp.mean(hidden * hidden, -1, keepdims=True) + EPSILON)
        x_all[0] = (hidden * scale2 * gains_ref[1:2]).astype(BF16)
        gather.spread()
        outs[3].start()
        for r in (1, 2, 3):
            wire.arrived(gate_all.at[r], gate_slot + r - 1, ids[r])
        for r in range(gate_all.shape[0]):
            zeros = jnp.zeros((SMALL - GATE_ROWS, tokens), F32)
            turned_gates = jnp.transpose(jnp.concatenate([gate_all[r], zeros], 0))
            both = [
                jnp.sum(jnp.where(lanes == e * EXP_DEV + i, turned_gates, 0.0), -1, keepdims=True)
                for i in range(EXP_DEV)
            ]
            gates_ref[r] = jnp.where(lanes == 0, both[0], jnp.where(lanes == 1, both[1], 0.0))
        for copy in outs:
            copy.wait()
        wire.finish()

    def token_phase(w_gu, w_dn, cot_all, a_all, dgu_all, stage, ins, x_turned, cot_turned):
        expert.ins = ins
        scatter_dx.part = lambda r, half: x_all.at[r, :, pl.ds(half * width // 2, width // 2)]
        sources = [
            (w_gu_hbm.at[0], w_gu.at[0]),
            (w_dn_hbm.at[0], w_dn.at[0]),
            (d_out_hbm, cot_all.at[0]),
            (w_gu_hbm.at[1], w_gu.at[1]),
            (w_dn_hbm.at[1], w_dn.at[1]),
            (cot_hbm.at[1:], cot_all.at[1:]),
        ]
        loads = [
            pltpu.make_async_copy(source, dest, load_sems.at[n])
            for n, (source, dest) in enumerate(sources)
        ]
        for copy in loads[:5]:
            copy.start()
        step = 256
        wide = 512
        dg_lanes[...] = jnp.zeros_like(dg_lanes)

        def hidden_units(r, i, count=1):
            lane = lax.broadcasted_iota(jnp.int32, (1, SMALL), 1)
            here = pl.ds(r, count)
            flat = count * tokens

            @pl.loop(0, ff // step)
            def _(f):
                column = pl.multiple_of(f * step, step)
                rows = x_all[here].reshape(flat, width)
                grads = cot_all[here].reshape(flat, width)
                gate_part = dot_nn(rows, w_gu[i, :, pl.ds(column, step)])
                up_part = dot_nn(rows, w_gu[i, :, pl.ds(ff + column, step)])
                raw = dot_nt(grads, w_dn[i, pl.ds(column, step), :])
                gate = gates_ref[here].reshape(flat, SMALL)
                gate = jnp.sum(jnp.where(lane == i, gate, 0.0), -1, keepdims=True)
                sigma = jax.nn.sigmoid(gate_part)
                silu = gate_part * sigma
                act = silu * up_part
                lanes = lax.broadcasted_iota(jnp.int32, (flat, SMALL), 1)
                d_gate = jnp.where(
                    lanes == e * EXP_DEV + i, jnp.sum(act * raw, -1, keepdims=True), 0.0
                )
                dg_lanes[here] += d_gate.reshape(count, tokens, SMALL)

                def put(ref, first, values):
                    values = values.astype(BF16).reshape(count, tokens, step)
                    ref[here, :, pl.ds(pl.multiple_of(first, step), step)] = values

                put(a_all, i * ff + column, act * gate)
                d_act = raw * gate
                d_gate_part = d_act * up_part * sigma * (1.0 + gate_part * (1.0 - sigma))
                put(dgu_all, i * 2 * ff + column, d_gate_part)
                put(dgu_all, i * 2 * ff + ff + column, d_act * silu)

        def turn(rows, turned, r):
            @pl.loop(0, width // wide)
            def _(n):
                columns = pl.ds(pl.multiple_of(n * wide, wide), wide)
                turned[columns, pl.ds(r * tokens, tokens)] = jnp.transpose(rows[r, :, columns])

        def y_copy(r):
            return pltpu.make_async_copy(cot_all.at[r], y_hbm.at[r], out_sems.at[r])

        def outputs(r, count=1):
            here = pl.ds(r, count)
            flat = count * tokens

            @pl.loop(0, width // wide)
            def _(n):
                columns = pl.ds(pl.multiple_of(n * wide, wide), wide)
                low = dgu_all[here].reshape(flat, EXP_DEV * 2 * ff)
                d_rows = dot_nt(low[:, : 2 * ff], w_gu[0, columns, :])
                d_rows += dot_nt(low[:, 2 * ff :], w_gu[1, columns, :])
                weight = w_dn[:, :, columns].reshape(EXP_DEV * ff, wide)
                out = dot_nn(a_all[here].reshape(flat, EXP_DEV * ff), weight).astype(BF16)
                for k in range(count):
                    rows = slice(k * tokens, (k + 1) * tokens)
                    cot_all[r + k, :, columns] = out[rows]
                    if r == 0:
                        d_in_ref[:, columns] = d_rows
                    else:
                        x_all[r + k, :, columns] = d_rows[rows].astype(BF16)

            for k in range(r, r + count):
                y_copy(k).start()
                dg_part[k] = jnp.transpose(dg_lanes[k])[:GATE_ROWS]
                if k:
                    wire_1.start(dg_part.at[k], dg_land.at[k - 1], dg_slot + k - 1, ids[k])

        half_rows = width // nc // 2
        def where(k):
            high = lax.rem(lax.div(z, 2) + 1 + lax.div(k, 2), 2)
            return 2 * high + lax.rem(z + 1 + k, 2)

        def keep(i, k):
            slot = lax.rem(k, 2)
            return pltpu.make_async_copy(
                stage.at[slot, c], expert.part(base_hbm, where(k), i), stage_sems.at[slot]
            )

        def hand(i, k):
            return pltpu.make_async_remote_copy(
                src_ref=stage.at[lax.rem(k, 2), 1 - c],
                dst_ref=core_land.at[k],
                send_sem=hand_sends.at[i * nc + k],
                recv_sem=hand_recvs.at[i * nc + k],
                device_id=sibling,
                device_id_type=MESH,
            )

        def settle(i, k):
            hand(i, k).wait_recv()
            add_into(stage.at[lax.rem(k, 2), c], core_land.at[k])
            keep(i, k).start()

        def clear(i, k):
            keep(i, k).wait()
            hand(i, k).wait_send()

        def leave(i, r):
            if r == 1:
                expert.send(i, r, when=even if i else None)
            elif r == 3 or r == 2 and i == 0:
                expert.send(i, r, when=expert.end)
            elif r == 2:
                expert.send(i, r, when=bottom)

        def weight_grads(i, between=lambda k: None):
            @pl.loop(0, nc)
            def _(k):
                @pl.when(k >= 2)
                def _():
                    clear(i, k - 2)

                for n in (2, 3):

                    @pl.when(k == n)
                    def _(n=n):
                        leave(i, 5 - n)

                rows_at = pl.ds(pl.multiple_of(where(k) * 2 * half_rows, 2 * half_rows), 2 * half_rows)
                for first, rows, grad, start, count in (
                    (0, x_turned[rows_at, :], dgu_all, i * 2 * ff, 2),
                    (2 * ff, cot_turned[rows_at, :], a_all, i * ff, 1),
                ):

                    @pl.loop(0, count)
                    def _(n):
                        column = pl.multiple_of(n * ff, ff)
                        part = grad[:, :, pl.ds(pl.multiple_of(start + column, ff), ff)]
                        result = dot_nn(rows, part.reshape(blocks * tokens, ff)).astype(BF16)
                        stage[lax.rem(k, 2), :, :, pl.ds(pl.multiple_of(first + column, ff), ff)] = (
                            result.reshape(2, half_rows, ff)
                        )

                if i:

                    @pl.when(k == 0)
                    def _():
                        pl.semaphore_wait(credits.at[3], 1)

                hand(i, k).start()

                @pl.when(k >= 1)
                def _():
                    settle(i, k - 1)

                between(k)

        for copy in loads[:3]:
            copy.wait()
        gather_cot.complete()
        loads[5].start()
        for copy in loads[3:5]:
            copy.wait()

        @pl.loop(0, EXP_DEV)
        def _(i):
            hidden_units(0, i)

        gather.forward()
        turn(x_all, x_turned, 0)
        turn(cot_all, cot_turned, 0)
        outputs(0)
        loads[5].wait()
        for r in range(1, blocks):
            turn(cot_all, cot_turned, r)
        gather.near(1)
        gather.near(2)
        turn(x_all, x_turned, 1)
        turn(x_all, x_turned, 2)
        hidden_units(1, 0, 2)
        gather.far()
        turn(x_all, x_turned, 3)
        hidden_units(3, 0)
        weight_grads(0)
        hidden_units(1, 1, 2)
        clear(0, nc - 2)
        leave(0, 1)
        settle(0, nc - 1)
        pl.semaphore_signal(credits.at[3], inc=1, device_id=sibling, device_id_type=MESH)
        wire_x.finish()
        outputs(1, 2)
        scatter_dx.near(1)
        scatter_dx.near(2)
        hidden_units(3, 1)
        expert.relay_begin(0, 2)
        outputs(3)
        scatter_dx.far()
        clear(0, nc - 1)
        expert.relay_add(0, 2)

        def between(k):
            @pl.when(k == 0)
            def _():
                expert.relay_send(0, 2)

            @pl.when(k == 1)
            def _():
                scatter_dx.relay()

            @pl.when(k == 2)
            def _():
                expert.relay_begin(0, 3)

            @pl.when(k == 3)
            def _():
                expert.relay_add(0, 3)

        weight_grads(1, between)
        expert.relay_send(0, 3)
        scatter_dx.total(d_in_ref)
        for r in (1, 2):
            pl.semaphore_signal(credits.at[r], inc=1, device_id=ids[r], device_id_type=MESH)
        settle(1, nc - 1)
        for k in (nc - 2, nc - 1):
            clear(1, k)
        leave(1, 1)
        for r in range(blocks):
            y_copy(r).wait()
        wire_1.finish()
        wire_c.finish()
        pl.semaphore_signal(credits.at[0], inc=1, device_id=sibling, device_id_type=MESH)

    def token_rows_phase(
        weight,
        grads_o,
        grads_q,
        x_ref,
        inputs_ref,
        query_ref,
        heads_ref,
        hidden_ref,
        d_hidden_ref,
        d_attn_ref,
        d_heads_ref,
        d_all_ref,
        rows_ref,
        dkv_acc,
        dkv_ref,
        y_relay,
        ins,
        out_wide,
    ):
        expert.ins, expert.out = ins, out_wide
        cot_ref, d_inputs_ref = d_heads_ref, hidden_ref
        scatter_y.part = lambda r, half: y_hbm.at[r, :, pl.ds(half * width // 2, width // 2)]
        y_loads = [
            pltpu.make_async_copy(scatter_y.part(2 - half, half), y_relay.at[half], y_sems.at[half])
            for half in range(2)
        ]
        for copy in y_loads:
            copy.start()
        planes = grads_o.shape[1]
        part = width // planes
        sources = (
            (hidden_hbm, hidden_ref),
            (d_out_hbm, cot_ref),
            (wo_hbm, weight),
            (heads_hbm, heads_ref),
            (query_hbm, query_ref),
            (x_hbm, x_ref),
            (inputs_hbm, inputs_ref),
        )
        loads = [
            pltpu.make_async_copy(source, dest, load_sems.at[4 + n])
            for n, (source, dest) in enumerate(sources)
        ]
        for copy in loads:
            copy.start()
        for r in (1, 2):
            scatter_y.near(r)
        scatter_y.far()

        def rows_scatter(buf, core, plane, lines, start, count, half):
            return RowsScatter(
                wire_2,
                buf,
                core,
                plane,
                lines,
                e,
                z,
                c,
                nc,
                start,
                count,
                half,
            )

        rows_of = part // 2
        scatter_o = rows_scatter(
            grads_o,
            x_all.at[:, pl.ds(0, rows_of)],
            lambda slot, half: dx_land.at[slot, pl.ds(0, rows_of)],
            lines_o,
            0,
            width,
            width // 2,
        )
        scatter_q = rows_scatter(
            grads_q,
            core_land.at[:, :, pl.ds(0, query_width)],
            lambda slot, half: plane_q.at[slot],
            lines_q,
            0,
            query_width,
            query_width // 2,
        )
        rest_half = rest // 256 * 128
        scatter_k = rows_scatter(
            grads_q,
            core_land.at[:, :, pl.ds(query_width, rest)],
            lambda slot, half: plane_k.at[
                slot, :, pl.ds(0, rest - rest_half if half else rest_half)
            ],
            lines_k,
            query_width,
            rest,
            rest_half,
        )
        scatter_kv = [
            LineSum(wire_2, lambda j, h=h: dkv_ref.at[h, j], dkv_land.at[h], z, nc, up=False)
            for h in range(KEY_VALUE_HEADS)
        ]

        for scatter in (scatter_o, scatter_q, scatter_k):
            scatter.line.clear()
        for line in scatter_kv:
            line.clear()

        loads[0].wait()
        loads[1].wait()
        hidden, d_in = hidden_ref[...], d_in_ref[...]
        scale2 = lax.rsqrt(jnp.mean(hidden * hidden, -1, keepdims=True) + EPSILON)
        scaled = d_in * gains_ref[1:2]
        mean = jnp.mean(scaled * hidden, -1, keepdims=True)
        d_hidden = cot_ref[...].astype(F32) + scale2 * scaled
        d_hidden = d_hidden - hidden * (scale2 * scale2 * scale2 * mean)
        d_hidden_ref[...] = d_hidden
        d_attn_ref[...] = d_hidden.astype(BF16)
        rows_ref[...] = jnp.zeros_like(rows_ref)
        rows_ref[experts + 1 : experts + 2, :] = jnp.sum(d_in * hidden * scale2, 0, keepdims=True)

        loads[2].wait()

        @pl.loop(0, query_width // 256)
        def _(n):
            columns = pl.ds(pl.multiple_of(n * 256, 256), 256)
            out = weight[:, :, :, :, columns].reshape(width, 256)
            d_heads_ref[:, columns] = dot_nn(d_attn_ref[...], out).astype(BF16)

        load_q = pltpu.make_async_copy(wq_hbm, weight, load_sems.at[0])
        load_q.start()
        loads[3].wait()

        def row_grads(buf, left, right, first, count, extra=None):
            @pl.loop(0, planes)
            def _(block):
                columns = pl.ds(pl.multiple_of(block * part, part), part)
                result = dot_tn(left[:, columns], right)
                if extra is not None:
                    result = result + extra(columns)
                result = result.astype(BF16).reshape(nc, 2, part // nc // 2, count)
                for half in range(2):
                    buf[half, block, :, pl.ds(first, count)] = result[:, half].reshape(
                        part // 2, count
                    )

        length = nc * tokens
        group = QUERY_HEADS // KEY_VALUE_HEADS
        loads[4].wait()
        dkv_acc[...] = jnp.zeros_like(dkv_acc)

        def attend(j, first, last):
            key = kv_ref[j, :, :, pl.ds(0, size)].reshape(length, size)
            value = kv_ref[j, :, :, pl.ds(size, size)].reshape(length, size)
            key_turned = jnp.transpose(key)

            @pl.loop(j * group + first, j * group + last)
            def _(h):
                columns = pl.ds(pl.multiple_of(h * size, size), size)
                query, grad = query_ref[:, columns], d_heads_ref[:, columns]
                scores = causal(dot_nt(key, query), z * tokens)
                largest = jnp.max(scores, 0, keepdims=True)
                expd = jnp.exp((scores - largest) * (size**-0.5))
                probs = expd * (1.0 / jnp.sum(expd, 0, keepdims=True))
                d_probs = dot_nt(value, grad)
                inner = jnp.sum(probs * d_probs, 0, keepdims=True)
                d_raw = (probs * (d_probs - inner) * (size**-0.5)).astype(BF16)
                d_query = jnp.transpose(dot_nn(key_turned, d_raw))
                d_query = d_query * cos_ref[...] - swap_halves(d_query) * sin_ref[...]
                d_all_ref[:, columns] = d_query.astype(BF16)
                dkv_acc[j, :, pl.ds(0, size)] += dot_nn(d_raw, query)
                dkv_acc[j, :, pl.ds(size, size)] += dot_nn(probs.astype(BF16), grad)

        def round_kv(j):
            for block in range(nc):
                rows = dkv_acc[j, pl.ds(block * tokens, tokens), :]
                dkv_ref[j, block] = rows.astype(BF16)

        def enter():
            pl.semaphore_wait(credits.at[1], 1)
            pl.semaphore_wait(credits.at[2], 1)

        attend(0, 0, group)
        round_kv(0)
        scatter_kv[0].send()
        attend(1, 0, group)
        round_kv(1)
        scatter_kv[1].send()
        expert.send(1, 2, when=top)
        expert.send(1, 1, when=odd)
        expert.relay_begin(1, 2)
        row_grads(grads_o, d_attn_ref, heads_ref[...], 0, width)
        expert.relay_add(1, 2)
        pl.semaphore_wait(credits.at[0], 1)
        scatter_o.share()
        y_own = pltpu.make_async_copy(y_hbm.at[0], heads_ref, load_sems.at[2])
        y_own.start()
        for copy in y_loads:
            copy.wait()
        scatter_y.relay(lambda r, half: y_relay.at[half])
        expert.relay_send(1, 2)
        scatter_o.merge(enter)

        for copy in loads[5:]:
            copy.wait()
        row_grads(grads_q, inputs_ref, d_all_ref[:, pl.ds(0, query_width)], 0, query_width)
        scatter_q.share()
        scatter_o.relay()
        expert.last(0, (sum_gu_hbm, sum_dn_hbm))
        scatter_q.merge()
        for h in range(KEY_VALUE_HEADS):
            grad = scatter_kv[h].total()
            d_key = grad[:, :size]
            d_key = d_key * cos_ref[...] - swap_halves(d_key) * sin_ref[...]
            d_all_ref[:, pl.ds(query_width + h * size, size)] = d_key.astype(BF16)
            d_all_ref[:, pl.ds(query_width + key_width + h * size, size)] = grad[:, size:].astype(
                BF16
            )
        y_own.wait()
        hidden_ref[...] += heads_ref[...].astype(F32)
        scatter_y.total(hidden_ref)
        heads_ref[...] = hidden_ref[...].astype(BF16)
        layer_out = pltpu.make_async_copy(heads_ref, layer_hbm, out_sems.at[0])
        layer_out.start()

        total = dg_part[0]
        for r in (1, 2, 3):
            wire_1.arrived(dg_land.at[r - 1], dg_slot + r - 1, ids[r])
            total = total + dg_land[r - 1]
        gates = gate_all[0]
        d_logits = gates * (total - jnp.sum(gates * total, 0, keepdims=True))
        d_logits = jnp.concatenate(
            [d_logits, jnp.zeros((SMALL - d_logits.shape[0], tokens), F32)], 0
        )
        d_all_ref[:, pl.ds(qkv_width, SMALL)] = jnp.transpose(d_logits).astype(BF16)

        load_q.wait()

        @pl.loop(0, planes)
        def _(block):
            columns = pl.ds(pl.multiple_of(block * part, part), part)
            rows_q = weight[block].reshape(part, query_width)
            rows_k = wk_all[block].reshape(part, rest)
            d_inputs_ref[:, columns] = dot_nt(
                d_all_ref[:, pl.ds(0, query_width)], rows_q
            ) + dot_nt(d_all_ref[:, pl.ds(query_width, rest)], rows_k)

        rows = x_ref[...].astype(F32)
        scale1 = lax.rsqrt(jnp.mean(rows * rows, -1, keepdims=True) + EPSILON)
        d_inputs = d_inputs_ref[...]
        rows_ref[experts : experts + 1, :] = jnp.sum(d_inputs * rows * scale1, 0, keepdims=True)

        def extra(columns):
            small = jnp.transpose(rows_ref[:, columns])
            return jnp.concatenate([jnp.zeros((part, rest - SMALL), F32), small], 1)

        row_grads(
            grads_q, inputs_ref, d_all_ref[:, pl.ds(query_width, rest)], query_width, rest, extra
        )
        scatter_k.share()
        scatter_o.total()
        scatter_o.line.send()
        expert.relay_begin(1, 3)
        scatter_q.relay()
        expert.relay_add(1, 3)
        scatter_k.merge()
        expert.relay_send(1, 3)
        scaled = d_inputs_ref[...] * gains_ref[0:1]
        rows = x_ref[...].astype(F32)
        scale1 = lax.rsqrt(jnp.mean(rows * rows, -1, keepdims=True) + EPSILON)
        mean = jnp.mean(scaled * rows, -1, keepdims=True)
        d_x = d_hidden_ref[...] + scale1 * scaled - rows * (scale1 * scale1 * scale1 * mean)
        inputs_ref[...] = d_x.astype(BF16)
        d_x_out = pltpu.make_async_copy(inputs_ref, d_x_hbm, out_sems.at[1])
        d_x_out.start()
        scatter_q.total()
        scatter_q.line.send()
        scatter_k.relay()
        scatter_k.total()
        scatter_k.line.send()
        sum_o_ref[...] = scatter_o.line.total()
        expert.last(1, (sum_gu_hbm, sum_dn_hbm))
        sum_q_ref[:, pl.ds(0, query_width)] = scatter_q.line.total()
        sum_q_ref[:, pl.ds(query_width, rest)] = scatter_k.line.total()
        layer_out.wait()
        d_x_out.wait()
        wire_2.finish()
        expert.finish()

    held = EXP_DEV
    weight_shape = wq_hbm.shape
    pl.run_scoped(
        front_phase,
        pltpu.VMEM(weight_shape, BF16),
        pltpu.VMEM(weight_shape, BF16),
        pltpu.VMEM((tokens, width), BF16),
        pltpu.VMEM((tokens, width), BF16),
        pltpu.VMEM((tokens, query_width), BF16),
        pltpu.VMEM((tokens, query_width), BF16),
        pltpu.VMEM((tokens, width), F32),
        pltpu.VMEM((tokens, rest), F32),
        pltpu.VMEM((tokens, query_width), F32),
    )
    shard, step = width // nc // 2, 48
    pl.run_scoped(
        token_phase,
        pltpu.VMEM((held, width, 2 * ff), BF16),
        pltpu.VMEM((held, ff, width), BF16),
        pltpu.VMEM((blocks, tokens, width), BF16),
        pltpu.VMEM((blocks, tokens, held * ff), BF16),
        pltpu.VMEM((blocks, tokens, held * 2 * ff), BF16),
        pltpu.VMEM((2, 2, shard, grad_width // held), BF16),
        pltpu.VMEM((2, shard // step, step, grad_width // held), BF16),
        pltpu.VMEM((width, blocks * tokens), BF16),
        pltpu.VMEM((width, blocks * tokens), BF16),
    )
    rows_half = width // blocks // 2
    pl.run_scoped(
        token_rows_phase,
        pltpu.VMEM(weight_shape, BF16),
        pltpu.VMEM((2, blocks, rows_half, width), BF16),
        pltpu.VMEM((2, blocks, rows_half, qkv_width + SMALL), BF16),
        pltpu.VMEM((tokens, width), BF16),
        pltpu.VMEM((tokens, width), BF16),
        pltpu.VMEM((tokens, query_width), BF16),
        pltpu.VMEM((tokens, query_width), BF16),
        pltpu.VMEM((tokens, width), F32),
        pltpu.VMEM((tokens, width), F32),
        pltpu.VMEM((tokens, width), BF16),
        pltpu.VMEM((tokens, query_width), BF16),
        pltpu.VMEM((tokens, qkv_width + SMALL), BF16),
        pltpu.VMEM((SMALL, width), F32),
        pltpu.VMEM((KEY_VALUE_HEADS, nc * tokens, 2 * size), F32),
        pltpu.VMEM((KEY_VALUE_HEADS, nc, tokens, 2 * size), BF16),
        pltpu.VMEM((2, tokens, width // 2), BF16),
        pltpu.VMEM((4, shard // step, step, grad_width // held), BF16),
        pltpu.VMEM((2, step, grad_width // held), F32),
    )


def layer(operands, sizes):
    ne, nc, nd = sizes
    qkv_shard, x = operands[3], operands[6]
    w_dn = operands[9]
    tokens, width = x.shape
    held, ff = w_dn.shape[0], w_dn.shape[1]
    query_width = QUERY_HEADS * HEAD_DIMENSION
    rows, qkv_width = qkv_shard.shape
    rest = qkv_width - query_width + SMALL
    rest_half = rest // 256 * 128
    shard, grads = width // (nc * nd), held * 3 * ff
    kv_size = 2 * HEAD_DIMENSION
    weight = (ne, nc, nd, rows, query_width)
    shapes = [
        ((tokens, width), BF16),
        ((tokens, width), BF16),
        ((rows, qkv_width + SMALL), F32),
        ((rows, width), F32),
        ((held, shard, 2 * ff), F32),
        ((held, shard, ff), F32),
        ((nc, shard, grads), BF16),
        ((nc + 2, shard, grads), BF16),
        ((ne, tokens, width), BF16),
        (weight, BF16),
        (weight, BF16),
        ((ne, tokens, width), BF16),
        ((tokens, width), BF16),
        ((tokens, query_width), BF16),
        ((tokens, query_width), BF16),
        ((tokens, width), F32),
    ]
    vmem = pl.BlockSpec(memory_space=pltpu.VMEM)
    anywhere = pl.BlockSpec(memory_space=pl.ANY)
    units = nc * held
    sems = [120, 110, 6, 6, 6, 6, 10, 10, 64, 64, 2 * units, (nc + 2) * held, units, units, 2, 12, 6]
    return pl.pallas_call(
        functools.partial(layer_kernel, nc, EXP_DEV * ne),
        out_shape=[jax.ShapeDtypeStruct(*s) for s in shapes],
        in_specs=[vmem] * 6 + [anywhere] * (len(operands) - 6),
        out_specs=[anywhere] * 2 + [vmem] * 2 + [anywhere] * (len(shapes) - 4),
        scratch_shapes=[
            pltpu.VMEM((ne, nc, nd, rows, rest), BF16),
            pltpu.VMEM((KEY_VALUE_HEADS, nc, tokens, kv_size), BF16),
            pltpu.VMEM((ne, GATE_ROWS, tokens), F32),
            pltpu.VMEM((ne, tokens, SMALL), F32),
            pltpu.VMEM((8, width), F32),
            pltpu.VMEM((ne, tokens, width), BF16),
            pltpu.VMEM((6, tokens, width // 2), BF16),
            pltpu.VMEM((6, tokens, width // 2), BF16),
            pltpu.VMEM((nc, shard, grads // held), BF16),
            pltpu.VMEM((6, nc * rows, query_width // 2), BF16),
            pltpu.VMEM((6, nc * rows, rest - rest_half), BF16),
            pltpu.VMEM((nc, rows, width), BF16),
            pltpu.VMEM((nc, rows, query_width), BF16),
            pltpu.VMEM((nc, rows, rest), BF16),
            pltpu.VMEM((KEY_VALUE_HEADS, nc, tokens, kv_size), BF16),
            pltpu.VMEM((tokens, width), F32),
            pltpu.VMEM((ne, tokens, SMALL), F32),
            pltpu.VMEM((ne, GATE_ROWS, tokens), F32),
            pltpu.VMEM((ne - 1, GATE_ROWS, tokens), F32),
        ]
        + [pltpu.SemaphoreType.DMA((count,)) for count in sems]
        + [
            pltpu.SemaphoreType.DMA((20,)),
            pltpu.SemaphoreType.DMA((2,)),
            pltpu.SemaphoreType.REGULAR((4,)),
        ],
        compiler_params=pltpu.CompilerParams(
            collective_id=0, has_side_effects=True, vmem_limit_bytes=63 * MIB
        ),
    )(*operands)


def finish_kernel(experts, *refs):
    sources, dests = refs[:6], refs[6:12]
    router_ref, first_ref, second_ref = refs[12:]
    sum_q = sources[0]
    qkv_width = dests[0].shape[-1]
    dests[0][...] = sum_q[:, pl.ds(0, qkv_width)]
    for source, dest in zip(sources[1:], dests[1:]):
        dest[...] = source[...]
    small = sum_q[:, pl.ds(qkv_width, SMALL)]
    rows = small.shape[0]
    filled = jnp.concatenate([small, jnp.zeros((SMALL - rows, SMALL), F32)], 0)
    turned = jnp.transpose(filled)[:, :rows]
    router_ref[...] = turned[:experts]
    first_ref[...] = turned[experts : experts + 1]
    second_ref[...] = turned[experts + 1 : experts + 2]


def finish(sum_q, others, experts):
    rows, q_width = sum_q.shape
    vmem = pl.BlockSpec(memory_space=pltpu.VMEM)
    shapes = [jax.ShapeDtypeStruct((rows, q_width - SMALL), F32)]
    shapes += [jax.ShapeDtypeStruct(o.shape, o.dtype) for o in others]
    shapes += [jax.ShapeDtypeStruct((count, rows), F32) for count in (experts, 1, 1)]
    return pl.pallas_call(
        functools.partial(finish_kernel, experts),
        out_shape=shapes,
        in_specs=[vmem] * 6,
        out_specs=[vmem] * 9,
        compiler_params=pltpu.CompilerParams(vmem_limit_bytes=60 * MIB),
    )(sum_q, *others)


def local_plain(
    layer_input,
    gain_attn,
    query_key_value_weight,
    w_out,
    w_router,
    gain_ffn,
    w_gate_up,
    w_down,
    routes,
    d_out,
):
    tokens = layer_input.shape[1]
    model_width = layer_input.shape[2]
    ne, nc, nd = (lax.axis_size(a) for a in ("expert", "context", "dp"))
    expert_total = EXP_DEV * ne
    ff = w_down.shape[1]
    me = lax.axis_index("expert")
    first_row = lax.axis_index("context") * tokens
    query_width = QUERY_HEADS * HEAD_DIMENSION
    key_width = KEY_VALUE_HEADS * HEAD_DIMENSION
    qkv_width = query_width + 2 * key_width

    small = jnp.concatenate([w_router, gain_attn[:, None], gain_ffn[:, None]], -1)
    small = jnp.pad(small, ((0, 0), (0, 128 - small.shape[1])))
    gathered = gather_rows(jnp.concatenate([query_key_value_weight, small], -1))
    out_turned = gather_rows(w_out.T)
    qkv_weight = gathered[:, :qkv_width]
    router_weight = gathered[:, qkv_width : qkv_width + expert_total]
    gains = gathered[:, qkv_width + expert_total : qkv_width + expert_total + 2].T.astype(F32)
    gain_first, gain_second = gains[0], gains[1]
    cotangent_all = plane_gather(d_out[0])

    token_rows = layer_input[0].astype(F32)
    scale1 = lax.rsqrt(jnp.mean(token_rows * token_rows, -1, keepdims=True) + EPSILON)
    inputs1 = (token_rows * scale1 * gain_first).astype(BF16)
    query_key_value = dot_nn(inputs1, qkv_weight)
    cosine_values, sine_values = rope_tables(first_row + jnp.arange(tokens), HEAD_DIMENSION)
    rotated = rotate_half(
        query_key_value[:, : query_width + key_width].reshape(tokens, -1, HEAD_DIMENSION),
        cosine_values,
        sine_values,
    ).reshape(tokens, -1)
    query = rotated[:, :query_width].astype(BF16)
    key_value_local = jnp.concatenate(
        [rotated[:, query_width:], query_key_value[:, query_width + key_width :]], -1
    ).astype(BF16)
    key_value = line_gather(key_value_local, "context", both=False).reshape(nc * tokens, -1)
    first = first_row.astype(jnp.int32).reshape(1)
    heads = attend_forward(first, query, key_value)

    logits = dot_nn(inputs1, router_weight)
    chosen_ids = routes[0]
    picks = (chosen_ids[:, :, None] == jnp.arange(expert_total)[None, None, :]).astype(F32)
    chosen = jnp.sum(picks * logits[:, None, :], -1)
    gates = jax.nn.softmax(chosen, axis=-1)
    gate_dense = jnp.sum(picks * gates[:, :, None], 1).T
    gate_blocks = cube_gather(gate_dense, "expert", axis_masks("expert"))
    gate_local = jnp.concatenate(
        [lax.dynamic_slice_in_dim(b, me * EXP_DEV, EXP_DEV, 0) for b in gate_blocks], 1
    )

    attn = dot_nt(heads, out_turned)
    hidden = token_rows + attn
    scale2 = lax.rsqrt(jnp.mean(hidden * hidden, -1, keepdims=True) + EPSILON)
    expert_in = (hidden * scale2 * gain_second).astype(BF16)

    rows_all = plane_gather(expert_in)
    gate_up = jnp.einsum("td,edf->etf", rows_all, w_gate_up, preferred_element_type=F32)
    gate_part, up_part = gate_up[..., :ff], gate_up[..., ff:]
    sigma = jax.nn.sigmoid(gate_part)
    silu = gate_part * sigma
    act = silu * up_part
    gate_column = gate_local[:, :, None]
    act_gated = (act * gate_column).astype(BF16)
    partial_out = jnp.einsum("etf,efd->td", act_gated, w_down, preferred_element_type=F32)
    mixture = plane_scatter(partial_out.astype(BF16), tokens)
    layer_result = (hidden + mixture).astype(BF16)

    d_act_raw = jnp.einsum("td,efd->etf", cotangent_all, w_down, preferred_element_type=F32)
    d_gates_local = jnp.sum(d_act_raw * act, -1)
    d_act = d_act_raw * gate_column
    d_gate_part = d_act * up_part * sigma * (1.0 + gate_part * (1.0 - sigma))
    d_up_part = d_act * silu
    d_gate_up = jnp.concatenate([d_gate_part, d_up_part], -1).astype(BF16)
    d_rows = jnp.einsum("etf,edf->td", d_gate_up, w_gate_up, preferred_element_type=F32)
    grad_down = jnp.einsum("td,etf->edf", cotangent_all, act_gated, preferred_element_type=F32)
    grad_gate_up = jnp.einsum("td,etf->edf", rows_all, d_gate_up, preferred_element_type=F32)

    d_expert_in = plane_scatter(d_rows.astype(BF16), tokens)
    d_gate_blocks = d_gates_local.reshape(EXP_DEV, ne, tokens)
    d_gates_dense = jnp.zeros((expert_total, tokens), F32)
    for r in range(ne):
        arrived = d_gate_blocks[:, r]
        if r:
            arrived = exchange(arrived, "expert", r)
        d_gates_dense = lax.dynamic_update_slice(d_gates_dense, arrived, ((me ^ r) * EXP_DEV, 0))
    d_gates = jnp.sum(picks * d_gates_dense.T[:, None, :], -1)
    d_chosen = gates * (d_gates - jnp.sum(gates * d_gates, -1, keepdims=True))
    d_logits = jnp.sum(picks * d_chosen[:, :, None], 1).astype(BF16)
    grad_router = dot_tn(inputs1, d_logits)

    core = lax.axis_index("dp")
    part = model_width // (nc * nd)

    def scatter_experts(grad):
        blocks = grad.reshape(EXP_DEV, nc, nd, part, -1)
        mine = cube_scatter(
            [lax.dynamic_index_in_dim(blocks, core ^ r, 2, keepdims=False) for r in range(nd)],
            "dp",
            axis_masks("dp"),
        )
        return line_scatter(
            lambda j: lax.dynamic_index_in_dim(mine, j, 1, keepdims=False), "context"
        )

    sum_gate_up = scatter_experts(grad_gate_up)
    sum_down = jnp.swapaxes(scatter_experts(grad_down), 1, 2)

    cotangent = d_out[0].astype(F32)
    scaled2 = d_expert_in * gain_second
    d_hidden = (
        cotangent
        + scale2 * scaled2
        - hidden * (scale2 * scale2 * scale2) * jnp.mean(scaled2 * hidden, -1, keepdims=True)
    )
    grad_gain_second = jnp.sum(d_expert_in * hidden * scale2, 0)
    d_attn = d_hidden.astype(BF16)
    grad_out_turned = dot_tn(d_attn, heads)
    sum_out = scatter_rows(grad_out_turned).T
    d_heads = dot_nn(d_attn, out_turned).astype(BF16)
    d_query, d_key_all, d_value_all = attend_backward(first, query, key_value, d_heads)
    d_key_value_all = jnp.concatenate([d_key_all, d_value_all], -1).reshape(nc, tokens, -1)
    d_key_value = line_scatter(
        lambda j: lax.dynamic_index_in_dim(d_key_value_all, j, 0, keepdims=False),
        "context",
        up=False,
    )
    d_rotated = rotate_back(
        jnp.concatenate([d_query, d_key_value[:, :key_width]], -1).reshape(
            tokens, -1, HEAD_DIMENSION
        ),
        cosine_values,
        sine_values,
    ).reshape(tokens, -1)
    d_qkv = jnp.concatenate([d_rotated, d_key_value[:, key_width:]], -1).astype(BF16)
    d_inputs = dot_nt(d_qkv, qkv_weight) + dot_nt(d_logits, router_weight)
    grad_gain_first = jnp.sum(d_inputs * token_rows * scale1, 0)
    grad_qkv = dot_tn(inputs1, d_qkv)
    small_grads = jnp.concatenate(
        [grad_router, grad_gain_first[:, None], grad_gain_second[:, None]], -1
    )
    small_grads = jnp.pad(small_grads, ((0, 0), (0, 128 - small_grads.shape[1])))
    sum_rows = scatter_rows(jnp.concatenate([grad_qkv, small_grads], -1))
    sum_qkv = sum_rows[:, :qkv_width]
    sum_router = sum_rows[:, qkv_width : qkv_width + expert_total]
    sum_gain_first = sum_rows[:, qkv_width + expert_total]
    sum_gain_second = sum_rows[:, qkv_width + expert_total + 1]
    scaled1 = d_inputs * gain_first
    d_input_rows = (
        d_hidden
        + scale1 * scaled1
        - token_rows
        * (scale1 * scale1 * scale1)
        * jnp.mean(scaled1 * token_rows, -1, keepdims=True)
    ).astype(BF16)
    return (
        layer_result[None],
        d_input_rows[None],
        sum_gain_first,
        sum_qkv,
        sum_out,
        sum_router,
        sum_gain_second,
        sum_gate_up,
        sum_down,
    )


def local_fused(
    layer_input,
    gain_attn,
    query_key_value_weight,
    w_out,
    w_router,
    gain_ffn,
    w_gate_up,
    w_down,
    routes,
    d_out,
):
    tokens = layer_input.shape[1]
    ne, nc, nd = sizes = tuple(lax.axis_size(a) for a in ("expert", "context", "dp"))
    expert_total = EXP_DEV * ne
    first_row = lax.axis_index("context") * tokens
    query_width = QUERY_HEADS * HEAD_DIMENSION
    key_width = KEY_VALUE_HEADS * HEAD_DIMENSION
    qkv_width = query_width + 2 * key_width

    small = jnp.concatenate([w_router, gain_attn[:, None], gain_ffn[:, None]], -1)
    small = jnp.pad(small, ((0, 0), (0, SMALL - small.shape[1])))
    cosine_values, sine_values = rope_tables(first_row + jnp.arange(tokens), HEAD_DIMENSION)
    sine_values = sine_values * jnp.where(
        jnp.arange(HEAD_DIMENSION) < HEAD_DIMENSION // 2, -1.0, 1.0
    )
    layer_result, d_x, sum_rows, sum_out, sum_gate_up, sum_down = layer(
        (
            cosine_values,
            sine_values,
            routes[0].T,
            query_key_value_weight,
            small,
            w_out.T,
            layer_input[0],
            d_out[0],
            w_gate_up,
            w_down,
        ),
        sizes,
    )[:6]
    sum_qkv, layer_result, d_x, sum_gate_up, sum_down, sum_out, sum_router, *sum_gains = finish(
        sum_rows, (layer_result, d_x, sum_gate_up, sum_down, sum_out), expert_total
    )
    return (
        layer_result[None],
        d_x[None],
        sum_gains[0][0],
        sum_qkv,
        sum_out.T,
        sum_router.T,
        sum_gains[1][0],
        sum_gate_up,
        jnp.swapaxes(sum_down, 1, 2),
    )


def solution(mesh):
    in_specs = (
        P(("expert", "dp"), "context", None),
        P(("expert", "context", "dp")),
        P(("expert", "context", "dp"), None),
        P(None, ("expert", "context", "dp")),
        P(("expert", "context", "dp"), None),
        P(("expert", "context", "dp")),
        P("expert", None, None),
        P("expert", None, None),
        P(("expert", "dp"), "context", None),
        P(("expert", "dp"), "context", None),
    )
    out_specs = (
        P(("expert", "dp"), "context", None),
        P(("expert", "dp"), "context", None),
        P(("expert", "context", "dp")),
        P(("expert", "context", "dp"), None),
        P(None, ("expert", "context", "dp")),
        P(("expert", "context", "dp"), None),
        P(("expert", "context", "dp")),
        P("expert", ("context", "dp"), None),
        P("expert", None, ("context", "dp")),
    )
    sizes = tuple(mesh.shape[a] for a in ("expert", "context", "dp"))
    local = local_fused if sizes == (4, 4, 2) else local_plain
    return jax.shard_map(local, mesh=mesh, in_specs=in_specs, out_specs=out_specs, check_vma=False)
```

```python
import functools
import math

import jax
import jax.numpy as jnp
from jax import lax
from jax.experimental import pallas as pl
from jax.experimental.pallas import tpu as pltpu
from jax.sharding import PartitionSpec as P

QUERY_HEADS = 12
KEY_VALUE_HEADS = 2
HEAD_DIMENSION = 128
TOP = 4
EXP_DEV = 2

EPSILON = 1e-06
ROPE_BASE = 10000.0
MASKED = -1e30

F32 = jnp.float32
BF16 = jnp.bfloat16


def rope_tables(positions, width):
    halfway = width // 2
    fraction = jnp.arange(halfway, dtype=jnp.float32) * (2.0 / width)
    frequency = jnp.exp(-math.log(ROPE_BASE) * fraction)
    angles = positions.astype(jnp.float32)[:, None] * frequency[None, :]
    cosine_values = jnp.cos(angles)
    sine_values = jnp.sin(angles)
    return (
        jnp.concatenate([cosine_values, cosine_values], -1),
        jnp.concatenate([sine_values, sine_values], -1),
    )


def rotate_half(values, cosine_values, sine_values):
    halfway = values.shape[-1] // 2
    turned = jnp.concatenate([-values[..., halfway:], values[..., :halfway]], -1)
    return values * cosine_values[:, None, :] + turned * sine_values[:, None, :]


def rotate_back(grads, cosine_values, sine_values):
    halfway = grads.shape[-1] // 2
    scaled = grads * sine_values[:, None, :]
    turned = jnp.concatenate([scaled[..., halfway:], -scaled[..., :halfway]], -1)
    return grads * cosine_values[:, None, :] + turned


def dot_nt(a, b):
    return lax.dot_general(a, b, (((1,), (1,)), ((), ())), preferred_element_type=F32)


def dot_tn(a, b):
    return lax.dot_general(a, b, (((0,), (0,)), ((), ())), preferred_element_type=F32)


def dot_nn(a, b):
    return jnp.dot(a, b, preferred_element_type=F32)


def masked_probs(first_row, query, key):
    scores = dot_nt(query, key) * (HEAD_DIMENSION**-0.5)
    rows = first_row + lax.broadcasted_iota(jnp.int32, scores.shape, 0)
    columns = lax.broadcasted_iota(jnp.int32, scores.shape, 1)
    scores = jnp.where(columns <= rows, scores, MASKED)
    expd = jnp.exp(scores - jnp.max(scores, axis=-1, keepdims=True))
    return expd / jnp.sum(expd, axis=-1, keepdims=True)


def attend_forward_kernel(first_ref, query_ref, key_ref, value_ref, heads_ref):
    probs = masked_probs(first_ref[0], query_ref[...], key_ref[...])
    heads_ref[...] = dot_nn(probs.astype(BF16), value_ref[...]).astype(BF16)


def attend_forward(first_row, query, key_value):
    tokens, width = query.shape
    length = key_value.shape[0]
    group = QUERY_HEADS // KEY_VALUE_HEADS
    size = HEAD_DIMENSION
    return pl.pallas_call(
        attend_forward_kernel,
        grid_spec=pltpu.PrefetchScalarGridSpec(
            num_scalar_prefetch=1,
            grid=(QUERY_HEADS,),
            in_specs=[
                pl.BlockSpec((tokens, size), lambda h, s: (0, h)),
                pl.BlockSpec((length, size), lambda h, s: (0, h // group)),
                pl.BlockSpec((length, size), lambda h, s: (0, KEY_VALUE_HEADS + h // group)),
            ],
            out_specs=pl.BlockSpec((tokens, size), lambda h, s: (0, h)),
        ),
        out_shape=jax.ShapeDtypeStruct((tokens, width), BF16),
        compiler_params=pltpu.CompilerParams(vmem_limit_bytes=32 * 1024 * 1024),
        cost_estimate=pl.CostEstimate(
            flops=4 * tokens * length * width, bytes_accessed=4 * tokens * width, transcendentals=0
        ),
    )(first_row, query, key_value, key_value)


def attend_backward_kernel(
    first_ref, query_ref, key_ref, value_ref, grad_ref, d_query_ref, d_key_ref, d_value_ref
):
    query, key, value, grad = query_ref[...], key_ref[...], value_ref[...], grad_ref[...]
    probs = masked_probs(first_ref[0], query, key)
    d_probs = dot_nt(grad, value)
    inner = jnp.sum(probs * d_probs, axis=-1, keepdims=True)
    d_raw = (probs * (d_probs - inner) * (HEAD_DIMENSION**-0.5)).astype(BF16)
    d_query_ref[...] = dot_nn(d_raw, key)
    d_key = dot_tn(d_raw, query)
    d_value = dot_tn(probs.astype(BF16), grad)

    @pl.when(pl.program_id(1) == 0)
    def _():
        d_key_ref[...] = d_key
        d_value_ref[...] = d_value

    @pl.when(pl.program_id(1) > 0)
    def _():
        d_key_ref[...] += d_key
        d_value_ref[...] += d_value


def attend_backward(first_row, query, key_value, grad):
    tokens, width = query.shape
    length = key_value.shape[0]
    group = QUERY_HEADS // KEY_VALUE_HEADS
    size = HEAD_DIMENSION
    row_spec = pl.BlockSpec((tokens, size), lambda j, g, s: (0, j * group + g))
    return pl.pallas_call(
        attend_backward_kernel,
        grid_spec=pltpu.PrefetchScalarGridSpec(
            num_scalar_prefetch=1,
            grid=(KEY_VALUE_HEADS, group),
            in_specs=[
                row_spec,
                pl.BlockSpec((length, size), lambda j, g, s: (0, j)),
                pl.BlockSpec((length, size), lambda j, g, s: (0, KEY_VALUE_HEADS + j)),
                row_spec,
            ],
            out_specs=[
                row_spec,
                pl.BlockSpec((length, size), lambda j, g, s: (0, j)),
                pl.BlockSpec((length, size), lambda j, g, s: (0, j)),
            ],
        ),
        out_shape=[
            jax.ShapeDtypeStruct((tokens, width), F32),
            jax.ShapeDtypeStruct((length, KEY_VALUE_HEADS * size), F32),
            jax.ShapeDtypeStruct((length, KEY_VALUE_HEADS * size), F32),
        ],
        compiler_params=pltpu.CompilerParams(vmem_limit_bytes=32 * 1024 * 1024),
        cost_estimate=pl.CostEstimate(
            flops=10 * tokens * length * width, bytes_accessed=8 * tokens * width, transcendentals=0
        ),
    )(first_row, query, key_value, key_value, grad)


def exchange(values, axis, mask):
    size = lax.axis_size(axis)
    return lax.ppermute(values, axis, [(i, i ^ mask) for i in range(size)])


def axis_masks(axis):
    size = lax.axis_size(axis)
    masks, bit = [], 1
    while bit < size:
        masks.append(bit)
        bit *= 2
    return masks


def cube_gather(values, axis, masks):
    held = {0: values}
    for mask in masks:
        for r, block in list(held.items()):
            held[r ^ mask] = exchange(block, axis, mask)
    return [held[r] for r in range(lax.axis_size(axis))]


def cube_scatter(blocks, axis, masks):
    held = dict(enumerate(blocks))
    for mask in masks:
        kept = {}
        for r in list(held):
            if not r & mask:
                arrived = exchange(held[r ^ mask].astype(BF16), axis, mask)
                kept[r] = held[r].astype(F32) + arrived.astype(F32)
        held = kept
    return held[0]


def line_steps(values, axis, up):
    size = lax.axis_size(axis)
    pairs = [(i, i + 1) if up else (i + 1, i) for i in range(size - 1)]
    return lax.ppermute(values, axis, pairs)


def line_gather(values, axis, both=True):
    size = lax.axis_size(axis)
    me = lax.axis_index(axis)
    result = jnp.zeros((size + 1,) + values.shape, values.dtype)
    result = lax.dynamic_update_index_in_dim(result, values, me, 0)
    up = down = values
    for step in range(1, size):
        up = line_steps(up, axis, True)
        result = lax.dynamic_update_index_in_dim(
            result, up, jnp.where(me - step >= 0, me - step, size), 0
        )
        if both:
            down = line_steps(down, axis, False)
            result = lax.dynamic_update_index_in_dim(result, down, jnp.minimum(me + step, size), 0)
    return result[:size]


def line_scatter(take, axis, up=True, down=True):
    size = lax.axis_size(axis)
    me = lax.axis_index(axis)
    total = take(me).astype(F32)
    for active, sign in ((up, 1), (down, -1)):
        if not active:
            continue
        arrived = None
        for step in range(1, size):
            block = take((me + sign * (size - step)) % size).astype(F32)
            if arrived is not None:
                block = block + arrived.astype(F32)
            arrived = line_steps(block.astype(BF16), axis, sign > 0)
        total = total + arrived.astype(F32)
    return total


def gather_rows(shard):
    ne, nc, nd = (lax.axis_size(a) for a in ("expert", "context", "dp"))
    rows, width = shard.shape
    lines = line_gather(shard, "context")
    masks = axis_masks("expert")
    half = width // 256 * 128
    parts = [lines[..., :half], lines[..., half:]]
    me = lax.axis_index("expert")
    result = jnp.zeros((ne, nc, rows, width), shard.dtype)
    for start, part, order in ((0, parts[0], masks), (half, parts[1], masks[::-1])):
        for r, block in enumerate(cube_gather(part, "expert", order)):
            result = lax.dynamic_update_slice(result, block[None], (me ^ r, 0, 0, start))
    core = lax.axis_index("dp")
    whole = jnp.zeros((ne, nc, nd, rows, width), shard.dtype)
    for r, block in enumerate(cube_gather(result, "dp", axis_masks("dp"))):
        whole = lax.dynamic_update_slice(whole, block[:, :, None], (0, 0, core ^ r, 0, 0))
    return whole.reshape(-1, width)


def scatter_rows(grad):
    ne, nc, nd = (lax.axis_size(a) for a in ("expert", "context", "dp"))
    width = grad.shape[-1]
    rows = grad.shape[0] // (ne * nc * nd)
    blocks = grad.reshape(ne, nc, nd, rows, width)
    core, me = lax.axis_index("dp"), lax.axis_index("expert")
    mine = cube_scatter(
        [
            lax.dynamic_index_in_dim(blocks, core ^ r, 2, keepdims=False)
            for r in range(nd)
        ],
        "dp",
        axis_masks("dp"),
    )
    masks = axis_masks("expert")
    half = width // 256 * 128
    sums = []
    for part, order in ((mine[..., :half], masks), (mine[..., half:], masks[::-1])):
        sums.append(
            cube_scatter(
                [lax.dynamic_index_in_dim(part, me ^ r, 0, keepdims=False) for r in range(ne)],
                "expert",
                order,
            )
        )
    lines = jnp.concatenate(sums, -1)
    return line_scatter(
        lambda j: lax.dynamic_index_in_dim(lines, j, 0, keepdims=False), "context"
    )


def plane_gather(rows):
    masks = axis_masks("expert")
    half = rows.shape[-1] // 2
    left = cube_gather(rows[:, :half], "expert", masks)
    right = cube_gather(rows[:, half:], "expert", masks[::-1])
    return jnp.concatenate([jnp.concatenate(p, -1) for p in zip(left, right)], 0)


def plane_scatter(partial, tokens):
    masks = axis_masks("expert")
    size = lax.axis_size("expert")
    half = partial.shape[-1] // 2
    blocks = partial.reshape(size, tokens, -1)
    left = cube_scatter([blocks[r, :, :half] for r in range(size)], "expert", masks)
    right = cube_scatter([blocks[r, :, half:] for r in range(size)], "expert", masks[::-1])
    return jnp.concatenate([left, right], -1)


MESH = pl.DeviceIdType.MESH
MIB = 1024 * 1024
SMALL = 128
GATE_ROWS = 16


def flip(index, mask):
    bit = 1
    while bit <= mask:
        if mask & bit:
            index = index + bit - 2 * bit * lax.rem(lax.div(index, bit), 2)
        bit *= 2
    return index


class Wire:
    def __init__(self, sends, recvs):
        self.sends, self.recvs = sends, recvs
        self.n_sends = self.n_recvs = 0
        self.open = []

    def slots(self, count):
        first = self.n_recvs
        self.n_recvs += count
        return first

    def start(self, src, dst, recv, device, when=None):
        number = self.n_sends
        self.n_sends += 1

        def copy():
            return pltpu.make_async_remote_copy(
                src_ref=src() if callable(src) else src,
                dst_ref=dst() if callable(dst) else dst,
                send_sem=self.sends.at[number],
                recv_sem=self.recvs.at[recv],
                device_id=device,
                device_id_type=MESH,
            )

        guard(when, lambda: copy().start())
        self.open.append((when, copy))

    def arrived(self, dst, recv, device):
        pltpu.make_async_remote_copy(
            src_ref=dst,
            dst_ref=dst,
            send_sem=self.sends.at[0],
            recv_sem=self.recvs.at[recv],
            device_id=device,
            device_id_type=MESH,
        ).wait_recv()

    def finish(self):
        for when, copy in self.open:
            guard(when, lambda copy=copy: copy().wait_send())
        self.open = []


def guard(when, action):
    if when is None:
        action()
    else:
        pl.when(when)(action)


def add_into(dest, source, steps=4):
    rows = dest.shape[0] // steps

    @pl.loop(0, steps)
    def _(n):
        here = pl.ds(pl.multiple_of(n * rows, rows), rows)
        dest[here] = (dest[here].astype(F32) + source[here].astype(F32)).astype(BF16)


def greet(targets):
    barrier = pltpu.get_barrier_semaphore()
    for device, when in targets:
        guard(
            when,
            lambda device=device: pl.semaphore_signal(
                barrier, inc=1, device_id=device, device_id_type=MESH
            ),
        )
    count = sum(1 if when is None else when.astype(jnp.int32) for _, when in targets)
    pl.semaphore_wait(barrier, count)


def plane_ids(e):
    return {m: {"expert": flip(e, m)} for m in (1, 2, 3)}


class RowsGather:
    def __init__(self, wire, ref, e, z, c, nc, half):
        self.wire, self.ref, self.e, self.z, self.c, self.nc = wire, ref, e, z, c, nc
        self.cols = (pl.ds(0, half), pl.ds(half, ref.shape[-1] - half))
        self.line = wire.slots(nc)
        self.plane = wire.slots(nc * 6)
        self.core = wire.slots(nc)
        self.ids = plane_ids(e)

    def go(self, *steps):
        for step in steps:
            action = {"l": self.pass_on, "s": self.spread, "f": self.forward, "h": self.share, "c": self.complete}
            action[step[0]](*map(int, step[1:]))

    def shard(self, k):
        if k < 2:
            return flip(self.z, k)
        inner = (self.z > 0) & (self.z < self.nc - 1)
        return jnp.where(inner, flip(self.z, 5 - k), flip(self.z, k))

    def at(self, r, zs, half):
        return self.ref.at[flip(self.e, r), zs, self.c, :, self.cols[half]]

    def slot(self, k, r, half):
        return self.plane + k * 6 + (r - 1) * 2 + half

    def pass_on(self, k):
        z, nc = self.z, self.nc
        zs = self.shard(k)
        whole = self.ref.at[self.e, zs, self.c]
        if k:
            self.wire.arrived(whole, self.line + zs, {"context": zs})
            return
        for d in range(nc - 1, 0, -1):
            for near, wanted in ((z + d, z + d < nc), (z - d, z >= d)):
                self.wire.start(whole, whole, self.line + z, {"context": near}, when=wanted)

    def spread(self, k):
        zs = self.shard(k)
        for half, mask in ((0, 1), (1, 2), (1, 1), (0, 2)):
            part = self.at(0, zs, half)
            self.wire.start(part, part, self.slot(k, mask, half), self.ids[mask])

    def forward(self, k):
        zs = self.shard(k)
        for half, mask in ((0, 1), (1, 2)):
            part = self.at(mask, zs, half)
            self.wire.arrived(part, self.slot(k, mask, half), self.ids[mask])
            self.wire.start(part, part, self.slot(k, 3, half), self.ids[3 - mask])

    def share(self, k):
        zs = self.shard(k)
        for r, half in ((1, 1), (2, 0), (3, 0), (3, 1)):
            self.wire.arrived(self.at(r, zs, half), self.slot(k, r, half), self.ids[r])
        part = self.ref.at[:, zs, self.c]
        self.wire.start(part, part, self.core + k, {"dp": 1 - self.c})

    def complete(self):
        for k in range(self.nc):
            zs = self.shard(k)
            self.wire.arrived(self.ref.at[:, zs, 1 - self.c], self.core + k, {"dp": 1 - self.c})


class PlaneGather:
    def __init__(self, wire, ref, e, own=None):
        self.wire, self.ref, self.own = wire, ref, own
        self.half = ref.shape[-1] // 2
        self.ids = plane_ids(e)
        self.first = wire.slots(6)

    def at(self, r, half):
        columns = pl.ds(half * self.half, self.half)
        if r == 0 and self.own is not None:
            return self.own.at[:, columns]
        return self.ref.at[r, :, columns]

    def slot(self, r, half):
        return self.first + (r - 1) * 2 + half

    def send(self, r, half, to, mask):
        self.wire.start(
            lambda: self.at(r, half), lambda: self.at(to, half), self.slot(to, half), self.ids[mask]
        )

    def spread(self):
        for half, mask in ((0, 1), (1, 2), (1, 1), (0, 2)):
            self.send(0, half, mask, mask)

    def forward(self):
        for half, mask in ((0, 1), (1, 2)):
            self.wire.arrived(self.at(mask, half), self.slot(mask, half), self.ids[mask])
            self.send(mask, half, 3, 3 - mask)

    def near(self, r):
        half = 1 if r == 1 else 0
        self.wire.arrived(self.at(r, half), self.slot(r, half), self.ids[r])

    def far(self):
        for half in (0, 1):
            self.wire.arrived(self.at(3, half), self.slot(3, half), self.ids[3])

    def complete(self):
        self.near(1)
        self.near(2)
        self.far()


def causal(scores, first_row):
    place = lax.broadcasted_iota(jnp.int32, scores.shape, 0)
    row = first_row + lax.broadcasted_iota(jnp.int32, scores.shape, 1)
    return jnp.where(place <= row, scores, MASKED)


def swap_halves(values):
    return pltpu.roll(values, HEAD_DIMENSION // 2, 1)


class PlaneScatter:
    def __init__(self, wire, land, ids):
        self.wire, self.land, self.ids, self.part = wire, land, ids, None
        self.half = land.shape[-1]
        self.first = wire.slots(6)

    def send(self, source, mask, slot):
        self.wire.start(source, lambda: self.land.at[slot], self.first + slot, self.ids[mask])

    def near(self, r):
        self.send(self.part(r, r - 1), r, r - 1)

    def far(self):
        self.send(self.part(3, 0), 1, 2)
        self.send(self.part(3, 1), 2, 3)

    def relay(self, part=None):
        for half, r in ((0, 2), (1, 1)):
            slot = 2 + half
            self.wire.arrived(self.land.at[slot], self.first + slot, self.ids[3 - r])
            take = part or self.part
            mine = take(r, half)
            add_into(mine, self.land.at[slot])
            self.send(lambda r=r, half=half, take=take: take(r, half), r, 4 + half)

    def total(self, own):
        for slot, half, mask in ((0, 0, 1), (1, 1, 2), (4, 0, 2), (5, 1, 1)):
            self.wire.arrived(self.land.at[slot], self.first + slot, self.ids[mask])
            columns = pl.ds(half * self.half, self.half)
            rows = own.shape[0] // 4

            @pl.loop(0, 4)
            def _(n):
                here = pl.ds(pl.multiple_of(n * rows, rows), rows)
                own[here, columns] += self.land[slot, here].astype(F32)


class LineSum:
    def __init__(self, wire, block, land, z, nc, up=True):
        self.wire, self.block, self.land, self.z, self.nc, self.up = wire, block, land, z, nc, up
        self.first = wire.slots(nc)

    def clear(self):
        for slot in range(self.nc):

            def zero(slot=slot):
                self.land[slot] = jnp.zeros(self.land.shape[1:], BF16)

            pl.when(slot == self.z if self.up else slot <= self.z)(zero)

    def send(self):
        z = self.z
        for d in range(self.nc - 1, 0, -1):
            self.leave(z - d, z >= d)
            if self.up:
                self.leave(z + d, z + d < self.nc)

    def leave(self, j, wanted):
        self.wire.start(
            self.block(j), self.land.at[self.z], self.first + self.z, {"context": j}, when=wanted
        )

    def total(self):
        z = self.z
        for d in range(1, self.nc):
            for source, wanted in ((z + d, z + d < self.nc), (z - d, z >= d))[: 1 + self.up]:

                def wait(source=source):
                    self.wire.arrived(
                        self.land.at[source], self.first + source, {"context": source}
                    )

                pl.when(wanted)(wait)
        total = self.block(z)[...].astype(F32)
        for slot in range(self.nc):
            total = total + self.land[slot].astype(F32)
        return total


class RowsScatter:
    def __init__(self, wire, buf, core, plane, lines, e, z, c, nc, start, width, half):
        self.wire, self.buf, self.core, self.plane = wire, buf, core, plane
        self.e, self.c = e, c
        self.all = pl.ds(start, width)
        self.cols = (pl.ds(start, half), pl.ds(start + half, width - half))
        self.ids = plane_ids(e)
        self.core_slot = wire.slots(1)
        self.first = wire.slots(6)
        rows = buf.shape[2] // nc
        self.line = LineSum(
            wire,
            lambda j: buf.at[c, e, pl.ds(pl.multiple_of(j * rows, rows), rows), self.all],
            lines,
            z,
            nc,
        )

    def share(self):
        self.wire.start(
            self.buf.at[1 - self.c, :, :, self.all], self.core, self.core_slot, {"dp": 1 - self.c}
        )

    def at(self, r, half):
        return self.buf.at[self.c, flip(self.e, r), :, self.cols[half]]

    def send(self, r, half, mask, slot):
        self.wire.start(
            self.at(r, half), self.plane(slot, half), self.first + slot, self.ids[mask]
        )

    def merge(self, before=None):
        self.wire.arrived(self.core, self.core_slot, {"dp": 1 - self.c})
        for r in (3, 1, 2, 0):
            block = flip(self.e, r)
            part = self.buf.at[self.c, block, :, self.all]
            add_into(part, self.core.at[block])
            if r == 3:
                if before is not None:
                    before()
                self.send(3, 0, 1, 2)
                self.send(3, 1, 2, 3)
            elif r:
                self.send(r, r - 1, r, r - 1)

    def add(self, r, half, slot, mask):
        land = self.plane(slot, half)
        self.wire.arrived(land, self.first + slot, self.ids[mask])
        add_into(self.at(r, half), land)

    def relay(self):
        for half, r in ((0, 2), (1, 1)):
            self.add(r, half, 2 + half, 3 - r)
            self.send(r, half, r, 4 + half)

    def total(self):
        for slot, half, mask in ((0, 0, 1), (1, 1, 2), (4, 0, 2), (5, 1, 1)):
            self.add(0, half, slot, mask)


class ExpertLine:
    def __init__(self, wire, base, land, sems, z, nc):
        self.wire, self.base, self.land = wire, base, land
        self.ins, self.out, self.sems, self.z, self.nc = None, None, sems, z, nc
        self.end = (z == 0) | (z == nc - 1)
        self.inner = jnp.logical_not(self.end)
        self.width = base.shape[-1] // EXP_DEV
        self.first = wire.slots((nc + 2) * EXP_DEV)
        self.sent = []

    def part(self, ref, j, i):
        return ref.at[j, :, pl.ds(i * self.width, self.width)]

    def combine(self, sources, stores):
        out, step = self.out, self.ins.shape[2]
        count = sources[0].shape[0] // step

        def loads(p):
            rows = pl.ds(p * step, step)
            return [
                pltpu.make_async_copy(source.at[rows], self.ins.at[k, p], self.sems.at[4 * k + p])
                for k, source in enumerate(sources)
            ]

        def store(p):
            pairs = stores(pl.ds(p * step, step), out.at[p % 2])
            return [
                pltpu.make_async_copy(source, dest, self.sems.at[16 + 2 * n + p % 2])
                for n, (source, dest) in enumerate(pairs)
            ]

        for p in range(count):
            for copy in loads(p):
                copy.start()
        for p in range(count):
            for copy in loads(p):
                copy.wait()
            if p > 1:
                for copy in store(p - 2):
                    copy.wait()
            total = self.ins[0, p].astype(F32)
            for k in range(1, len(sources)):
                total = total + self.ins[k, p].astype(F32)
            out[p % 2] = total.astype(out.dtype)
            for copy in store(p):
                copy.start()
        for p in range(max(0, count - 2), count):
            for copy in store(p):
                copy.wait()

    def copy(self, i, r, number):
        target, slot = flip(self.z, r), self.z
        if r > 1:
            target = jnp.where(self.end, flip(self.z, 1), target)
            slot = jnp.where(self.end, self.nc + 3 - r, slot)
        return pltpu.make_async_remote_copy(
            src_ref=self.part(self.base, flip(self.z, r), i),
            dst_ref=self.part(self.land, slot, i),
            send_sem=self.wire.sends.at[number],
            recv_sem=self.wire.recvs.at[self.first + slot * EXP_DEV + i],
            device_id={"context": target},
            device_id_type=MESH,
        )

    def send(self, i, r, when=None):
        number = len(self.sent)
        guard(when, self.copy(i, r, number).start)
        self.sent.append((when, i, r, number))

    def finish(self):
        for when, i, r, number in self.sent:
            guard(when, self.copy(i, r, number).wait_send)

    def arrived(self, slot, i):
        land = self.part(self.land, slot, i)
        self.wire.arrived(land, self.first + slot * EXP_DEV + i, {"context": self.z})

    def relay_loads(self, i, r, p):
        step = self.ins.shape[2]
        rows = pl.ds(p * step, step)
        far = self.nc + r - 2
        sources = (self.part(self.base, flip(self.z, r), i), self.part(self.land, far, i))
        return [
            pltpu.make_async_copy(source.at[rows], self.ins.at[k, p], self.sems.at[4 * k + p])
            for k, source in enumerate(sources)
        ]

    def relay_store(self, i, r, p):
        step = self.ins.shape[2]
        mine = self.part(self.base, flip(self.z, r), i).at[pl.ds(p * step, step)]
        return pltpu.make_async_copy(self.ins.at[0, p], mine, self.sems.at[16 + p])

    def relay_steps(self):
        return range(self.base.shape[1] // self.ins.shape[2])

    def relay_begin(self, i, r):
        def begin():
            self.arrived(self.nc + r - 2, i)
            for p in self.relay_steps():
                for copy in self.relay_loads(i, r, p):
                    copy.start()

        pl.when(self.inner)(begin)

    def relay_add(self, i, r):
        def add():
            for p in self.relay_steps():
                for copy in self.relay_loads(i, r, p):
                    copy.wait()
                a, b = (self.ins[k, p].astype(F32) for k in range(2))
                self.ins[0, p] = (a + b).astype(BF16)
                self.relay_store(i, r, p).start()

        pl.when(self.inner)(add)

    def relay_send(self, i, r):
        def wait():
            for p in self.relay_steps():
                self.relay_store(i, r, p).wait()

        pl.when(self.inner)(wait)
        self.send(i, r, when=self.inner)

    def last(self, i, results):
        z = self.z
        other = jnp.where(self.inner, flip(z, 3), flip(z, 2))
        sources = [self.part(self.base, z, i)]
        for source in (flip(z, 1), other):
            self.arrived(source, i)
            sources.append(self.part(self.land, source, i))

        def stores(rows, wide):
            pairs, first = [], 0
            for result in results:
                columns = pl.ds(first, result.shape[-1])
                pairs.append((wide.at[:, columns], result.at[i, rows]))
                first += result.shape[-1]
            return pairs

        self.combine(sources, stores)


def layer_kernel(
    nc,
    experts,
    cos_ref,
    sin_ref,
    routes_ref,
    qkv_ref,
    small_ref,
    wo_shard_ref,
    x_hbm,
    d_out_hbm,
    w_gu_hbm,
    w_dn_hbm,
    layer_hbm,
    d_x_hbm,
    sum_q_ref,
    sum_o_ref,
    sum_gu_hbm,
    sum_dn_hbm,
    base_hbm,
    land_hbm,
    y_hbm,
    wq_hbm,
    wo_hbm,
    cot_hbm,
    inputs_hbm,
    query_hbm,
    heads_hbm,
    hidden_hbm,
    wk_all,
    kv_ref,
    gate_all,
    gates_ref,
    gains_ref,
    x_all,
    y_land,
    dx_land,
    core_land,
    plane_q,
    plane_k,
    lines_o,
    lines_q,
    lines_k,
    dkv_land,
    d_in_ref,
    dg_lanes,
    dg_part,
    dg_land,
    sends_f,
    recvs_f,
    sends_c,
    recvs_c,
    sends_x,
    recvs_x,
    sends_1,
    recvs_1,
    sends_2,
    recvs_2,
    sends_e,
    recvs_e,
    hand_sends,
    hand_recvs,
    stage_sems,
    load_sems,
    out_sems,
    sum_sems,
    y_sems,
    credits,
):
    e, z, c = (lax.axis_index(a) for a in ("expert", "context", "dp"))
    size = HEAD_DIMENSION
    blocks, tokens, width = cot_hbm.shape
    ff = w_dn_hbm.shape[1]
    query_width = QUERY_HEADS * size
    key_width = KEY_VALUE_HEADS * size
    qkv_width = query_width + 2 * key_width
    rest = wk_all.shape[-1]
    grad_width = base_hbm.shape[-1]
    ids = plane_ids(e)
    sibling = {"dp": 1 - c}
    bottom, even, odd, top = z == 0, lax.rem(z, 2) == 0, lax.rem(z, 2) == 1, z == nc - 1
    wire_1, wire_2, wire_e = Wire(sends_1, recvs_1), Wire(sends_2, recvs_2), Wire(sends_e, recvs_e)
    expert = ExpertLine(wire_e, base_hbm, land_hbm, sum_sems, z, nc)
    wire_c = Wire(sends_c, recvs_c)
    gather_cot = PlaneGather(wire_c, cot_hbm, e, d_out_hbm)
    wire_x = Wire(sends_x, recvs_x)
    gather = PlaneGather(wire_x, x_all, e)
    scatter_dx = PlaneScatter(wire_1, dx_land, ids)
    scatter_y = PlaneScatter(wire_2, y_land, ids)
    dg_slot = wire_1.slots(3)

    def front_phase(wq_ref, wo_ref, x_ref, inputs_ref, query_ref, heads_ref, hidden_ref, kv_scr, q_scr):
        wire = Wire(sends_f, recvs_f)
        kv_width = 2 * key_width
        load_x = pltpu.make_async_copy(x_hbm, x_ref, load_sems.at[0])
        load_x.start()
        wq_ref[e, z, c] = qkv_ref[:, pl.ds(0, query_width)]
        wo_ref[e, z, c] = wo_shard_ref[...]
        wk_all[e, z, c, :, pl.ds(0, kv_width)] = qkv_ref[:, pl.ds(query_width, kv_width)]
        wk_all[e, z, c, :, pl.ds(kv_width, SMALL)] = small_ref[...]
        greet(
            [(ids[m], None) for m in (1, 2, 3)]
            + [(sibling, None)]
            + [({"context": z + d}, z + d < nc) for d in range(1, nc)]
            + [({"context": z - d}, z >= d) for d in range(1, nc)]
        )
        gather_k = RowsGather(wire, wk_all, e, z, c, nc, 256)
        gather_q = RowsGather(wire, wq_ref, e, z, c, nc, 768)
        gather_o = RowsGather(wire, wo_ref, e, z, c, nc, 768)
        gather_k.go("l0")
        gather_q.go("l0")
        gather_k.go("s0")
        gather_q.go("s0")
        gather_k.go("l1", "s1", "f0", "l2", "s2", "f1", "h0", "l3", "s3")
        gather_o.go("l0")
        gather_k.go("f2", "h1", "f3")
        gather_q.go("l1", "s1", "f0")
        gather_k.go("h2", "h3")
        gather_q.go("l2", "s2")
        gather_k.go("c")
        load_x.wait()
        rows = x_ref[...].astype(F32)
        scale1 = lax.rsqrt(jnp.mean(rows * rows, -1, keepdims=True) + EPSILON)

        small = wk_all[:, :, :, :, pl.ds(kv_width, SMALL)].reshape(width, SMALL)
        small = jnp.transpose(small.astype(F32))
        gain_first, gain_second = small[experts : experts + 1], small[experts + 1 : experts + 2]
        gains_ref[0:1] = gain_first
        gains_ref[1:2] = gain_second
        inputs_ref[...] = (rows * scale1 * gain_first).astype(BF16)
        kv_scr[...] = dot_nn(inputs_ref[...], wk_all[...].reshape(width, kv_width + SMALL))

        def turned(head):
            return (head * cos_ref[...] + swap_halves(head) * sin_ref[...]).astype(BF16)

        line = wire.slots(KEY_VALUE_HEADS * nc)
        for j in range(KEY_VALUE_HEADS):
            kv_ref[j, z, :, pl.ds(0, size)] = turned(kv_scr[:, pl.ds(j * size, size)])
            value = kv_scr[:, pl.ds(kv_width // 2 + j * size, size)]
            kv_ref[j, z, :, pl.ds(size, size)] = value.astype(BF16)
            mine = kv_ref.at[j, z]
            for d in range(nc - 1, 0, -1):
                wire.start(mine, mine, line + j * nc + z, {"context": z + d}, when=z + d < nc)

        def keys_here(j):
            for d in range(1, nc):

                def wait(d=d):
                    wire.arrived(kv_ref.at[j, z - d], line + j * nc + z - d, {"context": z - d})

                pl.when(z >= d)(wait)

        outs = [
            pltpu.make_async_copy(source, dest, out_sems.at[n])
            for n, (source, dest) in enumerate(
                (
                    (inputs_ref, inputs_hbm),
                    (query_ref, query_hbm),
                    (heads_ref, heads_hbm),
                    (hidden_ref, hidden_hbm),
                    (wq_ref, wq_hbm),
                    (wo_ref, wo_hbm),
                )
            )
        ]
        outs[0].start()
        for later in range(1, nc):

            def clear(later=later):
                for j in range(KEY_VALUE_HEADS):
                    kv_ref[j, z + later] = jnp.zeros(kv_ref.shape[2:], BF16)

            pl.when(z + later < nc)(clear)
        gather_q.go("l3", "s3", "f1", "f2", "h0")
        gather_o.go("s0")
        gather_q.go("f3", "h1")
        gather_o.go("l1", "s1")
        gather_q.go("h2")
        gather_o.go("l2", "s2")
        gather_q.go("h3", "c")
        outs[4].start()
        gather_o.go("f0")

        @pl.loop(0, query_width // 256)
        def _(n):
            columns = pl.ds(pl.multiple_of(n * 256, 256), 256)
            q_scr[:, columns] = dot_nn(
                inputs_ref[...], wq_ref[:, :, :, :, columns].reshape(width, 256)
            )

        gather_o.go("l3", "s3", "f1")

        @pl.loop(0, QUERY_HEADS)
        def _(h):
            columns = pl.ds(pl.multiple_of(h * size, size), size)
            query_ref[:, columns] = turned(q_scr[:, columns])

        outs[1].start()

        logits = kv_scr[:, pl.ds(kv_width, SMALL)]
        lanes = lax.broadcasted_iota(jnp.int32, logits.shape, 1)
        routes = jnp.concatenate(
            [routes_ref[...].astype(F32), jnp.zeros((SMALL - TOP, tokens), F32)], 0
        )
        routes = jnp.transpose(routes).astype(jnp.int32)
        named = lanes == routes[:, 0:1]
        for k in range(1, TOP):
            named = named | (lanes == routes[:, k : k + 1])
        logits = jnp.where(named, logits, MASKED)
        expd = jnp.exp(logits - jnp.max(logits, -1, keepdims=True))
        gates = expd / jnp.sum(expd, -1, keepdims=True)
        gate_all[0] = jnp.transpose(gates)[:GATE_ROWS]
        gate_slot = wire.slots(3)
        for r in (1, 2, 3):
            wire.start(gate_all.at[0], gate_all.at[r], gate_slot + r - 1, ids[r])

        length = nc * tokens
        group = QUERY_HEADS // KEY_VALUE_HEADS

        def attend(first, last):
            j = first // group
            key = kv_ref[j, :, :, pl.ds(0, size)].reshape(length, size)
            value = kv_ref[j, :, :, pl.ds(size, size)].reshape(length, size)
            value_turned = jnp.transpose(value)

            @pl.loop(first, last)
            def _(h):
                column = pl.multiple_of(h * size, size)
                scores = causal(dot_nt(key, query_ref[:, pl.ds(column, size)]), z * tokens)
                largest = jnp.max(scores, 0, keepdims=True)
                expd = jnp.exp((scores - largest) * (size**-0.5))
                total = jnp.sum(expd, 0, keepdims=True)
                mixed = dot_nn(value_turned, expd.astype(BF16)) / total
                heads_ref[:, pl.ds(column, size)] = jnp.transpose(mixed).astype(BF16)

        half = group // 2
        gather_o.go("f2")
        keys_here(0)
        attend(0, half)
        gather_o.go("f3", "h0")
        gather_cot.spread()
        attend(half, group)
        gather_o.go("h1")
        keys_here(1)
        attend(group, group + half)
        gather_o.go("h2", "h3")
        attend(group + half, QUERY_HEADS)
        gather_o.go("c")
        outs[5].start()
        outs[2].start()
        part = width // wo_ref.shape[0]
        for block in range(wo_ref.shape[0]):
            weight = wo_ref[block].reshape(part, width)
            columns = pl.ds(block * part, part)
            hidden_ref[:, columns] = x_ref[:, columns].astype(F32) + dot_nt(heads_ref[...], weight)
        gather_cot.forward()
        hidden = hidden_ref[...]
        scale2 = lax.rsqrt(jnp.mean(hidden * hidden, -1, keepdims=True) + EPSILON)
        x_all[0] = (hidden * scale2 * gains_ref[1:2]).astype(BF16)
        gather.spread()
        outs[3].start()
        for r in (1, 2, 3):
            wire.arrived(gate_all.at[r], gate_slot + r - 1, ids[r])
        for r in range(gate_all.shape[0]):
            zeros = jnp.zeros((SMALL - GATE_ROWS, tokens), F32)
            turned_gates = jnp.transpose(jnp.concatenate([gate_all[r], zeros], 0))
            both = [
                jnp.sum(jnp.where(lanes == e * EXP_DEV + i, turned_gates, 0.0), -1, keepdims=True)
                for i in range(EXP_DEV)
            ]
            gates_ref[r] = jnp.where(lanes == 0, both[0], jnp.where(lanes == 1, both[1], 0.0))
        for copy in outs:
            copy.wait()
        wire.finish()

    def token_phase(w_gu, w_dn, cot_all, a_all, dgu_all, stage, ins, x_turned, cot_turned):
        expert.ins = ins
        scatter_dx.part = lambda r, half: x_all.at[r, :, pl.ds(half * width // 2, width // 2)]
        sources = [
            (w_gu_hbm.at[0], w_gu.at[0]),
            (w_dn_hbm.at[0], w_dn.at[0]),
            (d_out_hbm, cot_all.at[0]),
            (w_gu_hbm.at[1], w_gu.at[1]),
            (w_dn_hbm.at[1], w_dn.at[1]),
            (cot_hbm.at[1:], cot_all.at[1:]),
        ]
        loads = [
            pltpu.make_async_copy(source, dest, load_sems.at[n])
            for n, (source, dest) in enumerate(sources)
        ]
        for copy in loads[:5]:
            copy.start()
        step = 256
        wide = 512
        dg_lanes[...] = jnp.zeros_like(dg_lanes)

        def hidden_units(r, i, count=1):
            lane = lax.broadcasted_iota(jnp.int32, (1, SMALL), 1)
            here = pl.ds(r, count)
            flat = count * tokens

            @pl.loop(0, ff // step)
            def _(f):
                column = pl.multiple_of(f * step, step)
                rows = x_all[here].reshape(flat, width)
                grads = cot_all[here].reshape(flat, width)
                gate_part = dot_nn(rows, w_gu[i, :, pl.ds(column, step)])
                up_part = dot_nn(rows, w_gu[i, :, pl.ds(ff + column, step)])
                raw = dot_nt(grads, w_dn[i, pl.ds(column, step), :])
                gate = gates_ref[here].reshape(flat, SMALL)
                gate = jnp.sum(jnp.where(lane == i, gate, 0.0), -1, keepdims=True)
                sigma = jax.nn.sigmoid(gate_part)
                silu = gate_part * sigma
                act = silu * up_part
                lanes = lax.broadcasted_iota(jnp.int32, (flat, SMALL), 1)
                d_gate = jnp.where(
                    lanes == e * EXP_DEV + i, jnp.sum(act * raw, -1, keepdims=True), 0.0
                )
                dg_lanes[here] += d_gate.reshape(count, tokens, SMALL)

                def put(ref, first, values):
                    values = values.astype(BF16).reshape(count, tokens, step)
                    ref[here, :, pl.ds(pl.multiple_of(first, step), step)] = values

                put(a_all, i * ff + column, act * gate)
                d_act = raw * gate
                d_gate_part = d_act * up_part * sigma * (1.0 + gate_part * (1.0 - sigma))
                put(dgu_all, i * 2 * ff + column, d_gate_part)
                put(dgu_all, i * 2 * ff + ff + column, d_act * silu)

        def turn(rows, turned, r):
            @pl.loop(0, width // wide)
            def _(n):
                columns = pl.ds(pl.multiple_of(n * wide, wide), wide)
                turned[columns, pl.ds(r * tokens, tokens)] = jnp.transpose(rows[r, :, columns])

        def y_copy(r):
            return pltpu.make_async_copy(cot_all.at[r], y_hbm.at[r], out_sems.at[r])

        def outputs(r, count=1):
            here = pl.ds(r, count)
            flat = count * tokens

            @pl.loop(0, width // wide)
            def _(n):
                columns = pl.ds(pl.multiple_of(n * wide, wide), wide)
                low = dgu_all[here].reshape(flat, EXP_DEV * 2 * ff)
                d_rows = dot_nt(low[:, : 2 * ff], w_gu[0, columns, :])
                d_rows += dot_nt(low[:, 2 * ff :], w_gu[1, columns, :])
                weight = w_dn[:, :, columns].reshape(EXP_DEV * ff, wide)
                out = dot_nn(a_all[here].reshape(flat, EXP_DEV * ff), weight).astype(BF16)
                for k in range(count):
                    rows = slice(k * tokens, (k + 1) * tokens)
                    cot_all[r + k, :, columns] = out[rows]
                    if r == 0:
                        d_in_ref[:, columns] = d_rows
                    else:
                        x_all[r + k, :, columns] = d_rows[rows].astype(BF16)

            for k in range(r, r + count):
                y_copy(k).start()
                dg_part[k] = jnp.transpose(dg_lanes[k])[:GATE_ROWS]
                if k:
                    wire_1.start(dg_part.at[k], dg_land.at[k - 1], dg_slot + k - 1, ids[k])

        half_rows = width // nc // 2
        def where(k):
            high = lax.rem(lax.div(z, 2) + 1 + lax.div(k, 2), 2)
            return 2 * high + lax.rem(z + 1 + k, 2)

        def keep(i, k):
            slot = lax.rem(k, 2)
            return pltpu.make_async_copy(
                stage.at[slot, c], expert.part(base_hbm, where(k), i), stage_sems.at[slot]
            )

        def hand(i, k):
            return pltpu.make_async_remote_copy(
                src_ref=stage.at[lax.rem(k, 2), 1 - c],
                dst_ref=core_land.at[k],
                send_sem=hand_sends.at[i * nc + k],
                recv_sem=hand_recvs.at[i * nc + k],
                device_id=sibling,
                device_id_type=MESH,
            )

        def settle(i, k):
            hand(i, k).wait_recv()
            add_into(stage.at[lax.rem(k, 2), c], core_land.at[k])
            keep(i, k).start()

        def clear(i, k):
            keep(i, k).wait()
            hand(i, k).wait_send()

        def leave(i, r):
            if r == 1:
                expert.send(i, r, when=even if i else None)
            elif r == 3 or r == 2 and i == 0:
                expert.send(i, r, when=expert.end)
            elif r == 2:
                expert.send(i, r, when=bottom)

        def weight_grads(i, between=lambda k: None):
            @pl.loop(0, nc)
            def _(k):
                @pl.when(k >= 2)
                def _():
                    clear(i, k - 2)

                for n in (2, 3):

                    @pl.when(k == n)
                    def _(n=n):
                        leave(i, 5 - n)

                rows_at = pl.ds(pl.multiple_of(where(k) * 2 * half_rows, 2 * half_rows), 2 * half_rows)
                for first, rows, grad, start, count in (
                    (0, x_turned[rows_at, :], dgu_all, i * 2 * ff, 2),
                    (2 * ff, cot_turned[rows_at, :], a_all, i * ff, 1),
                ):

                    @pl.loop(0, count)
                    def _(n):
                        column = pl.multiple_of(n * ff, ff)
                        part = grad[:, :, pl.ds(pl.multiple_of(start + column, ff), ff)]
                        result = dot_nn(rows, part.reshape(blocks * tokens, ff)).astype(BF16)
                        stage[lax.rem(k, 2), :, :, pl.ds(pl.multiple_of(first + column, ff), ff)] = (
                            result.reshape(2, half_rows, ff)
                        )

                if i:

                    @pl.when(k == 0)
                    def _():
                        pl.semaphore_wait(credits.at[3], 1)

                hand(i, k).start()

                @pl.when(k >= 1)
                def _():
                    settle(i, k - 1)

                between(k)

        for copy in loads[:3]:
            copy.wait()
        gather_cot.complete()
        loads[5].start()
        for copy in loads[3:5]:
            copy.wait()

        @pl.loop(0, EXP_DEV)
        def _(i):
            hidden_units(0, i)

        gather.forward()
        turn(x_all, x_turned, 0)
        turn(cot_all, cot_turned, 0)
        loads[5].wait()
        for r in range(1, blocks):
            turn(cot_all, cot_turned, r)
        gather.near(1)
        gather.near(2)
        turn(x_all, x_turned, 1)
        turn(x_all, x_turned, 2)
        hidden_units(1, 0, 2)
        gather.far()
        turn(x_all, x_turned, 3)
        hidden_units(3, 0)
        weight_grads(0)
        hidden_units(1, 1, 2)
        clear(0, nc - 2)
        leave(0, 1)
        settle(0, nc - 1)
        pl.semaphore_signal(credits.at[3], inc=1, device_id=sibling, device_id_type=MESH)
        wire_x.finish()
        outputs(1, 2)
        scatter_dx.near(1)
        scatter_dx.near(2)
        hidden_units(3, 1)
        expert.relay_begin(0, 2)
        outputs(3)
        scatter_dx.far()
        clear(0, nc - 1)
        outputs(0)
        expert.relay_add(0, 2)

        def between(k):
            @pl.when(k == 0)
            def _():
                expert.relay_send(0, 2)

            @pl.when(k == 1)
            def _():
                scatter_dx.relay()

            @pl.when(k == 2)
            def _():
                expert.relay_begin(0, 3)

            @pl.when(k == 3)
            def _():
                expert.relay_add(0, 3)

        weight_grads(1, between)
        expert.relay_send(0, 3)
        scatter_dx.total(d_in_ref)
        for r in (1, 2):
            pl.semaphore_signal(credits.at[r], inc=1, device_id=ids[r], device_id_type=MESH)
        settle(1, nc - 1)
        for k in (nc - 2, nc - 1):
            clear(1, k)
        leave(1, 1)
        for r in range(blocks):
            y_copy(r).wait()
        wire_1.finish()
        wire_c.finish()
        pl.semaphore_signal(credits.at[0], inc=1, device_id=sibling, device_id_type=MESH)

    def token_rows_phase(
        weight,
        grads_o,
        grads_q,
        x_ref,
        inputs_ref,
        query_ref,
        heads_ref,
        hidden_ref,
        d_hidden_ref,
        d_attn_ref,
        d_heads_ref,
        d_all_ref,
        rows_ref,
        dkv_acc,
        dkv_ref,
        y_relay,
        ins,
        out_wide,
    ):
        expert.ins, expert.out = ins, out_wide
        cot_ref, d_inputs_ref = d_heads_ref, hidden_ref
        scatter_y.part = lambda r, half: y_hbm.at[r, :, pl.ds(half * width // 2, width // 2)]
        y_loads = [
            pltpu.make_async_copy(scatter_y.part(2 - half, half), y_relay.at[half], y_sems.at[half])
            for half in range(2)
        ]
        for copy in y_loads:
            copy.start()
        planes = grads_o.shape[1]
        part = width // planes
        sources = (
            (hidden_hbm, hidden_ref),
            (d_out_hbm, cot_ref),
            (wo_hbm, weight),
            (heads_hbm, heads_ref),
            (query_hbm, query_ref),
            (x_hbm, x_ref),
            (inputs_hbm, inputs_ref),
        )
        loads = [
            pltpu.make_async_copy(source, dest, load_sems.at[4 + n])
            for n, (source, dest) in enumerate(sources)
        ]
        for copy in loads:
            copy.start()
        for r in (1, 2):
            scatter_y.near(r)
        scatter_y.far()

        def rows_scatter(buf, core, plane, lines, start, count, half):
            return RowsScatter(
                wire_2,
                buf,
                core,
                plane,
                lines,
                e,
                z,
                c,
                nc,
                start,
                count,
                half,
            )

        rows_of = part // 2
        scatter_o = rows_scatter(
            grads_o,
            x_all.at[:, pl.ds(0, rows_of)],
            lambda slot, half: dx_land.at[slot, pl.ds(0, rows_of)],
            lines_o,
            0,
            width,
            width // 2,
        )
        scatter_q = rows_scatter(
            grads_q,
            core_land.at[:, :, pl.ds(0, query_width)],
            lambda slot, half: plane_q.at[slot],
            lines_q,
            0,
            query_width,
            query_width // 2,
        )
        rest_half = rest // 256 * 128
        scatter_k = rows_scatter(
            grads_q,
            core_land.at[:, :, pl.ds(query_width, rest)],
            lambda slot, half: plane_k.at[
                slot, :, pl.ds(0, rest - rest_half if half else rest_half)
            ],
            lines_k,
            query_width,
            rest,
            rest_half,
        )
        scatter_kv = [
            LineSum(wire_2, lambda j, h=h: dkv_ref.at[h, j], dkv_land.at[h], z, nc, up=False)
            for h in range(KEY_VALUE_HEADS)
        ]

        for scatter in (scatter_o, scatter_q, scatter_k):
            scatter.line.clear()
        for line in scatter_kv:
            line.clear()

        loads[0].wait()
        loads[1].wait()
        hidden, d_in = hidden_ref[...], d_in_ref[...]
        scale2 = lax.rsqrt(jnp.mean(hidden * hidden, -1, keepdims=True) + EPSILON)
        scaled = d_in * gains_ref[1:2]
        mean = jnp.mean(scaled * hidden, -1, keepdims=True)
        d_hidden = cot_ref[...].astype(F32) + scale2 * scaled
        d_hidden = d_hidden - hidden * (scale2 * scale2 * scale2 * mean)
        d_hidden_ref[...] = d_hidden
        d_attn_ref[...] = d_hidden.astype(BF16)
        rows_ref[...] = jnp.zeros_like(rows_ref)
        rows_ref[experts + 1 : experts + 2, :] = jnp.sum(d_in * hidden * scale2, 0, keepdims=True)

        loads[2].wait()

        @pl.loop(0, query_width // 256)
        def _(n):
            columns = pl.ds(pl.multiple_of(n * 256, 256), 256)
            out = weight[:, :, :, :, columns].reshape(width, 256)
            d_heads_ref[:, columns] = dot_nn(d_attn_ref[...], out).astype(BF16)

        load_q = pltpu.make_async_copy(wq_hbm, weight, load_sems.at[0])
        load_q.start()
        loads[3].wait()

        def row_grads(buf, left, right, first, count, extra=None):
            @pl.loop(0, planes)
            def _(block):
                columns = pl.ds(pl.multiple_of(block * part, part), part)
                result = dot_tn(left[:, columns], right)
                if extra is not None:
                    result = result + extra(columns)
                result = result.astype(BF16).reshape(nc, 2, part // nc // 2, count)
                for half in range(2):
                    buf[half, block, :, pl.ds(first, count)] = result[:, half].reshape(
                        part // 2, count
                    )

        length = nc * tokens
        group = QUERY_HEADS // KEY_VALUE_HEADS
        loads[4].wait()
        dkv_acc[...] = jnp.zeros_like(dkv_acc)

        def attend(j, first, last):
            key = kv_ref[j, :, :, pl.ds(0, size)].reshape(length, size)
            value = kv_ref[j, :, :, pl.ds(size, size)].reshape(length, size)
            key_turned = jnp.transpose(key)

            @pl.loop(j * group + first, j * group + last)
            def _(h):
                columns = pl.ds(pl.multiple_of(h * size, size), size)
                query, grad = query_ref[:, columns], d_heads_ref[:, columns]
                scores = causal(dot_nt(key, query), z * tokens)
                largest = jnp.max(scores, 0, keepdims=True)
                expd = jnp.exp((scores - largest) * (size**-0.5))
                probs = expd * (1.0 / jnp.sum(expd, 0, keepdims=True))
                d_probs = dot_nt(value, grad)
                inner = jnp.sum(probs * d_probs, 0, keepdims=True)
                d_raw = (probs * (d_probs - inner) * (size**-0.5)).astype(BF16)
                d_query = jnp.transpose(dot_nn(key_turned, d_raw))
                d_query = d_query * cos_ref[...] - swap_halves(d_query) * sin_ref[...]
                d_all_ref[:, columns] = d_query.astype(BF16)
                dkv_acc[j, :, pl.ds(0, size)] += dot_nn(d_raw, query)
                dkv_acc[j, :, pl.ds(size, size)] += dot_nn(probs.astype(BF16), grad)

        def round_kv(j):
            for block in range(nc):
                rows = dkv_acc[j, pl.ds(block * tokens, tokens), :]
                dkv_ref[j, block] = rows.astype(BF16)

        def enter():
            pl.semaphore_wait(credits.at[1], 1)
            pl.semaphore_wait(credits.at[2], 1)

        attend(0, 0, group)
        round_kv(0)
        scatter_kv[0].send()
        attend(1, 0, group)
        round_kv(1)
        scatter_kv[1].send()
        expert.send(1, 2, when=top)
        expert.send(1, 1, when=odd)
        expert.relay_begin(1, 2)
        row_grads(grads_o, d_attn_ref, heads_ref[...], 0, width)
        expert.relay_add(1, 2)
        pl.semaphore_wait(credits.at[0], 1)
        scatter_o.share()
        y_own = pltpu.make_async_copy(y_hbm.at[0], heads_ref, load_sems.at[2])
        y_own.start()
        for copy in y_loads:
            copy.wait()
        scatter_y.relay(lambda r, half: y_relay.at[half])
        expert.relay_send(1, 2)
        scatter_o.merge(enter)

        for copy in loads[5:]:
            copy.wait()
        row_grads(grads_q, inputs_ref, d_all_ref[:, pl.ds(0, query_width)], 0, query_width)
        scatter_q.share()
        scatter_o.relay()
        expert.last(0, (sum_gu_hbm, sum_dn_hbm))
        scatter_q.merge()
        for h in range(KEY_VALUE_HEADS):
            grad = scatter_kv[h].total()
            d_key = grad[:, :size]
            d_key = d_key * cos_ref[...] - swap_halves(d_key) * sin_ref[...]
            d_all_ref[:, pl.ds(query_width + h * size, size)] = d_key.astype(BF16)
            d_all_ref[:, pl.ds(query_width + key_width + h * size, size)] = grad[:, size:].astype(
                BF16
            )
        y_own.wait()
        hidden_ref[...] += heads_ref[...].astype(F32)
        scatter_y.total(hidden_ref)
        heads_ref[...] = hidden_ref[...].astype(BF16)
        layer_out = pltpu.make_async_copy(heads_ref, layer_hbm, out_sems.at[0])
        layer_out.start()

        total = dg_part[0]
        for r in (1, 2, 3):
            wire_1.arrived(dg_land.at[r - 1], dg_slot + r - 1, ids[r])
            total = total + dg_land[r - 1]
        gates = gate_all[0]
        d_logits = gates * (total - jnp.sum(gates * total, 0, keepdims=True))
        d_logits = jnp.concatenate(
            [d_logits, jnp.zeros((SMALL - d_logits.shape[0], tokens), F32)], 0
        )
        d_all_ref[:, pl.ds(qkv_width, SMALL)] = jnp.transpose(d_logits).astype(BF16)

        load_q.wait()

        @pl.loop(0, planes)
        def _(block):
            columns = pl.ds(pl.multiple_of(block * part, part), part)
            rows_q = weight[block].reshape(part, query_width)
            rows_k = wk_all[block].reshape(part, rest)
            d_inputs_ref[:, columns] = dot_nt(
                d_all_ref[:, pl.ds(0, query_width)], rows_q
            ) + dot_nt(d_all_ref[:, pl.ds(query_width, rest)], rows_k)

        rows = x_ref[...].astype(F32)
        scale1 = lax.rsqrt(jnp.mean(rows * rows, -1, keepdims=True) + EPSILON)
        d_inputs = d_inputs_ref[...]
        rows_ref[experts : experts + 1, :] = jnp.sum(d_inputs * rows * scale1, 0, keepdims=True)

        def extra(columns):
            small = jnp.transpose(rows_ref[:, columns])
            return jnp.concatenate([jnp.zeros((part, rest - SMALL), F32), small], 1)

        row_grads(
            grads_q, inputs_ref, d_all_ref[:, pl.ds(query_width, rest)], query_width, rest, extra
        )
        scatter_k.share()
        scatter_o.total()
        scatter_o.line.send()
        expert.relay_begin(1, 3)
        scatter_q.relay()
        expert.relay_add(1, 3)
        scatter_k.merge()
        expert.relay_send(1, 3)
        scaled = d_inputs_ref[...] * gains_ref[0:1]
        rows = x_ref[...].astype(F32)
        scale1 = lax.rsqrt(jnp.mean(rows * rows, -1, keepdims=True) + EPSILON)
        mean = jnp.mean(scaled * rows, -1, keepdims=True)
        d_x = d_hidden_ref[...] + scale1 * scaled - rows * (scale1 * scale1 * scale1 * mean)
        inputs_ref[...] = d_x.astype(BF16)
        d_x_out = pltpu.make_async_copy(inputs_ref, d_x_hbm, out_sems.at[1])
        d_x_out.start()
        scatter_q.total()
        scatter_q.line.send()
        scatter_k.relay()
        scatter_k.total()
        scatter_k.line.send()
        sum_o_ref[...] = scatter_o.line.total()
        expert.last(1, (sum_gu_hbm, sum_dn_hbm))
        sum_q_ref[:, pl.ds(0, query_width)] = scatter_q.line.total()
        sum_q_ref[:, pl.ds(query_width, rest)] = scatter_k.line.total()
        layer_out.wait()
        d_x_out.wait()
        wire_2.finish()
        expert.finish()

    held = EXP_DEV
    weight_shape = wq_hbm.shape
    pl.run_scoped(
        front_phase,
        pltpu.VMEM(weight_shape, BF16),
        pltpu.VMEM(weight_shape, BF16),
        pltpu.VMEM((tokens, width), BF16),
        pltpu.VMEM((tokens, width), BF16),
        pltpu.VMEM((tokens, query_width), BF16),
        pltpu.VMEM((tokens, query_width), BF16),
        pltpu.VMEM((tokens, width), F32),
        pltpu.VMEM((tokens, rest), F32),
        pltpu.VMEM((tokens, query_width), F32),
    )
    shard, step = width // nc // 2, 48
    pl.run_scoped(
        token_phase,
        pltpu.VMEM((held, width, 2 * ff), BF16),
        pltpu.VMEM((held, ff, width), BF16),
        pltpu.VMEM((blocks, tokens, width), BF16),
        pltpu.VMEM((blocks, tokens, held * ff), BF16),
        pltpu.VMEM((blocks, tokens, held * 2 * ff), BF16),
        pltpu.VMEM((2, 2, shard, grad_width // held), BF16),
        pltpu.VMEM((2, shard // step, step, grad_width // held), BF16),
        pltpu.VMEM((width, blocks * tokens), BF16),
        pltpu.VMEM((width, blocks * tokens), BF16),
    )
    rows_half = width // blocks // 2
    pl.run_scoped(
        token_rows_phase,
        pltpu.VMEM(weight_shape, BF16),
        pltpu.VMEM((2, blocks, rows_half, width), BF16),
        pltpu.VMEM((2, blocks, rows_half, qkv_width + SMALL), BF16),
        pltpu.VMEM((tokens, width), BF16),
        pltpu.VMEM((tokens, width), BF16),
        pltpu.VMEM((tokens, query_width), BF16),
        pltpu.VMEM((tokens, query_width), BF16),
        pltpu.VMEM((tokens, width), F32),
        pltpu.VMEM((tokens, width), F32),
        pltpu.VMEM((tokens, width), BF16),
        pltpu.VMEM((tokens, query_width), BF16),
        pltpu.VMEM((tokens, qkv_width + SMALL), BF16),
        pltpu.VMEM((SMALL, width), F32),
        pltpu.VMEM((KEY_VALUE_HEADS, nc * tokens, 2 * size), F32),
        pltpu.VMEM((KEY_VALUE_HEADS, nc, tokens, 2 * size), BF16),
        pltpu.VMEM((2, tokens, width // 2), BF16),
        pltpu.VMEM((4, shard // step, step, grad_width // held), BF16),
        pltpu.VMEM((2, step, grad_width // held), F32),
    )


def layer(operands, sizes):
    ne, nc, nd = sizes
    qkv_shard, x = operands[3], operands[6]
    w_dn = operands[9]
    tokens, width = x.shape
    held, ff = w_dn.shape[0], w_dn.shape[1]
    query_width = QUERY_HEADS * HEAD_DIMENSION
    rows, qkv_width = qkv_shard.shape
    rest = qkv_width - query_width + SMALL
    rest_half = rest // 256 * 128
    shard, grads = width // (nc * nd), held * 3 * ff
    kv_size = 2 * HEAD_DIMENSION
    weight = (ne, nc, nd, rows, query_width)
    shapes = [
        ((tokens, width), BF16),
        ((tokens, width), BF16),
        ((rows, qkv_width + SMALL), F32),
        ((rows, width), F32),
        ((held, shard, 2 * ff), F32),
        ((held, shard, ff), F32),
        ((nc, shard, grads), BF16),
        ((nc + 2, shard, grads), BF16),
        ((ne, tokens, width), BF16),
        (weight, BF16),
        (weight, BF16),
        ((ne, tokens, width), BF16),
        ((tokens, width), BF16),
        ((tokens, query_width), BF16),
        ((tokens, query_width), BF16),
        ((tokens, width), F32),
    ]
    vmem = pl.BlockSpec(memory_space=pltpu.VMEM)
    anywhere = pl.BlockSpec(memory_space=pl.ANY)
    units = nc * held
    sems = [132, 110, 6, 6, 6, 6, 10, 10, 64, 64, 2 * units, (nc + 2) * held, units, units, 2, 12, 6]
    return pl.pallas_call(
        functools.partial(layer_kernel, nc, EXP_DEV * ne),
        out_shape=[jax.ShapeDtypeStruct(*s) for s in shapes],
        in_specs=[vmem] * 6 + [anywhere] * (len(operands) - 6),
        out_specs=[anywhere] * 2 + [vmem] * 2 + [anywhere] * (len(shapes) - 4),
        scratch_shapes=[
            pltpu.VMEM((ne, nc, nd, rows, rest), BF16),
            pltpu.VMEM((KEY_VALUE_HEADS, nc, tokens, kv_size), BF16),
            pltpu.VMEM((ne, GATE_ROWS, tokens), F32),
            pltpu.VMEM((ne, tokens, SMALL), F32),
            pltpu.VMEM((8, width), F32),
            pltpu.VMEM((ne, tokens, width), BF16),
            pltpu.VMEM((6, tokens, width // 2), BF16),
            pltpu.VMEM((6, tokens, width // 2), BF16),
            pltpu.VMEM((nc, shard, grads // held), BF16),
            pltpu.VMEM((6, nc * rows, query_width // 2), BF16),
            pltpu.VMEM((6, nc * rows, rest - rest_half), BF16),
            pltpu.VMEM((nc, rows, width), BF16),
            pltpu.VMEM((nc, rows, query_width), BF16),
            pltpu.VMEM((nc, rows, rest), BF16),
            pltpu.VMEM((KEY_VALUE_HEADS, nc, tokens, kv_size), BF16),
            pltpu.VMEM((tokens, width), F32),
            pltpu.VMEM((ne, tokens, SMALL), F32),
            pltpu.VMEM((ne, GATE_ROWS, tokens), F32),
            pltpu.VMEM((ne - 1, GATE_ROWS, tokens), F32),
        ]
        + [pltpu.SemaphoreType.DMA((count,)) for count in sems]
        + [
            pltpu.SemaphoreType.DMA((20,)),
            pltpu.SemaphoreType.DMA((2,)),
            pltpu.SemaphoreType.REGULAR((4,)),
        ],
        compiler_params=pltpu.CompilerParams(
            collective_id=0, has_side_effects=True, vmem_limit_bytes=63 * MIB
        ),
    )(*operands)


def finish_kernel(experts, *refs):
    sources, dests = refs[:6], refs[6:12]
    router_ref, first_ref, second_ref = refs[12:]
    sum_q = sources[0]
    qkv_width = dests[0].shape[-1]
    dests[0][...] = sum_q[:, pl.ds(0, qkv_width)]
    for source, dest in zip(sources[1:], dests[1:]):
        dest[...] = source[...]
    small = sum_q[:, pl.ds(qkv_width, SMALL)]
    rows = small.shape[0]
    filled = jnp.concatenate([small, jnp.zeros((SMALL - rows, SMALL), F32)], 0)
    turned = jnp.transpose(filled)[:, :rows]
    router_ref[...] = turned[:experts]
    first_ref[...] = turned[experts : experts + 1]
    second_ref[...] = turned[experts + 1 : experts + 2]


def finish(sum_q, others, experts):
    rows, q_width = sum_q.shape
    vmem = pl.BlockSpec(memory_space=pltpu.VMEM)
    shapes = [jax.ShapeDtypeStruct((rows, q_width - SMALL), F32)]
    shapes += [jax.ShapeDtypeStruct(o.shape, o.dtype) for o in others]
    shapes += [jax.ShapeDtypeStruct((count, rows), F32) for count in (experts, 1, 1)]
    return pl.pallas_call(
        functools.partial(finish_kernel, experts),
        out_shape=shapes,
        in_specs=[vmem] * 6,
        out_specs=[vmem] * 9,
        compiler_params=pltpu.CompilerParams(vmem_limit_bytes=60 * MIB),
    )(sum_q, *others)


def local_plain(
    layer_input,
    gain_attn,
    query_key_value_weight,
    w_out,
    w_router,
    gain_ffn,
    w_gate_up,
    w_down,
    routes,
    d_out,
):
    tokens = layer_input.shape[1]
    model_width = layer_input.shape[2]
    ne, nc, nd = (lax.axis_size(a) for a in ("expert", "context", "dp"))
    expert_total = EXP_DEV * ne
    ff = w_down.shape[1]
    me = lax.axis_index("expert")
    first_row = lax.axis_index("context") * tokens
    query_width = QUERY_HEADS * HEAD_DIMENSION
    key_width = KEY_VALUE_HEADS * HEAD_DIMENSION
    qkv_width = query_width + 2 * key_width

    small = jnp.concatenate([w_router, gain_attn[:, None], gain_ffn[:, None]], -1)
    small = jnp.pad(small, ((0, 0), (0, 128 - small.shape[1])))
    gathered = gather_rows(jnp.concatenate([query_key_value_weight, small], -1))
    out_turned = gather_rows(w_out.T)
    qkv_weight = gathered[:, :qkv_width]
    router_weight = gathered[:, qkv_width : qkv_width + expert_total]
    gains = gathered[:, qkv_width + expert_total : qkv_width + expert_total + 2].T.astype(F32)
    gain_first, gain_second = gains[0], gains[1]
    cotangent_all = plane_gather(d_out[0])

    token_rows = layer_input[0].astype(F32)
    scale1 = lax.rsqrt(jnp.mean(token_rows * token_rows, -1, keepdims=True) + EPSILON)
    inputs1 = (token_rows * scale1 * gain_first).astype(BF16)
    query_key_value = dot_nn(inputs1, qkv_weight)
    cosine_values, sine_values = rope_tables(first_row + jnp.arange(tokens), HEAD_DIMENSION)
    rotated = rotate_half(
        query_key_value[:, : query_width + key_width].reshape(tokens, -1, HEAD_DIMENSION),
        cosine_values,
        sine_values,
    ).reshape(tokens, -1)
    query = rotated[:, :query_width].astype(BF16)
    key_value_local = jnp.concatenate(
        [rotated[:, query_width:], query_key_value[:, query_width + key_width :]], -1
    ).astype(BF16)
    key_value = line_gather(key_value_local, "context", both=False).reshape(nc * tokens, -1)
    first = first_row.astype(jnp.int32).reshape(1)
    heads = attend_forward(first, query, key_value)

    logits = dot_nn(inputs1, router_weight)
    chosen_ids = routes[0]
    picks = (chosen_ids[:, :, None] == jnp.arange(expert_total)[None, None, :]).astype(F32)
    chosen = jnp.sum(picks * logits[:, None, :], -1)
    gates = jax.nn.softmax(chosen, axis=-1)
    gate_dense = jnp.sum(picks * gates[:, :, None], 1).T
    gate_blocks = cube_gather(gate_dense, "expert", axis_masks("expert"))
    gate_local = jnp.concatenate(
        [lax.dynamic_slice_in_dim(b, me * EXP_DEV, EXP_DEV, 0) for b in gate_blocks], 1
    )

    attn = dot_nt(heads, out_turned)
    hidden = token_rows + attn
    scale2 = lax.rsqrt(jnp.mean(hidden * hidden, -1, keepdims=True) + EPSILON)
    expert_in = (hidden * scale2 * gain_second).astype(BF16)

    rows_all = plane_gather(expert_in)
    gate_up = jnp.einsum("td,edf->etf", rows_all, w_gate_up, preferred_element_type=F32)
    gate_part, up_part = gate_up[..., :ff], gate_up[..., ff:]
    sigma = jax.nn.sigmoid(gate_part)
    silu = gate_part * sigma
    act = silu * up_part
    gate_column = gate_local[:, :, None]
    act_gated = (act * gate_column).astype(BF16)
    partial_out = jnp.einsum("etf,efd->td", act_gated, w_down, preferred_element_type=F32)
    mixture = plane_scatter(partial_out.astype(BF16), tokens)
    layer_result = (hidden + mixture).astype(BF16)

    d_act_raw = jnp.einsum("td,efd->etf", cotangent_all, w_down, preferred_element_type=F32)
    d_gates_local = jnp.sum(d_act_raw * act, -1)
    d_act = d_act_raw * gate_column
    d_gate_part = d_act * up_part * sigma * (1.0 + gate_part * (1.0 - sigma))
    d_up_part = d_act * silu
    d_gate_up = jnp.concatenate([d_gate_part, d_up_part], -1).astype(BF16)
    d_rows = jnp.einsum("etf,edf->td", d_gate_up, w_gate_up, preferred_element_type=F32)
    grad_down = jnp.einsum("td,etf->edf", cotangent_all, act_gated, preferred_element_type=F32)
    grad_gate_up = jnp.einsum("td,etf->edf", rows_all, d_gate_up, preferred_element_type=F32)

    d_expert_in = plane_scatter(d_rows.astype(BF16), tokens)
    d_gate_blocks = d_gates_local.reshape(EXP_DEV, ne, tokens)
    d_gates_dense = jnp.zeros((expert_total, tokens), F32)
    for r in range(ne):
        arrived = d_gate_blocks[:, r]
        if r:
            arrived = exchange(arrived, "expert", r)
        d_gates_dense = lax.dynamic_update_slice(d_gates_dense, arrived, ((me ^ r) * EXP_DEV, 0))
    d_gates = jnp.sum(picks * d_gates_dense.T[:, None, :], -1)
    d_chosen = gates * (d_gates - jnp.sum(gates * d_gates, -1, keepdims=True))
    d_logits = jnp.sum(picks * d_chosen[:, :, None], 1).astype(BF16)
    grad_router = dot_tn(inputs1, d_logits)

    core = lax.axis_index("dp")
    part = model_width // (nc * nd)

    def scatter_experts(grad):
        blocks = grad.reshape(EXP_DEV, nc, nd, part, -1)
        mine = cube_scatter(
            [lax.dynamic_index_in_dim(blocks, core ^ r, 2, keepdims=False) for r in range(nd)],
            "dp",
            axis_masks("dp"),
        )
        return line_scatter(
            lambda j: lax.dynamic_index_in_dim(mine, j, 1, keepdims=False), "context"
        )

    sum_gate_up = scatter_experts(grad_gate_up)
    sum_down = jnp.swapaxes(scatter_experts(grad_down), 1, 2)

    cotangent = d_out[0].astype(F32)
    scaled2 = d_expert_in * gain_second
    d_hidden = (
        cotangent
        + scale2 * scaled2
        - hidden * (scale2 * scale2 * scale2) * jnp.mean(scaled2 * hidden, -1, keepdims=True)
    )
    grad_gain_second = jnp.sum(d_expert_in * hidden * scale2, 0)
    d_attn = d_hidden.astype(BF16)
    grad_out_turned = dot_tn(d_attn, heads)
    sum_out = scatter_rows(grad_out_turned).T
    d_heads = dot_nn(d_attn, out_turned).astype(BF16)
    d_query, d_key_all, d_value_all = attend_backward(first, query, key_value, d_heads)
    d_key_value_all = jnp.concatenate([d_key_all, d_value_all], -1).reshape(nc, tokens, -1)
    d_key_value = line_scatter(
        lambda j: lax.dynamic_index_in_dim(d_key_value_all, j, 0, keepdims=False),
        "context",
        up=False,
    )
    d_rotated = rotate_back(
        jnp.concatenate([d_query, d_key_value[:, :key_width]], -1).reshape(
            tokens, -1, HEAD_DIMENSION
        ),
        cosine_values,
        sine_values,
    ).reshape(tokens, -1)
    d_qkv = jnp.concatenate([d_rotated, d_key_value[:, key_width:]], -1).astype(BF16)
    d_inputs = dot_nt(d_qkv, qkv_weight) + dot_nt(d_logits, router_weight)
    grad_gain_first = jnp.sum(d_inputs * token_rows * scale1, 0)
    grad_qkv = dot_tn(inputs1, d_qkv)
    small_grads = jnp.concatenate(
        [grad_router, grad_gain_first[:, None], grad_gain_second[:, None]], -1
    )
    small_grads = jnp.pad(small_grads, ((0, 0), (0, 128 - small_grads.shape[1])))
    sum_rows = scatter_rows(jnp.concatenate([grad_qkv, small_grads], -1))
    sum_qkv = sum_rows[:, :qkv_width]
    sum_router = sum_rows[:, qkv_width : qkv_width + expert_total]
    sum_gain_first = sum_rows[:, qkv_width + expert_total]
    sum_gain_second = sum_rows[:, qkv_width + expert_total + 1]
    scaled1 = d_inputs * gain_first
    d_input_rows = (
        d_hidden
        + scale1 * scaled1
        - token_rows
        * (scale1 * scale1 * scale1)
        * jnp.mean(scaled1 * token_rows, -1, keepdims=True)
    ).astype(BF16)
    return (
        layer_result[None],
        d_input_rows[None],
        sum_gain_first,
        sum_qkv,
        sum_out,
        sum_router,
        sum_gain_second,
        sum_gate_up,
        sum_down,
    )


def local_fused(
    layer_input,
    gain_attn,
    query_key_value_weight,
    w_out,
    w_router,
    gain_ffn,
    w_gate_up,
    w_down,
    routes,
    d_out,
):
    tokens = layer_input.shape[1]
    ne, nc, nd = sizes = tuple(lax.axis_size(a) for a in ("expert", "context", "dp"))
    expert_total = EXP_DEV * ne
    first_row = lax.axis_index("context") * tokens
    query_width = QUERY_HEADS * HEAD_DIMENSION
    key_width = KEY_VALUE_HEADS * HEAD_DIMENSION
    qkv_width = query_width + 2 * key_width

    small = jnp.concatenate([w_router, gain_attn[:, None], gain_ffn[:, None]], -1)
    small = jnp.pad(small, ((0, 0), (0, SMALL - small.shape[1])))
    cosine_values, sine_values = rope_tables(first_row + jnp.arange(tokens), HEAD_DIMENSION)
    sine_values = sine_values * jnp.where(
        jnp.arange(HEAD_DIMENSION) < HEAD_DIMENSION // 2, -1.0, 1.0
    )
    layer_result, d_x, sum_rows, sum_out, sum_gate_up, sum_down = layer(
        (
            cosine_values,
            sine_values,
            routes[0].T,
            query_key_value_weight,
            small,
            w_out.T,
            layer_input[0],
            d_out[0],
            w_gate_up,
            w_down,
        ),
        sizes,
    )[:6]
    sum_qkv, layer_result, d_x, sum_gate_up, sum_down, sum_out, sum_router, *sum_gains = finish(
        sum_rows, (layer_result, d_x, sum_gate_up, sum_down, sum_out), expert_total
    )
    return (
        layer_result[None],
        d_x[None],
        sum_gains[0][0],
        sum_qkv,
        sum_out.T,
        sum_router.T,
        sum_gains[1][0],
        sum_gate_up,
        jnp.swapaxes(sum_down, 1, 2),
    )


def solution(mesh):
    in_specs = (
        P(("expert", "dp"), "context", None),
        P(("expert", "context", "dp")),
        P(("expert", "context", "dp"), None),
        P(None, ("expert", "context", "dp")),
        P(("expert", "context", "dp"), None),
        P(("expert", "context", "dp")),
        P("expert", None, None),
        P("expert", None, None),
        P(("expert", "dp"), "context", None),
        P(("expert", "dp"), "context", None),
    )
    out_specs = (
        P(("expert", "dp"), "context", None),
        P(("expert", "dp"), "context", None),
        P(("expert", "context", "dp")),
        P(("expert", "context", "dp"), None),
        P(None, ("expert", "context", "dp")),
        P(("expert", "context", "dp"), None),
        P(("expert", "context", "dp")),
        P("expert", ("context", "dp"), None),
        P("expert", None, ("context", "dp")),
    )
    sizes = tuple(mesh.shape[a] for a in ("expert", "context", "dp"))
    local = local_fused if sizes == (4, 4, 2) else local_plain
    return jax.shard_map(local, mesh=mesh, in_specs=in_specs, out_specs=out_specs, check_vma=False)
```

```python
import functools
import math

import jax
import jax.numpy as jnp
from jax import lax
from jax.experimental import pallas as pl
from jax.experimental.pallas import tpu as pltpu
from jax.sharding import PartitionSpec as P

QUERY_HEADS = 12
KEY_VALUE_HEADS = 2
HEAD_DIMENSION = 128
TOP = 4
EXP_DEV = 2

EPSILON = 1e-06
ROPE_BASE = 10000.0
MASKED = -1e30

F32 = jnp.float32
BF16 = jnp.bfloat16


def rope_tables(positions, width):
    halfway = width // 2
    fraction = jnp.arange(halfway, dtype=jnp.float32) * (2.0 / width)
    frequency = jnp.exp(-math.log(ROPE_BASE) * fraction)
    angles = positions.astype(jnp.float32)[:, None] * frequency[None, :]
    cosine_values = jnp.cos(angles)
    sine_values = jnp.sin(angles)
    return (
        jnp.concatenate([cosine_values, cosine_values], -1),
        jnp.concatenate([sine_values, sine_values], -1),
    )


def rotate_half(values, cosine_values, sine_values):
    halfway = values.shape[-1] // 2
    turned = jnp.concatenate([-values[..., halfway:], values[..., :halfway]], -1)
    return values * cosine_values[:, None, :] + turned * sine_values[:, None, :]


def rotate_back(grads, cosine_values, sine_values):
    halfway = grads.shape[-1] // 2
    scaled = grads * sine_values[:, None, :]
    turned = jnp.concatenate([scaled[..., halfway:], -scaled[..., :halfway]], -1)
    return grads * cosine_values[:, None, :] + turned


def dot_nt(a, b):
    return lax.dot_general(a, b, (((1,), (1,)), ((), ())), preferred_element_type=F32)


def dot_tn(a, b):
    return lax.dot_general(a, b, (((0,), (0,)), ((), ())), preferred_element_type=F32)


def dot_nn(a, b):
    return jnp.dot(a, b, preferred_element_type=F32)


def masked_probs(first_row, query, key):
    scores = dot_nt(query, key) * (HEAD_DIMENSION**-0.5)
    rows = first_row + lax.broadcasted_iota(jnp.int32, scores.shape, 0)
    columns = lax.broadcasted_iota(jnp.int32, scores.shape, 1)
    scores = jnp.where(columns <= rows, scores, MASKED)
    expd = jnp.exp(scores - jnp.max(scores, axis=-1, keepdims=True))
    return expd / jnp.sum(expd, axis=-1, keepdims=True)


def attend_forward_kernel(first_ref, query_ref, key_ref, value_ref, heads_ref):
    probs = masked_probs(first_ref[0], query_ref[...], key_ref[...])
    heads_ref[...] = dot_nn(probs.astype(BF16), value_ref[...]).astype(BF16)


def attend_forward(first_row, query, key_value):
    tokens, width = query.shape
    length = key_value.shape[0]
    group = QUERY_HEADS // KEY_VALUE_HEADS
    size = HEAD_DIMENSION
    return pl.pallas_call(
        attend_forward_kernel,
        grid_spec=pltpu.PrefetchScalarGridSpec(
            num_scalar_prefetch=1,
            grid=(QUERY_HEADS,),
            in_specs=[
                pl.BlockSpec((tokens, size), lambda h, s: (0, h)),
                pl.BlockSpec((length, size), lambda h, s: (0, h // group)),
                pl.BlockSpec((length, size), lambda h, s: (0, KEY_VALUE_HEADS + h // group)),
            ],
            out_specs=pl.BlockSpec((tokens, size), lambda h, s: (0, h)),
        ),
        out_shape=jax.ShapeDtypeStruct((tokens, width), BF16),
        compiler_params=pltpu.CompilerParams(vmem_limit_bytes=32 * 1024 * 1024),
        cost_estimate=pl.CostEstimate(
            flops=4 * tokens * length * width, bytes_accessed=4 * tokens * width, transcendentals=0
        ),
    )(first_row, query, key_value, key_value)


def attend_backward_kernel(
    first_ref, query_ref, key_ref, value_ref, grad_ref, d_query_ref, d_key_ref, d_value_ref
):
    query, key, value, grad = query_ref[...], key_ref[...], value_ref[...], grad_ref[...]
    probs = masked_probs(first_ref[0], query, key)
    d_probs = dot_nt(grad, value)
    inner = jnp.sum(probs * d_probs, axis=-1, keepdims=True)
    d_raw = (probs * (d_probs - inner) * (HEAD_DIMENSION**-0.5)).astype(BF16)
    d_query_ref[...] = dot_nn(d_raw, key)
    d_key = dot_tn(d_raw, query)
    d_value = dot_tn(probs.astype(BF16), grad)

    @pl.when(pl.program_id(1) == 0)
    def _():
        d_key_ref[...] = d_key
        d_value_ref[...] = d_value

    @pl.when(pl.program_id(1) > 0)
    def _():
        d_key_ref[...] += d_key
        d_value_ref[...] += d_value


def attend_backward(first_row, query, key_value, grad):
    tokens, width = query.shape
    length = key_value.shape[0]
    group = QUERY_HEADS // KEY_VALUE_HEADS
    size = HEAD_DIMENSION
    row_spec = pl.BlockSpec((tokens, size), lambda j, g, s: (0, j * group + g))
    return pl.pallas_call(
        attend_backward_kernel,
        grid_spec=pltpu.PrefetchScalarGridSpec(
            num_scalar_prefetch=1,
            grid=(KEY_VALUE_HEADS, group),
            in_specs=[
                row_spec,
                pl.BlockSpec((length, size), lambda j, g, s: (0, j)),
                pl.BlockSpec((length, size), lambda j, g, s: (0, KEY_VALUE_HEADS + j)),
                row_spec,
            ],
            out_specs=[
                row_spec,
                pl.BlockSpec((length, size), lambda j, g, s: (0, j)),
                pl.BlockSpec((length, size), lambda j, g, s: (0, j)),
            ],
        ),
        out_shape=[
            jax.ShapeDtypeStruct((tokens, width), F32),
            jax.ShapeDtypeStruct((length, KEY_VALUE_HEADS * size), F32),
            jax.ShapeDtypeStruct((length, KEY_VALUE_HEADS * size), F32),
        ],
        compiler_params=pltpu.CompilerParams(vmem_limit_bytes=32 * 1024 * 1024),
        cost_estimate=pl.CostEstimate(
            flops=10 * tokens * length * width, bytes_accessed=8 * tokens * width, transcendentals=0
        ),
    )(first_row, query, key_value, key_value, grad)


def exchange(values, axis, mask):
    size = lax.axis_size(axis)
    return lax.ppermute(values, axis, [(i, i ^ mask) for i in range(size)])


def axis_masks(axis):
    size = lax.axis_size(axis)
    masks, bit = [], 1
    while bit < size:
        masks.append(bit)
        bit *= 2
    return masks


def cube_gather(values, axis, masks):
    held = {0: values}
    for mask in masks:
        for r, block in list(held.items()):
            held[r ^ mask] = exchange(block, axis, mask)
    return [held[r] for r in range(lax.axis_size(axis))]


def cube_scatter(blocks, axis, masks):
    held = dict(enumerate(blocks))
    for mask in masks:
        kept = {}
        for r in list(held):
            if not r & mask:
                arrived = exchange(held[r ^ mask].astype(BF16), axis, mask)
                kept[r] = held[r].astype(F32) + arrived.astype(F32)
        held = kept
    return held[0]


def line_steps(values, axis, up):
    size = lax.axis_size(axis)
    pairs = [(i, i + 1) if up else (i + 1, i) for i in range(size - 1)]
    return lax.ppermute(values, axis, pairs)


def line_gather(values, axis, both=True):
    size = lax.axis_size(axis)
    me = lax.axis_index(axis)
    result = jnp.zeros((size + 1,) + values.shape, values.dtype)
    result = lax.dynamic_update_index_in_dim(result, values, me, 0)
    up = down = values
    for step in range(1, size):
        up = line_steps(up, axis, True)
        result = lax.dynamic_update_index_in_dim(
            result, up, jnp.where(me - step >= 0, me - step, size), 0
        )
        if both:
            down = line_steps(down, axis, False)
            result = lax.dynamic_update_index_in_dim(result, down, jnp.minimum(me + step, size), 0)
    return result[:size]


def line_scatter(take, axis, up=True, down=True):
    size = lax.axis_size(axis)
    me = lax.axis_index(axis)
    total = take(me).astype(F32)
    for active, sign in ((up, 1), (down, -1)):
        if not active:
            continue
        arrived = None
        for step in range(1, size):
            block = take((me + sign * (size - step)) % size).astype(F32)
            if arrived is not None:
                block = block + arrived.astype(F32)
            arrived = line_steps(block.astype(BF16), axis, sign > 0)
        total = total + arrived.astype(F32)
    return total


def gather_rows(shard):
    ne, nc, nd = (lax.axis_size(a) for a in ("expert", "context", "dp"))
    rows, width = shard.shape
    lines = line_gather(shard, "context")
    masks = axis_masks("expert")
    half = width // 256 * 128
    parts = [lines[..., :half], lines[..., half:]]
    me = lax.axis_index("expert")
    result = jnp.zeros((ne, nc, rows, width), shard.dtype)
    for start, part, order in ((0, parts[0], masks), (half, parts[1], masks[::-1])):
        for r, block in enumerate(cube_gather(part, "expert", order)):
            result = lax.dynamic_update_slice(result, block[None], (me ^ r, 0, 0, start))
    core = lax.axis_index("dp")
    whole = jnp.zeros((ne, nc, nd, rows, width), shard.dtype)
    for r, block in enumerate(cube_gather(result, "dp", axis_masks("dp"))):
        whole = lax.dynamic_update_slice(whole, block[:, :, None], (0, 0, core ^ r, 0, 0))
    return whole.reshape(-1, width)


def scatter_rows(grad):
    ne, nc, nd = (lax.axis_size(a) for a in ("expert", "context", "dp"))
    width = grad.shape[-1]
    rows = grad.shape[0] // (ne * nc * nd)
    blocks = grad.reshape(ne, nc, nd, rows, width)
    core, me = lax.axis_index("dp"), lax.axis_index("expert")
    mine = cube_scatter(
        [
            lax.dynamic_index_in_dim(blocks, core ^ r, 2, keepdims=False)
            for r in range(nd)
        ],
        "dp",
        axis_masks("dp"),
    )
    masks = axis_masks("expert")
    half = width // 256 * 128
    sums = []
    for part, order in ((mine[..., :half], masks), (mine[..., half:], masks[::-1])):
        sums.append(
            cube_scatter(
                [lax.dynamic_index_in_dim(part, me ^ r, 0, keepdims=False) for r in range(ne)],
                "expert",
                order,
            )
        )
    lines = jnp.concatenate(sums, -1)
    return line_scatter(
        lambda j: lax.dynamic_index_in_dim(lines, j, 0, keepdims=False), "context"
    )


def plane_gather(rows):
    masks = axis_masks("expert")
    half = rows.shape[-1] // 2
    left = cube_gather(rows[:, :half], "expert", masks)
    right = cube_gather(rows[:, half:], "expert", masks[::-1])
    return jnp.concatenate([jnp.concatenate(p, -1) for p in zip(left, right)], 0)


def plane_scatter(partial, tokens):
    masks = axis_masks("expert")
    size = lax.axis_size("expert")
    half = partial.shape[-1] // 2
    blocks = partial.reshape(size, tokens, -1)
    left = cube_scatter([blocks[r, :, :half] for r in range(size)], "expert", masks)
    right = cube_scatter([blocks[r, :, half:] for r in range(size)], "expert", masks[::-1])
    return jnp.concatenate([left, right], -1)


MESH = pl.DeviceIdType.MESH
MIB = 1024 * 1024
SMALL = 128
GATE_ROWS = 16


def flip(index, mask):
    bit = 1
    while bit <= mask:
        if mask & bit:
            index = index + bit - 2 * bit * lax.rem(lax.div(index, bit), 2)
        bit *= 2
    return index


class Wire:
    def __init__(self, sends, recvs):
        self.sends, self.recvs = sends, recvs
        self.n_sends = self.n_recvs = 0
        self.open = []

    def slots(self, count):
        first = self.n_recvs
        self.n_recvs += count
        return first

    def start(self, src, dst, recv, device, when=None):
        number = self.n_sends
        self.n_sends += 1

        def copy():
            return pltpu.make_async_remote_copy(
                src_ref=src() if callable(src) else src,
                dst_ref=dst() if callable(dst) else dst,
                send_sem=self.sends.at[number],
                recv_sem=self.recvs.at[recv],
                device_id=device,
                device_id_type=MESH,
            )

        guard(when, lambda: copy().start())
        self.open.append((when, copy))

    def arrived(self, dst, recv, device):
        pltpu.make_async_remote_copy(
            src_ref=dst,
            dst_ref=dst,
            send_sem=self.sends.at[0],
            recv_sem=self.recvs.at[recv],
            device_id=device,
            device_id_type=MESH,
        ).wait_recv()

    def finish(self):
        for when, copy in self.open:
            guard(when, lambda copy=copy: copy().wait_send())
        self.open = []


def guard(when, action):
    if when is None:
        action()
    else:
        pl.when(when)(action)


def add_into(dest, source, steps=4):
    rows = dest.shape[0] // steps

    @pl.loop(0, steps)
    def _(n):
        here = pl.ds(pl.multiple_of(n * rows, rows), rows)
        dest[here] = (dest[here].astype(F32) + source[here].astype(F32)).astype(BF16)


def greet(targets):
    barrier = pltpu.get_barrier_semaphore()
    for device, when in targets:
        guard(
            when,
            lambda device=device: pl.semaphore_signal(
                barrier, inc=1, device_id=device, device_id_type=MESH
            ),
        )
    count = sum(1 if when is None else when.astype(jnp.int32) for _, when in targets)
    pl.semaphore_wait(barrier, count)


def plane_ids(e):
    return {m: {"expert": flip(e, m)} for m in (1, 2, 3)}


class RowsGather:
    def __init__(self, wire, ref, e, z, c, nc, half):
        self.wire, self.ref, self.e, self.z, self.c, self.nc = wire, ref, e, z, c, nc
        self.cols = (pl.ds(0, half), pl.ds(half, ref.shape[-1] - half))
        self.line = wire.slots(nc)
        self.plane = wire.slots(nc * 6)
        self.core = wire.slots(nc)
        self.ids = plane_ids(e)

    def go(self, *steps):
        for step in steps:
            action = {"l": self.pass_on, "s": self.spread, "f": self.forward, "h": self.share, "c": self.complete}
            action[step[0]](*map(int, step[1:]))

    def shard(self, k):
        if k < 2:
            return flip(self.z, k)
        inner = (self.z > 0) & (self.z < self.nc - 1)
        return jnp.where(inner, flip(self.z, 5 - k), flip(self.z, k))

    def at(self, r, zs, half):
        return self.ref.at[flip(self.e, r), zs, self.c, :, self.cols[half]]

    def slot(self, k, r, half):
        return self.plane + k * 6 + (r - 1) * 2 + half

    def pass_on(self, k):
        z, nc = self.z, self.nc
        zs = self.shard(k)
        whole = self.ref.at[self.e, zs, self.c]
        if k:
            self.wire.arrived(whole, self.line + zs, {"context": zs})
            return
        for d in range(nc - 1, 0, -1):
            for near, wanted in ((z + d, z + d < nc), (z - d, z >= d)):
                self.wire.start(whole, whole, self.line + z, {"context": near}, when=wanted)

    def spread(self, k):
        zs = self.shard(k)
        for half, mask in ((0, 1), (1, 2), (1, 1), (0, 2)):
            part = self.at(0, zs, half)
            self.wire.start(part, part, self.slot(k, mask, half), self.ids[mask])

    def forward(self, k):
        zs = self.shard(k)
        for half, mask in ((0, 1), (1, 2)):
            part = self.at(mask, zs, half)
            self.wire.arrived(part, self.slot(k, mask, half), self.ids[mask])
            self.wire.start(part, part, self.slot(k, 3, half), self.ids[3 - mask])

    def share(self, k):
        zs = self.shard(k)
        for r, half in ((1, 1), (2, 0), (3, 0), (3, 1)):
            self.wire.arrived(self.at(r, zs, half), self.slot(k, r, half), self.ids[r])
        part = self.ref.at[:, zs, self.c]
        self.wire.start(part, part, self.core + k, {"dp": 1 - self.c})

    def complete(self):
        for k in range(self.nc):
            zs = self.shard(k)
            self.wire.arrived(self.ref.at[:, zs, 1 - self.c], self.core + k, {"dp": 1 - self.c})


class PlaneGather:
    def __init__(self, wire, ref, e, own=None):
        self.wire, self.ref, self.own = wire, ref, own
        self.half = ref.shape[-1] // 2
        self.ids = plane_ids(e)
        self.first = wire.slots(6)

    def at(self, r, half):
        columns = pl.ds(half * self.half, self.half)
        if r == 0 and self.own is not None:
            return self.own.at[:, columns]
        return self.ref.at[r, :, columns]

    def slot(self, r, half):
        return self.first + (r - 1) * 2 + half

    def send(self, r, half, to, mask):
        self.wire.start(
            lambda: self.at(r, half), lambda: self.at(to, half), self.slot(to, half), self.ids[mask]
        )

    def spread(self):
        for half, mask in ((0, 1), (1, 2), (1, 1), (0, 2)):
            self.send(0, half, mask, mask)

    def forward(self):
        for half, mask in ((0, 1), (1, 2)):
            self.wire.arrived(self.at(mask, half), self.slot(mask, half), self.ids[mask])
            self.send(mask, half, 3, 3 - mask)

    def near(self, r):
        half = 1 if r == 1 else 0
        self.wire.arrived(self.at(r, half), self.slot(r, half), self.ids[r])

    def far(self):
        for half in (0, 1):
            self.wire.arrived(self.at(3, half), self.slot(3, half), self.ids[3])

    def complete(self):
        self.near(1)
        self.near(2)
        self.far()


def causal(scores, first_row):
    place = lax.broadcasted_iota(jnp.int32, scores.shape, 0)
    row = first_row + lax.broadcasted_iota(jnp.int32, scores.shape, 1)
    return jnp.where(place <= row, scores, MASKED)


def swap_halves(values):
    return pltpu.roll(values, HEAD_DIMENSION // 2, 1)


class PlaneScatter:
    def __init__(self, wire, land, ids):
        self.wire, self.land, self.ids, self.part = wire, land, ids, None
        self.half = land.shape[-1]
        self.first = wire.slots(6)

    def send(self, source, mask, slot):
        self.wire.start(source, lambda: self.land.at[slot], self.first + slot, self.ids[mask])

    def near(self, r):
        self.send(self.part(r, r - 1), r, r - 1)

    def far(self):
        self.send(self.part(3, 0), 1, 2)
        self.send(self.part(3, 1), 2, 3)

    def relay(self, part=None):
        for half, r in ((0, 2), (1, 1)):
            slot = 2 + half
            self.wire.arrived(self.land.at[slot], self.first + slot, self.ids[3 - r])
            take = part or self.part
            mine = take(r, half)
            add_into(mine, self.land.at[slot])
            self.send(lambda r=r, half=half, take=take: take(r, half), r, 4 + half)

    def total(self, own):
        for slot, half, mask in ((0, 0, 1), (1, 1, 2), (4, 0, 2), (5, 1, 1)):
            self.wire.arrived(self.land.at[slot], self.first + slot, self.ids[mask])
            columns = pl.ds(half * self.half, self.half)
            rows = own.shape[0] // 4

            @pl.loop(0, 4)
            def _(n):
                here = pl.ds(pl.multiple_of(n * rows, rows), rows)
                own[here, columns] += self.land[slot, here].astype(F32)


class LineSum:
    def __init__(self, wire, block, land, z, nc, up=True):
        self.wire, self.block, self.land, self.z, self.nc, self.up = wire, block, land, z, nc, up
        self.first = wire.slots(nc)

    def clear(self):
        for slot in range(self.nc):

            def zero(slot=slot):
                self.land[slot] = jnp.zeros(self.land.shape[1:], BF16)

            pl.when(slot == self.z if self.up else slot <= self.z)(zero)

    def send(self):
        z = self.z
        for d in range(self.nc - 1, 0, -1):
            self.leave(z - d, z >= d)
            if self.up:
                self.leave(z + d, z + d < self.nc)

    def leave(self, j, wanted):
        self.wire.start(
            self.block(j), self.land.at[self.z], self.first + self.z, {"context": j}, when=wanted
        )

    def total(self):
        z = self.z
        for d in range(1, self.nc):
            for source, wanted in ((z + d, z + d < self.nc), (z - d, z >= d))[: 1 + self.up]:

                def wait(source=source):
                    self.wire.arrived(
                        self.land.at[source], self.first + source, {"context": source}
                    )

                pl.when(wanted)(wait)
        total = self.block(z)[...].astype(F32)
        for slot in range(self.nc):
            total = total + self.land[slot].astype(F32)
        return total


class RowsScatter:
    def __init__(self, wire, buf, core, plane, lines, e, z, c, nc, start, width, half):
        self.wire, self.buf, self.core, self.plane = wire, buf, core, plane
        self.e, self.c = e, c
        self.all = pl.ds(start, width)
        self.cols = (pl.ds(start, half), pl.ds(start + half, width - half))
        self.ids = plane_ids(e)
        self.core_slot = wire.slots(1)
        self.first = wire.slots(6)
        rows = buf.shape[2] // nc
        self.line = LineSum(
            wire,
            lambda j: buf.at[c, e, pl.ds(pl.multiple_of(j * rows, rows), rows), self.all],
            lines,
            z,
            nc,
        )

    def share(self):
        self.wire.start(
            self.buf.at[1 - self.c, :, :, self.all], self.core, self.core_slot, {"dp": 1 - self.c}
        )

    def at(self, r, half):
        return self.buf.at[self.c, flip(self.e, r), :, self.cols[half]]

    def send(self, r, half, mask, slot):
        self.wire.start(
            self.at(r, half), self.plane(slot, half), self.first + slot, self.ids[mask]
        )

    def merge(self, before=None):
        self.wire.arrived(self.core, self.core_slot, {"dp": 1 - self.c})
        for r in (3, 1, 2, 0):
            block = flip(self.e, r)
            part = self.buf.at[self.c, block, :, self.all]
            add_into(part, self.core.at[block])
            if r == 3:
                if before is not None:
                    before()
                self.send(3, 0, 1, 2)
                self.send(3, 1, 2, 3)
            elif r:
                self.send(r, r - 1, r, r - 1)

    def add(self, r, half, slot, mask):
        land = self.plane(slot, half)
        self.wire.arrived(land, self.first + slot, self.ids[mask])
        add_into(self.at(r, half), land)

    def relay(self):
        for half, r in ((0, 2), (1, 1)):
            self.add(r, half, 2 + half, 3 - r)
            self.send(r, half, r, 4 + half)

    def total(self):
        for slot, half, mask in ((0, 0, 1), (1, 1, 2), (4, 0, 2), (5, 1, 1)):
            self.add(0, half, slot, mask)


class ExpertLine:
    def __init__(self, wire, base, land, sems, z, nc):
        self.wire, self.base, self.land = wire, base, land
        self.ins, self.out, self.sems, self.z, self.nc = None, None, sems, z, nc
        self.end = (z == 0) | (z == nc - 1)
        self.inner = jnp.logical_not(self.end)
        self.width = base.shape[-1] // EXP_DEV
        self.first = wire.slots((nc + 2) * EXP_DEV)
        self.sent = []

    def part(self, ref, j, i):
        return ref.at[j, :, pl.ds(i * self.width, self.width)]

    def combine(self, sources, stores):
        out, step = self.out, self.ins.shape[2]
        count = sources[0].shape[0] // step

        def loads(p):
            rows = pl.ds(p * step, step)
            return [
                pltpu.make_async_copy(source.at[rows], self.ins.at[k, p], self.sems.at[4 * k + p])
                for k, source in enumerate(sources)
            ]

        def store(p):
            pairs = stores(pl.ds(p * step, step), out.at[p % 2])
            return [
                pltpu.make_async_copy(source, dest, self.sems.at[16 + 2 * n + p % 2])
                for n, (source, dest) in enumerate(pairs)
            ]

        for p in range(count):
            for copy in loads(p):
                copy.start()
        for p in range(count):
            for copy in loads(p):
                copy.wait()
            if p > 1:
                for copy in store(p - 2):
                    copy.wait()
            total = self.ins[0, p].astype(F32)
            for k in range(1, len(sources)):
                total = total + self.ins[k, p].astype(F32)
            out[p % 2] = total.astype(out.dtype)
            for copy in store(p):
                copy.start()
        for p in range(max(0, count - 2), count):
            for copy in store(p):
                copy.wait()

    def copy(self, i, r, number):
        target, slot = flip(self.z, r), self.z
        if r > 1:
            target = jnp.where(self.end, flip(self.z, 1), target)
            slot = jnp.where(self.end, self.nc + 3 - r, slot)
        return pltpu.make_async_remote_copy(
            src_ref=self.part(self.base, flip(self.z, r), i),
            dst_ref=self.part(self.land, slot, i),
            send_sem=self.wire.sends.at[number],
            recv_sem=self.wire.recvs.at[self.first + slot * EXP_DEV + i],
            device_id={"context": target},
            device_id_type=MESH,
        )

    def send(self, i, r, when=None):
        number = len(self.sent)
        guard(when, self.copy(i, r, number).start)
        self.sent.append((when, i, r, number))

    def finish(self):
        for when, i, r, number in self.sent:
            guard(when, self.copy(i, r, number).wait_send)

    def arrived(self, slot, i):
        land = self.part(self.land, slot, i)
        self.wire.arrived(land, self.first + slot * EXP_DEV + i, {"context": self.z})

    def relay_loads(self, i, r, p):
        step = self.ins.shape[2]
        rows = pl.ds(p * step, step)
        far = self.nc + r - 2
        sources = (self.part(self.base, flip(self.z, r), i), self.part(self.land, far, i))
        return [
            pltpu.make_async_copy(source.at[rows], self.ins.at[k, p], self.sems.at[4 * k + p])
            for k, source in enumerate(sources)
        ]

    def relay_store(self, i, r, p):
        step = self.ins.shape[2]
        mine = self.part(self.base, flip(self.z, r), i).at[pl.ds(p * step, step)]
        return pltpu.make_async_copy(self.ins.at[0, p], mine, self.sems.at[16 + p])

    def relay_steps(self):
        return range(self.base.shape[1] // self.ins.shape[2])

    def relay_begin(self, i, r):
        def begin():
            self.arrived(self.nc + r - 2, i)
            for p in self.relay_steps():
                for copy in self.relay_loads(i, r, p):
                    copy.start()

        pl.when(self.inner)(begin)

    def relay_add(self, i, r):
        def add():
            for p in self.relay_steps():
                for copy in self.relay_loads(i, r, p):
                    copy.wait()
                a, b = (self.ins[k, p].astype(F32) for k in range(2))
                self.ins[0, p] = (a + b).astype(BF16)
                self.relay_store(i, r, p).start()

        pl.when(self.inner)(add)

    def relay_send(self, i, r):
        def wait():
            for p in self.relay_steps():
                self.relay_store(i, r, p).wait()

        pl.when(self.inner)(wait)
        self.send(i, r, when=self.inner)

    def last(self, i, results):
        z = self.z
        other = jnp.where(self.inner, flip(z, 3), flip(z, 2))
        sources = [self.part(self.base, z, i)]
        for source in (flip(z, 1), other):
            self.arrived(source, i)
            sources.append(self.part(self.land, source, i))

        def stores(rows, wide):
            pairs, first = [], 0
            for result in results:
                columns = pl.ds(first, result.shape[-1])
                pairs.append((wide.at[:, columns], result.at[i, rows]))
                first += result.shape[-1]
            return pairs

        self.combine(sources, stores)


def layer_kernel(
    nc,
    experts,
    cos_ref,
    sin_ref,
    routes_ref,
    qkv_ref,
    small_ref,
    wo_shard_ref,
    x_hbm,
    d_out_hbm,
    w_gu_hbm,
    w_dn_hbm,
    layer_hbm,
    d_x_hbm,
    sum_q_ref,
    sum_o_ref,
    sum_gu_hbm,
    sum_dn_hbm,
    base_hbm,
    land_hbm,
    y_hbm,
    wq_hbm,
    wo_hbm,
    cot_hbm,
    inputs_hbm,
    query_hbm,
    heads_hbm,
    hidden_hbm,
    wk_all,
    kv_ref,
    gate_all,
    gates_ref,
    gains_ref,
    x_all,
    y_land,
    dx_land,
    core_land,
    plane_q,
    plane_k,
    lines_o,
    lines_q,
    lines_k,
    dkv_land,
    d_in_ref,
    dg_lanes,
    dg_part,
    dg_land,
    sends_f,
    recvs_f,
    sends_c,
    recvs_c,
    sends_x,
    recvs_x,
    sends_1,
    recvs_1,
    sends_2,
    recvs_2,
    sends_e,
    recvs_e,
    hand_sends,
    hand_recvs,
    stage_sems,
    load_sems,
    out_sems,
    sum_sems,
    y_sems,
    credits,
):
    e, z, c = (lax.axis_index(a) for a in ("expert", "context", "dp"))
    size = HEAD_DIMENSION
    blocks, tokens, width = cot_hbm.shape
    ff = w_dn_hbm.shape[1]
    query_width = QUERY_HEADS * size
    key_width = KEY_VALUE_HEADS * size
    qkv_width = query_width + 2 * key_width
    rest = wk_all.shape[-1]
    grad_width = base_hbm.shape[-1]
    ids = plane_ids(e)
    sibling = {"dp": 1 - c}
    bottom, even, odd, top = z == 0, lax.rem(z, 2) == 0, lax.rem(z, 2) == 1, z == nc - 1
    wire_1, wire_2, wire_e = Wire(sends_1, recvs_1), Wire(sends_2, recvs_2), Wire(sends_e, recvs_e)
    expert = ExpertLine(wire_e, base_hbm, land_hbm, sum_sems, z, nc)
    wire_c = Wire(sends_c, recvs_c)
    gather_cot = PlaneGather(wire_c, cot_hbm, e, d_out_hbm)
    wire_x = Wire(sends_x, recvs_x)
    gather = PlaneGather(wire_x, x_all, e)
    scatter_dx = PlaneScatter(wire_1, dx_land, ids)
    scatter_y = PlaneScatter(wire_2, y_land, ids)
    dg_slot = wire_1.slots(3)

    def front_phase(wq_ref, wo_ref, x_ref, inputs_ref, query_ref, heads_ref, hidden_ref, kv_scr, q_scr):
        wire = Wire(sends_f, recvs_f)
        kv_width = 2 * key_width
        load_x = pltpu.make_async_copy(x_hbm, x_ref, load_sems.at[0])
        load_x.start()
        wq_ref[e, z, c] = qkv_ref[:, pl.ds(0, query_width)]
        wo_ref[e, z, c] = wo_shard_ref[...]
        wk_all[e, z, c, :, pl.ds(0, kv_width)] = qkv_ref[:, pl.ds(query_width, kv_width)]
        wk_all[e, z, c, :, pl.ds(kv_width, SMALL)] = small_ref[...]
        greet(
            [(ids[m], None) for m in (1, 2, 3)]
            + [(sibling, None)]
            + [({"context": z + d}, z + d < nc) for d in range(1, nc)]
            + [({"context": z - d}, z >= d) for d in range(1, nc)]
        )
        gather_k = RowsGather(wire, wk_all, e, z, c, nc, 256)
        gather_q = RowsGather(wire, wq_ref, e, z, c, nc, 768)
        gather_o = RowsGather(wire, wo_ref, e, z, c, nc, 768)
        gather_k.go("l0", "s0")
        gather_q.go("s0")
        gather_k.go("l1", "s1", "f0", "l2", "s2")
        gather_q.go("l0")
        gather_k.go("f1", "h0", "l3", "s3")
        gather_o.go("l0")
        gather_k.go("f2", "h1", "f3")
        gather_q.go("l1", "s1", "f0")
        gather_k.go("h2", "h3")
        gather_q.go("l2", "s2")
        gather_k.go("c")
        load_x.wait()
        rows = x_ref[...].astype(F32)
        scale1 = lax.rsqrt(jnp.mean(rows * rows, -1, keepdims=True) + EPSILON)

        small = wk_all[:, :, :, :, pl.ds(kv_width, SMALL)].reshape(width, SMALL)
        small = jnp.transpose(small.astype(F32))
        gain_first, gain_second = small[experts : experts + 1], small[experts + 1 : experts + 2]
        gains_ref[0:1] = gain_first
        gains_ref[1:2] = gain_second
        inputs_ref[...] = (rows * scale1 * gain_first).astype(BF16)
        kv_scr[...] = dot_nn(inputs_ref[...], wk_all[...].reshape(width, kv_width + SMALL))

        def turned(head):
            return (head * cos_ref[...] + swap_halves(head) * sin_ref[...]).astype(BF16)

        line = wire.slots(KEY_VALUE_HEADS * nc)
        for j in range(KEY_VALUE_HEADS):
            kv_ref[j, z, :, pl.ds(0, size)] = turned(kv_scr[:, pl.ds(j * size, size)])
            value = kv_scr[:, pl.ds(kv_width // 2 + j * size, size)]
            kv_ref[j, z, :, pl.ds(size, size)] = value.astype(BF16)
            mine = kv_ref.at[j, z]
            for d in range(nc - 1, 0, -1):
                wire.start(mine, mine, line + j * nc + z, {"context": z + d}, when=z + d < nc)

        def keys_here(j):
            for d in range(1, nc):

                def wait(d=d):
                    wire.arrived(kv_ref.at[j, z - d], line + j * nc + z - d, {"context": z - d})

                pl.when(z >= d)(wait)

        outs = [
            pltpu.make_async_copy(source, dest, out_sems.at[n])
            for n, (source, dest) in enumerate(
                (
                    (inputs_ref, inputs_hbm),
                    (query_ref, query_hbm),
                    (heads_ref, heads_hbm),
                    (hidden_ref, hidden_hbm),
                    (wq_ref, wq_hbm),
                    (wo_ref, wo_hbm),
                )
            )
        ]
        outs[0].start()
        for later in range(1, nc):

            def clear(later=later):
                for j in range(KEY_VALUE_HEADS):
                    kv_ref[j, z + later] = jnp.zeros(kv_ref.shape[2:], BF16)

            pl.when(z + later < nc)(clear)
        gather_q.go("l3", "s3", "f1", "f2", "h0")
        gather_o.go("s0")
        gather_q.go("f3", "h1")
        gather_o.go("l1", "s1")
        gather_q.go("h2")
        gather_o.go("l2", "s2")
        gather_q.go("h3", "c")
        outs[4].start()
        gather_o.go("f0")

        @pl.loop(0, query_width // 256)
        def _(n):
            columns = pl.ds(pl.multiple_of(n * 256, 256), 256)
            q_scr[:, columns] = dot_nn(
                inputs_ref[...], wq_ref[:, :, :, :, columns].reshape(width, 256)
            )

        gather_o.go("l3", "s3", "f1")

        @pl.loop(0, QUERY_HEADS)
        def _(h):
            columns = pl.ds(pl.multiple_of(h * size, size), size)
            query_ref[:, columns] = turned(q_scr[:, columns])

        outs[1].start()

        logits = kv_scr[:, pl.ds(kv_width, SMALL)]
        lanes = lax.broadcasted_iota(jnp.int32, logits.shape, 1)
        routes = jnp.concatenate(
            [routes_ref[...].astype(F32), jnp.zeros((SMALL - TOP, tokens), F32)], 0
        )
        routes = jnp.transpose(routes).astype(jnp.int32)
        named = lanes == routes[:, 0:1]
        for k in range(1, TOP):
            named = named | (lanes == routes[:, k : k + 1])
        logits = jnp.where(named, logits, MASKED)
        expd = jnp.exp(logits - jnp.max(logits, -1, keepdims=True))
        gates = expd / jnp.sum(expd, -1, keepdims=True)
        gate_all[0] = jnp.transpose(gates)[:GATE_ROWS]
        gate_slot = wire.slots(3)
        for r in (1, 2, 3):
            wire.start(gate_all.at[0], gate_all.at[r], gate_slot + r - 1, ids[r])

        length = nc * tokens
        group = QUERY_HEADS // KEY_VALUE_HEADS

        def attend(first, last):
            j = first // group
            key = kv_ref[j, :, :, pl.ds(0, size)].reshape(length, size)
            value = kv_ref[j, :, :, pl.ds(size, size)].reshape(length, size)
            value_turned = jnp.transpose(value)

            @pl.loop(first, last)
            def _(h):
                column = pl.multiple_of(h * size, size)
                scores = causal(dot_nt(key, query_ref[:, pl.ds(column, size)]), z * tokens)
                largest = jnp.max(scores, 0, keepdims=True)
                expd = jnp.exp((scores - largest) * (size**-0.5))
                total = jnp.sum(expd, 0, keepdims=True)
                mixed = dot_nn(value_turned, expd.astype(BF16)) / total
                heads_ref[:, pl.ds(column, size)] = jnp.transpose(mixed).astype(BF16)

        half = group // 2
        gather_o.go("f2")
        keys_here(0)
        attend(0, half)
        gather_o.go("f3", "h0")
        gather_cot.spread()
        attend(half, group)
        gather_o.go("h1")
        keys_here(1)
        attend(group, group + half)
        gather_o.go("h2", "h3")
        attend(group + half, QUERY_HEADS)
        gather_o.go("c")
        outs[5].start()
        outs[2].start()
        part = width // wo_ref.shape[0]
        for block in range(wo_ref.shape[0]):
            weight = wo_ref[block].reshape(part, width)
            columns = pl.ds(block * part, part)
            hidden_ref[:, columns] = x_ref[:, columns].astype(F32) + dot_nt(heads_ref[...], weight)
        gather_cot.forward()
        hidden = hidden_ref[...]
        scale2 = lax.rsqrt(jnp.mean(hidden * hidden, -1, keepdims=True) + EPSILON)
        x_all[0] = (hidden * scale2 * gains_ref[1:2]).astype(BF16)
        gather.spread()
        outs[3].start()
        for r in (1, 2, 3):
            wire.arrived(gate_all.at[r], gate_slot + r - 1, ids[r])
        for r in range(gate_all.shape[0]):
            zeros = jnp.zeros((SMALL - GATE_ROWS, tokens), F32)
            turned_gates = jnp.transpose(jnp.concatenate([gate_all[r], zeros], 0))
            both = [
                jnp.sum(jnp.where(lanes == e * EXP_DEV + i, turned_gates, 0.0), -1, keepdims=True)
                for i in range(EXP_DEV)
            ]
            gates_ref[r] = jnp.where(lanes == 0, both[0], jnp.where(lanes == 1, both[1], 0.0))
        for copy in outs:
            copy.wait()
        wire.finish()

    def token_phase(w_gu, w_dn, cot_all, a_all, dgu_all, stage, ins, x_turned, cot_turned):
        expert.ins = ins
        scatter_dx.part = lambda r, half: x_all.at[r, :, pl.ds(half * width // 2, width // 2)]
        sources = [
            (w_gu_hbm.at[0], w_gu.at[0]),
            (w_dn_hbm.at[0], w_dn.at[0]),
            (d_out_hbm, cot_all.at[0]),
            (w_gu_hbm.at[1], w_gu.at[1]),
            (w_dn_hbm.at[1], w_dn.at[1]),
            (cot_hbm.at[1:], cot_all.at[1:]),
        ]
        loads = [
            pltpu.make_async_copy(source, dest, load_sems.at[n])
            for n, (source, dest) in enumerate(sources)
        ]
        for copy in loads[:5]:
            copy.start()
        step = 256
        wide = 512
        dg_lanes[...] = jnp.zeros_like(dg_lanes)

        def hidden_units(r, i, count=1):
            lane = lax.broadcasted_iota(jnp.int32, (1, SMALL), 1)
            here = pl.ds(r, count)
            flat = count * tokens

            @pl.loop(0, ff // step)
            def _(f):
                column = pl.multiple_of(f * step, step)
                rows = x_all[here].reshape(flat, width)
                grads = cot_all[here].reshape(flat, width)
                gate_part = dot_nn(rows, w_gu[i, :, pl.ds(column, step)])
                up_part = dot_nn(rows, w_gu[i, :, pl.ds(ff + column, step)])
                raw = dot_nt(grads, w_dn[i, pl.ds(column, step), :])
                gate = gates_ref[here].reshape(flat, SMALL)
                gate = jnp.sum(jnp.where(lane == i, gate, 0.0), -1, keepdims=True)
                sigma = jax.nn.sigmoid(gate_part)
                silu = gate_part * sigma
                act = silu * up_part
                lanes = lax.broadcasted_iota(jnp.int32, (flat, SMALL), 1)
                d_gate = jnp.where(
                    lanes == e * EXP_DEV + i, jnp.sum(act * raw, -1, keepdims=True), 0.0
                )
                dg_lanes[here] += d_gate.reshape(count, tokens, SMALL)

                def put(ref, first, values):
                    values = values.astype(BF16).reshape(count, tokens, step)
                    ref[here, :, pl.ds(pl.multiple_of(first, step), step)] = values

                put(a_all, i * ff + column, act * gate)
                d_act = raw * gate
                d_gate_part = d_act * up_part * sigma * (1.0 + gate_part * (1.0 - sigma))
                put(dgu_all, i * 2 * ff + column, d_gate_part)
                put(dgu_all, i * 2 * ff + ff + column, d_act * silu)

        def turn(rows, turned, r):
            @pl.loop(0, width // wide)
            def _(n):
                columns = pl.ds(pl.multiple_of(n * wide, wide), wide)
                turned[columns, pl.ds(r * tokens, tokens)] = jnp.transpose(rows[r, :, columns])

        def y_copy(r):
            return pltpu.make_async_copy(cot_all.at[r], y_hbm.at[r], out_sems.at[r])

        def outputs(r, count=1):
            here = pl.ds(r, count)
            flat = count * tokens

            @pl.loop(0, width // wide)
            def _(n):
                columns = pl.ds(pl.multiple_of(n * wide, wide), wide)
                low = dgu_all[here].reshape(flat, EXP_DEV * 2 * ff)
                d_rows = dot_nt(low[:, : 2 * ff], w_gu[0, columns, :])
                d_rows += dot_nt(low[:, 2 * ff :], w_gu[1, columns, :])
                weight = w_dn[:, :, columns].reshape(EXP_DEV * ff, wide)
                out = dot_nn(a_all[here].reshape(flat, EXP_DEV * ff), weight).astype(BF16)
                for k in range(count):
                    rows = slice(k * tokens, (k + 1) * tokens)
                    cot_all[r + k, :, columns] = out[rows]
                    if r == 0:
                        d_in_ref[:, columns] = d_rows
                    else:
                        x_all[r + k, :, columns] = d_rows[rows].astype(BF16)

            for k in range(r, r + count):
                y_copy(k).start()
                dg_part[k] = jnp.transpose(dg_lanes[k])[:GATE_ROWS]
                if k:
                    wire_1.start(dg_part.at[k], dg_land.at[k - 1], dg_slot + k - 1, ids[k])

        half_rows = width // nc // 2
        def where(k):
            high = lax.rem(lax.div(z, 2) + 1 + lax.div(k, 2), 2)
            return 2 * high + lax.rem(z + 1 + k, 2)

        def keep(i, k):
            slot = lax.rem(k, 2)
            return pltpu.make_async_copy(
                stage.at[slot, c], expert.part(base_hbm, where(k), i), stage_sems.at[slot]
            )

        def hand(i, k):
            return pltpu.make_async_remote_copy(
                src_ref=stage.at[lax.rem(k, 2), 1 - c],
                dst_ref=core_land.at[k],
                send_sem=hand_sends.at[i * nc + k],
                recv_sem=hand_recvs.at[i * nc + k],
                device_id=sibling,
                device_id_type=MESH,
            )

        def settle(i, k):
            hand(i, k).wait_recv()
            add_into(stage.at[lax.rem(k, 2), c], core_land.at[k])
            keep(i, k).start()

        def clear(i, k):
            keep(i, k).wait()
            hand(i, k).wait_send()

        def leave(i, r):
            if r == 1:
                expert.send(i, r, when=even if i else None)
            elif r == 3 or r == 2 and i == 0:
                expert.send(i, r, when=expert.end)
            elif r == 2:
                expert.send(i, r, when=bottom)

        def weight_grads(i, between=lambda k: None):
            @pl.loop(0, nc)
            def _(k):
                @pl.when(k >= 2)
                def _():
                    clear(i, k - 2)

                for n in (2, 3):

                    @pl.when(k == n)
                    def _(n=n):
                        leave(i, 5 - n)

                rows_at = pl.ds(pl.multiple_of(where(k) * 2 * half_rows, 2 * half_rows), 2 * half_rows)
                for first, rows, grad, start, count in (
                    (0, x_turned[rows_at, :], dgu_all, i * 2 * ff, 2),
                    (2 * ff, cot_turned[rows_at, :], a_all, i * ff, 1),
                ):

                    @pl.loop(0, count)
                    def _(n):
                        column = pl.multiple_of(n * ff, ff)
                        part = grad[:, :, pl.ds(pl.multiple_of(start + column, ff), ff)]
                        result = dot_nn(rows, part.reshape(blocks * tokens, ff)).astype(BF16)
                        stage[lax.rem(k, 2), :, :, pl.ds(pl.multiple_of(first + column, ff), ff)] = (
                            result.reshape(2, half_rows, ff)
                        )

                if i:

                    @pl.when(k == 0)
                    def _():
                        pl.semaphore_wait(credits.at[3], 1)

                hand(i, k).start()

                @pl.when(k >= 1)
                def _():
                    settle(i, k - 1)

                between(k)

        for copy in loads[:3]:
            copy.wait()
        gather_cot.complete()
        loads[5].start()
        for copy in loads[3:5]:
            copy.wait()

        @pl.loop(0, EXP_DEV)
        def _(i):
            hidden_units(0, i)

        gather.forward()
        turn(x_all, x_turned, 0)
        turn(cot_all, cot_turned, 0)
        outputs(0)
        loads[5].wait()
        for r in range(1, blocks):
            turn(cot_all, cot_turned, r)
        gather.near(1)
        gather.near(2)
        turn(x_all, x_turned, 1)
        turn(x_all, x_turned, 2)
        hidden_units(1, 0, 2)
        gather.far()
        turn(x_all, x_turned, 3)
        hidden_units(3, 0)
        weight_grads(0)
        hidden_units(1, 1, 2)
        clear(0, nc - 2)
        leave(0, 1)
        settle(0, nc - 1)
        pl.semaphore_signal(credits.at[3], inc=1, device_id=sibling, device_id_type=MESH)
        wire_x.finish()
        outputs(1, 2)
        scatter_dx.near(1)
        scatter_dx.near(2)
        hidden_units(3, 1)
        expert.relay_begin(0, 2)
        outputs(3)
        scatter_dx.far()
        clear(0, nc - 1)
        expert.relay_add(0, 2)

        def between(k):
            @pl.when(k == 0)
            def _():
                expert.relay_send(0, 2)

            @pl.when(k == 1)
            def _():
                scatter_dx.relay()

            @pl.when(k == 2)
            def _():
                expert.relay_begin(0, 3)

            @pl.when(k == 3)
            def _():
                expert.relay_add(0, 3)

        weight_grads(1, between)
        expert.relay_send(0, 3)
        scatter_dx.total(d_in_ref)
        for r in (1, 2):
            pl.semaphore_signal(credits.at[r], inc=1, device_id=ids[r], device_id_type=MESH)
        settle(1, nc - 1)
        for k in (nc - 2, nc - 1):
            clear(1, k)
        leave(1, 1)
        for r in range(blocks):
            y_copy(r).wait()
        wire_1.finish()
        wire_c.finish()
        pl.semaphore_signal(credits.at[0], inc=1, device_id=sibling, device_id_type=MESH)

    def token_rows_phase(
        weight,
        grads_o,
        grads_q,
        x_ref,
        inputs_ref,
        query_ref,
        heads_ref,
        hidden_ref,
        d_hidden_ref,
        d_attn_ref,
        d_heads_ref,
        d_all_ref,
        rows_ref,
        dkv_acc,
        dkv_ref,
        y_relay,
        ins,
        out_wide,
    ):
        expert.ins, expert.out = ins, out_wide
        cot_ref, d_inputs_ref = d_heads_ref, hidden_ref
        scatter_y.part = lambda r, half: y_hbm.at[r, :, pl.ds(half * width // 2, width // 2)]
        y_loads = [
            pltpu.make_async_copy(scatter_y.part(2 - half, half), y_relay.at[half], y_sems.at[half])
            for half in range(2)
        ]
        for copy in y_loads:
            copy.start()
        planes = grads_o.shape[1]
        part = width // planes
        sources = (
            (hidden_hbm, hidden_ref),
            (d_out_hbm, cot_ref),
            (wo_hbm, weight),
            (heads_hbm, heads_ref),
            (query_hbm, query_ref),
            (x_hbm, x_ref),
            (inputs_hbm, inputs_ref),
        )
        loads = [
            pltpu.make_async_copy(source, dest, load_sems.at[4 + n])
            for n, (source, dest) in enumerate(sources)
        ]
        for copy in loads:
            copy.start()
        for r in (1, 2):
            scatter_y.near(r)
        scatter_y.far()

        def rows_scatter(buf, core, plane, lines, start, count, half):
            return RowsScatter(
                wire_2,
                buf,
                core,
                plane,
                lines,
                e,
                z,
                c,
                nc,
                start,
                count,
                half,
            )

        rows_of = part // 2
        scatter_o = rows_scatter(
            grads_o,
            x_all.at[:, pl.ds(0, rows_of)],
            lambda slot, half: dx_land.at[slot, pl.ds(0, rows_of)],
            lines_o,
            0,
            width,
            width // 2,
        )
        scatter_q = rows_scatter(
            grads_q,
            core_land.at[:, :, pl.ds(0, query_width)],
            lambda slot, half: plane_q.at[slot],
            lines_q,
            0,
            query_width,
            query_width // 2,
        )
        rest_half = rest // 256 * 128
        scatter_k = rows_scatter(
            grads_q,
            core_land.at[:, :, pl.ds(query_width, rest)],
            lambda slot, half: plane_k.at[
                slot, :, pl.ds(0, rest - rest_half if half else rest_half)
            ],
            lines_k,
            query_width,
            rest,
            rest_half,
        )
        scatter_kv = [
            LineSum(wire_2, lambda j, h=h: dkv_ref.at[h, j], dkv_land.at[h], z, nc, up=False)
            for h in range(KEY_VALUE_HEADS)
        ]

        for scatter in (scatter_o, scatter_q, scatter_k):
            scatter.line.clear()
        for line in scatter_kv:
            line.clear()

        loads[0].wait()
        loads[1].wait()
        hidden, d_in = hidden_ref[...], d_in_ref[...]
        scale2 = lax.rsqrt(jnp.mean(hidden * hidden, -1, keepdims=True) + EPSILON)
        scaled = d_in * gains_ref[1:2]
        mean = jnp.mean(scaled * hidden, -1, keepdims=True)
        d_hidden = cot_ref[...].astype(F32) + scale2 * scaled
        d_hidden = d_hidden - hidden * (scale2 * scale2 * scale2 * mean)
        d_hidden_ref[...] = d_hidden
        d_attn_ref[...] = d_hidden.astype(BF16)
        rows_ref[...] = jnp.zeros_like(rows_ref)
        rows_ref[experts + 1 : experts + 2, :] = jnp.sum(d_in * hidden * scale2, 0, keepdims=True)

        loads[2].wait()

        @pl.loop(0, query_width // 256)
        def _(n):
            columns = pl.ds(pl.multiple_of(n * 256, 256), 256)
            out = weight[:, :, :, :, columns].reshape(width, 256)
            d_heads_ref[:, columns] = dot_nn(d_attn_ref[...], out).astype(BF16)

        load_q = pltpu.make_async_copy(wq_hbm, weight, load_sems.at[0])
        load_q.start()
        loads[3].wait()

        def row_grads(buf, left, right, first, count, extra=None):
            @pl.loop(0, planes)
            def _(block):
                columns = pl.ds(pl.multiple_of(block * part, part), part)
                result = dot_tn(left[:, columns], right)
                if extra is not None:
                    result = result + extra(columns)
                result = result.astype(BF16).reshape(nc, 2, part // nc // 2, count)
                for half in range(2):
                    buf[half, block, :, pl.ds(first, count)] = result[:, half].reshape(
                        part // 2, count
                    )

        length = nc * tokens
        group = QUERY_HEADS // KEY_VALUE_HEADS
        loads[4].wait()
        dkv_acc[...] = jnp.zeros_like(dkv_acc)

        def attend(j, first, last):
            key = kv_ref[j, :, :, pl.ds(0, size)].reshape(length, size)
            value = kv_ref[j, :, :, pl.ds(size, size)].reshape(length, size)
            key_turned = jnp.transpose(key)

            @pl.loop(j * group + first, j * group + last)
            def _(h):
                columns = pl.ds(pl.multiple_of(h * size, size), size)
                query, grad = query_ref[:, columns], d_heads_ref[:, columns]
                scores = causal(dot_nt(key, query), z * tokens)
                largest = jnp.max(scores, 0, keepdims=True)
                expd = jnp.exp((scores - largest) * (size**-0.5))
                probs = expd * (1.0 / jnp.sum(expd, 0, keepdims=True))
                d_probs = dot_nt(value, grad)
                inner = jnp.sum(probs * d_probs, 0, keepdims=True)
                d_raw = (probs * (d_probs - inner) * (size**-0.5)).astype(BF16)
                d_query = jnp.transpose(dot_nn(key_turned, d_raw))
                d_query = d_query * cos_ref[...] - swap_halves(d_query) * sin_ref[...]
                d_all_ref[:, columns] = d_query.astype(BF16)
                dkv_acc[j, :, pl.ds(0, size)] += dot_nn(d_raw, query)
                dkv_acc[j, :, pl.ds(size, size)] += dot_nn(probs.astype(BF16), grad)

        def round_kv(j):
            for block in range(nc):
                rows = dkv_acc[j, pl.ds(block * tokens, tokens), :]
                dkv_ref[j, block] = rows.astype(BF16)

        def enter():
            pl.semaphore_wait(credits.at[1], 1)
            pl.semaphore_wait(credits.at[2], 1)

        attend(0, 0, group)
        round_kv(0)
        scatter_kv[0].send()
        attend(1, 0, group)
        round_kv(1)
        scatter_kv[1].send()
        expert.send(1, 2, when=top)
        expert.send(1, 1, when=odd)
        expert.relay_begin(1, 2)
        row_grads(grads_o, d_attn_ref, heads_ref[...], 0, width)
        expert.relay_add(1, 2)
        pl.semaphore_wait(credits.at[0], 1)
        scatter_o.share()
        y_own = pltpu.make_async_copy(y_hbm.at[0], heads_ref, load_sems.at[2])
        y_own.start()
        for copy in y_loads:
            copy.wait()
        scatter_y.relay(lambda r, half: y_relay.at[half])
        expert.relay_send(1, 2)
        scatter_o.merge(enter)

        for copy in loads[5:]:
            copy.wait()
        row_grads(grads_q, inputs_ref, d_all_ref[:, pl.ds(0, query_width)], 0, query_width)
        scatter_q.share()
        scatter_o.relay()
        expert.last(0, (sum_gu_hbm, sum_dn_hbm))
        scatter_q.merge()
        for h in range(KEY_VALUE_HEADS):
            grad = scatter_kv[h].total()
            d_key = grad[:, :size]
            d_key = d_key * cos_ref[...] - swap_halves(d_key) * sin_ref[...]
            d_all_ref[:, pl.ds(query_width + h * size, size)] = d_key.astype(BF16)
            d_all_ref[:, pl.ds(query_width + key_width + h * size, size)] = grad[:, size:].astype(
                BF16
            )
        y_own.wait()
        hidden_ref[...] += heads_ref[...].astype(F32)
        scatter_y.total(hidden_ref)
        heads_ref[...] = hidden_ref[...].astype(BF16)
        layer_out = pltpu.make_async_copy(heads_ref, layer_hbm, out_sems.at[0])
        layer_out.start()

        total = dg_part[0]
        for r in (1, 2, 3):
            wire_1.arrived(dg_land.at[r - 1], dg_slot + r - 1, ids[r])
            total = total + dg_land[r - 1]
        gates = gate_all[0]
        d_logits = gates * (total - jnp.sum(gates * total, 0, keepdims=True))
        d_logits = jnp.concatenate(
            [d_logits, jnp.zeros((SMALL - d_logits.shape[0], tokens), F32)], 0
        )
        d_all_ref[:, pl.ds(qkv_width, SMALL)] = jnp.transpose(d_logits).astype(BF16)

        load_q.wait()

        @pl.loop(0, planes)
        def _(block):
            columns = pl.ds(pl.multiple_of(block * part, part), part)
            rows_q = weight[block].reshape(part, query_width)
            rows_k = wk_all[block].reshape(part, rest)
            d_inputs_ref[:, columns] = dot_nt(
                d_all_ref[:, pl.ds(0, query_width)], rows_q
            ) + dot_nt(d_all_ref[:, pl.ds(query_width, rest)], rows_k)

        rows = x_ref[...].astype(F32)
        scale1 = lax.rsqrt(jnp.mean(rows * rows, -1, keepdims=True) + EPSILON)
        d_inputs = d_inputs_ref[...]
        rows_ref[experts : experts + 1, :] = jnp.sum(d_inputs * rows * scale1, 0, keepdims=True)

        def extra(columns):
            small = jnp.transpose(rows_ref[:, columns])
            return jnp.concatenate([jnp.zeros((part, rest - SMALL), F32), small], 1)

        row_grads(
            grads_q, inputs_ref, d_all_ref[:, pl.ds(query_width, rest)], query_width, rest, extra
        )
        scatter_k.share()
        scatter_o.total()
        scatter_o.line.send()
        expert.relay_begin(1, 3)
        scatter_q.relay()
        expert.relay_add(1, 3)
        scatter_k.merge()
        expert.relay_send(1, 3)
        scaled = d_inputs_ref[...] * gains_ref[0:1]
        rows = x_ref[...].astype(F32)
        scale1 = lax.rsqrt(jnp.mean(rows * rows, -1, keepdims=True) + EPSILON)
        mean = jnp.mean(scaled * rows, -1, keepdims=True)
        d_x = d_hidden_ref[...] + scale1 * scaled - rows * (scale1 * scale1 * scale1 * mean)
        inputs_ref[...] = d_x.astype(BF16)
        d_x_out = pltpu.make_async_copy(inputs_ref, d_x_hbm, out_sems.at[1])
        d_x_out.start()
        scatter_q.total()
        scatter_q.line.send()
        scatter_k.relay()
        scatter_k.total()
        scatter_k.line.send()
        sum_o_ref[...] = scatter_o.line.total()
        expert.last(1, (sum_gu_hbm, sum_dn_hbm))
        sum_q_ref[:, pl.ds(0, query_width)] = scatter_q.line.total()
        sum_q_ref[:, pl.ds(query_width, rest)] = scatter_k.line.total()
        layer_out.wait()
        d_x_out.wait()
        wire_2.finish()
        expert.finish()

    held = EXP_DEV
    weight_shape = wq_hbm.shape
    pl.run_scoped(
        front_phase,
        pltpu.VMEM(weight_shape, BF16),
        pltpu.VMEM(weight_shape, BF16),
        pltpu.VMEM((tokens, width), BF16),
        pltpu.VMEM((tokens, width), BF16),
        pltpu.VMEM((tokens, query_width), BF16),
        pltpu.VMEM((tokens, query_width), BF16),
        pltpu.VMEM((tokens, width), F32),
        pltpu.VMEM((tokens, rest), F32),
        pltpu.VMEM((tokens, query_width), F32),
    )
    shard, step = width // nc // 2, 48
    pl.run_scoped(
        token_phase,
        pltpu.VMEM((held, width, 2 * ff), BF16),
        pltpu.VMEM((held, ff, width), BF16),
        pltpu.VMEM((blocks, tokens, width), BF16),
        pltpu.VMEM((blocks, tokens, held * ff), BF16),
        pltpu.VMEM((blocks, tokens, held * 2 * ff), BF16),
        pltpu.VMEM((2, 2, shard, grad_width // held), BF16),
        pltpu.VMEM((2, shard // step, step, grad_width // held), BF16),
        pltpu.VMEM((width, blocks * tokens), BF16),
        pltpu.VMEM((width, blocks * tokens), BF16),
    )
    rows_half = width // blocks // 2
    pl.run_scoped(
        token_rows_phase,
        pltpu.VMEM(weight_shape, BF16),
        pltpu.VMEM((2, blocks, rows_half, width), BF16),
        pltpu.VMEM((2, blocks, rows_half, qkv_width + SMALL), BF16),
        pltpu.VMEM((tokens, width), BF16),
        pltpu.VMEM((tokens, width), BF16),
        pltpu.VMEM((tokens, query_width), BF16),
        pltpu.VMEM((tokens, query_width), BF16),
        pltpu.VMEM((tokens, width), F32),
        pltpu.VMEM((tokens, width), F32),
        pltpu.VMEM((tokens, width), BF16),
        pltpu.VMEM((tokens, query_width), BF16),
        pltpu.VMEM((tokens, qkv_width + SMALL), BF16),
        pltpu.VMEM((SMALL, width), F32),
        pltpu.VMEM((KEY_VALUE_HEADS, nc * tokens, 2 * size), F32),
        pltpu.VMEM((KEY_VALUE_HEADS, nc, tokens, 2 * size), BF16),
        pltpu.VMEM((2, tokens, width // 2), BF16),
        pltpu.VMEM((4, shard // step, step, grad_width // held), BF16),
        pltpu.VMEM((2, step, grad_width // held), F32),
    )


def layer(operands, sizes):
    ne, nc, nd = sizes
    qkv_shard, x = operands[3], operands[6]
    w_dn = operands[9]
    tokens, width = x.shape
    held, ff = w_dn.shape[0], w_dn.shape[1]
    query_width = QUERY_HEADS * HEAD_DIMENSION
    rows, qkv_width = qkv_shard.shape
    rest = qkv_width - query_width + SMALL
    rest_half = rest // 256 * 128
    shard, grads = width // (nc * nd), held * 3 * ff
    kv_size = 2 * HEAD_DIMENSION
    weight = (ne, nc, nd, rows, query_width)
    shapes = [
        ((tokens, width), BF16),
        ((tokens, width), BF16),
        ((rows, qkv_width + SMALL), F32),
        ((rows, width), F32),
        ((held, shard, 2 * ff), F32),
        ((held, shard, ff), F32),
        ((nc, shard, grads), BF16),
        ((nc + 2, shard, grads), BF16),
        ((ne, tokens, width), BF16),
        (weight, BF16),
        (weight, BF16),
        ((ne, tokens, width), BF16),
        ((tokens, width), BF16),
        ((tokens, query_width), BF16),
        ((tokens, query_width), BF16),
        ((tokens, width), F32),
    ]
    vmem = pl.BlockSpec(memory_space=pltpu.VMEM)
    anywhere = pl.BlockSpec(memory_space=pl.ANY)
    units = nc * held
    sems = [132, 110, 6, 6, 6, 6, 10, 10, 64, 64, 2 * units, (nc + 2) * held, units, units, 2, 12, 6]
    return pl.pallas_call(
        functools.partial(layer_kernel, nc, EXP_DEV * ne),
        out_shape=[jax.ShapeDtypeStruct(*s) for s in shapes],
        in_specs=[vmem] * 6 + [anywhere] * (len(operands) - 6),
        out_specs=[anywhere] * 2 + [vmem] * 2 + [anywhere] * (len(shapes) - 4),
        scratch_shapes=[
            pltpu.VMEM((ne, nc, nd, rows, rest), BF16),
            pltpu.VMEM((KEY_VALUE_HEADS, nc, tokens, kv_size), BF16),
            pltpu.VMEM((ne, GATE_ROWS, tokens), F32),
            pltpu.VMEM((ne, tokens, SMALL), F32),
            pltpu.VMEM((8, width), F32),
            pltpu.VMEM((ne, tokens, width), BF16),
            pltpu.VMEM((6, tokens, width // 2), BF16),
            pltpu.VMEM((6, tokens, width // 2), BF16),
            pltpu.VMEM((nc, shard, grads // held), BF16),
            pltpu.VMEM((6, nc * rows, query_width // 2), BF16),
            pltpu.VMEM((6, nc * rows, rest - rest_half), BF16),
            pltpu.VMEM((nc, rows, width), BF16),
            pltpu.VMEM((nc, rows, query_width), BF16),
            pltpu.VMEM((nc, rows, rest), BF16),
            pltpu.VMEM((KEY_VALUE_HEADS, nc, tokens, kv_size), BF16),
            pltpu.VMEM((tokens, width), F32),
            pltpu.VMEM((ne, tokens, SMALL), F32),
            pltpu.VMEM((ne, GATE_ROWS, tokens), F32),
            pltpu.VMEM((ne - 1, GATE_ROWS, tokens), F32),
        ]
        + [pltpu.SemaphoreType.DMA((count,)) for count in sems]
        + [
            pltpu.SemaphoreType.DMA((20,)),
            pltpu.SemaphoreType.DMA((2,)),
            pltpu.SemaphoreType.REGULAR((4,)),
        ],
        compiler_params=pltpu.CompilerParams(
            collective_id=0, has_side_effects=True, vmem_limit_bytes=63 * MIB
        ),
    )(*operands)


def finish_kernel(experts, *refs):
    sources, dests = refs[:6], refs[6:12]
    router_ref, first_ref, second_ref = refs[12:]
    sum_q = sources[0]
    qkv_width = dests[0].shape[-1]
    dests[0][...] = sum_q[:, pl.ds(0, qkv_width)]
    for source, dest in zip(sources[1:], dests[1:]):
        dest[...] = source[...]
    small = sum_q[:, pl.ds(qkv_width, SMALL)]
    rows = small.shape[0]
    filled = jnp.concatenate([small, jnp.zeros((SMALL - rows, SMALL), F32)], 0)
    turned = jnp.transpose(filled)[:, :rows]
    router_ref[...] = turned[:experts]
    first_ref[...] = turned[experts : experts + 1]
    second_ref[...] = turned[experts + 1 : experts + 2]


def finish(sum_q, others, experts):
    rows, q_width = sum_q.shape
    vmem = pl.BlockSpec(memory_space=pltpu.VMEM)
    shapes = [jax.ShapeDtypeStruct((rows, q_width - SMALL), F32)]
    shapes += [jax.ShapeDtypeStruct(o.shape, o.dtype) for o in others]
    shapes += [jax.ShapeDtypeStruct((count, rows), F32) for count in (experts, 1, 1)]
    return pl.pallas_call(
        functools.partial(finish_kernel, experts),
        out_shape=shapes,
        in_specs=[vmem] * 6,
        out_specs=[vmem] * 9,
        compiler_params=pltpu.CompilerParams(vmem_limit_bytes=60 * MIB),
    )(sum_q, *others)


def local_plain(
    layer_input,
    gain_attn,
    query_key_value_weight,
    w_out,
    w_router,
    gain_ffn,
    w_gate_up,
    w_down,
    routes,
    d_out,
):
    tokens = layer_input.shape[1]
    model_width = layer_input.shape[2]
    ne, nc, nd = (lax.axis_size(a) for a in ("expert", "context", "dp"))
    expert_total = EXP_DEV * ne
    ff = w_down.shape[1]
    me = lax.axis_index("expert")
    first_row = lax.axis_index("context") * tokens
    query_width = QUERY_HEADS * HEAD_DIMENSION
    key_width = KEY_VALUE_HEADS * HEAD_DIMENSION
    qkv_width = query_width + 2 * key_width

    small = jnp.concatenate([w_router, gain_attn[:, None], gain_ffn[:, None]], -1)
    small = jnp.pad(small, ((0, 0), (0, 128 - small.shape[1])))
    gathered = gather_rows(jnp.concatenate([query_key_value_weight, small], -1))
    out_turned = gather_rows(w_out.T)
    qkv_weight = gathered[:, :qkv_width]
    router_weight = gathered[:, qkv_width : qkv_width + expert_total]
    gains = gathered[:, qkv_width + expert_total : qkv_width + expert_total + 2].T.astype(F32)
    gain_first, gain_second = gains[0], gains[1]
    cotangent_all = plane_gather(d_out[0])

    token_rows = layer_input[0].astype(F32)
    scale1 = lax.rsqrt(jnp.mean(token_rows * token_rows, -1, keepdims=True) + EPSILON)
    inputs1 = (token_rows * scale1 * gain_first).astype(BF16)
    query_key_value = dot_nn(inputs1, qkv_weight)
    cosine_values, sine_values = rope_tables(first_row + jnp.arange(tokens), HEAD_DIMENSION)
    rotated = rotate_half(
        query_key_value[:, : query_width + key_width].reshape(tokens, -1, HEAD_DIMENSION),
        cosine_values,
        sine_values,
    ).reshape(tokens, -1)
    query = rotated[:, :query_width].astype(BF16)
    key_value_local = jnp.concatenate(
        [rotated[:, query_width:], query_key_value[:, query_width + key_width :]], -1
    ).astype(BF16)
    key_value = line_gather(key_value_local, "context", both=False).reshape(nc * tokens, -1)
    first = first_row.astype(jnp.int32).reshape(1)
    heads = attend_forward(first, query, key_value)

    logits = dot_nn(inputs1, router_weight)
    chosen_ids = routes[0]
    picks = (chosen_ids[:, :, None] == jnp.arange(expert_total)[None, None, :]).astype(F32)
    chosen = jnp.sum(picks * logits[:, None, :], -1)
    gates = jax.nn.softmax(chosen, axis=-1)
    gate_dense = jnp.sum(picks * gates[:, :, None], 1).T
    gate_blocks = cube_gather(gate_dense, "expert", axis_masks("expert"))
    gate_local = jnp.concatenate(
        [lax.dynamic_slice_in_dim(b, me * EXP_DEV, EXP_DEV, 0) for b in gate_blocks], 1
    )

    attn = dot_nt(heads, out_turned)
    hidden = token_rows + attn
    scale2 = lax.rsqrt(jnp.mean(hidden * hidden, -1, keepdims=True) + EPSILON)
    expert_in = (hidden * scale2 * gain_second).astype(BF16)

    rows_all = plane_gather(expert_in)
    gate_up = jnp.einsum("td,edf->etf", rows_all, w_gate_up, preferred_element_type=F32)
    gate_part, up_part = gate_up[..., :ff], gate_up[..., ff:]
    sigma = jax.nn.sigmoid(gate_part)
    silu = gate_part * sigma
    act = silu * up_part
    gate_column = gate_local[:, :, None]
    act_gated = (act * gate_column).astype(BF16)
    partial_out = jnp.einsum("etf,efd->td", act_gated, w_down, preferred_element_type=F32)
    mixture = plane_scatter(partial_out.astype(BF16), tokens)
    layer_result = (hidden + mixture).astype(BF16)

    d_act_raw = jnp.einsum("td,efd->etf", cotangent_all, w_down, preferred_element_type=F32)
    d_gates_local = jnp.sum(d_act_raw * act, -1)
    d_act = d_act_raw * gate_column
    d_gate_part = d_act * up_part * sigma * (1.0 + gate_part * (1.0 - sigma))
    d_up_part = d_act * silu
    d_gate_up = jnp.concatenate([d_gate_part, d_up_part], -1).astype(BF16)
    d_rows = jnp.einsum("etf,edf->td", d_gate_up, w_gate_up, preferred_element_type=F32)
    grad_down = jnp.einsum("td,etf->edf", cotangent_all, act_gated, preferred_element_type=F32)
    grad_gate_up = jnp.einsum("td,etf->edf", rows_all, d_gate_up, preferred_element_type=F32)

    d_expert_in = plane_scatter(d_rows.astype(BF16), tokens)
    d_gate_blocks = d_gates_local.reshape(EXP_DEV, ne, tokens)
    d_gates_dense = jnp.zeros((expert_total, tokens), F32)
    for r in range(ne):
        arrived = d_gate_blocks[:, r]
        if r:
            arrived = exchange(arrived, "expert", r)
        d_gates_dense = lax.dynamic_update_slice(d_gates_dense, arrived, ((me ^ r) * EXP_DEV, 0))
    d_gates = jnp.sum(picks * d_gates_dense.T[:, None, :], -1)
    d_chosen = gates * (d_gates - jnp.sum(gates * d_gates, -1, keepdims=True))
    d_logits = jnp.sum(picks * d_chosen[:, :, None], 1).astype(BF16)
    grad_router = dot_tn(inputs1, d_logits)

    core = lax.axis_index("dp")
    part = model_width // (nc * nd)

    def scatter_experts(grad):
        blocks = grad.reshape(EXP_DEV, nc, nd, part, -1)
        mine = cube_scatter(
            [lax.dynamic_index_in_dim(blocks, core ^ r, 2, keepdims=False) for r in range(nd)],
            "dp",
            axis_masks("dp"),
        )
        return line_scatter(
            lambda j: lax.dynamic_index_in_dim(mine, j, 1, keepdims=False), "context"
        )

    sum_gate_up = scatter_experts(grad_gate_up)
    sum_down = jnp.swapaxes(scatter_experts(grad_down), 1, 2)

    cotangent = d_out[0].astype(F32)
    scaled2 = d_expert_in * gain_second
    d_hidden = (
        cotangent
        + scale2 * scaled2
        - hidden * (scale2 * scale2 * scale2) * jnp.mean(scaled2 * hidden, -1, keepdims=True)
    )
    grad_gain_second = jnp.sum(d_expert_in * hidden * scale2, 0)
    d_attn = d_hidden.astype(BF16)
    grad_out_turned = dot_tn(d_attn, heads)
    sum_out = scatter_rows(grad_out_turned).T
    d_heads = dot_nn(d_attn, out_turned).astype(BF16)
    d_query, d_key_all, d_value_all = attend_backward(first, query, key_value, d_heads)
    d_key_value_all = jnp.concatenate([d_key_all, d_value_all], -1).reshape(nc, tokens, -1)
    d_key_value = line_scatter(
        lambda j: lax.dynamic_index_in_dim(d_key_value_all, j, 0, keepdims=False),
        "context",
        up=False,
    )
    d_rotated = rotate_back(
        jnp.concatenate([d_query, d_key_value[:, :key_width]], -1).reshape(
            tokens, -1, HEAD_DIMENSION
        ),
        cosine_values,
        sine_values,
    ).reshape(tokens, -1)
    d_qkv = jnp.concatenate([d_rotated, d_key_value[:, key_width:]], -1).astype(BF16)
    d_inputs = dot_nt(d_qkv, qkv_weight) + dot_nt(d_logits, router_weight)
    grad_gain_first = jnp.sum(d_inputs * token_rows * scale1, 0)
    grad_qkv = dot_tn(inputs1, d_qkv)
    small_grads = jnp.concatenate(
        [grad_router, grad_gain_first[:, None], grad_gain_second[:, None]], -1
    )
    small_grads = jnp.pad(small_grads, ((0, 0), (0, 128 - small_grads.shape[1])))
    sum_rows = scatter_rows(jnp.concatenate([grad_qkv, small_grads], -1))
    sum_qkv = sum_rows[:, :qkv_width]
    sum_router = sum_rows[:, qkv_width : qkv_width + expert_total]
    sum_gain_first = sum_rows[:, qkv_width + expert_total]
    sum_gain_second = sum_rows[:, qkv_width + expert_total + 1]
    scaled1 = d_inputs * gain_first
    d_input_rows = (
        d_hidden
        + scale1 * scaled1
        - token_rows
        * (scale1 * scale1 * scale1)
        * jnp.mean(scaled1 * token_rows, -1, keepdims=True)
    ).astype(BF16)
    return (
        layer_result[None],
        d_input_rows[None],
        sum_gain_first,
        sum_qkv,
        sum_out,
        sum_router,
        sum_gain_second,
        sum_gate_up,
        sum_down,
    )


def local_fused(
    layer_input,
    gain_attn,
    query_key_value_weight,
    w_out,
    w_router,
    gain_ffn,
    w_gate_up,
    w_down,
    routes,
    d_out,
):
    tokens = layer_input.shape[1]
    ne, nc, nd = sizes = tuple(lax.axis_size(a) for a in ("expert", "context", "dp"))
    expert_total = EXP_DEV * ne
    first_row = lax.axis_index("context") * tokens
    query_width = QUERY_HEADS * HEAD_DIMENSION
    key_width = KEY_VALUE_HEADS * HEAD_DIMENSION
    qkv_width = query_width + 2 * key_width

    small = jnp.concatenate([w_router, gain_attn[:, None], gain_ffn[:, None]], -1)
    small = jnp.pad(small, ((0, 0), (0, SMALL - small.shape[1])))
    cosine_values, sine_values = rope_tables(first_row + jnp.arange(tokens), HEAD_DIMENSION)
    sine_values = sine_values * jnp.where(
        jnp.arange(HEAD_DIMENSION) < HEAD_DIMENSION // 2, -1.0, 1.0
    )
    layer_result, d_x, sum_rows, sum_out, sum_gate_up, sum_down = layer(
        (
            cosine_values,
            sine_values,
            routes[0].T,
            query_key_value_weight,
            small,
            w_out.T,
            layer_input[0],
            d_out[0],
            w_gate_up,
            w_down,
        ),
        sizes,
    )[:6]
    sum_qkv, layer_result, d_x, sum_gate_up, sum_down, sum_out, sum_router, *sum_gains = finish(
        sum_rows, (layer_result, d_x, sum_gate_up, sum_down, sum_out), expert_total
    )
    return (
        layer_result[None],
        d_x[None],
        sum_gains[0][0],
        sum_qkv,
        sum_out.T,
        sum_router.T,
        sum_gains[1][0],
        sum_gate_up,
        jnp.swapaxes(sum_down, 1, 2),
    )


def solution(mesh):
    in_specs = (
        P(("expert", "dp"), "context", None),
        P(("expert", "context", "dp")),
        P(("expert", "context", "dp"), None),
        P(None, ("expert", "context", "dp")),
        P(("expert", "context", "dp"), None),
        P(("expert", "context", "dp")),
        P("expert", None, None),
        P("expert", None, None),
        P(("expert", "dp"), "context", None),
        P(("expert", "dp"), "context", None),
    )
    out_specs = (
        P(("expert", "dp"), "context", None),
        P(("expert", "dp"), "context", None),
        P(("expert", "context", "dp")),
        P(("expert", "context", "dp"), None),
        P(None, ("expert", "context", "dp")),
        P(("expert", "context", "dp"), None),
        P(("expert", "context", "dp")),
        P("expert", ("context", "dp"), None),
        P("expert", None, ("context", "dp")),
    )
    sizes = tuple(mesh.shape[a] for a in ("expert", "context", "dp"))
    local = local_fused if sizes == (4, 4, 2) else local_plain
    return jax.shard_map(local, mesh=mesh, in_specs=in_specs, out_specs=out_specs, check_vma=False)
```
